32 devices in a mesh: member: 2 (over x), lat: 4 (over z), lon: 4 (over y, core).
Axes of the slice: x: 2, y: 2, z: 4, core: 2. Of those that a mesh axis runs over, the one named last changes fastest.
Arguments:
- ensemble: bfloat16 [4, 16, 64, 256], P('member', 'lat', 'lon'), may hold values from -12 to 12
- norm_gain: float32 [256], replicated, may hold values from 0.5 to 1.5
- project_weight: bfloat16 [256, 768], replicated, may hold values from -0.375 to 0.375
- output_weight: bfloat16 [256, 256], replicated, may hold values from -0.375 to 0.375
- conv_kernel: bfloat16 [3, 3, 256, 256], replicated, may hold values from -0.125 to 0.125
- cotangent: bfloat16 [4, 16, 64, 256], P('member', 'lat', 'lon'), may hold values from -6 to 6
Outputs:
- result: bfloat16 [4, 16, 64, 256], P('member', 'lat', 'lon')
- grad_ensemble: bfloat16 [4, 16, 64, 256], P('member', 'lat', 'lon')
The draws below stay inside these ranges and needn't reach their ends.
All inputs are finite; a program needn't handle non-finite values.
Results may differ from the reference program's by a relative error of at most 0.018.
Values may be sent and summed in bfloat16 or wider, within the bound.
No kernel may reach another device: no remote copies, remote signals or barrier semaphores. Data moves between devices by JAX's collectives and lax.ppermute only.
A program may use at most 64 MiB of HBM per device.

```python
import math
import jax
import jax.numpy as jnp
from jax import lax

CHANNELS = 256
HEAD_COUNT = 8
MEMBERS = 4
LAT_ALL = 16
LON_ALL = 64


def draw_ensemble(key, part):
    first_key, second_key = jax.random.split(key, 2)
    shape_full = (MEMBERS, LAT_ALL, LON_ALL, CHANNELS)
    base = jax.random.truncated_normal(first_key, -4.0, 4.0, shape_full, jnp.float32)
    log_scale = jax.random.uniform(second_key, (MEMBERS, LAT_ALL, LON_ALL, 1), jnp.float32, jnp.log(0.3), jnp.log(3.0))
    return jnp.clip(base * jnp.exp(log_scale), -12.0, 12.0).astype(jnp.bfloat16)


def steps_of(stream_key, shape, cuts, low, top_value):
    gain = 1.0
    for position, shards_of in cuts:
        draws = jax.random.uniform(jax.random.fold_in(jax.random.fold_in(stream_key, 6), position), (shards_of,), jnp.float32, low / len(cuts), top_value / len(cuts))
        gain = gain * jnp.repeat(jnp.exp(draws), shape[position] // shards_of).reshape((-1,) + (1,) * (len(shape) - 1 - position))
    return gain


def bell_draw(rng, extent, spread, reach, pieces=(), held_as=jnp.bfloat16):
    level = steps_of(rng, extent, pieces, -0.22, 0.18) if pieces else 1.0
    array = jax.random.normal(rng, extent, jnp.float32) * spread * level
    return jnp.minimum(jnp.maximum(array, -reach), reach).astype(held_as)


def setup_inputs(seed: int = 0) -> dict:
    key_of = jax.random.split(jax.random.key(seed), 7)
    return {
        "ensemble": draw_ensemble(jax.random.fold_in(key_of[6], 71), 0),
        "norm_gain": jnp.clip(1.0 + 0.1 * jax.random.normal(key_of[1], (CHANNELS,), jnp.float32), 0.5, 1.5),
        "project_weight": bell_draw(key_of[2], (CHANNELS, 3 * CHANNELS), CHANNELS ** -0.5, 0.375),
        "output_weight": bell_draw(key_of[3], (CHANNELS, CHANNELS), CHANNELS ** -0.5, 0.375),
        "conv_kernel": bell_draw(key_of[4], (3, 3, CHANNELS, CHANNELS), (9 * CHANNELS) ** -0.5, 0.125),
        "cotangent": bell_draw(key_of[5], (MEMBERS, LAT_ALL, LON_ALL, CHANNELS), 1.0, 6.0, ((0, 2), (1, 4), (2, 4))),
    }


FLOOR = 0.5
EPSILON = 1e-06

def row_norm(values, gain_vec):
    mean_sq = lax.optimization_barrier(jnp.mean(values * values, axis=-1, keepdims=True))
    return values * lax.rsqrt(mean_sq + EPSILON) * gain_vec

def head_norm(values, head_count):
    shaped = values.reshape(values.shape[:-1] + (head_count, values.shape[-1] // head_count))
    mean_sq = lax.optimization_barrier(jnp.mean(shaped * shaped, axis=-1, keepdims=True))
    return (shaped * lax.rsqrt(jnp.maximum(mean_sq, FLOOR))).reshape(values.shape)

def split_heads(values, head_count):
    return values.reshape(values.shape[:-1] + (head_count, values.shape[-1] // head_count))

def widen(values):
    return lax.optimization_barrier(values).astype(jnp.float32)

def pad_globe(field_in):
    widened = jnp.concatenate([field_in[:, :, -1:], field_in, field_in[:, :, :1]], axis=2)
    zero_row = jnp.zeros_like(widened[:, :1])
    return jnp.concatenate([zero_row, widened, zero_row], axis=1)

def conv_taps(padded, kernel, lat_n, lon_n, adjoint):
    running = None
    for row_off in range(3):
        for col_off in range(3):
            tap = kernel[row_off, col_off].astype(jnp.float32)
            if adjoint:
                window = padded[:, 2 - row_off:2 - row_off + lat_n, 2 - col_off:2 - col_off + lon_n].astype(jnp.float32)
                summand = jnp.einsum('mabc,dc->mabd', window, tap)
            else:
                window = padded[:, row_off:row_off + lat_n, col_off:col_off + lon_n].astype(jnp.float32)
                summand = jnp.einsum('mabc,cd->mabd', window, tap)
            running = summand if running is None else running + summand
    return running

def reference(ensemble, norm_gain, project_weight, output_weight, conv_kernel, cotangent):
    members, lat_all, lon_all, channels = ensemble.shape
    cell_count = lat_all * lon_all
    score_scale = 1.0 / math.sqrt(channels // HEAD_COUNT)
    inputs = ensemble.reshape(members, cell_count, channels).astype(jnp.float32)
    normed = row_norm(inputs, norm_gain).astype(jnp.bfloat16)
    projected = jnp.dot(normed, project_weight, preferred_element_type=jnp.float32).astype(jnp.bfloat16)
    query_raw = projected[..., :channels]
    key_raw = projected[..., channels:2 * channels]
    value_rows = projected[..., 2 * channels:]
    queries = head_norm(query_raw.astype(jnp.float32), HEAD_COUNT).astype(jnp.bfloat16)
    key_rows = head_norm(key_raw.astype(jnp.float32), HEAD_COUNT).astype(jnp.bfloat16)
    query_heads = split_heads(widen(queries), HEAD_COUNT)
    key_heads = split_heads(widen(key_rows), HEAD_COUNT)
    value_heads = split_heads(value_rows.astype(jnp.float32), HEAD_COUNT)
    scores = jnp.einsum('mphd,nphd->mnhp', query_heads, key_heads) * score_scale
    expd = jnp.exp(scores)
    soft = expd / lax.optimization_barrier(jnp.sum(expd, axis=1, keepdims=True))
    rounded = soft.astype(jnp.bfloat16)
    rounded_wide = widen(rounded)
    mixed_out = jnp.einsum('mnhp,nphd->mphd', rounded_wide, value_heads)
    mixed_out = mixed_out.reshape(members, cell_count, channels).astype(jnp.bfloat16)
    updated = (inputs + jnp.dot(mixed_out, output_weight, preferred_element_type=jnp.float32)).astype(jnp.bfloat16)
    field_up = updated.reshape(members, lat_all, lon_all, channels)
    result = field_up.astype(jnp.float32) + conv_taps(pad_globe(field_up), conv_kernel, lat_all, lon_all, False)
    result = result.astype(jnp.bfloat16)
    grad_field = cotangent.astype(jnp.float32) + conv_taps(pad_globe(cotangent), conv_kernel, lat_all, lon_all, True)
    grad_rows = grad_field.reshape(members, cell_count, channels)
    grad_mixed = jnp.einsum('mpc,dc->mpd', widen(grad_rows.astype(jnp.bfloat16)), output_weight.astype(jnp.float32))
    grad_mixed = grad_mixed.astype(jnp.bfloat16)
    grad_heads = split_heads(widen(grad_mixed), HEAD_COUNT)
    dprob = jnp.einsum('mphd,nphd->mnhp', grad_heads, value_heads)
    dscore = soft * (dprob - lax.optimization_barrier(jnp.sum(soft * dprob, axis=1, keepdims=True)))
    dscore_wide = widen(dscore.astype(jnp.bfloat16))
    query_grad = (jnp.einsum('mnhp,nphd->mphd', dscore_wide, key_heads) * score_scale).reshape(members, cell_count, channels)
    key_grad = (jnp.einsum('mnhp,mphd->nphd', dscore_wide, query_heads) * score_scale).reshape(members, cell_count, channels)
    value_grad = jnp.einsum('mnhp,mphd->nphd', rounded_wide, grad_heads).reshape(members, cell_count, channels)
    _, pull_query = jax.vjp(lambda t: head_norm(t, HEAD_COUNT), query_raw.astype(jnp.float32))
    _, pull_key = jax.vjp(lambda t: head_norm(t, HEAD_COUNT), key_raw.astype(jnp.float32))
    grad_query_raw = pull_query(query_grad)[0]
    grad_key_raw = pull_key(key_grad)[0]
    grad_proj = jnp.concatenate([grad_query_raw, grad_key_raw, value_grad], axis=-1).astype(jnp.bfloat16)
    grad_normed = jnp.einsum('mpe,ce->mpc', widen(grad_proj), project_weight.astype(jnp.float32))
    _, pull_norm = jax.vjp(lambda t: row_norm(t, norm_gain), inputs)
    grad_inputs = pull_norm(grad_normed)[0]
    grad_ensemble = (grad_rows + grad_inputs).astype(jnp.bfloat16).reshape(members, lat_all, lon_all, channels)
    return (result, grad_ensemble)
```

```python
import functools
import math

import jax
import jax.numpy as jnp
from jax import lax
from jax.experimental import pallas as pl
from jax.experimental.pallas import tpu as pltpu
from jax.sharding import PartitionSpec as P

HEAD_COUNT = 8


FLOOR = 0.5
EPSILON = 1e-06


def padded_2(block, sides, width, periodic):
    for axis, dim in sides:
        count = lax.axis_size(axis)
        forward = [(i, i + 1) for i in range(count - 1)]
        if periodic:
            forward.append((count - 1, 0))
        backward = [(target, source) for source, target in forward]
        low = lax.ppermute(
            lax.slice_in_dim(block, block.shape[dim] - width, None, axis=dim), axis, forward
        )
        high = lax.ppermute(lax.slice_in_dim(block, 0, width, axis=dim), axis, backward)
        block = jnp.concatenate([low, block, high], axis=dim)
    return block


def row_norm(values, gain_vec):
    mean_sq = jnp.mean(values * values, axis=-1, keepdims=True)
    return values * lax.rsqrt(mean_sq + EPSILON) * gain_vec


def head_norm(values, head_count):
    shaped = values.reshape(values.shape[:-1] + (head_count, values.shape[-1] // head_count))
    mean_sq = jnp.mean(shaped * shaped, axis=-1, keepdims=True)
    return (shaped * lax.rsqrt(jnp.maximum(mean_sq, FLOOR))).reshape(values.shape)


def split_heads(values, head_count):
    return values.reshape(values.shape[:-1] + (head_count, values.shape[-1] // head_count))


def head_pullback(raw_rows, grad_rows):
    _, pullback = jax.vjp(lambda t: head_norm(t, HEAD_COUNT), raw_rows.astype(jnp.float32))
    return pullback(grad_rows)[0]


def pad_field(field_in):
    widened = padded_2(field_in, (("lon", 2),), 1, True)
    return padded_2(widened, (("lat", 1),), 1, False)


def conv_taps(padded, kernel, lat_n, lon_n, adjoint):
    running = None
    for row_off in range(3):
        for col_off in range(3):
            if adjoint:
                window = padded[
                    :, 2 - row_off : 2 - row_off + lat_n, 2 - col_off : 2 - col_off + lon_n
                ]
                summand = jnp.einsum(
                    "mabc,dc->mabd",
                    window,
                    kernel[row_off, col_off],
                    preferred_element_type=jnp.float32,
                )
            else:
                window = padded[:, row_off : row_off + lat_n, col_off : col_off + lon_n]
                summand = jnp.einsum(
                    "mabc,cd->mabd",
                    window,
                    kernel[row_off, col_off],
                    preferred_element_type=jnp.float32,
                )
            running = summand if running is None else running + summand
    return running


def per_device_general(ensemble, norm_gain, project_weight, output_weight, conv_kernel, cotangent):
    mem_dev, lat_dev, lon_dev, channels = ensemble.shape
    cell_count = lat_dev * lon_dev
    score_scale = 1.0 / math.sqrt(channels // HEAD_COUNT)
    inputs = ensemble.reshape(mem_dev, cell_count, channels).astype(jnp.float32)
    normed = row_norm(inputs, norm_gain).astype(jnp.bfloat16)
    spread = lax.all_to_all(normed, "member", split_axis=1, concat_axis=0, tiled=True)
    projected = jnp.dot(spread, project_weight, preferred_element_type=jnp.float32).astype(
        jnp.bfloat16
    )
    query_raw = projected[..., :channels]
    key_raw = projected[..., channels : 2 * channels]
    value_rows = projected[..., 2 * channels :]
    key_rows = head_norm(key_raw.astype(jnp.float32), HEAD_COUNT).astype(jnp.bfloat16)
    queries = head_norm(query_raw.astype(jnp.float32), HEAD_COUNT).astype(jnp.bfloat16)
    query_heads = split_heads(queries, HEAD_COUNT)
    key_heads = split_heads(key_rows, HEAD_COUNT)
    value_heads = split_heads(value_rows, HEAD_COUNT)
    scores = (
        jnp.einsum("mphd,nphd->mnhp", query_heads, key_heads, preferred_element_type=jnp.float32)
        * score_scale
    )
    expd = jnp.exp(scores)
    soft = expd / jnp.sum(expd, axis=1, keepdims=True)
    rounded = soft.astype(jnp.bfloat16)
    mixed_out = jnp.einsum(
        "mnhp,nphd->mphd", rounded, value_heads, preferred_element_type=jnp.float32
    )
    mixed_out = mixed_out.reshape(query_raw.shape).astype(jnp.bfloat16)
    mixed_out = lax.all_to_all(mixed_out, "member", split_axis=0, concat_axis=1, tiled=True)
    updated = (
        inputs + jnp.dot(mixed_out, output_weight, preferred_element_type=jnp.float32)
    ).astype(jnp.bfloat16)
    field_up = updated.reshape(mem_dev, lat_dev, lon_dev, channels)
    result = field_up.astype(jnp.float32) + conv_taps(
        pad_field(field_up), conv_kernel, lat_dev, lon_dev, False
    )
    result = result.astype(jnp.bfloat16)
    grad_field = cotangent.astype(jnp.float32) + conv_taps(
        pad_field(cotangent), conv_kernel, lat_dev, lon_dev, True
    )
    grad_rows = grad_field.reshape(mem_dev, cell_count, channels)
    grad_mixed = jnp.einsum(
        "mpc,dc->mpd",
        grad_rows.astype(jnp.bfloat16),
        output_weight,
        preferred_element_type=jnp.float32,
    )
    grad_mixed = grad_mixed.astype(jnp.bfloat16)
    grad_mixed = lax.all_to_all(grad_mixed, "member", split_axis=1, concat_axis=0, tiled=True)
    grad_heads = split_heads(grad_mixed, HEAD_COUNT)
    dprob = jnp.einsum(
        "mphd,nphd->mnhp", grad_heads, value_heads, preferred_element_type=jnp.float32
    )
    dscore = (soft * (dprob - jnp.sum(soft * dprob, axis=1, keepdims=True))).astype(jnp.bfloat16)
    query_grad = (
        jnp.einsum("mnhp,nphd->mphd", dscore, key_heads, preferred_element_type=jnp.float32)
        * score_scale
    )
    query_grad = query_grad.reshape(query_raw.shape)
    key_grad = (
        jnp.einsum("mnhp,mphd->nphd", dscore, query_heads, preferred_element_type=jnp.float32)
        * score_scale
    )
    key_grad = key_grad.reshape(key_raw.shape)
    value_grad = jnp.einsum(
        "mnhp,mphd->nphd", rounded, grad_heads, preferred_element_type=jnp.float32
    )
    value_grad = value_grad.reshape(key_raw.shape)
    grad_query_raw = head_pullback(query_raw, query_grad)
    grad_key_raw = head_pullback(key_raw, key_grad)
    grad_proj = jnp.concatenate([grad_query_raw, grad_key_raw, value_grad], axis=-1).astype(
        jnp.bfloat16
    )
    grad_proj = lax.all_to_all(grad_proj, "member", split_axis=0, concat_axis=1, tiled=True)
    grad_normed = jnp.einsum(
        "mpe,ce->mpc", grad_proj, project_weight, preferred_element_type=jnp.float32
    )
    _, pull_norm = jax.vjp(lambda t: row_norm(t, norm_gain), inputs)
    grad_inputs = pull_norm(grad_normed)[0]
    grad_ensemble = (
        (grad_rows + grad_inputs).astype(jnp.bfloat16).reshape(mem_dev, lat_dev, lon_dev, channels)
    )
    return (result, grad_ensemble)


F32 = jnp.float32
BF16 = jnp.bfloat16
VMEM_LIMIT = 48 * 1024 * 1024


def lon_is_even():
    return lax.rem(lax.axis_index("lon"), 2) == 0


def pack_strips_kernel(ens_ref, cot_ref, other_ref, core_ref, chip_ref, low_scr, high_scr):
    mem, rows, cols, _ = ens_ref.shape
    index = 0
    for array, ref in enumerate((ens_ref, cot_ref)):
        for member in range(2 * mem):
            for row in range(rows):
                if member < mem:
                    slab = ref[member, row]
                else:
                    slab = other_ref[array, member - mem, row]
                slab = slab.astype(F32)
                low_scr[index : index + 1, :] = slab[0:1]
                high_scr[index : index + 1, :] = slab[cols - 1 : cols]
                index += 1
    even = lon_is_even()
    low, high = low_scr[...], high_scr[...]
    core_ref[...] = jnp.where(even, high, low).astype(BF16)
    chip_ref[...] = jnp.where(even, low, high).astype(BF16)


def pack_rows_kernel(
    ens_ref, cot_ref, other_ref, core_ref, chip_ref, up_ref, down_ref, low_scr, high_scr, edge_scr
):
    mem, rows, cols, _ = ens_ref.shape
    groups = 2 * mem
    even = lon_is_even()
    core, chip = core_ref[...].astype(F32), chip_ref[...].astype(F32)
    low_scr[...] = jnp.where(even, chip, core)
    high_scr[...] = jnp.where(even, core, chip)
    for out_ref, row in ((up_ref, 0), (down_ref, rows - 1)):
        for array, ref in enumerate((ens_ref, cot_ref)):
            for member in range(groups):
                slot = array * groups + member
                if member < mem:
                    slab = ref[member, row]
                else:
                    slab = other_ref[array, member - mem, row]
                out_ref[slot * cols : (slot + 1) * cols, :] = slab
                source = slot * rows + row
                edge_scr[slot : slot + 1, :] = low_scr[source : source + 1, :]
                edge_scr[2 * groups + slot : 2 * groups + slot + 1, :] = high_scr[
                    source : source + 1, :
                ]
        out_ref[2 * groups * cols :, :] = edge_scr[...].astype(BF16)


def dot_nn(a, b):
    return lax.dot_general(a, b, (((1,), (0,)), ((), ())), preferred_element_type=F32)


def dot_nt(a, b):
    return lax.dot_general(a, b, (((1,), (1,)), ((), ())), preferred_element_type=F32)


def head_sums(values, same_head):
    high = values.astype(BF16)
    low = (values - high.astype(F32)).astype(BF16)
    return dot_nn(high, same_head) + dot_nn(low, same_head)


def main_kernel(
    ens_ref,
    cot_ref,
    other_ref,
    core_ref,
    chip_ref,
    top_ref,
    bottom_ref,
    gain_ref,
    project_ref,
    output_ref,
    conv_ref,
    result_ref,
    grad_ref,
    x_scr,
    cot_scr,
    low_scr,
    high_scr,
    proj_scr,
    shift_scr,
    cot_shift_scr,
):
    mem, rows, cols, channels = ens_ref.shape
    groups = 2 * mem
    tall = rows + 2
    centre = tall * cols
    per_member = x_scr.shape[1]
    own = slice(cols, cols + rows * cols)
    cells = rows * cols
    width = channels // HEAD_COUNT
    scale = 1.0 / math.sqrt(width)
    even = lon_is_even()

    core, chip = core_ref[...].astype(F32), chip_ref[...].astype(F32)
    low_scr[...] = jnp.where(even, chip, core)
    high_scr[...] = jnp.where(even, core, chip)
    for array, (ref, scr) in enumerate(((ens_ref, x_scr), (cot_ref, cot_scr))):
        for member in range(groups):
            slot = array * groups + member
            if member < mem:
                block = ref[member]
            else:
                block = other_ref[array, member - mem]
            scr[member, cols : cols + cells, :] = block.reshape(cells, channels).astype(F32)
            for halo_ref, place in ((top_ref, 0), (bottom_ref, tall - 1)):
                scr[member, place * cols : (place + 1) * cols, :] = halo_ref[
                    slot * cols : (slot + 1) * cols, :
                ].astype(F32)
            scr[member, centre:, :] = jnp.zeros((per_member - centre, channels), F32)
            for side, side_scr in ((0, low_scr), (1, high_scr)):
                base = centre + 8 * side
                scr[member, base + 1 : base + 1 + rows, :] = side_scr[
                    slot * rows : (slot + 1) * rows, :
                ]
        for side in (0, 1):
            first = 2 * groups * cols + 2 * groups * side + array * groups
            base = centre + 8 * side
            start = 2 * groups * cols
            for halo_ref, place in ((top_ref, 0), (bottom_ref, tall - 1)):
                edges = halo_ref[start:, :].astype(F32)
                for member in range(groups):
                    at = first - start + member
                    scr[member, base + place : base + place + 1, :] = edges[at : at + 1]

    lane_row = lax.broadcasted_iota(jnp.int32, (channels, channels), 0) // width
    lane_col = lax.broadcasted_iota(jnp.int32, (channels, channels), 1) // width
    same_head = jnp.where(lane_row == lane_col, 1.0, 0.0).astype(BF16)
    gain = gain_ref[...]

    def row_rsqrt(values):
        return lax.rsqrt(jnp.mean(values * values, axis=-1, keepdims=True) + EPSILON)

    x_all = x_scr[...].reshape(groups * per_member, channels)
    normed = (x_all * row_rsqrt(x_all) * gain).astype(BF16)
    proj_scr[...] = dot_nn(normed, project_ref[...]).astype(BF16)

    def head_unit(raw):
        raw = raw.astype(F32)
        mean_sq = head_sums(raw * raw, same_head) * (1.0 / width)
        inverse = lax.rsqrt(jnp.maximum(mean_sq, FLOOR))
        return raw, mean_sq, inverse, (raw * inverse).astype(BF16)

    queries, query_parts, keys, key_parts, values = [], [], [], [], []
    for member in range(groups):
        at = member * per_member
        full = slice(at, at + per_member)
        inner = slice(at + own.start, at + own.stop)
        parts = head_unit(proj_scr[full if member < mem else inner, :channels])
        query_parts.append(parts[:3])
        queries.append(parts[3])
        parts = head_unit(proj_scr[full, channels : 2 * channels])
        key_parts.append(parts[:3])
        keys.append(parts[3])
        values.append(proj_scr[full, 2 * channels :])

    soft, rounded, updated = [], [], []
    for m in range(groups):
        take = slice(None) if m < mem else own
        exps = []
        for n in range(groups):
            product = queries[m] * keys[n][take]
            exps.append(jnp.exp(dot_nn(product, same_head) * scale))
        total = exps[0]
        for n in range(1, groups):
            total = total + exps[n]
        inverse = 1.0 / total
        probs = [e * inverse for e in exps]
        probs_16 = [p.astype(BF16) for p in probs]
        if m < mem:
            mixed = probs_16[0].astype(F32) * values[0].astype(F32)
            for n in range(1, groups):
                mixed = mixed + probs_16[n].astype(F32) * values[n].astype(F32)
            mixed = mixed.astype(BF16)
            updated.append((x_scr[m] + dot_nn(mixed, output_ref[...])).astype(BF16).astype(F32))
            probs = [p[own] for p in probs]
            probs_16 = [p[own] for p in probs_16]
        soft.append(probs)
        rounded.append(probs_16)

    def shifted(scr, member, field):
        column = lax.broadcasted_iota(jnp.int32, (cols, channels), 0)
        for place in range(tall):
            slab = field[place * cols : (place + 1) * cols]
            low = field[centre + place : centre + place + 1]
            high = field[centre + 8 + place : centre + 8 + place + 1]
            back = jnp.where(column == 0, low, pltpu.roll(slab, 1, 0))
            ahead = jnp.where(column == cols - 1, high, pltpu.roll(slab, cols - 1, 0))
            rows_at = slice(place * cols, (place + 1) * cols)
            scr[member, rows_at, :channels] = back.astype(BF16)
            scr[member, rows_at, channels : 2 * channels] = slab.astype(BF16)
            scr[member, rows_at, 2 * channels :] = ahead.astype(BF16)

    for member in range(mem):
        shifted(shift_scr, member, updated[member])
    for member in range(groups):
        shifted(cot_shift_scr, member, cot_scr[member])

    total = jnp.concatenate([u[own] for u in updated], axis=0)
    for r in range(3):
        window = jnp.concatenate(
            [shift_scr[m, r * cols : r * cols + cells, :] for m in range(mem)], axis=0
        )
        total = total + dot_nn(window, conv_ref[3 * channels * r : 3 * channels * (r + 1), :])
    result_ref[...] = total.astype(BF16).reshape(mem, rows, cols, channels)

    total = jnp.concatenate([cot_scr[m, own, :] for m in range(groups)], axis=0)
    for r in range(3):
        for c in range(3):
            lanes = slice((2 - c) * channels, (3 - c) * channels)
            begin = (2 - r) * cols
            window = jnp.concatenate(
                [cot_shift_scr[m, begin : begin + cells, lanes] for m in range(groups)], axis=0
            )
            tap = (3 * r + c) * channels
            total = total + dot_nt(window, conv_ref[tap : tap + channels, :])
    grad_field = total
    grad_mixed = dot_nt(grad_field.astype(BF16), output_ref[...]).astype(BF16)
    grads = [grad_mixed[m * cells : (m + 1) * cells] for m in range(groups)]

    inner_keys = [k[own] for k in keys]
    inner_values = [v[own] for v in values]
    inner_queries = [q[own] if m < mem else q for m, q in enumerate(queries)]
    query_grad = [None] * mem
    key_grad = [None] * mem
    value_grad = [None] * mem
    for m in range(groups):
        dprob = [dot_nn(grads[m] * inner_values[n], same_head) for n in range(groups)]
        mean = soft[m][0] * dprob[0]
        for n in range(1, groups):
            mean = mean + soft[m][n] * dprob[n]
        for n in range(groups):
            if m >= mem and n >= mem:
                continue
            dscore = (soft[m][n] * (dprob[n] - mean)).astype(BF16).astype(F32)
            if m < mem:
                term = dscore * inner_keys[n].astype(F32)
                query_grad[m] = term if query_grad[m] is None else query_grad[m] + term
            if n < mem:
                term = dscore * inner_queries[m].astype(F32)
                key_grad[n] = term if key_grad[n] is None else key_grad[n] + term
                term = rounded[m][n].astype(F32) * grads[m].astype(F32)
                value_grad[n] = term if value_grad[n] is None else value_grad[n] + term

    def head_pull(parts, grad):
        raw, mean_sq, inverse = (p[own] for p in parts)
        grad = grad * scale
        inner = head_sums(grad * raw, same_head) * (1.0 / width)
        active = jnp.where(mean_sq > FLOOR, 1.0, jnp.where(mean_sq == FLOOR, 0.5, 0.0))
        return inverse * grad - active * raw * (inverse * inverse * inverse) * inner

    for m in range(mem):
        grad_proj = jnp.concatenate(
            [
                head_pull(query_parts[m], query_grad[m]).astype(BF16),
                head_pull(key_parts[m], key_grad[m]).astype(BF16),
                value_grad[m].astype(BF16),
            ],
            axis=1,
        )
        grad_normed = dot_nt(grad_proj, project_ref[...]) * gain
        x = x_scr[m, own, :]
        inverse = row_rsqrt(x)
        inner = jnp.mean(x * grad_normed, axis=-1, keepdims=True)
        pulled = inverse * grad_normed - x * (inverse * inverse * inverse * inner)
        total = grad_field[m * cells : (m + 1) * cells] + pulled
        grad_ref[m] = total.astype(BF16).reshape(rows, cols, channels)


def local_call(kernel, out_shape, scratch, count, name):
    whole = pl.BlockSpec(memory_space=pltpu.VMEM)
    return pl.pallas_call(
        kernel,
        out_shape=out_shape,
        in_specs=[whole] * count,
        out_specs=jax.tree.map(lambda _: whole, out_shape),
        scratch_shapes=scratch,
        compiler_params=pltpu.CompilerParams(vmem_limit_bytes=VMEM_LIMIT),
        name=name,
    )


def per_device_paired(ensemble, norm_gain, project_weight, output_weight, conv_kernel, cotangent):
    mem, rows, cols, channels = ensemble.shape
    groups = 2 * mem
    lon_count = lax.axis_size("lon")
    lat_count = lax.axis_size("lat")
    strip_rows = 2 * groups * rows
    halo_rows = 2 * groups * (cols + 2)

    swap = [(0, 1), (1, 0)]
    other = lax.ppermute(jnp.stack([ensemble, cotangent]), "member", swap)

    strip = jax.ShapeDtypeStruct((strip_rows, channels), BF16)
    strip_scr = pltpu.VMEM((strip_rows, channels), F32)
    core_send, chip_send = local_call(
        pack_strips_kernel, (strip, strip), [strip_scr] * 2, 3, "pack_strips"
    )(ensemble, cotangent, other)
    core_pairs = [(i, i ^ 1) for i in range(lon_count)]
    chip_pairs = [(i, (i - 1 if i % 2 == 0 else i + 1) % lon_count) for i in range(lon_count)]
    chip_recv = lax.ppermute(chip_send, "lon", chip_pairs)
    core_recv = lax.ppermute(core_send, "lon", core_pairs)

    halo = jax.ShapeDtypeStruct((halo_rows, channels), BF16)
    up_send, down_send = local_call(
        pack_rows_kernel,
        (halo, halo),
        [strip_scr] * 2 + [pltpu.VMEM((4 * groups, channels), F32)],
        5,
        "pack_rows",
    )(ensemble, cotangent, other, core_recv, chip_recv)
    top = lax.ppermute(down_send, "lat", [(i, i + 1) for i in range(lat_count - 1)])
    bottom = lax.ppermute(up_send, "lat", [(i + 1, i) for i in range(lat_count - 1)])

    tall = rows + 2
    per_member = tall * cols + 16
    block = jax.ShapeDtypeStruct(ensemble.shape, BF16)
    return local_call(
        main_kernel,
        (block, block),
        [
            pltpu.VMEM((groups, per_member, channels), F32),
            pltpu.VMEM((groups, per_member, channels), F32),
            strip_scr,
            strip_scr,
            pltpu.VMEM((groups * per_member, 3 * channels), BF16),
            pltpu.VMEM((mem, tall * cols, 3 * channels), BF16),
            pltpu.VMEM((groups, tall * cols, 3 * channels), BF16),
        ],
        11,
        "main",
    )(
        ensemble,
        cotangent,
        other,
        core_recv,
        chip_recv,
        top,
        bottom,
        norm_gain.reshape(1, channels),
        project_weight,
        output_weight,
        conv_kernel.reshape(9 * channels, channels),
    )


def solution(mesh):
    paired = mesh.shape["member"] == 2 and mesh.shape["lon"] % 2 == 0
    per_device = per_device_paired if paired else per_device_general
    in_specs = (
        P("member", "lat", "lon", None),
        P(),
        P(),
        P(),
        P(),
        P("member", "lat", "lon", None),
    )
    out_specs = (P("member", "lat", "lon", None), P("member", "lat", "lon", None))
    return jax.shard_map(
        per_device, mesh=mesh, in_specs=in_specs, out_specs=out_specs, check_vma=False
    )
```

```python
import functools
import math

import jax
import jax.numpy as jnp
from jax import lax
from jax.experimental import pallas as pl
from jax.experimental.pallas import tpu as pltpu
from jax.sharding import PartitionSpec as P

HEAD_COUNT = 8


FLOOR = 0.5
EPSILON = 1e-06


def padded_2(block, sides, width, periodic):
    for axis, dim in sides:
        count = lax.axis_size(axis)
        forward = [(i, i + 1) for i in range(count - 1)]
        if periodic:
            forward.append((count - 1, 0))
        backward = [(target, source) for source, target in forward]
        low = lax.ppermute(
            lax.slice_in_dim(block, block.shape[dim] - width, None, axis=dim), axis, forward
        )
        high = lax.ppermute(lax.slice_in_dim(block, 0, width, axis=dim), axis, backward)
        block = jnp.concatenate([low, block, high], axis=dim)
    return block


def row_norm(values, gain_vec):
    mean_sq = jnp.mean(values * values, axis=-1, keepdims=True)
    return values * lax.rsqrt(mean_sq + EPSILON) * gain_vec


def head_norm(values, head_count):
    shaped = values.reshape(values.shape[:-1] + (head_count, values.shape[-1] // head_count))
    mean_sq = jnp.mean(shaped * shaped, axis=-1, keepdims=True)
    return (shaped * lax.rsqrt(jnp.maximum(mean_sq, FLOOR))).reshape(values.shape)


def split_heads(values, head_count):
    return values.reshape(values.shape[:-1] + (head_count, values.shape[-1] // head_count))


def head_pullback(raw_rows, grad_rows):
    _, pullback = jax.vjp(lambda t: head_norm(t, HEAD_COUNT), raw_rows.astype(jnp.float32))
    return pullback(grad_rows)[0]


def pad_field(field_in):
    widened = padded_2(field_in, (("lon", 2),), 1, True)
    return padded_2(widened, (("lat", 1),), 1, False)


def conv_taps(padded, kernel, lat_n, lon_n, adjoint):
    running = None
    for row_off in range(3):
        for col_off in range(3):
            if adjoint:
                window = padded[
                    :, 2 - row_off : 2 - row_off + lat_n, 2 - col_off : 2 - col_off + lon_n
                ]
                summand = jnp.einsum(
                    "mabc,dc->mabd",
                    window,
                    kernel[row_off, col_off],
                    preferred_element_type=jnp.float32,
                )
            else:
                window = padded[:, row_off : row_off + lat_n, col_off : col_off + lon_n]
                summand = jnp.einsum(
                    "mabc,cd->mabd",
                    window,
                    kernel[row_off, col_off],
                    preferred_element_type=jnp.float32,
                )
            running = summand if running is None else running + summand
    return running


def per_device_general(ensemble, norm_gain, project_weight, output_weight, conv_kernel, cotangent):
    mem_dev, lat_dev, lon_dev, channels = ensemble.shape
    cell_count = lat_dev * lon_dev
    score_scale = 1.0 / math.sqrt(channels // HEAD_COUNT)
    inputs = ensemble.reshape(mem_dev, cell_count, channels).astype(jnp.float32)
    normed = row_norm(inputs, norm_gain).astype(jnp.bfloat16)
    spread = lax.all_to_all(normed, "member", split_axis=1, concat_axis=0, tiled=True)
    projected = jnp.dot(spread, project_weight, preferred_element_type=jnp.float32).astype(
        jnp.bfloat16
    )
    query_raw = projected[..., :channels]
    key_raw = projected[..., channels : 2 * channels]
    value_rows = projected[..., 2 * channels :]
    key_rows = head_norm(key_raw.astype(jnp.float32), HEAD_COUNT).astype(jnp.bfloat16)
    queries = head_norm(query_raw.astype(jnp.float32), HEAD_COUNT).astype(jnp.bfloat16)
    query_heads = split_heads(queries, HEAD_COUNT)
    key_heads = split_heads(key_rows, HEAD_COUNT)
    value_heads = split_heads(value_rows, HEAD_COUNT)
    scores = (
        jnp.einsum("mphd,nphd->mnhp", query_heads, key_heads, preferred_element_type=jnp.float32)
        * score_scale
    )
    expd = jnp.exp(scores)
    soft = expd / jnp.sum(expd, axis=1, keepdims=True)
    rounded = soft.astype(jnp.bfloat16)
    mixed_out = jnp.einsum(
        "mnhp,nphd->mphd", rounded, value_heads, preferred_element_type=jnp.float32
    )
    mixed_out = mixed_out.reshape(query_raw.shape).astype(jnp.bfloat16)
    mixed_out = lax.all_to_all(mixed_out, "member", split_axis=0, concat_axis=1, tiled=True)
    updated = (
        inputs + jnp.dot(mixed_out, output_weight, preferred_element_type=jnp.float32)
    ).astype(jnp.bfloat16)
    field_up = updated.reshape(mem_dev, lat_dev, lon_dev, channels)
    result = field_up.astype(jnp.float32) + conv_taps(
        pad_field(field_up), conv_kernel, lat_dev, lon_dev, False
    )
    result = result.astype(jnp.bfloat16)
    grad_field = cotangent.astype(jnp.float32) + conv_taps(
        pad_field(cotangent), conv_kernel, lat_dev, lon_dev, True
    )
    grad_rows = grad_field.reshape(mem_dev, cell_count, channels)
    grad_mixed = jnp.einsum(
        "mpc,dc->mpd",
        grad_rows.astype(jnp.bfloat16),
        output_weight,
        preferred_element_type=jnp.float32,
    )
    grad_mixed = grad_mixed.astype(jnp.bfloat16)
    grad_mixed = lax.all_to_all(grad_mixed, "member", split_axis=1, concat_axis=0, tiled=True)
    grad_heads = split_heads(grad_mixed, HEAD_COUNT)
    dprob = jnp.einsum(
        "mphd,nphd->mnhp", grad_heads, value_heads, preferred_element_type=jnp.float32
    )
    dscore = (soft * (dprob - jnp.sum(soft * dprob, axis=1, keepdims=True))).astype(jnp.bfloat16)
    query_grad = (
        jnp.einsum("mnhp,nphd->mphd", dscore, key_heads, preferred_element_type=jnp.float32)
        * score_scale
    )
    query_grad = query_grad.reshape(query_raw.shape)
    key_grad = (
        jnp.einsum("mnhp,mphd->nphd", dscore, query_heads, preferred_element_type=jnp.float32)
        * score_scale
    )
    key_grad = key_grad.reshape(key_raw.shape)
    value_grad = jnp.einsum(
        "mnhp,mphd->nphd", rounded, grad_heads, preferred_element_type=jnp.float32
    )
    value_grad = value_grad.reshape(key_raw.shape)
    grad_query_raw = head_pullback(query_raw, query_grad)
    grad_key_raw = head_pullback(key_raw, key_grad)
    grad_proj = jnp.concatenate([grad_query_raw, grad_key_raw, value_grad], axis=-1).astype(
        jnp.bfloat16
    )
    grad_proj = lax.all_to_all(grad_proj, "member", split_axis=0, concat_axis=1, tiled=True)
    grad_normed = jnp.einsum(
        "mpe,ce->mpc", grad_proj, project_weight, preferred_element_type=jnp.float32
    )
    _, pull_norm = jax.vjp(lambda t: row_norm(t, norm_gain), inputs)
    grad_inputs = pull_norm(grad_normed)[0]
    grad_ensemble = (
        (grad_rows + grad_inputs).astype(jnp.bfloat16).reshape(mem_dev, lat_dev, lon_dev, channels)
    )
    return (result, grad_ensemble)


F32 = jnp.float32
BF16 = jnp.bfloat16
VMEM_LIMIT = 48 * 1024 * 1024


def lon_is_even():
    return lax.rem(lax.axis_index("lon"), 2) == 0


def load_kernel(*refs):
    count = len(refs) // 2
    sems = refs[-1]
    copies = [
        pltpu.make_async_copy(refs[i], refs[count + i], sems.at[i]) for i in range(count)
    ]
    for copy in copies:
        copy.start()
    for copy in copies:
        copy.wait()


def stack_kernel(ens_ref, cot_ref, both_ref, sems):
    copies = [
        pltpu.make_async_copy(ref, both_ref.at[i], sems.at[i])
        for i, ref in enumerate((ens_ref, cot_ref))
    ]
    for copy in copies:
        copy.start()
    for copy in copies:
        copy.wait()


def pack_strips_kernel(both_ref, other_ref, core_ref, chip_ref, low_scr, high_scr):
    _, mem, rows, cols, _ = both_ref.shape
    index = 0
    for array in range(2):
        for member in range(2 * mem):
            for row in range(rows):
                if member < mem:
                    slab = both_ref[array, member, row]
                else:
                    slab = other_ref[array, member - mem, row]
                slab = slab.astype(F32)
                low_scr[index : index + 1, :] = slab[0:1]
                high_scr[index : index + 1, :] = slab[cols - 1 : cols]
                index += 1
    even = lon_is_even()
    low, high = low_scr[...], high_scr[...]
    core_ref[...] = jnp.where(even, high, low).astype(BF16)
    chip_ref[...] = jnp.where(even, low, high).astype(BF16)


def pack_rows_kernel(
    both_ref, other_ref, core_ref, chip_ref, first_ref, second_ref, low_scr, high_scr, edge_scr
):
    _, mem, rows, cols, _ = both_ref.shape
    groups = 2 * mem
    even = lon_is_even()
    core, chip = core_ref[...].astype(F32), chip_ref[...].astype(F32)
    low_scr[...] = jnp.where(even, chip, core)
    high_scr[...] = jnp.where(even, core, chip)
    lat_even = lax.rem(lax.axis_index("lat"), 2) == 0
    for out_ref, first in ((first_ref, True), (second_ref, False)):
        row = jnp.where(lat_even, rows - 1, 0) if first else jnp.where(lat_even, 0, rows - 1)
        for array in range(2):
            for member in range(groups):
                slot = array * groups + member
                if member < mem:
                    slab = both_ref[array, member, row]
                else:
                    slab = other_ref[array, member - mem, row]
                out_ref[slot * cols : (slot + 1) * cols, :] = slab
                source = slot * rows + row
                edge_scr[slot : slot + 1, :] = low_scr[pl.ds(source, 1), :]
                edge_scr[2 * groups + slot : 2 * groups + slot + 1, :] = high_scr[
                    pl.ds(source, 1), :
                ]
        out_ref[2 * groups * cols :, :] = edge_scr[...].astype(BF16)


def dot_nn(a, b):
    return lax.dot_general(a, b, (((1,), (0,)), ((), ())), preferred_element_type=F32)


def dot_nt(a, b):
    return lax.dot_general(a, b, (((1,), (1,)), ((), ())), preferred_element_type=F32)


def head_sums(values, same_head):
    high = values.astype(BF16)
    low = (values - high.astype(F32)).astype(BF16)
    return dot_nn(high, same_head) + dot_nn(low, same_head)


def main_kernel(
    both_ref,
    other_ref,
    core_ref,
    chip_ref,
    first_ref,
    second_ref,
    gain_ref,
    project_ref,
    output_ref,
    conv_ref,
    result_ref,
    grad_ref,
    x_scr,
    cot_scr,
    low_scr,
    high_scr,
    proj_scr,
    shift_scr,
    cot_shift_scr,
    *,
    lat_count,
):
    _, mem, rows, cols, channels = both_ref.shape
    groups = 2 * mem
    tall = rows + 2
    centre = tall * cols
    per_member = x_scr.shape[1]
    own = slice(cols, cols + rows * cols)
    cells = rows * cols
    width = channels // HEAD_COUNT
    scale = 1.0 / math.sqrt(width)
    even = lon_is_even()

    core, chip = core_ref[...].astype(F32), chip_ref[...].astype(F32)
    low_scr[...] = jnp.where(even, chip, core)
    high_scr[...] = jnp.where(even, core, chip)
    lat = lax.axis_index("lat")
    lat_even = lax.rem(lat, 2) == 0

    def halos(at):
        first, second = first_ref[at, :].astype(F32), second_ref[at, :].astype(F32)
        top = jnp.where(lat == 0, 0.0, jnp.where(lat_even, second, first))
        bottom = jnp.where(lat == lat_count - 1, 0.0, jnp.where(lat_even, first, second))
        return ((top, 0), (bottom, tall - 1))

    for array, scr in enumerate((x_scr, cot_scr)):
        for member in range(groups):
            slot = array * groups + member
            if member < mem:
                block = both_ref[array, member]
            else:
                block = other_ref[array, member - mem]
            scr[member, cols : cols + cells, :] = block.reshape(cells, channels).astype(F32)
            for halo, place in halos(slice(slot * cols, (slot + 1) * cols)):
                scr[member, place * cols : (place + 1) * cols, :] = halo
            scr[member, centre:, :] = jnp.zeros((per_member - centre, channels), F32)
            for side, side_scr in ((0, low_scr), (1, high_scr)):
                base = centre + 8 * side
                scr[member, base + 1 : base + 1 + rows, :] = side_scr[
                    slot * rows : (slot + 1) * rows, :
                ]
        for side in (0, 1):
            first = 2 * groups * cols + 2 * groups * side + array * groups
            base = centre + 8 * side
            start = 2 * groups * cols
            for edges, place in halos(slice(start, start + 4 * groups)):
                for member in range(groups):
                    at = first - start + member
                    scr[member, base + place : base + place + 1, :] = edges[at : at + 1]

    lane_row = lax.broadcasted_iota(jnp.int32, (channels, channels), 0) // width
    lane_col = lax.broadcasted_iota(jnp.int32, (channels, channels), 1) // width
    same_head = jnp.where(lane_row == lane_col, 1.0, 0.0).astype(BF16)
    gain = gain_ref[...]

    def row_rsqrt(values):
        return lax.rsqrt(jnp.mean(values * values, axis=-1, keepdims=True) + EPSILON)

    x_all = x_scr[...].reshape(groups * per_member, channels)
    normed = (x_all * row_rsqrt(x_all) * gain).astype(BF16)
    proj_scr[...] = dot_nn(normed, project_ref[...]).astype(BF16)

    def head_unit(raw):
        raw = raw.astype(F32)
        mean_sq = head_sums(raw * raw, same_head) * (1.0 / width)
        inverse = lax.rsqrt(jnp.maximum(mean_sq, FLOOR))
        return raw, mean_sq, inverse, (raw * inverse).astype(BF16)

    queries, query_parts, keys, key_parts, values = [], [], [], [], []
    for member in range(groups):
        at = member * per_member
        full = slice(at, at + per_member)
        inner = slice(at + own.start, at + own.stop)
        parts = head_unit(proj_scr[full if member < mem else inner, :channels])
        query_parts.append(parts[:3])
        queries.append(parts[3])
        parts = head_unit(proj_scr[full, channels : 2 * channels])
        key_parts.append(parts[:3])
        keys.append(parts[3])
        values.append(proj_scr[full, 2 * channels :])

    soft, rounded, updated = [], [], []
    for m in range(groups):
        take = slice(None) if m < mem else own
        exps = []
        for n in range(groups):
            product = queries[m] * keys[n][take]
            exps.append(jnp.exp(dot_nn(product, same_head) * scale))
        total = exps[0]
        for n in range(1, groups):
            total = total + exps[n]
        inverse = 1.0 / total
        probs = [e * inverse for e in exps]
        probs_16 = [p.astype(BF16) for p in probs]
        if m < mem:
            mixed = probs_16[0].astype(F32) * values[0].astype(F32)
            for n in range(1, groups):
                mixed = mixed + probs_16[n].astype(F32) * values[n].astype(F32)
            mixed = mixed.astype(BF16)
            updated.append((x_scr[m] + dot_nn(mixed, output_ref[...])).astype(BF16).astype(F32))
            probs = [p[own] for p in probs]
            probs_16 = [p[own] for p in probs_16]
        soft.append(probs)
        rounded.append(probs_16)

    def shifted(scr, member, field):
        column = lax.broadcasted_iota(jnp.int32, (cols, channels), 0)
        for place in range(tall):
            slab = field[place * cols : (place + 1) * cols]
            low = field[centre + place : centre + place + 1]
            high = field[centre + 8 + place : centre + 8 + place + 1]
            back = jnp.where(column == 0, low, pltpu.roll(slab, 1, 0))
            ahead = jnp.where(column == cols - 1, high, pltpu.roll(slab, cols - 1, 0))
            rows_at = slice(place * cols, (place + 1) * cols)
            scr[member, rows_at, :channels] = back.astype(BF16)
            scr[member, rows_at, channels : 2 * channels] = slab.astype(BF16)
            scr[member, rows_at, 2 * channels :] = ahead.astype(BF16)

    for member in range(mem):
        shifted(shift_scr, member, updated[member])
    for member in range(groups):
        shifted(cot_shift_scr, member, cot_scr[member])

    total = jnp.concatenate([u[own] for u in updated], axis=0)
    for r in range(3):
        window = jnp.concatenate(
            [shift_scr[m, r * cols : r * cols + cells, :] for m in range(mem)], axis=0
        )
        total = total + dot_nn(window, conv_ref[3 * channels * r : 3 * channels * (r + 1), :])
    result_ref[...] = total.astype(BF16).reshape(mem, rows, cols, channels)

    total = jnp.concatenate([cot_scr[m, own, :] for m in range(groups)], axis=0)
    for r in range(3):
        for c in range(3):
            lanes = slice((2 - c) * channels, (3 - c) * channels)
            begin = (2 - r) * cols
            window = jnp.concatenate(
                [cot_shift_scr[m, begin : begin + cells, lanes] for m in range(groups)], axis=0
            )
            tap = (3 * r + c) * channels
            total = total + dot_nt(window, conv_ref[tap : tap + channels, :])
    grad_field = total
    grad_mixed = dot_nt(grad_field.astype(BF16), output_ref[...]).astype(BF16)
    grads = [grad_mixed[m * cells : (m + 1) * cells] for m in range(groups)]

    inner_keys = [k[own] for k in keys]
    inner_values = [v[own] for v in values]
    inner_queries = [q[own] if m < mem else q for m, q in enumerate(queries)]
    query_grad = [None] * mem
    key_grad = [None] * mem
    value_grad = [None] * mem
    for m in range(groups):
        dprob = [dot_nn(grads[m] * inner_values[n], same_head) for n in range(groups)]
        mean = soft[m][0] * dprob[0]
        for n in range(1, groups):
            mean = mean + soft[m][n] * dprob[n]
        for n in range(groups):
            if m >= mem and n >= mem:
                continue
            dscore = (soft[m][n] * (dprob[n] - mean)).astype(BF16).astype(F32)
            if m < mem:
                term = dscore * inner_keys[n].astype(F32)
                query_grad[m] = term if query_grad[m] is None else query_grad[m] + term
            if n < mem:
                term = dscore * inner_queries[m].astype(F32)
                key_grad[n] = term if key_grad[n] is None else key_grad[n] + term
                term = rounded[m][n].astype(F32) * grads[m].astype(F32)
                value_grad[n] = term if value_grad[n] is None else value_grad[n] + term

    def head_pull(parts, grad):
        raw, mean_sq, inverse = (p[own] for p in parts)
        grad = grad * scale
        inner = head_sums(grad * raw, same_head) * (1.0 / width)
        active = jnp.where(mean_sq > FLOOR, 1.0, jnp.where(mean_sq == FLOOR, 0.5, 0.0))
        return inverse * grad - active * raw * (inverse * inverse * inverse) * inner

    for m in range(mem):
        grad_proj = jnp.concatenate(
            [
                head_pull(query_parts[m], query_grad[m]).astype(BF16),
                head_pull(key_parts[m], key_grad[m]).astype(BF16),
                value_grad[m].astype(BF16),
            ],
            axis=1,
        )
        grad_normed = dot_nt(grad_proj, project_ref[...]) * gain
        x = x_scr[m, own, :]
        inverse = row_rsqrt(x)
        inner = jnp.mean(x * grad_normed, axis=-1, keepdims=True)
        pulled = inverse * grad_normed - x * (inverse * inverse * inverse * inner)
        total = grad_field[m * cells : (m + 1) * cells] + pulled
        grad_ref[m] = total.astype(BF16).reshape(rows, cols, channels)


def local_call(kernel, out_shape, scratch, name, in_space=None, count=0):
    whole = pl.BlockSpec(memory_space=pltpu.VMEM)

    def keep(shape):
        return pltpu.VMEM(shape.shape, shape.dtype) if in_space else shape

    out_shape = jax.tree.map(keep, out_shape)
    return pl.pallas_call(
        kernel,
        out_shape=out_shape,
        in_specs=[pl.BlockSpec(memory_space=in_space or pltpu.VMEM)] * count,
        out_specs=jax.tree.map(lambda _: whole, out_shape),
        scratch_shapes=scratch,
        compiler_params=pltpu.CompilerParams(vmem_limit_bytes=VMEM_LIMIT),
        name=name,
    )


def per_device_paired(ensemble, norm_gain, project_weight, output_weight, conv_kernel, cotangent):
    mem, rows, cols, channels = ensemble.shape
    groups = 2 * mem
    lon_count = lax.axis_size("lon")
    lat_count = lax.axis_size("lat")
    strip_rows = 2 * groups * rows
    halo_rows = 2 * groups * (cols + 2)

    in_hbm = functools.partial(pltpu.with_memory_space_constraint, memory_space=pltpu.HBM)
    both = local_call(
        stack_kernel,
        jax.ShapeDtypeStruct((2,) + ensemble.shape, BF16),
        [pltpu.SemaphoreType.DMA((2,))],
        "stack",
        pl.ANY,
        2,
    )(in_hbm(ensemble), in_hbm(cotangent))
    other = lax.ppermute(both, "member", [(0, 1), (1, 0)])

    weights = (
        norm_gain.reshape(1, channels),
        project_weight,
        output_weight,
        conv_kernel.reshape(9 * channels, channels),
    )
    weights = local_call(
        load_kernel,
        tuple(jax.ShapeDtypeStruct(w.shape, w.dtype) for w in weights),
        [pltpu.SemaphoreType.DMA((4,))],
        "load_weights",
        pl.ANY,
        4,
    )(*[in_hbm(w) for w in weights])

    strip = jax.ShapeDtypeStruct((strip_rows, channels), BF16)
    strip_scr = pltpu.VMEM((strip_rows, channels), F32)
    core_send, chip_send = local_call(
        pack_strips_kernel, (strip, strip), [strip_scr] * 2, "pack_strips", None, 2
    )(both, other)
    core_pairs = [(i, i ^ 1) for i in range(lon_count)]
    chip_pairs = [(i, (i - 1 if i % 2 == 0 else i + 1) % lon_count) for i in range(lon_count)]
    core_recv = lax.ppermute(core_send, "lon", core_pairs)
    chip_recv = lax.ppermute(chip_send, "lon", chip_pairs)

    halo = jax.ShapeDtypeStruct((halo_rows, channels), BF16)
    first_send, second_send = local_call(
        pack_rows_kernel,
        (halo, halo),
        [strip_scr] * 2 + [pltpu.VMEM((4 * groups, channels), F32)],
        "pack_rows",
        None,
        4,
    )(both, other, core_recv, chip_recv)

    def lat_pairs(offset):
        pairs = []
        for i in range(lat_count):
            partner = i + 1 if i % 2 == offset else i - 1
            pairs.append((i, partner if 0 <= partner < lat_count else i))
        return pairs

    first = lax.ppermute(first_send, "lat", lat_pairs(0))
    second = lax.ppermute(second_send, "lat", lat_pairs(1))

    tall = rows + 2
    per_member = tall * cols + 16
    block = jax.ShapeDtypeStruct(ensemble.shape, BF16)
    return local_call(
        functools.partial(main_kernel, lat_count=lat_count),
        (block, block),
        [
            pltpu.VMEM((groups, per_member, channels), F32),
            pltpu.VMEM((groups, per_member, channels), F32),
            strip_scr,
            strip_scr,
            pltpu.VMEM((groups * per_member, 3 * channels), BF16),
            pltpu.VMEM((mem, tall * cols, 3 * channels), BF16),
            pltpu.VMEM((groups, tall * cols, 3 * channels), BF16),
        ],
        "main",
        None,
        10,
    )(both, other, core_recv, chip_recv, first, second, *weights)


def solution(mesh):
    paired = mesh.shape["member"] == 2 and mesh.shape["lon"] % 2 == 0
    per_device = per_device_paired if paired else per_device_general
    in_specs = (
        P("member", "lat", "lon", None),
        P(),
        P(),
        P(),
        P(),
        P("member", "lat", "lon", None),
    )
    out_specs = (P("member", "lat", "lon", None), P("member", "lat", "lon", None))
    return jax.shard_map(
        per_device, mesh=mesh, in_specs=in_specs, out_specs=out_specs, check_vma=False
    )
```

```python
import functools
import math

import jax
import jax.numpy as jnp
from jax import lax
from jax.experimental import pallas as pl
from jax.experimental.pallas import tpu as pltpu
from jax.sharding import PartitionSpec as P

HEAD_COUNT = 8


FLOOR = 0.5
EPSILON = 1e-06


def padded_2(block, sides, width, periodic):
    for axis, dim in sides:
        count = lax.axis_size(axis)
        forward = [(i, i + 1) for i in range(count - 1)]
        if periodic:
            forward.append((count - 1, 0))
        backward = [(target, source) for source, target in forward]
        low = lax.ppermute(
            lax.slice_in_dim(block, block.shape[dim] - width, None, axis=dim), axis, forward
        )
        high = lax.ppermute(lax.slice_in_dim(block, 0, width, axis=dim), axis, backward)
        block = jnp.concatenate([low, block, high], axis=dim)
    return block


def row_norm(values, gain_vec):
    mean_sq = jnp.mean(values * values, axis=-1, keepdims=True)
    return values * lax.rsqrt(mean_sq + EPSILON) * gain_vec


def head_norm(values, head_count):
    shaped = values.reshape(values.shape[:-1] + (head_count, values.shape[-1] // head_count))
    mean_sq = jnp.mean(shaped * shaped, axis=-1, keepdims=True)
    return (shaped * lax.rsqrt(jnp.maximum(mean_sq, FLOOR))).reshape(values.shape)


def split_heads(values, head_count):
    return values.reshape(values.shape[:-1] + (head_count, values.shape[-1] // head_count))


def head_pullback(raw_rows, grad_rows):
    _, pullback = jax.vjp(lambda t: head_norm(t, HEAD_COUNT), raw_rows.astype(jnp.float32))
    return pullback(grad_rows)[0]


def pad_field(field_in):
    widened = padded_2(field_in, (("lon", 2),), 1, True)
    return padded_2(widened, (("lat", 1),), 1, False)


def conv_taps(padded, kernel, lat_n, lon_n, adjoint):
    running = None
    for row_off in range(3):
        for col_off in range(3):
            if adjoint:
                window = padded[
                    :, 2 - row_off : 2 - row_off + lat_n, 2 - col_off : 2 - col_off + lon_n
                ]
                summand = jnp.einsum(
                    "mabc,dc->mabd",
                    window,
                    kernel[row_off, col_off],
                    preferred_element_type=jnp.float32,
                )
            else:
                window = padded[:, row_off : row_off + lat_n, col_off : col_off + lon_n]
                summand = jnp.einsum(
                    "mabc,cd->mabd",
                    window,
                    kernel[row_off, col_off],
                    preferred_element_type=jnp.float32,
                )
            running = summand if running is None else running + summand
    return running


def per_device_general(ensemble, norm_gain, project_weight, output_weight, conv_kernel, cotangent):
    mem_dev, lat_dev, lon_dev, channels = ensemble.shape
    cell_count = lat_dev * lon_dev
    score_scale = 1.0 / math.sqrt(channels // HEAD_COUNT)
    inputs = ensemble.reshape(mem_dev, cell_count, channels).astype(jnp.float32)
    normed = row_norm(inputs, norm_gain).astype(jnp.bfloat16)
    spread = lax.all_to_all(normed, "member", split_axis=1, concat_axis=0, tiled=True)
    projected = jnp.dot(spread, project_weight, preferred_element_type=jnp.float32).astype(
        jnp.bfloat16
    )
    query_raw = projected[..., :channels]
    key_raw = projected[..., channels : 2 * channels]
    value_rows = projected[..., 2 * channels :]
    key_rows = head_norm(key_raw.astype(jnp.float32), HEAD_COUNT).astype(jnp.bfloat16)
    queries = head_norm(query_raw.astype(jnp.float32), HEAD_COUNT).astype(jnp.bfloat16)
    query_heads = split_heads(queries, HEAD_COUNT)
    key_heads = split_heads(key_rows, HEAD_COUNT)
    value_heads = split_heads(value_rows, HEAD_COUNT)
    scores = (
        jnp.einsum("mphd,nphd->mnhp", query_heads, key_heads, preferred_element_type=jnp.float32)
        * score_scale
    )
    expd = jnp.exp(scores)
    soft = expd / jnp.sum(expd, axis=1, keepdims=True)
    rounded = soft.astype(jnp.bfloat16)
    mixed_out = jnp.einsum(
        "mnhp,nphd->mphd", rounded, value_heads, preferred_element_type=jnp.float32
    )
    mixed_out = mixed_out.reshape(query_raw.shape).astype(jnp.bfloat16)
    mixed_out = lax.all_to_all(mixed_out, "member", split_axis=0, concat_axis=1, tiled=True)
    updated = (
        inputs + jnp.dot(mixed_out, output_weight, preferred_element_type=jnp.float32)
    ).astype(jnp.bfloat16)
    field_up = updated.reshape(mem_dev, lat_dev, lon_dev, channels)
    result = field_up.astype(jnp.float32) + conv_taps(
        pad_field(field_up), conv_kernel, lat_dev, lon_dev, False
    )
    result = result.astype(jnp.bfloat16)
    grad_field = cotangent.astype(jnp.float32) + conv_taps(
        pad_field(cotangent), conv_kernel, lat_dev, lon_dev, True
    )
    grad_rows = grad_field.reshape(mem_dev, cell_count, channels)
    grad_mixed = jnp.einsum(
        "mpc,dc->mpd",
        grad_rows.astype(jnp.bfloat16),
        output_weight,
        preferred_element_type=jnp.float32,
    )
    grad_mixed = grad_mixed.astype(jnp.bfloat16)
    grad_mixed = lax.all_to_all(grad_mixed, "member", split_axis=1, concat_axis=0, tiled=True)
    grad_heads = split_heads(grad_mixed, HEAD_COUNT)
    dprob = jnp.einsum(
        "mphd,nphd->mnhp", grad_heads, value_heads, preferred_element_type=jnp.float32
    )
    dscore = (soft * (dprob - jnp.sum(soft * dprob, axis=1, keepdims=True))).astype(jnp.bfloat16)
    query_grad = (
        jnp.einsum("mnhp,nphd->mphd", dscore, key_heads, preferred_element_type=jnp.float32)
        * score_scale
    )
    query_grad = query_grad.reshape(query_raw.shape)
    key_grad = (
        jnp.einsum("mnhp,mphd->nphd", dscore, query_heads, preferred_element_type=jnp.float32)
        * score_scale
    )
    key_grad = key_grad.reshape(key_raw.shape)
    value_grad = jnp.einsum(
        "mnhp,mphd->nphd", rounded, grad_heads, preferred_element_type=jnp.float32
    )
    value_grad = value_grad.reshape(key_raw.shape)
    grad_query_raw = head_pullback(query_raw, query_grad)
    grad_key_raw = head_pullback(key_raw, key_grad)
    grad_proj = jnp.concatenate([grad_query_raw, grad_key_raw, value_grad], axis=-1).astype(
        jnp.bfloat16
    )
    grad_proj = lax.all_to_all(grad_proj, "member", split_axis=0, concat_axis=1, tiled=True)
    grad_normed = jnp.einsum(
        "mpe,ce->mpc", grad_proj, project_weight, preferred_element_type=jnp.float32
    )
    _, pull_norm = jax.vjp(lambda t: row_norm(t, norm_gain), inputs)
    grad_inputs = pull_norm(grad_normed)[0]
    grad_ensemble = (
        (grad_rows + grad_inputs).astype(jnp.bfloat16).reshape(mem_dev, lat_dev, lon_dev, channels)
    )
    return (result, grad_ensemble)


F32 = jnp.float32
BF16 = jnp.bfloat16
VMEM_LIMIT = 48 * 1024 * 1024


def lon_is_even():
    return lax.rem(lax.axis_index("lon"), 2) == 0


def load_kernel(*refs):
    count = len(refs) // 2
    sems = refs[-1]
    copies = [
        pltpu.make_async_copy(refs[i], refs[count + i], sems.at[i]) for i in range(count)
    ]
    for copy in copies:
        copy.start()
    for copy in copies:
        copy.wait()


def stack_kernel(ens_ref, cot_ref, both_ref, sems):
    copies = [
        pltpu.make_async_copy(ref, both_ref.at[i], sems.at[i])
        for i, ref in enumerate((ens_ref, cot_ref))
    ]
    for copy in copies:
        copy.start()
    for copy in copies:
        copy.wait()


def pack_strips_kernel(both_ref, other_ref, core_ref, chip_ref, low_scr, high_scr):
    _, mem, rows, cols, _ = both_ref.shape
    other_ref = other_ref.at[1 - lax.axis_index("member")]
    index = 0
    for array in range(2):
        for member in range(2 * mem):
            for row in range(rows):
                if member < mem:
                    slab = both_ref[array, member, row]
                else:
                    slab = other_ref[array, member - mem, row]
                slab = slab.astype(F32)
                low_scr[index : index + 1, :] = slab[0:1]
                high_scr[index : index + 1, :] = slab[cols - 1 : cols]
                index += 1
    even = lon_is_even()
    low, high = low_scr[...], high_scr[...]
    core_ref[...] = jnp.where(even, high, low).astype(BF16)
    chip_ref[...] = jnp.where(even, low, high).astype(BF16)


def pack_rows_kernel(
    both_ref, other_ref, core_ref, chip_ref, first_ref, second_ref, low_scr, high_scr, edge_scr
):
    _, mem, rows, cols, _ = both_ref.shape
    other_ref = other_ref.at[1 - lax.axis_index("member")]
    groups = 2 * mem
    even = lon_is_even()
    core, chip = core_ref[...].astype(F32), chip_ref[...].astype(F32)
    low_scr[...] = jnp.where(even, chip, core)
    high_scr[...] = jnp.where(even, core, chip)
    lat_even = lax.rem(lax.axis_index("lat"), 2) == 0
    for out_ref, first in ((first_ref, True), (second_ref, False)):
        row = jnp.where(lat_even, rows - 1, 0) if first else jnp.where(lat_even, 0, rows - 1)
        for array in range(2):
            for member in range(groups):
                slot = array * groups + member
                if member < mem:
                    slab = both_ref[array, member, row]
                else:
                    slab = other_ref[array, member - mem, row]
                out_ref[slot * cols : (slot + 1) * cols, :] = slab
                source = slot * rows + row
                edge_scr[slot : slot + 1, :] = low_scr[pl.ds(source, 1), :]
                edge_scr[2 * groups + slot : 2 * groups + slot + 1, :] = high_scr[
                    pl.ds(source, 1), :
                ]
        out_ref[2 * groups * cols :, :] = edge_scr[...].astype(BF16)


def dot_nn(a, b):
    return lax.dot_general(a, b, (((1,), (0,)), ((), ())), preferred_element_type=F32)


def dot_nt(a, b):
    return lax.dot_general(a, b, (((1,), (1,)), ((), ())), preferred_element_type=F32)


def head_sums(values, same_head):
    high = values.astype(BF16)
    low = (values - high.astype(F32)).astype(BF16)
    return dot_nn(high, same_head) + dot_nn(low, same_head)


def main_kernel(
    both_ref,
    other_ref,
    core_ref,
    chip_ref,
    first_ref,
    second_ref,
    gain_ref,
    project_ref,
    output_ref,
    conv_ref,
    result_ref,
    grad_ref,
    x_scr,
    cot_scr,
    low_scr,
    high_scr,
    proj_scr,
    shift_scr,
    cot_shift_scr,
    *,
    lat_count,
):
    _, mem, rows, cols, channels = both_ref.shape
    other_ref = other_ref.at[1 - lax.axis_index("member")]
    groups = 2 * mem
    tall = rows + 2
    centre = tall * cols
    per_member = x_scr.shape[1]
    own = slice(cols, cols + rows * cols)
    cells = rows * cols
    width = channels // HEAD_COUNT
    scale = 1.0 / math.sqrt(width)
    even = lon_is_even()

    core, chip = core_ref[...].astype(F32), chip_ref[...].astype(F32)
    low_scr[...] = jnp.where(even, chip, core)
    high_scr[...] = jnp.where(even, core, chip)
    lat = lax.axis_index("lat")
    lat_even = lax.rem(lat, 2) == 0

    def halos(at):
        first, second = first_ref[at, :].astype(F32), second_ref[at, :].astype(F32)
        top = jnp.where(lat == 0, 0.0, jnp.where(lat_even, second, first))
        bottom = jnp.where(lat == lat_count - 1, 0.0, jnp.where(lat_even, first, second))
        return ((top, 0), (bottom, tall - 1))

    for array, scr in enumerate((x_scr, cot_scr)):
        for member in range(groups):
            slot = array * groups + member
            if member < mem:
                block = both_ref[array, member]
            else:
                block = other_ref[array, member - mem]
            scr[member, cols : cols + cells, :] = block.reshape(cells, channels).astype(F32)
            for halo, place in halos(slice(slot * cols, (slot + 1) * cols)):
                scr[member, place * cols : (place + 1) * cols, :] = halo
            scr[member, centre:, :] = jnp.zeros((per_member - centre, channels), F32)
            for side, side_scr in ((0, low_scr), (1, high_scr)):
                base = centre + 8 * side
                scr[member, base + 1 : base + 1 + rows, :] = side_scr[
                    slot * rows : (slot + 1) * rows, :
                ]
        for side in (0, 1):
            first = 2 * groups * cols + 2 * groups * side + array * groups
            base = centre + 8 * side
            start = 2 * groups * cols
            for edges, place in halos(slice(start, start + 4 * groups)):
                for member in range(groups):
                    at = first - start + member
                    scr[member, base + place : base + place + 1, :] = edges[at : at + 1]

    lane_row = lax.broadcasted_iota(jnp.int32, (channels, channels), 0) // width
    lane_col = lax.broadcasted_iota(jnp.int32, (channels, channels), 1) // width
    same_head = jnp.where(lane_row == lane_col, 1.0, 0.0).astype(BF16)
    gain = gain_ref[...]

    def row_rsqrt(values):
        return lax.rsqrt(jnp.mean(values * values, axis=-1, keepdims=True) + EPSILON)

    x_all = x_scr[...].reshape(groups * per_member, channels)
    normed = (x_all * row_rsqrt(x_all) * gain).astype(BF16)
    proj_scr[...] = dot_nn(normed, project_ref[...]).astype(BF16)

    def head_unit(raw):
        raw = raw.astype(F32)
        mean_sq = head_sums(raw * raw, same_head) * (1.0 / width)
        inverse = lax.rsqrt(jnp.maximum(mean_sq, FLOOR))
        return raw, mean_sq, inverse, (raw * inverse).astype(BF16)

    queries, query_parts, keys, key_parts, values = [], [], [], [], []
    for member in range(groups):
        at = member * per_member
        full = slice(at, at + per_member)
        inner = slice(at + own.start, at + own.stop)
        parts = head_unit(proj_scr[full if member < mem else inner, :channels])
        query_parts.append(parts[:3])
        queries.append(parts[3])
        parts = head_unit(proj_scr[full, channels : 2 * channels])
        key_parts.append(parts[:3])
        keys.append(parts[3])
        values.append(proj_scr[full, 2 * channels :])

    soft, rounded, updated = [], [], []
    for m in range(groups):
        take = slice(None) if m < mem else own
        exps = []
        for n in range(groups):
            product = queries[m] * keys[n][take]
            exps.append(jnp.exp(dot_nn(product, same_head) * scale))
        total = exps[0]
        for n in range(1, groups):
            total = total + exps[n]
        inverse = 1.0 / total
        probs = [e * inverse for e in exps]
        probs_16 = [p.astype(BF16) for p in probs]
        if m < mem:
            mixed = probs_16[0].astype(F32) * values[0].astype(F32)
            for n in range(1, groups):
                mixed = mixed + probs_16[n].astype(F32) * values[n].astype(F32)
            mixed = mixed.astype(BF16)
            updated.append((x_scr[m] + dot_nn(mixed, output_ref[...])).astype(BF16).astype(F32))
            probs = [p[own] for p in probs]
            probs_16 = [p[own] for p in probs_16]
        soft.append(probs)
        rounded.append(probs_16)

    def shifted(scr, member, field):
        column = lax.broadcasted_iota(jnp.int32, (cols, channels), 0)
        for place in range(tall):
            slab = field[place * cols : (place + 1) * cols]
            low = field[centre + place : centre + place + 1]
            high = field[centre + 8 + place : centre + 8 + place + 1]
            back = jnp.where(column == 0, low, pltpu.roll(slab, 1, 0))
            ahead = jnp.where(column == cols - 1, high, pltpu.roll(slab, cols - 1, 0))
            rows_at = slice(place * cols, (place + 1) * cols)
            scr[member, rows_at, :channels] = back.astype(BF16)
            scr[member, rows_at, channels : 2 * channels] = slab.astype(BF16)
            scr[member, rows_at, 2 * channels :] = ahead.astype(BF16)

    for member in range(mem):
        shifted(shift_scr, member, updated[member])
    for member in range(groups):
        shifted(cot_shift_scr, member, cot_scr[member])

    total = jnp.concatenate([u[own] for u in updated], axis=0)
    for r in range(3):
        window = jnp.concatenate(
            [shift_scr[m, r * cols : r * cols + cells, :] for m in range(mem)], axis=0
        )
        total = total + dot_nn(window, conv_ref[3 * channels * r : 3 * channels * (r + 1), :])
    result_ref[...] = total.astype(BF16).reshape(mem, rows, cols, channels)

    total = jnp.concatenate([cot_scr[m, own, :] for m in range(groups)], axis=0)
    for r in range(3):
        for c in range(3):
            lanes = slice((2 - c) * channels, (3 - c) * channels)
            begin = (2 - r) * cols
            window = jnp.concatenate(
                [cot_shift_scr[m, begin : begin + cells, lanes] for m in range(groups)], axis=0
            )
            tap = (3 * r + c) * channels
            total = total + dot_nt(window, conv_ref[tap : tap + channels, :])
    grad_field = total
    grad_mixed = dot_nt(grad_field.astype(BF16), output_ref[...]).astype(BF16)
    grads = [grad_mixed[m * cells : (m + 1) * cells] for m in range(groups)]

    inner_keys = [k[own] for k in keys]
    inner_values = [v[own] for v in values]
    inner_queries = [q[own] if m < mem else q for m, q in enumerate(queries)]
    query_grad = [None] * mem
    key_grad = [None] * mem
    value_grad = [None] * mem
    for m in range(groups):
        dprob = [dot_nn(grads[m] * inner_values[n], same_head) for n in range(groups)]
        mean = soft[m][0] * dprob[0]
        for n in range(1, groups):
            mean = mean + soft[m][n] * dprob[n]
        for n in range(groups):
            if m >= mem and n >= mem:
                continue
            dscore = (soft[m][n] * (dprob[n] - mean)).astype(BF16).astype(F32)
            if m < mem:
                term = dscore * inner_keys[n].astype(F32)
                query_grad[m] = term if query_grad[m] is None else query_grad[m] + term
            if n < mem:
                term = dscore * inner_queries[m].astype(F32)
                key_grad[n] = term if key_grad[n] is None else key_grad[n] + term
                term = rounded[m][n].astype(F32) * grads[m].astype(F32)
                value_grad[n] = term if value_grad[n] is None else value_grad[n] + term

    def head_pull(parts, grad):
        raw, mean_sq, inverse = (p[own] for p in parts)
        grad = grad * scale
        inner = head_sums(grad * raw, same_head) * (1.0 / width)
        active = jnp.where(mean_sq > FLOOR, 1.0, jnp.where(mean_sq == FLOOR, 0.5, 0.0))
        return inverse * grad - active * raw * (inverse * inverse * inverse) * inner

    for m in range(mem):
        grad_proj = jnp.concatenate(
            [
                head_pull(query_parts[m], query_grad[m]).astype(BF16),
                head_pull(key_parts[m], key_grad[m]).astype(BF16),
                value_grad[m].astype(BF16),
            ],
            axis=1,
        )
        grad_normed = dot_nt(grad_proj, project_ref[...]) * gain
        x = x_scr[m, own, :]
        inverse = row_rsqrt(x)
        inner = jnp.mean(x * grad_normed, axis=-1, keepdims=True)
        pulled = inverse * grad_normed - x * (inverse * inverse * inverse * inner)
        total = grad_field[m * cells : (m + 1) * cells] + pulled
        grad_ref[m] = total.astype(BF16).reshape(rows, cols, channels)


def local_call(kernel, out_shape, scratch, name, in_space=None, count=0):
    whole = pl.BlockSpec(memory_space=pltpu.VMEM)

    def keep(shape):
        return pltpu.VMEM(shape.shape, shape.dtype) if in_space else shape

    out_shape = jax.tree.map(keep, out_shape)
    return pl.pallas_call(
        kernel,
        out_shape=out_shape,
        in_specs=[pl.BlockSpec(memory_space=in_space or pltpu.VMEM)] * count,
        out_specs=jax.tree.map(lambda _: whole, out_shape),
        scratch_shapes=scratch,
        compiler_params=pltpu.CompilerParams(vmem_limit_bytes=VMEM_LIMIT),
        name=name,
    )


def per_device_paired(ensemble, norm_gain, project_weight, output_weight, conv_kernel, cotangent):
    mem, rows, cols, channels = ensemble.shape
    groups = 2 * mem
    lon_count = lax.axis_size("lon")
    lat_count = lax.axis_size("lat")
    strip_rows = 2 * groups * rows
    halo_rows = 2 * groups * (cols + 2)

    in_hbm = functools.partial(pltpu.with_memory_space_constraint, memory_space=pltpu.HBM)
    both = local_call(
        stack_kernel,
        jax.ShapeDtypeStruct((2,) + ensemble.shape, BF16),
        [pltpu.SemaphoreType.DMA((2,))],
        "stack",
        pl.ANY,
        2,
    )(in_hbm(ensemble), in_hbm(cotangent))
    other = lax.all_gather(both, "member")

    weights = (
        norm_gain.reshape(1, channels),
        project_weight,
        output_weight,
        conv_kernel.reshape(9 * channels, channels),
    )
    weights = local_call(
        load_kernel,
        tuple(jax.ShapeDtypeStruct(w.shape, w.dtype) for w in weights),
        [pltpu.SemaphoreType.DMA((4,))],
        "load_weights",
        pl.ANY,
        4,
    )(*[in_hbm(w) for w in weights])

    strip = jax.ShapeDtypeStruct((strip_rows, channels), BF16)
    strip_scr = pltpu.VMEM((strip_rows, channels), F32)
    core_send, chip_send = local_call(
        pack_strips_kernel, (strip, strip), [strip_scr] * 2, "pack_strips", None, 2
    )(both, other)
    core_pairs = [(i, i ^ 1) for i in range(lon_count)]
    chip_pairs = [(i, (i - 1 if i % 2 == 0 else i + 1) % lon_count) for i in range(lon_count)]
    core_recv = lax.ppermute(core_send, "lon", core_pairs)
    chip_recv = lax.ppermute(chip_send, "lon", chip_pairs)

    halo = jax.ShapeDtypeStruct((halo_rows, channels), BF16)
    first_send, second_send = local_call(
        pack_rows_kernel,
        (halo, halo),
        [strip_scr] * 2 + [pltpu.VMEM((4 * groups, channels), F32)],
        "pack_rows",
        None,
        4,
    )(both, other, core_recv, chip_recv)

    def lat_pairs(offset):
        pairs = []
        for i in range(lat_count):
            partner = i + 1 if i % 2 == offset else i - 1
            pairs.append((i, partner if 0 <= partner < lat_count else i))
        return pairs

    first = lax.ppermute(first_send, "lat", lat_pairs(0))
    second = lax.ppermute(second_send, "lat", lat_pairs(1))

    tall = rows + 2
    per_member = tall * cols + 16
    block = jax.ShapeDtypeStruct(ensemble.shape, BF16)
    return local_call(
        functools.partial(main_kernel, lat_count=lat_count),
        (block, block),
        [
            pltpu.VMEM((groups, per_member, channels), F32),
            pltpu.VMEM((groups, per_member, channels), F32),
            strip_scr,
            strip_scr,
            pltpu.VMEM((groups * per_member, 3 * channels), BF16),
            pltpu.VMEM((mem, tall * cols, 3 * channels), BF16),
            pltpu.VMEM((groups, tall * cols, 3 * channels), BF16),
        ],
        "main",
        None,
        10,
    )(both, other, core_recv, chip_recv, first, second, *weights)


def solution(mesh):
    paired = mesh.shape["member"] == 2 and mesh.shape["lon"] % 2 == 0
    per_device = per_device_paired if paired else per_device_general
    in_specs = (
        P("member", "lat", "lon", None),
        P(),
        P(),
        P(),
        P(),
        P("member", "lat", "lon", None),
    )
    out_specs = (P("member", "lat", "lon", None), P("member", "lat", "lon", None))
    return jax.shard_map(
        per_device, mesh=mesh, in_specs=in_specs, out_specs=out_specs, check_vma=False
    )
```

```python
import functools
import math

import jax
import jax.numpy as jnp
from jax import lax
from jax.experimental import pallas as pl
from jax.experimental.pallas import tpu as pltpu
from jax.sharding import PartitionSpec as P

HEAD_COUNT = 8


FLOOR = 0.5
EPSILON = 1e-06


def padded_2(block, sides, width, periodic):
    for axis, dim in sides:
        count = lax.axis_size(axis)
        forward = [(i, i + 1) for i in range(count - 1)]
        if periodic:
            forward.append((count - 1, 0))
        backward = [(target, source) for source, target in forward]
        low = lax.ppermute(
            lax.slice_in_dim(block, block.shape[dim] - width, None, axis=dim), axis, forward
        )
        high = lax.ppermute(lax.slice_in_dim(block, 0, width, axis=dim), axis, backward)
        block = jnp.concatenate([low, block, high], axis=dim)
    return block


def row_norm(values, gain_vec):
    mean_sq = jnp.mean(values * values, axis=-1, keepdims=True)
    return values * lax.rsqrt(mean_sq + EPSILON) * gain_vec


def head_norm(values, head_count):
    shaped = values.reshape(values.shape[:-1] + (head_count, values.shape[-1] // head_count))
    mean_sq = jnp.mean(shaped * shaped, axis=-1, keepdims=True)
    return (shaped * lax.rsqrt(jnp.maximum(mean_sq, FLOOR))).reshape(values.shape)


def split_heads(values, head_count):
    return values.reshape(values.shape[:-1] + (head_count, values.shape[-1] // head_count))


def head_pullback(raw_rows, grad_rows):
    _, pullback = jax.vjp(lambda t: head_norm(t, HEAD_COUNT), raw_rows.astype(jnp.float32))
    return pullback(grad_rows)[0]


def pad_field(field_in):
    widened = padded_2(field_in, (("lon", 2),), 1, True)
    return padded_2(widened, (("lat", 1),), 1, False)


def conv_taps(padded, kernel, lat_n, lon_n, adjoint):
    running = None
    for row_off in range(3):
        for col_off in range(3):
            if adjoint:
                window = padded[
                    :, 2 - row_off : 2 - row_off + lat_n, 2 - col_off : 2 - col_off + lon_n
                ]
                summand = jnp.einsum(
                    "mabc,dc->mabd",
                    window,
                    kernel[row_off, col_off],
                    preferred_element_type=jnp.float32,
                )
            else:
                window = padded[:, row_off : row_off + lat_n, col_off : col_off + lon_n]
                summand = jnp.einsum(
                    "mabc,cd->mabd",
                    window,
                    kernel[row_off, col_off],
                    preferred_element_type=jnp.float32,
                )
            running = summand if running is None else running + summand
    return running


def per_device_general(ensemble, norm_gain, project_weight, output_weight, conv_kernel, cotangent):
    mem_dev, lat_dev, lon_dev, channels = ensemble.shape
    cell_count = lat_dev * lon_dev
    score_scale = 1.0 / math.sqrt(channels // HEAD_COUNT)
    inputs = ensemble.reshape(mem_dev, cell_count, channels).astype(jnp.float32)
    normed = row_norm(inputs, norm_gain).astype(jnp.bfloat16)
    spread = lax.all_to_all(normed, "member", split_axis=1, concat_axis=0, tiled=True)
    projected = jnp.dot(spread, project_weight, preferred_element_type=jnp.float32).astype(
        jnp.bfloat16
    )
    query_raw = projected[..., :channels]
    key_raw = projected[..., channels : 2 * channels]
    value_rows = projected[..., 2 * channels :]
    key_rows = head_norm(key_raw.astype(jnp.float32), HEAD_COUNT).astype(jnp.bfloat16)
    queries = head_norm(query_raw.astype(jnp.float32), HEAD_COUNT).astype(jnp.bfloat16)
    query_heads = split_heads(queries, HEAD_COUNT)
    key_heads = split_heads(key_rows, HEAD_COUNT)
    value_heads = split_heads(value_rows, HEAD_COUNT)
    scores = (
        jnp.einsum("mphd,nphd->mnhp", query_heads, key_heads, preferred_element_type=jnp.float32)
        * score_scale
    )
    expd = jnp.exp(scores)
    soft = expd / jnp.sum(expd, axis=1, keepdims=True)
    rounded = soft.astype(jnp.bfloat16)
    mixed_out = jnp.einsum(
        "mnhp,nphd->mphd", rounded, value_heads, preferred_element_type=jnp.float32
    )
    mixed_out = mixed_out.reshape(query_raw.shape).astype(jnp.bfloat16)
    mixed_out = lax.all_to_all(mixed_out, "member", split_axis=0, concat_axis=1, tiled=True)
    updated = (
        inputs + jnp.dot(mixed_out, output_weight, preferred_element_type=jnp.float32)
    ).astype(jnp.bfloat16)
    field_up = updated.reshape(mem_dev, lat_dev, lon_dev, channels)
    result = field_up.astype(jnp.float32) + conv_taps(
        pad_field(field_up), conv_kernel, lat_dev, lon_dev, False
    )
    result = result.astype(jnp.bfloat16)
    grad_field = cotangent.astype(jnp.float32) + conv_taps(
        pad_field(cotangent), conv_kernel, lat_dev, lon_dev, True
    )
    grad_rows = grad_field.reshape(mem_dev, cell_count, channels)
    grad_mixed = jnp.einsum(
        "mpc,dc->mpd",
        grad_rows.astype(jnp.bfloat16),
        output_weight,
        preferred_element_type=jnp.float32,
    )
    grad_mixed = grad_mixed.astype(jnp.bfloat16)
    grad_mixed = lax.all_to_all(grad_mixed, "member", split_axis=1, concat_axis=0, tiled=True)
    grad_heads = split_heads(grad_mixed, HEAD_COUNT)
    dprob = jnp.einsum(
        "mphd,nphd->mnhp", grad_heads, value_heads, preferred_element_type=jnp.float32
    )
    dscore = (soft * (dprob - jnp.sum(soft * dprob, axis=1, keepdims=True))).astype(jnp.bfloat16)
    query_grad = (
        jnp.einsum("mnhp,nphd->mphd", dscore, key_heads, preferred_element_type=jnp.float32)
        * score_scale
    )
    query_grad = query_grad.reshape(query_raw.shape)
    key_grad = (
        jnp.einsum("mnhp,mphd->nphd", dscore, query_heads, preferred_element_type=jnp.float32)
        * score_scale
    )
    key_grad = key_grad.reshape(key_raw.shape)
    value_grad = jnp.einsum(
        "mnhp,mphd->nphd", rounded, grad_heads, preferred_element_type=jnp.float32
    )
    value_grad = value_grad.reshape(key_raw.shape)
    grad_query_raw = head_pullback(query_raw, query_grad)
    grad_key_raw = head_pullback(key_raw, key_grad)
    grad_proj = jnp.concatenate([grad_query_raw, grad_key_raw, value_grad], axis=-1).astype(
        jnp.bfloat16
    )
    grad_proj = lax.all_to_all(grad_proj, "member", split_axis=0, concat_axis=1, tiled=True)
    grad_normed = jnp.einsum(
        "mpe,ce->mpc", grad_proj, project_weight, preferred_element_type=jnp.float32
    )
    _, pull_norm = jax.vjp(lambda t: row_norm(t, norm_gain), inputs)
    grad_inputs = pull_norm(grad_normed)[0]
    grad_ensemble = (
        (grad_rows + grad_inputs).astype(jnp.bfloat16).reshape(mem_dev, lat_dev, lon_dev, channels)
    )
    return (result, grad_ensemble)


F32 = jnp.float32
BF16 = jnp.bfloat16
VMEM_LIMIT = 48 * 1024 * 1024


def load_kernel(*refs):
    count = len(refs) // 2
    sems = refs[-1]
    copies = [
        pltpu.make_async_copy(refs[i], refs[count + i], sems.at[i]) for i in range(count)
    ]
    for copy in copies:
        copy.start()
    for copy in copies:
        copy.wait()


def stack_kernel(ens_ref, cot_ref, both_ref, strips_ref, low_scr, high_scr, sems):
    _, mem, rows, cols, _ = both_ref.shape
    copies = [
        pltpu.make_async_copy(ref, both_ref.at[i], sems.at[i])
        for i, ref in enumerate((ens_ref, cot_ref))
    ]
    for copy in copies:
        copy.start()
    for copy in copies:
        copy.wait()
    index = 0
    for array in range(2):
        for member in range(mem):
            for row in range(rows):
                slab = both_ref[array, member, row].astype(F32)
                low_scr[index : index + 1, :] = slab[0:1]
                high_scr[index : index + 1, :] = slab[cols - 1 : cols]
                index += 1
    strips_ref[0] = low_scr[...].astype(BF16)
    strips_ref[1] = high_scr[...].astype(BF16)


def rim_strips(strips_ref, mem, rows, low_scr, high_scr):
    lon, lon_count = lax.axis_index("lon"), strips_ref.shape[1]
    me = lax.axis_index("member")
    west = lax.rem(lon + lon_count - 1, lon_count)
    east = lax.rem(lon + 1, lon_count)
    part = mem * rows
    for scr, at, side in ((low_scr, west, 1), (high_scr, east, 0)):
        for group, who in enumerate((me, 1 - me)):
            block = strips_ref[who, at, side].astype(F32)
            for array in range(2):
                start = (2 * array + group) * part
                scr[start : start + part, :] = block[array * part : (array + 1) * part]


def pack_rows_kernel(
    both_ref, other_ref, strips_ref, first_ref, second_ref, low_scr, high_scr, edge_scr
):
    _, mem, rows, cols, _ = both_ref.shape
    other_ref = other_ref.at[1 - lax.axis_index("member")]
    groups = 2 * mem
    rim_strips(strips_ref, mem, rows, low_scr, high_scr)
    lat_even = lax.rem(lax.axis_index("lat"), 2) == 0
    for out_ref, first in ((first_ref, True), (second_ref, False)):
        row = jnp.where(lat_even, rows - 1, 0) if first else jnp.where(lat_even, 0, rows - 1)
        for array in range(2):
            for member in range(groups):
                slot = array * groups + member
                if member < mem:
                    slab = both_ref[array, member, row]
                else:
                    slab = other_ref[array, member - mem, row]
                out_ref[slot * cols : (slot + 1) * cols, :] = slab
                source = slot * rows + row
                edge_scr[slot : slot + 1, :] = low_scr[pl.ds(source, 1), :]
                edge_scr[2 * groups + slot : 2 * groups + slot + 1, :] = high_scr[
                    pl.ds(source, 1), :
                ]
        out_ref[2 * groups * cols :, :] = edge_scr[...].astype(BF16)


def dot_nn(a, b):
    return lax.dot_general(a, b, (((1,), (0,)), ((), ())), preferred_element_type=F32)


def dot_nt(a, b):
    return lax.dot_general(a, b, (((1,), (1,)), ((), ())), preferred_element_type=F32)


def head_sums(values, same_head):
    high = values.astype(BF16)
    low = (values - high.astype(F32)).astype(BF16)
    return dot_nn(high, same_head) + dot_nn(low, same_head)


def main_kernel(
    both_ref,
    other_ref,
    strips_ref,
    first_ref,
    second_ref,
    gain_ref,
    project_ref,
    output_ref,
    conv_ref,
    result_ref,
    grad_ref,
    x_scr,
    cot_scr,
    low_scr,
    high_scr,
    proj_scr,
    shift_scr,
    cot_shift_scr,
    *,
    lat_count,
):
    _, mem, rows, cols, channels = both_ref.shape
    other_ref = other_ref.at[1 - lax.axis_index("member")]
    groups = 2 * mem
    tall = rows + 2
    centre = tall * cols
    per_member = x_scr.shape[1]
    own = slice(cols, cols + rows * cols)
    cells = rows * cols
    width = channels // HEAD_COUNT
    scale = 1.0 / math.sqrt(width)

    rim_strips(strips_ref, mem, rows, low_scr, high_scr)
    lat = lax.axis_index("lat")
    lat_even = lax.rem(lat, 2) == 0

    def halos(at):
        first, second = first_ref[at, :].astype(F32), second_ref[at, :].astype(F32)
        top = jnp.where(lat == 0, 0.0, jnp.where(lat_even, second, first))
        bottom = jnp.where(lat == lat_count - 1, 0.0, jnp.where(lat_even, first, second))
        return ((top, 0), (bottom, tall - 1))

    for array, scr in enumerate((x_scr, cot_scr)):
        for member in range(groups):
            slot = array * groups + member
            if member < mem:
                block = both_ref[array, member]
            else:
                block = other_ref[array, member - mem]
            scr[member, cols : cols + cells, :] = block.reshape(cells, channels).astype(F32)
            for halo, place in halos(slice(slot * cols, (slot + 1) * cols)):
                scr[member, place * cols : (place + 1) * cols, :] = halo
            scr[member, centre:, :] = jnp.zeros((per_member - centre, channels), F32)
            for side, side_scr in ((0, low_scr), (1, high_scr)):
                base = centre + 8 * side
                scr[member, base + 1 : base + 1 + rows, :] = side_scr[
                    slot * rows : (slot + 1) * rows, :
                ]
        for side in (0, 1):
            first = 2 * groups * cols + 2 * groups * side + array * groups
            base = centre + 8 * side
            start = 2 * groups * cols
            for edges, place in halos(slice(start, start + 4 * groups)):
                for member in range(groups):
                    at = first - start + member
                    scr[member, base + place : base + place + 1, :] = edges[at : at + 1]

    lane_row = lax.broadcasted_iota(jnp.int32, (channels, channels), 0) // width
    lane_col = lax.broadcasted_iota(jnp.int32, (channels, channels), 1) // width
    same_head = jnp.where(lane_row == lane_col, 1.0, 0.0).astype(BF16)
    gain = gain_ref[...]

    def row_rsqrt(values):
        return lax.rsqrt(jnp.mean(values * values, axis=-1, keepdims=True) + EPSILON)

    x_all = x_scr[...].reshape(groups * per_member, channels)
    normed = (x_all * row_rsqrt(x_all) * gain).astype(BF16)
    proj_scr[...] = dot_nn(normed, project_ref[...]).astype(BF16)

    def head_unit(raw):
        raw = raw.astype(F32)
        mean_sq = head_sums(raw * raw, same_head) * (1.0 / width)
        inverse = lax.rsqrt(jnp.maximum(mean_sq, FLOOR))
        return raw, mean_sq, inverse, (raw * inverse).astype(BF16)

    queries, query_parts, keys, key_parts, values = [], [], [], [], []
    for member in range(groups):
        at = member * per_member
        full = slice(at, at + per_member)
        inner = slice(at + own.start, at + own.stop)
        parts = head_unit(proj_scr[full if member < mem else inner, :channels])
        query_parts.append(parts[:3])
        queries.append(parts[3])
        parts = head_unit(proj_scr[full, channels : 2 * channels])
        key_parts.append(parts[:3])
        keys.append(parts[3])
        values.append(proj_scr[full, 2 * channels :])

    soft, rounded, updated = [], [], []
    for m in range(groups):
        take = slice(None) if m < mem else own
        exps = []
        for n in range(groups):
            product = queries[m] * keys[n][take]
            exps.append(jnp.exp(dot_nn(product, same_head) * scale))
        total = exps[0]
        for n in range(1, groups):
            total = total + exps[n]
        inverse = 1.0 / total
        probs = [e * inverse for e in exps]
        probs_16 = [p.astype(BF16) for p in probs]
        if m < mem:
            mixed = probs_16[0].astype(F32) * values[0].astype(F32)
            for n in range(1, groups):
                mixed = mixed + probs_16[n].astype(F32) * values[n].astype(F32)
            mixed = mixed.astype(BF16)
            updated.append((x_scr[m] + dot_nn(mixed, output_ref[...])).astype(BF16).astype(F32))
            probs = [p[own] for p in probs]
            probs_16 = [p[own] for p in probs_16]
        soft.append(probs)
        rounded.append(probs_16)

    def shifted(scr, member, field):
        column = lax.broadcasted_iota(jnp.int32, (cols, channels), 0)
        for place in range(tall):
            slab = field[place * cols : (place + 1) * cols]
            low = field[centre + place : centre + place + 1]
            high = field[centre + 8 + place : centre + 8 + place + 1]
            back = jnp.where(column == 0, low, pltpu.roll(slab, 1, 0))
            ahead = jnp.where(column == cols - 1, high, pltpu.roll(slab, cols - 1, 0))
            rows_at = slice(place * cols, (place + 1) * cols)
            scr[member, rows_at, :channels] = back.astype(BF16)
            scr[member, rows_at, channels : 2 * channels] = slab.astype(BF16)
            scr[member, rows_at, 2 * channels :] = ahead.astype(BF16)

    for member in range(mem):
        shifted(shift_scr, member, updated[member])
    for member in range(groups):
        shifted(cot_shift_scr, member, cot_scr[member])

    total = jnp.concatenate([u[own] for u in updated], axis=0)
    for r in range(3):
        window = jnp.concatenate(
            [shift_scr[m, r * cols : r * cols + cells, :] for m in range(mem)], axis=0
        )
        total = total + dot_nn(window, conv_ref[3 * channels * r : 3 * channels * (r + 1), :])
    result_ref[...] = total.astype(BF16).reshape(mem, rows, cols, channels)

    total = jnp.concatenate([cot_scr[m, own, :] for m in range(groups)], axis=0)
    for r in range(3):
        for c in range(3):
            lanes = slice((2 - c) * channels, (3 - c) * channels)
            begin = (2 - r) * cols
            window = jnp.concatenate(
                [cot_shift_scr[m, begin : begin + cells, lanes] for m in range(groups)], axis=0
            )
            tap = (3 * r + c) * channels
            total = total + dot_nt(window, conv_ref[tap : tap + channels, :])
    grad_field = total
    grad_mixed = dot_nt(grad_field.astype(BF16), output_ref[...]).astype(BF16)
    grads = [grad_mixed[m * cells : (m + 1) * cells] for m in range(groups)]

    inner_keys = [k[own] for k in keys]
    inner_values = [v[own] for v in values]
    inner_queries = [q[own] if m < mem else q for m, q in enumerate(queries)]
    query_grad = [None] * mem
    key_grad = [None] * mem
    value_grad = [None] * mem
    for m in range(groups):
        dprob = [dot_nn(grads[m] * inner_values[n], same_head) for n in range(groups)]
        mean = soft[m][0] * dprob[0]
        for n in range(1, groups):
            mean = mean + soft[m][n] * dprob[n]
        for n in range(groups):
            if m >= mem and n >= mem:
                continue
            dscore = (soft[m][n] * (dprob[n] - mean)).astype(BF16).astype(F32)
            if m < mem:
                term = dscore * inner_keys[n].astype(F32)
                query_grad[m] = term if query_grad[m] is None else query_grad[m] + term
            if n < mem:
                term = dscore * inner_queries[m].astype(F32)
                key_grad[n] = term if key_grad[n] is None else key_grad[n] + term
                term = rounded[m][n].astype(F32) * grads[m].astype(F32)
                value_grad[n] = term if value_grad[n] is None else value_grad[n] + term

    def head_pull(parts, grad):
        raw, mean_sq, inverse = (p[own] for p in parts)
        grad = grad * scale
        inner = head_sums(grad * raw, same_head) * (1.0 / width)
        active = jnp.where(mean_sq > FLOOR, 1.0, jnp.where(mean_sq == FLOOR, 0.5, 0.0))
        return inverse * grad - active * raw * (inverse * inverse * inverse) * inner

    for m in range(mem):
        grad_proj = jnp.concatenate(
            [
                head_pull(query_parts[m], query_grad[m]).astype(BF16),
                head_pull(key_parts[m], key_grad[m]).astype(BF16),
                value_grad[m].astype(BF16),
            ],
            axis=1,
        )
        grad_normed = dot_nt(grad_proj, project_ref[...]) * gain
        x = x_scr[m, own, :]
        inverse = row_rsqrt(x)
        inner = jnp.mean(x * grad_normed, axis=-1, keepdims=True)
        pulled = inverse * grad_normed - x * (inverse * inverse * inverse * inner)
        total = grad_field[m * cells : (m + 1) * cells] + pulled
        grad_ref[m] = total.astype(BF16).reshape(rows, cols, channels)


def local_call(kernel, out_shape, scratch, name, in_space=None, count=0):
    whole = pl.BlockSpec(memory_space=pltpu.VMEM)

    def keep(shape):
        return pltpu.VMEM(shape.shape, shape.dtype) if in_space else shape

    out_shape = jax.tree.map(keep, out_shape)
    return pl.pallas_call(
        kernel,
        out_shape=out_shape,
        in_specs=[pl.BlockSpec(memory_space=in_space or pltpu.VMEM)] * count,
        out_specs=jax.tree.map(lambda _: whole, out_shape),
        scratch_shapes=scratch,
        compiler_params=pltpu.CompilerParams(vmem_limit_bytes=VMEM_LIMIT),
        name=name,
    )


def per_device_paired(ensemble, norm_gain, project_weight, output_weight, conv_kernel, cotangent):
    mem, rows, cols, channels = ensemble.shape
    groups = 2 * mem
    lat_count = lax.axis_size("lat")
    strip_rows = 2 * groups * rows
    halo_rows = 2 * groups * (cols + 2)

    in_hbm = functools.partial(pltpu.with_memory_space_constraint, memory_space=pltpu.HBM)
    own_strips = 2 * mem * rows
    own_scr = pltpu.VMEM((own_strips, channels), F32)
    both, strips = local_call(
        stack_kernel,
        (
            jax.ShapeDtypeStruct((2,) + ensemble.shape, BF16),
            jax.ShapeDtypeStruct((2, own_strips, channels), BF16),
        ),
        [own_scr, own_scr, pltpu.SemaphoreType.DMA((2,))],
        "stack",
        pl.ANY,
        2,
    )(in_hbm(ensemble), in_hbm(cotangent))
    other = lax.all_gather(both, "member")
    strips = lax.all_gather(strips, ("member", "lon"))
    strips = strips.reshape((2, lax.axis_size("lon")) + strips.shape[1:])

    weights = (
        norm_gain.reshape(1, channels),
        project_weight,
        output_weight,
        conv_kernel.reshape(9 * channels, channels),
    )
    weights = local_call(
        load_kernel,
        tuple(jax.ShapeDtypeStruct(w.shape, w.dtype) for w in weights),
        [pltpu.SemaphoreType.DMA((4,))],
        "load_weights",
        pl.ANY,
        4,
    )(*[in_hbm(w) for w in weights])

    strip_scr = pltpu.VMEM((strip_rows, channels), F32)
    halo = jax.ShapeDtypeStruct((halo_rows, channels), BF16)
    first_send, second_send = local_call(
        pack_rows_kernel,
        (halo, halo),
        [strip_scr] * 2 + [pltpu.VMEM((4 * groups, channels), F32)],
        "pack_rows",
        None,
        3,
    )(both, other, strips)

    def lat_pairs(offset):
        pairs = []
        for i in range(lat_count):
            partner = i + 1 if i % 2 == offset else i - 1
            pairs.append((i, partner if 0 <= partner < lat_count else i))
        return pairs

    first = lax.ppermute(first_send, "lat", lat_pairs(0))
    second = lax.ppermute(second_send, "lat", lat_pairs(1))

    tall = rows + 2
    per_member = tall * cols + 16
    block = jax.ShapeDtypeStruct(ensemble.shape, BF16)
    return local_call(
        functools.partial(main_kernel, lat_count=lat_count),
        (block, block),
        [
            pltpu.VMEM((groups, per_member, channels), F32),
            pltpu.VMEM((groups, per_member, channels), F32),
            strip_scr,
            strip_scr,
            pltpu.VMEM((groups * per_member, 3 * channels), BF16),
            pltpu.VMEM((mem, tall * cols, 3 * channels), BF16),
            pltpu.VMEM((groups, tall * cols, 3 * channels), BF16),
        ],
        "main",
        None,
        9,
    )(both, other, strips, first, second, *weights)


def solution(mesh):
    paired = mesh.shape["member"] == 2
    per_device = per_device_paired if paired else per_device_general
    in_specs = (
        P("member", "lat", "lon", None),
        P(),
        P(),
        P(),
        P(),
        P("member", "lat", "lon", None),
    )
    out_specs = (P("member", "lat", "lon", None), P("member", "lat", "lon", None))
    return jax.shard_map(
        per_device, mesh=mesh, in_specs=in_specs, out_specs=out_specs, check_vma=False
    )
```

```python
import functools
import math

import jax
import jax.numpy as jnp
from jax import lax
from jax.experimental import pallas as pl
from jax.experimental.pallas import tpu as pltpu
from jax.sharding import PartitionSpec as P

HEAD_COUNT = 8


FLOOR = 0.5
EPSILON = 1e-06


def padded_2(block, sides, width, periodic):
    for axis, dim in sides:
        count = lax.axis_size(axis)
        forward = [(i, i + 1) for i in range(count - 1)]
        if periodic:
            forward.append((count - 1, 0))
        backward = [(target, source) for source, target in forward]
        low = lax.ppermute(
            lax.slice_in_dim(block, block.shape[dim] - width, None, axis=dim), axis, forward
        )
        high = lax.ppermute(lax.slice_in_dim(block, 0, width, axis=dim), axis, backward)
        block = jnp.concatenate([low, block, high], axis=dim)
    return block


def row_norm(values, gain_vec):
    mean_sq = jnp.mean(values * values, axis=-1, keepdims=True)
    return values * lax.rsqrt(mean_sq + EPSILON) * gain_vec


def head_norm(values, head_count):
    shaped = values.reshape(values.shape[:-1] + (head_count, values.shape[-1] // head_count))
    mean_sq = jnp.mean(shaped * shaped, axis=-1, keepdims=True)
    return (shaped * lax.rsqrt(jnp.maximum(mean_sq, FLOOR))).reshape(values.shape)


def split_heads(values, head_count):
    return values.reshape(values.shape[:-1] + (head_count, values.shape[-1] // head_count))


def head_pullback(raw_rows, grad_rows):
    _, pullback = jax.vjp(lambda t: head_norm(t, HEAD_COUNT), raw_rows.astype(jnp.float32))
    return pullback(grad_rows)[0]


def pad_field(field_in):
    widened = padded_2(field_in, (("lon", 2),), 1, True)
    return padded_2(widened, (("lat", 1),), 1, False)


def conv_taps(padded, kernel, lat_n, lon_n, adjoint):
    running = None
    for row_off in range(3):
        for col_off in range(3):
            if adjoint:
                window = padded[
                    :, 2 - row_off : 2 - row_off + lat_n, 2 - col_off : 2 - col_off + lon_n
                ]
                summand = jnp.einsum(
                    "mabc,dc->mabd",
                    window,
                    kernel[row_off, col_off],
                    preferred_element_type=jnp.float32,
                )
            else:
                window = padded[:, row_off : row_off + lat_n, col_off : col_off + lon_n]
                summand = jnp.einsum(
                    "mabc,cd->mabd",
                    window,
                    kernel[row_off, col_off],
                    preferred_element_type=jnp.float32,
                )
            running = summand if running is None else running + summand
    return running


def per_device_general(ensemble, norm_gain, project_weight, output_weight, conv_kernel, cotangent):
    mem_dev, lat_dev, lon_dev, channels = ensemble.shape
    cell_count = lat_dev * lon_dev
    score_scale = 1.0 / math.sqrt(channels // HEAD_COUNT)
    inputs = ensemble.reshape(mem_dev, cell_count, channels).astype(jnp.float32)
    normed = row_norm(inputs, norm_gain).astype(jnp.bfloat16)
    spread = lax.all_to_all(normed, "member", split_axis=1, concat_axis=0, tiled=True)
    projected = jnp.dot(spread, project_weight, preferred_element_type=jnp.float32).astype(
        jnp.bfloat16
    )
    query_raw = projected[..., :channels]
    key_raw = projected[..., channels : 2 * channels]
    value_rows = projected[..., 2 * channels :]
    key_rows = head_norm(key_raw.astype(jnp.float32), HEAD_COUNT).astype(jnp.bfloat16)
    queries = head_norm(query_raw.astype(jnp.float32), HEAD_COUNT).astype(jnp.bfloat16)
    query_heads = split_heads(queries, HEAD_COUNT)
    key_heads = split_heads(key_rows, HEAD_COUNT)
    value_heads = split_heads(value_rows, HEAD_COUNT)
    scores = (
        jnp.einsum("mphd,nphd->mnhp", query_heads, key_heads, preferred_element_type=jnp.float32)
        * score_scale
    )
    expd = jnp.exp(scores)
    soft = expd / jnp.sum(expd, axis=1, keepdims=True)
    rounded = soft.astype(jnp.bfloat16)
    mixed_out = jnp.einsum(
        "mnhp,nphd->mphd", rounded, value_heads, preferred_element_type=jnp.float32
    )
    mixed_out = mixed_out.reshape(query_raw.shape).astype(jnp.bfloat16)
    mixed_out = lax.all_to_all(mixed_out, "member", split_axis=0, concat_axis=1, tiled=True)
    updated = (
        inputs + jnp.dot(mixed_out, output_weight, preferred_element_type=jnp.float32)
    ).astype(jnp.bfloat16)
    field_up = updated.reshape(mem_dev, lat_dev, lon_dev, channels)
    result = field_up.astype(jnp.float32) + conv_taps(
        pad_field(field_up), conv_kernel, lat_dev, lon_dev, False
    )
    result = result.astype(jnp.bfloat16)
    grad_field = cotangent.astype(jnp.float32) + conv_taps(
        pad_field(cotangent), conv_kernel, lat_dev, lon_dev, True
    )
    grad_rows = grad_field.reshape(mem_dev, cell_count, channels)
    grad_mixed = jnp.einsum(
        "mpc,dc->mpd",
        grad_rows.astype(jnp.bfloat16),
        output_weight,
        preferred_element_type=jnp.float32,
    )
    grad_mixed = grad_mixed.astype(jnp.bfloat16)
    grad_mixed = lax.all_to_all(grad_mixed, "member", split_axis=1, concat_axis=0, tiled=True)
    grad_heads = split_heads(grad_mixed, HEAD_COUNT)
    dprob = jnp.einsum(
        "mphd,nphd->mnhp", grad_heads, value_heads, preferred_element_type=jnp.float32
    )
    dscore = (soft * (dprob - jnp.sum(soft * dprob, axis=1, keepdims=True))).astype(jnp.bfloat16)
    query_grad = (
        jnp.einsum("mnhp,nphd->mphd", dscore, key_heads, preferred_element_type=jnp.float32)
        * score_scale
    )
    query_grad = query_grad.reshape(query_raw.shape)
    key_grad = (
        jnp.einsum("mnhp,mphd->nphd", dscore, query_heads, preferred_element_type=jnp.float32)
        * score_scale
    )
    key_grad = key_grad.reshape(key_raw.shape)
    value_grad = jnp.einsum(
        "mnhp,mphd->nphd", rounded, grad_heads, preferred_element_type=jnp.float32
    )
    value_grad = value_grad.reshape(key_raw.shape)
    grad_query_raw = head_pullback(query_raw, query_grad)
    grad_key_raw = head_pullback(key_raw, key_grad)
    grad_proj = jnp.concatenate([grad_query_raw, grad_key_raw, value_grad], axis=-1).astype(
        jnp.bfloat16
    )
    grad_proj = lax.all_to_all(grad_proj, "member", split_axis=0, concat_axis=1, tiled=True)
    grad_normed = jnp.einsum(
        "mpe,ce->mpc", grad_proj, project_weight, preferred_element_type=jnp.float32
    )
    _, pull_norm = jax.vjp(lambda t: row_norm(t, norm_gain), inputs)
    grad_inputs = pull_norm(grad_normed)[0]
    grad_ensemble = (
        (grad_rows + grad_inputs).astype(jnp.bfloat16).reshape(mem_dev, lat_dev, lon_dev, channels)
    )
    return (result, grad_ensemble)


F32 = jnp.float32
BF16 = jnp.bfloat16
VMEM_LIMIT = 48 * 1024 * 1024


def is_even(axis):
    return lax.rem(lax.axis_index(axis), 2) == 0


def serves_south():
    return is_even("lat") == is_even("lon")


def half_index():
    return lax.rem(lax.axis_index("lon"), 2)


def stack_kernel(ens_ref, cot_ref, both_ref, hand_ref, sems):
    _, mem, rows, _, _ = both_ref.shape
    copies = [
        pltpu.make_async_copy(ref, both_ref.at[i], sems.at[i])
        for i, ref in enumerate((ens_ref, cot_ref))
    ]
    for copy in copies:
        copy.start()
    for copy in copies:
        copy.wait()
    row = jnp.where(serves_south(), 0, rows - 1)
    for array in range(2):
        for member in range(mem):
            hand_ref[array, member] = both_ref[array, member, row]


def pack_rows_kernel(both_ref, hand_ref, out_ref):
    _, mem, rows, _, _ = both_ref.shape
    half = half_index()
    row = jnp.where(serves_south(), rows - 1, 0)
    for array in range(2):
        for member in range(mem):
            out_ref[half, array, member] = both_ref[array, member, row]
            out_ref[1 - half, array, member] = hand_ref[array, member]


def share_kernel(near_ref, cross_ref, after_ref, out_ref):
    other_half = 1 - half_index()
    _, arrays, mem, _, _ = near_ref.shape
    for group, ref in enumerate((near_ref, cross_ref)):
        for array in range(arrays):
            for member in range(mem):
                out_ref[group, array, member] = ref[other_half, array, member]


def halo_rows(near_ref, cross_ref, far_ref, array, member, lat_count):
    mem = near_ref.shape[2]
    group, place = divmod(member, mem)
    near = (cross_ref if group else near_ref)[half_index(), array, place].astype(F32)
    far = far_ref[group, array, place].astype(F32)
    south = serves_south()
    lat = lax.axis_index("lat")
    top = jnp.where(lat == 0, 0.0, jnp.where(south, far, near))
    bottom = jnp.where(lat == lat_count - 1, 0.0, jnp.where(south, near, far))
    return top, bottom


def pack_strips_kernel(
    both_ref,
    other_ref,
    near_ref,
    cross_ref,
    far_ref,
    core_ref,
    chip_ref,
    low_scr,
    high_scr,
    *,
    lat_count,
):
    _, mem, rows, cols, _ = both_ref.shape
    index = 0
    for array in range(2):
        for member in range(2 * mem):
            if member < mem:
                block = both_ref[array, member]
            else:
                block = other_ref[array, member - mem]
            top, bottom = halo_rows(near_ref, cross_ref, far_ref, array, member, lat_count)
            slabs = [top] + [block[row].astype(F32) for row in range(rows)] + [bottom]
            for slab in slabs:
                low_scr[index : index + 1, :] = slab[0:1]
                high_scr[index : index + 1, :] = slab[cols - 1 : cols]
                index += 1
    even = is_even("lon")
    low, high = low_scr[...], high_scr[...]
    core_ref[...] = jnp.where(even, high, low).astype(BF16)
    chip_ref[...] = jnp.where(even, low, high).astype(BF16)


def dot_nn(a, b):
    return lax.dot_general(a, b, (((1,), (0,)), ((), ())), preferred_element_type=F32)


def dot_nt(a, b):
    return lax.dot_general(a, b, (((1,), (1,)), ((), ())), preferred_element_type=F32)


def same_head_matrix(channels):
    width = channels // HEAD_COUNT
    lane_row = lax.broadcasted_iota(jnp.int32, (channels, channels), 0) // width
    lane_col = lax.broadcasted_iota(jnp.int32, (channels, channels), 1) // width
    return jnp.where(lane_row == lane_col, 1.0, 0.0).astype(BF16)


def head_sums(values, same_head):
    high = values.astype(BF16)
    low = (values - high.astype(F32)).astype(BF16)
    return dot_nn(high, same_head) + dot_nn(low, same_head)


def head_unit(raw, same_head):
    raw = raw.astype(F32)
    mean_sq = head_sums(raw * raw, same_head) * (HEAD_COUNT / raw.shape[-1])
    inverse = lax.rsqrt(jnp.maximum(mean_sq, FLOOR))
    return raw, mean_sq, inverse, (raw * inverse).astype(BF16)


def row_rsqrt(values):
    return lax.rsqrt(jnp.mean(values * values, axis=-1, keepdims=True) + EPSILON)


def attend(query, keys, values, same_head, scale):
    exps = [jnp.exp(dot_nn(query * key, same_head) * scale) for key in keys]
    total = exps[0]
    for e in exps[1:]:
        total = total + e
    inverse = 1.0 / total
    probs = [e * inverse for e in exps]
    mixed = None
    if values is not None:
        for prob, value in zip(probs, values):
            term = prob.astype(BF16).astype(F32) * value.astype(F32)
            mixed = term if mixed is None else mixed + term
        mixed = mixed.astype(BF16)
    return probs, mixed


def own_kernel(
    both_ref,
    other_ref,
    gain_hbm,
    project_hbm,
    output_hbm,
    conv_hbm,
    gain_ref,
    project_ref,
    output_ref,
    conv_ref,
    proj_ref,
    unit_ref,
    soft_ref,
    inverse_ref,
    pull_ref,
    updated_ref,
    sems,
):
    _, mem, rows, cols, channels = both_ref.shape
    groups = 2 * mem
    cells = rows * cols
    width = channels // HEAD_COUNT
    scale = 1.0 / math.sqrt(width)
    loads = [
        pltpu.make_async_copy(source, target, sems.at[i])
        for i, (source, target) in enumerate(
            (
                (gain_hbm, gain_ref),
                (project_hbm, project_ref),
                (output_hbm, output_ref),
                (conv_hbm, conv_ref),
            )
        )
    ]
    for load in loads:
        load.start()
    same_head = same_head_matrix(channels)
    own = both_ref[0].reshape(mem * cells, channels)
    other = other_ref[0].reshape(mem * cells, channels)
    x = jnp.concatenate([own, other], axis=0).astype(F32)
    scaled = x * row_rsqrt(x)
    loads[0].wait()
    normed = (scaled * gain_ref[...]).astype(BF16)
    loads[1].wait()
    proj_ref[...] = (
        dot_nn(normed, project_ref[...]).astype(BF16).reshape(groups, cells, 3 * channels)
    )
    for kind in range(2):
        for member in range(groups):
            lanes = slice(kind * channels, (kind + 1) * channels)
            raw, mean_sq, inverse, unit = head_unit(proj_ref[member, :, lanes], same_head)
            unit_ref[kind, member] = unit
            if member < mem:
                active = jnp.where(mean_sq > FLOOR, 1.0, jnp.where(mean_sq == FLOOR, 0.5, 0.0))
                inverse_ref[kind, member] = inverse
                pull_ref[kind, member] = active * raw * (inverse * inverse * inverse) / width
    loads[2].wait()
    keys = [unit_ref[1, n] for n in range(groups)]
    values = [proj_ref[n, :, 2 * channels :] for n in range(groups)]
    for m in range(groups):
        probs, mixed = attend(unit_ref[0, m], keys, values if m < mem else None, same_head, scale)
        for n in range(groups):
            soft_ref[m * groups + n] = probs[n]
        if m < mem:
            x = both_ref[0, m].reshape(cells, channels).astype(F32)
            updated_ref[m] = (x + dot_nn(mixed, output_ref[...])).astype(BF16)
    loads[3].wait()


def main_kernel(
    both_ref,
    other_ref,
    near_ref,
    cross_ref,
    far_ref,
    core_ref,
    chip_ref,
    gain_ref,
    project_ref,
    output_ref,
    conv_ref,
    proj_ref,
    unit_ref,
    soft_ref,
    inverse_ref,
    pull_ref,
    updated_ref,
    result_ref,
    grad_ref,
    x_scr,
    cot_scr,
    proj_scr,
    shift_scr,
    cot_shift_scr,
    *,
    lat_count,
):
    _, mem, rows, cols, channels = both_ref.shape
    groups = 2 * mem
    tall = rows + 2
    centre = tall * cols
    cells = rows * cols
    rim = x_scr.shape[1]
    width = channels // HEAD_COUNT
    scale = 1.0 / math.sqrt(width)
    even = is_even("lon")
    core, chip = core_ref[...].astype(F32), chip_ref[...].astype(F32)
    low, high = jnp.where(even, chip, core), jnp.where(even, core, chip)

    for array, scr in enumerate((x_scr, cot_scr)):
        for member in range(groups):
            top, bottom = halo_rows(near_ref, cross_ref, far_ref, array, member, lat_count)
            if array == 0:
                scr[member, :cols, :] = top
                scr[member, cols : 2 * cols, :] = bottom
                edge = 2 * cols
            else:
                ref, at = (both_ref, member) if member < mem else (other_ref, member - mem)
                scr[member, :cols, :] = top
                scr[member, cols : cols + cells, :] = (
                    ref[1, at].reshape(cells, channels).astype(F32)
                )
                scr[member, cols + cells : centre, :] = bottom
                edge = centre
            scr[member, edge:, :] = jnp.zeros((16, channels), F32)
            slot = (array * groups + member) * tall
            scr[member, edge : edge + tall, :] = low[slot : slot + tall]
            scr[member, edge + 8 : edge + 8 + tall, :] = high[slot : slot + tall]

    same_head = same_head_matrix(channels)
    gain = gain_ref[...]

    x_all = x_scr[...].reshape(groups * rim, channels)
    normed = (x_all * row_rsqrt(x_all) * gain).astype(BF16)
    proj_scr[...] = dot_nn(normed, project_ref[...]).astype(BF16)
    keys = [
        head_unit(proj_scr[n * rim : (n + 1) * rim, channels : 2 * channels], same_head)[3]
        for n in range(groups)
    ]
    values = [proj_scr[n * rim : (n + 1) * rim, 2 * channels :] for n in range(groups)]
    updated = []
    for m in range(mem):
        query = head_unit(proj_scr[m * rim : (m + 1) * rim, :channels], same_head)[3]
        _, mixed = attend(query, keys, values, same_head, scale)
        field = (x_scr[m] + dot_nn(mixed, output_ref[...])).astype(BF16).astype(F32)
        updated.append(
            jnp.concatenate(
                [field[:cols], updated_ref[m].astype(F32), field[cols:]],
                axis=0,
            )
        )

    def shifted(scr, member, field):
        column = lax.broadcasted_iota(jnp.int32, (cols, channels), 0)
        for place in range(tall):
            slab = field[place * cols : (place + 1) * cols]
            west = field[centre + place : centre + place + 1]
            east = field[centre + 8 + place : centre + 8 + place + 1]
            back = jnp.where(column == 0, west, pltpu.roll(slab, 1, 0))
            ahead = jnp.where(column == cols - 1, east, pltpu.roll(slab, cols - 1, 0))
            rows_at = slice(place * cols, (place + 1) * cols)
            scr[member, rows_at, :channels] = back.astype(BF16)
            scr[member, rows_at, channels : 2 * channels] = slab.astype(BF16)
            scr[member, rows_at, 2 * channels :] = ahead.astype(BF16)

    for member in range(mem):
        shifted(shift_scr, member, updated[member])
    for member in range(groups):
        shifted(cot_shift_scr, member, cot_scr[member])

    total = updated_ref[...].reshape(mem * cells, channels).astype(F32)
    for r in range(3):
        window = jnp.concatenate(
            [shift_scr[m, r * cols : r * cols + cells, :] for m in range(mem)], axis=0
        )
        total = total + dot_nn(window, conv_ref[3 * channels * r : 3 * channels * (r + 1), :])
    result_ref[...] = total.astype(BF16).reshape(mem, rows, cols, channels)

    total = jnp.concatenate([cot_scr[m, cols : cols + cells, :] for m in range(groups)], axis=0)
    for r in range(3):
        for c in range(3):
            lanes = slice((2 - c) * channels, (3 - c) * channels)
            begin = (2 - r) * cols
            window = jnp.concatenate(
                [cot_shift_scr[m, begin : begin + cells, lanes] for m in range(groups)], axis=0
            )
            tap = (3 * r + c) * channels
            total = total + dot_nt(window, conv_ref[tap : tap + channels, :])
    grad_field = total
    grad_mixed = dot_nt(grad_field.astype(BF16), output_ref[...]).astype(BF16)
    grads = [grad_mixed[m * cells : (m + 1) * cells] for m in range(groups)]

    values = [proj_ref[n, :, 2 * channels :] for n in range(groups)]
    query_grad = [None] * mem
    key_grad = [None] * mem
    value_grad = [None] * mem
    for m in range(groups):
        soft = [soft_ref[m * groups + n] for n in range(groups)]
        dprob = [dot_nn(grads[m] * values[n], same_head) for n in range(groups)]
        mean = soft[0] * dprob[0]
        for n in range(1, groups):
            mean = mean + soft[n] * dprob[n]
        for n in range(groups):
            if m >= mem and n >= mem:
                continue
            dscore = (soft[n] * (dprob[n] - mean)).astype(BF16).astype(F32)
            if m < mem:
                term = dscore * unit_ref[1, n].astype(F32)
                query_grad[m] = term if query_grad[m] is None else query_grad[m] + term
            if n < mem:
                term = dscore * unit_ref[0, m].astype(F32)
                key_grad[n] = term if key_grad[n] is None else key_grad[n] + term
                term = soft[n].astype(BF16).astype(F32) * grads[m].astype(F32)
                value_grad[n] = term if value_grad[n] is None else value_grad[n] + term

    def head_pull(kind, member, grad):
        grad = grad * scale
        raw = proj_ref[member, :, kind * channels : (kind + 1) * channels].astype(F32)
        inner = head_sums(grad * raw, same_head)
        return inverse_ref[kind, member] * grad - pull_ref[kind, member] * inner

    for m in range(mem):
        grad_proj = jnp.concatenate(
            [
                head_pull(0, m, query_grad[m]).astype(BF16),
                head_pull(1, m, key_grad[m]).astype(BF16),
                value_grad[m].astype(BF16),
            ],
            axis=1,
        )
        grad_normed = dot_nt(grad_proj, project_ref[...]) * gain
        x = both_ref[0, m].reshape(cells, channels).astype(F32)
        inverse = row_rsqrt(x)
        inner = jnp.mean(x * grad_normed, axis=-1, keepdims=True)
        pulled = inverse * grad_normed - x * (inverse * inverse * inverse * inner)
        total = grad_field[m * cells : (m + 1) * cells] + pulled
        grad_ref[m] = total.astype(BF16).reshape(rows, cols, channels)


def local_call(kernel, name, operands, out_shape, scratch, pinned=False):
    whole = pl.BlockSpec(memory_space=pltpu.VMEM)
    anywhere = pl.BlockSpec(memory_space=pl.ANY)
    specs = [anywhere if in_hbm else whole for _, in_hbm in operands]
    arrays = [
        pltpu.with_memory_space_constraint(array, pltpu.HBM) if in_hbm else array
        for array, in_hbm in operands
    ]

    def keep(shape):
        return pltpu.VMEM(shape.shape, shape.dtype) if pinned else shape

    return pl.pallas_call(
        kernel,
        out_shape=jax.tree.map(keep, out_shape),
        in_specs=specs,
        out_specs=jax.tree.map(lambda _: whole, out_shape),
        scratch_shapes=scratch,
        compiler_params=pltpu.CompilerParams(vmem_limit_bytes=VMEM_LIMIT),
        name=name,
    )(*arrays)


def here(*arrays):
    return [(array, False) for array in arrays]


def in_hbm(*arrays):
    return [(array, True) for array in arrays]


def per_device_paired(ensemble, norm_gain, project_weight, output_weight, conv_kernel, cotangent):
    mem, rows, cols, channels = ensemble.shape
    groups = 2 * mem
    cells = rows * cols
    tall = rows + 2
    lon_count = lax.axis_size("lon")
    lat_count = lax.axis_size("lat")
    lat_kernel = functools.partial(functools.partial, lat_count=lat_count)
    bf16 = functools.partial(jax.ShapeDtypeStruct, dtype=BF16)
    f32 = functools.partial(jax.ShapeDtypeStruct, dtype=F32)
    row = (2, mem, cols, channels)

    def lat_partner(lat, lon):
        partner = lat + 1 if lat % 2 == lon % 2 else lat - 1
        return partner if 0 <= partner < lat_count else None

    core_pairs = [(i, i ^ 1) for i in range(lon_count)]
    chip_pairs = [(i, (i - 1 if i % 2 == 0 else i + 1) % lon_count) for i in range(lon_count)]
    near_pairs, cross_pairs = [], []
    for member in range(2):
        for lat in range(lat_count):
            for lon in range(lon_count):
                me = (member * lat_count + lat) * lon_count + lon
                partner = lat_partner(lat, lon)
                if partner is None:
                    near = cross = me
                else:
                    near = (member * lat_count + partner) * lon_count + lon
                    cross = ((1 - member) * lat_count + partner) * lon_count + lon
                near_pairs.append((me, near))
                cross_pairs.append((me, cross))
    everyone = ("member", "lat", "lon")

    both, hand = local_call(
        stack_kernel,
        "stack",
        in_hbm(ensemble, cotangent),
        (bf16((2,) + ensemble.shape), bf16(row)),
        [pltpu.SemaphoreType.DMA((2,))],
        pinned=True,
    )
    handed = lax.ppermute(hand, "lon", core_pairs)
    other = lax.ppermute(both, "member", [(0, 1), (1, 0)])
    sent = local_call(pack_rows_kernel, "pack_rows", here(both, handed), bf16((2,) + row), [])
    cross = lax.ppermute(sent, everyone, cross_pairs)
    near = lax.ppermute(sent, everyone, near_pairs)

    weights = (
        norm_gain.reshape(1, channels),
        project_weight,
        output_weight,
        conv_kernel.reshape(9 * channels, channels),
    )
    held = local_call(
        own_kernel,
        "own_cells",
        here(both, other) + in_hbm(*weights),
        tuple(jax.ShapeDtypeStruct(w.shape, w.dtype) for w in weights)
        + (
            bf16((groups, cells, 3 * channels)),
            bf16((2, groups, cells, channels)),
            f32((groups * groups, cells, channels)),
            f32((2, mem, cells, channels)),
            f32((2, mem, cells, channels)),
            bf16((mem, cells, channels)),
        ),
        [pltpu.SemaphoreType.DMA((4,))],
        pinned=True,
    )

    share = local_call(share_kernel, "share", here(near, cross, held[0]), bf16((2,) + row), [])
    far = lax.ppermute(share, "lon", core_pairs)
    strip = (2 * groups * tall, channels)
    core_send, chip_send = local_call(
        lat_kernel(pack_strips_kernel),
        "pack_strips",
        here(both, other, near, cross, far),
        (bf16(strip), bf16(strip)),
        [pltpu.VMEM(strip, F32)] * 2,
    )
    core = lax.ppermute(core_send, "lon", core_pairs)
    chip = lax.ppermute(chip_send, "lon", chip_pairs)

    rim = 2 * cols + 16
    return local_call(
        lat_kernel(main_kernel),
        "main",
        here(both, other, near, cross, far, core, chip, *held),
        (bf16(ensemble.shape), bf16(ensemble.shape)),
        [
            pltpu.VMEM((groups, rim, channels), F32),
            pltpu.VMEM((groups, tall * cols + 16, channels), F32),
            pltpu.VMEM((groups * rim, 3 * channels), BF16),
            pltpu.VMEM((mem, tall * cols, 3 * channels), BF16),
            pltpu.VMEM((groups, tall * cols, 3 * channels), BF16),
        ],
    )


def solution(mesh):
    paired = mesh.shape["member"] == 2 and mesh.shape["lon"] % 2 == 0
    per_device = per_device_paired if paired else per_device_general
    in_specs = (
        P("member", "lat", "lon", None),
        P(),
        P(),
        P(),
        P(),
        P("member", "lat", "lon", None),
    )
    out_specs = (P("member", "lat", "lon", None), P("member", "lat", "lon", None))
    return jax.shard_map(
        per_device, mesh=mesh, in_specs=in_specs, out_specs=out_specs, check_vma=False
    )
```

```python
import functools
import math

import jax
import jax.numpy as jnp
from jax import lax
from jax.experimental import pallas as pl
from jax.experimental.pallas import tpu as pltpu
from jax.sharding import PartitionSpec as P

HEAD_COUNT = 8


FLOOR = 0.5
EPSILON = 1e-06


def padded_2(block, sides, width, periodic):
    for axis, dim in sides:
        count = lax.axis_size(axis)
        forward = [(i, i + 1) for i in range(count - 1)]
        if periodic:
            forward.append((count - 1, 0))
        backward = [(target, source) for source, target in forward]
        low = lax.ppermute(
            lax.slice_in_dim(block, block.shape[dim] - width, None, axis=dim), axis, forward
        )
        high = lax.ppermute(lax.slice_in_dim(block, 0, width, axis=dim), axis, backward)
        block = jnp.concatenate([low, block, high], axis=dim)
    return block


def row_norm(values, gain_vec):
    mean_sq = jnp.mean(values * values, axis=-1, keepdims=True)
    return values * lax.rsqrt(mean_sq + EPSILON) * gain_vec


def head_norm(values, head_count):
    shaped = values.reshape(values.shape[:-1] + (head_count, values.shape[-1] // head_count))
    mean_sq = jnp.mean(shaped * shaped, axis=-1, keepdims=True)
    return (shaped * lax.rsqrt(jnp.maximum(mean_sq, FLOOR))).reshape(values.shape)


def split_heads(values, head_count):
    return values.reshape(values.shape[:-1] + (head_count, values.shape[-1] // head_count))


def head_pullback(raw_rows, grad_rows):
    _, pullback = jax.vjp(lambda t: head_norm(t, HEAD_COUNT), raw_rows.astype(jnp.float32))
    return pullback(grad_rows)[0]


def pad_field(field_in):
    widened = padded_2(field_in, (("lon", 2),), 1, True)
    return padded_2(widened, (("lat", 1),), 1, False)


def conv_taps(padded, kernel, lat_n, lon_n, adjoint):
    running = None
    for row_off in range(3):
        for col_off in range(3):
            if adjoint:
                window = padded[
                    :, 2 - row_off : 2 - row_off + lat_n, 2 - col_off : 2 - col_off + lon_n
                ]
                summand = jnp.einsum(
                    "mabc,dc->mabd",
                    window,
                    kernel[row_off, col_off],
                    preferred_element_type=jnp.float32,
                )
            else:
                window = padded[:, row_off : row_off + lat_n, col_off : col_off + lon_n]
                summand = jnp.einsum(
                    "mabc,cd->mabd",
                    window,
                    kernel[row_off, col_off],
                    preferred_element_type=jnp.float32,
                )
            running = summand if running is None else running + summand
    return running


def per_device_general(ensemble, norm_gain, project_weight, output_weight, conv_kernel, cotangent):
    mem_dev, lat_dev, lon_dev, channels = ensemble.shape
    cell_count = lat_dev * lon_dev
    score_scale = 1.0 / math.sqrt(channels // HEAD_COUNT)
    inputs = ensemble.reshape(mem_dev, cell_count, channels).astype(jnp.float32)
    normed = row_norm(inputs, norm_gain).astype(jnp.bfloat16)
    spread = lax.all_to_all(normed, "member", split_axis=1, concat_axis=0, tiled=True)
    projected = jnp.dot(spread, project_weight, preferred_element_type=jnp.float32).astype(
        jnp.bfloat16
    )
    query_raw = projected[..., :channels]
    key_raw = projected[..., channels : 2 * channels]
    value_rows = projected[..., 2 * channels :]
    key_rows = head_norm(key_raw.astype(jnp.float32), HEAD_COUNT).astype(jnp.bfloat16)
    queries = head_norm(query_raw.astype(jnp.float32), HEAD_COUNT).astype(jnp.bfloat16)
    query_heads = split_heads(queries, HEAD_COUNT)
    key_heads = split_heads(key_rows, HEAD_COUNT)
    value_heads = split_heads(value_rows, HEAD_COUNT)
    scores = (
        jnp.einsum("mphd,nphd->mnhp", query_heads, key_heads, preferred_element_type=jnp.float32)
        * score_scale
    )
    expd = jnp.exp(scores)
    soft = expd / jnp.sum(expd, axis=1, keepdims=True)
    rounded = soft.astype(jnp.bfloat16)
    mixed_out = jnp.einsum(
        "mnhp,nphd->mphd", rounded, value_heads, preferred_element_type=jnp.float32
    )
    mixed_out = mixed_out.reshape(query_raw.shape).astype(jnp.bfloat16)
    mixed_out = lax.all_to_all(mixed_out, "member", split_axis=0, concat_axis=1, tiled=True)
    updated = (
        inputs + jnp.dot(mixed_out, output_weight, preferred_element_type=jnp.float32)
    ).astype(jnp.bfloat16)
    field_up = updated.reshape(mem_dev, lat_dev, lon_dev, channels)
    result = field_up.astype(jnp.float32) + conv_taps(
        pad_field(field_up), conv_kernel, lat_dev, lon_dev, False
    )
    result = result.astype(jnp.bfloat16)
    grad_field = cotangent.astype(jnp.float32) + conv_taps(
        pad_field(cotangent), conv_kernel, lat_dev, lon_dev, True
    )
    grad_rows = grad_field.reshape(mem_dev, cell_count, channels)
    grad_mixed = jnp.einsum(
        "mpc,dc->mpd",
        grad_rows.astype(jnp.bfloat16),
        output_weight,
        preferred_element_type=jnp.float32,
    )
    grad_mixed = grad_mixed.astype(jnp.bfloat16)
    grad_mixed = lax.all_to_all(grad_mixed, "member", split_axis=1, concat_axis=0, tiled=True)
    grad_heads = split_heads(grad_mixed, HEAD_COUNT)
    dprob = jnp.einsum(
        "mphd,nphd->mnhp", grad_heads, value_heads, preferred_element_type=jnp.float32
    )
    dscore = (soft * (dprob - jnp.sum(soft * dprob, axis=1, keepdims=True))).astype(jnp.bfloat16)
    query_grad = (
        jnp.einsum("mnhp,nphd->mphd", dscore, key_heads, preferred_element_type=jnp.float32)
        * score_scale
    )
    query_grad = query_grad.reshape(query_raw.shape)
    key_grad = (
        jnp.einsum("mnhp,mphd->nphd", dscore, query_heads, preferred_element_type=jnp.float32)
        * score_scale
    )
    key_grad = key_grad.reshape(key_raw.shape)
    value_grad = jnp.einsum(
        "mnhp,mphd->nphd", rounded, grad_heads, preferred_element_type=jnp.float32
    )
    value_grad = value_grad.reshape(key_raw.shape)
    grad_query_raw = head_pullback(query_raw, query_grad)
    grad_key_raw = head_pullback(key_raw, key_grad)
    grad_proj = jnp.concatenate([grad_query_raw, grad_key_raw, value_grad], axis=-1).astype(
        jnp.bfloat16
    )
    grad_proj = lax.all_to_all(grad_proj, "member", split_axis=0, concat_axis=1, tiled=True)
    grad_normed = jnp.einsum(
        "mpe,ce->mpc", grad_proj, project_weight, preferred_element_type=jnp.float32
    )
    _, pull_norm = jax.vjp(lambda t: row_norm(t, norm_gain), inputs)
    grad_inputs = pull_norm(grad_normed)[0]
    grad_ensemble = (
        (grad_rows + grad_inputs).astype(jnp.bfloat16).reshape(mem_dev, lat_dev, lon_dev, channels)
    )
    return (result, grad_ensemble)


F32 = jnp.float32
BF16 = jnp.bfloat16
VMEM_LIMIT = 48 * 1024 * 1024


def is_even(axis):
    return lax.rem(lax.axis_index(axis), 2) == 0


def stack_kernel(ens_ref, cot_ref, both_ref, first_ref, second_ref, sems):
    _, mem, rows, _, _ = both_ref.shape
    copies = [
        pltpu.make_async_copy(ref, both_ref.at[i], sems.at[i])
        for i, ref in enumerate((ens_ref, cot_ref))
    ]
    for copy in copies:
        copy.start()
    for copy in copies:
        copy.wait()
    even = is_even("lat")
    for array in range(2):
        for member in range(mem):
            first_ref[array, member] = both_ref[array, member, jnp.where(even, rows - 1, 0)]
            second_ref[array, member] = both_ref[array, member, jnp.where(even, 0, rows - 1)]


def halo_kernel(first_ref, second_ref, after_ref, halo_ref, *, lat_count):
    arrays, mem, _, _ = first_ref.shape
    even = is_even("lat")
    lat = lax.axis_index("lat")
    for array in range(arrays):
        for member in range(mem):
            first = first_ref[array, member].astype(F32)
            second = second_ref[array, member].astype(F32)
            north = jnp.where(lat == 0, 0.0, jnp.where(even, second, first))
            south = jnp.where(lat == lat_count - 1, 0.0, jnp.where(even, first, second))
            halo_ref[0, array, member] = north.astype(BF16)
            halo_ref[1, array, member] = south.astype(BF16)


def pack_strips_kernel(
    both_ref, other_ref, halo_ref, other_halo_ref, after_ref, core_ref, chip_ref, low_scr, high_scr
):
    _, mem, rows, cols, _ = both_ref.shape
    index = 0
    for array in range(2):
        for member in range(2 * mem):
            if member < mem:
                block, halo, at = both_ref, halo_ref, member
            else:
                block, halo, at = other_ref, other_halo_ref, member - mem
            slabs = [halo[0, array, at]] + [block[array, at, row] for row in range(rows)]
            slabs.append(halo[1, array, at])
            for slab in slabs:
                slab = slab.astype(F32)
                low_scr[index : index + 1, :] = slab[0:1]
                high_scr[index : index + 1, :] = slab[cols - 1 : cols]
                index += 1
    even = is_even("lon")
    low, high = low_scr[...], high_scr[...]
    core_ref[...] = jnp.where(even, high, low).astype(BF16)
    chip_ref[...] = jnp.where(even, low, high).astype(BF16)


def dot_nn(a, b):
    return lax.dot_general(a, b, (((1,), (0,)), ((), ())), preferred_element_type=F32)


def same_head_matrix(channels):
    width = channels // HEAD_COUNT
    lane_row = lax.broadcasted_iota(jnp.int32, (channels, channels), 0) // width
    lane_col = lax.broadcasted_iota(jnp.int32, (channels, channels), 1) // width
    return jnp.where(lane_row == lane_col, 1.0, 0.0).astype(BF16)


def head_sums(values, same_head):
    high = values.astype(BF16)
    low = (values - high.astype(F32)).astype(BF16)
    return dot_nn(high, same_head) + dot_nn(low, same_head)


def head_unit(raw, same_head):
    raw = raw.astype(F32)
    mean_sq = head_sums(raw * raw, same_head) * (HEAD_COUNT / raw.shape[-1])
    inverse = lax.rsqrt(jnp.maximum(mean_sq, FLOOR))
    return raw, mean_sq, inverse, (raw * inverse).astype(BF16)


def row_rsqrt(values):
    return lax.rsqrt(jnp.mean(values * values, axis=-1, keepdims=True) + EPSILON)


def attend(query, keys, values, same_head, scale):
    exps = [jnp.exp(dot_nn(query * key, same_head) * scale) for key in keys]
    total = exps[0]
    for e in exps[1:]:
        total = total + e
    inverse = 1.0 / total
    probs = [e * inverse for e in exps]
    mixed = None
    if values is not None:
        for prob, value in zip(probs, values):
            term = prob.astype(BF16).astype(F32) * value.astype(F32)
            mixed = term if mixed is None else mixed + term
        mixed = mixed.astype(BF16)
    return probs, mixed


def weights_kernel(
    gain_hbm,
    project_hbm,
    output_hbm,
    conv_hbm,
    gain_ref,
    project_ref,
    output_ref,
    conv_ref,
    project_t_ref,
    output_t_ref,
    conv_t_ref,
    sems,
):
    channels = output_ref.shape[0]
    loads = [
        pltpu.make_async_copy(source, target, sems.at[i])
        for i, (source, target) in enumerate(
            (
                (gain_hbm, gain_ref),
                (project_hbm, project_ref),
                (output_hbm, output_ref),
                (conv_hbm, conv_ref),
            )
        )
    ]
    for load in loads:
        load.start()
    loads[0].wait()
    loads[1].wait()
    for kind in range(3):
        lanes = slice(kind * channels, (kind + 1) * channels)
        project_t_ref[lanes, :] = project_ref[:, lanes].T
    loads[2].wait()
    output_t_ref[...] = output_ref[...].T
    loads[3].wait()
    for r in range(3):
        for c in range(3):
            tap = (3 * r + c) * channels
            turned = (3 * r + 2 - c) * channels
            conv_t_ref[turned : turned + channels, :] = conv_ref[tap : tap + channels, :].T


def own_kernel(
    both_ref,
    other_ref,
    gain_ref,
    project_ref,
    output_ref,
    proj_ref,
    unit_ref,
    soft_ref,
    inverse_ref,
    pull_ref,
    updated_ref,
):
    _, mem, rows, cols, channels = both_ref.shape
    groups = 2 * mem
    cells = rows * cols
    width = channels // HEAD_COUNT
    scale = 1.0 / math.sqrt(width)
    same_head = same_head_matrix(channels)
    own = both_ref[0].reshape(mem * cells, channels)
    other = other_ref[0].reshape(mem * cells, channels)
    x = jnp.concatenate([own, other], axis=0).astype(F32)
    normed = (x * row_rsqrt(x) * gain_ref[...]).astype(BF16)
    proj_ref[...] = (
        dot_nn(normed, project_ref[...]).astype(BF16).reshape(groups, cells, 3 * channels)
    )
    for kind in range(2):
        for member in range(groups):
            lanes = slice(kind * channels, (kind + 1) * channels)
            raw, mean_sq, inverse, unit = head_unit(proj_ref[member, :, lanes], same_head)
            unit_ref[kind, member] = unit
            if member < mem:
                active = jnp.where(mean_sq > FLOOR, 1.0, jnp.where(mean_sq == FLOOR, 0.5, 0.0))
                inverse_ref[kind, member] = inverse
                pull_ref[kind, member] = active * raw * (inverse * inverse * inverse) / width
    keys = [unit_ref[1, n] for n in range(groups)]
    values = [proj_ref[n, :, 2 * channels :] for n in range(groups)]
    for m in range(groups):
        probs, mixed = attend(unit_ref[0, m], keys, values if m < mem else None, same_head, scale)
        for n in range(groups):
            soft_ref[m * groups + n] = probs[n]
        if m < mem:
            x = both_ref[0, m].reshape(cells, channels).astype(F32)
            updated_ref[m] = (x + dot_nn(mixed, output_ref[...])).astype(BF16)


def main_kernel(
    both_ref,
    other_ref,
    halo_ref,
    other_halo_ref,
    core_ref,
    chip_ref,
    gain_ref,
    project_ref,
    output_ref,
    conv_ref,
    project_t_ref,
    output_t_ref,
    conv_t_ref,
    proj_ref,
    unit_ref,
    soft_ref,
    inverse_ref,
    pull_ref,
    updated_ref,
    result_ref,
    grad_ref,
    x_scr,
    cot_scr,
    proj_scr,
    shift_scr,
    cot_shift_scr,
):
    _, mem, rows, cols, channels = both_ref.shape
    groups = 2 * mem
    tall = rows + 2
    centre = tall * cols
    cells = rows * cols
    rim = x_scr.shape[1]
    width = channels // HEAD_COUNT
    scale = 1.0 / math.sqrt(width)
    even = is_even("lon")
    core, chip = core_ref[...].astype(F32), chip_ref[...].astype(F32)
    low, high = jnp.where(even, chip, core), jnp.where(even, core, chip)

    for array, scr in enumerate((x_scr, cot_scr)):
        for member in range(groups):
            ref, at = (halo_ref, member) if member < mem else (other_halo_ref, member - mem)
            top, bottom = ref[0, array, at].astype(F32), ref[1, array, at].astype(F32)
            if array == 0:
                scr[member, :cols, :] = top
                scr[member, cols : 2 * cols, :] = bottom
                edge = 2 * cols
            else:
                ref, at = (both_ref, member) if member < mem else (other_ref, member - mem)
                scr[member, :cols, :] = top
                scr[member, cols : cols + cells, :] = (
                    ref[1, at].reshape(cells, channels).astype(F32)
                )
                scr[member, cols + cells : centre, :] = bottom
                edge = centre
            scr[member, edge:, :] = jnp.zeros((16, channels), F32)
            slot = (array * groups + member) * tall
            scr[member, edge : edge + tall, :] = low[slot : slot + tall]
            scr[member, edge + 8 : edge + 8 + tall, :] = high[slot : slot + tall]

    same_head = same_head_matrix(channels)
    gain = gain_ref[...]

    x_all = x_scr[...].reshape(groups * rim, channels)
    normed = (x_all * row_rsqrt(x_all) * gain).astype(BF16)
    proj_scr[...] = dot_nn(normed, project_ref[...]).astype(BF16)
    keys = [
        head_unit(proj_scr[n * rim : (n + 1) * rim, channels : 2 * channels], same_head)[3]
        for n in range(groups)
    ]
    values = [proj_scr[n * rim : (n + 1) * rim, 2 * channels :] for n in range(groups)]
    updated = []
    for m in range(mem):
        query = head_unit(proj_scr[m * rim : (m + 1) * rim, :channels], same_head)[3]
        _, mixed = attend(query, keys, values, same_head, scale)
        field = (x_scr[m] + dot_nn(mixed, output_ref[...])).astype(BF16).astype(F32)
        updated.append(
            jnp.concatenate(
                [field[:cols], updated_ref[m].astype(F32), field[cols:]],
                axis=0,
            )
        )

    def shifted(scr, member, field):
        column = lax.broadcasted_iota(jnp.int32, (cols, channels), 0)
        for place in range(tall):
            slab = field[place * cols : (place + 1) * cols]
            west = field[centre + place : centre + place + 1]
            east = field[centre + 8 + place : centre + 8 + place + 1]
            back = jnp.where(column == 0, west, pltpu.roll(slab, 1, 0))
            ahead = jnp.where(column == cols - 1, east, pltpu.roll(slab, cols - 1, 0))
            rows_at = slice(place * cols, (place + 1) * cols)
            scr[member, rows_at, :channels] = back.astype(BF16)
            scr[member, rows_at, channels : 2 * channels] = slab.astype(BF16)
            scr[member, rows_at, 2 * channels :] = ahead.astype(BF16)

    for member in range(mem):
        shifted(shift_scr, member, updated[member])
    for member in range(groups):
        shifted(cot_shift_scr, member, cot_scr[member])

    total = updated_ref[...].reshape(mem * cells, channels).astype(F32)
    for r in range(3):
        window = jnp.concatenate(
            [shift_scr[m, r * cols : r * cols + cells, :] for m in range(mem)], axis=0
        )
        total = total + dot_nn(window, conv_ref[3 * channels * r : 3 * channels * (r + 1), :])
    result_ref[...] = total.astype(BF16).reshape(mem, rows, cols, channels)

    total = jnp.concatenate([cot_scr[m, cols : cols + cells, :] for m in range(groups)], axis=0)
    for r in range(3):
        begin = (2 - r) * cols
        window = jnp.concatenate(
            [cot_shift_scr[m, begin : begin + cells, :] for m in range(groups)], axis=0
        )
        total = total + dot_nn(window, conv_t_ref[3 * channels * r : 3 * channels * (r + 1), :])
    grad_field = total
    grad_mixed = dot_nn(grad_field.astype(BF16), output_t_ref[...]).astype(BF16)
    grads = [grad_mixed[m * cells : (m + 1) * cells] for m in range(groups)]

    values = [proj_ref[n, :, 2 * channels :] for n in range(groups)]
    query_grad = [None] * mem
    key_grad = [None] * mem
    value_grad = [None] * mem
    for m in range(groups):
        soft = [soft_ref[m * groups + n] for n in range(groups)]
        dprob = [dot_nn(grads[m] * values[n], same_head) for n in range(groups)]
        mean = soft[0] * dprob[0]
        for n in range(1, groups):
            mean = mean + soft[n] * dprob[n]
        for n in range(groups):
            if m >= mem and n >= mem:
                continue
            dscore = (soft[n] * (dprob[n] - mean)).astype(BF16).astype(F32)
            if m < mem:
                term = dscore * unit_ref[1, n].astype(F32)
                query_grad[m] = term if query_grad[m] is None else query_grad[m] + term
            if n < mem:
                term = dscore * unit_ref[0, m].astype(F32)
                key_grad[n] = term if key_grad[n] is None else key_grad[n] + term
                term = soft[n].astype(BF16).astype(F32) * grads[m].astype(F32)
                value_grad[n] = term if value_grad[n] is None else value_grad[n] + term

    def head_pull(kind, member, grad):
        grad = grad * scale
        raw = proj_ref[member, :, kind * channels : (kind + 1) * channels].astype(F32)
        inner = head_sums(grad * raw, same_head)
        return inverse_ref[kind, member] * grad - pull_ref[kind, member] * inner

    for m in range(mem):
        grad_proj = jnp.concatenate(
            [
                head_pull(0, m, query_grad[m]).astype(BF16),
                head_pull(1, m, key_grad[m]).astype(BF16),
                value_grad[m].astype(BF16),
            ],
            axis=1,
        )
        grad_normed = dot_nn(grad_proj, project_t_ref[...]) * gain
        x = both_ref[0, m].reshape(cells, channels).astype(F32)
        inverse = row_rsqrt(x)
        inner = jnp.mean(x * grad_normed, axis=-1, keepdims=True)
        pulled = inverse * grad_normed - x * (inverse * inverse * inverse * inner)
        total = grad_field[m * cells : (m + 1) * cells] + pulled
        grad_ref[m] = total.astype(BF16).reshape(rows, cols, channels)


def local_call(kernel, name, operands, out_shape, scratch, pinned=False, cost=None):
    whole = pl.BlockSpec(memory_space=pltpu.VMEM)
    anywhere = pl.BlockSpec(memory_space=pl.ANY)
    specs = [anywhere if in_hbm else whole for _, in_hbm in operands]
    arrays = [
        pltpu.with_memory_space_constraint(array, pltpu.HBM) if in_hbm else array
        for array, in_hbm in operands
    ]

    def keep(shape):
        return pltpu.VMEM(shape.shape, shape.dtype) if pinned else shape

    return pl.pallas_call(
        kernel,
        out_shape=jax.tree.map(keep, out_shape),
        in_specs=specs,
        out_specs=jax.tree.map(lambda _: whole, out_shape),
        scratch_shapes=scratch,
        compiler_params=pltpu.CompilerParams(vmem_limit_bytes=VMEM_LIMIT),
        cost_estimate=cost,
        name=name,
    )(*arrays)


def here(*arrays):
    return [(array, False) for array in arrays]


def in_hbm(*arrays):
    return [(array, True) for array in arrays]


def per_device_paired(ensemble, norm_gain, project_weight, output_weight, conv_kernel, cotangent):
    mem, rows, cols, channels = ensemble.shape
    groups = 2 * mem
    cells = rows * cols
    tall = rows + 2
    lon_count = lax.axis_size("lon")
    lat_count = lax.axis_size("lat")
    bf16 = functools.partial(jax.ShapeDtypeStruct, dtype=BF16)
    f32 = functools.partial(jax.ShapeDtypeStruct, dtype=F32)
    row = (2, mem, cols, channels)
    swap = [(0, 1), (1, 0)]
    core_pairs = [(i, i ^ 1) for i in range(lon_count)]
    chip_pairs = [(i, (i - 1 if i % 2 == 0 else i + 1) % lon_count) for i in range(lon_count)]

    def lat_pairs(offset):
        pairs = []
        for i in range(lat_count):
            partner = i + 1 if i % 2 == offset else i - 1
            pairs.append((i, partner if 0 <= partner < lat_count else i))
        return pairs

    both, first, second = local_call(
        stack_kernel,
        "stack",
        in_hbm(ensemble, cotangent),
        (bf16((2,) + ensemble.shape), bf16(row), bf16(row)),
        [pltpu.SemaphoreType.DMA((2,))],
        pinned=True,
    )
    first = lax.ppermute(first, "lat", lat_pairs(0))
    second = lax.ppermute(second, "lat", lat_pairs(1))
    other = lax.ppermute(both, "member", swap)

    weights = (
        norm_gain.reshape(1, channels),
        project_weight,
        output_weight,
        conv_kernel.reshape(9 * channels, channels),
    )
    weights = local_call(
        weights_kernel,
        "load_weights",
        in_hbm(*weights),
        tuple(jax.ShapeDtypeStruct(w.shape, w.dtype) for w in weights)
        + (
            bf16((3 * channels, channels)),
            bf16((channels, channels)),
            bf16((9 * channels, channels)),
        ),
        [pltpu.SemaphoreType.DMA((4,))],
        pinned=True,
        cost=pl.CostEstimate(flops=20_000_000_000, bytes_accessed=4_000_000, transcendentals=0),
    )
    halo = local_call(
        functools.partial(halo_kernel, lat_count=lat_count),
        "halo",
        here(first, second, weights[0]),
        bf16((2,) + row),
        [],
    )
    other_halo = lax.ppermute(halo, "member", swap)

    held = local_call(
        own_kernel,
        "own_cells",
        here(both, other, *weights[:3]),
        (
            bf16((groups, cells, 3 * channels)),
            bf16((2, groups, cells, channels)),
            f32((groups * groups, cells, channels)),
            f32((2, mem, cells, channels)),
            f32((2, mem, cells, channels)),
            bf16((mem, cells, channels)),
        ),
        [],
        pinned=True,
    )

    strip = (2 * groups * tall, channels)
    core_send, chip_send = local_call(
        pack_strips_kernel,
        "pack_strips",
        here(both, other, halo, other_halo, held[-1]),
        (bf16(strip), bf16(strip)),
        [pltpu.VMEM(strip, F32)] * 2,
    )
    core = lax.ppermute(core_send, "lon", core_pairs)
    chip = lax.ppermute(chip_send, "lon", chip_pairs)

    rim = 2 * cols + 16
    return local_call(
        main_kernel,
        "main",
        here(both, other, halo, other_halo, core, chip, *weights, *held),
        (bf16(ensemble.shape), bf16(ensemble.shape)),
        [
            pltpu.VMEM((groups, rim, channels), F32),
            pltpu.VMEM((groups, tall * cols + 16, channels), F32),
            pltpu.VMEM((groups * rim, 3 * channels), BF16),
            pltpu.VMEM((mem, tall * cols, 3 * channels), BF16),
            pltpu.VMEM((groups, tall * cols, 3 * channels), BF16),
        ],
    )


def solution(mesh):
    paired = mesh.shape["member"] == 2 and mesh.shape["lon"] % 2 == 0
    per_device = per_device_paired if paired else per_device_general
    in_specs = (
        P("member", "lat", "lon", None),
        P(),
        P(),
        P(),
        P(),
        P("member", "lat", "lon", None),
    )
    out_specs = (P("member", "lat", "lon", None), P("member", "lat", "lon", None))
    return jax.shard_map(
        per_device, mesh=mesh, in_specs=in_specs, out_specs=out_specs, check_vma=False
    )
```

```python
import functools
import math

import jax
import jax.numpy as jnp
from jax import lax
from jax.experimental import pallas as pl
from jax.experimental.pallas import tpu as pltpu
from jax.sharding import PartitionSpec as P

HEAD_COUNT = 8


FLOOR = 0.5
EPSILON = 1e-06


def padded_2(block, sides, width, periodic):
    for axis, dim in sides:
        count = lax.axis_size(axis)
        forward = [(i, i + 1) for i in range(count - 1)]
        if periodic:
            forward.append((count - 1, 0))
        backward = [(target, source) for source, target in forward]
        low = lax.ppermute(
            lax.slice_in_dim(block, block.shape[dim] - width, None, axis=dim), axis, forward
        )
        high = lax.ppermute(lax.slice_in_dim(block, 0, width, axis=dim), axis, backward)
        block = jnp.concatenate([low, block, high], axis=dim)
    return block


def row_norm(values, gain_vec):
    mean_sq = jnp.mean(values * values, axis=-1, keepdims=True)
    return values * lax.rsqrt(mean_sq + EPSILON) * gain_vec


def head_norm(values, head_count):
    shaped = values.reshape(values.shape[:-1] + (head_count, values.shape[-1] // head_count))
    mean_sq = jnp.mean(shaped * shaped, axis=-1, keepdims=True)
    return (shaped * lax.rsqrt(jnp.maximum(mean_sq, FLOOR))).reshape(values.shape)


def split_heads(values, head_count):
    return values.reshape(values.shape[:-1] + (head_count, values.shape[-1] // head_count))


def head_pullback(raw_rows, grad_rows):
    _, pullback = jax.vjp(lambda t: head_norm(t, HEAD_COUNT), raw_rows.astype(jnp.float32))
    return pullback(grad_rows)[0]


def pad_field(field_in):
    widened = padded_2(field_in, (("lon", 2),), 1, True)
    return padded_2(widened, (("lat", 1),), 1, False)


def conv_taps(padded, kernel, lat_n, lon_n, adjoint):
    running = None
    for row_off in range(3):
        for col_off in range(3):
            if adjoint:
                window = padded[
                    :, 2 - row_off : 2 - row_off + lat_n, 2 - col_off : 2 - col_off + lon_n
                ]
                summand = jnp.einsum(
                    "mabc,dc->mabd",
                    window,
                    kernel[row_off, col_off],
                    preferred_element_type=jnp.float32,
                )
            else:
                window = padded[:, row_off : row_off + lat_n, col_off : col_off + lon_n]
                summand = jnp.einsum(
                    "mabc,cd->mabd",
                    window,
                    kernel[row_off, col_off],
                    preferred_element_type=jnp.float32,
                )
            running = summand if running is None else running + summand
    return running


def per_device_general(ensemble, norm_gain, project_weight, output_weight, conv_kernel, cotangent):
    mem_dev, lat_dev, lon_dev, channels = ensemble.shape
    cell_count = lat_dev * lon_dev
    score_scale = 1.0 / math.sqrt(channels // HEAD_COUNT)
    inputs = ensemble.reshape(mem_dev, cell_count, channels).astype(jnp.float32)
    normed = row_norm(inputs, norm_gain).astype(jnp.bfloat16)
    spread = lax.all_to_all(normed, "member", split_axis=1, concat_axis=0, tiled=True)
    projected = jnp.dot(spread, project_weight, preferred_element_type=jnp.float32).astype(
        jnp.bfloat16
    )
    query_raw = projected[..., :channels]
    key_raw = projected[..., channels : 2 * channels]
    value_rows = projected[..., 2 * channels :]
    key_rows = head_norm(key_raw.astype(jnp.float32), HEAD_COUNT).astype(jnp.bfloat16)
    queries = head_norm(query_raw.astype(jnp.float32), HEAD_COUNT).astype(jnp.bfloat16)
    query_heads = split_heads(queries, HEAD_COUNT)
    key_heads = split_heads(key_rows, HEAD_COUNT)
    value_heads = split_heads(value_rows, HEAD_COUNT)
    scores = (
        jnp.einsum("mphd,nphd->mnhp", query_heads, key_heads, preferred_element_type=jnp.float32)
        * score_scale
    )
    expd = jnp.exp(scores)
    soft = expd / jnp.sum(expd, axis=1, keepdims=True)
    rounded = soft.astype(jnp.bfloat16)
    mixed_out = jnp.einsum(
        "mnhp,nphd->mphd", rounded, value_heads, preferred_element_type=jnp.float32
    )
    mixed_out = mixed_out.reshape(query_raw.shape).astype(jnp.bfloat16)
    mixed_out = lax.all_to_all(mixed_out, "member", split_axis=0, concat_axis=1, tiled=True)
    updated = (
        inputs + jnp.dot(mixed_out, output_weight, preferred_element_type=jnp.float32)
    ).astype(jnp.bfloat16)
    field_up = updated.reshape(mem_dev, lat_dev, lon_dev, channels)
    result = field_up.astype(jnp.float32) + conv_taps(
        pad_field(field_up), conv_kernel, lat_dev, lon_dev, False
    )
    result = result.astype(jnp.bfloat16)
    grad_field = cotangent.astype(jnp.float32) + conv_taps(
        pad_field(cotangent), conv_kernel, lat_dev, lon_dev, True
    )
    grad_rows = grad_field.reshape(mem_dev, cell_count, channels)
    grad_mixed = jnp.einsum(
        "mpc,dc->mpd",
        grad_rows.astype(jnp.bfloat16),
        output_weight,
        preferred_element_type=jnp.float32,
    )
    grad_mixed = grad_mixed.astype(jnp.bfloat16)
    grad_mixed = lax.all_to_all(grad_mixed, "member", split_axis=1, concat_axis=0, tiled=True)
    grad_heads = split_heads(grad_mixed, HEAD_COUNT)
    dprob = jnp.einsum(
        "mphd,nphd->mnhp", grad_heads, value_heads, preferred_element_type=jnp.float32
    )
    dscore = (soft * (dprob - jnp.sum(soft * dprob, axis=1, keepdims=True))).astype(jnp.bfloat16)
    query_grad = (
        jnp.einsum("mnhp,nphd->mphd", dscore, key_heads, preferred_element_type=jnp.float32)
        * score_scale
    )
    query_grad = query_grad.reshape(query_raw.shape)
    key_grad = (
        jnp.einsum("mnhp,mphd->nphd", dscore, query_heads, preferred_element_type=jnp.float32)
        * score_scale
    )
    key_grad = key_grad.reshape(key_raw.shape)
    value_grad = jnp.einsum(
        "mnhp,mphd->nphd", rounded, grad_heads, preferred_element_type=jnp.float32
    )
    value_grad = value_grad.reshape(key_raw.shape)
    grad_query_raw = head_pullback(query_raw, query_grad)
    grad_key_raw = head_pullback(key_raw, key_grad)
    grad_proj = jnp.concatenate([grad_query_raw, grad_key_raw, value_grad], axis=-1).astype(
        jnp.bfloat16
    )
    grad_proj = lax.all_to_all(grad_proj, "member", split_axis=0, concat_axis=1, tiled=True)
    grad_normed = jnp.einsum(
        "mpe,ce->mpc", grad_proj, project_weight, preferred_element_type=jnp.float32
    )
    _, pull_norm = jax.vjp(lambda t: row_norm(t, norm_gain), inputs)
    grad_inputs = pull_norm(grad_normed)[0]
    grad_ensemble = (
        (grad_rows + grad_inputs).astype(jnp.bfloat16).reshape(mem_dev, lat_dev, lon_dev, channels)
    )
    return (result, grad_ensemble)


F32 = jnp.float32
BF16 = jnp.bfloat16
VMEM_LIMIT = 48 * 1024 * 1024


def is_even(axis):
    return lax.rem(lax.axis_index(axis), 2) == 0


def stack_kernel(ens_ref, cot_ref, both_ref, first_ref, second_ref, sems):
    _, mem, rows, _, _ = both_ref.shape
    copies = [
        pltpu.make_async_copy(ref, both_ref.at[i], sems.at[i])
        for i, ref in enumerate((ens_ref, cot_ref))
    ]
    for copy in copies:
        copy.start()
    for copy in copies:
        copy.wait()
    even = is_even("lat")
    for array in range(2):
        for member in range(mem):
            first_ref[array, member] = both_ref[array, member, jnp.where(even, rows - 1, 0)]
            second_ref[array, member] = both_ref[array, member, jnp.where(even, 0, rows - 1)]


def pack_strips_kernel(
    both_ref,
    other_ref,
    first_ref,
    second_ref,
    cross_first_ref,
    cross_second_ref,
    after_ref,
    halo_ref,
    core_ref,
    chip_ref,
    low_scr,
    high_scr,
    *,
    lat_count,
):
    _, mem, rows, cols, _ = both_ref.shape
    lat_even = is_even("lat")
    lat = lax.axis_index("lat")
    index = 0
    for array in range(2):
        for member in range(2 * mem):
            if member < mem:
                block, at = both_ref, member
                first, second = first_ref[array, at], second_ref[array, at]
            else:
                block, at = other_ref, member - mem
                first, second = cross_first_ref[array, at], cross_second_ref[array, at]
            first, second = first.astype(F32), second.astype(F32)
            north = jnp.where(lat == 0, 0.0, jnp.where(lat_even, second, first))
            south = jnp.where(lat == lat_count - 1, 0.0, jnp.where(lat_even, first, second))
            halo_ref[0, array, member] = north.astype(BF16)
            halo_ref[1, array, member] = south.astype(BF16)
            slabs = [block[array, at, row].astype(F32) for row in range(rows)]
            for slab in [north] + slabs + [south]:
                low_scr[index : index + 1, :] = slab[0:1]
                high_scr[index : index + 1, :] = slab[cols - 1 : cols]
                index += 1
    even = is_even("lon")
    low, high = low_scr[...], high_scr[...]
    core_ref[...] = jnp.where(even, high, low).astype(BF16)
    chip_ref[...] = jnp.where(even, low, high).astype(BF16)


def dot_nn(a, b):
    return lax.dot_general(a, b, (((1,), (0,)), ((), ())), preferred_element_type=F32)


def same_head_matrix(channels):
    width = channels // HEAD_COUNT
    lane_row = lax.broadcasted_iota(jnp.int32, (channels, channels), 0) // width
    lane_col = lax.broadcasted_iota(jnp.int32, (channels, channels), 1) // width
    return jnp.where(lane_row == lane_col, 1.0, 0.0).astype(BF16)


def head_sums(values, same_head):
    high = values.astype(BF16)
    low = (values - high.astype(F32)).astype(BF16)
    return dot_nn(high, same_head) + dot_nn(low, same_head)


def head_unit(raw, same_head):
    raw = raw.astype(F32)
    mean_sq = head_sums(raw * raw, same_head) * (HEAD_COUNT / raw.shape[-1])
    inverse = lax.rsqrt(jnp.maximum(mean_sq, FLOOR))
    return raw, mean_sq, inverse, (raw * inverse).astype(BF16)


def row_rsqrt(values):
    return lax.rsqrt(jnp.mean(values * values, axis=-1, keepdims=True) + EPSILON)


def attend(query, keys, values, same_head, scale):
    exps = [jnp.exp(dot_nn(query * key, same_head) * scale) for key in keys]
    total = exps[0]
    for e in exps[1:]:
        total = total + e
    inverse = 1.0 / total
    probs = [e * inverse for e in exps]
    mixed = None
    if values is not None:
        for prob, value in zip(probs, values):
            term = prob.astype(BF16).astype(F32) * value.astype(F32)
            mixed = term if mixed is None else mixed + term
        mixed = mixed.astype(BF16)
    return probs, mixed


def weights_kernel(
    gain_hbm,
    project_hbm,
    output_hbm,
    conv_hbm,
    gain_ref,
    project_ref,
    output_ref,
    conv_ref,
    project_t_ref,
    output_t_ref,
    conv_t_ref,
    sems,
):
    channels = output_ref.shape[0]
    loads = [
        pltpu.make_async_copy(source, target, sems.at[i])
        for i, (source, target) in enumerate(
            (
                (gain_hbm, gain_ref),
                (project_hbm, project_ref),
                (output_hbm, output_ref),
                (conv_hbm, conv_ref),
            )
        )
    ]
    for load in loads:
        load.start()
    loads[0].wait()
    loads[1].wait()
    for kind in range(3):
        lanes = slice(kind * channels, (kind + 1) * channels)
        project_t_ref[lanes, :] = project_ref[:, lanes].T
    loads[2].wait()
    output_t_ref[...] = output_ref[...].T
    loads[3].wait()
    for r in range(3):
        for c in range(3):
            tap = (3 * r + c) * channels
            turned = (3 * r + 2 - c) * channels
            conv_t_ref[turned : turned + channels, :] = conv_ref[tap : tap + channels, :].T


def own_kernel(
    both_ref,
    other_ref,
    gain_ref,
    project_ref,
    output_ref,
    proj_ref,
    unit_ref,
    soft_ref,
    inverse_ref,
    pull_ref,
    updated_ref,
):
    _, mem, rows, cols, channels = both_ref.shape
    groups = 2 * mem
    cells = rows * cols
    width = channels // HEAD_COUNT
    scale = 1.0 / math.sqrt(width)
    same_head = same_head_matrix(channels)
    own = both_ref[0].reshape(mem * cells, channels)
    other = other_ref[0].reshape(mem * cells, channels)
    x = jnp.concatenate([own, other], axis=0).astype(F32)
    normed = (x * row_rsqrt(x) * gain_ref[...]).astype(BF16)
    proj_ref[...] = (
        dot_nn(normed, project_ref[...]).astype(BF16).reshape(groups, cells, 3 * channels)
    )
    for kind in range(2):
        for member in range(groups):
            lanes = slice(kind * channels, (kind + 1) * channels)
            raw, mean_sq, inverse, unit = head_unit(proj_ref[member, :, lanes], same_head)
            unit_ref[kind, member] = unit
            if member < mem:
                active = jnp.where(mean_sq > FLOOR, 1.0, jnp.where(mean_sq == FLOOR, 0.5, 0.0))
                inverse_ref[kind, member] = inverse
                pull_ref[kind, member] = active * raw * (inverse * inverse * inverse) / width
    keys = [unit_ref[1, n] for n in range(groups)]
    values = [proj_ref[n, :, 2 * channels :] for n in range(groups)]
    for m in range(groups):
        probs, mixed = attend(unit_ref[0, m], keys, values if m < mem else None, same_head, scale)
        for n in range(groups):
            soft_ref[m * groups + n] = probs[n]
        if m < mem:
            x = both_ref[0, m].reshape(cells, channels).astype(F32)
            updated_ref[m] = (x + dot_nn(mixed, output_ref[...])).astype(BF16)


def main_kernel(
    both_ref,
    other_ref,
    halo_ref,
    core_ref,
    chip_ref,
    gain_ref,
    project_ref,
    output_ref,
    conv_ref,
    project_t_ref,
    output_t_ref,
    conv_t_ref,
    proj_ref,
    unit_ref,
    soft_ref,
    inverse_ref,
    pull_ref,
    updated_ref,
    result_ref,
    grad_ref,
    x_scr,
    cot_scr,
    proj_scr,
    shift_scr,
    cot_shift_scr,
):
    _, mem, rows, cols, channels = both_ref.shape
    groups = 2 * mem
    tall = rows + 2
    centre = tall * cols
    cells = rows * cols
    rim = x_scr.shape[1]
    width = channels // HEAD_COUNT
    scale = 1.0 / math.sqrt(width)
    even = is_even("lon")
    core, chip = core_ref[...].astype(F32), chip_ref[...].astype(F32)
    low, high = jnp.where(even, chip, core), jnp.where(even, core, chip)

    for array, scr in enumerate((x_scr, cot_scr)):
        for member in range(groups):
            top = halo_ref[0, array, member].astype(F32)
            bottom = halo_ref[1, array, member].astype(F32)
            if array == 0:
                scr[member, :cols, :] = top
                scr[member, cols : 2 * cols, :] = bottom
                edge = 2 * cols
            else:
                ref, at = (both_ref, member) if member < mem else (other_ref, member - mem)
                scr[member, :cols, :] = top
                scr[member, cols : cols + cells, :] = (
                    ref[1, at].reshape(cells, channels).astype(F32)
                )
                scr[member, cols + cells : centre, :] = bottom
                edge = centre
            scr[member, edge:, :] = jnp.zeros((16, channels), F32)
            slot = (array * groups + member) * tall
            scr[member, edge : edge + tall, :] = low[slot : slot + tall]
            scr[member, edge + 8 : edge + 8 + tall, :] = high[slot : slot + tall]

    same_head = same_head_matrix(channels)
    gain = gain_ref[...]

    x_all = x_scr[...].reshape(groups * rim, channels)
    normed = (x_all * row_rsqrt(x_all) * gain).astype(BF16)
    proj_scr[...] = dot_nn(normed, project_ref[...]).astype(BF16)
    keys = [
        head_unit(proj_scr[n * rim : (n + 1) * rim, channels : 2 * channels], same_head)[3]
        for n in range(groups)
    ]
    values = [proj_scr[n * rim : (n + 1) * rim, 2 * channels :] for n in range(groups)]
    updated = []
    for m in range(mem):
        query = head_unit(proj_scr[m * rim : (m + 1) * rim, :channels], same_head)[3]
        _, mixed = attend(query, keys, values, same_head, scale)
        field = (x_scr[m] + dot_nn(mixed, output_ref[...])).astype(BF16).astype(F32)
        updated.append(
            jnp.concatenate(
                [field[:cols], updated_ref[m].astype(F32), field[cols:]],
                axis=0,
            )
        )

    def shifted(scr, member, field):
        column = lax.broadcasted_iota(jnp.int32, (cols, channels), 0)
        for place in range(tall):
            slab = field[place * cols : (place + 1) * cols]
            west = field[centre + place : centre + place + 1]
            east = field[centre + 8 + place : centre + 8 + place + 1]
            back = jnp.where(column == 0, west, pltpu.roll(slab, 1, 0))
            ahead = jnp.where(column == cols - 1, east, pltpu.roll(slab, cols - 1, 0))
            rows_at = slice(place * cols, (place + 1) * cols)
            scr[member, rows_at, :channels] = back.astype(BF16)
            scr[member, rows_at, channels : 2 * channels] = slab.astype(BF16)
            scr[member, rows_at, 2 * channels :] = ahead.astype(BF16)

    for member in range(mem):
        shifted(shift_scr, member, updated[member])
    for member in range(groups):
        shifted(cot_shift_scr, member, cot_scr[member])

    total = updated_ref[...].reshape(mem * cells, channels).astype(F32)
    for r in range(3):
        window = jnp.concatenate(
            [shift_scr[m, r * cols : r * cols + cells, :] for m in range(mem)], axis=0
        )
        total = total + dot_nn(window, conv_ref[3 * channels * r : 3 * channels * (r + 1), :])
    result_ref[...] = total.astype(BF16).reshape(mem, rows, cols, channels)

    total = jnp.concatenate([cot_scr[m, cols : cols + cells, :] for m in range(groups)], axis=0)
    for r in range(3):
        begin = (2 - r) * cols
        window = jnp.concatenate(
            [cot_shift_scr[m, begin : begin + cells, :] for m in range(groups)], axis=0
        )
        total = total + dot_nn(window, conv_t_ref[3 * channels * r : 3 * channels * (r + 1), :])
    grad_field = total
    grad_mixed = dot_nn(grad_field.astype(BF16), output_t_ref[...]).astype(BF16)
    grads = [grad_mixed[m * cells : (m + 1) * cells] for m in range(groups)]

    values = [proj_ref[n, :, 2 * channels :] for n in range(groups)]
    query_grad = [None] * mem
    key_grad = [None] * mem
    value_grad = [None] * mem
    for m in range(groups):
        soft = [soft_ref[m * groups + n] for n in range(groups)]
        dprob = [dot_nn(grads[m] * values[n], same_head) for n in range(groups)]
        mean = soft[0] * dprob[0]
        for n in range(1, groups):
            mean = mean + soft[n] * dprob[n]
        for n in range(groups):
            if m >= mem and n >= mem:
                continue
            dscore = (soft[n] * (dprob[n] - mean)).astype(BF16).astype(F32)
            if m < mem:
                term = dscore * unit_ref[1, n].astype(F32)
                query_grad[m] = term if query_grad[m] is None else query_grad[m] + term
            if n < mem:
                term = dscore * unit_ref[0, m].astype(F32)
                key_grad[n] = term if key_grad[n] is None else key_grad[n] + term
                term = soft[n].astype(BF16).astype(F32) * grads[m].astype(F32)
                value_grad[n] = term if value_grad[n] is None else value_grad[n] + term

    def head_pull(kind, member, grad):
        grad = grad * scale
        raw = proj_ref[member, :, kind * channels : (kind + 1) * channels].astype(F32)
        inner = head_sums(grad * raw, same_head)
        return inverse_ref[kind, member] * grad - pull_ref[kind, member] * inner

    for m in range(mem):
        grad_proj = jnp.concatenate(
            [
                head_pull(0, m, query_grad[m]).astype(BF16),
                head_pull(1, m, key_grad[m]).astype(BF16),
                value_grad[m].astype(BF16),
            ],
            axis=1,
        )
        grad_normed = dot_nn(grad_proj, project_t_ref[...]) * gain
        x = both_ref[0, m].reshape(cells, channels).astype(F32)
        inverse = row_rsqrt(x)
        inner = jnp.mean(x * grad_normed, axis=-1, keepdims=True)
        pulled = inverse * grad_normed - x * (inverse * inverse * inverse * inner)
        total = grad_field[m * cells : (m + 1) * cells] + pulled
        grad_ref[m] = total.astype(BF16).reshape(rows, cols, channels)


def local_call(kernel, name, operands, out_shape, scratch, pinned=False, cost=None):
    whole = pl.BlockSpec(memory_space=pltpu.VMEM)
    anywhere = pl.BlockSpec(memory_space=pl.ANY)
    specs = [anywhere if in_hbm else whole for _, in_hbm in operands]
    arrays = [
        pltpu.with_memory_space_constraint(array, pltpu.HBM) if in_hbm else array
        for array, in_hbm in operands
    ]

    def keep(shape):
        return pltpu.VMEM(shape.shape, shape.dtype) if pinned else shape

    return pl.pallas_call(
        kernel,
        out_shape=jax.tree.map(keep, out_shape),
        in_specs=specs,
        out_specs=jax.tree.map(lambda _: whole, out_shape),
        scratch_shapes=scratch,
        compiler_params=pltpu.CompilerParams(vmem_limit_bytes=VMEM_LIMIT),
        cost_estimate=cost,
        name=name,
    )(*arrays)


def here(*arrays):
    return [(array, False) for array in arrays]


def in_hbm(*arrays):
    return [(array, True) for array in arrays]


def per_device_paired(ensemble, norm_gain, project_weight, output_weight, conv_kernel, cotangent):
    mem, rows, cols, channels = ensemble.shape
    groups = 2 * mem
    cells = rows * cols
    tall = rows + 2
    lon_count = lax.axis_size("lon")
    lat_count = lax.axis_size("lat")
    bf16 = functools.partial(jax.ShapeDtypeStruct, dtype=BF16)
    f32 = functools.partial(jax.ShapeDtypeStruct, dtype=F32)
    row = (2, mem, cols, channels)
    swap = [(0, 1), (1, 0)]
    core_pairs = [(i, i ^ 1) for i in range(lon_count)]
    chip_pairs = [(i, (i - 1 if i % 2 == 0 else i + 1) % lon_count) for i in range(lon_count)]

    def lat_partner(lat, offset):
        partner = lat + 1 if lat % 2 == offset else lat - 1
        if lat_count % 2 == 0:
            return partner % lat_count
        return partner if 0 <= partner < lat_count else lat

    def cross_pairs(offset):
        lats = range(lat_count)
        return [
            (m * lat_count + lat, (1 - m) * lat_count + lat_partner(lat, offset))
            for m in (0, 1)
            for lat in lats
        ]

    both, first_send, second_send = local_call(
        stack_kernel,
        "stack",
        in_hbm(ensemble, cotangent),
        (bf16((2,) + ensemble.shape), bf16(row), bf16(row)),
        [pltpu.SemaphoreType.DMA((2,))],
        pinned=True,
    )
    other = lax.ppermute(both, "member", swap)
    lats = range(lat_count)
    first = lax.ppermute(first_send, "lat", [(i, lat_partner(i, 0)) for i in lats])
    second = lax.ppermute(second_send, "lat", [(i, lat_partner(i, 1)) for i in lats])
    cross_first = lax.ppermute(first_send, ("member", "lat"), cross_pairs(0))
    cross_second = lax.ppermute(second_send, ("member", "lat"), cross_pairs(1))

    weights = (
        norm_gain.reshape(1, channels),
        project_weight,
        output_weight,
        conv_kernel.reshape(9 * channels, channels),
    )
    weights = local_call(
        weights_kernel,
        "load_weights",
        in_hbm(*weights),
        tuple(jax.ShapeDtypeStruct(w.shape, w.dtype) for w in weights)
        + (
            bf16((3 * channels, channels)),
            bf16((channels, channels)),
            bf16((9 * channels, channels)),
        ),
        [pltpu.SemaphoreType.DMA((4,))],
        pinned=True,
        cost=pl.CostEstimate(flops=20_000_000_000, bytes_accessed=4_000_000, transcendentals=0),
    )
    strip = (2 * groups * tall, channels)
    halo, core_send, chip_send = local_call(
        functools.partial(pack_strips_kernel, lat_count=lat_count),
        "pack_strips",
        here(both, other, first, second, cross_first, cross_second, weights[0]),
        (bf16((2, 2, groups, cols, channels)), bf16(strip), bf16(strip)),
        [pltpu.VMEM(strip, F32)] * 2,
    )
    core = lax.ppermute(core_send, "lon", core_pairs)
    chip = lax.ppermute(chip_send, "lon", chip_pairs)

    held = local_call(
        own_kernel,
        "own_cells",
        here(both, other, *weights[:3]),
        (
            bf16((groups, cells, 3 * channels)),
            bf16((2, groups, cells, channels)),
            f32((groups * groups, cells, channels)),
            f32((2, mem, cells, channels)),
            f32((2, mem, cells, channels)),
            bf16((mem, cells, channels)),
        ),
        [],
        pinned=True,
    )

    rim = 2 * cols + 16
    return local_call(
        main_kernel,
        "main",
        here(both, other, halo, core, chip, *weights, *held),
        (bf16(ensemble.shape), bf16(ensemble.shape)),
        [
            pltpu.VMEM((groups, rim, channels), F32),
            pltpu.VMEM((groups, tall * cols + 16, channels), F32),
            pltpu.VMEM((groups * rim, 3 * channels), BF16),
            pltpu.VMEM((mem, tall * cols, 3 * channels), BF16),
            pltpu.VMEM((groups, tall * cols, 3 * channels), BF16),
        ],
    )


def solution(mesh):
    paired = mesh.shape["member"] == 2 and mesh.shape["lon"] % 2 == 0
    per_device = per_device_paired if paired else per_device_general
    in_specs = (
        P("member", "lat", "lon", None),
        P(),
        P(),
        P(),
        P(),
        P("member", "lat", "lon", None),
    )
    out_specs = (P("member", "lat", "lon", None), P("member", "lat", "lon", None))
    return jax.shard_map(
        per_device, mesh=mesh, in_specs=in_specs, out_specs=out_specs, check_vma=False
    )
```

```python
import functools
import math

import jax
import jax.numpy as jnp
from jax import lax
from jax.experimental import pallas as pl
from jax.experimental.pallas import tpu as pltpu
from jax.sharding import PartitionSpec as P

HEAD_COUNT = 8


FLOOR = 0.5
EPSILON = 1e-06


def padded_2(block, sides, width, periodic):
    for axis, dim in sides:
        count = lax.axis_size(axis)
        forward = [(i, i + 1) for i in range(count - 1)]
        if periodic:
            forward.append((count - 1, 0))
        backward = [(target, source) for source, target in forward]
        low = lax.ppermute(
            lax.slice_in_dim(block, block.shape[dim] - width, None, axis=dim), axis, forward
        )
        high = lax.ppermute(lax.slice_in_dim(block, 0, width, axis=dim), axis, backward)
        block = jnp.concatenate([low, block, high], axis=dim)
    return block


def row_norm(values, gain_vec):
    mean_sq = jnp.mean(values * values, axis=-1, keepdims=True)
    return values * lax.rsqrt(mean_sq + EPSILON) * gain_vec


def head_norm(values, head_count):
    shaped = values.reshape(values.shape[:-1] + (head_count, values.shape[-1] // head_count))
    mean_sq = jnp.mean(shaped * shaped, axis=-1, keepdims=True)
    return (shaped * lax.rsqrt(jnp.maximum(mean_sq, FLOOR))).reshape(values.shape)


def split_heads(values, head_count):
    return values.reshape(values.shape[:-1] + (head_count, values.shape[-1] // head_count))


def head_pullback(raw_rows, grad_rows):
    _, pullback = jax.vjp(lambda t: head_norm(t, HEAD_COUNT), raw_rows.astype(jnp.float32))
    return pullback(grad_rows)[0]


def pad_field(field_in):
    widened = padded_2(field_in, (("lon", 2),), 1, True)
    return padded_2(widened, (("lat", 1),), 1, False)


def conv_taps(padded, kernel, lat_n, lon_n, adjoint):
    running = None
    for row_off in range(3):
        for col_off in range(3):
            if adjoint:
                window = padded[
                    :, 2 - row_off : 2 - row_off + lat_n, 2 - col_off : 2 - col_off + lon_n
                ]
                summand = jnp.einsum(
                    "mabc,dc->mabd",
                    window,
                    kernel[row_off, col_off],
                    preferred_element_type=jnp.float32,
                )
            else:
                window = padded[:, row_off : row_off + lat_n, col_off : col_off + lon_n]
                summand = jnp.einsum(
                    "mabc,cd->mabd",
                    window,
                    kernel[row_off, col_off],
                    preferred_element_type=jnp.float32,
                )
            running = summand if running is None else running + summand
    return running


def per_device_general(ensemble, norm_gain, project_weight, output_weight, conv_kernel, cotangent):
    mem_dev, lat_dev, lon_dev, channels = ensemble.shape
    cell_count = lat_dev * lon_dev
    score_scale = 1.0 / math.sqrt(channels // HEAD_COUNT)
    inputs = ensemble.reshape(mem_dev, cell_count, channels).astype(jnp.float32)
    normed = row_norm(inputs, norm_gain).astype(jnp.bfloat16)
    spread = lax.all_to_all(normed, "member", split_axis=1, concat_axis=0, tiled=True)
    projected = jnp.dot(spread, project_weight, preferred_element_type=jnp.float32).astype(
        jnp.bfloat16
    )
    query_raw = projected[..., :channels]
    key_raw = projected[..., channels : 2 * channels]
    value_rows = projected[..., 2 * channels :]
    key_rows = head_norm(key_raw.astype(jnp.float32), HEAD_COUNT).astype(jnp.bfloat16)
    queries = head_norm(query_raw.astype(jnp.float32), HEAD_COUNT).astype(jnp.bfloat16)
    query_heads = split_heads(queries, HEAD_COUNT)
    key_heads = split_heads(key_rows, HEAD_COUNT)
    value_heads = split_heads(value_rows, HEAD_COUNT)
    scores = (
        jnp.einsum("mphd,nphd->mnhp", query_heads, key_heads, preferred_element_type=jnp.float32)
        * score_scale
    )
    expd = jnp.exp(scores)
    soft = expd / jnp.sum(expd, axis=1, keepdims=True)
    rounded = soft.astype(jnp.bfloat16)
    mixed_out = jnp.einsum(
        "mnhp,nphd->mphd", rounded, value_heads, preferred_element_type=jnp.float32
    )
    mixed_out = mixed_out.reshape(query_raw.shape).astype(jnp.bfloat16)
    mixed_out = lax.all_to_all(mixed_out, "member", split_axis=0, concat_axis=1, tiled=True)
    updated = (
        inputs + jnp.dot(mixed_out, output_weight, preferred_element_type=jnp.float32)
    ).astype(jnp.bfloat16)
    field_up = updated.reshape(mem_dev, lat_dev, lon_dev, channels)
    result = field_up.astype(jnp.float32) + conv_taps(
        pad_field(field_up), conv_kernel, lat_dev, lon_dev, False
    )
    result = result.astype(jnp.bfloat16)
    grad_field = cotangent.astype(jnp.float32) + conv_taps(
        pad_field(cotangent), conv_kernel, lat_dev, lon_dev, True
    )
    grad_rows = grad_field.reshape(mem_dev, cell_count, channels)
    grad_mixed = jnp.einsum(
        "mpc,dc->mpd",
        grad_rows.astype(jnp.bfloat16),
        output_weight,
        preferred_element_type=jnp.float32,
    )
    grad_mixed = grad_mixed.astype(jnp.bfloat16)
    grad_mixed = lax.all_to_all(grad_mixed, "member", split_axis=1, concat_axis=0, tiled=True)
    grad_heads = split_heads(grad_mixed, HEAD_COUNT)
    dprob = jnp.einsum(
        "mphd,nphd->mnhp", grad_heads, value_heads, preferred_element_type=jnp.float32
    )
    dscore = (soft * (dprob - jnp.sum(soft * dprob, axis=1, keepdims=True))).astype(jnp.bfloat16)
    query_grad = (
        jnp.einsum("mnhp,nphd->mphd", dscore, key_heads, preferred_element_type=jnp.float32)
        * score_scale
    )
    query_grad = query_grad.reshape(query_raw.shape)
    key_grad = (
        jnp.einsum("mnhp,mphd->nphd", dscore, query_heads, preferred_element_type=jnp.float32)
        * score_scale
    )
    key_grad = key_grad.reshape(key_raw.shape)
    value_grad = jnp.einsum(
        "mnhp,mphd->nphd", rounded, grad_heads, preferred_element_type=jnp.float32
    )
    value_grad = value_grad.reshape(key_raw.shape)
    grad_query_raw = head_pullback(query_raw, query_grad)
    grad_key_raw = head_pullback(key_raw, key_grad)
    grad_proj = jnp.concatenate([grad_query_raw, grad_key_raw, value_grad], axis=-1).astype(
        jnp.bfloat16
    )
    grad_proj = lax.all_to_all(grad_proj, "member", split_axis=0, concat_axis=1, tiled=True)
    grad_normed = jnp.einsum(
        "mpe,ce->mpc", grad_proj, project_weight, preferred_element_type=jnp.float32
    )
    _, pull_norm = jax.vjp(lambda t: row_norm(t, norm_gain), inputs)
    grad_inputs = pull_norm(grad_normed)[0]
    grad_ensemble = (
        (grad_rows + grad_inputs).astype(jnp.bfloat16).reshape(mem_dev, lat_dev, lon_dev, channels)
    )
    return (result, grad_ensemble)


F32 = jnp.float32
BF16 = jnp.bfloat16
VMEM_LIMIT = 48 * 1024 * 1024


def is_even(axis):
    return lax.rem(lax.axis_index(axis), 2) == 0


def stack_kernel(ens_ref, cot_ref, both_ref, first_ref, second_ref, sems):
    _, mem, rows, _, _ = both_ref.shape
    copies = [
        pltpu.make_async_copy(ref, both_ref.at[i], sems.at[i])
        for i, ref in enumerate((ens_ref, cot_ref))
    ]
    for copy in copies:
        copy.start()
    for copy in copies:
        copy.wait()
    even = is_even("lat")
    for array in range(2):
        for member in range(mem):
            first_ref[array, member] = both_ref[array, member, jnp.where(even, rows - 1, 0)]
            second_ref[array, member] = both_ref[array, member, jnp.where(even, 0, rows - 1)]


def pack_strips_kernel(
    both_ref,
    other_ref,
    first_ref,
    second_ref,
    cross_first_ref,
    cross_second_ref,
    after_ref,
    halo_ref,
    core_ref,
    chip_ref,
    low_scr,
    high_scr,
    *,
    lat_count,
):
    _, mem, rows, cols, _ = both_ref.shape
    lat_even = is_even("lat")
    lat = lax.axis_index("lat")
    index = 0
    for array in range(2):
        for member in range(2 * mem):
            if member < mem:
                block, at = both_ref, member
                first, second = first_ref[array, at], second_ref[array, at]
            else:
                block, at = other_ref, member - mem
                first, second = cross_first_ref[array, at], cross_second_ref[array, at]
            first, second = first.astype(F32), second.astype(F32)
            north = jnp.where(lat == 0, 0.0, jnp.where(lat_even, second, first))
            south = jnp.where(lat == lat_count - 1, 0.0, jnp.where(lat_even, first, second))
            halo_ref[0, array, member] = north.astype(BF16)
            halo_ref[1, array, member] = south.astype(BF16)
            slabs = [block[array, at, row].astype(F32) for row in range(rows)]
            for slab in [north] + slabs + [south]:
                low_scr[index : index + 1, :] = slab[0:1]
                high_scr[index : index + 1, :] = slab[cols - 1 : cols]
                index += 1
    even = is_even("lon")
    low, high = low_scr[...], high_scr[...]
    core_ref[...] = jnp.where(even, high, low).astype(BF16)
    chip_ref[...] = jnp.where(even, low, high).astype(BF16)


def dot_nn(a, b):
    return lax.dot_general(a, b, (((1,), (0,)), ((), ())), preferred_element_type=F32)


def same_head_matrix(channels):
    width = channels // HEAD_COUNT
    lane_row = lax.broadcasted_iota(jnp.int32, (channels, channels), 0) // width
    lane_col = lax.broadcasted_iota(jnp.int32, (channels, channels), 1) // width
    return jnp.where(lane_row == lane_col, 1.0, 0.0).astype(BF16)


def head_sums(values, same_head):
    high = values.astype(BF16)
    low = (values - high.astype(F32)).astype(BF16)
    return dot_nn(high, same_head) + dot_nn(low, same_head)


def head_unit(raw, same_head):
    raw = raw.astype(F32)
    mean_sq = head_sums(raw * raw, same_head) * (HEAD_COUNT / raw.shape[-1])
    inverse = lax.rsqrt(jnp.maximum(mean_sq, FLOOR))
    return raw, mean_sq, inverse, (raw * inverse).astype(BF16)


def row_rsqrt(values):
    return lax.rsqrt(jnp.mean(values * values, axis=-1, keepdims=True) + EPSILON)


def attend(query, keys, values, same_head, scale):
    exps = [jnp.exp(dot_nn(query * key, same_head) * scale) for key in keys]
    total = exps[0]
    for e in exps[1:]:
        total = total + e
    inverse = 1.0 / total
    probs = [e * inverse for e in exps]
    mixed = None
    if values is not None:
        for prob, value in zip(probs, values):
            term = prob.astype(BF16).astype(F32) * value.astype(F32)
            mixed = term if mixed is None else mixed + term
        mixed = mixed.astype(BF16)
    return probs, mixed


def weights_kernel(
    gain_hbm,
    project_hbm,
    output_hbm,
    conv_hbm,
    gain_ref,
    project_ref,
    output_ref,
    conv_ref,
    project_t_ref,
    output_t_ref,
    conv_t_ref,
    sems,
):
    channels = output_ref.shape[0]
    loads = [
        pltpu.make_async_copy(source, target, sems.at[i])
        for i, (source, target) in enumerate(
            (
                (gain_hbm, gain_ref),
                (project_hbm, project_ref),
                (output_hbm, output_ref),
                (conv_hbm, conv_ref),
            )
        )
    ]
    for load in loads:
        load.start()
    loads[0].wait()
    loads[1].wait()
    for kind in range(3):
        lanes = slice(kind * channels, (kind + 1) * channels)
        project_t_ref[lanes, :] = project_ref[:, lanes].T
    loads[2].wait()
    output_t_ref[...] = output_ref[...].T
    loads[3].wait()
    for r in range(3):
        for c in range(3):
            tap = (3 * r + c) * channels
            turned = (3 * r + 2 - c) * channels
            conv_t_ref[turned : turned + channels, :] = conv_ref[tap : tap + channels, :].T


def own_kernel(
    both_ref,
    other_ref,
    gain_ref,
    project_ref,
    output_ref,
    proj_ref,
    unit_ref,
    soft_ref,
    inverse_ref,
    pull_ref,
    updated_ref,
):
    _, mem, rows, cols, channels = both_ref.shape
    groups = 2 * mem
    cells = rows * cols
    width = channels // HEAD_COUNT
    scale = 1.0 / math.sqrt(width)
    same_head = same_head_matrix(channels)
    own = both_ref[0].reshape(mem * cells, channels)
    other = other_ref[0].reshape(mem * cells, channels)
    x = jnp.concatenate([own, other], axis=0).astype(F32)
    normed = (x * row_rsqrt(x) * gain_ref[...]).astype(BF16)
    proj_ref[...] = (
        dot_nn(normed, project_ref[...]).astype(BF16).reshape(groups, cells, 3 * channels)
    )
    for kind in range(2):
        for member in range(groups):
            lanes = slice(kind * channels, (kind + 1) * channels)
            raw, mean_sq, inverse, unit = head_unit(proj_ref[member, :, lanes], same_head)
            unit_ref[kind, member] = unit
            if member < mem:
                active = jnp.where(mean_sq > FLOOR, 1.0, jnp.where(mean_sq == FLOOR, 0.5, 0.0))
                inverse_ref[kind, member] = inverse
                pull_ref[kind, member] = active * raw * (inverse * inverse * inverse) / width
    keys = [unit_ref[1, n] for n in range(groups)]
    values = [proj_ref[n, :, 2 * channels :] for n in range(groups)]
    for m in range(groups):
        probs, mixed = attend(unit_ref[0, m], keys, values if m < mem else None, same_head, scale)
        for n in range(groups):
            soft_ref[m * groups + n] = probs[n]
        if m < mem:
            x = both_ref[0, m].reshape(cells, channels).astype(F32)
            updated_ref[m] = (x + dot_nn(mixed, output_ref[...])).astype(BF16)


def main_kernel(
    both_ref,
    other_ref,
    halo_ref,
    core_ref,
    chip_ref,
    gain_ref,
    project_ref,
    output_ref,
    conv_ref,
    project_t_ref,
    output_t_ref,
    conv_t_ref,
    proj_ref,
    unit_ref,
    soft_ref,
    inverse_ref,
    pull_ref,
    updated_ref,
    result_ref,
    grad_ref,
    x_scr,
    cot_scr,
    proj_scr,
    shift_scr,
    cot_shift_scr,
):
    _, mem, rows, cols, channels = both_ref.shape
    groups = 2 * mem
    tall = rows + 2
    centre = tall * cols
    cells = rows * cols
    rim = x_scr.shape[1]
    width = channels // HEAD_COUNT
    scale = 1.0 / math.sqrt(width)
    even = is_even("lon")
    core, chip = core_ref[...].astype(F32), chip_ref[...].astype(F32)
    low, high = jnp.where(even, chip, core), jnp.where(even, core, chip)

    for array, scr in enumerate((x_scr, cot_scr)):
        for member in range(groups):
            top = halo_ref[0, array, member].astype(F32)
            bottom = halo_ref[1, array, member].astype(F32)
            if array == 0:
                scr[member, :cols, :] = top
                scr[member, cols : 2 * cols, :] = bottom
                edge = 2 * cols
            else:
                ref, at = (both_ref, member) if member < mem else (other_ref, member - mem)
                scr[member, :cols, :] = top
                scr[member, cols : cols + cells, :] = (
                    ref[1, at].reshape(cells, channels).astype(F32)
                )
                scr[member, cols + cells : centre, :] = bottom
                edge = centre
            scr[member, edge:, :] = jnp.zeros((16, channels), F32)
            slot = (array * groups + member) * tall
            scr[member, edge : edge + tall, :] = low[slot : slot + tall]
            scr[member, edge + 8 : edge + 8 + tall, :] = high[slot : slot + tall]

    same_head = same_head_matrix(channels)
    gain = gain_ref[...]

    x_all = x_scr[...].reshape(groups * rim, channels)
    normed = (x_all * row_rsqrt(x_all) * gain).astype(BF16)
    proj_scr[...] = dot_nn(normed, project_ref[...]).astype(BF16)
    keys = [
        head_unit(proj_scr[n * rim : (n + 1) * rim, channels : 2 * channels], same_head)[3]
        for n in range(groups)
    ]
    values = [proj_scr[n * rim : (n + 1) * rim, 2 * channels :] for n in range(groups)]
    updated = []
    for m in range(mem):
        query = head_unit(proj_scr[m * rim : (m + 1) * rim, :channels], same_head)[3]
        _, mixed = attend(query, keys, values, same_head, scale)
        field = (x_scr[m] + dot_nn(mixed, output_ref[...])).astype(BF16).astype(F32)
        updated.append(
            jnp.concatenate(
                [field[:cols], updated_ref[m].astype(F32), field[cols:]],
                axis=0,
            )
        )

    def shifted(scr, member, field):
        column = lax.broadcasted_iota(jnp.int32, (cols, channels), 0)
        for place in range(tall):
            slab = field[place * cols : (place + 1) * cols]
            west = field[centre + place : centre + place + 1]
            east = field[centre + 8 + place : centre + 8 + place + 1]
            back = jnp.where(column == 0, west, pltpu.roll(slab, 1, 0))
            ahead = jnp.where(column == cols - 1, east, pltpu.roll(slab, cols - 1, 0))
            rows_at = slice(place * cols, (place + 1) * cols)
            scr[member, rows_at, :channels] = back.astype(BF16)
            scr[member, rows_at, channels : 2 * channels] = slab.astype(BF16)
            scr[member, rows_at, 2 * channels :] = ahead.astype(BF16)

    for member in range(mem):
        shifted(shift_scr, member, updated[member])
    for member in range(groups):
        shifted(cot_shift_scr, member, cot_scr[member])

    total = updated_ref[...].reshape(mem * cells, channels).astype(F32)
    for r in range(3):
        window = jnp.concatenate(
            [shift_scr[m, r * cols : r * cols + cells, :] for m in range(mem)], axis=0
        )
        total = total + dot_nn(window, conv_ref[3 * channels * r : 3 * channels * (r + 1), :])
    result_ref[...] = total.astype(BF16).reshape(mem, rows, cols, channels)

    total = jnp.concatenate([cot_scr[m, cols : cols + cells, :] for m in range(groups)], axis=0)
    for r in range(3):
        begin = (2 - r) * cols
        window = jnp.concatenate(
            [cot_shift_scr[m, begin : begin + cells, :] for m in range(groups)], axis=0
        )
        total = total + dot_nn(window, conv_t_ref[3 * channels * r : 3 * channels * (r + 1), :])
    grad_field = total
    grad_mixed = dot_nn(grad_field.astype(BF16), output_t_ref[...]).astype(BF16)
    grads = [grad_mixed[m * cells : (m + 1) * cells] for m in range(groups)]

    values = [proj_ref[n, :, 2 * channels :] for n in range(groups)]
    query_grad = [None] * mem
    key_grad = [None] * mem
    value_grad = [None] * mem
    for m in range(groups):
        soft = [soft_ref[m * groups + n] for n in range(groups)]
        dprob = [dot_nn(grads[m] * values[n], same_head) for n in range(groups)]
        mean = soft[0] * dprob[0]
        for n in range(1, groups):
            mean = mean + soft[n] * dprob[n]
        for n in range(groups):
            if m >= mem and n >= mem:
                continue
            dscore = (soft[n] * (dprob[n] - mean)).astype(BF16).astype(F32)
            if m < mem:
                term = dscore * unit_ref[1, n].astype(F32)
                query_grad[m] = term if query_grad[m] is None else query_grad[m] + term
            if n < mem:
                term = dscore * unit_ref[0, m].astype(F32)
                key_grad[n] = term if key_grad[n] is None else key_grad[n] + term
                term = soft[n].astype(BF16).astype(F32) * grads[m].astype(F32)
                value_grad[n] = term if value_grad[n] is None else value_grad[n] + term

    def head_pull(kind, member, grad):
        grad = grad * scale
        raw = proj_ref[member, :, kind * channels : (kind + 1) * channels].astype(F32)
        inner = head_sums(grad * raw, same_head)
        return inverse_ref[kind, member] * grad - pull_ref[kind, member] * inner

    for m in range(mem):
        grad_proj = jnp.concatenate(
            [
                head_pull(0, m, query_grad[m]).astype(BF16),
                head_pull(1, m, key_grad[m]).astype(BF16),
                value_grad[m].astype(BF16),
            ],
            axis=1,
        )
        grad_normed = dot_nn(grad_proj, project_t_ref[...]) * gain
        x = both_ref[0, m].reshape(cells, channels).astype(F32)
        inverse = row_rsqrt(x)
        inner = jnp.mean(x * grad_normed, axis=-1, keepdims=True)
        pulled = inverse * grad_normed - x * (inverse * inverse * inverse * inner)
        total = grad_field[m * cells : (m + 1) * cells] + pulled
        grad_ref[m] = total.astype(BF16).reshape(rows, cols, channels)


def local_call(kernel, name, operands, out_shape, scratch, pinned=False, cost=None):
    whole = pl.BlockSpec(memory_space=pltpu.VMEM)
    anywhere = pl.BlockSpec(memory_space=pl.ANY)
    specs = [anywhere if in_hbm else whole for _, in_hbm in operands]
    arrays = [
        pltpu.with_memory_space_constraint(array, pltpu.HBM) if in_hbm else array
        for array, in_hbm in operands
    ]

    def keep(shape):
        return pltpu.VMEM(shape.shape, shape.dtype) if pinned else shape

    return pl.pallas_call(
        kernel,
        out_shape=jax.tree.map(keep, out_shape),
        in_specs=specs,
        out_specs=jax.tree.map(lambda _: whole, out_shape),
        scratch_shapes=scratch,
        compiler_params=pltpu.CompilerParams(vmem_limit_bytes=VMEM_LIMIT),
        cost_estimate=cost,
        name=name,
    )(*arrays)


def here(*arrays):
    return [(array, False) for array in arrays]


def in_hbm(*arrays):
    return [(array, True) for array in arrays]


def per_device_paired(ensemble, norm_gain, project_weight, output_weight, conv_kernel, cotangent):
    mem, rows, cols, channels = ensemble.shape
    groups = 2 * mem
    cells = rows * cols
    tall = rows + 2
    lon_count = lax.axis_size("lon")
    lat_count = lax.axis_size("lat")
    bf16 = functools.partial(jax.ShapeDtypeStruct, dtype=BF16)
    f32 = functools.partial(jax.ShapeDtypeStruct, dtype=F32)
    row = (2, mem, cols, channels)
    swap = [(0, 1), (1, 0)]
    core_pairs = [(i, i ^ 1) for i in range(lon_count)]
    chip_pairs = [(i, (i - 1 if i % 2 == 0 else i + 1) % lon_count) for i in range(lon_count)]

    def lat_swap(offset, across):
        pairs = []
        for member in range(2):
            for lat in range(lat_count):
                for lon in range(lon_count):
                    to = (member, lat + 1 if lat % 2 == offset else lat - 1, lon)
                    if not 0 <= to[1] < lat_count:
                        to = (member, lat, lon ^ 1)
                    elif across:
                        to = (1 - member,) + to[1:]
                    me = (member * lat_count + lat) * lon_count + lon
                    pairs.append((me, (to[0] * lat_count + to[1]) * lon_count + to[2]))
        return pairs

    both, first_send, second_send = local_call(
        stack_kernel,
        "stack",
        in_hbm(ensemble, cotangent),
        (bf16((2,) + ensemble.shape), bf16(row), bf16(row)),
        [pltpu.SemaphoreType.DMA((2,))],
        pinned=True,
    )
    other = lax.ppermute(both, "member", swap)
    everyone = ("member", "lat", "lon")
    first = lax.ppermute(first_send, everyone, lat_swap(0, False))
    second = lax.ppermute(second_send, everyone, lat_swap(1, False))
    cross_first = lax.ppermute(first_send, everyone, lat_swap(0, True))
    cross_second = lax.ppermute(second_send, everyone, lat_swap(1, True))

    weights = (
        norm_gain.reshape(1, channels),
        project_weight,
        output_weight,
        conv_kernel.reshape(9 * channels, channels),
    )
    weights = local_call(
        weights_kernel,
        "load_weights",
        in_hbm(*weights),
        tuple(jax.ShapeDtypeStruct(w.shape, w.dtype) for w in weights)
        + (
            bf16((3 * channels, channels)),
            bf16((channels, channels)),
            bf16((9 * channels, channels)),
        ),
        [pltpu.SemaphoreType.DMA((4,))],
        pinned=True,
    )
    strip = (2 * groups * tall, channels)
    halo, core_send, chip_send = local_call(
        functools.partial(pack_strips_kernel, lat_count=lat_count),
        "pack_strips",
        here(both, other, first, second, cross_first, cross_second, weights[0]),
        (bf16((2, 2, groups, cols, channels)), bf16(strip), bf16(strip)),
        [pltpu.VMEM(strip, F32)] * 2,
    )
    core = lax.ppermute(core_send, "lon", core_pairs)
    chip = lax.ppermute(chip_send, "lon", chip_pairs)

    held = local_call(
        own_kernel,
        "own_cells",
        here(both, other, *weights[:3]),
        (
            bf16((groups, cells, 3 * channels)),
            bf16((2, groups, cells, channels)),
            f32((groups * groups, cells, channels)),
            f32((2, mem, cells, channels)),
            f32((2, mem, cells, channels)),
            bf16((mem, cells, channels)),
        ),
        [],
        pinned=True,
    )

    rim = 2 * cols + 16
    return local_call(
        main_kernel,
        "main",
        here(both, other, halo, core, chip, *weights, *held),
        (bf16(ensemble.shape), bf16(ensemble.shape)),
        [
            pltpu.VMEM((groups, rim, channels), F32),
            pltpu.VMEM((groups, tall * cols + 16, channels), F32),
            pltpu.VMEM((groups * rim, 3 * channels), BF16),
            pltpu.VMEM((mem, tall * cols, 3 * channels), BF16),
            pltpu.VMEM((groups, tall * cols, 3 * channels), BF16),
        ],
    )


def solution(mesh):
    paired = mesh.shape["member"] == 2 and mesh.shape["lon"] % 2 == 0
    per_device = per_device_paired if paired else per_device_general
    in_specs = (
        P("member", "lat", "lon", None),
        P(),
        P(),
        P(),
        P(),
        P("member", "lat", "lon", None),
    )
    out_specs = (P("member", "lat", "lon", None), P("member", "lat", "lon", None))
    return jax.shard_map(
        per_device, mesh=mesh, in_specs=in_specs, out_specs=out_specs, check_vma=False
    )
```

```python
import functools
import math

import jax
import jax.numpy as jnp
from jax import lax
from jax.experimental import pallas as pl
from jax.experimental.pallas import tpu as pltpu
from jax.sharding import PartitionSpec as P

HEAD_COUNT = 8


FLOOR = 0.5
EPSILON = 1e-06


def padded_2(block, sides, width, periodic):
    for axis, dim in sides:
        count = lax.axis_size(axis)
        forward = [(i, i + 1) for i in range(count - 1)]
        if periodic:
            forward.append((count - 1, 0))
        backward = [(target, source) for source, target in forward]
        low = lax.ppermute(
            lax.slice_in_dim(block, block.shape[dim] - width, None, axis=dim), axis, forward
        )
        high = lax.ppermute(lax.slice_in_dim(block, 0, width, axis=dim), axis, backward)
        block = jnp.concatenate([low, block, high], axis=dim)
    return block


def row_norm(values, gain_vec):
    mean_sq = jnp.mean(values * values, axis=-1, keepdims=True)
    return values * lax.rsqrt(mean_sq + EPSILON) * gain_vec


def head_norm(values, head_count):
    shaped = values.reshape(values.shape[:-1] + (head_count, values.shape[-1] // head_count))
    mean_sq = jnp.mean(shaped * shaped, axis=-1, keepdims=True)
    return (shaped * lax.rsqrt(jnp.maximum(mean_sq, FLOOR))).reshape(values.shape)


def split_heads(values, head_count):
    return values.reshape(values.shape[:-1] + (head_count, values.shape[-1] // head_count))


def head_pullback(raw_rows, grad_rows):
    _, pullback = jax.vjp(lambda t: head_norm(t, HEAD_COUNT), raw_rows.astype(jnp.float32))
    return pullback(grad_rows)[0]


def pad_field(field_in):
    widened = padded_2(field_in, (("lon", 2),), 1, True)
    return padded_2(widened, (("lat", 1),), 1, False)


def conv_taps(padded, kernel, lat_n, lon_n, adjoint):
    running = None
    for row_off in range(3):
        for col_off in range(3):
            if adjoint:
                window = padded[
                    :, 2 - row_off : 2 - row_off + lat_n, 2 - col_off : 2 - col_off + lon_n
                ]
                summand = jnp.einsum(
                    "mabc,dc->mabd",
                    window,
                    kernel[row_off, col_off],
                    preferred_element_type=jnp.float32,
                )
            else:
                window = padded[:, row_off : row_off + lat_n, col_off : col_off + lon_n]
                summand = jnp.einsum(
                    "mabc,cd->mabd",
                    window,
                    kernel[row_off, col_off],
                    preferred_element_type=jnp.float32,
                )
            running = summand if running is None else running + summand
    return running


def per_device_general(ensemble, norm_gain, project_weight, output_weight, conv_kernel, cotangent):
    mem_dev, lat_dev, lon_dev, channels = ensemble.shape
    cell_count = lat_dev * lon_dev
    score_scale = 1.0 / math.sqrt(channels // HEAD_COUNT)
    inputs = ensemble.reshape(mem_dev, cell_count, channels).astype(jnp.float32)
    normed = row_norm(inputs, norm_gain).astype(jnp.bfloat16)
    spread = lax.all_to_all(normed, "member", split_axis=1, concat_axis=0, tiled=True)
    projected = jnp.dot(spread, project_weight, preferred_element_type=jnp.float32).astype(
        jnp.bfloat16
    )
    query_raw = projected[..., :channels]
    key_raw = projected[..., channels : 2 * channels]
    value_rows = projected[..., 2 * channels :]
    key_rows = head_norm(key_raw.astype(jnp.float32), HEAD_COUNT).astype(jnp.bfloat16)
    queries = head_norm(query_raw.astype(jnp.float32), HEAD_COUNT).astype(jnp.bfloat16)
    query_heads = split_heads(queries, HEAD_COUNT)
    key_heads = split_heads(key_rows, HEAD_COUNT)
    value_heads = split_heads(value_rows, HEAD_COUNT)
    scores = (
        jnp.einsum("mphd,nphd->mnhp", query_heads, key_heads, preferred_element_type=jnp.float32)
        * score_scale
    )
    expd = jnp.exp(scores)
    soft = expd / jnp.sum(expd, axis=1, keepdims=True)
    rounded = soft.astype(jnp.bfloat16)
    mixed_out = jnp.einsum(
        "mnhp,nphd->mphd", rounded, value_heads, preferred_element_type=jnp.float32
    )
    mixed_out = mixed_out.reshape(query_raw.shape).astype(jnp.bfloat16)
    mixed_out = lax.all_to_all(mixed_out, "member", split_axis=0, concat_axis=1, tiled=True)
    updated = (
        inputs + jnp.dot(mixed_out, output_weight, preferred_element_type=jnp.float32)
    ).astype(jnp.bfloat16)
    field_up = updated.reshape(mem_dev, lat_dev, lon_dev, channels)
    result = field_up.astype(jnp.float32) + conv_taps(
        pad_field(field_up), conv_kernel, lat_dev, lon_dev, False
    )
    result = result.astype(jnp.bfloat16)
    grad_field = cotangent.astype(jnp.float32) + conv_taps(
        pad_field(cotangent), conv_kernel, lat_dev, lon_dev, True
    )
    grad_rows = grad_field.reshape(mem_dev, cell_count, channels)
    grad_mixed = jnp.einsum(
        "mpc,dc->mpd",
        grad_rows.astype(jnp.bfloat16),
        output_weight,
        preferred_element_type=jnp.float32,
    )
    grad_mixed = grad_mixed.astype(jnp.bfloat16)
    grad_mixed = lax.all_to_all(grad_mixed, "member", split_axis=1, concat_axis=0, tiled=True)
    grad_heads = split_heads(grad_mixed, HEAD_COUNT)
    dprob = jnp.einsum(
        "mphd,nphd->mnhp", grad_heads, value_heads, preferred_element_type=jnp.float32
    )
    dscore = (soft * (dprob - jnp.sum(soft * dprob, axis=1, keepdims=True))).astype(jnp.bfloat16)
    query_grad = (
        jnp.einsum("mnhp,nphd->mphd", dscore, key_heads, preferred_element_type=jnp.float32)
        * score_scale
    )
    query_grad = query_grad.reshape(query_raw.shape)
    key_grad = (
        jnp.einsum("mnhp,mphd->nphd", dscore, query_heads, preferred_element_type=jnp.float32)
        * score_scale
    )
    key_grad = key_grad.reshape(key_raw.shape)
    value_grad = jnp.einsum(
        "mnhp,mphd->nphd", rounded, grad_heads, preferred_element_type=jnp.float32
    )
    value_grad = value_grad.reshape(key_raw.shape)
    grad_query_raw = head_pullback(query_raw, query_grad)
    grad_key_raw = head_pullback(key_raw, key_grad)
    grad_proj = jnp.concatenate([grad_query_raw, grad_key_raw, value_grad], axis=-1).astype(
        jnp.bfloat16
    )
    grad_proj = lax.all_to_all(grad_proj, "member", split_axis=0, concat_axis=1, tiled=True)
    grad_normed = jnp.einsum(
        "mpe,ce->mpc", grad_proj, project_weight, preferred_element_type=jnp.float32
    )
    _, pull_norm = jax.vjp(lambda t: row_norm(t, norm_gain), inputs)
    grad_inputs = pull_norm(grad_normed)[0]
    grad_ensemble = (
        (grad_rows + grad_inputs).astype(jnp.bfloat16).reshape(mem_dev, lat_dev, lon_dev, channels)
    )
    return (result, grad_ensemble)


F32 = jnp.float32
BF16 = jnp.bfloat16
VMEM_LIMIT = 48 * 1024 * 1024


def is_even(axis):
    return lax.rem(lax.axis_index(axis), 2) == 0


def serves_south():
    return is_even("lat") == is_even("lon")


def half_index():
    return lax.rem(lax.axis_index("lon"), 2)


def stack_kernel(ens_ref, cot_ref, both_ref, sems):
    copies = [
        pltpu.make_async_copy(ref, both_ref.at[i], sems.at[i])
        for i, ref in enumerate((ens_ref, cot_ref))
    ]
    for copy in copies:
        copy.start()
    for copy in copies:
        copy.wait()


def pack_rows_kernel(both_ref, hand_ref, out_ref):
    _, mem, rows, _, _ = both_ref.shape
    half = half_index()
    row = jnp.where(serves_south(), rows - 1, 0)
    for array in range(2):
        for member in range(mem):
            out_ref[half, array, member] = both_ref[array, member, row]
            out_ref[1 - half, array, member] = hand_ref[array, member, row]


def share_kernel(near_ref, cross_ref, after_ref, also_after_ref, out_ref):
    other_half = 1 - half_index()
    _, arrays, mem, _, _ = near_ref.shape
    for group, ref in enumerate((near_ref, cross_ref)):
        for array in range(arrays):
            for member in range(mem):
                out_ref[group, array, member] = ref[other_half, array, member]


def pack_strips_kernel(
    both_ref,
    other_ref,
    near_ref,
    cross_ref,
    far_ref,
    halo_ref,
    core_ref,
    chip_ref,
    low_scr,
    high_scr,
    *,
    lat_count,
):
    _, mem, rows, cols, _ = both_ref.shape
    south_here = serves_south()
    half = half_index()
    lat = lax.axis_index("lat")
    index = 0
    for array in range(2):
        for member in range(2 * mem):
            group, at = divmod(member, mem)
            block = other_ref if group else both_ref
            here_row = (cross_ref if group else near_ref)[half, array, at].astype(F32)
            far_row = far_ref[group, array, at].astype(F32)
            north = jnp.where(lat == 0, 0.0, jnp.where(south_here, far_row, here_row))
            south = jnp.where(lat == lat_count - 1, 0.0, jnp.where(south_here, here_row, far_row))
            halo_ref[0, array, member] = north.astype(BF16)
            halo_ref[1, array, member] = south.astype(BF16)
            slabs = [block[array, at, row].astype(F32) for row in range(rows)]
            for slab in [north] + slabs + [south]:
                low_scr[index : index + 1, :] = slab[0:1]
                high_scr[index : index + 1, :] = slab[cols - 1 : cols]
                index += 1
    even = is_even("lon")
    low, high = low_scr[...], high_scr[...]
    core_ref[...] = jnp.where(even, high, low).astype(BF16)
    chip_ref[...] = jnp.where(even, low, high).astype(BF16)


def dot_nn(a, b):
    return lax.dot_general(a, b, (((1,), (0,)), ((), ())), preferred_element_type=F32)


def same_head_matrix(channels):
    width = channels // HEAD_COUNT
    lane_row = lax.broadcasted_iota(jnp.int32, (channels, channels), 0) // width
    lane_col = lax.broadcasted_iota(jnp.int32, (channels, channels), 1) // width
    return jnp.where(lane_row == lane_col, 1.0, 0.0).astype(BF16)


def head_sums(values, same_head):
    high = values.astype(BF16)
    low = (values - high.astype(F32)).astype(BF16)
    return dot_nn(high, same_head) + dot_nn(low, same_head)


def head_unit(raw, same_head):
    raw = raw.astype(F32)
    mean_sq = head_sums(raw * raw, same_head) * (HEAD_COUNT / raw.shape[-1])
    inverse = lax.rsqrt(jnp.maximum(mean_sq, FLOOR))
    return raw, mean_sq, inverse, (raw * inverse).astype(BF16)


def row_rsqrt(values):
    return lax.rsqrt(jnp.mean(values * values, axis=-1, keepdims=True) + EPSILON)


def attend(query, keys, values, same_head, scale):
    exps = [jnp.exp(dot_nn(query * key, same_head) * scale) for key in keys]
    total = exps[0]
    for e in exps[1:]:
        total = total + e
    inverse = 1.0 / total
    probs = [e * inverse for e in exps]
    mixed = None
    if values is not None:
        for prob, value in zip(probs, values):
            term = prob.astype(BF16).astype(F32) * value.astype(F32)
            mixed = term if mixed is None else mixed + term
        mixed = mixed.astype(BF16)
    return probs, mixed


def weights_kernel(
    gain_hbm,
    project_hbm,
    output_hbm,
    conv_hbm,
    gain_ref,
    project_ref,
    output_ref,
    conv_ref,
    project_t_ref,
    output_t_ref,
    conv_t_ref,
    sems,
):
    channels = output_ref.shape[0]
    loads = [
        pltpu.make_async_copy(source, target, sems.at[i])
        for i, (source, target) in enumerate(
            (
                (gain_hbm, gain_ref),
                (project_hbm, project_ref),
                (output_hbm, output_ref),
                (conv_hbm, conv_ref),
            )
        )
    ]
    for load in loads:
        load.start()
    loads[0].wait()
    loads[1].wait()
    for kind in range(3):
        lanes = slice(kind * channels, (kind + 1) * channels)
        project_t_ref[lanes, :] = project_ref[:, lanes].T
    loads[2].wait()
    output_t_ref[...] = output_ref[...].T
    loads[3].wait()
    for r in range(3):
        for c in range(3):
            tap = (3 * r + c) * channels
            turned = (3 * r + 2 - c) * channels
            conv_t_ref[turned : turned + channels, :] = conv_ref[tap : tap + channels, :].T


def own_kernel(
    both_ref,
    other_ref,
    gain_ref,
    project_ref,
    output_ref,
    proj_ref,
    unit_ref,
    soft_ref,
    inverse_ref,
    pull_ref,
    updated_ref,
):
    _, mem, rows, cols, channels = both_ref.shape
    groups = 2 * mem
    cells = rows * cols
    width = channels // HEAD_COUNT
    scale = 1.0 / math.sqrt(width)
    same_head = same_head_matrix(channels)
    own = both_ref[0].reshape(mem * cells, channels)
    other = other_ref[0].reshape(mem * cells, channels)
    x = jnp.concatenate([own, other], axis=0).astype(F32)
    normed = (x * row_rsqrt(x) * gain_ref[...]).astype(BF16)
    proj_ref[...] = (
        dot_nn(normed, project_ref[...]).astype(BF16).reshape(groups, cells, 3 * channels)
    )
    for kind in range(2):
        for member in range(groups):
            lanes = slice(kind * channels, (kind + 1) * channels)
            raw, mean_sq, inverse, unit = head_unit(proj_ref[member, :, lanes], same_head)
            unit_ref[kind, member] = unit
            if member < mem:
                active = jnp.where(mean_sq > FLOOR, 1.0, jnp.where(mean_sq == FLOOR, 0.5, 0.0))
                inverse_ref[kind, member] = inverse
                pull_ref[kind, member] = active * raw * (inverse * inverse * inverse) / width
    keys = [unit_ref[1, n] for n in range(groups)]
    values = [proj_ref[n, :, 2 * channels :] for n in range(groups)]
    for m in range(groups):
        probs, mixed = attend(unit_ref[0, m], keys, values if m < mem else None, same_head, scale)
        for n in range(groups):
            soft_ref[m * groups + n] = probs[n]
        if m < mem:
            x = both_ref[0, m].reshape(cells, channels).astype(F32)
            updated_ref[m] = (x + dot_nn(mixed, output_ref[...])).astype(BF16)


def main_kernel(
    both_ref,
    other_ref,
    halo_ref,
    core_ref,
    chip_ref,
    gain_ref,
    project_ref,
    output_ref,
    conv_ref,
    project_t_ref,
    output_t_ref,
    conv_t_ref,
    proj_ref,
    unit_ref,
    soft_ref,
    inverse_ref,
    pull_ref,
    updated_ref,
    result_ref,
    grad_ref,
    x_scr,
    cot_scr,
    proj_scr,
    shift_scr,
    cot_shift_scr,
):
    _, mem, rows, cols, channels = both_ref.shape
    groups = 2 * mem
    tall = rows + 2
    centre = tall * cols
    cells = rows * cols
    rim = x_scr.shape[1]
    width = channels // HEAD_COUNT
    scale = 1.0 / math.sqrt(width)
    even = is_even("lon")
    core, chip = core_ref[...].astype(F32), chip_ref[...].astype(F32)
    low, high = jnp.where(even, chip, core), jnp.where(even, core, chip)

    for array, scr in enumerate((x_scr, cot_scr)):
        for member in range(groups):
            top = halo_ref[0, array, member].astype(F32)
            bottom = halo_ref[1, array, member].astype(F32)
            if array == 0:
                scr[member, :cols, :] = top
                scr[member, cols : 2 * cols, :] = bottom
                edge = 2 * cols
            else:
                ref, at = (both_ref, member) if member < mem else (other_ref, member - mem)
                scr[member, :cols, :] = top
                scr[member, cols : cols + cells, :] = (
                    ref[1, at].reshape(cells, channels).astype(F32)
                )
                scr[member, cols + cells : centre, :] = bottom
                edge = centre
            scr[member, edge:, :] = jnp.zeros((16, channels), F32)
            slot = (array * groups + member) * tall
            scr[member, edge : edge + tall, :] = low[slot : slot + tall]
            scr[member, edge + 8 : edge + 8 + tall, :] = high[slot : slot + tall]

    same_head = same_head_matrix(channels)
    gain = gain_ref[...]

    x_all = x_scr[...].reshape(groups * rim, channels)
    normed = (x_all * row_rsqrt(x_all) * gain).astype(BF16)
    proj_scr[...] = dot_nn(normed, project_ref[...]).astype(BF16)
    keys = [
        head_unit(proj_scr[n * rim : (n + 1) * rim, channels : 2 * channels], same_head)[3]
        for n in range(groups)
    ]
    values = [proj_scr[n * rim : (n + 1) * rim, 2 * channels :] for n in range(groups)]
    updated = []
    for m in range(mem):
        query = head_unit(proj_scr[m * rim : (m + 1) * rim, :channels], same_head)[3]
        _, mixed = attend(query, keys, values, same_head, scale)
        field = (x_scr[m] + dot_nn(mixed, output_ref[...])).astype(BF16).astype(F32)
        updated.append(
            jnp.concatenate(
                [field[:cols], updated_ref[m].astype(F32), field[cols:]],
                axis=0,
            )
        )

    def shifted(scr, member, field):
        column = lax.broadcasted_iota(jnp.int32, (cols, channels), 0)
        for place in range(tall):
            slab = field[place * cols : (place + 1) * cols]
            west = field[centre + place : centre + place + 1]
            east = field[centre + 8 + place : centre + 8 + place + 1]
            back = jnp.where(column == 0, west, pltpu.roll(slab, 1, 0))
            ahead = jnp.where(column == cols - 1, east, pltpu.roll(slab, cols - 1, 0))
            rows_at = slice(place * cols, (place + 1) * cols)
            scr[member, rows_at, :channels] = back.astype(BF16)
            scr[member, rows_at, channels : 2 * channels] = slab.astype(BF16)
            scr[member, rows_at, 2 * channels :] = ahead.astype(BF16)

    for member in range(mem):
        shifted(shift_scr, member, updated[member])
    for member in range(groups):
        shifted(cot_shift_scr, member, cot_scr[member])

    total = updated_ref[...].reshape(mem * cells, channels).astype(F32)
    for r in range(3):
        window = jnp.concatenate(
            [shift_scr[m, r * cols : r * cols + cells, :] for m in range(mem)], axis=0
        )
        total = total + dot_nn(window, conv_ref[3 * channels * r : 3 * channels * (r + 1), :])
    result_ref[...] = total.astype(BF16).reshape(mem, rows, cols, channels)

    total = jnp.concatenate([cot_scr[m, cols : cols + cells, :] for m in range(groups)], axis=0)
    for r in range(3):
        begin = (2 - r) * cols
        window = jnp.concatenate(
            [cot_shift_scr[m, begin : begin + cells, :] for m in range(groups)], axis=0
        )
        total = total + dot_nn(window, conv_t_ref[3 * channels * r : 3 * channels * (r + 1), :])
    grad_field = total
    grad_mixed = dot_nn(grad_field.astype(BF16), output_t_ref[...]).astype(BF16)
    grads = [grad_mixed[m * cells : (m + 1) * cells] for m in range(groups)]

    values = [proj_ref[n, :, 2 * channels :] for n in range(groups)]
    query_grad = [None] * mem
    key_grad = [None] * mem
    value_grad = [None] * mem
    for m in range(groups):
        soft = [soft_ref[m * groups + n] for n in range(groups)]
        dprob = [dot_nn(grads[m] * values[n], same_head) for n in range(groups)]
        mean = soft[0] * dprob[0]
        for n in range(1, groups):
            mean = mean + soft[n] * dprob[n]
        for n in range(groups):
            if m >= mem and n >= mem:
                continue
            dscore = (soft[n] * (dprob[n] - mean)).astype(BF16).astype(F32)
            if m < mem:
                term = dscore * unit_ref[1, n].astype(F32)
                query_grad[m] = term if query_grad[m] is None else query_grad[m] + term
            if n < mem:
                term = dscore * unit_ref[0, m].astype(F32)
                key_grad[n] = term if key_grad[n] is None else key_grad[n] + term
                term = soft[n].astype(BF16).astype(F32) * grads[m].astype(F32)
                value_grad[n] = term if value_grad[n] is None else value_grad[n] + term

    def head_pull(kind, member, grad):
        grad = grad * scale
        raw = proj_ref[member, :, kind * channels : (kind + 1) * channels].astype(F32)
        inner = head_sums(grad * raw, same_head)
        return inverse_ref[kind, member] * grad - pull_ref[kind, member] * inner

    for m in range(mem):
        grad_proj = jnp.concatenate(
            [
                head_pull(0, m, query_grad[m]).astype(BF16),
                head_pull(1, m, key_grad[m]).astype(BF16),
                value_grad[m].astype(BF16),
            ],
            axis=1,
        )
        grad_normed = dot_nn(grad_proj, project_t_ref[...]) * gain
        x = both_ref[0, m].reshape(cells, channels).astype(F32)
        inverse = row_rsqrt(x)
        inner = jnp.mean(x * grad_normed, axis=-1, keepdims=True)
        pulled = inverse * grad_normed - x * (inverse * inverse * inverse * inner)
        total = grad_field[m * cells : (m + 1) * cells] + pulled
        grad_ref[m] = total.astype(BF16).reshape(rows, cols, channels)


def local_call(kernel, name, operands, out_shape, scratch, pinned=False, cost=None):
    whole = pl.BlockSpec(memory_space=pltpu.VMEM)
    anywhere = pl.BlockSpec(memory_space=pl.ANY)
    specs = [anywhere if in_hbm else whole for _, in_hbm in operands]
    arrays = [
        pltpu.with_memory_space_constraint(array, pltpu.HBM) if in_hbm else array
        for array, in_hbm in operands
    ]

    def keep(shape):
        return pltpu.VMEM(shape.shape, shape.dtype) if pinned else shape

    return pl.pallas_call(
        kernel,
        out_shape=jax.tree.map(keep, out_shape),
        in_specs=specs,
        out_specs=jax.tree.map(lambda _: whole, out_shape),
        scratch_shapes=scratch,
        compiler_params=pltpu.CompilerParams(vmem_limit_bytes=VMEM_LIMIT),
        cost_estimate=cost,
        name=name,
    )(*arrays)


def here(*arrays):
    return [(array, False) for array in arrays]


def in_hbm(*arrays):
    return [(array, True) for array in arrays]


def per_device_paired(ensemble, norm_gain, project_weight, output_weight, conv_kernel, cotangent):
    mem, rows, cols, channels = ensemble.shape
    groups = 2 * mem
    cells = rows * cols
    tall = rows + 2
    lon_count = lax.axis_size("lon")
    lat_count = lax.axis_size("lat")
    bf16 = functools.partial(jax.ShapeDtypeStruct, dtype=BF16)
    f32 = functools.partial(jax.ShapeDtypeStruct, dtype=F32)
    row = (2, mem, cols, channels)
    swap = [(0, 1), (1, 0)]
    core_pairs = [(i, i ^ 1) for i in range(lon_count)]
    chip_pairs = [(i, (i - 1 if i % 2 == 0 else i + 1) % lon_count) for i in range(lon_count)]

    def lat_swap(across):
        pairs = []
        for member in range(2):
            for lat in range(lat_count):
                for lon in range(lon_count):
                    to = (1 - member if across else member, lat + 1 if lat % 2 == lon % 2 else lat - 1)
                    if not 0 <= to[1] < lat_count:
                        to = (1 - member, lat)
                    me = (member * lat_count + lat) * lon_count + lon
                    pairs.append((me, (to[0] * lat_count + to[1]) * lon_count + lon))
        return pairs

    both = local_call(
        stack_kernel,
        "stack",
        in_hbm(ensemble, cotangent),
        bf16((2,) + ensemble.shape),
        [pltpu.SemaphoreType.DMA((2,))],
        pinned=True,
    )
    handed = lax.ppermute(both, "lon", core_pairs)
    other = lax.ppermute(both, "member", swap)
    sent = local_call(pack_rows_kernel, "pack_rows", here(both, handed), bf16((2,) + row), [])
    everyone = ("member", "lat", "lon")
    near = lax.ppermute(sent, everyone, lat_swap(False))
    cross = lax.ppermute(sent, everyone, lat_swap(True))

    weights = (
        norm_gain.reshape(1, channels),
        project_weight,
        output_weight,
        conv_kernel.reshape(9 * channels, channels),
    )
    weights = local_call(
        weights_kernel,
        "load_weights",
        in_hbm(*weights),
        tuple(jax.ShapeDtypeStruct(w.shape, w.dtype) for w in weights)
        + (
            bf16((3 * channels, channels)),
            bf16((channels, channels)),
            bf16((9 * channels, channels)),
        ),
        [pltpu.SemaphoreType.DMA((4,))],
        pinned=True,
    )
    share = local_call(share_kernel, "share", here(near, cross, weights[0], other), bf16((2,) + row), [])
    far = lax.ppermute(share, "lon", core_pairs)
    strip = (2 * groups * tall, channels)
    halo, core_send, chip_send = local_call(
        functools.partial(pack_strips_kernel, lat_count=lat_count),
        "pack_strips",
        here(both, other, near, cross, far),
        (bf16((2, 2, groups, cols, channels)), bf16(strip), bf16(strip)),
        [pltpu.VMEM(strip, F32)] * 2,
    )
    core = lax.ppermute(core_send, "lon", core_pairs)
    chip = lax.ppermute(chip_send, "lon", chip_pairs)

    held = local_call(
        own_kernel,
        "own_cells",
        here(both, other, *weights[:3]),
        (
            bf16((groups, cells, 3 * channels)),
            bf16((2, groups, cells, channels)),
            f32((groups * groups, cells, channels)),
            f32((2, mem, cells, channels)),
            f32((2, mem, cells, channels)),
            bf16((mem, cells, channels)),
        ),
        [],
        pinned=True,
    )

    rim = 2 * cols + 16
    return local_call(
        main_kernel,
        "main",
        here(both, other, halo, core, chip, *weights, *held),
        (bf16(ensemble.shape), bf16(ensemble.shape)),
        [
            pltpu.VMEM((groups, rim, channels), F32),
            pltpu.VMEM((groups, tall * cols + 16, channels), F32),
            pltpu.VMEM((groups * rim, 3 * channels), BF16),
            pltpu.VMEM((mem, tall * cols, 3 * channels), BF16),
            pltpu.VMEM((groups, tall * cols, 3 * channels), BF16),
        ],
    )


def solution(mesh):
    paired = mesh.shape["member"] == 2 and mesh.shape["lon"] % 2 == 0
    per_device = per_device_paired if paired else per_device_general
    in_specs = (
        P("member", "lat", "lon", None),
        P(),
        P(),
        P(),
        P(),
        P("member", "lat", "lon", None),
    )
    out_specs = (P("member", "lat", "lon", None), P("member", "lat", "lon", None))
    return jax.shard_map(
        per_device, mesh=mesh, in_specs=in_specs, out_specs=out_specs, check_vma=False
    )
```

```python
import functools
import math

import jax
import jax.numpy as jnp
from jax import lax
from jax.experimental import pallas as pl
from jax.experimental.pallas import tpu as pltpu
from jax.sharding import PartitionSpec as P

HEAD_COUNT = 8


FLOOR = 0.5
EPSILON = 1e-06


def padded_2(block, sides, width, periodic):
    for axis, dim in sides:
        count = lax.axis_size(axis)
        forward = [(i, i + 1) for i in range(count - 1)]
        if periodic:
            forward.append((count - 1, 0))
        backward = [(target, source) for source, target in forward]
        low = lax.ppermute(
            lax.slice_in_dim(block, block.shape[dim] - width, None, axis=dim), axis, forward
        )
        high = lax.ppermute(lax.slice_in_dim(block, 0, width, axis=dim), axis, backward)
        block = jnp.concatenate([low, block, high], axis=dim)
    return block


def row_norm(values, gain_vec):
    mean_sq = jnp.mean(values * values, axis=-1, keepdims=True)
    return values * lax.rsqrt(mean_sq + EPSILON) * gain_vec


def head_norm(values, head_count):
    shaped = values.reshape(values.shape[:-1] + (head_count, values.shape[-1] // head_count))
    mean_sq = jnp.mean(shaped * shaped, axis=-1, keepdims=True)
    return (shaped * lax.rsqrt(jnp.maximum(mean_sq, FLOOR))).reshape(values.shape)


def split_heads(values, head_count):
    return values.reshape(values.shape[:-1] + (head_count, values.shape[-1] // head_count))


def head_pullback(raw_rows, grad_rows):
    _, pullback = jax.vjp(lambda t: head_norm(t, HEAD_COUNT), raw_rows.astype(jnp.float32))
    return pullback(grad_rows)[0]


def pad_field(field_in):
    widened = padded_2(field_in, (("lon", 2),), 1, True)
    return padded_2(widened, (("lat", 1),), 1, False)


def conv_taps(padded, kernel, lat_n, lon_n, adjoint):
    running = None
    for row_off in range(3):
        for col_off in range(3):
            if adjoint:
                window = padded[
                    :, 2 - row_off : 2 - row_off + lat_n, 2 - col_off : 2 - col_off + lon_n
                ]
                summand = jnp.einsum(
                    "mabc,dc->mabd",
                    window,
                    kernel[row_off, col_off],
                    preferred_element_type=jnp.float32,
                )
            else:
                window = padded[:, row_off : row_off + lat_n, col_off : col_off + lon_n]
                summand = jnp.einsum(
                    "mabc,cd->mabd",
                    window,
                    kernel[row_off, col_off],
                    preferred_element_type=jnp.float32,
                )
            running = summand if running is None else running + summand
    return running


def per_device_general(ensemble, norm_gain, project_weight, output_weight, conv_kernel, cotangent):
    mem_dev, lat_dev, lon_dev, channels = ensemble.shape
    cell_count = lat_dev * lon_dev
    score_scale = 1.0 / math.sqrt(channels // HEAD_COUNT)
    inputs = ensemble.reshape(mem_dev, cell_count, channels).astype(jnp.float32)
    normed = row_norm(inputs, norm_gain).astype(jnp.bfloat16)
    spread = lax.all_to_all(normed, "member", split_axis=1, concat_axis=0, tiled=True)
    projected = jnp.dot(spread, project_weight, preferred_element_type=jnp.float32).astype(
        jnp.bfloat16
    )
    query_raw = projected[..., :channels]
    key_raw = projected[..., channels : 2 * channels]
    value_rows = projected[..., 2 * channels :]
    key_rows = head_norm(key_raw.astype(jnp.float32), HEAD_COUNT).astype(jnp.bfloat16)
    queries = head_norm(query_raw.astype(jnp.float32), HEAD_COUNT).astype(jnp.bfloat16)
    query_heads = split_heads(queries, HEAD_COUNT)
    key_heads = split_heads(key_rows, HEAD_COUNT)
    value_heads = split_heads(value_rows, HEAD_COUNT)
    scores = (
        jnp.einsum("mphd,nphd->mnhp", query_heads, key_heads, preferred_element_type=jnp.float32)
        * score_scale
    )
    expd = jnp.exp(scores)
    soft = expd / jnp.sum(expd, axis=1, keepdims=True)
    rounded = soft.astype(jnp.bfloat16)
    mixed_out = jnp.einsum(
        "mnhp,nphd->mphd", rounded, value_heads, preferred_element_type=jnp.float32
    )
    mixed_out = mixed_out.reshape(query_raw.shape).astype(jnp.bfloat16)
    mixed_out = lax.all_to_all(mixed_out, "member", split_axis=0, concat_axis=1, tiled=True)
    updated = (
        inputs + jnp.dot(mixed_out, output_weight, preferred_element_type=jnp.float32)
    ).astype(jnp.bfloat16)
    field_up = updated.reshape(mem_dev, lat_dev, lon_dev, channels)
    result = field_up.astype(jnp.float32) + conv_taps(
        pad_field(field_up), conv_kernel, lat_dev, lon_dev, False
    )
    result = result.astype(jnp.bfloat16)
    grad_field = cotangent.astype(jnp.float32) + conv_taps(
        pad_field(cotangent), conv_kernel, lat_dev, lon_dev, True
    )
    grad_rows = grad_field.reshape(mem_dev, cell_count, channels)
    grad_mixed = jnp.einsum(
        "mpc,dc->mpd",
        grad_rows.astype(jnp.bfloat16),
        output_weight,
        preferred_element_type=jnp.float32,
    )
    grad_mixed = grad_mixed.astype(jnp.bfloat16)
    grad_mixed = lax.all_to_all(grad_mixed, "member", split_axis=1, concat_axis=0, tiled=True)
    grad_heads = split_heads(grad_mixed, HEAD_COUNT)
    dprob = jnp.einsum(
        "mphd,nphd->mnhp", grad_heads, value_heads, preferred_element_type=jnp.float32
    )
    dscore = (soft * (dprob - jnp.sum(soft * dprob, axis=1, keepdims=True))).astype(jnp.bfloat16)
    query_grad = (
        jnp.einsum("mnhp,nphd->mphd", dscore, key_heads, preferred_element_type=jnp.float32)
        * score_scale
    )
    query_grad = query_grad.reshape(query_raw.shape)
    key_grad = (
        jnp.einsum("mnhp,mphd->nphd", dscore, query_heads, preferred_element_type=jnp.float32)
        * score_scale
    )
    key_grad = key_grad.reshape(key_raw.shape)
    value_grad = jnp.einsum(
        "mnhp,mphd->nphd", rounded, grad_heads, preferred_element_type=jnp.float32
    )
    value_grad = value_grad.reshape(key_raw.shape)
    grad_query_raw = head_pullback(query_raw, query_grad)
    grad_key_raw = head_pullback(key_raw, key_grad)
    grad_proj = jnp.concatenate([grad_query_raw, grad_key_raw, value_grad], axis=-1).astype(
        jnp.bfloat16
    )
    grad_proj = lax.all_to_all(grad_proj, "member", split_axis=0, concat_axis=1, tiled=True)
    grad_normed = jnp.einsum(
        "mpe,ce->mpc", grad_proj, project_weight, preferred_element_type=jnp.float32
    )
    _, pull_norm = jax.vjp(lambda t: row_norm(t, norm_gain), inputs)
    grad_inputs = pull_norm(grad_normed)[0]
    grad_ensemble = (
        (grad_rows + grad_inputs).astype(jnp.bfloat16).reshape(mem_dev, lat_dev, lon_dev, channels)
    )
    return (result, grad_ensemble)


F32 = jnp.float32
BF16 = jnp.bfloat16
VMEM_LIMIT = 48 * 1024 * 1024


def is_even(axis):
    return lax.rem(lax.axis_index(axis), 2) == 0


def stack_kernel(ens_ref, cot_ref, both_ref, first_ref, second_ref, sems):
    _, mem, rows, _, _ = both_ref.shape
    copies = [
        pltpu.make_async_copy(ref, both_ref.at[i], sems.at[i])
        for i, ref in enumerate((ens_ref, cot_ref))
    ]
    for copy in copies:
        copy.start()
    for copy in copies:
        copy.wait()
    even = is_even("lat")
    for array in range(2):
        for member in range(mem):
            first_ref[array, member] = both_ref[array, member, jnp.where(even, rows - 1, 0)]
            second_ref[array, member] = both_ref[array, member, jnp.where(even, 0, rows - 1)]


def pack_strips_kernel(
    both_ref,
    other_ref,
    first_ref,
    second_ref,
    cross_first_ref,
    cross_second_ref,
    after_ref,
    halo_ref,
    core_ref,
    chip_ref,
    low_scr,
    high_scr,
    *,
    lat_count,
):
    _, mem, rows, cols, _ = both_ref.shape
    lat_even = is_even("lat")
    lat = lax.axis_index("lat")
    index = 0
    for array in range(2):
        for member in range(2 * mem):
            if member < mem:
                block, at = both_ref, member
                first, second = first_ref[array, at], second_ref[array, at]
            else:
                block, at = other_ref, member - mem
                first, second = cross_first_ref[array, at], cross_second_ref[array, at]
            first, second = first.astype(F32), second.astype(F32)
            north = jnp.where(lat == 0, 0.0, jnp.where(lat_even, second, first))
            south = jnp.where(lat == lat_count - 1, 0.0, jnp.where(lat_even, first, second))
            halo_ref[0, array, member] = north.astype(BF16)
            halo_ref[1, array, member] = south.astype(BF16)
            slabs = [block[array, at, row].astype(F32) for row in range(rows)]
            for slab in [north] + slabs + [south]:
                low_scr[index : index + 1, :] = slab[0:1]
                high_scr[index : index + 1, :] = slab[cols - 1 : cols]
                index += 1
    even = is_even("lon")
    low, high = low_scr[...], high_scr[...]
    core_ref[...] = jnp.where(even, high, low).astype(BF16)
    chip_ref[...] = jnp.where(even, low, high).astype(BF16)


def dot_nn(a, b):
    return lax.dot_general(a, b, (((1,), (0,)), ((), ())), preferred_element_type=F32)


def same_head_matrix(channels):
    width = channels // HEAD_COUNT
    lane_row = lax.broadcasted_iota(jnp.int32, (channels, channels), 0) // width
    lane_col = lax.broadcasted_iota(jnp.int32, (channels, channels), 1) // width
    return jnp.where(lane_row == lane_col, 1.0, 0.0).astype(BF16)


def head_sums(values, same_head):
    high = values.astype(BF16)
    low = (values - high.astype(F32)).astype(BF16)
    return dot_nn(high, same_head) + dot_nn(low, same_head)


def head_units(raw, same_head):
    raw = raw.astype(F32)
    mean_sq = head_sums(raw * raw, same_head) * (HEAD_COUNT / raw.shape[-1])
    inverse = lax.rsqrt(jnp.maximum(mean_sq, FLOOR))
    return raw, mean_sq, inverse, (raw * inverse).astype(BF16)


def row_rsqrt(values):
    return lax.rsqrt(jnp.mean(values * values, axis=-1, keepdims=True) + EPSILON)


def split_rows(array, count):
    size = array.shape[0] // count
    return [array[i * size : (i + 1) * size] for i in range(count)]


def softmax_members(queries, keys, same_head, scale):
    products = [query * key for query in queries for key in keys]
    scores = dot_nn(jnp.concatenate(products, axis=0), same_head) * scale
    exps = split_rows(jnp.exp(scores), len(products))
    soft = []
    for m in range(len(queries)):
        mine = exps[m * len(keys) : (m + 1) * len(keys)]
        total = mine[0]
        for e in mine[1:]:
            total = total + e
        inverse = 1.0 / total
        soft.append([e * inverse for e in mine])
    return soft


def mix_values(probs, values):
    mixed = None
    for prob, value in zip(probs, values):
        term = prob.astype(BF16).astype(F32) * value.astype(F32)
        mixed = term if mixed is None else mixed + term
    return mixed.astype(BF16)


def forward_cells(x, mem, groups, gain, project_ref, output_ref, same_head):
    channels = x.shape[-1]
    own_rows = x.shape[0] // groups * mem
    scale = 1.0 / math.sqrt(channels // HEAD_COUNT)
    normed = (x * row_rsqrt(x) * gain).astype(BF16)
    query_raw = dot_nn(normed[:own_rows], project_ref[:, :channels]).astype(BF16)
    key_raw = dot_nn(normed, project_ref[:, channels : 2 * channels]).astype(BF16)
    values = dot_nn(normed, project_ref[:, 2 * channels :]).astype(BF16)
    units = head_units(jnp.concatenate([query_raw, key_raw], axis=0), same_head)[3]
    queries = split_rows(units[:own_rows], mem)
    keys = split_rows(units[own_rows:], groups)
    values = split_rows(values, groups)
    soft = softmax_members(queries, keys, same_head, scale)
    mixed = jnp.concatenate([mix_values(soft[m], values) for m in range(mem)], axis=0)
    return (x[:own_rows] + dot_nn(mixed, output_ref[...])).astype(BF16)


def weights_kernel(
    gain_hbm,
    project_hbm,
    output_hbm,
    conv_hbm,
    gain_ref,
    project_ref,
    output_ref,
    conv_ref,
    project_t_ref,
    output_t_ref,
    conv_t_ref,
    sems,
):
    channels = output_ref.shape[0]
    loads = [
        pltpu.make_async_copy(source, target, sems.at[i])
        for i, (source, target) in enumerate(
            (
                (gain_hbm, gain_ref),
                (project_hbm, project_ref),
                (output_hbm, output_ref),
                (conv_hbm, conv_ref),
            )
        )
    ]
    for load in loads:
        load.start()
    loads[0].wait()
    loads[1].wait()
    for kind in range(3):
        lanes = slice(kind * channels, (kind + 1) * channels)
        project_t_ref[lanes, :] = project_ref[:, lanes].T
    loads[2].wait()
    output_t_ref[...] = output_ref[...].T
    loads[3].wait()
    for r in range(3):
        for c in range(3):
            tap = (3 * r + c) * channels
            turned = (3 * r + 2 - c) * channels
            conv_t_ref[turned : turned + channels, :] = conv_ref[tap : tap + channels, :].T


def own_kernel(
    both_ref,
    other_ref,
    gain_ref,
    project_ref,
    output_ref,
    proj_ref,
    unit_ref,
    soft_ref,
    inverse_ref,
    pull_ref,
    updated_ref,
):
    _, mem, rows, cols, channels = both_ref.shape
    groups = 2 * mem
    cells = rows * cols
    width = channels // HEAD_COUNT
    scale = 1.0 / math.sqrt(width)
    same_head = same_head_matrix(channels)
    own = both_ref[0].reshape(mem * cells, channels)
    other = other_ref[0].reshape(mem * cells, channels)
    x = jnp.concatenate([own, other], axis=0).astype(F32)
    normed = (x * row_rsqrt(x) * gain_ref[...]).astype(BF16)
    proj = dot_nn(normed, project_ref[...]).astype(BF16)
    proj_ref[...] = proj.reshape(groups, cells, 3 * channels)
    both_raw = jnp.concatenate([proj[:, :channels], proj[:, channels : 2 * channels]], axis=0)
    raw, mean_sq, inverse, units = head_units(both_raw, same_head)
    unit_ref[...] = units.reshape(2, groups, cells, channels)
    active = jnp.where(mean_sq > FLOOR, 1.0, jnp.where(mean_sq == FLOOR, 0.5, 0.0))
    pull = active * raw * (inverse * inverse * inverse) / width
    for kind in range(2):
        at = kind * groups * cells
        mine = slice(at, at + mem * cells)
        inverse_ref[kind] = inverse[mine].reshape(mem, cells, channels)
        pull_ref[kind] = pull[mine].reshape(mem, cells, channels)
    units = split_rows(units, 2 * groups)
    soft = softmax_members(units[:groups], units[groups:], same_head, scale)
    for m in range(groups):
        for n in range(groups):
            soft_ref[m * groups + n] = soft[m][n]
    values = split_rows(proj[:, 2 * channels :], groups)
    mixed = jnp.concatenate([mix_values(soft[m], values) for m in range(mem)], axis=0)
    updated = x[: mem * cells] + dot_nn(mixed, output_ref[...])
    updated_ref[...] = updated.astype(BF16).reshape(mem, cells, channels)


def centre_kernel(
    both_ref,
    other_ref,
    halo_ref,
    gain_ref,
    project_ref,
    output_ref,
    conv_ref,
    conv_t_ref,
    updated_ref,
    result_ref,
    grad_ref,
    shift_scr,
    cot_shift_scr,
):
    _, mem, rows, cols, channels = both_ref.shape
    groups = 2 * mem
    tall = rows + 2
    cells = rows * cols
    column = lax.broadcasted_iota(jnp.int32, (cols, channels), 0)

    def shifted(scr, member, place, slab):
        back = jnp.where(column == 0, 0.0, pltpu.roll(slab, 1, 0))
        ahead = jnp.where(column == cols - 1, 0.0, pltpu.roll(slab, cols - 1, 0))
        rows_at = slice(place * cols, (place + 1) * cols)
        scr[member, rows_at, :channels] = back.astype(BF16)
        scr[member, rows_at, channels : 2 * channels] = slab.astype(BF16)
        scr[member, rows_at, 2 * channels :] = ahead.astype(BF16)

    for member in range(groups):
        ref, at = (both_ref, member) if member < mem else (other_ref, member - mem)
        slabs = [halo_ref[0, 1, member]] + [ref[1, at, row] for row in range(rows)]
        slabs.append(halo_ref[1, 1, member])
        for place, slab in enumerate(slabs):
            shifted(cot_shift_scr, member, place, slab.astype(F32))

    halo = [halo_ref[side, 0, member] for member in range(groups) for side in range(2)]
    x = jnp.concatenate(halo, axis=0).astype(F32)
    same_head = same_head_matrix(channels)
    fresh = forward_cells(x, mem, groups, gain_ref[...], project_ref, output_ref, same_head)
    fresh = split_rows(fresh.astype(F32), 2 * mem)
    for member in range(mem):
        slabs = [fresh[2 * member]]
        for row in range(rows):
            slabs.append(updated_ref[member, row * cols : (row + 1) * cols, :].astype(F32))
        slabs.append(fresh[2 * member + 1])
        for place, slab in enumerate(slabs):
            shifted(shift_scr, member, place, slab)

    both = both_ref[1].reshape(mem * cells, channels)
    other = other_ref[1].reshape(mem * cells, channels)
    total = jnp.concatenate([both, other], axis=0).astype(F32)
    for r in range(3):
        begin = (2 - r) * cols
        window = jnp.concatenate(
            [cot_shift_scr[m, begin : begin + cells, :] for m in range(groups)], axis=0
        )
        total = total + dot_nn(window, conv_t_ref[3 * channels * r : 3 * channels * (r + 1), :])
    grad_ref[...] = total

    total = updated_ref[...].reshape(mem * cells, channels).astype(F32)
    for r in range(3):
        window = jnp.concatenate(
            [shift_scr[m, r * cols : r * cols + cells, :] for m in range(mem)], axis=0
        )
        total = total + dot_nn(window, conv_ref[3 * channels * r : 3 * channels * (r + 1), :])
    result_ref[...] = total


def main_kernel(
    both_ref,
    core_ref,
    chip_ref,
    gain_ref,
    project_ref,
    output_ref,
    conv_ref,
    project_t_ref,
    output_t_ref,
    conv_t_ref,
    proj_ref,
    unit_ref,
    soft_ref,
    inverse_ref,
    pull_ref,
    result_part_ref,
    grad_part_ref,
    result_ref,
    grad_ref,
    strip_scr,
):
    _, mem, rows, cols, channels = both_ref.shape
    groups = 2 * mem
    tall = rows + 2
    cells = rows * cols
    scale = 1.0 / math.sqrt(channels // HEAD_COUNT)
    even = is_even("lon")
    gain = gain_ref[...]
    same_head = same_head_matrix(channels)

    core, chip = core_ref[...].astype(F32), chip_ref[...].astype(F32)
    low, high = jnp.where(even, chip, core), jnp.where(even, core, chip)
    for slot in range(2 * groups):
        strip_scr[slot] = jnp.zeros((16, channels), F32)
        strip_scr[slot, :tall, :] = low[slot * tall : (slot + 1) * tall]
        strip_scr[slot, 8 : 8 + tall, :] = high[slot * tall : (slot + 1) * tall]

    def rim_part(fields, taps_ref, turned):
        sums = []
        for side in range(2):
            total = None
            for r in range(3):
                begin = 8 * side + (2 - r if turned else r)
                window = jnp.concatenate([f[begin : begin + rows] for f in fields], axis=0)
                tap = (3 * r + 2 * side) * channels
                term = dot_nn(window.astype(BF16), taps_ref[tap : tap + channels, :])
                total = term if total is None else total + term
            sums.append(total)
        column = lax.broadcasted_iota(jnp.int32, (cols, channels), 0)
        added = []
        for i in range(len(fields) * rows):
            west, east = sums[0][i : i + 1], sums[1][i : i + 1]
            added.append(
                jnp.where(column == 0, west, 0.0) + jnp.where(column == cols - 1, east, 0.0)
            )
        return jnp.concatenate(added, axis=0)

    cots = [strip_scr[groups + m] for m in range(groups)]
    grad_field = grad_part_ref[...] + rim_part(cots, conv_t_ref, True)
    grad_mixed = dot_nn(grad_field.astype(BF16), output_t_ref[...]).astype(BF16)
    grads = split_rows(grad_mixed, groups)

    x = strip_scr[:groups].reshape(groups * 16, channels)
    fresh = forward_cells(x, mem, groups, gain, project_ref, output_ref, same_head)
    fresh = split_rows(fresh.astype(F32), mem)
    total = result_part_ref[...] + rim_part(fresh, conv_ref, False)
    result_ref[...] = total.astype(BF16).reshape(mem, rows, cols, channels)

    values = [proj_ref[n, :, 2 * channels :] for n in range(groups)]
    products = [grads[m] * values[n] for m in range(groups) for n in range(groups)]
    dprobs = split_rows(dot_nn(jnp.concatenate(products, axis=0), same_head), len(products))
    query_grad = [None] * mem
    key_grad = [None] * mem
    value_grad = [None] * mem
    for m in range(groups):
        soft = [soft_ref[m * groups + n] for n in range(groups)]
        dprob = dprobs[m * groups : (m + 1) * groups]
        mean = soft[0] * dprob[0]
        for n in range(1, groups):
            mean = mean + soft[n] * dprob[n]
        for n in range(groups):
            if m >= mem and n >= mem:
                continue
            dscore = (soft[n] * (dprob[n] - mean)).astype(BF16).astype(F32)
            if m < mem:
                term = dscore * unit_ref[1, n].astype(F32)
                query_grad[m] = term if query_grad[m] is None else query_grad[m] + term
            if n < mem:
                term = dscore * unit_ref[0, m].astype(F32)
                key_grad[n] = term if key_grad[n] is None else key_grad[n] + term
                term = soft[n].astype(BF16).astype(F32) * grads[m].astype(F32)
                value_grad[n] = term if value_grad[n] is None else value_grad[n] + term

    pulled = []
    unit_grads = [jnp.concatenate(g, axis=0) * scale for g in (query_grad, key_grad)]
    raws = [
        proj_ref[:mem, :, kind * channels : (kind + 1) * channels]
        .reshape(mem * cells, channels)
        .astype(F32)
        for kind in range(2)
    ]
    inner = head_sums(
        jnp.concatenate([g * raw for g, raw in zip(unit_grads, raws)], axis=0), same_head
    )
    inner = split_rows(inner, 2)
    for kind in range(2):
        inverse = inverse_ref[kind].reshape(mem * cells, channels)
        pull = pull_ref[kind].reshape(mem * cells, channels)
        pulled.append((inverse * unit_grads[kind] - pull * inner[kind]).astype(BF16))
    pulled.append(jnp.concatenate(value_grad, axis=0).astype(BF16))
    grad_proj = jnp.concatenate(pulled, axis=1)
    grad_normed = dot_nn(grad_proj, project_t_ref[...]) * gain
    x = both_ref[0].reshape(mem * cells, channels).astype(F32)
    inverse = row_rsqrt(x)
    inner = jnp.mean(x * grad_normed, axis=-1, keepdims=True)
    total = grad_field[: mem * cells] + inverse * grad_normed
    total = total - x * (inverse * inverse * inverse * inner)
    grad_ref[...] = total.astype(BF16).reshape(mem, rows, cols, channels)


def local_call(kernel, name, operands, out_shape, scratch, pinned=False, cost=None):
    whole = pl.BlockSpec(memory_space=pltpu.VMEM)
    anywhere = pl.BlockSpec(memory_space=pl.ANY)
    specs = [anywhere if in_hbm else whole for _, in_hbm in operands]
    arrays = [
        pltpu.with_memory_space_constraint(array, pltpu.HBM) if in_hbm else array
        for array, in_hbm in operands
    ]

    def keep(shape):
        return pltpu.VMEM(shape.shape, shape.dtype) if pinned else shape

    return pl.pallas_call(
        kernel,
        out_shape=jax.tree.map(keep, out_shape),
        in_specs=specs,
        out_specs=jax.tree.map(lambda _: whole, out_shape),
        scratch_shapes=scratch,
        compiler_params=pltpu.CompilerParams(vmem_limit_bytes=VMEM_LIMIT),
        cost_estimate=cost,
        name=name,
    )(*arrays)


def here(*arrays):
    return [(array, False) for array in arrays]


def in_hbm(*arrays):
    return [(array, True) for array in arrays]


def per_device_paired(ensemble, norm_gain, project_weight, output_weight, conv_kernel, cotangent):
    mem, rows, cols, channels = ensemble.shape
    groups = 2 * mem
    cells = rows * cols
    tall = rows + 2
    lon_count = lax.axis_size("lon")
    lat_count = lax.axis_size("lat")
    bf16 = functools.partial(jax.ShapeDtypeStruct, dtype=BF16)
    f32 = functools.partial(jax.ShapeDtypeStruct, dtype=F32)
    row = (2, mem, cols, channels)
    swap = [(0, 1), (1, 0)]
    core_pairs = [(i, i ^ 1) for i in range(lon_count)]
    chip_pairs = [(i, (i - 1 if i % 2 == 0 else i + 1) % lon_count) for i in range(lon_count)]

    def lat_swap(offset, across):
        pairs = []
        for member in range(2):
            for lat in range(lat_count):
                for lon in range(lon_count):
                    to = (member, lat + 1 if lat % 2 == offset else lat - 1, lon)
                    if not 0 <= to[1] < lat_count:
                        to = (member, lat, lon ^ 1)
                    elif across:
                        to = (1 - member,) + to[1:]
                    me = (member * lat_count + lat) * lon_count + lon
                    pairs.append((me, (to[0] * lat_count + to[1]) * lon_count + to[2]))
        return pairs

    both, first_send, second_send = local_call(
        stack_kernel,
        "stack",
        in_hbm(ensemble, cotangent),
        (bf16((2,) + ensemble.shape), bf16(row), bf16(row)),
        [pltpu.SemaphoreType.DMA((2,))],
        pinned=True,
    )
    other = lax.ppermute(both, "member", swap)
    everyone = ("member", "lat", "lon")
    first = lax.ppermute(first_send, everyone, lat_swap(0, False))
    second = lax.ppermute(second_send, everyone, lat_swap(1, False))
    cross_first = lax.ppermute(first_send, everyone, lat_swap(0, True))
    cross_second = lax.ppermute(second_send, everyone, lat_swap(1, True))

    weights = (
        norm_gain.reshape(1, channels),
        project_weight,
        output_weight,
        conv_kernel.reshape(9 * channels, channels),
    )
    weights = local_call(
        weights_kernel,
        "load_weights",
        in_hbm(*weights),
        tuple(jax.ShapeDtypeStruct(w.shape, w.dtype) for w in weights)
        + (
            bf16((3 * channels, channels)),
            bf16((channels, channels)),
            bf16((9 * channels, channels)),
        ),
        [pltpu.SemaphoreType.DMA((4,))],
        pinned=True,
    )
    held = local_call(
        own_kernel,
        "own_cells",
        here(both, other, *weights[:3]),
        (
            bf16((groups, cells, 3 * channels)),
            bf16((2, groups, cells, channels)),
            f32((groups * groups, cells, channels)),
            f32((2, mem, cells, channels)),
            f32((2, mem, cells, channels)),
            bf16((mem, cells, channels)),
        ),
        [],
        pinned=True,
    )

    strip = (2 * groups * tall, channels)
    halo, core_send, chip_send = local_call(
        functools.partial(pack_strips_kernel, lat_count=lat_count),
        "pack_strips",
        here(both, other, first, second, cross_first, cross_second, held[-1]),
        (bf16((2, 2, groups, cols, channels)), bf16(strip), bf16(strip)),
        [pltpu.VMEM(strip, F32)] * 2,
    )
    core = lax.ppermute(core_send, "lon", core_pairs)
    chip = lax.ppermute(chip_send, "lon", chip_pairs)

    gain, project, output, conv, _, _, conv_t = weights
    parts = local_call(
        centre_kernel,
        "centre",
        here(both, other, halo, gain, project, output, conv, conv_t, held[-1]),
        (f32((mem * cells, channels)), f32((groups * cells, channels))),
        [
            pltpu.VMEM((mem, tall * cols, 3 * channels), BF16),
            pltpu.VMEM((groups, tall * cols, 3 * channels), BF16),
        ],
        pinned=True,
    )
    return local_call(
        main_kernel,
        "main",
        here(both, core, chip, *weights, *held[:-1], *parts),
        (bf16(ensemble.shape), bf16(ensemble.shape)),
        [pltpu.VMEM((2 * groups, 16, channels), F32)],
    )


def solution(mesh):
    paired = mesh.shape["member"] == 2 and mesh.shape["lon"] % 2 == 0
    per_device = per_device_paired if paired else per_device_general
    in_specs = (
        P("member", "lat", "lon", None),
        P(),
        P(),
        P(),
        P(),
        P("member", "lat", "lon", None),
    )
    out_specs = (P("member", "lat", "lon", None), P("member", "lat", "lon", None))
    return jax.shard_map(
        per_device, mesh=mesh, in_specs=in_specs, out_specs=out_specs, check_vma=False
    )
```

```python
import functools
import math

import jax
import jax.numpy as jnp
from jax import lax
from jax.experimental import pallas as pl
from jax.experimental.pallas import tpu as pltpu
from jax.sharding import PartitionSpec as P

HEAD_COUNT = 8


FLOOR = 0.5
EPSILON = 1e-06


def padded_2(block, sides, width, periodic):
    for axis, dim in sides:
        count = lax.axis_size(axis)
        forward = [(i, i + 1) for i in range(count - 1)]
        if periodic:
            forward.append((count - 1, 0))
        backward = [(target, source) for source, target in forward]
        low = lax.ppermute(
            lax.slice_in_dim(block, block.shape[dim] - width, None, axis=dim), axis, forward
        )
        high = lax.ppermute(lax.slice_in_dim(block, 0, width, axis=dim), axis, backward)
        block = jnp.concatenate([low, block, high], axis=dim)
    return block


def row_norm(values, gain_vec):
    mean_sq = jnp.mean(values * values, axis=-1, keepdims=True)
    return values * lax.rsqrt(mean_sq + EPSILON) * gain_vec


def head_norm(values, head_count):
    shaped = values.reshape(values.shape[:-1] + (head_count, values.shape[-1] // head_count))
    mean_sq = jnp.mean(shaped * shaped, axis=-1, keepdims=True)
    return (shaped * lax.rsqrt(jnp.maximum(mean_sq, FLOOR))).reshape(values.shape)


def split_heads(values, head_count):
    return values.reshape(values.shape[:-1] + (head_count, values.shape[-1] // head_count))


def head_pullback(raw_rows, grad_rows):
    _, pullback = jax.vjp(lambda t: head_norm(t, HEAD_COUNT), raw_rows.astype(jnp.float32))
    return pullback(grad_rows)[0]


def pad_field(field_in):
    widened = padded_2(field_in, (("lon", 2),), 1, True)
    return padded_2(widened, (("lat", 1),), 1, False)


def conv_taps(padded, kernel, lat_n, lon_n, adjoint):
    running = None
    for row_off in range(3):
        for col_off in range(3):
            if adjoint:
                window = padded[
                    :, 2 - row_off : 2 - row_off + lat_n, 2 - col_off : 2 - col_off + lon_n
                ]
                summand = jnp.einsum(
                    "mabc,dc->mabd",
                    window,
                    kernel[row_off, col_off],
                    preferred_element_type=jnp.float32,
                )
            else:
                window = padded[:, row_off : row_off + lat_n, col_off : col_off + lon_n]
                summand = jnp.einsum(
                    "mabc,cd->mabd",
                    window,
                    kernel[row_off, col_off],
                    preferred_element_type=jnp.float32,
                )
            running = summand if running is None else running + summand
    return running


def per_device_general(ensemble, norm_gain, project_weight, output_weight, conv_kernel, cotangent):
    mem_dev, lat_dev, lon_dev, channels = ensemble.shape
    cell_count = lat_dev * lon_dev
    score_scale = 1.0 / math.sqrt(channels // HEAD_COUNT)
    inputs = ensemble.reshape(mem_dev, cell_count, channels).astype(jnp.float32)
    normed = row_norm(inputs, norm_gain).astype(jnp.bfloat16)
    spread = lax.all_to_all(normed, "member", split_axis=1, concat_axis=0, tiled=True)
    projected = jnp.dot(spread, project_weight, preferred_element_type=jnp.float32).astype(
        jnp.bfloat16
    )
    query_raw = projected[..., :channels]
    key_raw = projected[..., channels : 2 * channels]
    value_rows = projected[..., 2 * channels :]
    key_rows = head_norm(key_raw.astype(jnp.float32), HEAD_COUNT).astype(jnp.bfloat16)
    queries = head_norm(query_raw.astype(jnp.float32), HEAD_COUNT).astype(jnp.bfloat16)
    query_heads = split_heads(queries, HEAD_COUNT)
    key_heads = split_heads(key_rows, HEAD_COUNT)
    value_heads = split_heads(value_rows, HEAD_COUNT)
    scores = (
        jnp.einsum("mphd,nphd->mnhp", query_heads, key_heads, preferred_element_type=jnp.float32)
        * score_scale
    )
    expd = jnp.exp(scores)
    soft = expd / jnp.sum(expd, axis=1, keepdims=True)
    rounded = soft.astype(jnp.bfloat16)
    mixed_out = jnp.einsum(
        "mnhp,nphd->mphd", rounded, value_heads, preferred_element_type=jnp.float32
    )
    mixed_out = mixed_out.reshape(query_raw.shape).astype(jnp.bfloat16)
    mixed_out = lax.all_to_all(mixed_out, "member", split_axis=0, concat_axis=1, tiled=True)
    updated = (
        inputs + jnp.dot(mixed_out, output_weight, preferred_element_type=jnp.float32)
    ).astype(jnp.bfloat16)
    field_up = updated.reshape(mem_dev, lat_dev, lon_dev, channels)
    result = field_up.astype(jnp.float32) + conv_taps(
        pad_field(field_up), conv_kernel, lat_dev, lon_dev, False
    )
    result = result.astype(jnp.bfloat16)
    grad_field = cotangent.astype(jnp.float32) + conv_taps(
        pad_field(cotangent), conv_kernel, lat_dev, lon_dev, True
    )
    grad_rows = grad_field.reshape(mem_dev, cell_count, channels)
    grad_mixed = jnp.einsum(
        "mpc,dc->mpd",
        grad_rows.astype(jnp.bfloat16),
        output_weight,
        preferred_element_type=jnp.float32,
    )
    grad_mixed = grad_mixed.astype(jnp.bfloat16)
    grad_mixed = lax.all_to_all(grad_mixed, "member", split_axis=1, concat_axis=0, tiled=True)
    grad_heads = split_heads(grad_mixed, HEAD_COUNT)
    dprob = jnp.einsum(
        "mphd,nphd->mnhp", grad_heads, value_heads, preferred_element_type=jnp.float32
    )
    dscore = (soft * (dprob - jnp.sum(soft * dprob, axis=1, keepdims=True))).astype(jnp.bfloat16)
    query_grad = (
        jnp.einsum("mnhp,nphd->mphd", dscore, key_heads, preferred_element_type=jnp.float32)
        * score_scale
    )
    query_grad = query_grad.reshape(query_raw.shape)
    key_grad = (
        jnp.einsum("mnhp,mphd->nphd", dscore, query_heads, preferred_element_type=jnp.float32)
        * score_scale
    )
    key_grad = key_grad.reshape(key_raw.shape)
    value_grad = jnp.einsum(
        "mnhp,mphd->nphd", rounded, grad_heads, preferred_element_type=jnp.float32
    )
    value_grad = value_grad.reshape(key_raw.shape)
    grad_query_raw = head_pullback(query_raw, query_grad)
    grad_key_raw = head_pullback(key_raw, key_grad)
    grad_proj = jnp.concatenate([grad_query_raw, grad_key_raw, value_grad], axis=-1).astype(
        jnp.bfloat16
    )
    grad_proj = lax.all_to_all(grad_proj, "member", split_axis=0, concat_axis=1, tiled=True)
    grad_normed = jnp.einsum(
        "mpe,ce->mpc", grad_proj, project_weight, preferred_element_type=jnp.float32
    )
    _, pull_norm = jax.vjp(lambda t: row_norm(t, norm_gain), inputs)
    grad_inputs = pull_norm(grad_normed)[0]
    grad_ensemble = (
        (grad_rows + grad_inputs).astype(jnp.bfloat16).reshape(mem_dev, lat_dev, lon_dev, channels)
    )
    return (result, grad_ensemble)


F32 = jnp.float32
BF16 = jnp.bfloat16
VMEM_LIMIT = 48 * 1024 * 1024


def is_even(axis):
    return lax.rem(lax.axis_index(axis), 2) == 0


def stack_kernel(ens_ref, cot_ref, both_ref, first_ref, second_ref, sems):
    _, mem, rows, _, _ = both_ref.shape
    copies = [
        pltpu.make_async_copy(ref, both_ref.at[i], sems.at[i])
        for i, ref in enumerate((ens_ref, cot_ref))
    ]
    for copy in copies:
        copy.start()
    for copy in copies:
        copy.wait()
    even = is_even("lat")
    for array in range(2):
        for member in range(mem):
            first_ref[array, member] = both_ref[array, member, jnp.where(even, 0, rows - 1)]
            second_ref[array, member] = both_ref[array, member, jnp.where(even, rows - 1, 0)]


def pack_strips_kernel(
    both_ref,
    other_ref,
    first_ref,
    second_ref,
    cross_first_ref,
    cross_second_ref,
    after_ref,
    halo_ref,
    chip_ref,
    core_ref,
    low_scr,
    high_scr,
    *,
    lat_count,
):
    _, mem, rows, cols, _ = both_ref.shape
    lat_even = is_even("lat")
    lat = lax.axis_index("lat")
    index = 0
    for array in range(2):
        for member in range(2 * mem):
            if member < mem:
                block, at = both_ref, member
                first, second = first_ref[array, at], second_ref[array, at]
            else:
                block, at = other_ref, member - mem
                first, second = cross_first_ref[array, at], cross_second_ref[array, at]
            first, second = first.astype(F32), second.astype(F32)
            north = jnp.where(lat == 0, 0.0, jnp.where(lat_even, first, second))
            south = jnp.where(lat == lat_count - 1, 0.0, jnp.where(lat_even, second, first))
            halo_ref[0, array, member] = north.astype(BF16)
            halo_ref[1, array, member] = south.astype(BF16)
            slabs = [block[array, at, row].astype(F32) for row in range(rows)]
            for slab in [north] + slabs + [south]:
                low_scr[index : index + 1, :] = slab[0:1]
                high_scr[index : index + 1, :] = slab[cols - 1 : cols]
                index += 1
    even = is_even("lon")
    low, high = low_scr[...], high_scr[...]
    core_ref[...] = jnp.where(even, high, low).astype(BF16)
    chip_ref[...] = jnp.where(even, low, high).astype(BF16)


def dot_nn(a, b):
    return lax.dot_general(a, b, (((1,), (0,)), ((), ())), preferred_element_type=F32)


def same_head_matrix(channels):
    width = channels // HEAD_COUNT
    lane_row = lax.broadcasted_iota(jnp.int32, (channels, channels), 0) // width
    lane_col = lax.broadcasted_iota(jnp.int32, (channels, channels), 1) // width
    return jnp.where(lane_row == lane_col, 1.0, 0.0).astype(BF16)


def head_sums(values, same_head):
    high = values.astype(BF16)
    low = (values - high.astype(F32)).astype(BF16)
    return dot_nn(high, same_head) + dot_nn(low, same_head)


def head_units(raw, same_head):
    raw = raw.astype(F32)
    mean_sq = head_sums(raw * raw, same_head) * (HEAD_COUNT / raw.shape[-1])
    inverse = lax.rsqrt(jnp.maximum(mean_sq, FLOOR))
    return raw, mean_sq, inverse, (raw * inverse).astype(BF16)


def row_rsqrt(values):
    return lax.rsqrt(jnp.mean(values * values, axis=-1, keepdims=True) + EPSILON)


def split_rows(array, count):
    size = array.shape[0] // count
    return [array[i * size : (i + 1) * size] for i in range(count)]


def softmax_members(queries, keys, same_head, scale):
    products = [query * key for query in queries for key in keys]
    scores = dot_nn(jnp.concatenate(products, axis=0), same_head) * scale
    exps = split_rows(jnp.exp(scores), len(products))
    soft = []
    for m in range(len(queries)):
        mine = exps[m * len(keys) : (m + 1) * len(keys)]
        total = mine[0]
        for e in mine[1:]:
            total = total + e
        inverse = 1.0 / total
        soft.append([e * inverse for e in mine])
    return soft


def mix_values(probs, values):
    mixed = None
    for prob, value in zip(probs, values):
        term = prob.astype(BF16).astype(F32) * value.astype(F32)
        mixed = term if mixed is None else mixed + term
    return mixed.astype(BF16)


def forward_cells(x, mem, groups, gain, project_ref, output_ref, same_head):
    channels = x.shape[-1]
    own_rows = x.shape[0] // groups * mem
    scale = 1.0 / math.sqrt(channels // HEAD_COUNT)
    normed = (x * row_rsqrt(x) * gain).astype(BF16)
    query_raw = dot_nn(normed[:own_rows], project_ref[:, :channels]).astype(BF16)
    key_raw = dot_nn(normed, project_ref[:, channels : 2 * channels]).astype(BF16)
    values = dot_nn(normed, project_ref[:, 2 * channels :]).astype(BF16)
    units = head_units(jnp.concatenate([query_raw, key_raw], axis=0), same_head)[3]
    queries = split_rows(units[:own_rows], mem)
    keys = split_rows(units[own_rows:], groups)
    values = split_rows(values, groups)
    soft = softmax_members(queries, keys, same_head, scale)
    mixed = jnp.concatenate([mix_values(soft[m], values) for m in range(mem)], axis=0)
    return (x[:own_rows] + dot_nn(mixed, output_ref[...])).astype(BF16)


def weights_kernel(
    gain_hbm,
    project_hbm,
    output_hbm,
    gain_ref,
    project_ref,
    output_ref,
    project_t_ref,
    output_t_ref,
    sems,
):
    channels = output_ref.shape[0]
    loads = [
        pltpu.make_async_copy(source, target, sems.at[i])
        for i, (source, target) in enumerate(
            ((gain_hbm, gain_ref), (project_hbm, project_ref), (output_hbm, output_ref))
        )
    ]
    for load in loads:
        load.start()
    loads[0].wait()
    loads[1].wait()
    for kind in range(3):
        lanes = slice(kind * channels, (kind + 1) * channels)
        project_t_ref[lanes, :] = project_ref[:, lanes].T
    loads[2].wait()
    output_t_ref[...] = output_ref[...].T


def own_kernel(
    both_ref,
    other_ref,
    gain_ref,
    project_ref,
    output_ref,
    conv_hbm,
    conv_ref,
    proj_ref,
    unit_ref,
    soft_ref,
    inverse_ref,
    pull_ref,
    updated_ref,
    sem,
):
    load = pltpu.make_async_copy(conv_hbm, conv_ref, sem)
    load.start()
    _, mem, rows, cols, channels = both_ref.shape
    groups = 2 * mem
    cells = rows * cols
    width = channels // HEAD_COUNT
    scale = 1.0 / math.sqrt(width)
    same_head = same_head_matrix(channels)
    own = both_ref[0].reshape(mem * cells, channels)
    other = other_ref[0].reshape(mem * cells, channels)
    x = jnp.concatenate([own, other], axis=0).astype(F32)
    normed = (x * row_rsqrt(x) * gain_ref[...]).astype(BF16)
    proj = dot_nn(normed, project_ref[...]).astype(BF16)
    proj_ref[...] = proj.reshape(groups, cells, 3 * channels)
    both_raw = jnp.concatenate([proj[:, :channels], proj[:, channels : 2 * channels]], axis=0)
    raw, mean_sq, inverse, units = head_units(both_raw, same_head)
    unit_ref[...] = units.reshape(2, groups, cells, channels)
    active = jnp.where(mean_sq > FLOOR, 1.0, jnp.where(mean_sq == FLOOR, 0.5, 0.0))
    pull = active * raw * (inverse * inverse * inverse) / width
    for kind in range(2):
        at = kind * groups * cells
        mine = slice(at, at + mem * cells)
        inverse_ref[kind] = inverse[mine].reshape(mem, cells, channels)
        pull_ref[kind] = pull[mine].reshape(mem, cells, channels)
    units = split_rows(units, 2 * groups)
    soft = softmax_members(units[:groups], units[groups:], same_head, scale)
    for m in range(groups):
        for n in range(groups):
            soft_ref[m * groups + n] = soft[m][n]
    values = split_rows(proj[:, 2 * channels :], groups)
    mixed = jnp.concatenate([mix_values(soft[m], values) for m in range(mem)], axis=0)
    updated = x[: mem * cells] + dot_nn(mixed, output_ref[...])
    updated_ref[...] = updated.astype(BF16).reshape(mem, cells, channels)
    load.wait()


def centre_kernel(
    both_ref,
    other_ref,
    halo_ref,
    gain_ref,
    project_ref,
    output_ref,
    conv_ref,
    updated_ref,
    conv_t_ref,
    result_ref,
    grad_ref,
    shift_scr,
    cot_shift_scr,
):
    _, mem, rows, cols, channels = both_ref.shape
    groups = 2 * mem
    tall = rows + 2
    cells = rows * cols
    column = lax.broadcasted_iota(jnp.int32, (cols, channels), 0)
    for r in range(3):
        for c in range(3):
            tap = (3 * r + c) * channels
            turned = (3 * r + 2 - c) * channels
            conv_t_ref[turned : turned + channels, :] = conv_ref[tap : tap + channels, :].T

    def shifted(scr, member, place, slab):
        back = jnp.where(column == 0, 0.0, pltpu.roll(slab, 1, 0))
        ahead = jnp.where(column == cols - 1, 0.0, pltpu.roll(slab, cols - 1, 0))
        rows_at = slice(place * cols, (place + 1) * cols)
        scr[member, rows_at, :channels] = back.astype(BF16)
        scr[member, rows_at, channels : 2 * channels] = slab.astype(BF16)
        scr[member, rows_at, 2 * channels :] = ahead.astype(BF16)

    for member in range(groups):
        ref, at = (both_ref, member) if member < mem else (other_ref, member - mem)
        slabs = [halo_ref[0, 1, member]] + [ref[1, at, row] for row in range(rows)]
        slabs.append(halo_ref[1, 1, member])
        for place, slab in enumerate(slabs):
            shifted(cot_shift_scr, member, place, slab.astype(F32))

    halo = [halo_ref[side, 0, member] for member in range(groups) for side in range(2)]
    x = jnp.concatenate(halo, axis=0).astype(F32)
    same_head = same_head_matrix(channels)
    fresh = forward_cells(x, mem, groups, gain_ref[...], project_ref, output_ref, same_head)
    fresh = split_rows(fresh.astype(F32), 2 * mem)
    for member in range(mem):
        slabs = [fresh[2 * member]]
        for row in range(rows):
            slabs.append(updated_ref[member, row * cols : (row + 1) * cols, :].astype(F32))
        slabs.append(fresh[2 * member + 1])
        for place, slab in enumerate(slabs):
            shifted(shift_scr, member, place, slab)

    both = both_ref[1].reshape(mem * cells, channels)
    other = other_ref[1].reshape(mem * cells, channels)
    total = jnp.concatenate([both, other], axis=0).astype(F32)
    for r in range(3):
        begin = (2 - r) * cols
        window = jnp.concatenate(
            [cot_shift_scr[m, begin : begin + cells, :] for m in range(groups)], axis=0
        )
        total = total + dot_nn(window, conv_t_ref[3 * channels * r : 3 * channels * (r + 1), :])
    grad_ref[...] = total

    total = updated_ref[...].reshape(mem * cells, channels).astype(F32)
    for r in range(3):
        window = jnp.concatenate(
            [shift_scr[m, r * cols : r * cols + cells, :] for m in range(mem)], axis=0
        )
        total = total + dot_nn(window, conv_ref[3 * channels * r : 3 * channels * (r + 1), :])
    result_ref[...] = total


def main_kernel(
    both_ref,
    chip_ref,
    core_ref,
    gain_ref,
    project_ref,
    output_ref,
    conv_ref,
    project_t_ref,
    output_t_ref,
    conv_t_ref,
    proj_ref,
    unit_ref,
    soft_ref,
    inverse_ref,
    pull_ref,
    result_part_ref,
    grad_part_ref,
    result_ref,
    grad_ref,
    strip_scr,
):
    _, mem, rows, cols, channels = both_ref.shape
    groups = 2 * mem
    tall = rows + 2
    cells = rows * cols
    scale = 1.0 / math.sqrt(channels // HEAD_COUNT)
    even = is_even("lon")
    gain = gain_ref[...]
    same_head = same_head_matrix(channels)

    core, chip = core_ref[...].astype(F32), chip_ref[...].astype(F32)
    low, high = jnp.where(even, chip, core), jnp.where(even, core, chip)
    for slot in range(2 * groups):
        strip_scr[slot] = jnp.zeros((16, channels), F32)
        strip_scr[slot, :tall, :] = low[slot * tall : (slot + 1) * tall]
        strip_scr[slot, 8 : 8 + tall, :] = high[slot * tall : (slot + 1) * tall]

    def rim_part(fields, taps_ref, turned):
        sums = []
        for side in range(2):
            total = None
            for r in range(3):
                begin = 8 * side + (2 - r if turned else r)
                window = jnp.concatenate([f[begin : begin + rows] for f in fields], axis=0)
                tap = (3 * r + 2 * side) * channels
                term = dot_nn(window.astype(BF16), taps_ref[tap : tap + channels, :])
                total = term if total is None else total + term
            sums.append(total)
        column = lax.broadcasted_iota(jnp.int32, (cols, channels), 0)
        added = []
        for i in range(len(fields) * rows):
            west, east = sums[0][i : i + 1], sums[1][i : i + 1]
            added.append(
                jnp.where(column == 0, west, 0.0) + jnp.where(column == cols - 1, east, 0.0)
            )
        return jnp.concatenate(added, axis=0)

    cots = [strip_scr[groups + m] for m in range(groups)]
    grad_field = grad_part_ref[...] + rim_part(cots, conv_t_ref, True)
    grad_mixed = dot_nn(grad_field.astype(BF16), output_t_ref[...]).astype(BF16)
    grads = split_rows(grad_mixed, groups)

    x = strip_scr[:groups].reshape(groups * 16, channels)
    fresh = forward_cells(x, mem, groups, gain, project_ref, output_ref, same_head)
    fresh = split_rows(fresh.astype(F32), mem)
    total = result_part_ref[...] + rim_part(fresh, conv_ref, False)
    result_ref[...] = total.astype(BF16).reshape(mem, rows, cols, channels)

    values = [proj_ref[n, :, 2 * channels :] for n in range(groups)]
    products = [grads[m] * values[n] for m in range(groups) for n in range(groups)]
    dprobs = split_rows(dot_nn(jnp.concatenate(products, axis=0), same_head), len(products))
    query_grad = [None] * mem
    key_grad = [None] * mem
    value_grad = [None] * mem
    for m in range(groups):
        soft = [soft_ref[m * groups + n] for n in range(groups)]
        dprob = dprobs[m * groups : (m + 1) * groups]
        mean = soft[0] * dprob[0]
        for n in range(1, groups):
            mean = mean + soft[n] * dprob[n]
        for n in range(groups):
            if m >= mem and n >= mem:
                continue
            dscore = (soft[n] * (dprob[n] - mean)).astype(BF16).astype(F32)
            if m < mem:
                term = dscore * unit_ref[1, n].astype(F32)
                query_grad[m] = term if query_grad[m] is None else query_grad[m] + term
            if n < mem:
                term = dscore * unit_ref[0, m].astype(F32)
                key_grad[n] = term if key_grad[n] is None else key_grad[n] + term
                term = soft[n].astype(BF16).astype(F32) * grads[m].astype(F32)
                value_grad[n] = term if value_grad[n] is None else value_grad[n] + term

    pulled = []
    unit_grads = [jnp.concatenate(g, axis=0) * scale for g in (query_grad, key_grad)]
    raws = [
        proj_ref[:mem, :, kind * channels : (kind + 1) * channels]
        .reshape(mem * cells, channels)
        .astype(F32)
        for kind in range(2)
    ]
    inner = head_sums(
        jnp.concatenate([g * raw for g, raw in zip(unit_grads, raws)], axis=0), same_head
    )
    inner = split_rows(inner, 2)
    for kind in range(2):
        inverse = inverse_ref[kind].reshape(mem * cells, channels)
        pull = pull_ref[kind].reshape(mem * cells, channels)
        pulled.append((inverse * unit_grads[kind] - pull * inner[kind]).astype(BF16))
    pulled.append(jnp.concatenate(value_grad, axis=0).astype(BF16))
    grad_proj = jnp.concatenate(pulled, axis=1)
    grad_normed = dot_nn(grad_proj, project_t_ref[...]) * gain
    x = both_ref[0].reshape(mem * cells, channels).astype(F32)
    inverse = row_rsqrt(x)
    inner = jnp.mean(x * grad_normed, axis=-1, keepdims=True)
    total = grad_field[: mem * cells] + inverse * grad_normed
    total = total - x * (inverse * inverse * inverse * inner)
    grad_ref[...] = total.astype(BF16).reshape(mem, rows, cols, channels)


def local_call(kernel, name, operands, out_shape, scratch, pinned=False, cost=None):
    whole = pl.BlockSpec(memory_space=pltpu.VMEM)
    anywhere = pl.BlockSpec(memory_space=pl.ANY)
    specs = [anywhere if in_hbm else whole for _, in_hbm in operands]
    arrays = [
        pltpu.with_memory_space_constraint(array, pltpu.HBM) if in_hbm else array
        for array, in_hbm in operands
    ]

    def keep(shape):
        return pltpu.VMEM(shape.shape, shape.dtype) if pinned else shape

    return pl.pallas_call(
        kernel,
        out_shape=jax.tree.map(keep, out_shape),
        in_specs=specs,
        out_specs=jax.tree.map(lambda _: whole, out_shape),
        scratch_shapes=scratch,
        compiler_params=pltpu.CompilerParams(vmem_limit_bytes=VMEM_LIMIT),
        cost_estimate=cost,
        name=name,
    )(*arrays)


def here(*arrays):
    return [(array, False) for array in arrays]


def in_hbm(*arrays):
    return [(array, True) for array in arrays]


def per_device_paired(ensemble, norm_gain, project_weight, output_weight, conv_kernel, cotangent):
    mem, rows, cols, channels = ensemble.shape
    groups = 2 * mem
    cells = rows * cols
    tall = rows + 2
    lon_count = lax.axis_size("lon")
    lat_count = lax.axis_size("lat")
    bf16 = functools.partial(jax.ShapeDtypeStruct, dtype=BF16)
    f32 = functools.partial(jax.ShapeDtypeStruct, dtype=F32)
    row = (2, mem, cols, channels)
    swap = [(0, 1), (1, 0)]
    core_pairs = [(i, i ^ 1) for i in range(lon_count)]
    chip_pairs = [(i, (i - 1 if i % 2 == 0 else i + 1) % lon_count) for i in range(lon_count)]

    def lat_swap(offset, across):
        pairs = []
        for member in range(2):
            for lat in range(lat_count):
                for lon in range(lon_count):
                    to = (member, lat + 1 if lat % 2 == offset else lat - 1, lon)
                    if not 0 <= to[1] < lat_count:
                        to = (member, lat, lon ^ 1)
                    elif across:
                        to = (1 - member,) + to[1:]
                    me = (member * lat_count + lat) * lon_count + lon
                    pairs.append((me, (to[0] * lat_count + to[1]) * lon_count + to[2]))
        return pairs

    both, first_send, second_send = local_call(
        stack_kernel,
        "stack",
        in_hbm(ensemble, cotangent),
        (bf16((2,) + ensemble.shape), bf16(row), bf16(row)),
        [pltpu.SemaphoreType.DMA((2,))],
        pinned=True,
    )
    other = lax.ppermute(both, "member", swap)
    everyone = ("member", "lat", "lon")
    first = lax.ppermute(first_send, everyone, lat_swap(1, False))
    second = lax.ppermute(second_send, everyone, lat_swap(0, False))
    cross_first = lax.ppermute(first_send, everyone, lat_swap(1, True))
    cross_second = lax.ppermute(second_send, everyone, lat_swap(0, True))

    weights = (norm_gain.reshape(1, channels), project_weight, output_weight)
    weights = local_call(
        weights_kernel,
        "load_weights",
        in_hbm(*weights),
        (
            f32((1, channels)),
            bf16(project_weight.shape),
            bf16(output_weight.shape),
            bf16((3 * channels, channels)),
            bf16((channels, channels)),
        ),
        [pltpu.SemaphoreType.DMA((3,))],
        pinned=True,
    )
    conv, *held = local_call(
        own_kernel,
        "own_cells",
        here(both, other, *weights[:3]) + in_hbm(conv_kernel.reshape(9 * channels, channels)),
        (
            bf16((9 * channels, channels)),
            bf16((groups, cells, 3 * channels)),
            bf16((2, groups, cells, channels)),
            f32((groups * groups, cells, channels)),
            f32((2, mem, cells, channels)),
            f32((2, mem, cells, channels)),
            bf16((mem, cells, channels)),
        ),
        [pltpu.SemaphoreType.DMA],
        pinned=True,
    )

    strip = (2 * groups * tall, channels)
    halo, chip_send, core_send = local_call(
        functools.partial(pack_strips_kernel, lat_count=lat_count),
        "pack_strips",
        here(both, other, first, second, cross_first, cross_second, held[-1]),
        (bf16((2, 2, groups, cols, channels)), bf16(strip), bf16(strip)),
        [pltpu.VMEM(strip, F32)] * 2,
    )
    chip = lax.ppermute(chip_send, "lon", chip_pairs)
    core = lax.ppermute(core_send, "lon", core_pairs)

    gain, project, output, project_t, output_t = weights
    conv_t, *parts = local_call(
        centre_kernel,
        "centre",
        here(both, other, halo, gain, project, output, conv, held[-1]),
        (
            bf16((9 * channels, channels)),
            f32((mem * cells, channels)),
            f32((groups * cells, channels)),
        ),
        [
            pltpu.VMEM((mem, tall * cols, 3 * channels), BF16),
            pltpu.VMEM((groups, tall * cols, 3 * channels), BF16),
        ],
        pinned=True,
    )
    main_weights = (gain, project, output, conv, project_t, output_t, conv_t)
    return local_call(
        main_kernel,
        "main",
        here(both, chip, core, *main_weights, *held[:-1], *parts),
        (bf16(ensemble.shape), bf16(ensemble.shape)),
        [pltpu.VMEM((2 * groups, 16, channels), F32)],
    )


def solution(mesh):
    paired = mesh.shape["member"] == 2 and mesh.shape["lon"] % 2 == 0
    per_device = per_device_paired if paired else per_device_general
    in_specs = (
        P("member", "lat", "lon", None),
        P(),
        P(),
        P(),
        P(),
        P("member", "lat", "lon", None),
    )
    out_specs = (P("member", "lat", "lon", None), P("member", "lat", "lon", None))
    return jax.shard_map(
        per_device, mesh=mesh, in_specs=in_specs, out_specs=out_specs, check_vma=False
    )
```

```python
import functools
import math

import jax
import jax.numpy as jnp
from jax import lax
from jax.experimental import pallas as pl
from jax.experimental.pallas import tpu as pltpu
from jax.sharding import PartitionSpec as P

HEAD_COUNT = 8


FLOOR = 0.5
EPSILON = 1e-06


def padded_2(block, sides, width, periodic):
    for axis, dim in sides:
        count = lax.axis_size(axis)
        forward = [(i, i + 1) for i in range(count - 1)]
        if periodic:
            forward.append((count - 1, 0))
        backward = [(target, source) for source, target in forward]
        low = lax.ppermute(
            lax.slice_in_dim(block, block.shape[dim] - width, None, axis=dim), axis, forward
        )
        high = lax.ppermute(lax.slice_in_dim(block, 0, width, axis=dim), axis, backward)
        block = jnp.concatenate([low, block, high], axis=dim)
    return block


def row_norm(values, gain_vec):
    mean_sq = jnp.mean(values * values, axis=-1, keepdims=True)
    return values * lax.rsqrt(mean_sq + EPSILON) * gain_vec


def head_norm(values, head_count):
    shaped = values.reshape(values.shape[:-1] + (head_count, values.shape[-1] // head_count))
    mean_sq = jnp.mean(shaped * shaped, axis=-1, keepdims=True)
    return (shaped * lax.rsqrt(jnp.maximum(mean_sq, FLOOR))).reshape(values.shape)


def split_heads(values, head_count):
    return values.reshape(values.shape[:-1] + (head_count, values.shape[-1] // head_count))


def head_pullback(raw_rows, grad_rows):
    _, pullback = jax.vjp(lambda t: head_norm(t, HEAD_COUNT), raw_rows.astype(jnp.float32))
    return pullback(grad_rows)[0]


def pad_field(field_in):
    widened = padded_2(field_in, (("lon", 2),), 1, True)
    return padded_2(widened, (("lat", 1),), 1, False)


def conv_taps(padded, kernel, lat_n, lon_n, adjoint):
    running = None
    for row_off in range(3):
        for col_off in range(3):
            if adjoint:
                window = padded[
                    :, 2 - row_off : 2 - row_off + lat_n, 2 - col_off : 2 - col_off + lon_n
                ]
                summand = jnp.einsum(
                    "mabc,dc->mabd",
                    window,
                    kernel[row_off, col_off],
                    preferred_element_type=jnp.float32,
                )
            else:
                window = padded[:, row_off : row_off + lat_n, col_off : col_off + lon_n]
                summand = jnp.einsum(
                    "mabc,cd->mabd",
                    window,
                    kernel[row_off, col_off],
                    preferred_element_type=jnp.float32,
                )
            running = summand if running is None else running + summand
    return running


def per_device_general(ensemble, norm_gain, project_weight, output_weight, conv_kernel, cotangent):
    mem_dev, lat_dev, lon_dev, channels = ensemble.shape
    cell_count = lat_dev * lon_dev
    score_scale = 1.0 / math.sqrt(channels // HEAD_COUNT)
    inputs = ensemble.reshape(mem_dev, cell_count, channels).astype(jnp.float32)
    normed = row_norm(inputs, norm_gain).astype(jnp.bfloat16)
    spread = lax.all_to_all(normed, "member", split_axis=1, concat_axis=0, tiled=True)
    projected = jnp.dot(spread, project_weight, preferred_element_type=jnp.float32).astype(
        jnp.bfloat16
    )
    query_raw = projected[..., :channels]
    key_raw = projected[..., channels : 2 * channels]
    value_rows = projected[..., 2 * channels :]
    key_rows = head_norm(key_raw.astype(jnp.float32), HEAD_COUNT).astype(jnp.bfloat16)
    queries = head_norm(query_raw.astype(jnp.float32), HEAD_COUNT).astype(jnp.bfloat16)
    query_heads = split_heads(queries, HEAD_COUNT)
    key_heads = split_heads(key_rows, HEAD_COUNT)
    value_heads = split_heads(value_rows, HEAD_COUNT)
    scores = (
        jnp.einsum("mphd,nphd->mnhp", query_heads, key_heads, preferred_element_type=jnp.float32)
        * score_scale
    )
    expd = jnp.exp(scores)
    soft = expd / jnp.sum(expd, axis=1, keepdims=True)
    rounded = soft.astype(jnp.bfloat16)
    mixed_out = jnp.einsum(
        "mnhp,nphd->mphd", rounded, value_heads, preferred_element_type=jnp.float32
    )
    mixed_out = mixed_out.reshape(query_raw.shape).astype(jnp.bfloat16)
    mixed_out = lax.all_to_all(mixed_out, "member", split_axis=0, concat_axis=1, tiled=True)
    updated = (
        inputs + jnp.dot(mixed_out, output_weight, preferred_element_type=jnp.float32)
    ).astype(jnp.bfloat16)
    field_up = updated.reshape(mem_dev, lat_dev, lon_dev, channels)
    result = field_up.astype(jnp.float32) + conv_taps(
        pad_field(field_up), conv_kernel, lat_dev, lon_dev, False
    )
    result = result.astype(jnp.bfloat16)
    grad_field = cotangent.astype(jnp.float32) + conv_taps(
        pad_field(cotangent), conv_kernel, lat_dev, lon_dev, True
    )
    grad_rows = grad_field.reshape(mem_dev, cell_count, channels)
    grad_mixed = jnp.einsum(
        "mpc,dc->mpd",
        grad_rows.astype(jnp.bfloat16),
        output_weight,
        preferred_element_type=jnp.float32,
    )
    grad_mixed = grad_mixed.astype(jnp.bfloat16)
    grad_mixed = lax.all_to_all(grad_mixed, "member", split_axis=1, concat_axis=0, tiled=True)
    grad_heads = split_heads(grad_mixed, HEAD_COUNT)
    dprob = jnp.einsum(
        "mphd,nphd->mnhp", grad_heads, value_heads, preferred_element_type=jnp.float32
    )
    dscore = (soft * (dprob - jnp.sum(soft * dprob, axis=1, keepdims=True))).astype(jnp.bfloat16)
    query_grad = (
        jnp.einsum("mnhp,nphd->mphd", dscore, key_heads, preferred_element_type=jnp.float32)
        * score_scale
    )
    query_grad = query_grad.reshape(query_raw.shape)
    key_grad = (
        jnp.einsum("mnhp,mphd->nphd", dscore, query_heads, preferred_element_type=jnp.float32)
        * score_scale
    )
    key_grad = key_grad.reshape(key_raw.shape)
    value_grad = jnp.einsum(
        "mnhp,mphd->nphd", rounded, grad_heads, preferred_element_type=jnp.float32
    )
    value_grad = value_grad.reshape(key_raw.shape)
    grad_query_raw = head_pullback(query_raw, query_grad)
    grad_key_raw = head_pullback(key_raw, key_grad)
    grad_proj = jnp.concatenate([grad_query_raw, grad_key_raw, value_grad], axis=-1).astype(
        jnp.bfloat16
    )
    grad_proj = lax.all_to_all(grad_proj, "member", split_axis=0, concat_axis=1, tiled=True)
    grad_normed = jnp.einsum(
        "mpe,ce->mpc", grad_proj, project_weight, preferred_element_type=jnp.float32
    )
    _, pull_norm = jax.vjp(lambda t: row_norm(t, norm_gain), inputs)
    grad_inputs = pull_norm(grad_normed)[0]
    grad_ensemble = (
        (grad_rows + grad_inputs).astype(jnp.bfloat16).reshape(mem_dev, lat_dev, lon_dev, channels)
    )
    return (result, grad_ensemble)


F32 = jnp.float32
BF16 = jnp.bfloat16
VMEM_LIMIT = 48 * 1024 * 1024


def is_even(axis):
    return lax.rem(lax.axis_index(axis), 2) == 0


def stack_kernel(ens_ref, cot_ref, both_ref, first_ref, second_ref, sems):
    _, mem, rows, _, _ = both_ref.shape
    copies = [
        pltpu.make_async_copy(ref, both_ref.at[i], sems.at[i])
        for i, ref in enumerate((ens_ref, cot_ref))
    ]
    for copy in copies:
        copy.start()
    for copy in copies:
        copy.wait()
    even = is_even("lat")
    for array in range(2):
        for member in range(mem):
            first_ref[array, member] = both_ref[array, member, jnp.where(even, rows - 1, 0)]
            second_ref[array, member] = both_ref[array, member, jnp.where(even, 0, rows - 1)]


def pack_strips_kernel(
    both_ref,
    other_ref,
    first_ref,
    second_ref,
    cross_first_ref,
    cross_second_ref,
    after_ref,
    halo_ref,
    chip_ref,
    core_ref,
    low_scr,
    high_scr,
    *,
    lat_count,
):
    _, mem, rows, cols, _ = both_ref.shape
    lat_even = is_even("lat")
    lat = lax.axis_index("lat")
    index = 0
    for array in range(2):
        for member in range(2 * mem):
            if member < mem:
                block, at = both_ref, member
                first, second = first_ref[array, at], second_ref[array, at]
            else:
                block, at = other_ref, member - mem
                first, second = cross_first_ref[array, at], cross_second_ref[array, at]
            first, second = first.astype(F32), second.astype(F32)
            north = jnp.where(lat == 0, 0.0, jnp.where(lat_even, second, first))
            south = jnp.where(lat == lat_count - 1, 0.0, jnp.where(lat_even, first, second))
            halo_ref[0, array, member] = north.astype(BF16)
            halo_ref[1, array, member] = south.astype(BF16)
            slabs = [block[array, at, row].astype(F32) for row in range(rows)]
            for slab in [north] + slabs + [south]:
                low_scr[index : index + 1, :] = slab[0:1]
                high_scr[index : index + 1, :] = slab[cols - 1 : cols]
                index += 1
    even = is_even("lon")
    low, high = low_scr[...], high_scr[...]
    core_ref[...] = jnp.where(even, high, low).astype(BF16)
    chip_ref[...] = jnp.where(even, low, high).astype(BF16)


def dot_nn(a, b):
    return lax.dot_general(a, b, (((1,), (0,)), ((), ())), preferred_element_type=F32)


def same_head_matrix(channels):
    width = channels // HEAD_COUNT
    lane_row = lax.broadcasted_iota(jnp.int32, (channels, channels), 0) // width
    lane_col = lax.broadcasted_iota(jnp.int32, (channels, channels), 1) // width
    return jnp.where(lane_row == lane_col, 1.0, 0.0).astype(BF16)


def head_sums(values, same_head):
    high = values.astype(BF16)
    low = (values - high.astype(F32)).astype(BF16)
    return dot_nn(high, same_head) + dot_nn(low, same_head)


def head_units(raw, same_head):
    raw = raw.astype(F32)
    mean_sq = head_sums(raw * raw, same_head) * (HEAD_COUNT / raw.shape[-1])
    inverse = lax.rsqrt(jnp.maximum(mean_sq, FLOOR))
    return raw, mean_sq, inverse, (raw * inverse).astype(BF16)


def row_rsqrt(values):
    return lax.rsqrt(jnp.mean(values * values, axis=-1, keepdims=True) + EPSILON)


def split_rows(array, count):
    size = array.shape[0] // count
    return [array[i * size : (i + 1) * size] for i in range(count)]


def softmax_members(queries, keys, same_head, scale):
    products = [query * key for query in queries for key in keys]
    scores = dot_nn(jnp.concatenate(products, axis=0), same_head) * scale
    exps = split_rows(jnp.exp(scores), len(products))
    soft = []
    for m in range(len(queries)):
        mine = exps[m * len(keys) : (m + 1) * len(keys)]
        total = mine[0]
        for e in mine[1:]:
            total = total + e
        inverse = 1.0 / total
        soft.append([e * inverse for e in mine])
    return soft


def mix_values(probs, values):
    mixed = None
    for prob, value in zip(probs, values):
        term = prob * value.astype(F32)
        mixed = term if mixed is None else mixed + term
    return mixed.astype(BF16)


def forward_cells(x, mem, groups, gain, project_ref, output_ref, same_head):
    channels = x.shape[-1]
    own_rows = x.shape[0] // groups * mem
    scale = 1.0 / math.sqrt(channels // HEAD_COUNT)
    normed = (x * row_rsqrt(x) * gain).astype(BF16)
    query_raw = dot_nn(normed[:own_rows], project_ref[:, :channels]).astype(BF16)
    key_raw = dot_nn(normed, project_ref[:, channels : 2 * channels]).astype(BF16)
    values = dot_nn(normed, project_ref[:, 2 * channels :]).astype(BF16)
    units = head_units(jnp.concatenate([query_raw, key_raw], axis=0), same_head)[3]
    queries = split_rows(units[:own_rows], mem)
    keys = split_rows(units[own_rows:], groups)
    values = split_rows(values, groups)
    soft = softmax_members(queries, keys, same_head, scale)
    mixed = jnp.concatenate([mix_values(soft[m], values) for m in range(mem)], axis=0)
    return (x[:own_rows] + dot_nn(mixed, output_ref[...])).astype(BF16)


def weights_kernel(
    gain_hbm,
    project_hbm,
    output_hbm,
    gain_ref,
    project_ref,
    output_ref,
    project_t_ref,
    output_t_ref,
    sems,
):
    channels = output_ref.shape[0]
    half = channels // 2
    pieces = [(gain_hbm, gain_ref), (output_hbm, output_ref)]
    for part in range(2):
        rows = pl.ds(part * half, half)
        pieces.append((project_hbm.at[rows], project_ref.at[rows]))
    loads = [
        pltpu.make_async_copy(source, target, sems.at[i])
        for i, (source, target) in enumerate(pieces)
    ]
    for load in loads:
        load.start()
    for load in loads:
        load.wait()
    for kind in range(3):
        lanes = slice(kind * channels, (kind + 1) * channels)
        project_t_ref[lanes, :] = project_ref[:, lanes].T
    output_t_ref[...] = output_ref[...].T


def own_kernel(
    both_ref,
    other_ref,
    gain_ref,
    project_ref,
    output_ref,
    conv_hbm,
    conv_ref,
    proj_ref,
    unit_ref,
    soft_ref,
    inverse_ref,
    pull_ref,
    updated_ref,
    sems,
):
    size = conv_ref.shape[0] // 9
    loads = []
    for tap in range(9):
        at = pl.ds(tap * size, size)
        loads.append(pltpu.make_async_copy(conv_hbm.at[at], conv_ref.at[at], sems.at[tap]))
    for load in loads:
        load.start()
    _, mem, rows, cols, channels = both_ref.shape
    groups = 2 * mem
    cells = rows * cols
    width = channels // HEAD_COUNT
    scale = 1.0 / math.sqrt(width)
    same_head = same_head_matrix(channels)
    own = both_ref[0].reshape(mem * cells, channels)
    other = other_ref[0].reshape(mem * cells, channels)
    x = jnp.concatenate([own, other], axis=0).astype(F32)
    normed = (x * row_rsqrt(x) * gain_ref[...]).astype(BF16)
    proj = dot_nn(normed, project_ref[...]).astype(BF16)
    proj_ref[...] = proj.reshape(groups, cells, 3 * channels)
    both_raw = jnp.concatenate([proj[:, :channels], proj[:, channels : 2 * channels]], axis=0)
    raw, mean_sq, inverse, units = head_units(both_raw, same_head)
    unit_ref[...] = units.reshape(2, groups, cells, channels)
    active = jnp.where(mean_sq > FLOOR, 1.0, jnp.where(mean_sq == FLOOR, 0.5, 0.0))
    pull = active * raw * (inverse * inverse * inverse) / width
    for kind in range(2):
        at = kind * groups * cells
        mine = slice(at, at + mem * cells)
        inverse_ref[kind] = inverse[mine].reshape(mem, cells, channels)
        pull_ref[kind] = pull[mine].reshape(mem, cells, channels)
    units = split_rows(units, 2 * groups)
    soft = softmax_members(units[:groups], units[groups:], same_head, scale)
    for m in range(groups):
        for n in range(groups):
            soft_ref[m * groups + n] = soft[m][n]
    values = split_rows(proj[:, 2 * channels :], groups)
    mixed = jnp.concatenate([mix_values(soft[m], values) for m in range(mem)], axis=0)
    updated = x[: mem * cells] + dot_nn(mixed, output_ref[...])
    updated_ref[...] = updated.astype(BF16).reshape(mem, cells, channels)
    for load in loads:
        load.wait()


def centre_kernel(
    both_ref,
    other_ref,
    halo_ref,
    gain_ref,
    project_ref,
    output_ref,
    conv_ref,
    updated_ref,
    strip_ref,
    strip_out_ref,
    conv_t_ref,
    result_ref,
    grad_ref,
    shift_scr,
    cot_shift_scr,
):
    strip_out_ref[...] = strip_ref[...]
    _, mem, rows, cols, channels = both_ref.shape
    groups = 2 * mem
    tall = rows + 2
    cells = rows * cols
    column = lax.broadcasted_iota(jnp.int32, (cols, channels), 0)
    for r in range(3):
        for c in range(3):
            tap = (3 * r + c) * channels
            turned = (3 * r + 2 - c) * channels
            conv_t_ref[turned : turned + channels, :] = conv_ref[tap : tap + channels, :].T

    def shifted(scr, member, place, slab):
        back = jnp.where(column == 0, 0.0, pltpu.roll(slab, 1, 0))
        ahead = jnp.where(column == cols - 1, 0.0, pltpu.roll(slab, cols - 1, 0))
        rows_at = slice(place * cols, (place + 1) * cols)
        scr[member, rows_at, :channels] = back.astype(BF16)
        scr[member, rows_at, channels : 2 * channels] = slab.astype(BF16)
        scr[member, rows_at, 2 * channels :] = ahead.astype(BF16)

    for member in range(groups):
        ref, at = (both_ref, member) if member < mem else (other_ref, member - mem)
        slabs = [halo_ref[0, 1, member]] + [ref[1, at, row] for row in range(rows)]
        slabs.append(halo_ref[1, 1, member])
        for place, slab in enumerate(slabs):
            shifted(cot_shift_scr, member, place, slab.astype(F32))

    halo = [halo_ref[side, 0, member] for member in range(groups) for side in range(2)]
    x = jnp.concatenate(halo, axis=0).astype(F32)
    same_head = same_head_matrix(channels)
    fresh = forward_cells(x, mem, groups, gain_ref[...], project_ref, output_ref, same_head)
    fresh = split_rows(fresh.astype(F32), 2 * mem)
    for member in range(mem):
        slabs = [fresh[2 * member]]
        for row in range(rows):
            slabs.append(updated_ref[member, row * cols : (row + 1) * cols, :].astype(F32))
        slabs.append(fresh[2 * member + 1])
        for place, slab in enumerate(slabs):
            shifted(shift_scr, member, place, slab)

    both = both_ref[1].reshape(mem * cells, channels)
    other = other_ref[1].reshape(mem * cells, channels)
    total = jnp.concatenate([both, other], axis=0).astype(F32)
    for r in range(3):
        begin = (2 - r) * cols
        window = jnp.concatenate(
            [cot_shift_scr[m, begin : begin + cells, :] for m in range(groups)], axis=0
        )
        total = total + dot_nn(window, conv_t_ref[3 * channels * r : 3 * channels * (r + 1), :])
    grad_ref[...] = total

    total = updated_ref[...].reshape(mem * cells, channels).astype(F32)
    for r in range(3):
        window = jnp.concatenate(
            [shift_scr[m, r * cols : r * cols + cells, :] for m in range(mem)], axis=0
        )
        total = total + dot_nn(window, conv_ref[3 * channels * r : 3 * channels * (r + 1), :])
    result_ref[...] = total


def main_kernel(
    both_ref,
    chip_ref,
    core_ref,
    gain_ref,
    project_ref,
    output_ref,
    conv_ref,
    project_t_ref,
    output_t_ref,
    conv_t_ref,
    proj_ref,
    unit_ref,
    soft_ref,
    inverse_ref,
    pull_ref,
    result_part_ref,
    grad_part_ref,
    result_ref,
    grad_ref,
    strip_scr,
):
    _, mem, rows, cols, channels = both_ref.shape
    groups = 2 * mem
    tall = rows + 2
    cells = rows * cols
    scale = 1.0 / math.sqrt(channels // HEAD_COUNT)
    even = is_even("lon")
    gain = gain_ref[...]
    same_head = same_head_matrix(channels)

    core, chip = core_ref[...].astype(F32), chip_ref[...].astype(F32)
    low, high = jnp.where(even, chip, core), jnp.where(even, core, chip)
    for slot in range(2 * groups):
        strip_scr[slot] = jnp.zeros((16, channels), F32)
        strip_scr[slot, :tall, :] = low[slot * tall : (slot + 1) * tall]
        strip_scr[slot, 8 : 8 + tall, :] = high[slot * tall : (slot + 1) * tall]

    def rim_part(fields, taps_ref, turned):
        sums = []
        for side in range(2):
            total = None
            for r in range(3):
                begin = 8 * side + (2 - r if turned else r)
                window = jnp.concatenate([f[begin : begin + rows] for f in fields], axis=0)
                tap = (3 * r + 2 * side) * channels
                term = dot_nn(window.astype(BF16), taps_ref[tap : tap + channels, :])
                total = term if total is None else total + term
            sums.append(total)
        column = lax.broadcasted_iota(jnp.int32, (cols, channels), 0)
        added = []
        for i in range(len(fields) * rows):
            west, east = sums[0][i : i + 1], sums[1][i : i + 1]
            added.append(
                jnp.where(column == 0, west, 0.0) + jnp.where(column == cols - 1, east, 0.0)
            )
        return jnp.concatenate(added, axis=0)

    cots = [strip_scr[groups + m] for m in range(groups)]
    grad_field = grad_part_ref[...] + rim_part(cots, conv_t_ref, True)
    grad_mixed = dot_nn(grad_field.astype(BF16), output_t_ref[...]).astype(BF16)
    grads = split_rows(grad_mixed, groups)

    x = strip_scr[:groups].reshape(groups * 16, channels)
    fresh = forward_cells(x, mem, groups, gain, project_ref, output_ref, same_head)
    fresh = split_rows(fresh.astype(F32), mem)
    total = result_part_ref[...] + rim_part(fresh, conv_ref, False)
    result_ref[...] = total.astype(BF16).reshape(mem, rows, cols, channels)

    values = [proj_ref[n, :, 2 * channels :] for n in range(groups)]
    products = [grads[m] * values[n] for m in range(groups) for n in range(groups)]
    dprobs = split_rows(dot_nn(jnp.concatenate(products, axis=0), same_head), len(products))
    query_grad = [None] * mem
    key_grad = [None] * mem
    value_grad = [None] * mem
    for m in range(groups):
        soft = [soft_ref[m * groups + n] for n in range(groups)]
        dprob = dprobs[m * groups : (m + 1) * groups]
        mean = soft[0] * dprob[0]
        for n in range(1, groups):
            mean = mean + soft[n] * dprob[n]
        for n in range(groups):
            if m >= mem and n >= mem:
                continue
            dscore = soft[n] * (dprob[n] - mean)
            if m < mem:
                term = dscore * unit_ref[1, n].astype(F32)
                query_grad[m] = term if query_grad[m] is None else query_grad[m] + term
            if n < mem:
                term = dscore * unit_ref[0, m].astype(F32)
                key_grad[n] = term if key_grad[n] is None else key_grad[n] + term
                term = soft[n] * grads[m].astype(F32)
                value_grad[n] = term if value_grad[n] is None else value_grad[n] + term

    pulled = []
    unit_grads = [jnp.concatenate(g, axis=0) * scale for g in (query_grad, key_grad)]
    raws = [
        proj_ref[:mem, :, kind * channels : (kind + 1) * channels]
        .reshape(mem * cells, channels)
        .astype(F32)
        for kind in range(2)
    ]
    inner = head_sums(
        jnp.concatenate([g * raw for g, raw in zip(unit_grads, raws)], axis=0), same_head
    )
    inner = split_rows(inner, 2)
    for kind in range(2):
        inverse = inverse_ref[kind].reshape(mem * cells, channels)
        pull = pull_ref[kind].reshape(mem * cells, channels)
        pulled.append((inverse * unit_grads[kind] - pull * inner[kind]).astype(BF16))
    pulled.append(jnp.concatenate(value_grad, axis=0).astype(BF16))
    grad_proj = jnp.concatenate(pulled, axis=1)
    grad_normed = dot_nn(grad_proj, project_t_ref[...]) * gain
    x = both_ref[0].reshape(mem * cells, channels).astype(F32)
    inverse = row_rsqrt(x)
    inner = jnp.mean(x * grad_normed, axis=-1, keepdims=True)
    total = grad_field[: mem * cells] + inverse * grad_normed
    total = total - x * (inverse * inverse * inverse * inner)
    grad_ref[...] = total.astype(BF16).reshape(mem, rows, cols, channels)


def local_call(kernel, name, operands, out_shape, scratch, pinned=False, cost=None):
    whole = pl.BlockSpec(memory_space=pltpu.VMEM)
    anywhere = pl.BlockSpec(memory_space=pl.ANY)
    specs = [anywhere if in_hbm else whole for _, in_hbm in operands]
    arrays = [
        pltpu.with_memory_space_constraint(array, pltpu.HBM) if in_hbm else array
        for array, in_hbm in operands
    ]

    def keep(shape):
        return pltpu.VMEM(shape.shape, shape.dtype) if pinned else shape

    return pl.pallas_call(
        kernel,
        out_shape=jax.tree.map(keep, out_shape),
        in_specs=specs,
        out_specs=jax.tree.map(lambda _: whole, out_shape),
        scratch_shapes=scratch,
        compiler_params=pltpu.CompilerParams(vmem_limit_bytes=VMEM_LIMIT),
        cost_estimate=cost,
        name=name,
    )(*arrays)


def here(*arrays):
    return [(array, False) for array in arrays]


def in_hbm(*arrays):
    return [(array, True) for array in arrays]


def per_device_paired(ensemble, norm_gain, project_weight, output_weight, conv_kernel, cotangent):
    mem, rows, cols, channels = ensemble.shape
    groups = 2 * mem
    cells = rows * cols
    tall = rows + 2
    lon_count = lax.axis_size("lon")
    lat_count = lax.axis_size("lat")
    bf16 = functools.partial(jax.ShapeDtypeStruct, dtype=BF16)
    f32 = functools.partial(jax.ShapeDtypeStruct, dtype=F32)
    row = (2, mem, cols, channels)
    swap = [(0, 1), (1, 0)]
    core_pairs = [(i, i ^ 1) for i in range(lon_count)]
    chip_pairs = [(i, (i - 1 if i % 2 == 0 else i + 1) % lon_count) for i in range(lon_count)]

    def lat_swap(offset, across):
        pairs = []
        for member in range(2):
            for lat in range(lat_count):
                for lon in range(lon_count):
                    to = (member, lat + 1 if lat % 2 == offset else lat - 1, lon)
                    if not 0 <= to[1] < lat_count:
                        to = (member, lat, lon ^ 1)
                    elif across:
                        to = (1 - member,) + to[1:]
                    me = (member * lat_count + lat) * lon_count + lon
                    pairs.append((me, (to[0] * lat_count + to[1]) * lon_count + to[2]))
        return pairs

    both, first_send, second_send = local_call(
        stack_kernel,
        "stack",
        in_hbm(ensemble, cotangent),
        (bf16((2,) + ensemble.shape), bf16(row), bf16(row)),
        [pltpu.SemaphoreType.DMA((2,))],
        pinned=True,
    )
    other = lax.ppermute(both, "member", swap)
    everyone = ("member", "lat", "lon")
    first = lax.ppermute(first_send, everyone, lat_swap(0, False))
    second = lax.ppermute(second_send, everyone, lat_swap(1, False))
    cross_first = lax.ppermute(first_send, everyone, lat_swap(0, True))
    cross_second = lax.ppermute(second_send, everyone, lat_swap(1, True))

    weights = (norm_gain.reshape(1, channels), project_weight, output_weight)
    weights = local_call(
        weights_kernel,
        "load_weights",
        in_hbm(*weights),
        (
            f32((1, channels)),
            bf16(project_weight.shape),
            bf16(output_weight.shape),
            bf16((3 * channels, channels)),
            bf16((channels, channels)),
        ),
        [pltpu.SemaphoreType.DMA((4,))],
        pinned=True,
    )
    conv, *held = local_call(
        own_kernel,
        "own_cells",
        here(both, other, *weights[:3]) + in_hbm(conv_kernel.reshape(9 * channels, channels)),
        (
            bf16((9 * channels, channels)),
            bf16((groups, cells, 3 * channels)),
            bf16((2, groups, cells, channels)),
            f32((groups * groups, cells, channels)),
            f32((2, mem, cells, channels)),
            f32((2, mem, cells, channels)),
            bf16((mem, cells, channels)),
        ),
        [pltpu.SemaphoreType.DMA((9,))],
        pinned=True,
    )

    strip = (2 * groups * tall, channels)
    halo, chip_send, core_send = local_call(
        functools.partial(pack_strips_kernel, lat_count=lat_count),
        "pack_strips",
        here(both, other, first, second, cross_first, cross_second, held[-1]),
        (bf16((2, 2, groups, cols, channels)), bf16(strip), bf16(strip)),
        [pltpu.VMEM(strip, F32)] * 2,
    )
    chip = lax.ppermute(chip_send, "lon", chip_pairs)

    gain, project, output, project_t, output_t = weights
    core_send, conv_t, *parts = local_call(
        centre_kernel,
        "centre",
        here(both, other, halo, gain, project, output, conv, held[-1], core_send),
        (
            bf16(strip),
            bf16((9 * channels, channels)),
            f32((mem * cells, channels)),
            f32((groups * cells, channels)),
        ),
        [
            pltpu.VMEM((mem, tall * cols, 3 * channels), BF16),
            pltpu.VMEM((groups, tall * cols, 3 * channels), BF16),
        ],
        pinned=True,
    )
    core = lax.ppermute(core_send, "lon", core_pairs)
    main_weights = (gain, project, output, conv, project_t, output_t, conv_t)
    return local_call(
        main_kernel,
        "main",
        here(both, chip, core, *main_weights, *held[:-1], *parts),
        (bf16(ensemble.shape), bf16(ensemble.shape)),
        [pltpu.VMEM((2 * groups, 16, channels), F32)],
    )


def solution(mesh):
    paired = mesh.shape["member"] == 2 and mesh.shape["lon"] % 2 == 0
    per_device = per_device_paired if paired else per_device_general
    in_specs = (
        P("member", "lat", "lon", None),
        P(),
        P(),
        P(),
        P(),
        P("member", "lat", "lon", None),
    )
    out_specs = (P("member", "lat", "lon", None), P("member", "lat", "lon", None))
    return jax.shard_map(
        per_device, mesh=mesh, in_specs=in_specs, out_specs=out_specs, check_vma=False
    )
```

```python
import functools
import math

import jax
import jax.numpy as jnp
from jax import lax
from jax.experimental import pallas as pl
from jax.experimental.pallas import tpu as pltpu
from jax.sharding import PartitionSpec as P

HEAD_COUNT = 8


FLOOR = 0.5
EPSILON = 1e-06


def padded_2(block, sides, width, periodic):
    for axis, dim in sides:
        count = lax.axis_size(axis)
        forward = [(i, i + 1) for i in range(count - 1)]
        if periodic:
            forward.append((count - 1, 0))
        backward = [(target, source) for source, target in forward]
        low = lax.ppermute(
            lax.slice_in_dim(block, block.shape[dim] - width, None, axis=dim), axis, forward
        )
        high = lax.ppermute(lax.slice_in_dim(block, 0, width, axis=dim), axis, backward)
        block = jnp.concatenate([low, block, high], axis=dim)
    return block


def row_norm(values, gain_vec):
    mean_sq = jnp.mean(values * values, axis=-1, keepdims=True)
    return values * lax.rsqrt(mean_sq + EPSILON) * gain_vec


def head_norm(values, head_count):
    shaped = values.reshape(values.shape[:-1] + (head_count, values.shape[-1] // head_count))
    mean_sq = jnp.mean(shaped * shaped, axis=-1, keepdims=True)
    return (shaped * lax.rsqrt(jnp.maximum(mean_sq, FLOOR))).reshape(values.shape)


def split_heads(values, head_count):
    return values.reshape(values.shape[:-1] + (head_count, values.shape[-1] // head_count))


def head_pullback(raw_rows, grad_rows):
    _, pullback = jax.vjp(lambda t: head_norm(t, HEAD_COUNT), raw_rows.astype(jnp.float32))
    return pullback(grad_rows)[0]


def pad_field(field_in):
    widened = padded_2(field_in, (("lon", 2),), 1, True)
    return padded_2(widened, (("lat", 1),), 1, False)


def conv_taps(padded, kernel, lat_n, lon_n, adjoint):
    running = None
    for row_off in range(3):
        for col_off in range(3):
            if adjoint:
                window = padded[
                    :, 2 - row_off : 2 - row_off + lat_n, 2 - col_off : 2 - col_off + lon_n
                ]
                summand = jnp.einsum(
                    "mabc,dc->mabd",
                    window,
                    kernel[row_off, col_off],
                    preferred_element_type=jnp.float32,
                )
            else:
                window = padded[:, row_off : row_off + lat_n, col_off : col_off + lon_n]
                summand = jnp.einsum(
                    "mabc,cd->mabd",
                    window,
                    kernel[row_off, col_off],
                    preferred_element_type=jnp.float32,
                )
            running = summand if running is None else running + summand
    return running


def per_device_general(ensemble, norm_gain, project_weight, output_weight, conv_kernel, cotangent):
    mem_dev, lat_dev, lon_dev, channels = ensemble.shape
    cell_count = lat_dev * lon_dev
    score_scale = 1.0 / math.sqrt(channels // HEAD_COUNT)
    inputs = ensemble.reshape(mem_dev, cell_count, channels).astype(jnp.float32)
    normed = row_norm(inputs, norm_gain).astype(jnp.bfloat16)
    spread = lax.all_to_all(normed, "member", split_axis=1, concat_axis=0, tiled=True)
    projected = jnp.dot(spread, project_weight, preferred_element_type=jnp.float32).astype(
        jnp.bfloat16
    )
    query_raw = projected[..., :channels]
    key_raw = projected[..., channels : 2 * channels]
    value_rows = projected[..., 2 * channels :]
    key_rows = head_norm(key_raw.astype(jnp.float32), HEAD_COUNT).astype(jnp.bfloat16)
    queries = head_norm(query_raw.astype(jnp.float32), HEAD_COUNT).astype(jnp.bfloat16)
    query_heads = split_heads(queries, HEAD_COUNT)
    key_heads = split_heads(key_rows, HEAD_COUNT)
    value_heads = split_heads(value_rows, HEAD_COUNT)
    scores = (
        jnp.einsum("mphd,nphd->mnhp", query_heads, key_heads, preferred_element_type=jnp.float32)
        * score_scale
    )
    expd = jnp.exp(scores)
    soft = expd / jnp.sum(expd, axis=1, keepdims=True)
    rounded = soft.astype(jnp.bfloat16)
    mixed_out = jnp.einsum(
        "mnhp,nphd->mphd", rounded, value_heads, preferred_element_type=jnp.float32
    )
    mixed_out = mixed_out.reshape(query_raw.shape).astype(jnp.bfloat16)
    mixed_out = lax.all_to_all(mixed_out, "member", split_axis=0, concat_axis=1, tiled=True)
    updated = (
        inputs + jnp.dot(mixed_out, output_weight, preferred_element_type=jnp.float32)
    ).astype(jnp.bfloat16)
    field_up = updated.reshape(mem_dev, lat_dev, lon_dev, channels)
    result = field_up.astype(jnp.float32) + conv_taps(
        pad_field(field_up), conv_kernel, lat_dev, lon_dev, False
    )
    result = result.astype(jnp.bfloat16)
    grad_field = cotangent.astype(jnp.float32) + conv_taps(
        pad_field(cotangent), conv_kernel, lat_dev, lon_dev, True
    )
    grad_rows = grad_field.reshape(mem_dev, cell_count, channels)
    grad_mixed = jnp.einsum(
        "mpc,dc->mpd",
        grad_rows.astype(jnp.bfloat16),
        output_weight,
        preferred_element_type=jnp.float32,
    )
    grad_mixed = grad_mixed.astype(jnp.bfloat16)
    grad_mixed = lax.all_to_all(grad_mixed, "member", split_axis=1, concat_axis=0, tiled=True)
    grad_heads = split_heads(grad_mixed, HEAD_COUNT)
    dprob = jnp.einsum(
        "mphd,nphd->mnhp", grad_heads, value_heads, preferred_element_type=jnp.float32
    )
    dscore = (soft * (dprob - jnp.sum(soft * dprob, axis=1, keepdims=True))).astype(jnp.bfloat16)
    query_grad = (
        jnp.einsum("mnhp,nphd->mphd", dscore, key_heads, preferred_element_type=jnp.float32)
        * score_scale
    )
    query_grad = query_grad.reshape(query_raw.shape)
    key_grad = (
        jnp.einsum("mnhp,mphd->nphd", dscore, query_heads, preferred_element_type=jnp.float32)
        * score_scale
    )
    key_grad = key_grad.reshape(key_raw.shape)
    value_grad = jnp.einsum(
        "mnhp,mphd->nphd", rounded, grad_heads, preferred_element_type=jnp.float32
    )
    value_grad = value_grad.reshape(key_raw.shape)
    grad_query_raw = head_pullback(query_raw, query_grad)
    grad_key_raw = head_pullback(key_raw, key_grad)
    grad_proj = jnp.concatenate([grad_query_raw, grad_key_raw, value_grad], axis=-1).astype(
        jnp.bfloat16
    )
    grad_proj = lax.all_to_all(grad_proj, "member", split_axis=0, concat_axis=1, tiled=True)
    grad_normed = jnp.einsum(
        "mpe,ce->mpc", grad_proj, project_weight, preferred_element_type=jnp.float32
    )
    _, pull_norm = jax.vjp(lambda t: row_norm(t, norm_gain), inputs)
    grad_inputs = pull_norm(grad_normed)[0]
    grad_ensemble = (
        (grad_rows + grad_inputs).astype(jnp.bfloat16).reshape(mem_dev, lat_dev, lon_dev, channels)
    )
    return (result, grad_ensemble)


F32 = jnp.float32
BF16 = jnp.bfloat16
VMEM_LIMIT = 24 * 1024 * 1024


def is_even(axis):
    return lax.rem(lax.axis_index(axis), 2) == 0


def load_kernel(*refs):
    count = len(refs) // 2
    sems = refs[-1]
    copies = [pltpu.make_async_copy(refs[i], refs[count + i], sems.at[i]) for i in range(count)]
    for copy in copies:
        copy.start()
    for copy in copies:
        copy.wait()


def stack_kernel(ens_ref, cot_ref, both_ref, ring_ref, inner_ref, end_scr, sems):
    _, mem, rows, cols, _ = both_ref.shape
    copies = [
        pltpu.make_async_copy(ref, both_ref.at[i], sems.at[i])
        for i, ref in enumerate((ens_ref, cot_ref))
    ]
    for copy in copies:
        copy.start()
    for copy in copies:
        copy.wait()
    index = 0
    for array in range(2):
        for member in range(mem):
            slot = array * mem + member
            for side, row in enumerate((0, rows - 1)):
                at = (2 * slot + side) * cols
                ring_ref[at : at + cols, :] = both_ref[array, member, row]
            for row in range(1, rows - 1):
                slab = both_ref[array, member, row]
                inner_ref[array, member, row - 1] = slab
                slab = slab.astype(F32)
                end_scr[index : index + 1, :] = slab[0:1]
                end_scr[index + 1 : index + 2, :] = slab[cols - 1 : cols]
                index += 2
    ring_ref[4 * mem * cols :, :] = end_scr[...].astype(BF16)


def ring_row(ring_ref, mem, cols, array, member, side):
    at = (2 * (array * mem + member) + side) * cols
    return ring_ref[at : at + cols, :]


def pack_strips_kernel(both_ref, ring_ref, after_ref, chip_ref, core_ref, low_scr, high_scr):
    _, mem, rows, cols, _ = both_ref.shape
    ends = ring_ref[4 * mem * cols :, :].astype(F32)
    index = 0
    for array in range(2):
        for member in range(2 * mem):
            for row in range(rows):
                if member < mem:
                    slab = both_ref[array, member, row].astype(F32)
                elif row in (0, rows - 1):
                    side = 0 if row == 0 else 1
                    slab = ring_row(ring_ref, mem, cols, array, member - mem, side).astype(F32)
                else:
                    at = 2 * ((array * mem + member - mem) * (rows - 2) + row - 1)
                    slab = ends[at : at + 2]
                low_scr[index : index + 1, :] = slab[0:1]
                high_scr[index : index + 1, :] = slab[slab.shape[0] - 1 :]
                index += 1
    even = is_even("lon")
    low, high = low_scr[...], high_scr[...]
    core_ref[...] = jnp.where(even, high, low).astype(BF16)
    chip_ref[...] = jnp.where(even, low, high).astype(BF16)


def rim_columns(chip_ref, core_ref):
    even = is_even("lon")
    chip, core = chip_ref[...].astype(F32), core_ref[...].astype(F32)
    return jnp.where(even, chip, core), jnp.where(even, core, chip)


def pack_rows_kernel(
    both_ref, ring_ref, chip_ref, core_ref, after_ref, first_ref, second_ref, edge_scr
):
    _, mem, rows, cols, _ = both_ref.shape
    slots = 4 * mem
    even = is_even("lat")
    west, east = rim_columns(chip_ref, core_ref)
    for slot in range(slots):
        array, member = divmod(slot, 2 * mem)
        if member < mem:
            pair = [both_ref[array, member, row] for row in (0, rows - 1)]
        else:
            pair = [ring_row(ring_ref, mem, cols, array, member - mem, side) for side in (0, 1)]
        start, stop = (slab.astype(F32) for slab in pair)
        at = slice(slot * cols, (slot + 1) * cols)
        first_ref[at, :] = jnp.where(even, stop, start).astype(BF16)
        second_ref[at, :] = jnp.where(even, start, stop).astype(BF16)
        top, low = slot * rows, (slot + 1) * rows - 1
        for side, column in enumerate((west, east)):
            place = side * slots + slot
            start, stop = column[top : top + 1], column[low : low + 1]
            edge_scr[0, place : place + 1, :] = jnp.where(even, stop, start)
            edge_scr[1, place : place + 1, :] = jnp.where(even, start, stop)
    first_ref[slots * cols :, :] = edge_scr[0].astype(BF16)
    second_ref[slots * cols :, :] = edge_scr[1].astype(BF16)


def dot_nn(a, b):
    return lax.dot_general(a, b, (((1,), (0,)), ((), ())), preferred_element_type=F32)


def same_head_matrix(channels):
    width = channels // HEAD_COUNT
    lane_row = lax.broadcasted_iota(jnp.int32, (channels, channels), 0) // width
    lane_col = lax.broadcasted_iota(jnp.int32, (channels, channels), 1) // width
    return jnp.where(lane_row == lane_col, 1.0, 0.0).astype(BF16)


def head_sums(values, same_head):
    high = values.astype(BF16)
    low = (values - high.astype(F32)).astype(BF16)
    return dot_nn(high, same_head) + dot_nn(low, same_head)


def head_units(raw, same_head):
    raw = raw.astype(F32)
    mean_sq = head_sums(raw * raw, same_head) * (HEAD_COUNT / raw.shape[-1])
    inverse = lax.rsqrt(jnp.maximum(mean_sq, FLOOR))
    return raw, mean_sq, inverse, (raw * inverse).astype(BF16)


def row_rsqrt(values):
    return lax.rsqrt(jnp.mean(values * values, axis=-1, keepdims=True) + EPSILON)


def split_rows(array, count):
    size = array.shape[0] // count
    return [array[i * size : (i + 1) * size] for i in range(count)]


def softmax_members(queries, keys, same_head, scale):
    products = [query * key for query in queries for key in keys]
    scores = dot_nn(jnp.concatenate(products, axis=0), same_head) * scale
    exps = split_rows(jnp.exp(scores), len(products))
    soft = []
    for m in range(len(queries)):
        mine = exps[m * len(keys) : (m + 1) * len(keys)]
        total = mine[0]
        for e in mine[1:]:
            total = total + e
        inverse = 1.0 / total
        soft.append([e * inverse for e in mine])
    return soft


def mix_values(probs, values):
    mixed = None
    for prob, value in zip(probs, values):
        term = prob.astype(BF16).astype(F32) * value.astype(F32)
        mixed = term if mixed is None else mixed + term
    return mixed.astype(BF16)


def forward_cells(x, mem, groups, gain, project_ref, output_ref, same_head):
    channels = x.shape[-1]
    own_rows = x.shape[0] // groups * mem
    scale = 1.0 / math.sqrt(channels // HEAD_COUNT)
    normed = (x * row_rsqrt(x) * gain).astype(BF16)
    query_raw = dot_nn(normed[:own_rows], project_ref[:, :channels]).astype(BF16)
    key_raw = dot_nn(normed, project_ref[:, channels : 2 * channels]).astype(BF16)
    values = dot_nn(normed, project_ref[:, 2 * channels :]).astype(BF16)
    units = head_units(jnp.concatenate([query_raw, key_raw], axis=0), same_head)[3]
    queries = split_rows(units[:own_rows], mem)
    keys = split_rows(units[own_rows:], groups)
    values = split_rows(values, groups)
    soft = softmax_members(queries, keys, same_head, scale)
    mixed = jnp.concatenate([mix_values(soft[m], values) for m in range(mem)], axis=0)
    return (x[:own_rows] + dot_nn(mixed, output_ref[...])).astype(BF16)


def shift_row(scr, member, place, slab, west, east):
    cols, channels = slab.shape
    column = lax.broadcasted_iota(jnp.int32, (cols, channels), 0)
    back = jnp.where(column == 0, west, pltpu.roll(slab, 1, 0))
    ahead = jnp.where(column == cols - 1, east, pltpu.roll(slab, cols - 1, 0))
    rows_at = slice(place * cols, (place + 1) * cols)
    scr[member, rows_at, :channels] = back.astype(BF16)
    scr[member, rows_at, channels : 2 * channels] = slab.astype(BF16)
    scr[member, rows_at, 2 * channels :] = ahead.astype(BF16)


def tap_rows(taps_ref, r):
    size = taps_ref.shape[0] // 3
    return taps_ref[r * size : (r + 1) * size, :]


def own_kernel(
    both_ref,
    ring_ref,
    inner_ref,
    gain_ref,
    project_ref,
    output_ref,
    conv_ref,
    project_t_ref,
    output_t_ref,
    conv_t_ref,
    proj_ref,
    unit_ref,
    soft_ref,
    inverse_ref,
    pull_ref,
    updated_ref,
):
    _, mem, rows, cols, channels = both_ref.shape
    groups = 2 * mem
    cells = rows * cols
    width = channels // HEAD_COUNT
    scale = 1.0 / math.sqrt(width)
    same_head = same_head_matrix(channels)
    slabs = [both_ref[0].reshape(mem * cells, channels)]
    for member in range(mem):
        slabs.append(ring_row(ring_ref, mem, cols, 0, member, 0))
        slabs.append(inner_ref[0, member].reshape((rows - 2) * cols, channels))
        slabs.append(ring_row(ring_ref, mem, cols, 0, member, 1))
    x = jnp.concatenate(slabs, axis=0).astype(F32)
    normed = (x * row_rsqrt(x) * gain_ref[...]).astype(BF16)
    proj = dot_nn(normed, project_ref[...]).astype(BF16)
    proj_ref[...] = proj.reshape(groups, cells, 3 * channels)
    both_raw = jnp.concatenate([proj[:, :channels], proj[:, channels : 2 * channels]], axis=0)
    raw, mean_sq, inverse, units = head_units(both_raw, same_head)
    unit_ref[...] = units.reshape(2, groups, cells, channels)
    active = jnp.where(mean_sq > FLOOR, 1.0, jnp.where(mean_sq == FLOOR, 0.5, 0.0))
    pull = active * raw * (inverse * inverse * inverse) / width
    for kind in range(2):
        at = kind * groups * cells
        mine = slice(at, at + mem * cells)
        inverse_ref[kind] = inverse[mine].reshape(mem, cells, channels)
        pull_ref[kind] = pull[mine].reshape(mem, cells, channels)
    units = split_rows(units, 2 * groups)
    soft = softmax_members(units[:groups], units[groups:], same_head, scale)
    for m in range(groups):
        for n in range(groups):
            soft_ref[m * groups + n] = soft[m][n]
    values = split_rows(proj[:, 2 * channels :], groups)
    mixed = jnp.concatenate([mix_values(soft[m], values) for m in range(mem)], axis=0)
    updated = x[: mem * cells] + dot_nn(mixed, output_ref[...])
    updated_ref[...] = updated.astype(BF16).reshape(mem, cells, channels)
    output_t_ref[...] = output_ref[...].T
    for kind in range(3):
        lanes = slice(kind * channels, (kind + 1) * channels)
        project_t_ref[lanes, :] = project_ref[:, lanes].T
    for r in range(3):
        for c in range(3):
            tap = (3 * r + c) * channels
            turned = (3 * r + 2 - c) * channels
            conv_t_ref[turned : turned + channels, :] = conv_ref[tap : tap + channels, :].T


def backward_cells(
    pick, grad_field, x, gain, weights_t, proj_ref, unit_ref, soft_ref, inverse_ref, pull_ref
):
    project_t_ref, output_t_ref = weights_t
    groups = proj_ref.shape[0]
    mem = inverse_ref.shape[1]
    channels = x.shape[-1]
    scale = 1.0 / math.sqrt(channels // HEAD_COUNT)
    same_head = same_head_matrix(channels)
    grad_mixed = dot_nn(grad_field.astype(BF16), output_t_ref[...]).astype(BF16)
    grads = split_rows(grad_mixed, groups)
    values = [pick(proj_ref[n, :, 2 * channels :]) for n in range(groups)]
    products = [grads[m] * values[n] for m in range(groups) for n in range(groups)]
    dprobs = split_rows(dot_nn(jnp.concatenate(products, axis=0), same_head), len(products))
    units = [[pick(unit_ref[k, n]).astype(F32) for n in range(groups)] for k in range(2)]
    query_grad = [None] * mem
    key_grad = [None] * mem
    value_grad = [None] * mem
    for m in range(groups):
        soft = [pick(soft_ref[m * groups + n]) for n in range(groups)]
        dprob = dprobs[m * groups : (m + 1) * groups]
        mean = soft[0] * dprob[0]
        for n in range(1, groups):
            mean = mean + soft[n] * dprob[n]
        for n in range(groups):
            if m >= mem and n >= mem:
                continue
            dscore = soft[n] * (dprob[n] - mean)
            if m < mem:
                term = dscore * units[1][n]
                query_grad[m] = term if query_grad[m] is None else query_grad[m] + term
            if n < mem:
                term = dscore * units[0][m]
                key_grad[n] = term if key_grad[n] is None else key_grad[n] + term
                term = soft[n] * grads[m].astype(F32)
                value_grad[n] = term if value_grad[n] is None else value_grad[n] + term

    unit_grads = [jnp.concatenate(g, axis=0) * scale for g in (query_grad, key_grad)]

    def members(take):
        return jnp.concatenate([pick(take(m)) for m in range(mem)], axis=0)

    raws = []
    for kind in range(2):
        lanes = slice(kind * channels, (kind + 1) * channels)
        raws.append(members(lambda m: proj_ref[m, :, lanes]).astype(F32))
    inner = head_sums(
        jnp.concatenate([g * raw for g, raw in zip(unit_grads, raws)], axis=0), same_head
    )
    inner = split_rows(inner, 2)
    pulled = []
    for kind in range(2):
        inverse = members(lambda m: inverse_ref[kind, m])
        pull = members(lambda m: pull_ref[kind, m])
        pulled.append((inverse * unit_grads[kind] - pull * inner[kind]).astype(BF16))
    pulled.append(jnp.concatenate(value_grad, axis=0).astype(BF16))
    grad_normed = dot_nn(jnp.concatenate(pulled, axis=1), project_t_ref[...]) * gain
    inverse = row_rsqrt(x)
    inner = jnp.mean(x * grad_normed, axis=-1, keepdims=True)
    total = grad_field[: x.shape[0]] + inverse * grad_normed
    return (total - x * (inverse * inverse * inverse * inner)).astype(BF16)


def centre_kernel(
    both_ref,
    ring_ref,
    inner_ref,
    chip_ref,
    core_ref,
    gain_ref,
    project_ref,
    output_ref,
    conv_ref,
    project_t_ref,
    output_t_ref,
    conv_t_ref,
    proj_ref,
    unit_ref,
    soft_ref,
    inverse_ref,
    pull_ref,
    updated_ref,
    result_ref,
    grad_ref,
    result_part_ref,
    grad_part_ref,
    shift_scr,
    cot_shift_scr,
    strip_scr,
):
    _, mem, rows, cols, channels = both_ref.shape
    groups = 2 * mem
    cells = rows * cols
    gain = gain_ref[...]
    same_head = same_head_matrix(channels)
    west, east = rim_columns(chip_ref, core_ref)

    def convolve(scr, count, start, taps_ref, turned):
        sums = [
            [start[(m * rows + a) * cols : (m * rows + a + 1) * cols] for a in range(rows)]
            for m in range(count)
        ]
        for r in range(3):
            step = 1 - r if turned else r - 1
            outs = [a for a in range(rows) if 0 <= a + step < rows]
            begin, end = outs[0] + step, outs[-1] + step + 1
            window = jnp.concatenate(
                [scr[m, begin * cols : end * cols, :] for m in range(count)], axis=0
            )
            terms = split_rows(dot_nn(window, tap_rows(taps_ref, r)), count * len(outs))
            for m in range(count):
                for i, a in enumerate(outs):
                    sums[m][a] = sums[m][a] + terms[m * len(outs) + i]
        return sums

    cots = []
    for member in range(groups):
        for row in range(rows):
            if member < mem:
                slab = both_ref[1, member, row]
            elif row in (0, rows - 1):
                slab = ring_row(ring_ref, mem, cols, 1, member - mem, 0 if row == 0 else 1)
            else:
                slab = inner_ref[1, member - mem, row - 1]
            slab = slab.astype(F32)
            cots.append(slab)
            at = (groups + member) * rows + row
            shift_row(cot_shift_scr, member, row, slab, west[at : at + 1], east[at : at + 1])
    sums = convolve(cot_shift_scr, groups, jnp.concatenate(cots, axis=0), conv_t_ref, True)
    for member in range(groups):
        grad_part_ref[member, :cols, :] = sums[member][0]
        grad_part_ref[member, cols:, :] = sums[member][rows - 1]
    grad_field = jnp.concatenate([slab for s in sums for slab in s[1 : rows - 1]], axis=0)

    for member in range(groups):
        at = member * rows
        strip_scr[member] = jnp.zeros((16, channels), F32)
        strip_scr[member, :rows, :] = west[at : at + rows]
        strip_scr[member, 8 : 8 + rows, :] = east[at : at + rows]
    x = strip_scr[...].reshape(groups * 16, channels)
    fresh = forward_cells(x, mem, groups, gain, project_ref, output_ref, same_head)
    fresh = split_rows(fresh.astype(F32), mem)

    pick = lambda array: array[cols : cells - cols]
    x = both_ref[0, :, 1 : rows - 1].reshape(mem * (cells - 2 * cols), channels).astype(F32)
    total = backward_cells(
        pick,
        grad_field,
        x,
        gain,
        (project_t_ref, output_t_ref),
        proj_ref,
        unit_ref,
        soft_ref,
        inverse_ref,
        pull_ref,
    )
    grad_ref[...] = total.reshape(mem, rows - 2, cols, channels)

    for member in range(mem):
        for row in range(rows):
            slab = updated_ref[member, row * cols : (row + 1) * cols, :].astype(F32)
            ends = fresh[member][row : row + 1], fresh[member][8 + row : 9 + row]
            shift_row(shift_scr, member, row, slab, *ends)
    start = updated_ref[...].reshape(mem * cells, channels).astype(F32)
    sums = convolve(shift_scr, mem, start, conv_ref, False)
    for member in range(mem):
        result_part_ref[member, :cols, :] = sums[member][0]
        result_part_ref[member, cols:, :] = sums[member][rows - 1]
        for row in range(1, rows - 1):
            result_ref[member, row - 1] = sums[member][row].astype(BF16)


def main_kernel(
    both_ref,
    first_ref,
    second_ref,
    gain_ref,
    project_ref,
    output_ref,
    conv_ref,
    project_t_ref,
    output_t_ref,
    conv_t_ref,
    proj_ref,
    unit_ref,
    soft_ref,
    inverse_ref,
    pull_ref,
    inner_result_ref,
    inner_grad_ref,
    result_part_ref,
    grad_part_ref,
    result_ref,
    grad_ref,
    shift_scr,
    cot_shift_scr,
    corner_scr,
    *,
    lat_count,
):
    _, mem, rows, cols, channels = both_ref.shape
    groups = 2 * mem
    slots = 2 * groups
    cells = rows * cols
    gain = gain_ref[...]
    same_head = same_head_matrix(channels)
    lat_even = is_even("lat")
    lat = lax.axis_index("lat")

    def halos(at):
        first, second = first_ref[at, :].astype(F32), second_ref[at, :].astype(F32)
        north = jnp.where(lat == 0, 0.0, jnp.where(lat_even, second, first))
        south = jnp.where(lat == lat_count - 1, 0.0, jnp.where(lat_even, first, second))
        return north, south

    halo = [halos(slice(slot * cols, (slot + 1) * cols)) for slot in range(slots)]
    corners = halos(slice(slots * cols, slots * cols + 2 * slots))

    def corner(side, slot, end):
        at = end * slots + slot
        return corners[side][at : at + 1]

    def halo_part(scr, count, taps_ref, turned):
        north, south = (2, 0) if turned else (0, 2)
        parts = []
        for side, r in ((0, north), (1, south)):
            window = jnp.concatenate(
                [scr[m, side * cols : (side + 1) * cols, :] for m in range(count)], axis=0
            )
            parts.append(split_rows(dot_nn(window, tap_rows(taps_ref, r)), count))
        return jnp.concatenate([parts[side][m] for m in range(count) for side in (0, 1)], axis=0)

    for member in range(groups):
        slot = groups + member
        for side in (0, 1):
            ends = corner(side, slot, 0), corner(side, slot, 1)
            shift_row(cot_shift_scr, member, side, halo[slot][side], *ends)
    grad_field = grad_part_ref[...].reshape(groups * 2 * cols, channels)
    grad_field = grad_field + halo_part(cot_shift_scr, groups, conv_t_ref, True)

    blocks = []
    for member in range(groups):
        corner_scr[member] = jnp.zeros((16, channels), F32)
        for side in (0, 1):
            for end in (0, 1):
                at = 2 * side + end
                corner_scr[member, at : at + 1, :] = corner(side, member, end)
        blocks += [halo[member][0], halo[member][1], corner_scr[member]]
    x = jnp.concatenate(blocks, axis=0)
    fresh = forward_cells(x, mem, groups, gain, project_ref, output_ref, same_head)
    fresh = split_rows(fresh.astype(F32), mem)

    pick = lambda array: jnp.concatenate([array[:cols], array[cells - cols :]], axis=0)
    x = [both_ref[0, m, row] for m in range(mem) for row in (0, rows - 1)]
    total = backward_cells(
        pick,
        grad_field,
        jnp.concatenate(x, axis=0).astype(F32),
        gain,
        (project_t_ref, output_t_ref),
        proj_ref,
        unit_ref,
        soft_ref,
        inverse_ref,
        pull_ref,
    )

    for member in range(mem):
        for side in (0, 1):
            slab = fresh[member][side * cols : (side + 1) * cols]
            at = 2 * cols + 2 * side
            ends = fresh[member][at : at + 1], fresh[member][at + 1 : at + 2]
            shift_row(shift_scr, member, side, slab, *ends)
    outer = result_part_ref[...].reshape(mem * 2 * cols, channels)
    outer = (outer + halo_part(shift_scr, mem, conv_ref, False)).astype(BF16)
    outputs = (
        (result_ref, inner_result_ref, split_rows(outer, 2 * mem)),
        (grad_ref, inner_grad_ref, split_rows(total, 2 * mem)),
    )
    for out_ref, inner_ref, edge in outputs:
        for member in range(mem):
            out_ref[member, 0] = edge[2 * member]
            out_ref[member, rows - 1] = edge[2 * member + 1]
            for row in range(1, rows - 1):
                out_ref[member, row] = inner_ref[member, row - 1]


def local_call(kernel, name, operands, out_shape, scratch, pinned=False, cost=None):
    whole = pl.BlockSpec(memory_space=pltpu.VMEM)
    anywhere = pl.BlockSpec(memory_space=pl.ANY)
    specs = [anywhere if in_hbm else whole for _, in_hbm in operands]
    arrays = [
        pltpu.with_memory_space_constraint(array, pltpu.HBM) if in_hbm else array
        for array, in_hbm in operands
    ]

    def keep(shape):
        return pltpu.VMEM(shape.shape, shape.dtype) if pinned else shape

    return pl.pallas_call(
        kernel,
        out_shape=jax.tree.map(keep, out_shape),
        in_specs=specs,
        out_specs=jax.tree.map(lambda _: whole, out_shape),
        scratch_shapes=scratch,
        compiler_params=pltpu.CompilerParams(vmem_limit_bytes=VMEM_LIMIT),
        cost_estimate=cost,
        name=name,
    )(*arrays)


def here(*arrays):
    return [(array, False) for array in arrays]


def in_hbm(*arrays):
    return [(array, True) for array in arrays]


def per_device_paired(ensemble, norm_gain, project_weight, output_weight, conv_kernel, cotangent):
    mem, rows, cols, channels = ensemble.shape
    if rows < 3 or cols % 16 or (4 * mem * (rows - 2)) % 16:
        return per_device_general(
            ensemble, norm_gain, project_weight, output_weight, conv_kernel, cotangent
        )
    groups = 2 * mem
    slots = 2 * groups
    cells = rows * cols
    lon_count = lax.axis_size("lon")
    lat_count = lax.axis_size("lat")
    bf16 = functools.partial(jax.ShapeDtypeStruct, dtype=BF16)
    f32 = functools.partial(jax.ShapeDtypeStruct, dtype=F32)
    swap = [(0, 1), (1, 0)]
    core_pairs = [(i, i ^ 1) for i in range(lon_count)]
    chip_pairs = [(i, (i - 1 if i % 2 == 0 else i + 1) % lon_count) for i in range(lon_count)]

    def lat_swap(offset):
        pairs = []
        for lat in range(lat_count):
            for lon in range(lon_count):
                to = (lat + 1 if lat % 2 == offset else lat - 1, lon)
                if not 0 <= to[0] < lat_count:
                    to = (lat, lon ^ 1)
                pairs.append((lat * lon_count + lon, to[0] * lon_count + to[1]))
        return pairs

    ends = 4 * mem * (rows - 2)
    inner_shape = (2, mem, rows - 2, cols, channels)
    both, ring, inner = local_call(
        stack_kernel,
        "stack",
        in_hbm(ensemble, cotangent),
        (
            bf16((2,) + ensemble.shape),
            bf16((4 * mem * cols + ends, channels)),
            bf16(inner_shape),
        ),
        [pltpu.VMEM((ends, channels), F32), pltpu.SemaphoreType.DMA((2,))],
        pinned=True,
    )
    ring = lax.ppermute(ring, "member", swap)
    inner = lax.ppermute(inner, "member", swap)

    weights = (
        norm_gain.reshape(1, channels),
        project_weight,
        output_weight,
        conv_kernel.reshape(9 * channels, channels),
    )
    weights = local_call(
        load_kernel,
        "load_weights",
        in_hbm(*weights),
        tuple(jax.ShapeDtypeStruct(w.shape, w.dtype) for w in weights),
        [pltpu.SemaphoreType.DMA((4,))],
        pinned=True,
    )

    strip = (slots * rows, channels)
    chip_send, core_send = local_call(
        pack_strips_kernel,
        "pack_strips",
        here(both, ring, weights[0]),
        (bf16(strip), bf16(strip)),
        [pltpu.VMEM(strip, F32)] * 2,
    )
    chip = lax.ppermute(chip_send, "lon", chip_pairs)
    core = lax.ppermute(core_send, "lon", core_pairs)

    held = local_call(
        own_kernel,
        "own_cells",
        here(both, ring, inner, *weights),
        (
            bf16((3 * channels, channels)),
            bf16((channels, channels)),
            bf16((9 * channels, channels)),
            bf16((groups, cells, 3 * channels)),
            bf16((2, groups, cells, channels)),
            f32((groups * groups, cells, channels)),
            f32((2, mem, cells, channels)),
            f32((2, mem, cells, channels)),
            bf16((mem, cells, channels)),
        ),
        [],
        pinned=True,
    )
    *held, updated = held

    halo = bf16((slots * (cols + 2), channels))
    first_send, second_send = local_call(
        pack_rows_kernel,
        "pack_rows",
        here(both, ring, chip, core, updated),
        (halo, halo),
        [pltpu.VMEM((2, 2 * slots, channels), F32)],
    )
    first = lax.ppermute(first_send, ("lat", "lon"), lat_swap(0))
    second = lax.ppermute(second_send, ("lat", "lon"), lat_swap(1))

    parts = local_call(
        centre_kernel,
        "centre",
        here(both, ring, inner, chip, core, *weights, *held, updated),
        (
            bf16((mem, rows - 2, cols, channels)),
            bf16((mem, rows - 2, cols, channels)),
            f32((mem, 2 * cols, channels)),
            f32((groups, 2 * cols, channels)),
        ),
        [
            pltpu.VMEM((mem, cells, 3 * channels), BF16),
            pltpu.VMEM((groups, cells, 3 * channels), BF16),
            pltpu.VMEM((groups, 16, channels), F32),
        ],
        pinned=True,
    )
    return local_call(
        functools.partial(main_kernel, lat_count=lat_count),
        "main",
        here(both, first, second, *weights, *held, *parts),
        (bf16(ensemble.shape), bf16(ensemble.shape)),
        [
            pltpu.VMEM((mem, 2 * cols, 3 * channels), BF16),
            pltpu.VMEM((groups, 2 * cols, 3 * channels), BF16),
            pltpu.VMEM((groups, 16, channels), F32),
        ],
    )


def solution(mesh):
    paired = mesh.shape["member"] == 2 and mesh.shape["lon"] % 2 == 0
    per_device = per_device_paired if paired else per_device_general
    in_specs = (
        P("member", "lat", "lon", None),
        P(),
        P(),
        P(),
        P(),
        P("member", "lat", "lon", None),
    )
    out_specs = (P("member", "lat", "lon", None), P("member", "lat", "lon", None))
    return jax.shard_map(
        per_device, mesh=mesh, in_specs=in_specs, out_specs=out_specs, check_vma=False
    )
```

```python
import functools
import math

import jax
import jax.numpy as jnp
from jax import lax
from jax.experimental import pallas as pl
from jax.experimental.pallas import tpu as pltpu
from jax.sharding import PartitionSpec as P

HEAD_COUNT = 8


FLOOR = 0.5
EPSILON = 1e-06


def padded_2(block, sides, width, periodic):
    for axis, dim in sides:
        count = lax.axis_size(axis)
        forward = [(i, i + 1) for i in range(count - 1)]
        if periodic:
            forward.append((count - 1, 0))
        backward = [(target, source) for source, target in forward]
        low = lax.ppermute(
            lax.slice_in_dim(block, block.shape[dim] - width, None, axis=dim), axis, forward
        )
        high = lax.ppermute(lax.slice_in_dim(block, 0, width, axis=dim), axis, backward)
        block = jnp.concatenate([low, block, high], axis=dim)
    return block


def row_norm(values, gain_vec):
    mean_sq = jnp.mean(values * values, axis=-1, keepdims=True)
    return values * lax.rsqrt(mean_sq + EPSILON) * gain_vec


def head_norm(values, head_count):
    shaped = values.reshape(values.shape[:-1] + (head_count, values.shape[-1] // head_count))
    mean_sq = jnp.mean(shaped * shaped, axis=-1, keepdims=True)
    return (shaped * lax.rsqrt(jnp.maximum(mean_sq, FLOOR))).reshape(values.shape)


def split_heads(values, head_count):
    return values.reshape(values.shape[:-1] + (head_count, values.shape[-1] // head_count))


def head_pullback(raw_rows, grad_rows):
    _, pullback = jax.vjp(lambda t: head_norm(t, HEAD_COUNT), raw_rows.astype(jnp.float32))
    return pullback(grad_rows)[0]


def pad_field(field_in):
    widened = padded_2(field_in, (("lon", 2),), 1, True)
    return padded_2(widened, (("lat", 1),), 1, False)


def conv_taps(padded, kernel, lat_n, lon_n, adjoint):
    running = None
    for row_off in range(3):
        for col_off in range(3):
            if adjoint:
                window = padded[
                    :, 2 - row_off : 2 - row_off + lat_n, 2 - col_off : 2 - col_off + lon_n
                ]
                summand = jnp.einsum(
                    "mabc,dc->mabd",
                    window,
                    kernel[row_off, col_off],
                    preferred_element_type=jnp.float32,
                )
            else:
                window = padded[:, row_off : row_off + lat_n, col_off : col_off + lon_n]
                summand = jnp.einsum(
                    "mabc,cd->mabd",
                    window,
                    kernel[row_off, col_off],
                    preferred_element_type=jnp.float32,
                )
            running = summand if running is None else running + summand
    return running


def per_device_general(ensemble, norm_gain, project_weight, output_weight, conv_kernel, cotangent):
    mem_dev, lat_dev, lon_dev, channels = ensemble.shape
    cell_count = lat_dev * lon_dev
    score_scale = 1.0 / math.sqrt(channels // HEAD_COUNT)
    inputs = ensemble.reshape(mem_dev, cell_count, channels).astype(jnp.float32)
    normed = row_norm(inputs, norm_gain).astype(jnp.bfloat16)
    spread = lax.all_to_all(normed, "member", split_axis=1, concat_axis=0, tiled=True)
    projected = jnp.dot(spread, project_weight, preferred_element_type=jnp.float32).astype(
        jnp.bfloat16
    )
    query_raw = projected[..., :channels]
    key_raw = projected[..., channels : 2 * channels]
    value_rows = projected[..., 2 * channels :]
    key_rows = head_norm(key_raw.astype(jnp.float32), HEAD_COUNT).astype(jnp.bfloat16)
    queries = head_norm(query_raw.astype(jnp.float32), HEAD_COUNT).astype(jnp.bfloat16)
    query_heads = split_heads(queries, HEAD_COUNT)
    key_heads = split_heads(key_rows, HEAD_COUNT)
    value_heads = split_heads(value_rows, HEAD_COUNT)
    scores = (
        jnp.einsum("mphd,nphd->mnhp", query_heads, key_heads, preferred_element_type=jnp.float32)
        * score_scale
    )
    expd = jnp.exp(scores)
    soft = expd / jnp.sum(expd, axis=1, keepdims=True)
    rounded = soft.astype(jnp.bfloat16)
    mixed_out = jnp.einsum(
        "mnhp,nphd->mphd", rounded, value_heads, preferred_element_type=jnp.float32
    )
    mixed_out = mixed_out.reshape(query_raw.shape).astype(jnp.bfloat16)
    mixed_out = lax.all_to_all(mixed_out, "member", split_axis=0, concat_axis=1, tiled=True)
    updated = (
        inputs + jnp.dot(mixed_out, output_weight, preferred_element_type=jnp.float32)
    ).astype(jnp.bfloat16)
    field_up = updated.reshape(mem_dev, lat_dev, lon_dev, channels)
    result = field_up.astype(jnp.float32) + conv_taps(
        pad_field(field_up), conv_kernel, lat_dev, lon_dev, False
    )
    result = result.astype(jnp.bfloat16)
    grad_field = cotangent.astype(jnp.float32) + conv_taps(
        pad_field(cotangent), conv_kernel, lat_dev, lon_dev, True
    )
    grad_rows = grad_field.reshape(mem_dev, cell_count, channels)
    grad_mixed = jnp.einsum(
        "mpc,dc->mpd",
        grad_rows.astype(jnp.bfloat16),
        output_weight,
        preferred_element_type=jnp.float32,
    )
    grad_mixed = grad_mixed.astype(jnp.bfloat16)
    grad_mixed = lax.all_to_all(grad_mixed, "member", split_axis=1, concat_axis=0, tiled=True)
    grad_heads = split_heads(grad_mixed, HEAD_COUNT)
    dprob = jnp.einsum(
        "mphd,nphd->mnhp", grad_heads, value_heads, preferred_element_type=jnp.float32
    )
    dscore = (soft * (dprob - jnp.sum(soft * dprob, axis=1, keepdims=True))).astype(jnp.bfloat16)
    query_grad = (
        jnp.einsum("mnhp,nphd->mphd", dscore, key_heads, preferred_element_type=jnp.float32)
        * score_scale
    )
    query_grad = query_grad.reshape(query_raw.shape)
    key_grad = (
        jnp.einsum("mnhp,mphd->nphd", dscore, query_heads, preferred_element_type=jnp.float32)
        * score_scale
    )
    key_grad = key_grad.reshape(key_raw.shape)
    value_grad = jnp.einsum(
        "mnhp,mphd->nphd", rounded, grad_heads, preferred_element_type=jnp.float32
    )
    value_grad = value_grad.reshape(key_raw.shape)
    grad_query_raw = head_pullback(query_raw, query_grad)
    grad_key_raw = head_pullback(key_raw, key_grad)
    grad_proj = jnp.concatenate([grad_query_raw, grad_key_raw, value_grad], axis=-1).astype(
        jnp.bfloat16
    )
    grad_proj = lax.all_to_all(grad_proj, "member", split_axis=0, concat_axis=1, tiled=True)
    grad_normed = jnp.einsum(
        "mpe,ce->mpc", grad_proj, project_weight, preferred_element_type=jnp.float32
    )
    _, pull_norm = jax.vjp(lambda t: row_norm(t, norm_gain), inputs)
    grad_inputs = pull_norm(grad_normed)[0]
    grad_ensemble = (
        (grad_rows + grad_inputs).astype(jnp.bfloat16).reshape(mem_dev, lat_dev, lon_dev, channels)
    )
    return (result, grad_ensemble)


F32 = jnp.float32
BF16 = jnp.bfloat16
VMEM_LIMIT = 24 * 1024 * 1024


def is_even(axis):
    return lax.rem(lax.axis_index(axis), 2) == 0


def load_kernel(both_ref, *refs):
    count = len(refs) // 2 - 1
    inner_ref, sems = refs[-2:]
    copies = [pltpu.make_async_copy(refs[i], refs[count + i], sems.at[i]) for i in range(count)]
    for copy in copies:
        copy.start()
    rows = both_ref.shape[2]
    inner_ref[...] = both_ref[:, :, 1 : rows - 1]
    for copy in copies:
        copy.wait()


def stack_kernel(ens_ref, cot_ref, both_ref, ring_ref, end_scr, sems):
    _, mem, rows, cols, _ = both_ref.shape
    copies = [
        pltpu.make_async_copy(ref, both_ref.at[i], sems.at[i])
        for i, ref in enumerate((ens_ref, cot_ref))
    ]
    for copy in copies:
        copy.start()
    for copy in copies:
        copy.wait()
    index = 0
    for array in range(2):
        for member in range(mem):
            slot = array * mem + member
            for side, row in enumerate((0, rows - 1)):
                at = (2 * slot + side) * cols
                ring_ref[at : at + cols, :] = both_ref[array, member, row]
            for row in range(1, rows - 1):
                slab = both_ref[array, member, row].astype(F32)
                end_scr[index : index + 1, :] = slab[0:1]
                end_scr[index + 1 : index + 2, :] = slab[cols - 1 : cols]
                index += 2
    ring_ref[4 * mem * cols :, :] = end_scr[...].astype(BF16)


def ring_row(ring_ref, mem, cols, array, member, side):
    at = (2 * (array * mem + member) + side) * cols
    return ring_ref[at : at + cols, :]


def pack_strips_kernel(both_ref, ring_ref, after_ref, chip_ref, core_ref, low_scr, high_scr):
    _, mem, rows, cols, _ = both_ref.shape
    ends = ring_ref[4 * mem * cols :, :].astype(F32)
    index = 0
    for array in range(2):
        for member in range(2 * mem):
            for row in range(rows):
                if member < mem:
                    slab = both_ref[array, member, row].astype(F32)
                elif row in (0, rows - 1):
                    side = 0 if row == 0 else 1
                    slab = ring_row(ring_ref, mem, cols, array, member - mem, side).astype(F32)
                else:
                    at = 2 * ((array * mem + member - mem) * (rows - 2) + row - 1)
                    slab = ends[at : at + 2]
                low_scr[index : index + 1, :] = slab[0:1]
                high_scr[index : index + 1, :] = slab[slab.shape[0] - 1 :]
                index += 1
    even = is_even("lon")
    low, high = low_scr[...], high_scr[...]
    core_ref[...] = jnp.where(even, high, low).astype(BF16)
    chip_ref[...] = jnp.where(even, low, high).astype(BF16)


def rim_columns(chip_ref, core_ref):
    even = is_even("lon")
    chip, core = chip_ref[...].astype(F32), core_ref[...].astype(F32)
    return jnp.where(even, chip, core), jnp.where(even, core, chip)


def pack_rows_kernel(
    both_ref, ring_ref, chip_ref, core_ref, after_ref, first_ref, second_ref, edge_scr
):
    _, mem, rows, cols, _ = both_ref.shape
    slots = 4 * mem
    even = is_even("lat")
    west, east = rim_columns(chip_ref, core_ref)
    for slot in range(slots):
        array, member = divmod(slot, 2 * mem)
        if member < mem:
            pair = [both_ref[array, member, row] for row in (0, rows - 1)]
        else:
            pair = [ring_row(ring_ref, mem, cols, array, member - mem, side) for side in (0, 1)]
        start, stop = (slab.astype(F32) for slab in pair)
        at = slice(slot * cols, (slot + 1) * cols)
        first_ref[at, :] = jnp.where(even, stop, start).astype(BF16)
        second_ref[at, :] = jnp.where(even, start, stop).astype(BF16)
        top, low = slot * rows, (slot + 1) * rows - 1
        for side, column in enumerate((west, east)):
            place = side * slots + slot
            start, stop = column[top : top + 1], column[low : low + 1]
            edge_scr[0, place : place + 1, :] = jnp.where(even, stop, start)
            edge_scr[1, place : place + 1, :] = jnp.where(even, start, stop)
    first_ref[slots * cols :, :] = edge_scr[0].astype(BF16)
    second_ref[slots * cols :, :] = edge_scr[1].astype(BF16)


def dot_nn(a, b):
    return lax.dot_general(a, b, (((1,), (0,)), ((), ())), preferred_element_type=F32)


def same_head_matrix(channels):
    width = channels // HEAD_COUNT
    lane_row = lax.broadcasted_iota(jnp.int32, (channels, channels), 0) // width
    lane_col = lax.broadcasted_iota(jnp.int32, (channels, channels), 1) // width
    return jnp.where(lane_row == lane_col, 1.0, 0.0).astype(BF16)


def head_sums(values, same_head):
    high = values.astype(BF16)
    low = (values - high.astype(F32)).astype(BF16)
    return dot_nn(high, same_head) + dot_nn(low, same_head)


def rounded_sums(values, same_head):
    return dot_nn(values.astype(BF16), same_head)


def head_units(raw, same_head, sums=head_sums):
    raw = raw.astype(F32)
    mean_sq = sums(raw * raw, same_head) * (HEAD_COUNT / raw.shape[-1])
    inverse = lax.rsqrt(jnp.maximum(mean_sq, FLOOR))
    return raw, mean_sq, inverse, (raw * inverse).astype(BF16)


def row_rsqrt(values):
    return lax.rsqrt(jnp.mean(values * values, axis=-1, keepdims=True) + EPSILON)


def split_rows(array, count):
    size = array.shape[0] // count
    return [array[i * size : (i + 1) * size] for i in range(count)]


def softmax_members(queries, keys, same_head, scale):
    products = [query * key for query in queries for key in keys]
    scores = dot_nn(jnp.concatenate(products, axis=0), same_head) * scale
    exps = split_rows(jnp.exp(scores), len(products))
    soft = []
    for m in range(len(queries)):
        mine = exps[m * len(keys) : (m + 1) * len(keys)]
        total = mine[0]
        for e in mine[1:]:
            total = total + e
        inverse = 1.0 / total
        soft.append([e * inverse for e in mine])
    return soft


def mix_values(probs, values):
    mixed = None
    for prob, value in zip(probs, values):
        term = prob.astype(BF16).astype(F32) * value.astype(F32)
        mixed = term if mixed is None else mixed + term
    return mixed.astype(BF16)


def forward_cells(x, mem, groups, gain, project_ref, output_ref, same_head):
    channels = x.shape[-1]
    own_rows = x.shape[0] // groups * mem
    scale = 1.0 / math.sqrt(channels // HEAD_COUNT)
    normed = (x * row_rsqrt(x) * gain).astype(BF16)
    query_raw = dot_nn(normed[:own_rows], project_ref[:, :channels]).astype(BF16)
    key_raw = dot_nn(normed, project_ref[:, channels : 2 * channels]).astype(BF16)
    values = dot_nn(normed, project_ref[:, 2 * channels :]).astype(BF16)
    raw = jnp.concatenate([query_raw, key_raw], axis=0)
    units = head_units(raw, same_head, rounded_sums)[3]
    queries = split_rows(units[:own_rows], mem)
    keys = split_rows(units[own_rows:], groups)
    values = split_rows(values, groups)
    soft = softmax_members(queries, keys, same_head, scale)
    mixed = jnp.concatenate([mix_values(soft[m], values) for m in range(mem)], axis=0)
    return (x[:own_rows] + dot_nn(mixed, output_ref[...])).astype(BF16)


def shift_row(scr, member, place, slab, west, east):
    cols, channels = slab.shape
    column = lax.broadcasted_iota(jnp.int32, (cols, channels), 0)
    back = jnp.where(column == 0, west, pltpu.roll(slab, 1, 0))
    ahead = jnp.where(column == cols - 1, east, pltpu.roll(slab, cols - 1, 0))
    rows_at = slice(place * cols, (place + 1) * cols)
    scr[member, rows_at, :channels] = back.astype(BF16)
    scr[member, rows_at, channels : 2 * channels] = slab.astype(BF16)
    scr[member, rows_at, 2 * channels :] = ahead.astype(BF16)


def tap_rows(taps_ref, r):
    size = taps_ref.shape[0] // 3
    return taps_ref[r * size : (r + 1) * size, :]


def own_kernel(
    both_ref,
    ring_ref,
    inner_ref,
    gain_ref,
    project_ref,
    output_ref,
    conv_ref,
    project_t_ref,
    output_t_ref,
    conv_t_ref,
    proj_ref,
    unit_ref,
    soft_ref,
    inverse_ref,
    pull_ref,
    updated_ref,
):
    _, mem, rows, cols, channels = both_ref.shape
    groups = 2 * mem
    cells = rows * cols
    width = channels // HEAD_COUNT
    scale = 1.0 / math.sqrt(width)
    same_head = same_head_matrix(channels)
    slabs = [both_ref[0].reshape(mem * cells, channels)]
    for member in range(mem):
        slabs.append(ring_row(ring_ref, mem, cols, 0, member, 0))
        slabs.append(inner_ref[0, member].reshape((rows - 2) * cols, channels))
        slabs.append(ring_row(ring_ref, mem, cols, 0, member, 1))
    x = jnp.concatenate(slabs, axis=0).astype(F32)
    normed = (x * row_rsqrt(x) * gain_ref[...]).astype(BF16)
    proj = dot_nn(normed, project_ref[...]).astype(BF16)
    proj_ref[...] = proj.reshape(groups, cells, 3 * channels)
    both_raw = jnp.concatenate([proj[:, :channels], proj[:, channels : 2 * channels]], axis=0)
    raw, mean_sq, inverse, units = head_units(both_raw, same_head)
    unit_ref[...] = units.reshape(2, groups, cells, channels)
    active = jnp.where(mean_sq > FLOOR, 1.0, jnp.where(mean_sq == FLOOR, 0.5, 0.0))
    pull = active * raw * (inverse * inverse * inverse) / width
    for kind in range(2):
        at = kind * groups * cells
        mine = slice(at, at + mem * cells)
        inverse_ref[kind] = inverse[mine].reshape(mem, cells, channels)
        pull_ref[kind] = pull[mine].reshape(mem, cells, channels)
    units = split_rows(units, 2 * groups)
    soft = softmax_members(units[:groups], units[groups:], same_head, scale)
    for m in range(groups):
        for n in range(groups):
            soft_ref[m * groups + n] = soft[m][n]
    values = split_rows(proj[:, 2 * channels :], groups)
    mixed = jnp.concatenate([mix_values(soft[m], values) for m in range(mem)], axis=0)
    updated = x[: mem * cells] + dot_nn(mixed, output_ref[...])
    updated_ref[...] = updated.astype(BF16).reshape(mem, cells, channels)
    output_t_ref[...] = output_ref[...].T
    for kind in range(3):
        lanes = slice(kind * channels, (kind + 1) * channels)
        project_t_ref[lanes, :] = project_ref[:, lanes].T
    for r in range(3):
        for c in range(3):
            tap = (3 * r + c) * channels
            turned = (3 * r + 2 - c) * channels
            conv_t_ref[turned : turned + channels, :] = conv_ref[tap : tap + channels, :].T


def backward_cells(
    pick, grad_field, x, gain, weights_t, proj_ref, unit_ref, soft_ref, inverse_ref, pull_ref
):
    project_t_ref, output_t_ref = weights_t
    groups = proj_ref.shape[0]
    mem = inverse_ref.shape[1]
    channels = x.shape[-1]
    scale = 1.0 / math.sqrt(channels // HEAD_COUNT)
    same_head = same_head_matrix(channels)
    grad_mixed = dot_nn(grad_field.astype(BF16), output_t_ref[...]).astype(BF16)
    grads = split_rows(grad_mixed, groups)
    values = [pick(proj_ref[n, :, 2 * channels :]) for n in range(groups)]
    products = [grads[m] * values[n] for m in range(groups) for n in range(groups)]
    dprobs = split_rows(dot_nn(jnp.concatenate(products, axis=0), same_head), len(products))
    units = [[pick(unit_ref[k, n]).astype(F32) for n in range(groups)] for k in range(2)]
    query_grad = [None] * mem
    key_grad = [None] * mem
    value_grad = [None] * mem
    for m in range(groups):
        soft = [pick(soft_ref[m * groups + n]) for n in range(groups)]
        dprob = dprobs[m * groups : (m + 1) * groups]
        mean = soft[0] * dprob[0]
        for n in range(1, groups):
            mean = mean + soft[n] * dprob[n]
        for n in range(groups):
            if m >= mem and n >= mem:
                continue
            dscore = soft[n] * (dprob[n] - mean)
            if m < mem:
                term = dscore * units[1][n]
                query_grad[m] = term if query_grad[m] is None else query_grad[m] + term
            if n < mem:
                term = dscore * units[0][m]
                key_grad[n] = term if key_grad[n] is None else key_grad[n] + term
                term = soft[n] * grads[m].astype(F32)
                value_grad[n] = term if value_grad[n] is None else value_grad[n] + term

    unit_grads = [jnp.concatenate(g, axis=0) * scale for g in (query_grad, key_grad)]

    def members(take):
        return jnp.concatenate([pick(take(m)) for m in range(mem)], axis=0)

    raws = []
    for kind in range(2):
        lanes = slice(kind * channels, (kind + 1) * channels)
        raws.append(members(lambda m: proj_ref[m, :, lanes]).astype(F32))
    inner = rounded_sums(
        jnp.concatenate([g * raw for g, raw in zip(unit_grads, raws)], axis=0), same_head
    )
    inner = split_rows(inner, 2)
    pulled = []
    for kind in range(2):
        inverse = members(lambda m: inverse_ref[kind, m])
        pull = members(lambda m: pull_ref[kind, m])
        pulled.append((inverse * unit_grads[kind] - pull * inner[kind]).astype(BF16))
    pulled.append(jnp.concatenate(value_grad, axis=0).astype(BF16))
    grad_normed = dot_nn(jnp.concatenate(pulled, axis=1), project_t_ref[...]) * gain
    inverse = row_rsqrt(x)
    inner = jnp.mean(x * grad_normed, axis=-1, keepdims=True)
    total = grad_field[: x.shape[0]] + inverse * grad_normed
    return (total - x * (inverse * inverse * inverse * inner)).astype(BF16)


def centre_kernel(
    both_ref,
    ring_ref,
    inner_ref,
    chip_ref,
    core_ref,
    gain_ref,
    project_ref,
    output_ref,
    conv_ref,
    project_t_ref,
    output_t_ref,
    conv_t_ref,
    proj_ref,
    unit_ref,
    soft_ref,
    inverse_ref,
    pull_ref,
    updated_ref,
    result_ref,
    grad_ref,
    result_part_ref,
    grad_part_ref,
    shift_scr,
    cot_shift_scr,
    strip_scr,
):
    _, mem, rows, cols, channels = both_ref.shape
    groups = 2 * mem
    cells = rows * cols
    gain = gain_ref[...]
    same_head = same_head_matrix(channels)
    west, east = rim_columns(chip_ref, core_ref)

    def convolve(scr, count, start, taps_ref, turned):
        sums = [
            [start[(m * rows + a) * cols : (m * rows + a + 1) * cols] for a in range(rows)]
            for m in range(count)
        ]
        for r in range(3):
            step = 1 - r if turned else r - 1
            outs = [a for a in range(rows) if 0 <= a + step < rows]
            begin, end = outs[0] + step, outs[-1] + step + 1
            window = jnp.concatenate(
                [scr[m, begin * cols : end * cols, :] for m in range(count)], axis=0
            )
            terms = split_rows(dot_nn(window, tap_rows(taps_ref, r)), count * len(outs))
            for m in range(count):
                for i, a in enumerate(outs):
                    sums[m][a] = sums[m][a] + terms[m * len(outs) + i]
        return sums

    cots = []
    for member in range(groups):
        for row in range(rows):
            if member < mem:
                slab = both_ref[1, member, row]
            elif row in (0, rows - 1):
                slab = ring_row(ring_ref, mem, cols, 1, member - mem, 0 if row == 0 else 1)
            else:
                slab = inner_ref[1, member - mem, row - 1]
            slab = slab.astype(F32)
            cots.append(slab)
            at = (groups + member) * rows + row
            shift_row(cot_shift_scr, member, row, slab, west[at : at + 1], east[at : at + 1])
    sums = convolve(cot_shift_scr, groups, jnp.concatenate(cots, axis=0), conv_t_ref, True)
    for member in range(groups):
        grad_part_ref[member, :cols, :] = sums[member][0]
        grad_part_ref[member, cols:, :] = sums[member][rows - 1]
    grad_field = jnp.concatenate([slab for s in sums for slab in s[1 : rows - 1]], axis=0)

    for member in range(groups):
        at = member * rows
        strip_scr[member] = jnp.zeros((16, channels), F32)
        strip_scr[member, :rows, :] = west[at : at + rows]
        strip_scr[member, 8 : 8 + rows, :] = east[at : at + rows]
    x = strip_scr[...].reshape(groups * 16, channels)
    fresh = forward_cells(x, mem, groups, gain, project_ref, output_ref, same_head)
    fresh = split_rows(fresh.astype(F32), mem)

    pick = lambda array: array[cols : cells - cols]
    x = both_ref[0, :, 1 : rows - 1].reshape(mem * (cells - 2 * cols), channels).astype(F32)
    total = backward_cells(
        pick,
        grad_field,
        x,
        gain,
        (project_t_ref, output_t_ref),
        proj_ref,
        unit_ref,
        soft_ref,
        inverse_ref,
        pull_ref,
    )
    grad_ref[...] = total.reshape(mem, rows - 2, cols, channels)

    for member in range(mem):
        for row in range(rows):
            slab = updated_ref[member, row * cols : (row + 1) * cols, :].astype(F32)
            ends = fresh[member][row : row + 1], fresh[member][8 + row : 9 + row]
            shift_row(shift_scr, member, row, slab, *ends)
    start = updated_ref[...].reshape(mem * cells, channels).astype(F32)
    sums = convolve(shift_scr, mem, start, conv_ref, False)
    for member in range(mem):
        result_part_ref[member, :cols, :] = sums[member][0]
        result_part_ref[member, cols:, :] = sums[member][rows - 1]
        for row in range(1, rows - 1):
            result_ref[member, row - 1] = sums[member][row].astype(BF16)


def main_kernel(
    both_ref,
    first_ref,
    second_ref,
    gain_ref,
    project_ref,
    output_ref,
    conv_ref,
    project_t_ref,
    output_t_ref,
    conv_t_ref,
    proj_ref,
    unit_ref,
    soft_ref,
    inverse_ref,
    pull_ref,
    inner_result_ref,
    inner_grad_ref,
    result_part_ref,
    grad_part_ref,
    result_ref,
    grad_ref,
    shift_scr,
    cot_shift_scr,
    corner_scr,
    *,
    lat_count,
):
    _, mem, rows, cols, channels = both_ref.shape
    groups = 2 * mem
    slots = 2 * groups
    cells = rows * cols
    gain = gain_ref[...]
    same_head = same_head_matrix(channels)
    lat_even = is_even("lat")
    lat = lax.axis_index("lat")

    def halos(at):
        first, second = first_ref[at, :].astype(F32), second_ref[at, :].astype(F32)
        north = jnp.where(lat == 0, 0.0, jnp.where(lat_even, second, first))
        south = jnp.where(lat == lat_count - 1, 0.0, jnp.where(lat_even, first, second))
        return north, south

    halo = [halos(slice(slot * cols, (slot + 1) * cols)) for slot in range(slots)]
    corners = halos(slice(slots * cols, slots * cols + 2 * slots))

    def corner(side, slot, end):
        at = end * slots + slot
        return corners[side][at : at + 1]

    def halo_part(scr, count, taps_ref, turned):
        north, south = (2, 0) if turned else (0, 2)
        parts = []
        for side, r in ((0, north), (1, south)):
            window = jnp.concatenate(
                [scr[m, side * cols : (side + 1) * cols, :] for m in range(count)], axis=0
            )
            parts.append(split_rows(dot_nn(window, tap_rows(taps_ref, r)), count))
        return jnp.concatenate([parts[side][m] for m in range(count) for side in (0, 1)], axis=0)

    for member in range(groups):
        slot = groups + member
        for side in (0, 1):
            ends = corner(side, slot, 0), corner(side, slot, 1)
            shift_row(cot_shift_scr, member, side, halo[slot][side], *ends)
    grad_field = grad_part_ref[...].reshape(groups * 2 * cols, channels)
    grad_field = grad_field + halo_part(cot_shift_scr, groups, conv_t_ref, True)

    blocks = []
    for member in range(groups):
        corner_scr[member] = jnp.zeros((16, channels), F32)
        for side in (0, 1):
            for end in (0, 1):
                at = 2 * side + end
                corner_scr[member, at : at + 1, :] = corner(side, member, end)
        blocks += [halo[member][0], halo[member][1], corner_scr[member]]
    x = jnp.concatenate(blocks, axis=0)
    fresh = forward_cells(x, mem, groups, gain, project_ref, output_ref, same_head)
    fresh = split_rows(fresh.astype(F32), mem)

    pick = lambda array: jnp.concatenate([array[:cols], array[cells - cols :]], axis=0)
    x = [both_ref[0, m, row] for m in range(mem) for row in (0, rows - 1)]
    total = backward_cells(
        pick,
        grad_field,
        jnp.concatenate(x, axis=0).astype(F32),
        gain,
        (project_t_ref, output_t_ref),
        proj_ref,
        unit_ref,
        soft_ref,
        inverse_ref,
        pull_ref,
    )

    for member in range(mem):
        for side in (0, 1):
            slab = fresh[member][side * cols : (side + 1) * cols]
            at = 2 * cols + 2 * side
            ends = fresh[member][at : at + 1], fresh[member][at + 1 : at + 2]
            shift_row(shift_scr, member, side, slab, *ends)
    outer = result_part_ref[...].reshape(mem * 2 * cols, channels)
    outer = (outer + halo_part(shift_scr, mem, conv_ref, False)).astype(BF16)
    outputs = (
        (result_ref, inner_result_ref, split_rows(outer, 2 * mem)),
        (grad_ref, inner_grad_ref, split_rows(total, 2 * mem)),
    )
    for out_ref, inner_ref, edge in outputs:
        for member in range(mem):
            out_ref[member, 0] = edge[2 * member]
            out_ref[member, rows - 1] = edge[2 * member + 1]
            for row in range(1, rows - 1):
                out_ref[member, row] = inner_ref[member, row - 1]


def local_call(kernel, name, operands, out_shape, scratch, pinned=False, cost=None):
    whole = pl.BlockSpec(memory_space=pltpu.VMEM)
    anywhere = pl.BlockSpec(memory_space=pl.ANY)
    specs = [anywhere if in_hbm else whole for _, in_hbm in operands]
    arrays = [
        pltpu.with_memory_space_constraint(array, pltpu.HBM) if in_hbm else array
        for array, in_hbm in operands
    ]

    def keep(shape):
        return pltpu.VMEM(shape.shape, shape.dtype) if pinned else shape

    return pl.pallas_call(
        kernel,
        out_shape=jax.tree.map(keep, out_shape),
        in_specs=specs,
        out_specs=jax.tree.map(lambda _: whole, out_shape),
        scratch_shapes=scratch,
        compiler_params=pltpu.CompilerParams(vmem_limit_bytes=VMEM_LIMIT),
        cost_estimate=cost,
        name=name,
    )(*arrays)


def here(*arrays):
    return [(array, False) for array in arrays]


def in_hbm(*arrays):
    return [(array, True) for array in arrays]


def per_device_paired(ensemble, norm_gain, project_weight, output_weight, conv_kernel, cotangent):
    mem, rows, cols, channels = ensemble.shape
    if rows < 3 or cols % 16 or (4 * mem * (rows - 2)) % 16:
        return per_device_general(
            ensemble, norm_gain, project_weight, output_weight, conv_kernel, cotangent
        )
    groups = 2 * mem
    slots = 2 * groups
    cells = rows * cols
    lon_count = lax.axis_size("lon")
    lat_count = lax.axis_size("lat")
    bf16 = functools.partial(jax.ShapeDtypeStruct, dtype=BF16)
    f32 = functools.partial(jax.ShapeDtypeStruct, dtype=F32)
    swap = [(0, 1), (1, 0)]
    core_pairs = [(i, i ^ 1) for i in range(lon_count)]
    chip_pairs = [(i, (i - 1 if i % 2 == 0 else i + 1) % lon_count) for i in range(lon_count)]

    def lat_swap(offset):
        pairs = []
        for lat in range(lat_count):
            for lon in range(lon_count):
                to = (lat + 1 if lat % 2 == offset else lat - 1, lon)
                if not 0 <= to[0] < lat_count:
                    to = (lat, lon ^ 1)
                pairs.append((lat * lon_count + lon, to[0] * lon_count + to[1]))
        return pairs

    ends = 4 * mem * (rows - 2)
    inner_shape = (2, mem, rows - 2, cols, channels)
    both, ring = local_call(
        stack_kernel,
        "stack",
        in_hbm(ensemble, cotangent),
        (
            bf16((2,) + ensemble.shape),
            bf16((4 * mem * cols + ends, channels)),
        ),
        [pltpu.VMEM((ends, channels), F32), pltpu.SemaphoreType.DMA((2,))],
        pinned=True,
    )
    ring = lax.ppermute(ring, "member", swap)

    weights = (
        norm_gain.reshape(1, channels),
        project_weight,
        output_weight,
        conv_kernel.reshape(9 * channels, channels),
    )
    *weights, inner = local_call(
        load_kernel,
        "load_weights",
        here(both) + in_hbm(*weights),
        tuple(jax.ShapeDtypeStruct(w.shape, w.dtype) for w in weights) + (bf16(inner_shape),),
        [pltpu.SemaphoreType.DMA((4,))],
        pinned=True,
    )
    inner = lax.ppermute(inner, "member", swap)

    strip = (slots * rows, channels)
    chip_send, core_send = local_call(
        pack_strips_kernel,
        "pack_strips",
        here(both, ring, weights[0]),
        (bf16(strip), bf16(strip)),
        [pltpu.VMEM(strip, F32)] * 2,
    )
    chip = lax.ppermute(chip_send, "lon", chip_pairs)
    core = lax.ppermute(core_send, "lon", core_pairs)

    held = local_call(
        own_kernel,
        "own_cells",
        here(both, ring, inner, *weights),
        (
            bf16((3 * channels, channels)),
            bf16((channels, channels)),
            bf16((9 * channels, channels)),
            bf16((groups, cells, 3 * channels)),
            bf16((2, groups, cells, channels)),
            f32((groups * groups, cells, channels)),
            f32((2, mem, cells, channels)),
            f32((2, mem, cells, channels)),
            bf16((mem, cells, channels)),
        ),
        [],
        pinned=True,
    )
    *held, updated = held

    halo = bf16((slots * (cols + 2), channels))
    first_send, second_send = local_call(
        pack_rows_kernel,
        "pack_rows",
        here(both, ring, chip, core, updated),
        (halo, halo),
        [pltpu.VMEM((2, 2 * slots, channels), F32)],
    )
    first = lax.ppermute(first_send, ("lat", "lon"), lat_swap(0))
    second = lax.ppermute(second_send, ("lat", "lon"), lat_swap(1))

    parts = local_call(
        centre_kernel,
        "centre",
        here(both, ring, inner, chip, core, *weights, *held, updated),
        (
            bf16((mem, rows - 2, cols, channels)),
            bf16((mem, rows - 2, cols, channels)),
            f32((mem, 2 * cols, channels)),
            f32((groups, 2 * cols, channels)),
        ),
        [
            pltpu.VMEM((mem, cells, 3 * channels), BF16),
            pltpu.VMEM((groups, cells, 3 * channels), BF16),
            pltpu.VMEM((groups, 16, channels), F32),
        ],
        pinned=True,
    )
    return local_call(
        functools.partial(main_kernel, lat_count=lat_count),
        "main",
        here(both, first, second, *weights, *held, *parts),
        (bf16(ensemble.shape), bf16(ensemble.shape)),
        [
            pltpu.VMEM((mem, 2 * cols, 3 * channels), BF16),
            pltpu.VMEM((groups, 2 * cols, 3 * channels), BF16),
            pltpu.VMEM((groups, 16, channels), F32),
        ],
    )


def solution(mesh):
    paired = mesh.shape["member"] == 2 and mesh.shape["lon"] % 2 == 0
    per_device = per_device_paired if paired else per_device_general
    in_specs = (
        P("member", "lat", "lon", None),
        P(),
        P(),
        P(),
        P(),
        P("member", "lat", "lon", None),
    )
    out_specs = (P("member", "lat", "lon", None), P("member", "lat", "lon", None))
    return jax.shard_map(
        per_device, mesh=mesh, in_specs=in_specs, out_specs=out_specs, check_vma=False
    )
```

```python
import functools
import math

import jax
import jax.numpy as jnp
from jax import lax
from jax.experimental import pallas as pl
from jax.experimental.pallas import tpu as pltpu
from jax.sharding import PartitionSpec as P

HEAD_COUNT = 8


FLOOR = 0.5
EPSILON = 1e-06


def padded_2(block, sides, width, periodic):
    for axis, dim in sides:
        count = lax.axis_size(axis)
        forward = [(i, i + 1) for i in range(count - 1)]
        if periodic:
            forward.append((count - 1, 0))
        backward = [(target, source) for source, target in forward]
        low = lax.ppermute(
            lax.slice_in_dim(block, block.shape[dim] - width, None, axis=dim), axis, forward
        )
        high = lax.ppermute(lax.slice_in_dim(block, 0, width, axis=dim), axis, backward)
        block = jnp.concatenate([low, block, high], axis=dim)
    return block


def row_norm(values, gain_vec):
    mean_sq = jnp.mean(values * values, axis=-1, keepdims=True)
    return values * lax.rsqrt(mean_sq + EPSILON) * gain_vec


def head_norm(values, head_count):
    shaped = values.reshape(values.shape[:-1] + (head_count, values.shape[-1] // head_count))
    mean_sq = jnp.mean(shaped * shaped, axis=-1, keepdims=True)
    return (shaped * lax.rsqrt(jnp.maximum(mean_sq, FLOOR))).reshape(values.shape)


def split_heads(values, head_count):
    return values.reshape(values.shape[:-1] + (head_count, values.shape[-1] // head_count))


def head_pullback(raw_rows, grad_rows):
    _, pullback = jax.vjp(lambda t: head_norm(t, HEAD_COUNT), raw_rows.astype(jnp.float32))
    return pullback(grad_rows)[0]


def pad_field(field_in):
    widened = padded_2(field_in, (("lon", 2),), 1, True)
    return padded_2(widened, (("lat", 1),), 1, False)


def conv_taps(padded, kernel, lat_n, lon_n, adjoint):
    running = None
    for row_off in range(3):
        for col_off in range(3):
            if adjoint:
                window = padded[
                    :, 2 - row_off : 2 - row_off + lat_n, 2 - col_off : 2 - col_off + lon_n
                ]
                summand = jnp.einsum(
                    "mabc,dc->mabd",
                    window,
                    kernel[row_off, col_off],
                    preferred_element_type=jnp.float32,
                )
            else:
                window = padded[:, row_off : row_off + lat_n, col_off : col_off + lon_n]
                summand = jnp.einsum(
                    "mabc,cd->mabd",
                    window,
                    kernel[row_off, col_off],
                    preferred_element_type=jnp.float32,
                )
            running = summand if running is None else running + summand
    return running


def per_device_general(ensemble, norm_gain, project_weight, output_weight, conv_kernel, cotangent):
    mem_dev, lat_dev, lon_dev, channels = ensemble.shape
    cell_count = lat_dev * lon_dev
    score_scale = 1.0 / math.sqrt(channels // HEAD_COUNT)
    inputs = ensemble.reshape(mem_dev, cell_count, channels).astype(jnp.float32)
    normed = row_norm(inputs, norm_gain).astype(jnp.bfloat16)
    spread = lax.all_to_all(normed, "member", split_axis=1, concat_axis=0, tiled=True)
    projected = jnp.dot(spread, project_weight, preferred_element_type=jnp.float32).astype(
        jnp.bfloat16
    )
    query_raw = projected[..., :channels]
    key_raw = projected[..., channels : 2 * channels]
    value_rows = projected[..., 2 * channels :]
    key_rows = head_norm(key_raw.astype(jnp.float32), HEAD_COUNT).astype(jnp.bfloat16)
    queries = head_norm(query_raw.astype(jnp.float32), HEAD_COUNT).astype(jnp.bfloat16)
    query_heads = split_heads(queries, HEAD_COUNT)
    key_heads = split_heads(key_rows, HEAD_COUNT)
    value_heads = split_heads(value_rows, HEAD_COUNT)
    scores = (
        jnp.einsum("mphd,nphd->mnhp", query_heads, key_heads, preferred_element_type=jnp.float32)
        * score_scale
    )
    expd = jnp.exp(scores)
    soft = expd / jnp.sum(expd, axis=1, keepdims=True)
    rounded = soft.astype(jnp.bfloat16)
    mixed_out = jnp.einsum(
        "mnhp,nphd->mphd", rounded, value_heads, preferred_element_type=jnp.float32
    )
    mixed_out = mixed_out.reshape(query_raw.shape).astype(jnp.bfloat16)
    mixed_out = lax.all_to_all(mixed_out, "member", split_axis=0, concat_axis=1, tiled=True)
    updated = (
        inputs + jnp.dot(mixed_out, output_weight, preferred_element_type=jnp.float32)
    ).astype(jnp.bfloat16)
    field_up = updated.reshape(mem_dev, lat_dev, lon_dev, channels)
    result = field_up.astype(jnp.float32) + conv_taps(
        pad_field(field_up), conv_kernel, lat_dev, lon_dev, False
    )
    result = result.astype(jnp.bfloat16)
    grad_field = cotangent.astype(jnp.float32) + conv_taps(
        pad_field(cotangent), conv_kernel, lat_dev, lon_dev, True
    )
    grad_rows = grad_field.reshape(mem_dev, cell_count, channels)
    grad_mixed = jnp.einsum(
        "mpc,dc->mpd",
        grad_rows.astype(jnp.bfloat16),
        output_weight,
        preferred_element_type=jnp.float32,
    )
    grad_mixed = grad_mixed.astype(jnp.bfloat16)
    grad_mixed = lax.all_to_all(grad_mixed, "member", split_axis=1, concat_axis=0, tiled=True)
    grad_heads = split_heads(grad_mixed, HEAD_COUNT)
    dprob = jnp.einsum(
        "mphd,nphd->mnhp", grad_heads, value_heads, preferred_element_type=jnp.float32
    )
    dscore = (soft * (dprob - jnp.sum(soft * dprob, axis=1, keepdims=True))).astype(jnp.bfloat16)
    query_grad = (
        jnp.einsum("mnhp,nphd->mphd", dscore, key_heads, preferred_element_type=jnp.float32)
        * score_scale
    )
    query_grad = query_grad.reshape(query_raw.shape)
    key_grad = (
        jnp.einsum("mnhp,mphd->nphd", dscore, query_heads, preferred_element_type=jnp.float32)
        * score_scale
    )
    key_grad = key_grad.reshape(key_raw.shape)
    value_grad = jnp.einsum(
        "mnhp,mphd->nphd", rounded, grad_heads, preferred_element_type=jnp.float32
    )
    value_grad = value_grad.reshape(key_raw.shape)
    grad_query_raw = head_pullback(query_raw, query_grad)
    grad_key_raw = head_pullback(key_raw, key_grad)
    grad_proj = jnp.concatenate([grad_query_raw, grad_key_raw, value_grad], axis=-1).astype(
        jnp.bfloat16
    )
    grad_proj = lax.all_to_all(grad_proj, "member", split_axis=0, concat_axis=1, tiled=True)
    grad_normed = jnp.einsum(
        "mpe,ce->mpc", grad_proj, project_weight, preferred_element_type=jnp.float32
    )
    _, pull_norm = jax.vjp(lambda t: row_norm(t, norm_gain), inputs)
    grad_inputs = pull_norm(grad_normed)[0]
    grad_ensemble = (
        (grad_rows + grad_inputs).astype(jnp.bfloat16).reshape(mem_dev, lat_dev, lon_dev, channels)
    )
    return (result, grad_ensemble)


F32 = jnp.float32
BF16 = jnp.bfloat16
VMEM_LIMIT = 24 * 1024 * 1024
LONG = pl.CostEstimate(flops=20_000_000_000, bytes_accessed=4_000_000, transcendentals=0)


def is_even(axis):
    return lax.rem(lax.axis_index(axis), 2) == 0


def load_kernel(both_ref, *refs):
    count = len(refs) // 2 - 1
    inner_ref, sems = refs[-2:]
    copies = [pltpu.make_async_copy(refs[i], refs[count + i], sems.at[i]) for i in range(count)]
    for copy in copies:
        copy.start()
    rows = both_ref.shape[2]
    inner_ref[...] = both_ref[:, :, 1 : rows - 1]
    for copy in copies:
        copy.wait()


def stack_kernel(ens_ref, cot_ref, both_ref, ring_ref, end_scr, sems):
    _, mem, rows, cols, _ = both_ref.shape
    copies = [
        pltpu.make_async_copy(ref, both_ref.at[i], sems.at[i])
        for i, ref in enumerate((ens_ref, cot_ref))
    ]
    for copy in copies:
        copy.start()
    for copy in copies:
        copy.wait()
    index = 0
    for array in range(2):
        for member in range(mem):
            slot = array * mem + member
            for side, row in enumerate((0, rows - 1)):
                at = (2 * slot + side) * cols
                ring_ref[at : at + cols, :] = both_ref[array, member, row]
            for row in range(1, rows - 1):
                slab = both_ref[array, member, row].astype(F32)
                end_scr[index : index + 1, :] = slab[0:1]
                end_scr[index + 1 : index + 2, :] = slab[cols - 1 : cols]
                index += 2
    ring_ref[4 * mem * cols :, :] = end_scr[...].astype(BF16)


def ring_row(ring_ref, mem, cols, array, member, side):
    at = (2 * (array * mem + member) + side) * cols
    return ring_ref[at : at + cols, :]


def pack_strips_kernel(both_ref, ring_ref, after_ref, chip_ref, core_ref, low_scr, high_scr):
    _, mem, rows, cols, _ = both_ref.shape
    ends = ring_ref[4 * mem * cols :, :].astype(F32)
    index = 0
    for array in range(2):
        for member in range(2 * mem):
            for row in range(rows):
                if member < mem:
                    slab = both_ref[array, member, row].astype(F32)
                elif row in (0, rows - 1):
                    side = 0 if row == 0 else 1
                    slab = ring_row(ring_ref, mem, cols, array, member - mem, side).astype(F32)
                else:
                    at = 2 * ((array * mem + member - mem) * (rows - 2) + row - 1)
                    slab = ends[at : at + 2]
                low_scr[index : index + 1, :] = slab[0:1]
                high_scr[index : index + 1, :] = slab[slab.shape[0] - 1 :]
                index += 1
    even = is_even("lon")
    low, high = low_scr[...], high_scr[...]
    core_ref[...] = jnp.where(even, high, low).astype(BF16)
    chip_ref[...] = jnp.where(even, low, high).astype(BF16)


def rim_columns(chip_ref, core_ref):
    even = is_even("lon")
    chip, core = chip_ref[...].astype(F32), core_ref[...].astype(F32)
    return jnp.where(even, chip, core), jnp.where(even, core, chip)


def pack_rows_kernel(
    both_ref, ring_ref, chip_ref, core_ref, after_ref, first_ref, second_ref, edge_scr
):
    _, mem, rows, cols, _ = both_ref.shape
    slots = 4 * mem
    even = is_even("lat")
    west, east = rim_columns(chip_ref, core_ref)
    for slot in range(slots):
        array, member = divmod(slot, 2 * mem)
        if member < mem:
            pair = [both_ref[array, member, row] for row in (0, rows - 1)]
        else:
            pair = [ring_row(ring_ref, mem, cols, array, member - mem, side) for side in (0, 1)]
        start, stop = (slab.astype(F32) for slab in pair)
        at = slice(slot * cols, (slot + 1) * cols)
        first_ref[at, :] = jnp.where(even, stop, start).astype(BF16)
        second_ref[at, :] = jnp.where(even, start, stop).astype(BF16)
        top, low = slot * rows, (slot + 1) * rows - 1
        for side, column in enumerate((west, east)):
            place = side * slots + slot
            start, stop = column[top : top + 1], column[low : low + 1]
            edge_scr[0, place : place + 1, :] = jnp.where(even, stop, start)
            edge_scr[1, place : place + 1, :] = jnp.where(even, start, stop)
    first_ref[slots * cols :, :] = edge_scr[0].astype(BF16)
    second_ref[slots * cols :, :] = edge_scr[1].astype(BF16)


def dot_nn(a, b):
    return lax.dot_general(a, b, (((1,), (0,)), ((), ())), preferred_element_type=F32)


def same_head_matrix(channels):
    width = channels // HEAD_COUNT
    lane_row = lax.broadcasted_iota(jnp.int32, (channels, channels), 0) // width
    lane_col = lax.broadcasted_iota(jnp.int32, (channels, channels), 1) // width
    return jnp.where(lane_row == lane_col, 1.0, 0.0).astype(BF16)


def head_sums(values, same_head):
    high = values.astype(BF16)
    low = (values - high.astype(F32)).astype(BF16)
    return dot_nn(high, same_head) + dot_nn(low, same_head)


def rounded_sums(values, same_head):
    return dot_nn(values.astype(BF16), same_head)


def head_units(raw, same_head, sums=head_sums):
    raw = raw.astype(F32)
    mean_sq = sums(raw * raw, same_head) * (HEAD_COUNT / raw.shape[-1])
    inverse = lax.rsqrt(jnp.maximum(mean_sq, FLOOR))
    return raw, mean_sq, inverse, (raw * inverse).astype(BF16)


def row_rsqrt(values):
    return lax.rsqrt(jnp.mean(values * values, axis=-1, keepdims=True) + EPSILON)


def split_rows(array, count):
    size = array.shape[0] // count
    return [array[i * size : (i + 1) * size] for i in range(count)]


def softmax_members(queries, keys, same_head, scale):
    products = [query * key for query in queries for key in keys]
    scores = dot_nn(jnp.concatenate(products, axis=0), same_head) * scale
    exps = split_rows(jnp.exp(scores), len(products))
    soft = []
    for m in range(len(queries)):
        mine = exps[m * len(keys) : (m + 1) * len(keys)]
        total = mine[0]
        for e in mine[1:]:
            total = total + e
        inverse = 1.0 / total
        soft.append([e * inverse for e in mine])
    return soft


def mix_values(probs, values):
    mixed = None
    for prob, value in zip(probs, values):
        term = prob.astype(BF16).astype(F32) * value.astype(F32)
        mixed = term if mixed is None else mixed + term
    return mixed.astype(BF16)


def forward_cells(x, mem, groups, gain, project_ref, output_ref, same_head):
    channels = x.shape[-1]
    own_rows = x.shape[0] // groups * mem
    scale = 1.0 / math.sqrt(channels // HEAD_COUNT)
    normed = (x * row_rsqrt(x) * gain).astype(BF16)
    query_raw = dot_nn(normed[:own_rows], project_ref[:, :channels]).astype(BF16)
    key_raw = dot_nn(normed, project_ref[:, channels : 2 * channels]).astype(BF16)
    values = dot_nn(normed, project_ref[:, 2 * channels :]).astype(BF16)
    raw = jnp.concatenate([query_raw, key_raw], axis=0)
    units = head_units(raw, same_head, rounded_sums)[3]
    queries = split_rows(units[:own_rows], mem)
    keys = split_rows(units[own_rows:], groups)
    values = split_rows(values, groups)
    soft = softmax_members(queries, keys, same_head, scale)
    mixed = jnp.concatenate([mix_values(soft[m], values) for m in range(mem)], axis=0)
    return (x[:own_rows] + dot_nn(mixed, output_ref[...])).astype(BF16)


def shift_row(scr, member, place, slab, west, east):
    cols, channels = slab.shape
    column = lax.broadcasted_iota(jnp.int32, (cols, channels), 0)
    back = jnp.where(column == 0, west, pltpu.roll(slab, 1, 0))
    ahead = jnp.where(column == cols - 1, east, pltpu.roll(slab, cols - 1, 0))
    rows_at = slice(place * cols, (place + 1) * cols)
    scr[member, rows_at, :channels] = back.astype(BF16)
    scr[member, rows_at, channels : 2 * channels] = slab.astype(BF16)
    scr[member, rows_at, 2 * channels :] = ahead.astype(BF16)


def tap_rows(taps_ref, r):
    size = taps_ref.shape[0] // 3
    return taps_ref[r * size : (r + 1) * size, :]


def turn_kernel(project_ref, output_ref, conv_ref, project_t_ref, output_t_ref, conv_t_ref):
    channels = output_ref.shape[0]
    output_t_ref[...] = output_ref[...].T
    for kind in range(3):
        lanes = slice(kind * channels, (kind + 1) * channels)
        project_t_ref[lanes, :] = project_ref[:, lanes].T
    for r in range(3):
        for c in range(3):
            tap = (3 * r + c) * channels
            turned = (3 * r + 2 - c) * channels
            conv_t_ref[turned : turned + channels, :] = conv_ref[tap : tap + channels, :].T


def own_kernel(
    both_ref,
    ring_ref,
    inner_ref,
    gain_ref,
    project_ref,
    output_ref,
    after_ref,
    proj_ref,
    unit_ref,
    soft_ref,
    inverse_ref,
    pull_ref,
    updated_ref,
):
    _, mem, rows, cols, channels = both_ref.shape
    groups = 2 * mem
    cells = rows * cols
    width = channels // HEAD_COUNT
    scale = 1.0 / math.sqrt(width)
    same_head = same_head_matrix(channels)
    slabs = [both_ref[0].reshape(mem * cells, channels)]
    for member in range(mem):
        slabs.append(ring_row(ring_ref, mem, cols, 0, member, 0))
        slabs.append(inner_ref[0, member].reshape((rows - 2) * cols, channels))
        slabs.append(ring_row(ring_ref, mem, cols, 0, member, 1))
    x = jnp.concatenate(slabs, axis=0).astype(F32)
    normed = (x * row_rsqrt(x) * gain_ref[...]).astype(BF16)
    proj = dot_nn(normed, project_ref[...]).astype(BF16)
    proj_ref[...] = proj.reshape(groups, cells, 3 * channels)
    both_raw = jnp.concatenate([proj[:, :channels], proj[:, channels : 2 * channels]], axis=0)
    raw, mean_sq, inverse, units = head_units(both_raw, same_head)
    unit_ref[...] = units.reshape(2, groups, cells, channels)
    active = jnp.where(mean_sq > FLOOR, 1.0, jnp.where(mean_sq == FLOOR, 0.5, 0.0))
    pull = active * raw * (inverse * inverse * inverse) / width
    for kind in range(2):
        at = kind * groups * cells
        mine = slice(at, at + mem * cells)
        inverse_ref[kind] = inverse[mine].reshape(mem, cells, channels)
        pull_ref[kind] = pull[mine].reshape(mem, cells, channels)
    units = split_rows(units, 2 * groups)
    soft = softmax_members(units[:groups], units[groups:], same_head, scale)
    for m in range(groups):
        for n in range(groups):
            soft_ref[m * groups + n] = soft[m][n]
    values = split_rows(proj[:, 2 * channels :], groups)
    mixed = jnp.concatenate([mix_values(soft[m], values) for m in range(mem)], axis=0)
    updated = x[: mem * cells] + dot_nn(mixed, output_ref[...])
    updated_ref[...] = updated.astype(BF16).reshape(mem, cells, channels)


def backward_cells(
    pick, grad_field, x, gain, weights_t, proj_ref, unit_ref, soft_ref, inverse_ref, pull_ref
):
    project_t_ref, output_t_ref = weights_t
    groups = proj_ref.shape[0]
    mem = inverse_ref.shape[1]
    channels = x.shape[-1]
    scale = 1.0 / math.sqrt(channels // HEAD_COUNT)
    same_head = same_head_matrix(channels)
    grad_mixed = dot_nn(grad_field.astype(BF16), output_t_ref[...]).astype(BF16)
    grads = split_rows(grad_mixed, groups)
    values = [pick(proj_ref[n, :, 2 * channels :]) for n in range(groups)]
    products = [grads[m] * values[n] for m in range(groups) for n in range(groups)]
    dprobs = split_rows(dot_nn(jnp.concatenate(products, axis=0), same_head), len(products))
    units = [[pick(unit_ref[k, n]).astype(F32) for n in range(groups)] for k in range(2)]
    query_grad = [None] * mem
    key_grad = [None] * mem
    value_grad = [None] * mem
    for m in range(groups):
        soft = [pick(soft_ref[m * groups + n]) for n in range(groups)]
        dprob = dprobs[m * groups : (m + 1) * groups]
        mean = soft[0] * dprob[0]
        for n in range(1, groups):
            mean = mean + soft[n] * dprob[n]
        for n in range(groups):
            if m >= mem and n >= mem:
                continue
            dscore = soft[n] * (dprob[n] - mean)
            if m < mem:
                term = dscore * units[1][n]
                query_grad[m] = term if query_grad[m] is None else query_grad[m] + term
            if n < mem:
                term = dscore * units[0][m]
                key_grad[n] = term if key_grad[n] is None else key_grad[n] + term
                term = soft[n] * grads[m].astype(F32)
                value_grad[n] = term if value_grad[n] is None else value_grad[n] + term

    unit_grads = [jnp.concatenate(g, axis=0) * scale for g in (query_grad, key_grad)]

    def members(take):
        return jnp.concatenate([pick(take(m)) for m in range(mem)], axis=0)

    raws = []
    for kind in range(2):
        lanes = slice(kind * channels, (kind + 1) * channels)
        raws.append(members(lambda m: proj_ref[m, :, lanes]).astype(F32))
    inner = rounded_sums(
        jnp.concatenate([g * raw for g, raw in zip(unit_grads, raws)], axis=0), same_head
    )
    inner = split_rows(inner, 2)
    pulled = []
    for kind in range(2):
        inverse = members(lambda m: inverse_ref[kind, m])
        pull = members(lambda m: pull_ref[kind, m])
        pulled.append((inverse * unit_grads[kind] - pull * inner[kind]).astype(BF16))
    pulled.append(jnp.concatenate(value_grad, axis=0).astype(BF16))
    grad_normed = dot_nn(jnp.concatenate(pulled, axis=1), project_t_ref[...]) * gain
    inverse = row_rsqrt(x)
    inner = jnp.mean(x * grad_normed, axis=-1, keepdims=True)
    total = grad_field[: x.shape[0]] + inverse * grad_normed
    return (total - x * (inverse * inverse * inverse * inner)).astype(BF16)


def centre_kernel(
    both_ref,
    ring_ref,
    inner_ref,
    chip_ref,
    core_ref,
    gain_ref,
    project_ref,
    output_ref,
    conv_ref,
    project_t_ref,
    output_t_ref,
    conv_t_ref,
    proj_ref,
    unit_ref,
    soft_ref,
    inverse_ref,
    pull_ref,
    updated_ref,
    result_ref,
    grad_ref,
    result_part_ref,
    grad_part_ref,
    shift_scr,
    cot_shift_scr,
    strip_scr,
):
    _, mem, rows, cols, channels = both_ref.shape
    groups = 2 * mem
    cells = rows * cols
    gain = gain_ref[...]
    same_head = same_head_matrix(channels)
    west, east = rim_columns(chip_ref, core_ref)

    def convolve(scr, count, start, taps_ref, turned):
        sums = [
            [start[(m * rows + a) * cols : (m * rows + a + 1) * cols] for a in range(rows)]
            for m in range(count)
        ]
        for r in range(3):
            step = 1 - r if turned else r - 1
            outs = [a for a in range(rows) if 0 <= a + step < rows]
            begin, end = outs[0] + step, outs[-1] + step + 1
            window = jnp.concatenate(
                [scr[m, begin * cols : end * cols, :] for m in range(count)], axis=0
            )
            terms = split_rows(dot_nn(window, tap_rows(taps_ref, r)), count * len(outs))
            for m in range(count):
                for i, a in enumerate(outs):
                    sums[m][a] = sums[m][a] + terms[m * len(outs) + i]
        return sums

    cots = []
    for member in range(groups):
        for row in range(rows):
            if member < mem:
                slab = both_ref[1, member, row]
            elif row in (0, rows - 1):
                slab = ring_row(ring_ref, mem, cols, 1, member - mem, 0 if row == 0 else 1)
            else:
                slab = inner_ref[1, member - mem, row - 1]
            slab = slab.astype(F32)
            cots.append(slab)
            at = (groups + member) * rows + row
            shift_row(cot_shift_scr, member, row, slab, west[at : at + 1], east[at : at + 1])
    sums = convolve(cot_shift_scr, groups, jnp.concatenate(cots, axis=0), conv_t_ref, True)
    for member in range(groups):
        grad_part_ref[member, :cols, :] = sums[member][0]
        grad_part_ref[member, cols:, :] = sums[member][rows - 1]
    grad_field = jnp.concatenate([slab for s in sums for slab in s[1 : rows - 1]], axis=0)

    for member in range(groups):
        at = member * rows
        strip_scr[member] = jnp.zeros((16, channels), F32)
        strip_scr[member, :rows, :] = west[at : at + rows]
        strip_scr[member, 8 : 8 + rows, :] = east[at : at + rows]
    x = strip_scr[...].reshape(groups * 16, channels)
    fresh = forward_cells(x, mem, groups, gain, project_ref, output_ref, same_head)
    fresh = split_rows(fresh.astype(F32), mem)

    pick = lambda array: array[cols : cells - cols]
    x = both_ref[0, :, 1 : rows - 1].reshape(mem * (cells - 2 * cols), channels).astype(F32)
    total = backward_cells(
        pick,
        grad_field,
        x,
        gain,
        (project_t_ref, output_t_ref),
        proj_ref,
        unit_ref,
        soft_ref,
        inverse_ref,
        pull_ref,
    )
    grad_ref[...] = total.reshape(mem, rows - 2, cols, channels)

    for member in range(mem):
        for row in range(rows):
            slab = updated_ref[member, row * cols : (row + 1) * cols, :].astype(F32)
            ends = fresh[member][row : row + 1], fresh[member][8 + row : 9 + row]
            shift_row(shift_scr, member, row, slab, *ends)
    start = updated_ref[...].reshape(mem * cells, channels).astype(F32)
    sums = convolve(shift_scr, mem, start, conv_ref, False)
    for member in range(mem):
        result_part_ref[member, :cols, :] = sums[member][0]
        result_part_ref[member, cols:, :] = sums[member][rows - 1]
        for row in range(1, rows - 1):
            result_ref[member, row - 1] = sums[member][row].astype(BF16)


def main_kernel(
    both_ref,
    second_ref,
    first_ref,
    gain_ref,
    project_ref,
    output_ref,
    conv_ref,
    project_t_ref,
    output_t_ref,
    conv_t_ref,
    proj_ref,
    unit_ref,
    soft_ref,
    inverse_ref,
    pull_ref,
    inner_result_ref,
    inner_grad_ref,
    result_part_ref,
    grad_part_ref,
    result_ref,
    grad_ref,
    shift_scr,
    cot_shift_scr,
    corner_scr,
    *,
    lat_count,
):
    _, mem, rows, cols, channels = both_ref.shape
    groups = 2 * mem
    slots = 2 * groups
    cells = rows * cols
    gain = gain_ref[...]
    same_head = same_head_matrix(channels)
    lat_even = is_even("lat")
    lat = lax.axis_index("lat")

    def halos(at):
        first, second = first_ref[at, :].astype(F32), second_ref[at, :].astype(F32)
        north = jnp.where(lat == 0, 0.0, jnp.where(lat_even, second, first))
        south = jnp.where(lat == lat_count - 1, 0.0, jnp.where(lat_even, first, second))
        return north, south

    halo = [halos(slice(slot * cols, (slot + 1) * cols)) for slot in range(slots)]
    corners = halos(slice(slots * cols, slots * cols + 2 * slots))

    def corner(side, slot, end):
        at = end * slots + slot
        return corners[side][at : at + 1]

    def halo_part(scr, count, taps_ref, turned):
        north, south = (2, 0) if turned else (0, 2)
        parts = []
        for side, r in ((0, north), (1, south)):
            window = jnp.concatenate(
                [scr[m, side * cols : (side + 1) * cols, :] for m in range(count)], axis=0
            )
            parts.append(split_rows(dot_nn(window, tap_rows(taps_ref, r)), count))
        return jnp.concatenate([parts[side][m] for m in range(count) for side in (0, 1)], axis=0)

    for member in range(groups):
        slot = groups + member
        for side in (0, 1):
            ends = corner(side, slot, 0), corner(side, slot, 1)
            shift_row(cot_shift_scr, member, side, halo[slot][side], *ends)
    grad_field = grad_part_ref[...].reshape(groups * 2 * cols, channels)
    grad_field = grad_field + halo_part(cot_shift_scr, groups, conv_t_ref, True)

    blocks = []
    for member in range(groups):
        corner_scr[member] = jnp.zeros((16, channels), F32)
        for side in (0, 1):
            for end in (0, 1):
                at = 2 * side + end
                corner_scr[member, at : at + 1, :] = corner(side, member, end)
        blocks += [halo[member][0], halo[member][1], corner_scr[member]]
    x = jnp.concatenate(blocks, axis=0)
    fresh = forward_cells(x, mem, groups, gain, project_ref, output_ref, same_head)
    fresh = split_rows(fresh.astype(F32), mem)

    pick = lambda array: jnp.concatenate([array[:cols], array[cells - cols :]], axis=0)
    x = [both_ref[0, m, row] for m in range(mem) for row in (0, rows - 1)]
    total = backward_cells(
        pick,
        grad_field,
        jnp.concatenate(x, axis=0).astype(F32),
        gain,
        (project_t_ref, output_t_ref),
        proj_ref,
        unit_ref,
        soft_ref,
        inverse_ref,
        pull_ref,
    )

    for member in range(mem):
        for side in (0, 1):
            slab = fresh[member][side * cols : (side + 1) * cols]
            at = 2 * cols + 2 * side
            ends = fresh[member][at : at + 1], fresh[member][at + 1 : at + 2]
            shift_row(shift_scr, member, side, slab, *ends)
    outer = result_part_ref[...].reshape(mem * 2 * cols, channels)
    outer = (outer + halo_part(shift_scr, mem, conv_ref, False)).astype(BF16)
    outputs = (
        (result_ref, inner_result_ref, split_rows(outer, 2 * mem)),
        (grad_ref, inner_grad_ref, split_rows(total, 2 * mem)),
    )
    for out_ref, inner_ref, edge in outputs:
        for member in range(mem):
            out_ref[member, 0] = edge[2 * member]
            out_ref[member, rows - 1] = edge[2 * member + 1]
            for row in range(1, rows - 1):
                out_ref[member, row] = inner_ref[member, row - 1]


def local_call(kernel, name, operands, out_shape, scratch, pinned=False, cost=None):
    whole = pl.BlockSpec(memory_space=pltpu.VMEM)
    anywhere = pl.BlockSpec(memory_space=pl.ANY)
    specs = [anywhere if in_hbm else whole for _, in_hbm in operands]
    arrays = [
        pltpu.with_memory_space_constraint(array, pltpu.HBM) if in_hbm else array
        for array, in_hbm in operands
    ]

    def keep(shape):
        return pltpu.VMEM(shape.shape, shape.dtype) if pinned else shape

    return pl.pallas_call(
        kernel,
        out_shape=jax.tree.map(keep, out_shape),
        in_specs=specs,
        out_specs=jax.tree.map(lambda _: whole, out_shape),
        scratch_shapes=scratch,
        compiler_params=pltpu.CompilerParams(vmem_limit_bytes=VMEM_LIMIT),
        cost_estimate=cost,
        name=name,
    )(*arrays)


def here(*arrays):
    return [(array, False) for array in arrays]


def in_hbm(*arrays):
    return [(array, True) for array in arrays]


def per_device_paired(ensemble, norm_gain, project_weight, output_weight, conv_kernel, cotangent):
    mem, rows, cols, channels = ensemble.shape
    if rows < 3 or cols % 16 or (4 * mem * (rows - 2)) % 16:
        return per_device_general(
            ensemble, norm_gain, project_weight, output_weight, conv_kernel, cotangent
        )
    groups = 2 * mem
    slots = 2 * groups
    cells = rows * cols
    lon_count = lax.axis_size("lon")
    lat_count = lax.axis_size("lat")
    bf16 = functools.partial(jax.ShapeDtypeStruct, dtype=BF16)
    f32 = functools.partial(jax.ShapeDtypeStruct, dtype=F32)
    swap = [(0, 1), (1, 0)]
    core_pairs = [(i, i ^ 1) for i in range(lon_count)]
    chip_pairs = [(i, (i - 1 if i % 2 == 0 else i + 1) % lon_count) for i in range(lon_count)]

    def lat_swap(offset):
        pairs = []
        for lat in range(lat_count):
            for lon in range(lon_count):
                to = (lat + 1 if lat % 2 == offset else lat - 1, lon)
                if not 0 <= to[0] < lat_count:
                    to = (lat, lon ^ 1)
                pairs.append((lat * lon_count + lon, to[0] * lon_count + to[1]))
        return pairs

    ends = 4 * mem * (rows - 2)
    inner_shape = (2, mem, rows - 2, cols, channels)
    both, ring = local_call(
        stack_kernel,
        "stack",
        in_hbm(ensemble, cotangent),
        (
            bf16((2,) + ensemble.shape),
            bf16((4 * mem * cols + ends, channels)),
        ),
        [pltpu.VMEM((ends, channels), F32), pltpu.SemaphoreType.DMA((2,))],
        pinned=True,
    )
    ring = lax.ppermute(ring, "member", swap)

    weights = (
        norm_gain.reshape(1, channels),
        project_weight,
        output_weight,
        conv_kernel.reshape(9 * channels, channels),
    )
    *weights, inner = local_call(
        load_kernel,
        "load_weights",
        here(both) + in_hbm(*weights),
        tuple(jax.ShapeDtypeStruct(w.shape, w.dtype) for w in weights) + (bf16(inner_shape),),
        [pltpu.SemaphoreType.DMA((4,))],
        pinned=True,
    )
    inner = lax.ppermute(inner, "member", swap)

    strip = (slots * rows, channels)
    chip_send, core_send = local_call(
        pack_strips_kernel,
        "pack_strips",
        here(both, ring, weights[0]),
        (bf16(strip), bf16(strip)),
        [pltpu.VMEM(strip, F32)] * 2,
    )
    chip = lax.ppermute(chip_send, "lon", chip_pairs)
    core = lax.ppermute(core_send, "lon", core_pairs)

    turned = local_call(
        turn_kernel,
        "turn_weights",
        here(*weights[1:]),
        (
            bf16((3 * channels, channels)),
            bf16((channels, channels)),
            bf16((9 * channels, channels)),
        ),
        [],
        pinned=True,
    )
    halo = bf16((slots * (cols + 2), channels))
    first_send, second_send = local_call(
        pack_rows_kernel,
        "pack_rows",
        here(both, ring, chip, core, turned[1]),
        (halo, halo),
        [pltpu.VMEM((2, 2 * slots, channels), F32)],
    )
    first = lax.ppermute(first_send, ("lat", "lon"), lat_swap(0))
    second = lax.ppermute(second_send, ("lat", "lon"), lat_swap(1))

    *held, updated = local_call(
        own_kernel,
        "own_cells",
        here(both, ring, inner, *weights[:3], second_send),
        (
            bf16((groups, cells, 3 * channels)),
            bf16((2, groups, cells, channels)),
            f32((groups * groups, cells, channels)),
            f32((2, mem, cells, channels)),
            f32((2, mem, cells, channels)),
            bf16((mem, cells, channels)),
        ),
        [],
        pinned=True,
        cost=LONG,
    )
    held = [*turned, *held]
    parts = local_call(
        centre_kernel,
        "centre",
        here(both, ring, inner, chip, core, *weights, *held, updated),
        (
            bf16((mem, rows - 2, cols, channels)),
            bf16((mem, rows - 2, cols, channels)),
            f32((mem, 2 * cols, channels)),
            f32((groups, 2 * cols, channels)),
        ),
        [
            pltpu.VMEM((mem, cells, 3 * channels), BF16),
            pltpu.VMEM((groups, cells, 3 * channels), BF16),
            pltpu.VMEM((groups, 16, channels), F32),
        ],
        pinned=True,
        cost=LONG,
    )
    return local_call(
        functools.partial(main_kernel, lat_count=lat_count),
        "main",
        here(both, second, first, *weights, *held, *parts),
        (bf16(ensemble.shape), bf16(ensemble.shape)),
        [
            pltpu.VMEM((mem, 2 * cols, 3 * channels), BF16),
            pltpu.VMEM((groups, 2 * cols, 3 * channels), BF16),
            pltpu.VMEM((groups, 16, channels), F32),
        ],
    )


def solution(mesh):
    paired = mesh.shape["member"] == 2 and mesh.shape["lon"] % 2 == 0
    per_device = per_device_paired if paired else per_device_general
    in_specs = (
        P("member", "lat", "lon", None),
        P(),
        P(),
        P(),
        P(),
        P("member", "lat", "lon", None),
    )
    out_specs = (P("member", "lat", "lon", None), P("member", "lat", "lon", None))
    return jax.shard_map(
        per_device, mesh=mesh, in_specs=in_specs, out_specs=out_specs, check_vma=False
    )
```

```python
import functools
import math

import jax
import jax.numpy as jnp
from jax import lax
from jax.experimental import pallas as pl
from jax.experimental.pallas import tpu as pltpu
from jax.sharding import PartitionSpec as P

HEAD_COUNT = 8


FLOOR = 0.5
EPSILON = 1e-06


def padded_2(block, sides, width, periodic):
    for axis, dim in sides:
        count = lax.axis_size(axis)
        forward = [(i, i + 1) for i in range(count - 1)]
        if periodic:
            forward.append((count - 1, 0))
        backward = [(target, source) for source, target in forward]
        low = lax.ppermute(
            lax.slice_in_dim(block, block.shape[dim] - width, None, axis=dim), axis, forward
        )
        high = lax.ppermute(lax.slice_in_dim(block, 0, width, axis=dim), axis, backward)
        block = jnp.concatenate([low, block, high], axis=dim)
    return block


def row_norm(values, gain_vec):
    mean_sq = jnp.mean(values * values, axis=-1, keepdims=True)
    return values * lax.rsqrt(mean_sq + EPSILON) * gain_vec


def head_norm(values, head_count):
    shaped = values.reshape(values.shape[:-1] + (head_count, values.shape[-1] // head_count))
    mean_sq = jnp.mean(shaped * shaped, axis=-1, keepdims=True)
    return (shaped * lax.rsqrt(jnp.maximum(mean_sq, FLOOR))).reshape(values.shape)


def split_heads(values, head_count):
    return values.reshape(values.shape[:-1] + (head_count, values.shape[-1] // head_count))


def head_pullback(raw_rows, grad_rows):
    _, pullback = jax.vjp(lambda t: head_norm(t, HEAD_COUNT), raw_rows.astype(jnp.float32))
    return pullback(grad_rows)[0]


def pad_field(field_in):
    widened = padded_2(field_in, (("lon", 2),), 1, True)
    return padded_2(widened, (("lat", 1),), 1, False)


def conv_taps(padded, kernel, lat_n, lon_n, adjoint):
    running = None
    for row_off in range(3):
        for col_off in range(3):
            if adjoint:
                window = padded[
                    :, 2 - row_off : 2 - row_off + lat_n, 2 - col_off : 2 - col_off + lon_n
                ]
                summand = jnp.einsum(
                    "mabc,dc->mabd",
                    window,
                    kernel[row_off, col_off],
                    preferred_element_type=jnp.float32,
                )
            else:
                window = padded[:, row_off : row_off + lat_n, col_off : col_off + lon_n]
                summand = jnp.einsum(
                    "mabc,cd->mabd",
                    window,
                    kernel[row_off, col_off],
                    preferred_element_type=jnp.float32,
                )
            running = summand if running is None else running + summand
    return running


def per_device_general(ensemble, norm_gain, project_weight, output_weight, conv_kernel, cotangent):
    mem_dev, lat_dev, lon_dev, channels = ensemble.shape
    cell_count = lat_dev * lon_dev
    score_scale = 1.0 / math.sqrt(channels // HEAD_COUNT)
    inputs = ensemble.reshape(mem_dev, cell_count, channels).astype(jnp.float32)
    normed = row_norm(inputs, norm_gain).astype(jnp.bfloat16)
    spread = lax.all_to_all(normed, "member", split_axis=1, concat_axis=0, tiled=True)
    projected = jnp.dot(spread, project_weight, preferred_element_type=jnp.float32).astype(
        jnp.bfloat16
    )
    query_raw = projected[..., :channels]
    key_raw = projected[..., channels : 2 * channels]
    value_rows = projected[..., 2 * channels :]
    key_rows = head_norm(key_raw.astype(jnp.float32), HEAD_COUNT).astype(jnp.bfloat16)
    queries = head_norm(query_raw.astype(jnp.float32), HEAD_COUNT).astype(jnp.bfloat16)
    query_heads = split_heads(queries, HEAD_COUNT)
    key_heads = split_heads(key_rows, HEAD_COUNT)
    value_heads = split_heads(value_rows, HEAD_COUNT)
    scores = (
        jnp.einsum("mphd,nphd->mnhp", query_heads, key_heads, preferred_element_type=jnp.float32)
        * score_scale
    )
    expd = jnp.exp(scores)
    soft = expd / jnp.sum(expd, axis=1, keepdims=True)
    rounded = soft.astype(jnp.bfloat16)
    mixed_out = jnp.einsum(
        "mnhp,nphd->mphd", rounded, value_heads, preferred_element_type=jnp.float32
    )
    mixed_out = mixed_out.reshape(query_raw.shape).astype(jnp.bfloat16)
    mixed_out = lax.all_to_all(mixed_out, "member", split_axis=0, concat_axis=1, tiled=True)
    updated = (
        inputs + jnp.dot(mixed_out, output_weight, preferred_element_type=jnp.float32)
    ).astype(jnp.bfloat16)
    field_up = updated.reshape(mem_dev, lat_dev, lon_dev, channels)
    result = field_up.astype(jnp.float32) + conv_taps(
        pad_field(field_up), conv_kernel, lat_dev, lon_dev, False
    )
    result = result.astype(jnp.bfloat16)
    grad_field = cotangent.astype(jnp.float32) + conv_taps(
        pad_field(cotangent), conv_kernel, lat_dev, lon_dev, True
    )
    grad_rows = grad_field.reshape(mem_dev, cell_count, channels)
    grad_mixed = jnp.einsum(
        "mpc,dc->mpd",
        grad_rows.astype(jnp.bfloat16),
        output_weight,
        preferred_element_type=jnp.float32,
    )
    grad_mixed = grad_mixed.astype(jnp.bfloat16)
    grad_mixed = lax.all_to_all(grad_mixed, "member", split_axis=1, concat_axis=0, tiled=True)
    grad_heads = split_heads(grad_mixed, HEAD_COUNT)
    dprob = jnp.einsum(
        "mphd,nphd->mnhp", grad_heads, value_heads, preferred_element_type=jnp.float32
    )
    dscore = (soft * (dprob - jnp.sum(soft * dprob, axis=1, keepdims=True))).astype(jnp.bfloat16)
    query_grad = (
        jnp.einsum("mnhp,nphd->mphd", dscore, key_heads, preferred_element_type=jnp.float32)
        * score_scale
    )
    query_grad = query_grad.reshape(query_raw.shape)
    key_grad = (
        jnp.einsum("mnhp,mphd->nphd", dscore, query_heads, preferred_element_type=jnp.float32)
        * score_scale
    )
    key_grad = key_grad.reshape(key_raw.shape)
    value_grad = jnp.einsum(
        "mnhp,mphd->nphd", rounded, grad_heads, preferred_element_type=jnp.float32
    )
    value_grad = value_grad.reshape(key_raw.shape)
    grad_query_raw = head_pullback(query_raw, query_grad)
    grad_key_raw = head_pullback(key_raw, key_grad)
    grad_proj = jnp.concatenate([grad_query_raw, grad_key_raw, value_grad], axis=-1).astype(
        jnp.bfloat16
    )
    grad_proj = lax.all_to_all(grad_proj, "member", split_axis=0, concat_axis=1, tiled=True)
    grad_normed = jnp.einsum(
        "mpe,ce->mpc", grad_proj, project_weight, preferred_element_type=jnp.float32
    )
    _, pull_norm = jax.vjp(lambda t: row_norm(t, norm_gain), inputs)
    grad_inputs = pull_norm(grad_normed)[0]
    grad_ensemble = (
        (grad_rows + grad_inputs).astype(jnp.bfloat16).reshape(mem_dev, lat_dev, lon_dev, channels)
    )
    return (result, grad_ensemble)


F32 = jnp.float32
BF16 = jnp.bfloat16
VMEM_LIMIT = 24 * 1024 * 1024
LONG = pl.CostEstimate(flops=20_000_000_000, bytes_accessed=4_000_000, transcendentals=0)
MIDDLING = pl.CostEstimate(flops=3_000_000_000, bytes_accessed=2_000_000, transcendentals=0)


def is_even(axis):
    return lax.rem(lax.axis_index(axis), 2) == 0


def load_kernel(
    gain_hbm,
    project_hbm,
    output_hbm,
    conv_hbm,
    gain_ref,
    project_ref,
    output_ref,
    conv_ref,
    project_t_ref,
    output_t_ref,
    sems,
):
    channels = output_ref.shape[0]
    pairs = (
        (gain_hbm, gain_ref),
        (project_hbm, project_ref),
        (output_hbm, output_ref),
        (conv_hbm, conv_ref),
    )
    loads = [
        pltpu.make_async_copy(source, target, sems.at[i])
        for i, (source, target) in enumerate(pairs)
    ]
    for load in loads:
        load.start()
    for load in loads[:3]:
        load.wait()
    output_t_ref[...] = output_ref[...].T
    for kind in range(3):
        lanes = slice(kind * channels, (kind + 1) * channels)
        project_t_ref[lanes, :] = project_ref[:, lanes].T
    loads[3].wait()


def stack_kernel(ens_ref, cot_ref, both_ref, ends_ref, low_scr, high_scr, sems):
    _, mem, rows, cols, _ = both_ref.shape
    copies = [
        pltpu.make_async_copy(ref, both_ref.at[i], sems.at[i])
        for i, ref in enumerate((ens_ref, cot_ref))
    ]
    for copy in copies:
        copy.start()
    for copy in copies:
        copy.wait()
    index = 0
    for array in range(2):
        for member in range(mem):
            for row in range(rows):
                slab = both_ref[array, member, row].astype(F32)
                low_scr[index : index + 1, :] = slab[0:1]
                high_scr[index : index + 1, :] = slab[cols - 1 : cols]
                index += 1
    ends_ref[0] = low_scr[...].astype(BF16)
    ends_ref[1] = high_scr[...].astype(BF16)


def pack_strips_kernel(ends_ref, other_ends_ref, chip_ref, core_ref, low_scr, high_scr):
    part = ends_ref.shape[1] // 2
    for side, scr in ((0, low_scr), (1, high_scr)):
        for group, ref in enumerate((ends_ref, other_ends_ref)):
            column = ref[side].astype(F32)
            for array in range(2):
                at = (2 * array + group) * part
                scr[at : at + part, :] = column[array * part : (array + 1) * part]
    even = is_even("lon")
    low, high = low_scr[...], high_scr[...]
    core_ref[...] = jnp.where(even, high, low).astype(BF16)
    chip_ref[...] = jnp.where(even, low, high).astype(BF16)


def rim_columns(chip_ref, core_ref):
    even = is_even("lon")
    chip, core = chip_ref[...].astype(F32), core_ref[...].astype(F32)
    return jnp.where(even, chip, core), jnp.where(even, core, chip)


def pack_rows_kernel(
    both_ref, other_ref, chip_ref, core_ref, after_ref, first_ref, second_ref, edge_scr
):
    _, mem, rows, cols, _ = both_ref.shape
    slots = 4 * mem
    even = is_even("lat")
    west, east = rim_columns(chip_ref, core_ref)
    for slot in range(slots):
        array, member = divmod(slot, 2 * mem)
        ref, who = (both_ref, member) if member < mem else (other_ref, member - mem)
        start, stop = (ref[array, who, row].astype(F32) for row in (0, rows - 1))
        at = slice(slot * cols, (slot + 1) * cols)
        first_ref[at, :] = jnp.where(even, stop, start).astype(BF16)
        second_ref[at, :] = jnp.where(even, start, stop).astype(BF16)
        top, low = slot * rows, (slot + 1) * rows - 1
        for side, column in enumerate((west, east)):
            place = side * slots + slot
            start, stop = column[top : top + 1], column[low : low + 1]
            edge_scr[0, place : place + 1, :] = jnp.where(even, stop, start)
            edge_scr[1, place : place + 1, :] = jnp.where(even, start, stop)
    first_ref[slots * cols :, :] = edge_scr[0].astype(BF16)
    second_ref[slots * cols :, :] = edge_scr[1].astype(BF16)


def dot_nn(a, b):
    return lax.dot_general(a, b, (((1,), (0,)), ((), ())), preferred_element_type=F32)


def same_head_matrix(channels):
    width = channels // HEAD_COUNT
    lane_row = lax.broadcasted_iota(jnp.int32, (channels, channels), 0) // width
    lane_col = lax.broadcasted_iota(jnp.int32, (channels, channels), 1) // width
    return jnp.where(lane_row == lane_col, 1.0, 0.0).astype(BF16)


def head_sums(values, same_head):
    high = values.astype(BF16)
    low = (values - high.astype(F32)).astype(BF16)
    return dot_nn(high, same_head) + dot_nn(low, same_head)


def rounded_sums(values, same_head):
    return dot_nn(values.astype(BF16), same_head)


def head_units(raw, same_head, sums=head_sums):
    raw = raw.astype(F32)
    mean_sq = sums(raw * raw, same_head) * (HEAD_COUNT / raw.shape[-1])
    inverse = lax.rsqrt(jnp.maximum(mean_sq, FLOOR))
    return raw, mean_sq, inverse, (raw * inverse).astype(BF16)


def row_rsqrt(values):
    return lax.rsqrt(jnp.mean(values * values, axis=-1, keepdims=True) + EPSILON)


def split_rows(array, count):
    size = array.shape[0] // count
    return [array[i * size : (i + 1) * size] for i in range(count)]


def softmax_members(queries, keys, same_head, scale):
    products = [query * key for query in queries for key in keys]
    scores = dot_nn(jnp.concatenate(products, axis=0), same_head) * scale
    exps = split_rows(jnp.exp(scores), len(products))
    soft = []
    for m in range(len(queries)):
        mine = exps[m * len(keys) : (m + 1) * len(keys)]
        total = mine[0]
        for e in mine[1:]:
            total = total + e
        inverse = 1.0 / total
        soft.append([e * inverse for e in mine])
    return soft


def mix_values(probs, values):
    mixed = None
    for prob, value in zip(probs, values):
        term = prob.astype(BF16).astype(F32) * value.astype(F32)
        mixed = term if mixed is None else mixed + term
    return mixed.astype(BF16)


def forward_cells(x, mem, groups, gain, project_ref, output_ref, same_head):
    channels = x.shape[-1]
    own_rows = x.shape[0] // groups * mem
    scale = 1.0 / math.sqrt(channels // HEAD_COUNT)
    normed = (x * row_rsqrt(x) * gain).astype(BF16)
    query_raw = dot_nn(normed[:own_rows], project_ref[:, :channels]).astype(BF16)
    key_raw = dot_nn(normed, project_ref[:, channels : 2 * channels]).astype(BF16)
    values = dot_nn(normed, project_ref[:, 2 * channels :]).astype(BF16)
    raw = jnp.concatenate([query_raw, key_raw], axis=0)
    units = head_units(raw, same_head, rounded_sums)[3]
    queries = split_rows(units[:own_rows], mem)
    keys = split_rows(units[own_rows:], groups)
    values = split_rows(values, groups)
    soft = softmax_members(queries, keys, same_head, scale)
    mixed = jnp.concatenate([mix_values(soft[m], values) for m in range(mem)], axis=0)
    return (x[:own_rows] + dot_nn(mixed, output_ref[...])).astype(BF16)


def shift_row(scr, member, place, slab, west, east):
    cols, channels = slab.shape
    column = lax.broadcasted_iota(jnp.int32, (cols, channels), 0)
    back = jnp.where(column == 0, west, pltpu.roll(slab, 1, 0))
    ahead = jnp.where(column == cols - 1, east, pltpu.roll(slab, cols - 1, 0))
    rows_at = slice(place * cols, (place + 1) * cols)
    scr[member, rows_at, :channels] = back.astype(BF16)
    scr[member, rows_at, channels : 2 * channels] = slab.astype(BF16)
    scr[member, rows_at, 2 * channels :] = ahead.astype(BF16)


def tap_rows(taps_ref, r):
    size = taps_ref.shape[0] // 3
    return taps_ref[r * size : (r + 1) * size, :]


def own_kernel(
    both_ref,
    other_ref,
    gain_ref,
    project_ref,
    output_ref,
    after_ref,
    proj_ref,
    unit_ref,
    soft_ref,
    inverse_ref,
    pull_ref,
    updated_ref,
):
    _, mem, rows, cols, channels = both_ref.shape
    groups = 2 * mem
    cells = rows * cols
    width = channels // HEAD_COUNT
    scale = 1.0 / math.sqrt(width)
    same_head = same_head_matrix(channels)
    own = both_ref[0].reshape(mem * cells, channels)
    other = other_ref[0].reshape(mem * cells, channels)
    x = jnp.concatenate([own, other], axis=0).astype(F32)
    normed = (x * row_rsqrt(x) * gain_ref[...]).astype(BF16)
    proj = dot_nn(normed, project_ref[...]).astype(BF16)
    proj_ref[...] = proj.reshape(groups, cells, 3 * channels)
    both_raw = jnp.concatenate([proj[:, :channels], proj[:, channels : 2 * channels]], axis=0)
    raw, mean_sq, inverse, units = head_units(both_raw, same_head)
    unit_ref[...] = units.reshape(2, groups, cells, channels)
    active = jnp.where(mean_sq > FLOOR, 1.0, jnp.where(mean_sq == FLOOR, 0.5, 0.0))
    pull = active * raw * (inverse * inverse * inverse) / width
    for kind in range(2):
        at = kind * groups * cells
        mine = slice(at, at + mem * cells)
        inverse_ref[kind] = inverse[mine].reshape(mem, cells, channels)
        pull_ref[kind] = pull[mine].reshape(mem, cells, channels)
    units = split_rows(units, 2 * groups)
    soft = softmax_members(units[:groups], units[groups:], same_head, scale)
    for m in range(groups):
        for n in range(groups):
            soft_ref[m * groups + n] = soft[m][n]
    values = split_rows(proj[:, 2 * channels :], groups)
    mixed = jnp.concatenate([mix_values(soft[m], values) for m in range(mem)], axis=0)
    updated = x[: mem * cells] + dot_nn(mixed, output_ref[...])
    updated_ref[...] = updated.astype(BF16).reshape(mem, cells, channels)


def backward_cells(
    pick, grad_field, x, gain, weights_t, proj_ref, unit_ref, soft_ref, inverse_ref, pull_ref
):
    project_t_ref, output_t_ref = weights_t
    groups = proj_ref.shape[0]
    mem = inverse_ref.shape[1]
    channels = x.shape[-1]
    scale = 1.0 / math.sqrt(channels // HEAD_COUNT)
    same_head = same_head_matrix(channels)
    grad_mixed = dot_nn(grad_field.astype(BF16), output_t_ref[...]).astype(BF16)
    grads = split_rows(grad_mixed, groups)
    values = [pick(proj_ref[n, :, 2 * channels :]) for n in range(groups)]
    products = [grads[m] * values[n] for m in range(groups) for n in range(groups)]
    dprobs = split_rows(dot_nn(jnp.concatenate(products, axis=0), same_head), len(products))
    units = [[pick(unit_ref[k, n]).astype(F32) for n in range(groups)] for k in range(2)]
    query_grad = [None] * mem
    key_grad = [None] * mem
    value_grad = [None] * mem
    for m in range(groups):
        soft = [pick(soft_ref[m * groups + n]) for n in range(groups)]
        dprob = dprobs[m * groups : (m + 1) * groups]
        mean = soft[0] * dprob[0]
        for n in range(1, groups):
            mean = mean + soft[n] * dprob[n]
        for n in range(groups):
            if m >= mem and n >= mem:
                continue
            dscore = soft[n] * (dprob[n] - mean)
            if m < mem:
                term = dscore * units[1][n]
                query_grad[m] = term if query_grad[m] is None else query_grad[m] + term
            if n < mem:
                term = dscore * units[0][m]
                key_grad[n] = term if key_grad[n] is None else key_grad[n] + term
                term = soft[n] * grads[m].astype(F32)
                value_grad[n] = term if value_grad[n] is None else value_grad[n] + term

    unit_grads = [jnp.concatenate(g, axis=0) * scale for g in (query_grad, key_grad)]

    def members(take):
        return jnp.concatenate([pick(take(m)) for m in range(mem)], axis=0)

    raws = []
    for kind in range(2):
        lanes = slice(kind * channels, (kind + 1) * channels)
        raws.append(members(lambda m: proj_ref[m, :, lanes]).astype(F32))
    inner = rounded_sums(
        jnp.concatenate([g * raw for g, raw in zip(unit_grads, raws)], axis=0), same_head
    )
    inner = split_rows(inner, 2)
    pulled = []
    for kind in range(2):
        inverse = members(lambda m: inverse_ref[kind, m])
        pull = members(lambda m: pull_ref[kind, m])
        pulled.append((inverse * unit_grads[kind] - pull * inner[kind]).astype(BF16))
    pulled.append(jnp.concatenate(value_grad, axis=0).astype(BF16))
    grad_normed = dot_nn(jnp.concatenate(pulled, axis=1), project_t_ref[...]) * gain
    inverse = row_rsqrt(x)
    inner = jnp.mean(x * grad_normed, axis=-1, keepdims=True)
    total = grad_field[: x.shape[0]] + inverse * grad_normed
    return (total - x * (inverse * inverse * inverse * inner)).astype(BF16)


def centre_kernel(
    both_ref,
    other_ref,
    chip_ref,
    core_ref,
    gain_ref,
    project_ref,
    output_ref,
    conv_ref,
    project_t_ref,
    output_t_ref,
    proj_ref,
    unit_ref,
    soft_ref,
    inverse_ref,
    pull_ref,
    updated_ref,
    conv_t_ref,
    result_ref,
    grad_ref,
    result_part_ref,
    grad_part_ref,
    shift_scr,
    cot_shift_scr,
    strip_scr,
):
    _, mem, rows, cols, channels = both_ref.shape
    groups = 2 * mem
    cells = rows * cols
    gain = gain_ref[...]
    same_head = same_head_matrix(channels)
    west, east = rim_columns(chip_ref, core_ref)
    for r in range(3):
        for c in range(3):
            tap = (3 * r + c) * channels
            turned = (3 * r + 2 - c) * channels
            conv_t_ref[turned : turned + channels, :] = conv_ref[tap : tap + channels, :].T

    def convolve(scr, count, start, taps_ref, turned):
        sums = [
            [start[(m * rows + a) * cols : (m * rows + a + 1) * cols] for a in range(rows)]
            for m in range(count)
        ]
        for r in range(3):
            step = 1 - r if turned else r - 1
            outs = [a for a in range(rows) if 0 <= a + step < rows]
            begin, end = outs[0] + step, outs[-1] + step + 1
            window = jnp.concatenate(
                [scr[m, begin * cols : end * cols, :] for m in range(count)], axis=0
            )
            terms = split_rows(dot_nn(window, tap_rows(taps_ref, r)), count * len(outs))
            for m in range(count):
                for i, a in enumerate(outs):
                    sums[m][a] = sums[m][a] + terms[m * len(outs) + i]
        return sums

    cots = []
    for member in range(groups):
        for row in range(rows):
            ref, who = (both_ref, member) if member < mem else (other_ref, member - mem)
            slab = ref[1, who, row].astype(F32)
            cots.append(slab)
            at = (groups + member) * rows + row
            shift_row(cot_shift_scr, member, row, slab, west[at : at + 1], east[at : at + 1])
    sums = convolve(cot_shift_scr, groups, jnp.concatenate(cots, axis=0), conv_t_ref, True)
    for member in range(groups):
        grad_part_ref[member, :cols, :] = sums[member][0]
        grad_part_ref[member, cols:, :] = sums[member][rows - 1]
    grad_field = jnp.concatenate([slab for s in sums for slab in s[1 : rows - 1]], axis=0)

    for member in range(groups):
        at = member * rows
        strip_scr[member] = jnp.zeros((16, channels), F32)
        strip_scr[member, :rows, :] = west[at : at + rows]
        strip_scr[member, 8 : 8 + rows, :] = east[at : at + rows]
    x = strip_scr[...].reshape(groups * 16, channels)
    fresh = forward_cells(x, mem, groups, gain, project_ref, output_ref, same_head)
    fresh = split_rows(fresh.astype(F32), mem)

    pick = lambda array: array[cols : cells - cols]
    x = both_ref[0, :, 1 : rows - 1].reshape(mem * (cells - 2 * cols), channels).astype(F32)
    total = backward_cells(
        pick,
        grad_field,
        x,
        gain,
        (project_t_ref, output_t_ref),
        proj_ref,
        unit_ref,
        soft_ref,
        inverse_ref,
        pull_ref,
    )
    grad_ref[...] = total.reshape(mem, rows - 2, cols, channels)

    for member in range(mem):
        for row in range(rows):
            slab = updated_ref[member, row * cols : (row + 1) * cols, :].astype(F32)
            ends = fresh[member][row : row + 1], fresh[member][8 + row : 9 + row]
            shift_row(shift_scr, member, row, slab, *ends)
    start = updated_ref[...].reshape(mem * cells, channels).astype(F32)
    sums = convolve(shift_scr, mem, start, conv_ref, False)
    for member in range(mem):
        result_part_ref[member, :cols, :] = sums[member][0]
        result_part_ref[member, cols:, :] = sums[member][rows - 1]
        for row in range(1, rows - 1):
            result_ref[member, row - 1] = sums[member][row].astype(BF16)


def main_kernel(
    both_ref,
    second_ref,
    first_ref,
    gain_ref,
    project_ref,
    output_ref,
    conv_ref,
    project_t_ref,
    output_t_ref,
    conv_t_ref,
    proj_ref,
    unit_ref,
    soft_ref,
    inverse_ref,
    pull_ref,
    inner_result_ref,
    inner_grad_ref,
    result_part_ref,
    grad_part_ref,
    result_ref,
    grad_ref,
    shift_scr,
    cot_shift_scr,
    corner_scr,
    *,
    lat_count,
):
    _, mem, rows, cols, channels = both_ref.shape
    groups = 2 * mem
    slots = 2 * groups
    cells = rows * cols
    gain = gain_ref[...]
    same_head = same_head_matrix(channels)
    lat_even = is_even("lat")
    lat = lax.axis_index("lat")

    def halos(at):
        first, second = first_ref[at, :].astype(F32), second_ref[at, :].astype(F32)
        north = jnp.where(lat == 0, 0.0, jnp.where(lat_even, second, first))
        south = jnp.where(lat == lat_count - 1, 0.0, jnp.where(lat_even, first, second))
        return north, south

    halo = [halos(slice(slot * cols, (slot + 1) * cols)) for slot in range(slots)]
    corners = halos(slice(slots * cols, slots * cols + 2 * slots))

    def corner(side, slot, end):
        at = end * slots + slot
        return corners[side][at : at + 1]

    def halo_part(scr, count, taps_ref, turned):
        north, south = (2, 0) if turned else (0, 2)
        parts = []
        for side, r in ((0, north), (1, south)):
            window = jnp.concatenate(
                [scr[m, side * cols : (side + 1) * cols, :] for m in range(count)], axis=0
            )
            parts.append(split_rows(dot_nn(window, tap_rows(taps_ref, r)), count))
        return jnp.concatenate([parts[side][m] for m in range(count) for side in (0, 1)], axis=0)

    for member in range(groups):
        slot = groups + member
        for side in (0, 1):
            ends = corner(side, slot, 0), corner(side, slot, 1)
            shift_row(cot_shift_scr, member, side, halo[slot][side], *ends)
    grad_field = grad_part_ref[...].reshape(groups * 2 * cols, channels)
    grad_field = grad_field + halo_part(cot_shift_scr, groups, conv_t_ref, True)

    blocks = []
    for member in range(groups):
        corner_scr[member] = jnp.zeros((16, channels), F32)
        for side in (0, 1):
            for end in (0, 1):
                at = 2 * side + end
                corner_scr[member, at : at + 1, :] = corner(side, member, end)
        blocks += [halo[member][0], halo[member][1], corner_scr[member]]
    x = jnp.concatenate(blocks, axis=0)
    fresh = forward_cells(x, mem, groups, gain, project_ref, output_ref, same_head)
    fresh = split_rows(fresh.astype(F32), mem)

    pick = lambda array: jnp.concatenate([array[:cols], array[cells - cols :]], axis=0)
    x = [both_ref[0, m, row] for m in range(mem) for row in (0, rows - 1)]
    total = backward_cells(
        pick,
        grad_field,
        jnp.concatenate(x, axis=0).astype(F32),
        gain,
        (project_t_ref, output_t_ref),
        proj_ref,
        unit_ref,
        soft_ref,
        inverse_ref,
        pull_ref,
    )

    for member in range(mem):
        for side in (0, 1):
            slab = fresh[member][side * cols : (side + 1) * cols]
            at = 2 * cols + 2 * side
            ends = fresh[member][at : at + 1], fresh[member][at + 1 : at + 2]
            shift_row(shift_scr, member, side, slab, *ends)
    outer = result_part_ref[...].reshape(mem * 2 * cols, channels)
    outer = (outer + halo_part(shift_scr, mem, conv_ref, False)).astype(BF16)
    outputs = (
        (result_ref, inner_result_ref, split_rows(outer, 2 * mem)),
        (grad_ref, inner_grad_ref, split_rows(total, 2 * mem)),
    )
    for out_ref, inner_ref, edge in outputs:
        for member in range(mem):
            out_ref[member, 0] = edge[2 * member]
            out_ref[member, rows - 1] = edge[2 * member + 1]
            for row in range(1, rows - 1):
                out_ref[member, row] = inner_ref[member, row - 1]


def local_call(kernel, name, operands, out_shape, scratch, pinned=False, cost=None):
    whole = pl.BlockSpec(memory_space=pltpu.VMEM)
    anywhere = pl.BlockSpec(memory_space=pl.ANY)
    specs = [anywhere if in_hbm else whole for _, in_hbm in operands]
    arrays = [
        pltpu.with_memory_space_constraint(array, pltpu.HBM) if in_hbm else array
        for array, in_hbm in operands
    ]

    def keep(shape):
        return pltpu.VMEM(shape.shape, shape.dtype) if pinned else shape

    return pl.pallas_call(
        kernel,
        out_shape=jax.tree.map(keep, out_shape),
        in_specs=specs,
        out_specs=jax.tree.map(lambda _: whole, out_shape),
        scratch_shapes=scratch,
        compiler_params=pltpu.CompilerParams(vmem_limit_bytes=VMEM_LIMIT),
        cost_estimate=cost,
        name=name,
    )(*arrays)


def here(*arrays):
    return [(array, False) for array in arrays]


def in_hbm(*arrays):
    return [(array, True) for array in arrays]


def per_device_paired(ensemble, norm_gain, project_weight, output_weight, conv_kernel, cotangent):
    mem, rows, cols, channels = ensemble.shape
    if rows < 3 or cols % 16 or (2 * mem * rows) % 16:
        return per_device_general(
            ensemble, norm_gain, project_weight, output_weight, conv_kernel, cotangent
        )
    groups = 2 * mem
    slots = 2 * groups
    cells = rows * cols
    lon_count = lax.axis_size("lon")
    lat_count = lax.axis_size("lat")
    bf16 = functools.partial(jax.ShapeDtypeStruct, dtype=BF16)
    f32 = functools.partial(jax.ShapeDtypeStruct, dtype=F32)
    swap = [(0, 1), (1, 0)]
    core_pairs = [(i, i ^ 1) for i in range(lon_count)]
    chip_pairs = [(i, (i - 1 if i % 2 == 0 else i + 1) % lon_count) for i in range(lon_count)]

    def lat_swap(offset):
        pairs = []
        for lat in range(lat_count):
            for lon in range(lon_count):
                to = (lat + 1 if lat % 2 == offset else lat - 1, lon)
                if not 0 <= to[0] < lat_count:
                    to = (lat, lon ^ 1)
                pairs.append((lat * lon_count + lon, to[0] * lon_count + to[1]))
        return pairs

    ends_shape = (2, 2 * mem * rows, channels)
    both, ends = local_call(
        stack_kernel,
        "stack",
        in_hbm(ensemble, cotangent),
        (bf16((2,) + ensemble.shape), bf16(ends_shape)),
        [pltpu.VMEM(ends_shape[1:], F32)] * 2 + [pltpu.SemaphoreType.DMA((2,))],
        pinned=True,
    )
    other_ends = lax.ppermute(ends, "member", swap)
    other = lax.ppermute(both, "member", swap)

    strip = (slots * rows, channels)
    chip_send, core_send = local_call(
        pack_strips_kernel,
        "pack_strips",
        here(ends, other_ends),
        (bf16(strip), bf16(strip)),
        [pltpu.VMEM(strip, F32)] * 2,
    )
    chip = lax.ppermute(chip_send, "lon", chip_pairs)
    core = lax.ppermute(core_send, "lon", core_pairs)

    weights = (
        norm_gain.reshape(1, channels),
        project_weight,
        output_weight,
        conv_kernel.reshape(9 * channels, channels),
    )
    *weights, project_t, output_t = local_call(
        load_kernel,
        "load_weights",
        in_hbm(*weights),
        tuple(jax.ShapeDtypeStruct(w.shape, w.dtype) for w in weights)
        + (bf16((3 * channels, channels)), bf16((channels, channels))),
        [pltpu.SemaphoreType.DMA((4,))],
        pinned=True,
        cost=MIDDLING,
    )
    halo = bf16((slots * (cols + 2), channels))
    first_send, second_send = local_call(
        pack_rows_kernel,
        "pack_rows",
        here(both, other, chip, core, weights[0]),
        (halo, halo),
        [pltpu.VMEM((2, 2 * slots, channels), F32)],
    )
    first = lax.ppermute(first_send, ("lat", "lon"), lat_swap(0))
    second = lax.ppermute(second_send, ("lat", "lon"), lat_swap(1))

    *held, updated = local_call(
        own_kernel,
        "own_cells",
        here(both, other, *weights[:3], second_send),
        (
            bf16((groups, cells, 3 * channels)),
            bf16((2, groups, cells, channels)),
            f32((groups * groups, cells, channels)),
            f32((2, mem, cells, channels)),
            f32((2, mem, cells, channels)),
            bf16((mem, cells, channels)),
        ),
        [],
        pinned=True,
        cost=LONG,
    )
    conv_t, *parts = local_call(
        centre_kernel,
        "centre",
        here(both, other, chip, core, *weights, project_t, output_t, *held, updated),
        (
            bf16((9 * channels, channels)),
            bf16((mem, rows - 2, cols, channels)),
            bf16((mem, rows - 2, cols, channels)),
            f32((mem, 2 * cols, channels)),
            f32((groups, 2 * cols, channels)),
        ),
        [
            pltpu.VMEM((mem, cells, 3 * channels), BF16),
            pltpu.VMEM((groups, cells, 3 * channels), BF16),
            pltpu.VMEM((groups, 16, channels), F32),
        ],
        pinned=True,
        cost=LONG,
    )
    return local_call(
        functools.partial(main_kernel, lat_count=lat_count),
        "main",
        here(both, second, first, *weights, project_t, output_t, conv_t, *held, *parts),
        (bf16(ensemble.shape), bf16(ensemble.shape)),
        [
            pltpu.VMEM((mem, 2 * cols, 3 * channels), BF16),
            pltpu.VMEM((groups, 2 * cols, 3 * channels), BF16),
            pltpu.VMEM((groups, 16, channels), F32),
        ],
    )


def solution(mesh):
    paired = mesh.shape["member"] == 2 and mesh.shape["lon"] % 2 == 0
    per_device = per_device_paired if paired else per_device_general
    in_specs = (
        P("member", "lat", "lon", None),
        P(),
        P(),
        P(),
        P(),
        P("member", "lat", "lon", None),
    )
    out_specs = (P("member", "lat", "lon", None), P("member", "lat", "lon", None))
    return jax.shard_map(
        per_device, mesh=mesh, in_specs=in_specs, out_specs=out_specs, check_vma=False
    )
```

```python
import functools
import math

import jax
import jax.numpy as jnp
from jax import lax
from jax.experimental import pallas as pl
from jax.experimental.pallas import tpu as pltpu
from jax.sharding import PartitionSpec as P

HEAD_COUNT = 8


FLOOR = 0.5
EPSILON = 1e-06


def padded_2(block, sides, width, periodic):
    for axis, dim in sides:
        count = lax.axis_size(axis)
        forward = [(i, i + 1) for i in range(count - 1)]
        if periodic:
            forward.append((count - 1, 0))
        backward = [(target, source) for source, target in forward]
        low = lax.ppermute(
            lax.slice_in_dim(block, block.shape[dim] - width, None, axis=dim), axis, forward
        )
        high = lax.ppermute(lax.slice_in_dim(block, 0, width, axis=dim), axis, backward)
        block = jnp.concatenate([low, block, high], axis=dim)
    return block


def row_norm(values, gain_vec):
    mean_sq = jnp.mean(values * values, axis=-1, keepdims=True)
    return values * lax.rsqrt(mean_sq + EPSILON) * gain_vec


def head_norm(values, head_count):
    shaped = values.reshape(values.shape[:-1] + (head_count, values.shape[-1] // head_count))
    mean_sq = jnp.mean(shaped * shaped, axis=-1, keepdims=True)
    return (shaped * lax.rsqrt(jnp.maximum(mean_sq, FLOOR))).reshape(values.shape)


def split_heads(values, head_count):
    return values.reshape(values.shape[:-1] + (head_count, values.shape[-1] // head_count))


def head_pullback(raw_rows, grad_rows):
    _, pullback = jax.vjp(lambda t: head_norm(t, HEAD_COUNT), raw_rows.astype(jnp.float32))
    return pullback(grad_rows)[0]


def pad_field(field_in):
    widened = padded_2(field_in, (("lon", 2),), 1, True)
    return padded_2(widened, (("lat", 1),), 1, False)


def conv_taps(padded, kernel, lat_n, lon_n, adjoint):
    running = None
    for row_off in range(3):
        for col_off in range(3):
            if adjoint:
                window = padded[
                    :, 2 - row_off : 2 - row_off + lat_n, 2 - col_off : 2 - col_off + lon_n
                ]
                summand = jnp.einsum(
                    "mabc,dc->mabd",
                    window,
                    kernel[row_off, col_off],
                    preferred_element_type=jnp.float32,
                )
            else:
                window = padded[:, row_off : row_off + lat_n, col_off : col_off + lon_n]
                summand = jnp.einsum(
                    "mabc,cd->mabd",
                    window,
                    kernel[row_off, col_off],
                    preferred_element_type=jnp.float32,
                )
            running = summand if running is None else running + summand
    return running


def per_device_general(ensemble, norm_gain, project_weight, output_weight, conv_kernel, cotangent):
    mem_dev, lat_dev, lon_dev, channels = ensemble.shape
    cell_count = lat_dev * lon_dev
    score_scale = 1.0 / math.sqrt(channels // HEAD_COUNT)
    inputs = ensemble.reshape(mem_dev, cell_count, channels).astype(jnp.float32)
    normed = row_norm(inputs, norm_gain).astype(jnp.bfloat16)
    spread = lax.all_to_all(normed, "member", split_axis=1, concat_axis=0, tiled=True)
    projected = jnp.dot(spread, project_weight, preferred_element_type=jnp.float32).astype(
        jnp.bfloat16
    )
    query_raw = projected[..., :channels]
    key_raw = projected[..., channels : 2 * channels]
    value_rows = projected[..., 2 * channels :]
    key_rows = head_norm(key_raw.astype(jnp.float32), HEAD_COUNT).astype(jnp.bfloat16)
    queries = head_norm(query_raw.astype(jnp.float32), HEAD_COUNT).astype(jnp.bfloat16)
    query_heads = split_heads(queries, HEAD_COUNT)
    key_heads = split_heads(key_rows, HEAD_COUNT)
    value_heads = split_heads(value_rows, HEAD_COUNT)
    scores = (
        jnp.einsum("mphd,nphd->mnhp", query_heads, key_heads, preferred_element_type=jnp.float32)
        * score_scale
    )
    expd = jnp.exp(scores)
    soft = expd / jnp.sum(expd, axis=1, keepdims=True)
    rounded = soft.astype(jnp.bfloat16)
    mixed_out = jnp.einsum(
        "mnhp,nphd->mphd", rounded, value_heads, preferred_element_type=jnp.float32
    )
    mixed_out = mixed_out.reshape(query_raw.shape).astype(jnp.bfloat16)
    mixed_out = lax.all_to_all(mixed_out, "member", split_axis=0, concat_axis=1, tiled=True)
    updated = (
        inputs + jnp.dot(mixed_out, output_weight, preferred_element_type=jnp.float32)
    ).astype(jnp.bfloat16)
    field_up = updated.reshape(mem_dev, lat_dev, lon_dev, channels)
    result = field_up.astype(jnp.float32) + conv_taps(
        pad_field(field_up), conv_kernel, lat_dev, lon_dev, False
    )
    result = result.astype(jnp.bfloat16)
    grad_field = cotangent.astype(jnp.float32) + conv_taps(
        pad_field(cotangent), conv_kernel, lat_dev, lon_dev, True
    )
    grad_rows = grad_field.reshape(mem_dev, cell_count, channels)
    grad_mixed = jnp.einsum(
        "mpc,dc->mpd",
        grad_rows.astype(jnp.bfloat16),
        output_weight,
        preferred_element_type=jnp.float32,
    )
    grad_mixed = grad_mixed.astype(jnp.bfloat16)
    grad_mixed = lax.all_to_all(grad_mixed, "member", split_axis=1, concat_axis=0, tiled=True)
    grad_heads = split_heads(grad_mixed, HEAD_COUNT)
    dprob = jnp.einsum(
        "mphd,nphd->mnhp", grad_heads, value_heads, preferred_element_type=jnp.float32
    )
    dscore = (soft * (dprob - jnp.sum(soft * dprob, axis=1, keepdims=True))).astype(jnp.bfloat16)
    query_grad = (
        jnp.einsum("mnhp,nphd->mphd", dscore, key_heads, preferred_element_type=jnp.float32)
        * score_scale
    )
    query_grad = query_grad.reshape(query_raw.shape)
    key_grad = (
        jnp.einsum("mnhp,mphd->nphd", dscore, query_heads, preferred_element_type=jnp.float32)
        * score_scale
    )
    key_grad = key_grad.reshape(key_raw.shape)
    value_grad = jnp.einsum(
        "mnhp,mphd->nphd", rounded, grad_heads, preferred_element_type=jnp.float32
    )
    value_grad = value_grad.reshape(key_raw.shape)
    grad_query_raw = head_pullback(query_raw, query_grad)
    grad_key_raw = head_pullback(key_raw, key_grad)
    grad_proj = jnp.concatenate([grad_query_raw, grad_key_raw, value_grad], axis=-1).astype(
        jnp.bfloat16
    )
    grad_proj = lax.all_to_all(grad_proj, "member", split_axis=0, concat_axis=1, tiled=True)
    grad_normed = jnp.einsum(
        "mpe,ce->mpc", grad_proj, project_weight, preferred_element_type=jnp.float32
    )
    _, pull_norm = jax.vjp(lambda t: row_norm(t, norm_gain), inputs)
    grad_inputs = pull_norm(grad_normed)[0]
    grad_ensemble = (
        (grad_rows + grad_inputs).astype(jnp.bfloat16).reshape(mem_dev, lat_dev, lon_dev, channels)
    )
    return (result, grad_ensemble)


F32 = jnp.float32
BF16 = jnp.bfloat16
VMEM_LIMIT = 24 * 1024 * 1024
LONG = pl.CostEstimate(flops=20_000_000_000, bytes_accessed=4_000_000, transcendentals=0)
MIDDLING = pl.CostEstimate(flops=3_000_000_000, bytes_accessed=2_000_000, transcendentals=0)


def is_even(axis):
    return lax.rem(lax.axis_index(axis), 2) == 0


def load_kernel(
    gain_hbm,
    project_hbm,
    output_hbm,
    conv_hbm,
    gain_ref,
    project_ref,
    output_ref,
    conv_ref,
    project_t_ref,
    output_t_ref,
    sems,
):
    channels = output_ref.shape[0]
    pairs = (
        (gain_hbm, gain_ref),
        (project_hbm, project_ref),
        (output_hbm, output_ref),
        (conv_hbm, conv_ref),
    )
    loads = [
        pltpu.make_async_copy(source, target, sems.at[i])
        for i, (source, target) in enumerate(pairs)
    ]
    for load in loads:
        load.start()
    for load in loads[:3]:
        load.wait()
    output_t_ref[...] = output_ref[...].T
    for kind in range(3):
        lanes = slice(kind * channels, (kind + 1) * channels)
        project_t_ref[lanes, :] = project_ref[:, lanes].T
    loads[3].wait()


def stack_kernel(ens_ref, cot_ref, both_ref, ends_ref, low_scr, high_scr, sems):
    _, mem, rows, cols, _ = both_ref.shape
    copies = [
        pltpu.make_async_copy(ref, both_ref.at[i], sems.at[i])
        for i, ref in enumerate((ens_ref, cot_ref))
    ]
    for copy in copies:
        copy.start()
    for copy in copies:
        copy.wait()
    index = 0
    for array in range(2):
        for member in range(mem):
            for row in range(rows):
                slab = both_ref[array, member, row].astype(F32)
                low_scr[index : index + 1, :] = slab[0:1]
                high_scr[index : index + 1, :] = slab[cols - 1 : cols]
                index += 1
    ends_ref[0] = low_scr[...].astype(BF16)
    ends_ref[1] = high_scr[...].astype(BF16)


def pack_strips_kernel(ends_ref, other_ends_ref, chip_ref, core_ref, low_scr, high_scr):
    part = ends_ref.shape[1] // 2
    for side, scr in ((0, low_scr), (1, high_scr)):
        for group, ref in enumerate((ends_ref, other_ends_ref)):
            column = ref[side].astype(F32)
            for array in range(2):
                at = (2 * array + group) * part
                scr[at : at + part, :] = column[array * part : (array + 1) * part]
    even = is_even("lon")
    low, high = low_scr[...], high_scr[...]
    core_ref[...] = jnp.where(even, high, low).astype(BF16)
    chip_ref[...] = jnp.where(even, low, high).astype(BF16)


def rim_columns(chip_ref, core_ref):
    even = is_even("lon")
    chip, core = chip_ref[...].astype(F32), core_ref[...].astype(F32)
    return jnp.where(even, chip, core), jnp.where(even, core, chip)


def pack_rows_kernel(
    both_ref, other_ref, chip_ref, core_ref, after_ref, first_ref, second_ref, edge_scr
):
    _, mem, rows, cols, _ = both_ref.shape
    slots = 4 * mem
    even = is_even("lat")
    west, east = rim_columns(chip_ref, core_ref)
    for slot in range(slots):
        array, member = divmod(slot, 2 * mem)
        ref, who = (both_ref, member) if member < mem else (other_ref, member - mem)
        start, stop = (ref[array, who, row].astype(F32) for row in (0, rows - 1))
        at = slice(slot * cols, (slot + 1) * cols)
        first_ref[at, :] = jnp.where(even, stop, start).astype(BF16)
        second_ref[at, :] = jnp.where(even, start, stop).astype(BF16)
        top, low = slot * rows, (slot + 1) * rows - 1
        for side, column in enumerate((west, east)):
            place = side * slots + slot
            start, stop = column[top : top + 1], column[low : low + 1]
            edge_scr[0, place : place + 1, :] = jnp.where(even, stop, start)
            edge_scr[1, place : place + 1, :] = jnp.where(even, start, stop)
    first_ref[slots * cols :, :] = edge_scr[0].astype(BF16)
    second_ref[slots * cols :, :] = edge_scr[1].astype(BF16)


def dot_nn(a, b):
    return lax.dot_general(a, b, (((1,), (0,)), ((), ())), preferred_element_type=F32)


def same_head_matrix(channels):
    width = channels // HEAD_COUNT
    lane_row = lax.broadcasted_iota(jnp.int32, (channels, channels), 0) // width
    lane_col = lax.broadcasted_iota(jnp.int32, (channels, channels), 1) // width
    return jnp.where(lane_row == lane_col, 1.0, 0.0).astype(BF16)


def head_sums(values, same_head):
    high = values.astype(BF16)
    low = (values - high.astype(F32)).astype(BF16)
    return dot_nn(high, same_head) + dot_nn(low, same_head)


def rounded_sums(values, same_head):
    return dot_nn(values.astype(BF16), same_head)


def head_units(raw, same_head, sums=head_sums):
    raw = raw.astype(F32)
    mean_sq = sums(raw * raw, same_head) * (HEAD_COUNT / raw.shape[-1])
    inverse = lax.rsqrt(jnp.maximum(mean_sq, FLOOR))
    return raw, mean_sq, inverse, (raw * inverse).astype(BF16)


def row_rsqrt(values):
    return lax.rsqrt(jnp.mean(values * values, axis=-1, keepdims=True) + EPSILON)


def split_rows(array, count):
    size = array.shape[0] // count
    return [array[i * size : (i + 1) * size] for i in range(count)]


def softmax_members(queries, keys, same_head, scale):
    products = [query * key for query in queries for key in keys]
    scores = dot_nn(jnp.concatenate(products, axis=0), same_head) * scale
    exps = split_rows(jnp.exp(scores), len(products))
    soft = []
    for m in range(len(queries)):
        mine = exps[m * len(keys) : (m + 1) * len(keys)]
        total = mine[0]
        for e in mine[1:]:
            total = total + e
        inverse = 1.0 / total
        soft.append([e * inverse for e in mine])
    return soft


def mix_values(probs, values):
    mixed = None
    for prob, value in zip(probs, values):
        term = prob.astype(BF16).astype(F32) * value.astype(F32)
        mixed = term if mixed is None else mixed + term
    return mixed.astype(BF16)


def forward_cells(x, mem, groups, gain, project_ref, output_ref, same_head):
    channels = x.shape[-1]
    own_rows = x.shape[0] // groups * mem
    scale = 1.0 / math.sqrt(channels // HEAD_COUNT)
    normed = (x * row_rsqrt(x) * gain).astype(BF16)
    query_raw = dot_nn(normed[:own_rows], project_ref[:, :channels]).astype(BF16)
    key_raw = dot_nn(normed, project_ref[:, channels : 2 * channels]).astype(BF16)
    values = dot_nn(normed, project_ref[:, 2 * channels :]).astype(BF16)
    yield
    raw = jnp.concatenate([query_raw, key_raw], axis=0)
    units = head_units(raw, same_head, rounded_sums)[3]
    yield
    queries = split_rows(units[:own_rows], mem)
    keys = split_rows(units[own_rows:], groups)
    values = split_rows(values, groups)
    soft = softmax_members(queries, keys, same_head, scale)
    yield
    mixed = jnp.concatenate([mix_values(soft[m], values) for m in range(mem)], axis=0)
    return (x[:own_rows] + dot_nn(mixed, output_ref[...])).astype(BF16)


def together(*chains):
    results = [None] * len(chains)
    active = list(range(len(chains)))
    while active:
        for i in list(active):
            try:
                next(chains[i])
            except StopIteration as stop:
                results[i] = stop.value
                active.remove(i)
    return results


def shift_row(scr, member, place, slab, west, east):
    cols, channels = slab.shape
    column = lax.broadcasted_iota(jnp.int32, (cols, channels), 0)
    back = jnp.where(column == 0, west, pltpu.roll(slab, 1, 0))
    ahead = jnp.where(column == cols - 1, east, pltpu.roll(slab, cols - 1, 0))
    rows_at = slice(place * cols, (place + 1) * cols)
    scr[member, rows_at, :channels] = back.astype(BF16)
    scr[member, rows_at, channels : 2 * channels] = slab.astype(BF16)
    scr[member, rows_at, 2 * channels :] = ahead.astype(BF16)


def tap_rows(taps_ref, r):
    size = taps_ref.shape[0] // 3
    return taps_ref[r * size : (r + 1) * size, :]


def own_kernel(
    both_ref,
    other_ref,
    gain_ref,
    project_ref,
    output_ref,
    after_ref,
    proj_ref,
    unit_ref,
    soft_ref,
    inverse_ref,
    pull_ref,
    updated_ref,
):
    _, mem, rows, cols, channels = both_ref.shape
    groups = 2 * mem
    cells = rows * cols
    width = channels // HEAD_COUNT
    scale = 1.0 / math.sqrt(width)
    same_head = same_head_matrix(channels)
    own = both_ref[0].reshape(mem * cells, channels)
    other = other_ref[0].reshape(mem * cells, channels)
    x = jnp.concatenate([own, other], axis=0).astype(F32)
    normed = (x * row_rsqrt(x) * gain_ref[...]).astype(BF16)
    proj = dot_nn(normed, project_ref[...]).astype(BF16)
    proj_ref[...] = proj.reshape(groups, cells, 3 * channels)
    both_raw = jnp.concatenate([proj[:, :channels], proj[:, channels : 2 * channels]], axis=0)
    raw, mean_sq, inverse, units = head_units(both_raw, same_head)
    unit_ref[...] = units.reshape(2, groups, cells, channels)
    active = jnp.where(mean_sq > FLOOR, 1.0, jnp.where(mean_sq == FLOOR, 0.5, 0.0))
    pull = active * raw * (inverse * inverse * inverse) / width
    for kind in range(2):
        at = kind * groups * cells
        mine = slice(at, at + mem * cells)
        inverse_ref[kind] = inverse[mine].reshape(mem, cells, channels)
        pull_ref[kind] = pull[mine].reshape(mem, cells, channels)
    units = split_rows(units, 2 * groups)
    soft = softmax_members(units[:groups], units[groups:], same_head, scale)
    for m in range(groups):
        for n in range(groups):
            soft_ref[m * groups + n] = soft[m][n]
    values = split_rows(proj[:, 2 * channels :], groups)
    mixed = jnp.concatenate([mix_values(soft[m], values) for m in range(mem)], axis=0)
    updated = x[: mem * cells] + dot_nn(mixed, output_ref[...])
    updated_ref[...] = updated.astype(BF16).reshape(mem, cells, channels)


def backward_cells(
    pick, grad_field, x, gain, weights_t, proj_ref, unit_ref, soft_ref, inverse_ref, pull_ref
):
    project_t_ref, output_t_ref = weights_t
    groups = proj_ref.shape[0]
    mem = inverse_ref.shape[1]
    channels = x.shape[-1]
    scale = 1.0 / math.sqrt(channels // HEAD_COUNT)
    same_head = same_head_matrix(channels)
    grad_mixed = dot_nn(grad_field.astype(BF16), output_t_ref[...]).astype(BF16)
    grads = split_rows(grad_mixed, groups)
    yield
    values = [pick(proj_ref[n, :, 2 * channels :]) for n in range(groups)]
    products = [grads[m] * values[n] for m in range(groups) for n in range(groups)]
    dprobs = split_rows(dot_nn(jnp.concatenate(products, axis=0), same_head), len(products))
    yield
    units = [[pick(unit_ref[k, n]).astype(F32) for n in range(groups)] for k in range(2)]
    query_grad = [None] * mem
    key_grad = [None] * mem
    value_grad = [None] * mem
    for m in range(groups):
        soft = [pick(soft_ref[m * groups + n]) for n in range(groups)]
        dprob = dprobs[m * groups : (m + 1) * groups]
        mean = soft[0] * dprob[0]
        for n in range(1, groups):
            mean = mean + soft[n] * dprob[n]
        for n in range(groups):
            if m >= mem and n >= mem:
                continue
            dscore = soft[n] * (dprob[n] - mean)
            if m < mem:
                term = dscore * units[1][n]
                query_grad[m] = term if query_grad[m] is None else query_grad[m] + term
            if n < mem:
                term = dscore * units[0][m]
                key_grad[n] = term if key_grad[n] is None else key_grad[n] + term
                term = soft[n] * grads[m].astype(F32)
                value_grad[n] = term if value_grad[n] is None else value_grad[n] + term

    unit_grads = [jnp.concatenate(g, axis=0) * scale for g in (query_grad, key_grad)]

    def members(take):
        return jnp.concatenate([pick(take(m)) for m in range(mem)], axis=0)

    raws = []
    for kind in range(2):
        lanes = slice(kind * channels, (kind + 1) * channels)
        raws.append(members(lambda m: proj_ref[m, :, lanes]).astype(F32))
    inner = rounded_sums(
        jnp.concatenate([g * raw for g, raw in zip(unit_grads, raws)], axis=0), same_head
    )
    inner = split_rows(inner, 2)
    yield
    pulled = []
    for kind in range(2):
        inverse = members(lambda m: inverse_ref[kind, m])
        pull = members(lambda m: pull_ref[kind, m])
        pulled.append((inverse * unit_grads[kind] - pull * inner[kind]).astype(BF16))
    pulled.append(jnp.concatenate(value_grad, axis=0).astype(BF16))
    grad_normed = dot_nn(jnp.concatenate(pulled, axis=1), project_t_ref[...]) * gain
    yield
    inverse = row_rsqrt(x)
    inner = jnp.mean(x * grad_normed, axis=-1, keepdims=True)
    total = grad_field[: x.shape[0]] + inverse * grad_normed
    return (total - x * (inverse * inverse * inverse * inner)).astype(BF16)


def centre_kernel(
    both_ref,
    other_ref,
    chip_ref,
    core_ref,
    gain_ref,
    project_ref,
    output_ref,
    conv_ref,
    project_t_ref,
    output_t_ref,
    proj_ref,
    unit_ref,
    soft_ref,
    inverse_ref,
    pull_ref,
    updated_ref,
    conv_t_ref,
    result_ref,
    grad_ref,
    result_part_ref,
    grad_part_ref,
    shift_scr,
    cot_shift_scr,
    strip_scr,
):
    _, mem, rows, cols, channels = both_ref.shape
    groups = 2 * mem
    cells = rows * cols
    gain = gain_ref[...]
    same_head = same_head_matrix(channels)
    west, east = rim_columns(chip_ref, core_ref)
    for r in range(3):
        for c in range(3):
            tap = (3 * r + c) * channels
            turned = (3 * r + 2 - c) * channels
            conv_t_ref[turned : turned + channels, :] = conv_ref[tap : tap + channels, :].T

    def convolve(scr, count, start, taps_ref, turned):
        sums = [
            [start[(m * rows + a) * cols : (m * rows + a + 1) * cols] for a in range(rows)]
            for m in range(count)
        ]
        for r in range(3):
            step = 1 - r if turned else r - 1
            outs = [a for a in range(rows) if 0 <= a + step < rows]
            begin, end = outs[0] + step, outs[-1] + step + 1
            window = jnp.concatenate(
                [scr[m, begin * cols : end * cols, :] for m in range(count)], axis=0
            )
            terms = split_rows(dot_nn(window, tap_rows(taps_ref, r)), count * len(outs))
            for m in range(count):
                for i, a in enumerate(outs):
                    sums[m][a] = sums[m][a] + terms[m * len(outs) + i]
        return sums

    cots = []
    for member in range(groups):
        for row in range(rows):
            ref, who = (both_ref, member) if member < mem else (other_ref, member - mem)
            slab = ref[1, who, row].astype(F32)
            cots.append(slab)
            at = (groups + member) * rows + row
            shift_row(cot_shift_scr, member, row, slab, west[at : at + 1], east[at : at + 1])
    sums = convolve(cot_shift_scr, groups, jnp.concatenate(cots, axis=0), conv_t_ref, True)
    for member in range(groups):
        grad_part_ref[member, :cols, :] = sums[member][0]
        grad_part_ref[member, cols:, :] = sums[member][rows - 1]
    grad_field = jnp.concatenate([slab for s in sums for slab in s[1 : rows - 1]], axis=0)

    for member in range(groups):
        at = member * rows
        strip_scr[member] = jnp.zeros((16, channels), F32)
        strip_scr[member, :rows, :] = west[at : at + rows]
        strip_scr[member, 8 : 8 + rows, :] = east[at : at + rows]
    x = strip_scr[...].reshape(groups * 16, channels)
    forward = forward_cells(x, mem, groups, gain, project_ref, output_ref, same_head)
    x = both_ref[0, :, 1 : rows - 1].reshape(mem * (cells - 2 * cols), channels).astype(F32)
    backward = backward_cells(
        lambda array: array[cols : cells - cols],
        grad_field,
        x,
        gain,
        (project_t_ref, output_t_ref),
        proj_ref,
        unit_ref,
        soft_ref,
        inverse_ref,
        pull_ref,
    )
    total, fresh = together(backward, forward)
    fresh = split_rows(fresh.astype(F32), mem)
    grad_ref[...] = total.reshape(mem, rows - 2, cols, channels)

    for member in range(mem):
        for row in range(rows):
            slab = updated_ref[member, row * cols : (row + 1) * cols, :].astype(F32)
            ends = fresh[member][row : row + 1], fresh[member][8 + row : 9 + row]
            shift_row(shift_scr, member, row, slab, *ends)
    start = updated_ref[...].reshape(mem * cells, channels).astype(F32)
    sums = convolve(shift_scr, mem, start, conv_ref, False)
    for member in range(mem):
        result_part_ref[member, :cols, :] = sums[member][0]
        result_part_ref[member, cols:, :] = sums[member][rows - 1]
        for row in range(1, rows - 1):
            result_ref[member, row - 1] = sums[member][row].astype(BF16)


def main_kernel(
    both_ref,
    second_ref,
    first_ref,
    gain_ref,
    project_ref,
    output_ref,
    conv_ref,
    project_t_ref,
    output_t_ref,
    conv_t_ref,
    proj_ref,
    unit_ref,
    soft_ref,
    inverse_ref,
    pull_ref,
    inner_result_ref,
    inner_grad_ref,
    result_part_ref,
    grad_part_ref,
    result_ref,
    grad_ref,
    shift_scr,
    cot_shift_scr,
    corner_scr,
    outer_scr,
    sems,
    *,
    lat_count,
):
    _, mem, rows, cols, channels = both_ref.shape
    copies = []
    for i, (ref, out_ref) in enumerate(
        ((inner_result_ref, result_ref), (inner_grad_ref, grad_ref))
    ):
        copy = pltpu.make_async_copy(ref, out_ref.at[:, pl.ds(1, rows - 2)], sems.at[i])
        copy.start()
        copies.append(copy)
    groups = 2 * mem
    slots = 2 * groups
    cells = rows * cols
    gain = gain_ref[...]
    same_head = same_head_matrix(channels)
    lat_even = is_even("lat")
    lat = lax.axis_index("lat")

    def halos(at):
        first, second = first_ref[at, :].astype(F32), second_ref[at, :].astype(F32)
        north = jnp.where(lat == 0, 0.0, jnp.where(lat_even, second, first))
        south = jnp.where(lat == lat_count - 1, 0.0, jnp.where(lat_even, first, second))
        return north, south

    halo = [halos(slice(slot * cols, (slot + 1) * cols)) for slot in range(slots)]
    corners = halos(slice(slots * cols, slots * cols + 2 * slots))

    def corner(side, slot, end):
        at = end * slots + slot
        return corners[side][at : at + 1]

    def halo_part(scr, count, taps_ref, turned):
        north, south = (2, 0) if turned else (0, 2)
        parts = []
        for side, r in ((0, north), (1, south)):
            window = jnp.concatenate(
                [scr[m, side * cols : (side + 1) * cols, :] for m in range(count)], axis=0
            )
            parts.append(split_rows(dot_nn(window, tap_rows(taps_ref, r)), count))
        return jnp.concatenate([parts[side][m] for m in range(count) for side in (0, 1)], axis=0)

    for member in range(groups):
        slot = groups + member
        for side in (0, 1):
            ends = corner(side, slot, 0), corner(side, slot, 1)
            shift_row(cot_shift_scr, member, side, halo[slot][side], *ends)
    grad_field = grad_part_ref[...].reshape(groups * 2 * cols, channels)
    grad_field = grad_field + halo_part(cot_shift_scr, groups, conv_t_ref, True)

    blocks = []
    for member in range(groups):
        corner_scr[member] = jnp.zeros((16, channels), F32)
        for side in (0, 1):
            for end in (0, 1):
                at = 2 * side + end
                corner_scr[member, at : at + 1, :] = corner(side, member, end)
        blocks += [halo[member][0], halo[member][1], corner_scr[member]]
    x = jnp.concatenate(blocks, axis=0)
    forward = forward_cells(x, mem, groups, gain, project_ref, output_ref, same_head)
    x = [both_ref[0, m, row] for m in range(mem) for row in (0, rows - 1)]
    backward = backward_cells(
        lambda array: jnp.concatenate([array[:cols], array[cells - cols :]], axis=0),
        grad_field,
        jnp.concatenate(x, axis=0).astype(F32),
        gain,
        (project_t_ref, output_t_ref),
        proj_ref,
        unit_ref,
        soft_ref,
        inverse_ref,
        pull_ref,
    )

    def finish_result(chain):
        fresh = yield from chain
        fresh = split_rows(fresh.astype(F32), mem)
        for member in range(mem):
            for side in (0, 1):
                slab = fresh[member][side * cols : (side + 1) * cols]
                at = 2 * cols + 2 * side
                ends = fresh[member][at : at + 1], fresh[member][at + 1 : at + 2]
                shift_row(shift_scr, member, side, slab, *ends)
        yield
        outer = result_part_ref[...].reshape(mem * 2 * cols, channels)
        outer = (outer + halo_part(shift_scr, mem, conv_ref, False)).astype(BF16)
        store_outer(0, outer)

    def store_outer(which, outer):
        for i, slab in enumerate(split_rows(outer, 2 * mem)):
            outer_scr[which, i % 2, i // 2] = slab
        for side, row in ((0, 0), (1, rows - 1)):
            copy = pltpu.make_async_copy(
                outer_scr.at[which, side],
                (result_ref, grad_ref)[which].at[:, row],
                sems.at[2 + 2 * which + side],
            )
            copy.start()
            copies.append(copy)

    total, _ = together(backward, finish_result(forward))
    store_outer(1, total)
    for copy in copies:
        copy.wait()


def local_call(kernel, name, operands, out_shape, scratch, pinned=False, cost=None, copied=False):
    whole = pl.BlockSpec(memory_space=pltpu.VMEM)
    anywhere = pl.BlockSpec(memory_space=pl.ANY)
    specs = [anywhere if in_hbm else whole for _, in_hbm in operands]
    arrays = [
        pltpu.with_memory_space_constraint(array, pltpu.HBM) if in_hbm else array
        for array, in_hbm in operands
    ]

    def keep(shape):
        return pltpu.VMEM(shape.shape, shape.dtype) if pinned else shape

    return pl.pallas_call(
        kernel,
        out_shape=jax.tree.map(keep, out_shape),
        in_specs=specs,
        out_specs=jax.tree.map(lambda _: anywhere if copied else whole, out_shape),
        scratch_shapes=scratch,
        compiler_params=pltpu.CompilerParams(vmem_limit_bytes=VMEM_LIMIT),
        cost_estimate=cost,
        name=name,
    )(*arrays)


def here(*arrays):
    return [(array, False) for array in arrays]


def in_hbm(*arrays):
    return [(array, True) for array in arrays]


def per_device_paired(ensemble, norm_gain, project_weight, output_weight, conv_kernel, cotangent):
    mem, rows, cols, channels = ensemble.shape
    if rows < 3 or cols % 16 or (2 * mem * rows) % 16:
        return per_device_general(
            ensemble, norm_gain, project_weight, output_weight, conv_kernel, cotangent
        )
    groups = 2 * mem
    slots = 2 * groups
    cells = rows * cols
    lon_count = lax.axis_size("lon")
    lat_count = lax.axis_size("lat")
    bf16 = functools.partial(jax.ShapeDtypeStruct, dtype=BF16)
    f32 = functools.partial(jax.ShapeDtypeStruct, dtype=F32)
    swap = [(0, 1), (1, 0)]
    core_pairs = [(i, i ^ 1) for i in range(lon_count)]
    chip_pairs = [(i, (i - 1 if i % 2 == 0 else i + 1) % lon_count) for i in range(lon_count)]

    def lat_swap(offset):
        pairs = []
        for lat in range(lat_count):
            for lon in range(lon_count):
                to = (lat + 1 if lat % 2 == offset else lat - 1, lon)
                if not 0 <= to[0] < lat_count:
                    to = (lat, lon ^ 1)
                pairs.append((lat * lon_count + lon, to[0] * lon_count + to[1]))
        return pairs

    ends_shape = (2, 2 * mem * rows, channels)
    both, ends = local_call(
        stack_kernel,
        "stack",
        in_hbm(ensemble, cotangent),
        (bf16((2,) + ensemble.shape), bf16(ends_shape)),
        [pltpu.VMEM(ends_shape[1:], F32)] * 2 + [pltpu.SemaphoreType.DMA((2,))],
        pinned=True,
    )
    other_ends = lax.ppermute(ends, "member", swap)
    other = lax.ppermute(both, "member", swap)

    strip = (slots * rows, channels)
    chip_send, core_send = local_call(
        pack_strips_kernel,
        "pack_strips",
        here(ends, other_ends),
        (bf16(strip), bf16(strip)),
        [pltpu.VMEM(strip, F32)] * 2,
    )
    chip = lax.ppermute(chip_send, "lon", chip_pairs)
    core = lax.ppermute(core_send, "lon", core_pairs)

    weights = (
        norm_gain.reshape(1, channels),
        project_weight,
        output_weight,
        conv_kernel.reshape(9 * channels, channels),
    )
    *weights, project_t, output_t = local_call(
        load_kernel,
        "load_weights",
        in_hbm(*weights),
        tuple(jax.ShapeDtypeStruct(w.shape, w.dtype) for w in weights)
        + (bf16((3 * channels, channels)), bf16((channels, channels))),
        [pltpu.SemaphoreType.DMA((4,))],
        pinned=True,
        cost=MIDDLING,
    )
    halo = bf16((slots * (cols + 2), channels))
    first_send, second_send = local_call(
        pack_rows_kernel,
        "pack_rows",
        here(both, other, chip, core, weights[0]),
        (halo, halo),
        [pltpu.VMEM((2, 2 * slots, channels), F32)],
    )
    first = lax.ppermute(first_send, ("lat", "lon"), lat_swap(0))
    second = lax.ppermute(second_send, ("lat", "lon"), lat_swap(1))

    *held, updated = local_call(
        own_kernel,
        "own_cells",
        here(both, other, *weights[:3], second_send),
        (
            bf16((groups, cells, 3 * channels)),
            bf16((2, groups, cells, channels)),
            f32((groups * groups, cells, channels)),
            f32((2, mem, cells, channels)),
            f32((2, mem, cells, channels)),
            bf16((mem, cells, channels)),
        ),
        [],
        pinned=True,
        cost=LONG,
    )
    conv_t, *parts = local_call(
        centre_kernel,
        "centre",
        here(both, other, chip, core, *weights, project_t, output_t, *held, updated),
        (
            bf16((9 * channels, channels)),
            bf16((mem, rows - 2, cols, channels)),
            bf16((mem, rows - 2, cols, channels)),
            f32((mem, 2 * cols, channels)),
            f32((groups, 2 * cols, channels)),
        ),
        [
            pltpu.VMEM((mem, cells, 3 * channels), BF16),
            pltpu.VMEM((groups, cells, 3 * channels), BF16),
            pltpu.VMEM((groups, 16, channels), F32),
        ],
        pinned=True,
        cost=LONG,
    )
    return local_call(
        functools.partial(main_kernel, lat_count=lat_count),
        "main",
        here(both, second, first, *weights, project_t, output_t, conv_t, *held, *parts),
        (bf16(ensemble.shape), bf16(ensemble.shape)),
        [
            pltpu.VMEM((mem, 2 * cols, 3 * channels), BF16),
            pltpu.VMEM((groups, 2 * cols, 3 * channels), BF16),
            pltpu.VMEM((groups, 16, channels), F32),
            pltpu.VMEM((2, 2, mem, cols, channels), BF16),
            pltpu.SemaphoreType.DMA((6,)),
        ],
        copied=True,
    )


def solution(mesh):
    paired = mesh.shape["member"] == 2 and mesh.shape["lon"] % 2 == 0
    per_device = per_device_paired if paired else per_device_general
    in_specs = (
        P("member", "lat", "lon", None),
        P(),
        P(),
        P(),
        P(),
        P("member", "lat", "lon", None),
    )
    out_specs = (P("member", "lat", "lon", None), P("member", "lat", "lon", None))
    return jax.shard_map(
        per_device, mesh=mesh, in_specs=in_specs, out_specs=out_specs, check_vma=False
    )
```

```python
import functools
import math

import jax
import jax.numpy as jnp
from jax import lax
from jax.experimental import pallas as pl
from jax.experimental.pallas import tpu as pltpu
from jax.sharding import PartitionSpec as P

HEAD_COUNT = 8


FLOOR = 0.5
EPSILON = 1e-06


def padded_2(block, sides, width, periodic):
    for axis, dim in sides:
        count = lax.axis_size(axis)
        forward = [(i, i + 1) for i in range(count - 1)]
        if periodic:
            forward.append((count - 1, 0))
        backward = [(target, source) for source, target in forward]
        low = lax.ppermute(
            lax.slice_in_dim(block, block.shape[dim] - width, None, axis=dim), axis, forward
        )
        high = lax.ppermute(lax.slice_in_dim(block, 0, width, axis=dim), axis, backward)
        block = jnp.concatenate([low, block, high], axis=dim)
    return block


def row_norm(values, gain_vec):
    mean_sq = jnp.mean(values * values, axis=-1, keepdims=True)
    return values * lax.rsqrt(mean_sq + EPSILON) * gain_vec


def head_norm(values, head_count):
    shaped = values.reshape(values.shape[:-1] + (head_count, values.shape[-1] // head_count))
    mean_sq = jnp.mean(shaped * shaped, axis=-1, keepdims=True)
    return (shaped * lax.rsqrt(jnp.maximum(mean_sq, FLOOR))).reshape(values.shape)


def split_heads(values, head_count):
    return values.reshape(values.shape[:-1] + (head_count, values.shape[-1] // head_count))


def head_pullback(raw_rows, grad_rows):
    _, pullback = jax.vjp(lambda t: head_norm(t, HEAD_COUNT), raw_rows.astype(jnp.float32))
    return pullback(grad_rows)[0]


def pad_field(field_in):
    widened = padded_2(field_in, (("lon", 2),), 1, True)
    return padded_2(widened, (("lat", 1),), 1, False)


def conv_taps(padded, kernel, lat_n, lon_n, adjoint):
    running = None
    for row_off in range(3):
        for col_off in range(3):
            if adjoint:
                window = padded[
                    :, 2 - row_off : 2 - row_off + lat_n, 2 - col_off : 2 - col_off + lon_n
                ]
                summand = jnp.einsum(
                    "mabc,dc->mabd",
                    window,
                    kernel[row_off, col_off],
                    preferred_element_type=jnp.float32,
                )
            else:
                window = padded[:, row_off : row_off + lat_n, col_off : col_off + lon_n]
                summand = jnp.einsum(
                    "mabc,cd->mabd",
                    window,
                    kernel[row_off, col_off],
                    preferred_element_type=jnp.float32,
                )
            running = summand if running is None else running + summand
    return running


def per_device_general(ensemble, norm_gain, project_weight, output_weight, conv_kernel, cotangent):
    mem_dev, lat_dev, lon_dev, channels = ensemble.shape
    cell_count = lat_dev * lon_dev
    score_scale = 1.0 / math.sqrt(channels // HEAD_COUNT)
    inputs = ensemble.reshape(mem_dev, cell_count, channels).astype(jnp.float32)
    normed = row_norm(inputs, norm_gain).astype(jnp.bfloat16)
    spread = lax.all_to_all(normed, "member", split_axis=1, concat_axis=0, tiled=True)
    projected = jnp.dot(spread, project_weight, preferred_element_type=jnp.float32).astype(
        jnp.bfloat16
    )
    query_raw = projected[..., :channels]
    key_raw = projected[..., channels : 2 * channels]
    value_rows = projected[..., 2 * channels :]
    key_rows = head_norm(key_raw.astype(jnp.float32), HEAD_COUNT).astype(jnp.bfloat16)
    queries = head_norm(query_raw.astype(jnp.float32), HEAD_COUNT).astype(jnp.bfloat16)
    query_heads = split_heads(queries, HEAD_COUNT)
    key_heads = split_heads(key_rows, HEAD_COUNT)
    value_heads = split_heads(value_rows, HEAD_COUNT)
    scores = (
        jnp.einsum("mphd,nphd->mnhp", query_heads, key_heads, preferred_element_type=jnp.float32)
        * score_scale
    )
    expd = jnp.exp(scores)
    soft = expd / jnp.sum(expd, axis=1, keepdims=True)
    rounded = soft.astype(jnp.bfloat16)
    mixed_out = jnp.einsum(
        "mnhp,nphd->mphd", rounded, value_heads, preferred_element_type=jnp.float32
    )
    mixed_out = mixed_out.reshape(query_raw.shape).astype(jnp.bfloat16)
    mixed_out = lax.all_to_all(mixed_out, "member", split_axis=0, concat_axis=1, tiled=True)
    updated = (
        inputs + jnp.dot(mixed_out, output_weight, preferred_element_type=jnp.float32)
    ).astype(jnp.bfloat16)
    field_up = updated.reshape(mem_dev, lat_dev, lon_dev, channels)
    result = field_up.astype(jnp.float32) + conv_taps(
        pad_field(field_up), conv_kernel, lat_dev, lon_dev, False
    )
    result = result.astype(jnp.bfloat16)
    grad_field = cotangent.astype(jnp.float32) + conv_taps(
        pad_field(cotangent), conv_kernel, lat_dev, lon_dev, True
    )
    grad_rows = grad_field.reshape(mem_dev, cell_count, channels)
    grad_mixed = jnp.einsum(
        "mpc,dc->mpd",
        grad_rows.astype(jnp.bfloat16),
        output_weight,
        preferred_element_type=jnp.float32,
    )
    grad_mixed = grad_mixed.astype(jnp.bfloat16)
    grad_mixed = lax.all_to_all(grad_mixed, "member", split_axis=1, concat_axis=0, tiled=True)
    grad_heads = split_heads(grad_mixed, HEAD_COUNT)
    dprob = jnp.einsum(
        "mphd,nphd->mnhp", grad_heads, value_heads, preferred_element_type=jnp.float32
    )
    dscore = (soft * (dprob - jnp.sum(soft * dprob, axis=1, keepdims=True))).astype(jnp.bfloat16)
    query_grad = (
        jnp.einsum("mnhp,nphd->mphd", dscore, key_heads, preferred_element_type=jnp.float32)
        * score_scale
    )
    query_grad = query_grad.reshape(query_raw.shape)
    key_grad = (
        jnp.einsum("mnhp,mphd->nphd", dscore, query_heads, preferred_element_type=jnp.float32)
        * score_scale
    )
    key_grad = key_grad.reshape(key_raw.shape)
    value_grad = jnp.einsum(
        "mnhp,mphd->nphd", rounded, grad_heads, preferred_element_type=jnp.float32
    )
    value_grad = value_grad.reshape(key_raw.shape)
    grad_query_raw = head_pullback(query_raw, query_grad)
    grad_key_raw = head_pullback(key_raw, key_grad)
    grad_proj = jnp.concatenate([grad_query_raw, grad_key_raw, value_grad], axis=-1).astype(
        jnp.bfloat16
    )
    grad_proj = lax.all_to_all(grad_proj, "member", split_axis=0, concat_axis=1, tiled=True)
    grad_normed = jnp.einsum(
        "mpe,ce->mpc", grad_proj, project_weight, preferred_element_type=jnp.float32
    )
    _, pull_norm = jax.vjp(lambda t: row_norm(t, norm_gain), inputs)
    grad_inputs = pull_norm(grad_normed)[0]
    grad_ensemble = (
        (grad_rows + grad_inputs).astype(jnp.bfloat16).reshape(mem_dev, lat_dev, lon_dev, channels)
    )
    return (result, grad_ensemble)


F32 = jnp.float32
BF16 = jnp.bfloat16
VMEM_LIMIT = 24 * 1024 * 1024
LONG = pl.CostEstimate(flops=20_000_000_000, bytes_accessed=4_000_000, transcendentals=0)
LOAD_COST = pl.CostEstimate(flops=3_000_000_000, bytes_accessed=2_000_000, transcendentals=0)


def is_even(axis):
    return lax.rem(lax.axis_index(axis), 2) == 0


def load_kernel(
    gain_hbm,
    project_hbm,
    output_hbm,
    conv_hbm,
    gain_ref,
    project_ref,
    output_ref,
    conv_ref,
    project_t_ref,
    output_t_ref,
    sems,
):
    channels = output_ref.shape[0]
    pairs = (
        (gain_hbm, gain_ref),
        (project_hbm, project_ref),
        (output_hbm, output_ref),
        (conv_hbm, conv_ref),
    )
    loads = [
        pltpu.make_async_copy(source, target, sems.at[i])
        for i, (source, target) in enumerate(pairs)
    ]
    for load in loads:
        load.start()
    for load in loads[:3]:
        load.wait()
    output_t_ref[...] = output_ref[...].T
    for kind in range(3):
        lanes = slice(kind * channels, (kind + 1) * channels)
        project_t_ref[lanes, :] = project_ref[:, lanes].T
    loads[3].wait()


def stack_kernel(ens_ref, cot_ref, both_ref, ends_ref, low_scr, high_scr, sems):
    _, mem, rows, cols, _ = both_ref.shape
    copies = [
        pltpu.make_async_copy(ref, both_ref.at[i], sems.at[i])
        for i, ref in enumerate((ens_ref, cot_ref))
    ]
    for copy in copies:
        copy.start()
    for copy in copies:
        copy.wait()
    index = 0
    for array in range(2):
        for member in range(mem):
            for row in range(rows):
                slab = both_ref[array, member, row].astype(F32)
                low_scr[index : index + 1, :] = slab[0:1]
                high_scr[index : index + 1, :] = slab[cols - 1 : cols]
                index += 1
    ends_ref[0] = low_scr[...].astype(BF16)
    ends_ref[1] = high_scr[...].astype(BF16)


def pack_strips_kernel(
    ends_ref, other_ends_ref, after_ref, chip_ref, core_ref, low_scr, high_scr
):
    part = ends_ref.shape[1] // 2
    for side, scr in ((0, low_scr), (1, high_scr)):
        for group, ref in enumerate((ends_ref, other_ends_ref)):
            column = ref[side].astype(F32)
            for array in range(2):
                at = (2 * array + group) * part
                scr[at : at + part, :] = column[array * part : (array + 1) * part]
    even = is_even("lon")
    low, high = low_scr[...], high_scr[...]
    core_ref[...] = jnp.where(even, high, low).astype(BF16)
    chip_ref[...] = jnp.where(even, low, high).astype(BF16)


def rim_columns(chip_ref, core_ref):
    even = is_even("lon")
    chip, core = chip_ref[...].astype(F32), core_ref[...].astype(F32)
    return jnp.where(even, chip, core), jnp.where(even, core, chip)


def pack_rows_kernel(
    both_ref, other_ref, chip_ref, core_ref, updated_ref, first_ref, second_ref, edge_scr
):
    _, mem, rows, cols, _ = both_ref.shape
    groups = 2 * mem
    cells = rows * cols
    slots = 2 * groups
    even = is_even("lat")
    west, east = rim_columns(chip_ref, core_ref)
    for place in range(mem + groups):
        if place < mem:
            pair = updated_ref[place, :cols, :], updated_ref[place, cells - cols :, :]
        else:
            member = place - mem
            ref, who = (both_ref, member) if member < mem else (other_ref, member - mem)
            pair = ref[1, who, 0], ref[1, who, rows - 1]
        start, stop = (slab.astype(F32) for slab in pair)
        at = slice(place * cols, (place + 1) * cols)
        first_ref[at, :] = jnp.where(even, stop, start).astype(BF16)
        second_ref[at, :] = jnp.where(even, start, stop).astype(BF16)
    for slot in range(slots):
        top, low = slot * rows, (slot + 1) * rows - 1
        for side, column in enumerate((west, east)):
            place = side * slots + slot
            start, stop = column[top : top + 1], column[low : low + 1]
            edge_scr[0, place : place + 1, :] = jnp.where(even, stop, start)
            edge_scr[1, place : place + 1, :] = jnp.where(even, start, stop)
    first_ref[(mem + groups) * cols :, :] = edge_scr[0].astype(BF16)
    second_ref[(mem + groups) * cols :, :] = edge_scr[1].astype(BF16)


def dot_nn(a, b):
    return lax.dot_general(a, b, (((1,), (0,)), ((), ())), preferred_element_type=F32)


def same_head_matrix(channels):
    width = channels // HEAD_COUNT
    lane_row = lax.broadcasted_iota(jnp.int32, (channels, channels), 0) // width
    lane_col = lax.broadcasted_iota(jnp.int32, (channels, channels), 1) // width
    return jnp.where(lane_row == lane_col, 1.0, 0.0).astype(BF16)


def head_sums(values, same_head):
    high = values.astype(BF16)
    low = (values - high.astype(F32)).astype(BF16)
    return dot_nn(high, same_head) + dot_nn(low, same_head)


def rounded_sums(values, same_head):
    return dot_nn(values.astype(BF16), same_head)


def head_units(raw, same_head, sums=head_sums):
    raw = raw.astype(F32)
    mean_sq = sums(raw * raw, same_head) * (HEAD_COUNT / raw.shape[-1])
    inverse = lax.rsqrt(jnp.maximum(mean_sq, FLOOR))
    return raw, mean_sq, inverse, (raw * inverse).astype(BF16)


def row_rsqrt(values):
    return lax.rsqrt(jnp.mean(values * values, axis=-1, keepdims=True) + EPSILON)


def split_rows(array, count):
    size = array.shape[0] // count
    return [array[i * size : (i + 1) * size] for i in range(count)]


def softmax_members(queries, keys, same_head, scale):
    products = [query * key for query in queries for key in keys]
    scores = dot_nn(jnp.concatenate(products, axis=0), same_head) * scale
    exps = split_rows(jnp.exp(scores), len(products))
    soft = []
    for m in range(len(queries)):
        mine = exps[m * len(keys) : (m + 1) * len(keys)]
        total = mine[0]
        for e in mine[1:]:
            total = total + e
        inverse = 1.0 / total
        soft.append([e * inverse for e in mine])
    return soft


def mix_values(probs, values):
    mixed = None
    for prob, value in zip(probs, values):
        term = prob.astype(BF16).astype(F32) * value.astype(F32)
        mixed = term if mixed is None else mixed + term
    return mixed.astype(BF16)


def forward_cells(x, mem, groups, gain, project_ref, output_ref, same_head):
    channels = x.shape[-1]
    own_rows = x.shape[0] // groups * mem
    scale = 1.0 / math.sqrt(channels // HEAD_COUNT)
    normed = (x * row_rsqrt(x) * gain).astype(BF16)
    query_raw = dot_nn(normed[:own_rows], project_ref[:, :channels]).astype(BF16)
    key_raw = dot_nn(normed, project_ref[:, channels : 2 * channels]).astype(BF16)
    values = dot_nn(normed, project_ref[:, 2 * channels :]).astype(BF16)
    yield
    raw = jnp.concatenate([query_raw, key_raw], axis=0)
    units = head_units(raw, same_head, rounded_sums)[3]
    yield
    queries = split_rows(units[:own_rows], mem)
    keys = split_rows(units[own_rows:], groups)
    values = split_rows(values, groups)
    soft = softmax_members(queries, keys, same_head, scale)
    yield
    mixed = jnp.concatenate([mix_values(soft[m], values) for m in range(mem)], axis=0)
    return (x[:own_rows] + dot_nn(mixed, output_ref[...])).astype(BF16)


def run(chain):
    while True:
        try:
            next(chain)
        except StopIteration as stop:
            return stop.value


def shift_row(scr, member, place, slab, west, east):
    cols, channels = slab.shape
    column = lax.broadcasted_iota(jnp.int32, (cols, channels), 0)
    back = jnp.where(column == 0, west, pltpu.roll(slab, 1, 0))
    ahead = jnp.where(column == cols - 1, east, pltpu.roll(slab, cols - 1, 0))
    rows_at = slice(place * cols, (place + 1) * cols)
    scr[member, rows_at, :channels] = back.astype(BF16)
    scr[member, rows_at, channels : 2 * channels] = slab.astype(BF16)
    scr[member, rows_at, 2 * channels :] = ahead.astype(BF16)


def tap_rows(taps_ref, r):
    size = taps_ref.shape[0] // 3
    return taps_ref[r * size : (r + 1) * size, :]


def own_kernel(
    both_ref,
    other_ref,
    gain_ref,
    project_ref,
    output_ref,
    proj_ref,
    unit_ref,
    soft_ref,
    inverse_ref,
    pull_ref,
    updated_ref,
):
    _, mem, rows, cols, channels = both_ref.shape
    groups = 2 * mem
    cells = rows * cols
    width = channels // HEAD_COUNT
    scale = 1.0 / math.sqrt(width)
    same_head = same_head_matrix(channels)
    own = both_ref[0].reshape(mem * cells, channels)
    other = other_ref[0].reshape(mem * cells, channels)
    x = jnp.concatenate([own, other], axis=0).astype(F32)
    normed = (x * row_rsqrt(x) * gain_ref[...]).astype(BF16)
    proj = dot_nn(normed, project_ref[...]).astype(BF16)
    proj_ref[...] = proj.reshape(groups, cells, 3 * channels)
    both_raw = jnp.concatenate([proj[:, :channels], proj[:, channels : 2 * channels]], axis=0)
    raw, mean_sq, inverse, units = head_units(both_raw, same_head)
    unit_ref[...] = units.reshape(2, groups, cells, channels)
    active = jnp.where(mean_sq > FLOOR, 1.0, jnp.where(mean_sq == FLOOR, 0.5, 0.0))
    pull = active * raw * (inverse * inverse * inverse) / width
    for kind in range(2):
        at = kind * groups * cells
        mine = slice(at, at + mem * cells)
        inverse_ref[kind] = inverse[mine].reshape(mem, cells, channels)
        pull_ref[kind] = pull[mine].reshape(mem, cells, channels)
    units = split_rows(units, 2 * groups)
    soft = softmax_members(units[:groups], units[groups:], same_head, scale)
    for m in range(groups):
        for n in range(groups):
            soft_ref[m * groups + n] = soft[m][n]
    values = split_rows(proj[:, 2 * channels :], groups)
    mixed = jnp.concatenate([mix_values(soft[m], values) for m in range(mem)], axis=0)
    updated = x[: mem * cells] + dot_nn(mixed, output_ref[...])
    updated_ref[...] = updated.astype(BF16).reshape(mem, cells, channels)


def backward_cells(
    pick, grad_field, x, gain, weights_t, proj_ref, unit_ref, soft_ref, inverse_ref, pull_ref
):
    project_t_ref, output_t_ref = weights_t
    groups = proj_ref.shape[0]
    mem = inverse_ref.shape[1]
    channels = x.shape[-1]
    scale = 1.0 / math.sqrt(channels // HEAD_COUNT)
    same_head = same_head_matrix(channels)
    grad_mixed = dot_nn(grad_field.astype(BF16), output_t_ref[...]).astype(BF16)
    grads = split_rows(grad_mixed, groups)
    yield
    values = [pick(proj_ref[n, :, 2 * channels :]) for n in range(groups)]
    products = [grads[m] * values[n] for m in range(groups) for n in range(groups)]
    dprobs = split_rows(dot_nn(jnp.concatenate(products, axis=0), same_head), len(products))
    yield
    units = [[pick(unit_ref[k, n]).astype(F32) for n in range(groups)] for k in range(2)]
    query_grad = [None] * mem
    key_grad = [None] * mem
    value_grad = [None] * mem
    for m in range(groups):
        soft = [pick(soft_ref[m * groups + n]) for n in range(groups)]
        dprob = dprobs[m * groups : (m + 1) * groups]
        mean = soft[0] * dprob[0]
        for n in range(1, groups):
            mean = mean + soft[n] * dprob[n]
        for n in range(groups):
            if m >= mem and n >= mem:
                continue
            dscore = soft[n] * (dprob[n] - mean)
            if m < mem:
                term = dscore * units[1][n]
                query_grad[m] = term if query_grad[m] is None else query_grad[m] + term
            if n < mem:
                term = dscore * units[0][m]
                key_grad[n] = term if key_grad[n] is None else key_grad[n] + term
                term = soft[n] * grads[m].astype(F32)
                value_grad[n] = term if value_grad[n] is None else value_grad[n] + term

    unit_grads = [jnp.concatenate(g, axis=0) * scale for g in (query_grad, key_grad)]

    def members(take):
        return jnp.concatenate([pick(take(m)) for m in range(mem)], axis=0)

    raws = []
    for kind in range(2):
        lanes = slice(kind * channels, (kind + 1) * channels)
        raws.append(members(lambda m: proj_ref[m, :, lanes]).astype(F32))
    inner = rounded_sums(
        jnp.concatenate([g * raw for g, raw in zip(unit_grads, raws)], axis=0), same_head
    )
    inner = split_rows(inner, 2)
    yield
    pulled = []
    for kind in range(2):
        inverse = members(lambda m: inverse_ref[kind, m])
        pull = members(lambda m: pull_ref[kind, m])
        pulled.append((inverse * unit_grads[kind] - pull * inner[kind]).astype(BF16))
    pulled.append(jnp.concatenate(value_grad, axis=0).astype(BF16))
    grad_normed = dot_nn(jnp.concatenate(pulled, axis=1), project_t_ref[...]) * gain
    yield
    inverse = row_rsqrt(x)
    inner = jnp.mean(x * grad_normed, axis=-1, keepdims=True)
    total = grad_field[: x.shape[0]] + inverse * grad_normed
    return (total - x * (inverse * inverse * inverse * inner)).astype(BF16)


def centre_kernel(
    both_ref,
    other_ref,
    chip_ref,
    core_ref,
    gain_ref,
    project_ref,
    output_ref,
    conv_ref,
    project_t_ref,
    output_t_ref,
    proj_ref,
    unit_ref,
    soft_ref,
    inverse_ref,
    pull_ref,
    updated_ref,
    conv_t_ref,
    result_ref,
    grad_ref,
    result_part_ref,
    grad_part_ref,
    shift_scr,
    cot_shift_scr,
    strip_scr,
):
    _, mem, rows, cols, channels = both_ref.shape
    groups = 2 * mem
    cells = rows * cols
    gain = gain_ref[...]
    same_head = same_head_matrix(channels)
    west, east = rim_columns(chip_ref, core_ref)
    for r in range(3):
        for c in range(3):
            tap = (3 * r + c) * channels
            turned = (3 * r + 2 - c) * channels
            conv_t_ref[turned : turned + channels, :] = conv_ref[tap : tap + channels, :].T

    def convolve(scr, count, start, taps_ref, turned):
        sums = [
            [start[(m * rows + a) * cols : (m * rows + a + 1) * cols] for a in range(rows)]
            for m in range(count)
        ]
        for r in range(3):
            step = 1 - r if turned else r - 1
            outs = [a for a in range(rows) if 0 <= a + step < rows]
            begin, end = outs[0] + step, outs[-1] + step + 1
            window = jnp.concatenate(
                [scr[m, begin * cols : end * cols, :] for m in range(count)], axis=0
            )
            terms = split_rows(dot_nn(window, tap_rows(taps_ref, r)), count * len(outs))
            for m in range(count):
                for i, a in enumerate(outs):
                    sums[m][a] = sums[m][a] + terms[m * len(outs) + i]
        return sums

    cots = []
    for member in range(groups):
        for row in range(rows):
            ref, who = (both_ref, member) if member < mem else (other_ref, member - mem)
            slab = ref[1, who, row].astype(F32)
            cots.append(slab)
            at = (groups + member) * rows + row
            shift_row(cot_shift_scr, member, row, slab, west[at : at + 1], east[at : at + 1])
    sums = convolve(cot_shift_scr, groups, jnp.concatenate(cots, axis=0), conv_t_ref, True)
    for member in range(groups):
        grad_part_ref[member, :cols, :] = sums[member][0]
        grad_part_ref[member, cols:, :] = sums[member][rows - 1]
    grad_field = jnp.concatenate([slab for s in sums for slab in s[1 : rows - 1]], axis=0)

    for member in range(groups):
        at = member * rows
        strip_scr[member] = jnp.zeros((16, channels), F32)
        strip_scr[member, :rows, :] = west[at : at + rows]
        strip_scr[member, 8 : 8 + rows, :] = east[at : at + rows]
    x = strip_scr[...].reshape(groups * 16, channels)
    forward = forward_cells(x, mem, groups, gain, project_ref, output_ref, same_head)
    x = both_ref[0, :, 1 : rows - 1].reshape(mem * (cells - 2 * cols), channels).astype(F32)
    backward = backward_cells(
        lambda array: array[cols : cells - cols],
        grad_field,
        x,
        gain,
        (project_t_ref, output_t_ref),
        proj_ref,
        unit_ref,
        soft_ref,
        inverse_ref,
        pull_ref,
    )
    fresh, total = run(forward), run(backward)
    fresh = split_rows(fresh.astype(F32), mem)
    grad_ref[...] = total.reshape(mem, rows - 2, cols, channels)

    for member in range(mem):
        for row in range(rows):
            slab = updated_ref[member, row * cols : (row + 1) * cols, :].astype(F32)
            ends = fresh[member][row : row + 1], fresh[member][8 + row : 9 + row]
            shift_row(shift_scr, member, row, slab, *ends)
    start = updated_ref[...].reshape(mem * cells, channels).astype(F32)
    sums = convolve(shift_scr, mem, start, conv_ref, False)
    for member in range(mem):
        result_part_ref[member, :cols, :] = sums[member][0]
        result_part_ref[member, cols:, :] = sums[member][rows - 1]
        for row in range(1, rows - 1):
            result_ref[member, row - 1] = sums[member][row].astype(BF16)


def main_kernel(
    both_ref,
    first_ref,
    second_ref,
    gain_ref,
    project_ref,
    output_ref,
    conv_ref,
    project_t_ref,
    output_t_ref,
    conv_t_ref,
    proj_ref,
    unit_ref,
    soft_ref,
    inverse_ref,
    pull_ref,
    inner_result_ref,
    inner_grad_ref,
    result_part_ref,
    grad_part_ref,
    result_ref,
    grad_ref,
    shift_scr,
    cot_shift_scr,
    corner_scr,
    outer_scr,
    sems,
    *,
    lat_count,
):
    _, mem, rows, cols, channels = both_ref.shape
    copies = []
    for i, (ref, out_ref) in enumerate(
        ((inner_result_ref, result_ref), (inner_grad_ref, grad_ref))
    ):
        copy = pltpu.make_async_copy(ref, out_ref.at[:, pl.ds(1, rows - 2)], sems.at[i])
        copy.start()
        copies.append(copy)
    groups = 2 * mem
    slots = 2 * groups
    cells = rows * cols
    gain = gain_ref[...]
    same_head = same_head_matrix(channels)
    lat_even = is_even("lat")
    lat = lax.axis_index("lat")

    def halos(at):
        first, second = first_ref[at, :].astype(F32), second_ref[at, :].astype(F32)
        north = jnp.where(lat == 0, 0.0, jnp.where(lat_even, second, first))
        south = jnp.where(lat == lat_count - 1, 0.0, jnp.where(lat_even, first, second))
        return north, south

    halo = [halos(slice(i * cols, (i + 1) * cols)) for i in range(mem + groups)]
    corners = halos(slice((mem + groups) * cols, (mem + groups) * cols + 2 * slots))

    def corner(side, slot, end):
        at = end * slots + slot
        return corners[side][at : at + 1]

    def halo_part(scr, count, taps_ref, turned):
        north, south = (2, 0) if turned else (0, 2)
        parts = []
        for side, r in ((0, north), (1, south)):
            window = jnp.concatenate(
                [scr[m, side * cols : (side + 1) * cols, :] for m in range(count)], axis=0
            )
            parts.append(split_rows(dot_nn(window, tap_rows(taps_ref, r)), count))
        return jnp.concatenate([parts[side][m] for m in range(count) for side in (0, 1)], axis=0)

    for member in range(groups):
        slot = groups + member
        for side in (0, 1):
            ends = corner(side, slot, 0), corner(side, slot, 1)
            shift_row(cot_shift_scr, member, side, halo[mem + member][side], *ends)
    grad_field = grad_part_ref[...].reshape(groups * 2 * cols, channels)
    grad_field = grad_field + halo_part(cot_shift_scr, groups, conv_t_ref, True)

    for member in range(groups):
        corner_scr[member] = jnp.zeros((16, channels), F32)
        for side in (0, 1):
            for end in (0, 1):
                at = 2 * side + end
                corner_scr[member, at : at + 1, :] = corner(side, member, end)
    x = corner_scr[...].reshape(groups * 16, channels)
    forward = forward_cells(x, mem, groups, gain, project_ref, output_ref, same_head)
    x = [both_ref[0, m, row] for m in range(mem) for row in (0, rows - 1)]
    backward = backward_cells(
        lambda array: jnp.concatenate([array[:cols], array[cells - cols :]], axis=0),
        grad_field,
        jnp.concatenate(x, axis=0).astype(F32),
        gain,
        (project_t_ref, output_t_ref),
        proj_ref,
        unit_ref,
        soft_ref,
        inverse_ref,
        pull_ref,
    )

    def finish_result(chain):
        fresh = yield from chain
        fresh = split_rows(fresh.astype(F32), mem)
        for member in range(mem):
            for side in (0, 1):
                slab = halo[member][side]
                at = 2 * side
                ends = fresh[member][at : at + 1], fresh[member][at + 1 : at + 2]
                shift_row(shift_scr, member, side, slab, *ends)
        yield
        outer = result_part_ref[...].reshape(mem * 2 * cols, channels)
        outer = (outer + halo_part(shift_scr, mem, conv_ref, False)).astype(BF16)
        store_outer(0, outer)

    def store_outer(which, outer):
        for i, slab in enumerate(split_rows(outer, 2 * mem)):
            outer_scr[which, i % 2, i // 2] = slab
        for side, row in ((0, 0), (1, rows - 1)):
            copy = pltpu.make_async_copy(
                outer_scr.at[which, side],
                (result_ref, grad_ref)[which].at[:, row],
                sems.at[2 + 2 * which + side],
            )
            copy.start()
            copies.append(copy)

    run(finish_result(forward))
    store_outer(1, run(backward))
    for copy in copies:
        copy.wait()


def local_call(kernel, name, operands, out_shape, scratch, pinned=False, cost=None, copied=False):
    whole = pl.BlockSpec(memory_space=pltpu.VMEM)
    anywhere = pl.BlockSpec(memory_space=pl.ANY)
    specs = [anywhere if in_hbm else whole for _, in_hbm in operands]
    arrays = [
        pltpu.with_memory_space_constraint(array, pltpu.HBM) if in_hbm else array
        for array, in_hbm in operands
    ]

    def keep(shape):
        return pltpu.VMEM(shape.shape, shape.dtype) if pinned else shape

    return pl.pallas_call(
        kernel,
        out_shape=jax.tree.map(keep, out_shape),
        in_specs=specs,
        out_specs=jax.tree.map(lambda _: anywhere if copied else whole, out_shape),
        scratch_shapes=scratch,
        compiler_params=pltpu.CompilerParams(vmem_limit_bytes=VMEM_LIMIT),
        cost_estimate=cost,
        name=name,
    )(*arrays)


def here(*arrays):
    return [(array, False) for array in arrays]


def in_hbm(*arrays):
    return [(array, True) for array in arrays]


def per_device_paired(ensemble, norm_gain, project_weight, output_weight, conv_kernel, cotangent):
    mem, rows, cols, channels = ensemble.shape
    if rows < 3 or cols % 16 or (2 * mem * rows) % 16:
        return per_device_general(
            ensemble, norm_gain, project_weight, output_weight, conv_kernel, cotangent
        )
    groups = 2 * mem
    slots = 2 * groups
    cells = rows * cols
    lon_count = lax.axis_size("lon")
    lat_count = lax.axis_size("lat")
    bf16 = functools.partial(jax.ShapeDtypeStruct, dtype=BF16)
    f32 = functools.partial(jax.ShapeDtypeStruct, dtype=F32)
    swap = [(0, 1), (1, 0)]
    core_pairs = [(i, i ^ 1) for i in range(lon_count)]
    chip_pairs = [(i, (i - 1 if i % 2 == 0 else i + 1) % lon_count) for i in range(lon_count)]

    def lat_swap(offset):
        pairs = []
        for lat in range(lat_count):
            for lon in range(lon_count):
                to = (lat + 1 if lat % 2 == offset else lat - 1, lon)
                if not 0 <= to[0] < lat_count:
                    to = (lat, lon ^ 1)
                pairs.append((lat * lon_count + lon, to[0] * lon_count + to[1]))
        return pairs

    ends_shape = (2, 2 * mem * rows, channels)
    both, ends = local_call(
        stack_kernel,
        "stack",
        in_hbm(ensemble, cotangent),
        (bf16((2,) + ensemble.shape), bf16(ends_shape)),
        [pltpu.VMEM(ends_shape[1:], F32)] * 2 + [pltpu.SemaphoreType.DMA((2,))],
        pinned=True,
    )
    other_ends = lax.ppermute(ends, "member", swap)
    other = lax.ppermute(both, "member", swap)

    weights = (
        norm_gain.reshape(1, channels),
        project_weight,
        output_weight,
        conv_kernel.reshape(9 * channels, channels),
    )
    *weights, project_t, output_t = local_call(
        load_kernel,
        "load_weights",
        in_hbm(*weights),
        tuple(jax.ShapeDtypeStruct(w.shape, w.dtype) for w in weights)
        + (bf16((3 * channels, channels)), bf16((channels, channels))),
        [pltpu.SemaphoreType.DMA((4,))],
        pinned=True,
        cost=LOAD_COST,
    )
    strip = (slots * rows, channels)
    chip_send, core_send = local_call(
        pack_strips_kernel,
        "pack_strips",
        here(ends, other_ends, weights[0]),
        (bf16(strip), bf16(strip)),
        [pltpu.VMEM(strip, F32)] * 2,
    )
    chip = lax.ppermute(chip_send, "lon", chip_pairs)
    core = lax.ppermute(core_send, "lon", core_pairs)

    *held, updated = local_call(
        own_kernel,
        "own_cells",
        here(both, other, *weights[:3]),
        (
            bf16((groups, cells, 3 * channels)),
            bf16((2, groups, cells, channels)),
            f32((groups * groups, cells, channels)),
            f32((2, mem, cells, channels)),
            f32((2, mem, cells, channels)),
            bf16((mem, cells, channels)),
        ),
        [],
        pinned=True,
    )
    halo = bf16(((mem + groups) * cols + 2 * slots, channels))
    first_send, second_send = local_call(
        pack_rows_kernel,
        "pack_rows",
        here(both, other, chip, core, updated),
        (halo, halo),
        [pltpu.VMEM((2, 2 * slots, channels), F32)],
    )
    first = lax.ppermute(first_send, ("lat", "lon"), lat_swap(0))
    second = lax.ppermute(second_send, ("lat", "lon"), lat_swap(1))

    conv_t, *parts = local_call(
        centre_kernel,
        "centre",
        here(both, other, chip, core, *weights, project_t, output_t, *held, updated),
        (
            bf16((9 * channels, channels)),
            bf16((mem, rows - 2, cols, channels)),
            bf16((mem, rows - 2, cols, channels)),
            f32((mem, 2 * cols, channels)),
            f32((groups, 2 * cols, channels)),
        ),
        [
            pltpu.VMEM((mem, cells, 3 * channels), BF16),
            pltpu.VMEM((groups, cells, 3 * channels), BF16),
            pltpu.VMEM((groups, 16, channels), F32),
        ],
        pinned=True,
        cost=LONG,
    )
    return local_call(
        functools.partial(main_kernel, lat_count=lat_count),
        "main",
        here(both, first, second, *weights, project_t, output_t, conv_t, *held, *parts),
        (bf16(ensemble.shape), bf16(ensemble.shape)),
        [
            pltpu.VMEM((mem, 2 * cols, 3 * channels), BF16),
            pltpu.VMEM((groups, 2 * cols, 3 * channels), BF16),
            pltpu.VMEM((groups, 16, channels), F32),
            pltpu.VMEM((2, 2, mem, cols, channels), BF16),
            pltpu.SemaphoreType.DMA((6,)),
        ],
        copied=True,
    )


def solution(mesh):
    paired = mesh.shape["member"] == 2 and mesh.shape["lon"] % 2 == 0
    per_device = per_device_paired if paired else per_device_general
    in_specs = (
        P("member", "lat", "lon", None),
        P(),
        P(),
        P(),
        P(),
        P("member", "lat", "lon", None),
    )
    out_specs = (P("member", "lat", "lon", None), P("member", "lat", "lon", None))
    return jax.shard_map(
        per_device, mesh=mesh, in_specs=in_specs, out_specs=out_specs, check_vma=False
    )
```

```python
import functools
import math

import jax
import jax.numpy as jnp
from jax import lax
from jax.experimental import pallas as pl
from jax.experimental.pallas import tpu as pltpu
from jax.sharding import PartitionSpec as P

HEAD_COUNT = 8


FLOOR = 0.5
EPSILON = 1e-06


def padded_2(block, sides, width, periodic):
    for axis, dim in sides:
        count = lax.axis_size(axis)
        forward = [(i, i + 1) for i in range(count - 1)]
        if periodic:
            forward.append((count - 1, 0))
        backward = [(target, source) for source, target in forward]
        low = lax.ppermute(
            lax.slice_in_dim(block, block.shape[dim] - width, None, axis=dim), axis, forward
        )
        high = lax.ppermute(lax.slice_in_dim(block, 0, width, axis=dim), axis, backward)
        block = jnp.concatenate([low, block, high], axis=dim)
    return block


def row_norm(values, gain_vec):
    mean_sq = jnp.mean(values * values, axis=-1, keepdims=True)
    return values * lax.rsqrt(mean_sq + EPSILON) * gain_vec


def head_norm(values, head_count):
    shaped = values.reshape(values.shape[:-1] + (head_count, values.shape[-1] // head_count))
    mean_sq = jnp.mean(shaped * shaped, axis=-1, keepdims=True)
    return (shaped * lax.rsqrt(jnp.maximum(mean_sq, FLOOR))).reshape(values.shape)


def split_heads(values, head_count):
    return values.reshape(values.shape[:-1] + (head_count, values.shape[-1] // head_count))


def head_pullback(raw_rows, grad_rows):
    _, pullback = jax.vjp(lambda t: head_norm(t, HEAD_COUNT), raw_rows.astype(jnp.float32))
    return pullback(grad_rows)[0]


def pad_field(field_in):
    widened = padded_2(field_in, (("lon", 2),), 1, True)
    return padded_2(widened, (("lat", 1),), 1, False)


def conv_taps(padded, kernel, lat_n, lon_n, adjoint):
    running = None
    for row_off in range(3):
        for col_off in range(3):
            if adjoint:
                window = padded[
                    :, 2 - row_off : 2 - row_off + lat_n, 2 - col_off : 2 - col_off + lon_n
                ]
                summand = jnp.einsum(
                    "mabc,dc->mabd",
                    window,
                    kernel[row_off, col_off],
                    preferred_element_type=jnp.float32,
                )
            else:
                window = padded[:, row_off : row_off + lat_n, col_off : col_off + lon_n]
                summand = jnp.einsum(
                    "mabc,cd->mabd",
                    window,
                    kernel[row_off, col_off],
                    preferred_element_type=jnp.float32,
                )
            running = summand if running is None else running + summand
    return running


def per_device_general(ensemble, norm_gain, project_weight, output_weight, conv_kernel, cotangent):
    mem_dev, lat_dev, lon_dev, channels = ensemble.shape
    cell_count = lat_dev * lon_dev
    score_scale = 1.0 / math.sqrt(channels // HEAD_COUNT)
    inputs = ensemble.reshape(mem_dev, cell_count, channels).astype(jnp.float32)
    normed = row_norm(inputs, norm_gain).astype(jnp.bfloat16)
    spread = lax.all_to_all(normed, "member", split_axis=1, concat_axis=0, tiled=True)
    projected = jnp.dot(spread, project_weight, preferred_element_type=jnp.float32).astype(
        jnp.bfloat16
    )
    query_raw = projected[..., :channels]
    key_raw = projected[..., channels : 2 * channels]
    value_rows = projected[..., 2 * channels :]
    key_rows = head_norm(key_raw.astype(jnp.float32), HEAD_COUNT).astype(jnp.bfloat16)
    queries = head_norm(query_raw.astype(jnp.float32), HEAD_COUNT).astype(jnp.bfloat16)
    query_heads = split_heads(queries, HEAD_COUNT)
    key_heads = split_heads(key_rows, HEAD_COUNT)
    value_heads = split_heads(value_rows, HEAD_COUNT)
    scores = (
        jnp.einsum("mphd,nphd->mnhp", query_heads, key_heads, preferred_element_type=jnp.float32)
        * score_scale
    )
    expd = jnp.exp(scores)
    soft = expd / jnp.sum(expd, axis=1, keepdims=True)
    rounded = soft.astype(jnp.bfloat16)
    mixed_out = jnp.einsum(
        "mnhp,nphd->mphd", rounded, value_heads, preferred_element_type=jnp.float32
    )
    mixed_out = mixed_out.reshape(query_raw.shape).astype(jnp.bfloat16)
    mixed_out = lax.all_to_all(mixed_out, "member", split_axis=0, concat_axis=1, tiled=True)
    updated = (
        inputs + jnp.dot(mixed_out, output_weight, preferred_element_type=jnp.float32)
    ).astype(jnp.bfloat16)
    field_up = updated.reshape(mem_dev, lat_dev, lon_dev, channels)
    result = field_up.astype(jnp.float32) + conv_taps(
        pad_field(field_up), conv_kernel, lat_dev, lon_dev, False
    )
    result = result.astype(jnp.bfloat16)
    grad_field = cotangent.astype(jnp.float32) + conv_taps(
        pad_field(cotangent), conv_kernel, lat_dev, lon_dev, True
    )
    grad_rows = grad_field.reshape(mem_dev, cell_count, channels)
    grad_mixed = jnp.einsum(
        "mpc,dc->mpd",
        grad_rows.astype(jnp.bfloat16),
        output_weight,
        preferred_element_type=jnp.float32,
    )
    grad_mixed = grad_mixed.astype(jnp.bfloat16)
    grad_mixed = lax.all_to_all(grad_mixed, "member", split_axis=1, concat_axis=0, tiled=True)
    grad_heads = split_heads(grad_mixed, HEAD_COUNT)
    dprob = jnp.einsum(
        "mphd,nphd->mnhp", grad_heads, value_heads, preferred_element_type=jnp.float32
    )
    dscore = (soft * (dprob - jnp.sum(soft * dprob, axis=1, keepdims=True))).astype(jnp.bfloat16)
    query_grad = (
        jnp.einsum("mnhp,nphd->mphd", dscore, key_heads, preferred_element_type=jnp.float32)
        * score_scale
    )
    query_grad = query_grad.reshape(query_raw.shape)
    key_grad = (
        jnp.einsum("mnhp,mphd->nphd", dscore, query_heads, preferred_element_type=jnp.float32)
        * score_scale
    )
    key_grad = key_grad.reshape(key_raw.shape)
    value_grad = jnp.einsum(
        "mnhp,mphd->nphd", rounded, grad_heads, preferred_element_type=jnp.float32
    )
    value_grad = value_grad.reshape(key_raw.shape)
    grad_query_raw = head_pullback(query_raw, query_grad)
    grad_key_raw = head_pullback(key_raw, key_grad)
    grad_proj = jnp.concatenate([grad_query_raw, grad_key_raw, value_grad], axis=-1).astype(
        jnp.bfloat16
    )
    grad_proj = lax.all_to_all(grad_proj, "member", split_axis=0, concat_axis=1, tiled=True)
    grad_normed = jnp.einsum(
        "mpe,ce->mpc", grad_proj, project_weight, preferred_element_type=jnp.float32
    )
    _, pull_norm = jax.vjp(lambda t: row_norm(t, norm_gain), inputs)
    grad_inputs = pull_norm(grad_normed)[0]
    grad_ensemble = (
        (grad_rows + grad_inputs).astype(jnp.bfloat16).reshape(mem_dev, lat_dev, lon_dev, channels)
    )
    return (result, grad_ensemble)


F32 = jnp.float32
BF16 = jnp.bfloat16
VMEM_LIMIT = 24 * 1024 * 1024
LONG = pl.CostEstimate(flops=20_000_000_000, bytes_accessed=4_000_000, transcendentals=0)
MIDDLING = pl.CostEstimate(flops=3_000_000_000, bytes_accessed=2_000_000, transcendentals=0)


def is_even(axis):
    return lax.rem(lax.axis_index(axis), 2) == 0


def load_kernel(
    gain_hbm,
    project_hbm,
    output_hbm,
    conv_hbm,
    gain_ref,
    project_ref,
    output_ref,
    conv_ref,
    project_t_ref,
    output_t_ref,
    sems,
):
    channels = output_ref.shape[0]
    pairs = (
        (gain_hbm, gain_ref),
        (project_hbm, project_ref),
        (output_hbm, output_ref),
        (conv_hbm, conv_ref),
    )
    loads = [
        pltpu.make_async_copy(source, target, sems.at[i])
        for i, (source, target) in enumerate(pairs)
    ]
    for load in loads:
        load.start()
    for load in loads[:3]:
        load.wait()
    output_t_ref[...] = output_ref[...].T
    for kind in range(3):
        lanes = slice(kind * channels, (kind + 1) * channels)
        project_t_ref[lanes, :] = project_ref[:, lanes].T
    loads[3].wait()


def stack_kernel(ens_ref, cot_ref, both_ref, ends_ref, low_scr, high_scr, sems):
    _, mem, rows, cols, _ = both_ref.shape
    copies = [
        pltpu.make_async_copy(ref, both_ref.at[i], sems.at[i])
        for i, ref in enumerate((ens_ref, cot_ref))
    ]
    for copy in copies:
        copy.start()
    for copy in copies:
        copy.wait()
    index = 0
    for array in range(2):
        for member in range(mem):
            for row in range(rows):
                slab = both_ref[array, member, row].astype(F32)
                low_scr[index : index + 1, :] = slab[0:1]
                high_scr[index : index + 1, :] = slab[cols - 1 : cols]
                index += 1
    ends_ref[0] = low_scr[...].astype(BF16)
    ends_ref[1] = high_scr[...].astype(BF16)


def pack_strips_kernel(ends_ref, other_ends_ref, chip_ref, core_ref, low_scr, high_scr):
    part = ends_ref.shape[1] // 2
    for side, scr in ((0, low_scr), (1, high_scr)):
        for group, ref in enumerate((ends_ref, other_ends_ref)):
            column = ref[side].astype(F32)
            for array in range(2):
                at = (2 * array + group) * part
                scr[at : at + part, :] = column[array * part : (array + 1) * part]
    even = is_even("lon")
    low, high = low_scr[...], high_scr[...]
    core_ref[...] = jnp.where(even, high, low).astype(BF16)
    chip_ref[...] = jnp.where(even, low, high).astype(BF16)


def rim_columns(chip_ref, core_ref):
    even = is_even("lon")
    chip, core = chip_ref[...].astype(F32), core_ref[...].astype(F32)
    return jnp.where(even, chip, core), jnp.where(even, core, chip)


def pack_rows_kernel(
    both_ref, other_ref, chip_ref, core_ref, after_ref, first_ref, second_ref, edge_scr
):
    _, mem, rows, cols, _ = both_ref.shape
    slots = 4 * mem
    even = is_even("lat")
    west, east = rim_columns(chip_ref, core_ref)
    for slot in range(slots):
        array, member = divmod(slot, 2 * mem)
        ref, who = (both_ref, member) if member < mem else (other_ref, member - mem)
        start, stop = (ref[array, who, row].astype(F32) for row in (0, rows - 1))
        at = slice(slot * cols, (slot + 1) * cols)
        first_ref[at, :] = jnp.where(even, stop, start).astype(BF16)
        second_ref[at, :] = jnp.where(even, start, stop).astype(BF16)
        top, low = slot * rows, (slot + 1) * rows - 1
        for side, column in enumerate((west, east)):
            place = side * slots + slot
            start, stop = column[top : top + 1], column[low : low + 1]
            edge_scr[0, place : place + 1, :] = jnp.where(even, stop, start)
            edge_scr[1, place : place + 1, :] = jnp.where(even, start, stop)
    first_ref[slots * cols :, :] = edge_scr[0].astype(BF16)
    second_ref[slots * cols :, :] = edge_scr[1].astype(BF16)


def dot_nn(a, b):
    return lax.dot_general(a, b, (((1,), (0,)), ((), ())), preferred_element_type=F32)


def same_head_matrix(channels):
    width = channels // HEAD_COUNT
    lane_row = lax.broadcasted_iota(jnp.int32, (channels, channels), 0) // width
    lane_col = lax.broadcasted_iota(jnp.int32, (channels, channels), 1) // width
    return jnp.where(lane_row == lane_col, 1.0, 0.0).astype(BF16)


def head_sums(values, same_head):
    high = values.astype(BF16)
    low = (values - high.astype(F32)).astype(BF16)
    return dot_nn(high, same_head) + dot_nn(low, same_head)


def rounded_sums(values, same_head):
    return dot_nn(values.astype(BF16), same_head)


def head_units(raw, same_head, sums=head_sums):
    raw = raw.astype(F32)
    mean_sq = sums(raw * raw, same_head) * (HEAD_COUNT / raw.shape[-1])
    inverse = lax.rsqrt(jnp.maximum(mean_sq, FLOOR))
    return raw, mean_sq, inverse, (raw * inverse).astype(BF16)


def row_rsqrt(values):
    return lax.rsqrt(jnp.mean(values * values, axis=-1, keepdims=True) + EPSILON)


def split_rows(array, count):
    size = array.shape[0] // count
    return [array[i * size : (i + 1) * size] for i in range(count)]


def softmax_members(queries, keys, same_head, scale):
    products = [query * key for query in queries for key in keys]
    scores = dot_nn(jnp.concatenate(products, axis=0), same_head) * scale
    exps = split_rows(jnp.exp(scores), len(products))
    soft = []
    for m in range(len(queries)):
        mine = exps[m * len(keys) : (m + 1) * len(keys)]
        total = mine[0]
        for e in mine[1:]:
            total = total + e
        inverse = 1.0 / total
        soft.append([e * inverse for e in mine])
    return soft


def mix_values(probs, values):
    mixed = None
    for prob, value in zip(probs, values):
        term = prob.astype(BF16).astype(F32) * value.astype(F32)
        mixed = term if mixed is None else mixed + term
    return mixed.astype(BF16)


def forward_cells(x, mem, groups, gain, project_ref, output_ref, same_head):
    channels = x.shape[-1]
    own_rows = x.shape[0] // groups * mem
    scale = 1.0 / math.sqrt(channels // HEAD_COUNT)
    normed = (x * row_rsqrt(x) * gain).astype(BF16)
    query_raw = dot_nn(normed[:own_rows], project_ref[:, :channels]).astype(BF16)
    key_raw = dot_nn(normed, project_ref[:, channels : 2 * channels]).astype(BF16)
    values = dot_nn(normed, project_ref[:, 2 * channels :]).astype(BF16)
    yield
    raw = jnp.concatenate([query_raw, key_raw], axis=0)
    units = head_units(raw, same_head, rounded_sums)[3]
    yield
    queries = split_rows(units[:own_rows], mem)
    keys = split_rows(units[own_rows:], groups)
    values = split_rows(values, groups)
    soft = softmax_members(queries, keys, same_head, scale)
    yield
    mixed = jnp.concatenate([mix_values(soft[m], values) for m in range(mem)], axis=0)
    return (x[:own_rows] + dot_nn(mixed, output_ref[...])).astype(BF16)


def together(*chains):
    results = [None] * len(chains)
    active = list(range(len(chains)))
    while active:
        for i in list(active):
            try:
                next(chains[i])
            except StopIteration as stop:
                results[i] = stop.value
                active.remove(i)
    return results


def run(chain):
    while True:
        try:
            next(chain)
        except StopIteration as stop:
            return stop.value


def shift_row(scr, member, place, slab, west, east):
    cols, channels = slab.shape
    column = lax.broadcasted_iota(jnp.int32, (cols, channels), 0)
    back = jnp.where(column == 0, west, pltpu.roll(slab, 1, 0))
    ahead = jnp.where(column == cols - 1, east, pltpu.roll(slab, cols - 1, 0))
    rows_at = slice(place * cols, (place + 1) * cols)
    scr[member, rows_at, :channels] = back.astype(BF16)
    scr[member, rows_at, channels : 2 * channels] = slab.astype(BF16)
    scr[member, rows_at, 2 * channels :] = ahead.astype(BF16)


def tap_rows(taps_ref, r):
    size = taps_ref.shape[0] // 3
    return taps_ref[r * size : (r + 1) * size, :]


def own_kernel(
    both_ref,
    other_ref,
    gain_ref,
    project_ref,
    output_ref,
    after_ref,
    proj_ref,
    unit_ref,
    soft_ref,
    inverse_ref,
    pull_ref,
    updated_ref,
):
    _, mem, rows, cols, channels = both_ref.shape
    groups = 2 * mem
    cells = rows * cols
    width = channels // HEAD_COUNT
    scale = 1.0 / math.sqrt(width)
    same_head = same_head_matrix(channels)
    own = both_ref[0].reshape(mem * cells, channels)
    other = other_ref[0].reshape(mem * cells, channels)
    x = jnp.concatenate([own, other], axis=0).astype(F32)
    normed = (x * row_rsqrt(x) * gain_ref[...]).astype(BF16)
    proj = dot_nn(normed, project_ref[...]).astype(BF16)
    proj_ref[...] = proj.reshape(groups, cells, 3 * channels)
    both_raw = jnp.concatenate([proj[:, :channels], proj[:, channels : 2 * channels]], axis=0)
    raw, mean_sq, inverse, units = head_units(both_raw, same_head)
    unit_ref[...] = units.reshape(2, groups, cells, channels)
    active = jnp.where(mean_sq > FLOOR, 1.0, jnp.where(mean_sq == FLOOR, 0.5, 0.0))
    pull = active * raw * (inverse * inverse * inverse) / width
    for kind in range(2):
        at = kind * groups * cells
        mine = slice(at, at + mem * cells)
        inverse_ref[kind] = inverse[mine].reshape(mem, cells, channels)
        pull_ref[kind] = pull[mine].reshape(mem, cells, channels)
    units = split_rows(units, 2 * groups)
    soft = softmax_members(units[:groups], units[groups:], same_head, scale)
    for m in range(groups):
        for n in range(groups):
            soft_ref[m * groups + n] = soft[m][n]
    values = split_rows(proj[:, 2 * channels :], groups)
    mixed = jnp.concatenate([mix_values(soft[m], values) for m in range(mem)], axis=0)
    updated = x[: mem * cells] + dot_nn(mixed, output_ref[...])
    updated_ref[...] = updated.astype(BF16).reshape(mem, cells, channels)


def backward_cells(
    pick, grad_field, x, gain, weights_t, proj_ref, unit_ref, soft_ref, inverse_ref, pull_ref
):
    project_t_ref, output_t_ref = weights_t
    groups = proj_ref.shape[0]
    mem = inverse_ref.shape[1]
    channels = x.shape[-1]
    scale = 1.0 / math.sqrt(channels // HEAD_COUNT)
    same_head = same_head_matrix(channels)
    grad_mixed = dot_nn(grad_field.astype(BF16), output_t_ref[...]).astype(BF16)
    grads = split_rows(grad_mixed, groups)
    yield
    values = [pick(proj_ref[n, :, 2 * channels :]) for n in range(groups)]
    products = [grads[m] * values[n] for m in range(groups) for n in range(groups)]
    dprobs = split_rows(dot_nn(jnp.concatenate(products, axis=0), same_head), len(products))
    yield
    units = [[pick(unit_ref[k, n]).astype(F32) for n in range(groups)] for k in range(2)]
    query_grad = [None] * mem
    key_grad = [None] * mem
    value_grad = [None] * mem
    for m in range(groups):
        soft = [pick(soft_ref[m * groups + n]) for n in range(groups)]
        dprob = dprobs[m * groups : (m + 1) * groups]
        mean = soft[0] * dprob[0]
        for n in range(1, groups):
            mean = mean + soft[n] * dprob[n]
        for n in range(groups):
            if m >= mem and n >= mem:
                continue
            dscore = soft[n] * (dprob[n] - mean)
            if m < mem:
                term = dscore * units[1][n]
                query_grad[m] = term if query_grad[m] is None else query_grad[m] + term
            if n < mem:
                term = dscore * units[0][m]
                key_grad[n] = term if key_grad[n] is None else key_grad[n] + term
                term = soft[n] * grads[m].astype(F32)
                value_grad[n] = term if value_grad[n] is None else value_grad[n] + term

    unit_grads = [jnp.concatenate(g, axis=0) * scale for g in (query_grad, key_grad)]

    def members(take):
        return jnp.concatenate([pick(take(m)) for m in range(mem)], axis=0)

    raws = []
    for kind in range(2):
        lanes = slice(kind * channels, (kind + 1) * channels)
        raws.append(members(lambda m: proj_ref[m, :, lanes]).astype(F32))
    inner = rounded_sums(
        jnp.concatenate([g * raw for g, raw in zip(unit_grads, raws)], axis=0), same_head
    )
    inner = split_rows(inner, 2)
    yield
    pulled = []
    for kind in range(2):
        inverse = members(lambda m: inverse_ref[kind, m])
        pull = members(lambda m: pull_ref[kind, m])
        pulled.append((inverse * unit_grads[kind] - pull * inner[kind]).astype(BF16))
    pulled.append(jnp.concatenate(value_grad, axis=0).astype(BF16))
    grad_normed = dot_nn(jnp.concatenate(pulled, axis=1), project_t_ref[...]) * gain
    yield
    inverse = row_rsqrt(x)
    inner = jnp.mean(x * grad_normed, axis=-1, keepdims=True)
    total = grad_field[: x.shape[0]] + inverse * grad_normed
    return (total - x * (inverse * inverse * inverse * inner)).astype(BF16)


def centre_kernel(
    both_ref,
    other_ref,
    chip_ref,
    core_ref,
    gain_ref,
    project_ref,
    output_ref,
    conv_ref,
    project_t_ref,
    output_t_ref,
    proj_ref,
    unit_ref,
    soft_ref,
    inverse_ref,
    pull_ref,
    updated_ref,
    conv_t_ref,
    result_ref,
    grad_ref,
    result_part_ref,
    grad_part_ref,
    shift_scr,
    cot_shift_scr,
    strip_scr,
):
    _, mem, rows, cols, channels = both_ref.shape
    groups = 2 * mem
    cells = rows * cols
    gain = gain_ref[...]
    same_head = same_head_matrix(channels)
    west, east = rim_columns(chip_ref, core_ref)
    for r in range(3):
        for c in range(3):
            tap = (3 * r + c) * channels
            turned = (3 * r + 2 - c) * channels
            conv_t_ref[turned : turned + channels, :] = conv_ref[tap : tap + channels, :].T

    def convolve(scr, count, start, taps_ref, turned):
        sums = [
            [start[(m * rows + a) * cols : (m * rows + a + 1) * cols] for a in range(rows)]
            for m in range(count)
        ]
        for r in range(3):
            step = 1 - r if turned else r - 1
            outs = [a for a in range(rows) if 0 <= a + step < rows]
            begin, end = outs[0] + step, outs[-1] + step + 1
            window = jnp.concatenate(
                [scr[m, begin * cols : end * cols, :] for m in range(count)], axis=0
            )
            terms = split_rows(dot_nn(window, tap_rows(taps_ref, r)), count * len(outs))
            for m in range(count):
                for i, a in enumerate(outs):
                    sums[m][a] = sums[m][a] + terms[m * len(outs) + i]
        return sums

    cots = []
    for member in range(groups):
        for row in range(rows):
            ref, who = (both_ref, member) if member < mem else (other_ref, member - mem)
            slab = ref[1, who, row].astype(F32)
            cots.append(slab)
            at = (groups + member) * rows + row
            shift_row(cot_shift_scr, member, row, slab, west[at : at + 1], east[at : at + 1])
    sums = convolve(cot_shift_scr, groups, jnp.concatenate(cots, axis=0), conv_t_ref, True)
    for member in range(groups):
        grad_part_ref[member, :cols, :] = sums[member][0]
        grad_part_ref[member, cols:, :] = sums[member][rows - 1]
    grad_field = jnp.concatenate([slab for s in sums for slab in s[1 : rows - 1]], axis=0)

    for member in range(groups):
        at = member * rows
        strip_scr[member] = jnp.zeros((16, channels), F32)
        strip_scr[member, :rows, :] = west[at : at + rows]
        strip_scr[member, 8 : 8 + rows, :] = east[at : at + rows]
    x = strip_scr[...].reshape(groups * 16, channels)
    forward = forward_cells(x, mem, groups, gain, project_ref, output_ref, same_head)
    x = both_ref[0, :, 1 : rows - 1].reshape(mem * (cells - 2 * cols), channels).astype(F32)
    backward = backward_cells(
        lambda array: array[cols : cells - cols],
        grad_field,
        x,
        gain,
        (project_t_ref, output_t_ref),
        proj_ref,
        unit_ref,
        soft_ref,
        inverse_ref,
        pull_ref,
    )
    fresh, total = run(forward), run(backward)
    fresh = split_rows(fresh.astype(F32), mem)
    grad_ref[...] = total.reshape(mem, rows - 2, cols, channels)

    for member in range(mem):
        for row in range(rows):
            slab = updated_ref[member, row * cols : (row + 1) * cols, :].astype(F32)
            ends = fresh[member][row : row + 1], fresh[member][8 + row : 9 + row]
            shift_row(shift_scr, member, row, slab, *ends)
    start = updated_ref[...].reshape(mem * cells, channels).astype(F32)
    sums = convolve(shift_scr, mem, start, conv_ref, False)
    for member in range(mem):
        result_part_ref[member, :cols, :] = sums[member][0]
        result_part_ref[member, cols:, :] = sums[member][rows - 1]
        for row in range(1, rows - 1):
            result_ref[member, row - 1] = sums[member][row].astype(BF16)


def main_kernel(
    both_ref,
    second_ref,
    first_ref,
    gain_ref,
    project_ref,
    output_ref,
    conv_ref,
    project_t_ref,
    output_t_ref,
    conv_t_ref,
    proj_ref,
    unit_ref,
    soft_ref,
    inverse_ref,
    pull_ref,
    inner_result_ref,
    inner_grad_ref,
    result_part_ref,
    grad_part_ref,
    result_ref,
    grad_ref,
    shift_scr,
    cot_shift_scr,
    corner_scr,
    outer_scr,
    sems,
    *,
    lat_count,
):
    _, mem, rows, cols, channels = both_ref.shape
    copies = []
    for i, (ref, out_ref) in enumerate(
        ((inner_result_ref, result_ref), (inner_grad_ref, grad_ref))
    ):
        copy = pltpu.make_async_copy(ref, out_ref.at[:, pl.ds(1, rows - 2)], sems.at[i])
        copy.start()
        copies.append(copy)
    groups = 2 * mem
    slots = 2 * groups
    cells = rows * cols
    gain = gain_ref[...]
    same_head = same_head_matrix(channels)
    lat_even = is_even("lat")
    lat = lax.axis_index("lat")

    def halos(at):
        first, second = first_ref[at, :].astype(F32), second_ref[at, :].astype(F32)
        north = jnp.where(lat == 0, 0.0, jnp.where(lat_even, second, first))
        south = jnp.where(lat == lat_count - 1, 0.0, jnp.where(lat_even, first, second))
        return north, south

    halo = [halos(slice(slot * cols, (slot + 1) * cols)) for slot in range(slots)]
    corners = halos(slice(slots * cols, slots * cols + 2 * slots))

    def corner(side, slot, end):
        at = end * slots + slot
        return corners[side][at : at + 1]

    def halo_part(scr, count, taps_ref, turned):
        north, south = (2, 0) if turned else (0, 2)
        parts = []
        for side, r in ((0, north), (1, south)):
            window = jnp.concatenate(
                [scr[m, side * cols : (side + 1) * cols, :] for m in range(count)], axis=0
            )
            parts.append(split_rows(dot_nn(window, tap_rows(taps_ref, r)), count))
        return jnp.concatenate([parts[side][m] for m in range(count) for side in (0, 1)], axis=0)

    for member in range(groups):
        slot = groups + member
        for side in (0, 1):
            ends = corner(side, slot, 0), corner(side, slot, 1)
            shift_row(cot_shift_scr, member, side, halo[slot][side], *ends)
    grad_field = grad_part_ref[...].reshape(groups * 2 * cols, channels)
    grad_field = grad_field + halo_part(cot_shift_scr, groups, conv_t_ref, True)

    blocks = []
    for member in range(groups):
        corner_scr[member] = jnp.zeros((16, channels), F32)
        for side in (0, 1):
            for end in (0, 1):
                at = 2 * side + end
                corner_scr[member, at : at + 1, :] = corner(side, member, end)
        blocks += [halo[member][0], halo[member][1], corner_scr[member]]
    x = jnp.concatenate(blocks, axis=0)
    forward = forward_cells(x, mem, groups, gain, project_ref, output_ref, same_head)
    x = [both_ref[0, m, row] for m in range(mem) for row in (0, rows - 1)]
    backward = backward_cells(
        lambda array: jnp.concatenate([array[:cols], array[cells - cols :]], axis=0),
        grad_field,
        jnp.concatenate(x, axis=0).astype(F32),
        gain,
        (project_t_ref, output_t_ref),
        proj_ref,
        unit_ref,
        soft_ref,
        inverse_ref,
        pull_ref,
    )

    def finish_result(chain):
        fresh = yield from chain
        fresh = split_rows(fresh.astype(F32), mem)
        for member in range(mem):
            for side in (0, 1):
                slab = fresh[member][side * cols : (side + 1) * cols]
                at = 2 * cols + 2 * side
                ends = fresh[member][at : at + 1], fresh[member][at + 1 : at + 2]
                shift_row(shift_scr, member, side, slab, *ends)
        yield
        outer = result_part_ref[...].reshape(mem * 2 * cols, channels)
        outer = (outer + halo_part(shift_scr, mem, conv_ref, False)).astype(BF16)
        store_outer(0, outer)

    def store_outer(which, outer):
        for i, slab in enumerate(split_rows(outer, 2 * mem)):
            outer_scr[which, i % 2, i // 2] = slab
        for side, row in ((0, 0), (1, rows - 1)):
            copy = pltpu.make_async_copy(
                outer_scr.at[which, side],
                (result_ref, grad_ref)[which].at[:, row],
                sems.at[2 + 2 * which + side],
            )
            copy.start()
            copies.append(copy)

    total, _ = together(backward, finish_result(forward))
    store_outer(1, total)
    for copy in copies:
        copy.wait()


def local_call(kernel, name, operands, out_shape, scratch, pinned=False, cost=None, copied=False):
    whole = pl.BlockSpec(memory_space=pltpu.VMEM)
    anywhere = pl.BlockSpec(memory_space=pl.ANY)
    specs = [anywhere if in_hbm else whole for _, in_hbm in operands]
    arrays = [
        pltpu.with_memory_space_constraint(array, pltpu.HBM) if in_hbm else array
        for array, in_hbm in operands
    ]

    def keep(shape):
        return pltpu.VMEM(shape.shape, shape.dtype) if pinned else shape

    return pl.pallas_call(
        kernel,
        out_shape=jax.tree.map(keep, out_shape),
        in_specs=specs,
        out_specs=jax.tree.map(lambda _: anywhere if copied else whole, out_shape),
        scratch_shapes=scratch,
        compiler_params=pltpu.CompilerParams(vmem_limit_bytes=VMEM_LIMIT),
        cost_estimate=cost,
        name=name,
    )(*arrays)


def here(*arrays):
    return [(array, False) for array in arrays]


def in_hbm(*arrays):
    return [(array, True) for array in arrays]


def per_device_paired(ensemble, norm_gain, project_weight, output_weight, conv_kernel, cotangent):
    mem, rows, cols, channels = ensemble.shape
    if rows < 3 or cols % 16 or (2 * mem * rows) % 16:
        return per_device_general(
            ensemble, norm_gain, project_weight, output_weight, conv_kernel, cotangent
        )
    groups = 2 * mem
    slots = 2 * groups
    cells = rows * cols
    lon_count = lax.axis_size("lon")
    lat_count = lax.axis_size("lat")
    bf16 = functools.partial(jax.ShapeDtypeStruct, dtype=BF16)
    f32 = functools.partial(jax.ShapeDtypeStruct, dtype=F32)
    swap = [(0, 1), (1, 0)]
    core_pairs = [(i, i ^ 1) for i in range(lon_count)]
    chip_pairs = [(i, (i - 1 if i % 2 == 0 else i + 1) % lon_count) for i in range(lon_count)]

    def lat_swap(offset):
        pairs = []
        for lat in range(lat_count):
            for lon in range(lon_count):
                to = (lat + 1 if lat % 2 == offset else lat - 1, lon)
                if not 0 <= to[0] < lat_count:
                    to = (lat, lon ^ 1)
                pairs.append((lat * lon_count + lon, to[0] * lon_count + to[1]))
        return pairs

    ends_shape = (2, 2 * mem * rows, channels)
    both, ends = local_call(
        stack_kernel,
        "stack",
        in_hbm(ensemble, cotangent),
        (bf16((2,) + ensemble.shape), bf16(ends_shape)),
        [pltpu.VMEM(ends_shape[1:], F32)] * 2 + [pltpu.SemaphoreType.DMA((2,))],
        pinned=True,
    )
    other_ends = lax.ppermute(ends, "member", swap)
    other = lax.ppermute(both, "member", swap)

    strip = (slots * rows, channels)
    chip_send, core_send = local_call(
        pack_strips_kernel,
        "pack_strips",
        here(ends, other_ends),
        (bf16(strip), bf16(strip)),
        [pltpu.VMEM(strip, F32)] * 2,
    )
    chip = lax.ppermute(chip_send, "lon", chip_pairs)
    core = lax.ppermute(core_send, "lon", core_pairs)

    weights = (
        norm_gain.reshape(1, channels),
        project_weight,
        output_weight,
        conv_kernel.reshape(9 * channels, channels),
    )
    *weights, project_t, output_t = local_call(
        load_kernel,
        "load_weights",
        in_hbm(*weights),
        tuple(jax.ShapeDtypeStruct(w.shape, w.dtype) for w in weights)
        + (bf16((3 * channels, channels)), bf16((channels, channels))),
        [pltpu.SemaphoreType.DMA((4,))],
        pinned=True,
        cost=MIDDLING,
    )
    halo = bf16((slots * (cols + 2), channels))
    first_send, second_send = local_call(
        pack_rows_kernel,
        "pack_rows",
        here(both, other, chip, core, weights[0]),
        (halo, halo),
        [pltpu.VMEM((2, 2 * slots, channels), F32)],
    )
    first = lax.ppermute(first_send, ("lat", "lon"), lat_swap(0))
    second = lax.ppermute(second_send, ("lat", "lon"), lat_swap(1))

    *held, updated = local_call(
        own_kernel,
        "own_cells",
        here(both, other, *weights[:3], second_send),
        (
            bf16((groups, cells, 3 * channels)),
            bf16((2, groups, cells, channels)),
            f32((groups * groups, cells, channels)),
            f32((2, mem, cells, channels)),
            f32((2, mem, cells, channels)),
            bf16((mem, cells, channels)),
        ),
        [],
        pinned=True,
        cost=LONG,
    )
    conv_t, *parts = local_call(
        centre_kernel,
        "centre",
        here(both, other, chip, core, *weights, project_t, output_t, *held, updated),
        (
            bf16((9 * channels, channels)),
            bf16((mem, rows - 2, cols, channels)),
            bf16((mem, rows - 2, cols, channels)),
            f32((mem, 2 * cols, channels)),
            f32((groups, 2 * cols, channels)),
        ),
        [
            pltpu.VMEM((mem, cells, 3 * channels), BF16),
            pltpu.VMEM((groups, cells, 3 * channels), BF16),
            pltpu.VMEM((groups, 16, channels), F32),
        ],
        pinned=True,
        cost=LONG,
    )
    return local_call(
        functools.partial(main_kernel, lat_count=lat_count),
        "main",
        here(both, second, first, *weights, project_t, output_t, conv_t, *held, *parts),
        (bf16(ensemble.shape), bf16(ensemble.shape)),
        [
            pltpu.VMEM((mem, 2 * cols, 3 * channels), BF16),
            pltpu.VMEM((groups, 2 * cols, 3 * channels), BF16),
            pltpu.VMEM((groups, 16, channels), F32),
            pltpu.VMEM((2, 2, mem, cols, channels), BF16),
            pltpu.SemaphoreType.DMA((6,)),
        ],
        copied=True,
    )


def solution(mesh):
    paired = mesh.shape["member"] == 2 and mesh.shape["lon"] % 2 == 0
    per_device = per_device_paired if paired else per_device_general
    in_specs = (
        P("member", "lat", "lon", None),
        P(),
        P(),
        P(),
        P(),
        P("member", "lat", "lon", None),
    )
    out_specs = (P("member", "lat", "lon", None), P("member", "lat", "lon", None))
    return jax.shard_map(
        per_device, mesh=mesh, in_specs=in_specs, out_specs=out_specs, check_vma=False
    )
```

```python
import functools
import math

import jax
import jax.numpy as jnp
from jax import lax
from jax.experimental import pallas as pl
from jax.experimental.pallas import tpu as pltpu
from jax.sharding import PartitionSpec as P

HEAD_COUNT = 8


FLOOR = 0.5
EPSILON = 1e-06


def padded_2(block, sides, width, periodic):
    for axis, dim in sides:
        count = lax.axis_size(axis)
        forward = [(i, i + 1) for i in range(count - 1)]
        if periodic:
            forward.append((count - 1, 0))
        backward = [(target, source) for source, target in forward]
        low = lax.ppermute(
            lax.slice_in_dim(block, block.shape[dim] - width, None, axis=dim), axis, forward
        )
        high = lax.ppermute(lax.slice_in_dim(block, 0, width, axis=dim), axis, backward)
        block = jnp.concatenate([low, block, high], axis=dim)
    return block


def row_norm(values, gain_vec):
    mean_sq = jnp.mean(values * values, axis=-1, keepdims=True)
    return values * lax.rsqrt(mean_sq + EPSILON) * gain_vec


def head_norm(values, head_count):
    shaped = values.reshape(values.shape[:-1] + (head_count, values.shape[-1] // head_count))
    mean_sq = jnp.mean(shaped * shaped, axis=-1, keepdims=True)
    return (shaped * lax.rsqrt(jnp.maximum(mean_sq, FLOOR))).reshape(values.shape)


def split_heads(values, head_count):
    return values.reshape(values.shape[:-1] + (head_count, values.shape[-1] // head_count))


def head_pullback(raw_rows, grad_rows):
    _, pullback = jax.vjp(lambda t: head_norm(t, HEAD_COUNT), raw_rows.astype(jnp.float32))
    return pullback(grad_rows)[0]


def pad_field(field_in):
    widened = padded_2(field_in, (("lon", 2),), 1, True)
    return padded_2(widened, (("lat", 1),), 1, False)


def conv_taps(padded, kernel, lat_n, lon_n, adjoint):
    running = None
    for row_off in range(3):
        for col_off in range(3):
            if adjoint:
                window = padded[
                    :, 2 - row_off : 2 - row_off + lat_n, 2 - col_off : 2 - col_off + lon_n
                ]
                summand = jnp.einsum(
                    "mabc,dc->mabd",
                    window,
                    kernel[row_off, col_off],
                    preferred_element_type=jnp.float32,
                )
            else:
                window = padded[:, row_off : row_off + lat_n, col_off : col_off + lon_n]
                summand = jnp.einsum(
                    "mabc,cd->mabd",
                    window,
                    kernel[row_off, col_off],
                    preferred_element_type=jnp.float32,
                )
            running = summand if running is None else running + summand
    return running


def per_device_general(ensemble, norm_gain, project_weight, output_weight, conv_kernel, cotangent):
    mem_dev, lat_dev, lon_dev, channels = ensemble.shape
    cell_count = lat_dev * lon_dev
    score_scale = 1.0 / math.sqrt(channels // HEAD_COUNT)
    inputs = ensemble.reshape(mem_dev, cell_count, channels).astype(jnp.float32)
    normed = row_norm(inputs, norm_gain).astype(jnp.bfloat16)
    spread = lax.all_to_all(normed, "member", split_axis=1, concat_axis=0, tiled=True)
    projected = jnp.dot(spread, project_weight, preferred_element_type=jnp.float32).astype(
        jnp.bfloat16
    )
    query_raw = projected[..., :channels]
    key_raw = projected[..., channels : 2 * channels]
    value_rows = projected[..., 2 * channels :]
    key_rows = head_norm(key_raw.astype(jnp.float32), HEAD_COUNT).astype(jnp.bfloat16)
    queries = head_norm(query_raw.astype(jnp.float32), HEAD_COUNT).astype(jnp.bfloat16)
    query_heads = split_heads(queries, HEAD_COUNT)
    key_heads = split_heads(key_rows, HEAD_COUNT)
    value_heads = split_heads(value_rows, HEAD_COUNT)
    scores = (
        jnp.einsum("mphd,nphd->mnhp", query_heads, key_heads, preferred_element_type=jnp.float32)
        * score_scale
    )
    expd = jnp.exp(scores)
    soft = expd / jnp.sum(expd, axis=1, keepdims=True)
    rounded = soft.astype(jnp.bfloat16)
    mixed_out = jnp.einsum(
        "mnhp,nphd->mphd", rounded, value_heads, preferred_element_type=jnp.float32
    )
    mixed_out = mixed_out.reshape(query_raw.shape).astype(jnp.bfloat16)
    mixed_out = lax.all_to_all(mixed_out, "member", split_axis=0, concat_axis=1, tiled=True)
    updated = (
        inputs + jnp.dot(mixed_out, output_weight, preferred_element_type=jnp.float32)
    ).astype(jnp.bfloat16)
    field_up = updated.reshape(mem_dev, lat_dev, lon_dev, channels)
    result = field_up.astype(jnp.float32) + conv_taps(
        pad_field(field_up), conv_kernel, lat_dev, lon_dev, False
    )
    result = result.astype(jnp.bfloat16)
    grad_field = cotangent.astype(jnp.float32) + conv_taps(
        pad_field(cotangent), conv_kernel, lat_dev, lon_dev, True
    )
    grad_rows = grad_field.reshape(mem_dev, cell_count, channels)
    grad_mixed = jnp.einsum(
        "mpc,dc->mpd",
        grad_rows.astype(jnp.bfloat16),
        output_weight,
        preferred_element_type=jnp.float32,
    )
    grad_mixed = grad_mixed.astype(jnp.bfloat16)
    grad_mixed = lax.all_to_all(grad_mixed, "member", split_axis=1, concat_axis=0, tiled=True)
    grad_heads = split_heads(grad_mixed, HEAD_COUNT)
    dprob = jnp.einsum(
        "mphd,nphd->mnhp", grad_heads, value_heads, preferred_element_type=jnp.float32
    )
    dscore = (soft * (dprob - jnp.sum(soft * dprob, axis=1, keepdims=True))).astype(jnp.bfloat16)
    query_grad = (
        jnp.einsum("mnhp,nphd->mphd", dscore, key_heads, preferred_element_type=jnp.float32)
        * score_scale
    )
    query_grad = query_grad.reshape(query_raw.shape)
    key_grad = (
        jnp.einsum("mnhp,mphd->nphd", dscore, query_heads, preferred_element_type=jnp.float32)
        * score_scale
    )
    key_grad = key_grad.reshape(key_raw.shape)
    value_grad = jnp.einsum(
        "mnhp,mphd->nphd", rounded, grad_heads, preferred_element_type=jnp.float32
    )
    value_grad = value_grad.reshape(key_raw.shape)
    grad_query_raw = head_pullback(query_raw, query_grad)
    grad_key_raw = head_pullback(key_raw, key_grad)
    grad_proj = jnp.concatenate([grad_query_raw, grad_key_raw, value_grad], axis=-1).astype(
        jnp.bfloat16
    )
    grad_proj = lax.all_to_all(grad_proj, "member", split_axis=0, concat_axis=1, tiled=True)
    grad_normed = jnp.einsum(
        "mpe,ce->mpc", grad_proj, project_weight, preferred_element_type=jnp.float32
    )
    _, pull_norm = jax.vjp(lambda t: row_norm(t, norm_gain), inputs)
    grad_inputs = pull_norm(grad_normed)[0]
    grad_ensemble = (
        (grad_rows + grad_inputs).astype(jnp.bfloat16).reshape(mem_dev, lat_dev, lon_dev, channels)
    )
    return (result, grad_ensemble)


F32 = jnp.float32
BF16 = jnp.bfloat16
VMEM_LIMIT = 24 * 1024 * 1024
LONG = pl.CostEstimate(flops=20_000_000_000, bytes_accessed=4_000_000, transcendentals=0)
MIDDLING = pl.CostEstimate(flops=3_000_000_000, bytes_accessed=2_000_000, transcendentals=0)


def is_even(axis):
    return lax.rem(lax.axis_index(axis), 2) == 0


def load_pairs(pairs, sems):
    loads = [
        pltpu.make_async_copy(source, target, sems.at[i])
        for i, (source, target) in enumerate(pairs)
    ]
    for load in loads:
        load.start()
    return loads


def load_output_kernel(
    both_ref, gain_hbm, output_hbm, block_ref, gain_ref, output_ref, output_t_ref, sems
):
    loads = load_pairs(((gain_hbm, gain_ref), (output_hbm, output_ref)), sems)
    block_ref[...] = both_ref[...]
    for load in loads:
        load.wait()
    output_t_ref[...] = output_ref[...].T


def load_kernel(project_hbm, conv_hbm, project_ref, conv_ref, project_t_ref, sems):
    loads = load_pairs(((project_hbm, project_ref), (conv_hbm, conv_ref)), sems)
    loads[0].wait()
    channels = project_ref.shape[0]
    for kind in range(3):
        lanes = slice(kind * channels, (kind + 1) * channels)
        project_t_ref[lanes, :] = project_ref[:, lanes].T
    loads[1].wait()


def stack_kernel(ens_ref, cot_ref, both_ref, ends_ref, low_scr, high_scr, sems):
    _, mem, rows, cols, _ = both_ref.shape
    copies = [
        pltpu.make_async_copy(ref, both_ref.at[i], sems.at[i])
        for i, ref in enumerate((ens_ref, cot_ref))
    ]
    for copy in copies:
        copy.start()
    for copy in copies:
        copy.wait()
    index = 0
    for array in range(2):
        for member in range(mem):
            for row in range(rows):
                slab = both_ref[array, member, row].astype(F32)
                low_scr[index : index + 1, :] = slab[0:1]
                high_scr[index : index + 1, :] = slab[cols - 1 : cols]
                index += 1
    ends_ref[0] = low_scr[...].astype(BF16)
    ends_ref[1] = high_scr[...].astype(BF16)


def pack_strips_kernel(ends_ref, other_ends_ref, chip_ref, core_ref, low_scr, high_scr):
    part = ends_ref.shape[1] // 2
    for side, scr in ((0, low_scr), (1, high_scr)):
        for group, ref in enumerate((ends_ref, other_ends_ref)):
            column = ref[side].astype(F32)
            for array in range(2):
                at = (2 * array + group) * part
                scr[at : at + part, :] = column[array * part : (array + 1) * part]
    even = is_even("lon")
    low, high = low_scr[...], high_scr[...]
    core_ref[...] = jnp.where(even, high, low).astype(BF16)
    chip_ref[...] = jnp.where(even, low, high).astype(BF16)


def rim_columns(chip_ref, core_ref):
    even = is_even("lon")
    chip, core = chip_ref[...].astype(F32), core_ref[...].astype(F32)
    return jnp.where(even, chip, core), jnp.where(even, core, chip)


def pack_rows_kernel(
    both_ref, other_ref, chip_ref, core_ref, after_ref, first_ref, second_ref, edge_scr
):
    _, mem, rows, cols, _ = both_ref.shape
    slots = 4 * mem
    even = is_even("lat")
    west, east = rim_columns(chip_ref, core_ref)
    for slot in range(slots):
        array, member = divmod(slot, 2 * mem)
        ref, who = (both_ref, member) if member < mem else (other_ref, member - mem)
        start, stop = (ref[array, who, row].astype(F32) for row in (0, rows - 1))
        at = slice(slot * cols, (slot + 1) * cols)
        first_ref[at, :] = jnp.where(even, stop, start).astype(BF16)
        second_ref[at, :] = jnp.where(even, start, stop).astype(BF16)
        top, low = slot * rows, (slot + 1) * rows - 1
        for side, column in enumerate((west, east)):
            place = side * slots + slot
            start, stop = column[top : top + 1], column[low : low + 1]
            edge_scr[0, place : place + 1, :] = jnp.where(even, stop, start)
            edge_scr[1, place : place + 1, :] = jnp.where(even, start, stop)
    first_ref[slots * cols :, :] = edge_scr[0].astype(BF16)
    second_ref[slots * cols :, :] = edge_scr[1].astype(BF16)


def dot_nn(a, b):
    return lax.dot_general(a, b, (((1,), (0,)), ((), ())), preferred_element_type=F32)


def same_head_matrix(channels):
    width = channels // HEAD_COUNT
    lane_row = lax.broadcasted_iota(jnp.int32, (channels, channels), 0) // width
    lane_col = lax.broadcasted_iota(jnp.int32, (channels, channels), 1) // width
    return jnp.where(lane_row == lane_col, 1.0, 0.0).astype(BF16)


def head_sums(values, same_head):
    high = values.astype(BF16)
    low = (values - high.astype(F32)).astype(BF16)
    return dot_nn(high, same_head) + dot_nn(low, same_head)


def rounded_sums(values, same_head):
    return dot_nn(values.astype(BF16), same_head)


def head_units(raw, same_head, sums=head_sums):
    raw = raw.astype(F32)
    mean_sq = sums(raw * raw, same_head) * (HEAD_COUNT / raw.shape[-1])
    inverse = lax.rsqrt(jnp.maximum(mean_sq, FLOOR))
    return raw, mean_sq, inverse, (raw * inverse).astype(BF16)


def row_rsqrt(values):
    return lax.rsqrt(jnp.mean(values * values, axis=-1, keepdims=True) + EPSILON)


def split_rows(array, count):
    size = array.shape[0] // count
    return [array[i * size : (i + 1) * size] for i in range(count)]


def softmax_members(queries, keys, same_head, scale):
    products = [query * key for query in queries for key in keys]
    scores = dot_nn(jnp.concatenate(products, axis=0), same_head) * scale
    exps = split_rows(jnp.exp(scores), len(products))
    soft = []
    for m in range(len(queries)):
        mine = exps[m * len(keys) : (m + 1) * len(keys)]
        total = mine[0]
        for e in mine[1:]:
            total = total + e
        inverse = 1.0 / total
        soft.append([e * inverse for e in mine])
    return soft


def mix_values(probs, values):
    mixed = None
    for prob, value in zip(probs, values):
        term = prob.astype(BF16).astype(F32) * value.astype(F32)
        mixed = term if mixed is None else mixed + term
    return mixed.astype(BF16)


def forward_cells(x, mem, groups, gain, project_ref, output_ref, same_head):
    channels = x.shape[-1]
    own_rows = x.shape[0] // groups * mem
    scale = 1.0 / math.sqrt(channels // HEAD_COUNT)
    normed = (x * row_rsqrt(x) * gain).astype(BF16)
    query_raw = dot_nn(normed[:own_rows], project_ref[:, :channels]).astype(BF16)
    key_raw = dot_nn(normed, project_ref[:, channels : 2 * channels]).astype(BF16)
    values = dot_nn(normed, project_ref[:, 2 * channels :]).astype(BF16)
    yield
    raw = jnp.concatenate([query_raw, key_raw], axis=0)
    units = head_units(raw, same_head, rounded_sums)[3]
    yield
    queries = split_rows(units[:own_rows], mem)
    keys = split_rows(units[own_rows:], groups)
    values = split_rows(values, groups)
    soft = softmax_members(queries, keys, same_head, scale)
    yield
    mixed = jnp.concatenate([mix_values(soft[m], values) for m in range(mem)], axis=0)
    return (x[:own_rows] + dot_nn(mixed, output_ref[...])).astype(BF16)


def together(*chains):
    results = [None] * len(chains)
    active = list(range(len(chains)))
    while active:
        for i in list(active):
            try:
                next(chains[i])
            except StopIteration as stop:
                results[i] = stop.value
                active.remove(i)
    return results


def run(chain):
    while True:
        try:
            next(chain)
        except StopIteration as stop:
            return stop.value


def shift_row(scr, member, place, slab, west, east):
    cols, channels = slab.shape
    column = lax.broadcasted_iota(jnp.int32, (cols, channels), 0)
    back = jnp.where(column == 0, west, pltpu.roll(slab, 1, 0))
    ahead = jnp.where(column == cols - 1, east, pltpu.roll(slab, cols - 1, 0))
    rows_at = slice(place * cols, (place + 1) * cols)
    scr[member, rows_at, :channels] = back.astype(BF16)
    scr[member, rows_at, channels : 2 * channels] = slab.astype(BF16)
    scr[member, rows_at, 2 * channels :] = ahead.astype(BF16)


def tap_rows(taps_ref, r):
    size = taps_ref.shape[0] // 3
    return taps_ref[r * size : (r + 1) * size, :]


def own_kernel(
    both_ref,
    other_ref,
    gain_ref,
    project_ref,
    output_ref,
    after_ref,
    proj_ref,
    unit_ref,
    soft_ref,
    inverse_ref,
    pull_ref,
    updated_ref,
):
    _, mem, rows, cols, channels = both_ref.shape
    groups = 2 * mem
    cells = rows * cols
    width = channels // HEAD_COUNT
    scale = 1.0 / math.sqrt(width)
    same_head = same_head_matrix(channels)
    own = both_ref[0].reshape(mem * cells, channels)
    other = other_ref[0].reshape(mem * cells, channels)
    x = jnp.concatenate([own, other], axis=0).astype(F32)
    normed = (x * row_rsqrt(x) * gain_ref[...]).astype(BF16)
    proj = dot_nn(normed, project_ref[...]).astype(BF16)
    proj_ref[...] = proj.reshape(groups, cells, 3 * channels)
    both_raw = jnp.concatenate([proj[:, :channels], proj[:, channels : 2 * channels]], axis=0)
    raw, mean_sq, inverse, units = head_units(both_raw, same_head)
    unit_ref[...] = units.reshape(2, groups, cells, channels)
    active = jnp.where(mean_sq > FLOOR, 1.0, jnp.where(mean_sq == FLOOR, 0.5, 0.0))
    pull = active * raw * (inverse * inverse * inverse) / width
    for kind in range(2):
        at = kind * groups * cells
        mine = slice(at, at + mem * cells)
        inverse_ref[kind] = inverse[mine].reshape(mem, cells, channels)
        pull_ref[kind] = pull[mine].reshape(mem, cells, channels)
    units = split_rows(units, 2 * groups)
    soft = softmax_members(units[:groups], units[groups:], same_head, scale)
    for m in range(groups):
        for n in range(groups):
            soft_ref[m * groups + n] = soft[m][n]
    values = split_rows(proj[:, 2 * channels :], groups)
    mixed = jnp.concatenate([mix_values(soft[m], values) for m in range(mem)], axis=0)
    updated = x[: mem * cells] + dot_nn(mixed, output_ref[...])
    updated_ref[...] = updated.astype(BF16).reshape(mem, cells, channels)


def backward_cells(
    pick, grad_field, x, gain, weights_t, proj_ref, unit_ref, soft_ref, inverse_ref, pull_ref
):
    project_t_ref, output_t_ref = weights_t
    groups = proj_ref.shape[0]
    mem = inverse_ref.shape[1]
    channels = x.shape[-1]
    scale = 1.0 / math.sqrt(channels // HEAD_COUNT)
    same_head = same_head_matrix(channels)
    grad_mixed = dot_nn(grad_field.astype(BF16), output_t_ref[...]).astype(BF16)
    grads = split_rows(grad_mixed, groups)
    yield
    values = [pick(proj_ref[n, :, 2 * channels :]) for n in range(groups)]
    products = [grads[m] * values[n] for m in range(groups) for n in range(groups)]
    dprobs = split_rows(dot_nn(jnp.concatenate(products, axis=0), same_head), len(products))
    yield
    units = [[pick(unit_ref[k, n]).astype(F32) for n in range(groups)] for k in range(2)]
    query_grad = [None] * mem
    key_grad = [None] * mem
    value_grad = [None] * mem
    for m in range(groups):
        soft = [pick(soft_ref[m * groups + n]) for n in range(groups)]
        dprob = dprobs[m * groups : (m + 1) * groups]
        mean = soft[0] * dprob[0]
        for n in range(1, groups):
            mean = mean + soft[n] * dprob[n]
        for n in range(groups):
            if m >= mem and n >= mem:
                continue
            dscore = soft[n] * (dprob[n] - mean)
            if m < mem:
                term = dscore * units[1][n]
                query_grad[m] = term if query_grad[m] is None else query_grad[m] + term
            if n < mem:
                term = dscore * units[0][m]
                key_grad[n] = term if key_grad[n] is None else key_grad[n] + term
                term = soft[n] * grads[m].astype(F32)
                value_grad[n] = term if value_grad[n] is None else value_grad[n] + term

    unit_grads = [jnp.concatenate(g, axis=0) * scale for g in (query_grad, key_grad)]

    def members(take):
        return jnp.concatenate([pick(take(m)) for m in range(mem)], axis=0)

    raws = []
    for kind in range(2):
        lanes = slice(kind * channels, (kind + 1) * channels)
        raws.append(members(lambda m: proj_ref[m, :, lanes]).astype(F32))
    inner = rounded_sums(
        jnp.concatenate([g * raw for g, raw in zip(unit_grads, raws)], axis=0), same_head
    )
    inner = split_rows(inner, 2)
    yield
    pulled = []
    for kind in range(2):
        inverse = members(lambda m: inverse_ref[kind, m])
        pull = members(lambda m: pull_ref[kind, m])
        pulled.append((inverse * unit_grads[kind] - pull * inner[kind]).astype(BF16))
    pulled.append(jnp.concatenate(value_grad, axis=0).astype(BF16))
    grad_normed = dot_nn(jnp.concatenate(pulled, axis=1), project_t_ref[...]) * gain
    yield
    inverse = row_rsqrt(x)
    inner = jnp.mean(x * grad_normed, axis=-1, keepdims=True)
    total = grad_field[: x.shape[0]] + inverse * grad_normed
    return (total - x * (inverse * inverse * inverse * inner)).astype(BF16)


def centre_kernel(
    both_ref,
    other_ref,
    chip_ref,
    core_ref,
    gain_ref,
    project_ref,
    output_ref,
    conv_ref,
    project_t_ref,
    output_t_ref,
    proj_ref,
    unit_ref,
    soft_ref,
    inverse_ref,
    pull_ref,
    updated_ref,
    conv_t_ref,
    result_ref,
    grad_ref,
    result_part_ref,
    grad_part_ref,
    shift_scr,
    cot_shift_scr,
    strip_scr,
):
    _, mem, rows, cols, channels = both_ref.shape
    groups = 2 * mem
    cells = rows * cols
    gain = gain_ref[...]
    same_head = same_head_matrix(channels)
    west, east = rim_columns(chip_ref, core_ref)
    for r in range(3):
        for c in range(3):
            tap = (3 * r + c) * channels
            turned = (3 * r + 2 - c) * channels
            conv_t_ref[turned : turned + channels, :] = conv_ref[tap : tap + channels, :].T

    def convolve(scr, count, start, taps_ref, turned):
        sums = [
            [start[(m * rows + a) * cols : (m * rows + a + 1) * cols] for a in range(rows)]
            for m in range(count)
        ]
        for r in range(3):
            step = 1 - r if turned else r - 1
            outs = [a for a in range(rows) if 0 <= a + step < rows]
            begin, end = outs[0] + step, outs[-1] + step + 1
            window = jnp.concatenate(
                [scr[m, begin * cols : end * cols, :] for m in range(count)], axis=0
            )
            terms = split_rows(dot_nn(window, tap_rows(taps_ref, r)), count * len(outs))
            for m in range(count):
                for i, a in enumerate(outs):
                    sums[m][a] = sums[m][a] + terms[m * len(outs) + i]
        return sums

    cots = []
    for member in range(groups):
        for row in range(rows):
            ref, who = (both_ref, member) if member < mem else (other_ref, member - mem)
            slab = ref[1, who, row].astype(F32)
            cots.append(slab)
            at = (groups + member) * rows + row
            shift_row(cot_shift_scr, member, row, slab, west[at : at + 1], east[at : at + 1])
    sums = convolve(cot_shift_scr, groups, jnp.concatenate(cots, axis=0), conv_t_ref, True)
    for member in range(groups):
        grad_part_ref[member, :cols, :] = sums[member][0]
        grad_part_ref[member, cols:, :] = sums[member][rows - 1]
    grad_field = jnp.concatenate([slab for s in sums for slab in s[1 : rows - 1]], axis=0)

    for member in range(groups):
        at = member * rows
        strip_scr[member] = jnp.zeros((16, channels), F32)
        strip_scr[member, :rows, :] = west[at : at + rows]
        strip_scr[member, 8 : 8 + rows, :] = east[at : at + rows]
    x = strip_scr[...].reshape(groups * 16, channels)
    forward = forward_cells(x, mem, groups, gain, project_ref, output_ref, same_head)
    x = both_ref[0, :, 1 : rows - 1].reshape(mem * (cells - 2 * cols), channels).astype(F32)
    backward = backward_cells(
        lambda array: array[cols : cells - cols],
        grad_field,
        x,
        gain,
        (project_t_ref, output_t_ref),
        proj_ref,
        unit_ref,
        soft_ref,
        inverse_ref,
        pull_ref,
    )
    fresh, total = run(forward), run(backward)
    fresh = split_rows(fresh.astype(F32), mem)
    grad_ref[...] = total.reshape(mem, rows - 2, cols, channels)

    for member in range(mem):
        for row in range(rows):
            slab = updated_ref[member, row * cols : (row + 1) * cols, :].astype(F32)
            ends = fresh[member][row : row + 1], fresh[member][8 + row : 9 + row]
            shift_row(shift_scr, member, row, slab, *ends)
    start = updated_ref[...].reshape(mem * cells, channels).astype(F32)
    sums = convolve(shift_scr, mem, start, conv_ref, False)
    for member in range(mem):
        result_part_ref[member, :cols, :] = sums[member][0]
        result_part_ref[member, cols:, :] = sums[member][rows - 1]
        for row in range(1, rows - 1):
            result_ref[member, row - 1] = sums[member][row].astype(BF16)


def main_kernel(
    both_ref,
    second_ref,
    first_ref,
    gain_ref,
    project_ref,
    output_ref,
    conv_ref,
    project_t_ref,
    output_t_ref,
    conv_t_ref,
    proj_ref,
    unit_ref,
    soft_ref,
    inverse_ref,
    pull_ref,
    inner_result_ref,
    inner_grad_ref,
    result_part_ref,
    grad_part_ref,
    result_ref,
    grad_ref,
    shift_scr,
    cot_shift_scr,
    corner_scr,
    outer_scr,
    sems,
    *,
    lat_count,
):
    _, mem, rows, cols, channels = both_ref.shape
    copies = []
    for i, (ref, out_ref) in enumerate(
        ((inner_result_ref, result_ref), (inner_grad_ref, grad_ref))
    ):
        copy = pltpu.make_async_copy(ref, out_ref.at[:, pl.ds(1, rows - 2)], sems.at[i])
        copy.start()
        copies.append(copy)
    groups = 2 * mem
    slots = 2 * groups
    cells = rows * cols
    gain = gain_ref[...]
    same_head = same_head_matrix(channels)
    lat_even = is_even("lat")
    lat = lax.axis_index("lat")

    def halos(at):
        first, second = first_ref[at, :].astype(F32), second_ref[at, :].astype(F32)
        north = jnp.where(lat == 0, 0.0, jnp.where(lat_even, second, first))
        south = jnp.where(lat == lat_count - 1, 0.0, jnp.where(lat_even, first, second))
        return north, south

    halo = [halos(slice(slot * cols, (slot + 1) * cols)) for slot in range(slots)]
    corners = halos(slice(slots * cols, slots * cols + 2 * slots))

    def corner(side, slot, end):
        at = end * slots + slot
        return corners[side][at : at + 1]

    def halo_part(scr, count, taps_ref, turned):
        north, south = (2, 0) if turned else (0, 2)
        parts = []
        for side, r in ((0, north), (1, south)):
            window = jnp.concatenate(
                [scr[m, side * cols : (side + 1) * cols, :] for m in range(count)], axis=0
            )
            parts.append(split_rows(dot_nn(window, tap_rows(taps_ref, r)), count))
        return jnp.concatenate([parts[side][m] for m in range(count) for side in (0, 1)], axis=0)

    for member in range(groups):
        slot = groups + member
        for side in (0, 1):
            ends = corner(side, slot, 0), corner(side, slot, 1)
            shift_row(cot_shift_scr, member, side, halo[slot][side], *ends)
    grad_field = grad_part_ref[...].reshape(groups * 2 * cols, channels)
    grad_field = grad_field + halo_part(cot_shift_scr, groups, conv_t_ref, True)

    blocks = []
    for member in range(groups):
        corner_scr[member] = jnp.zeros((16, channels), F32)
        for side in (0, 1):
            for end in (0, 1):
                at = 2 * side + end
                corner_scr[member, at : at + 1, :] = corner(side, member, end)
        blocks += [halo[member][0], halo[member][1], corner_scr[member]]
    x = jnp.concatenate(blocks, axis=0)
    forward = forward_cells(x, mem, groups, gain, project_ref, output_ref, same_head)
    x = [both_ref[0, m, row] for m in range(mem) for row in (0, rows - 1)]
    backward = backward_cells(
        lambda array: jnp.concatenate([array[:cols], array[cells - cols :]], axis=0),
        grad_field,
        jnp.concatenate(x, axis=0).astype(F32),
        gain,
        (project_t_ref, output_t_ref),
        proj_ref,
        unit_ref,
        soft_ref,
        inverse_ref,
        pull_ref,
    )

    def finish_result(chain):
        fresh = yield from chain
        fresh = split_rows(fresh.astype(F32), mem)
        for member in range(mem):
            for side in (0, 1):
                slab = fresh[member][side * cols : (side + 1) * cols]
                at = 2 * cols + 2 * side
                ends = fresh[member][at : at + 1], fresh[member][at + 1 : at + 2]
                shift_row(shift_scr, member, side, slab, *ends)
        yield
        outer = result_part_ref[...].reshape(mem * 2 * cols, channels)
        outer = (outer + halo_part(shift_scr, mem, conv_ref, False)).astype(BF16)
        store_outer(0, outer)

    def store_outer(which, outer):
        for i, slab in enumerate(split_rows(outer, 2 * mem)):
            outer_scr[which, i % 2, i // 2] = slab
        for side, row in ((0, 0), (1, rows - 1)):
            copy = pltpu.make_async_copy(
                outer_scr.at[which, side],
                (result_ref, grad_ref)[which].at[:, row],
                sems.at[2 + 2 * which + side],
            )
            copy.start()
            copies.append(copy)

    total, _ = together(backward, finish_result(forward))
    store_outer(1, total)
    for copy in copies:
        copy.wait()


def local_call(kernel, name, operands, out_shape, scratch, pinned=False, cost=None, copied=False):
    whole = pl.BlockSpec(memory_space=pltpu.VMEM)
    anywhere = pl.BlockSpec(memory_space=pl.ANY)
    specs = [anywhere if in_hbm else whole for _, in_hbm in operands]
    arrays = [
        pltpu.with_memory_space_constraint(array, pltpu.HBM) if in_hbm else array
        for array, in_hbm in operands
    ]

    def keep(shape):
        return pltpu.VMEM(shape.shape, shape.dtype) if pinned else shape

    return pl.pallas_call(
        kernel,
        out_shape=jax.tree.map(keep, out_shape),
        in_specs=specs,
        out_specs=jax.tree.map(lambda _: anywhere if copied else whole, out_shape),
        scratch_shapes=scratch,
        compiler_params=pltpu.CompilerParams(vmem_limit_bytes=VMEM_LIMIT),
        cost_estimate=cost,
        name=name,
    )(*arrays)


def here(*arrays):
    return [(array, False) for array in arrays]


def in_hbm(*arrays):
    return [(array, True) for array in arrays]


def per_device_paired(ensemble, norm_gain, project_weight, output_weight, conv_kernel, cotangent):
    mem, rows, cols, channels = ensemble.shape
    if rows < 3 or cols % 16 or (2 * mem * rows) % 16:
        return per_device_general(
            ensemble, norm_gain, project_weight, output_weight, conv_kernel, cotangent
        )
    groups = 2 * mem
    slots = 2 * groups
    cells = rows * cols
    lon_count = lax.axis_size("lon")
    lat_count = lax.axis_size("lat")
    bf16 = functools.partial(jax.ShapeDtypeStruct, dtype=BF16)
    f32 = functools.partial(jax.ShapeDtypeStruct, dtype=F32)
    swap = [(0, 1), (1, 0)]
    core_pairs = [(i, i ^ 1) for i in range(lon_count)]
    chip_pairs = [(i, (i - 1 if i % 2 == 0 else i + 1) % lon_count) for i in range(lon_count)]

    def lat_swap(offset):
        pairs = []
        for lat in range(lat_count):
            for lon in range(lon_count):
                to = (lat + 1 if lat % 2 == offset else lat - 1, lon)
                if not 0 <= to[0] < lat_count:
                    to = (lat, lon ^ 1)
                pairs.append((lat * lon_count + lon, to[0] * lon_count + to[1]))
        return pairs

    ends_shape = (2, 2 * mem * rows, channels)
    both, ends = local_call(
        stack_kernel,
        "stack",
        in_hbm(ensemble, cotangent),
        (bf16((2,) + ensemble.shape), bf16(ends_shape)),
        [pltpu.VMEM(ends_shape[1:], F32)] * 2 + [pltpu.SemaphoreType.DMA((2,))],
        pinned=True,
    )
    other_ends = lax.ppermute(ends, "member", swap)
    block, gain, output, output_t = local_call(
        load_output_kernel,
        "load_output",
        here(both) + in_hbm(norm_gain.reshape(1, channels), output_weight),
        (
            bf16(both.shape),
            f32((1, channels)),
            bf16(output_weight.shape),
            bf16((channels, channels)),
        ),
        [pltpu.SemaphoreType.DMA((2,))],
        pinned=True,
        cost=LONG,
    )
    other = lax.ppermute(block, "member", swap)

    strip = (slots * rows, channels)
    chip_send, core_send = local_call(
        pack_strips_kernel,
        "pack_strips",
        here(ends, other_ends),
        (bf16(strip), bf16(strip)),
        [pltpu.VMEM(strip, F32)] * 2,
    )
    chip = lax.ppermute(chip_send, "lon", chip_pairs)
    core = lax.ppermute(core_send, "lon", core_pairs)

    project, conv, project_t = local_call(
        load_kernel,
        "load_weights",
        in_hbm(project_weight, conv_kernel.reshape(9 * channels, channels)),
        (
            bf16(project_weight.shape),
            bf16((9 * channels, channels)),
            bf16((3 * channels, channels)),
        ),
        [pltpu.SemaphoreType.DMA((2,))],
        pinned=True,
        cost=MIDDLING,
    )
    weights = (gain, project, output, conv)
    halo = bf16((slots * (cols + 2), channels))
    first_send, second_send = local_call(
        pack_rows_kernel,
        "pack_rows",
        here(both, other, chip, core, project),
        (halo, halo),
        [pltpu.VMEM((2, 2 * slots, channels), F32)],
    )
    first = lax.ppermute(first_send, ("lat", "lon"), lat_swap(0))
    second = lax.ppermute(second_send, ("lat", "lon"), lat_swap(1))

    *held, updated = local_call(
        own_kernel,
        "own_cells",
        here(both, other, *weights[:3], second_send),
        (
            bf16((groups, cells, 3 * channels)),
            bf16((2, groups, cells, channels)),
            f32((groups * groups, cells, channels)),
            f32((2, mem, cells, channels)),
            f32((2, mem, cells, channels)),
            bf16((mem, cells, channels)),
        ),
        [],
        pinned=True,
        cost=LONG,
    )
    conv_t, *parts = local_call(
        centre_kernel,
        "centre",
        here(both, other, chip, core, *weights, project_t, output_t, *held, updated),
        (
            bf16((9 * channels, channels)),
            bf16((mem, rows - 2, cols, channels)),
            bf16((mem, rows - 2, cols, channels)),
            f32((mem, 2 * cols, channels)),
            f32((groups, 2 * cols, channels)),
        ),
        [
            pltpu.VMEM((mem, cells, 3 * channels), BF16),
            pltpu.VMEM((groups, cells, 3 * channels), BF16),
            pltpu.VMEM((groups, 16, channels), F32),
        ],
        pinned=True,
        cost=LONG,
    )
    return local_call(
        functools.partial(main_kernel, lat_count=lat_count),
        "main",
        here(both, second, first, *weights, project_t, output_t, conv_t, *held, *parts),
        (bf16(ensemble.shape), bf16(ensemble.shape)),
        [
            pltpu.VMEM((mem, 2 * cols, 3 * channels), BF16),
            pltpu.VMEM((groups, 2 * cols, 3 * channels), BF16),
            pltpu.VMEM((groups, 16, channels), F32),
            pltpu.VMEM((2, 2, mem, cols, channels), BF16),
            pltpu.SemaphoreType.DMA((6,)),
        ],
        copied=True,
    )


def solution(mesh):
    paired = mesh.shape["member"] == 2 and mesh.shape["lon"] % 2 == 0
    per_device = per_device_paired if paired else per_device_general
    in_specs = (
        P("member", "lat", "lon", None),
        P(),
        P(),
        P(),
        P(),
        P("member", "lat", "lon", None),
    )
    out_specs = (P("member", "lat", "lon", None), P("member", "lat", "lon", None))
    return jax.shard_map(
        per_device, mesh=mesh, in_specs=in_specs, out_specs=out_specs, check_vma=False
    )
```

```python
import functools
import math

import jax
import jax.numpy as jnp
from jax import lax
from jax.experimental import pallas as pl
from jax.experimental.pallas import tpu as pltpu
from jax.sharding import PartitionSpec as P

HEAD_COUNT = 8


FLOOR = 0.5
EPSILON = 1e-06


def padded_2(block, sides, width, periodic):
    for axis, dim in sides:
        count = lax.axis_size(axis)
        forward = [(i, i + 1) for i in range(count - 1)]
        if periodic:
            forward.append((count - 1, 0))
        backward = [(target, source) for source, target in forward]
        low = lax.ppermute(
            lax.slice_in_dim(block, block.shape[dim] - width, None, axis=dim), axis, forward
        )
        high = lax.ppermute(lax.slice_in_dim(block, 0, width, axis=dim), axis, backward)
        block = jnp.concatenate([low, block, high], axis=dim)
    return block


def row_norm(values, gain_vec):
    mean_sq = jnp.mean(values * values, axis=-1, keepdims=True)
    return values * lax.rsqrt(mean_sq + EPSILON) * gain_vec


def head_norm(values, head_count):
    shaped = values.reshape(values.shape[:-1] + (head_count, values.shape[-1] // head_count))
    mean_sq = jnp.mean(shaped * shaped, axis=-1, keepdims=True)
    return (shaped * lax.rsqrt(jnp.maximum(mean_sq, FLOOR))).reshape(values.shape)


def split_heads(values, head_count):
    return values.reshape(values.shape[:-1] + (head_count, values.shape[-1] // head_count))


def head_pullback(raw_rows, grad_rows):
    _, pullback = jax.vjp(lambda t: head_norm(t, HEAD_COUNT), raw_rows.astype(jnp.float32))
    return pullback(grad_rows)[0]


def pad_field(field_in):
    widened = padded_2(field_in, (("lon", 2),), 1, True)
    return padded_2(widened, (("lat", 1),), 1, False)


def conv_taps(padded, kernel, lat_n, lon_n, adjoint):
    running = None
    for row_off in range(3):
        for col_off in range(3):
            if adjoint:
                window = padded[
                    :, 2 - row_off : 2 - row_off + lat_n, 2 - col_off : 2 - col_off + lon_n
                ]
                summand = jnp.einsum(
                    "mabc,dc->mabd",
                    window,
                    kernel[row_off, col_off],
                    preferred_element_type=jnp.float32,
                )
            else:
                window = padded[:, row_off : row_off + lat_n, col_off : col_off + lon_n]
                summand = jnp.einsum(
                    "mabc,cd->mabd",
                    window,
                    kernel[row_off, col_off],
                    preferred_element_type=jnp.float32,
                )
            running = summand if running is None else running + summand
    return running


def per_device_general(ensemble, norm_gain, project_weight, output_weight, conv_kernel, cotangent):
    mem_dev, lat_dev, lon_dev, channels = ensemble.shape
    cell_count = lat_dev * lon_dev
    score_scale = 1.0 / math.sqrt(channels // HEAD_COUNT)
    inputs = ensemble.reshape(mem_dev, cell_count, channels).astype(jnp.float32)
    normed = row_norm(inputs, norm_gain).astype(jnp.bfloat16)
    spread = lax.all_to_all(normed, "member", split_axis=1, concat_axis=0, tiled=True)
    projected = jnp.dot(spread, project_weight, preferred_element_type=jnp.float32).astype(
        jnp.bfloat16
    )
    query_raw = projected[..., :channels]
    key_raw = projected[..., channels : 2 * channels]
    value_rows = projected[..., 2 * channels :]
    key_rows = head_norm(key_raw.astype(jnp.float32), HEAD_COUNT).astype(jnp.bfloat16)
    queries = head_norm(query_raw.astype(jnp.float32), HEAD_COUNT).astype(jnp.bfloat16)
    query_heads = split_heads(queries, HEAD_COUNT)
    key_heads = split_heads(key_rows, HEAD_COUNT)
    value_heads = split_heads(value_rows, HEAD_COUNT)
    scores = (
        jnp.einsum("mphd,nphd->mnhp", query_heads, key_heads, preferred_element_type=jnp.float32)
        * score_scale
    )
    expd = jnp.exp(scores)
    soft = expd / jnp.sum(expd, axis=1, keepdims=True)
    rounded = soft.astype(jnp.bfloat16)
    mixed_out = jnp.einsum(
        "mnhp,nphd->mphd", rounded, value_heads, preferred_element_type=jnp.float32
    )
    mixed_out = mixed_out.reshape(query_raw.shape).astype(jnp.bfloat16)
    mixed_out = lax.all_to_all(mixed_out, "member", split_axis=0, concat_axis=1, tiled=True)
    updated = (
        inputs + jnp.dot(mixed_out, output_weight, preferred_element_type=jnp.float32)
    ).astype(jnp.bfloat16)
    field_up = updated.reshape(mem_dev, lat_dev, lon_dev, channels)
    result = field_up.astype(jnp.float32) + conv_taps(
        pad_field(field_up), conv_kernel, lat_dev, lon_dev, False
    )
    result = result.astype(jnp.bfloat16)
    grad_field = cotangent.astype(jnp.float32) + conv_taps(
        pad_field(cotangent), conv_kernel, lat_dev, lon_dev, True
    )
    grad_rows = grad_field.reshape(mem_dev, cell_count, channels)
    grad_mixed = jnp.einsum(
        "mpc,dc->mpd",
        grad_rows.astype(jnp.bfloat16),
        output_weight,
        preferred_element_type=jnp.float32,
    )
    grad_mixed = grad_mixed.astype(jnp.bfloat16)
    grad_mixed = lax.all_to_all(grad_mixed, "member", split_axis=1, concat_axis=0, tiled=True)
    grad_heads = split_heads(grad_mixed, HEAD_COUNT)
    dprob = jnp.einsum(
        "mphd,nphd->mnhp", grad_heads, value_heads, preferred_element_type=jnp.float32
    )
    dscore = (soft * (dprob - jnp.sum(soft * dprob, axis=1, keepdims=True))).astype(jnp.bfloat16)
    query_grad = (
        jnp.einsum("mnhp,nphd->mphd", dscore, key_heads, preferred_element_type=jnp.float32)
        * score_scale
    )
    query_grad = query_grad.reshape(query_raw.shape)
    key_grad = (
        jnp.einsum("mnhp,mphd->nphd", dscore, query_heads, preferred_element_type=jnp.float32)
        * score_scale
    )
    key_grad = key_grad.reshape(key_raw.shape)
    value_grad = jnp.einsum(
        "mnhp,mphd->nphd", rounded, grad_heads, preferred_element_type=jnp.float32
    )
    value_grad = value_grad.reshape(key_raw.shape)
    grad_query_raw = head_pullback(query_raw, query_grad)
    grad_key_raw = head_pullback(key_raw, key_grad)
    grad_proj = jnp.concatenate([grad_query_raw, grad_key_raw, value_grad], axis=-1).astype(
        jnp.bfloat16
    )
    grad_proj = lax.all_to_all(grad_proj, "member", split_axis=0, concat_axis=1, tiled=True)
    grad_normed = jnp.einsum(
        "mpe,ce->mpc", grad_proj, project_weight, preferred_element_type=jnp.float32
    )
    _, pull_norm = jax.vjp(lambda t: row_norm(t, norm_gain), inputs)
    grad_inputs = pull_norm(grad_normed)[0]
    grad_ensemble = (
        (grad_rows + grad_inputs).astype(jnp.bfloat16).reshape(mem_dev, lat_dev, lon_dev, channels)
    )
    return (result, grad_ensemble)


F32 = jnp.float32
BF16 = jnp.bfloat16
VMEM_LIMIT = 24 * 1024 * 1024
LONG = pl.CostEstimate(flops=20_000_000_000, bytes_accessed=4_000_000, transcendentals=0)
LOAD_COST = pl.CostEstimate(flops=3_000_000_000, bytes_accessed=2_000_000, transcendentals=0)


def is_even(axis):
    return lax.rem(lax.axis_index(axis), 2) == 0


def load_kernel(
    gain_hbm,
    project_hbm,
    output_hbm,
    gain_ref,
    project_ref,
    output_ref,
    project_t_ref,
    output_t_ref,
    sems,
):
    channels = output_ref.shape[0]
    pairs = ((gain_hbm, gain_ref), (project_hbm, project_ref), (output_hbm, output_ref))
    loads = [
        pltpu.make_async_copy(source, target, sems.at[i])
        for i, (source, target) in enumerate(pairs)
    ]
    for load in loads:
        load.start()
    for load in loads:
        load.wait()
    output_t_ref[...] = output_ref[...].T
    for kind in range(3):
        lanes = slice(kind * channels, (kind + 1) * channels)
        project_t_ref[lanes, :] = project_ref[:, lanes].T


def stack_kernel(ens_ref, cot_ref, both_ref, ends_ref, low_scr, high_scr, sems):
    _, mem, rows, cols, _ = both_ref.shape
    copies = [
        pltpu.make_async_copy(ref, both_ref.at[i], sems.at[i])
        for i, ref in enumerate((ens_ref, cot_ref))
    ]
    for copy in copies:
        copy.start()
    for copy in copies:
        copy.wait()
    index = 0
    for array in range(2):
        for member in range(mem):
            for row in range(rows):
                slab = both_ref[array, member, row].astype(F32)
                low_scr[index : index + 1, :] = slab[0:1]
                high_scr[index : index + 1, :] = slab[cols - 1 : cols]
                index += 1
    ends_ref[0] = low_scr[...].astype(BF16)
    ends_ref[1] = high_scr[...].astype(BF16)


def pack_strips_kernel(
    ends_ref, other_ends_ref, after_ref, chip_ref, core_ref, low_scr, high_scr
):
    part = ends_ref.shape[1] // 2
    for side, scr in ((0, low_scr), (1, high_scr)):
        for group, ref in enumerate((ends_ref, other_ends_ref)):
            column = ref[side].astype(F32)
            for array in range(2):
                at = (2 * array + group) * part
                scr[at : at + part, :] = column[array * part : (array + 1) * part]
    even = is_even("lon")
    low, high = low_scr[...], high_scr[...]
    core_ref[...] = jnp.where(even, high, low).astype(BF16)
    chip_ref[...] = jnp.where(even, low, high).astype(BF16)


def rim_columns(chip_ref, core_ref):
    even = is_even("lon")
    chip, core = chip_ref[...].astype(F32), core_ref[...].astype(F32)
    return jnp.where(even, chip, core), jnp.where(even, core, chip)


def pack_rows_kernel(
    both_ref, other_ref, chip_ref, core_ref, updated_ref, first_ref, second_ref, edge_scr
):
    _, mem, rows, cols, _ = both_ref.shape
    groups = 2 * mem
    cells = rows * cols
    slots = 2 * groups
    even = is_even("lat")
    west, east = rim_columns(chip_ref, core_ref)
    for place in range(mem + groups):
        if place < mem:
            pair = updated_ref[place, :cols, :], updated_ref[place, cells - cols :, :]
        else:
            member = place - mem
            ref, who = (both_ref, member) if member < mem else (other_ref, member - mem)
            pair = ref[1, who, 0], ref[1, who, rows - 1]
        start, stop = (slab.astype(F32) for slab in pair)
        at = slice(place * cols, (place + 1) * cols)
        first_ref[at, :] = jnp.where(even, stop, start).astype(BF16)
        second_ref[at, :] = jnp.where(even, start, stop).astype(BF16)
    for slot in range(slots):
        top, low = slot * rows, (slot + 1) * rows - 1
        for side, column in enumerate((west, east)):
            place = side * slots + slot
            start, stop = column[top : top + 1], column[low : low + 1]
            edge_scr[0, place : place + 1, :] = jnp.where(even, stop, start)
            edge_scr[1, place : place + 1, :] = jnp.where(even, start, stop)
    first_ref[(mem + groups) * cols :, :] = edge_scr[0].astype(BF16)
    second_ref[(mem + groups) * cols :, :] = edge_scr[1].astype(BF16)


def dot_nn(a, b):
    return lax.dot_general(a, b, (((1,), (0,)), ((), ())), preferred_element_type=F32)


def same_head_matrix(channels):
    width = channels // HEAD_COUNT
    lane_row = lax.broadcasted_iota(jnp.int32, (channels, channels), 0) // width
    lane_col = lax.broadcasted_iota(jnp.int32, (channels, channels), 1) // width
    return jnp.where(lane_row == lane_col, 1.0, 0.0).astype(BF16)


def head_sums(values, same_head):
    high = values.astype(BF16)
    low = (values - high.astype(F32)).astype(BF16)
    return dot_nn(high, same_head) + dot_nn(low, same_head)


def rounded_sums(values, same_head):
    return dot_nn(values.astype(BF16), same_head)


def head_units(raw, same_head, sums=head_sums):
    raw = raw.astype(F32)
    mean_sq = sums(raw * raw, same_head) * (HEAD_COUNT / raw.shape[-1])
    inverse = lax.rsqrt(jnp.maximum(mean_sq, FLOOR))
    return raw, mean_sq, inverse, (raw * inverse).astype(BF16)


def row_rsqrt(values):
    return lax.rsqrt(jnp.mean(values * values, axis=-1, keepdims=True) + EPSILON)


def split_rows(array, count):
    size = array.shape[0] // count
    return [array[i * size : (i + 1) * size] for i in range(count)]


def softmax_members(queries, keys, same_head, scale):
    products = [query * key for query in queries for key in keys]
    scores = dot_nn(jnp.concatenate(products, axis=0), same_head) * scale
    exps = split_rows(jnp.exp(scores), len(products))
    soft = []
    for m in range(len(queries)):
        mine = exps[m * len(keys) : (m + 1) * len(keys)]
        total = mine[0]
        for e in mine[1:]:
            total = total + e
        inverse = 1.0 / total
        soft.append([e * inverse for e in mine])
    return soft


def mix_values(probs, values):
    mixed = None
    for prob, value in zip(probs, values):
        term = prob.astype(BF16).astype(F32) * value.astype(F32)
        mixed = term if mixed is None else mixed + term
    return mixed.astype(BF16)


def forward_cells(x, mem, groups, gain, project_ref, output_ref, same_head):
    channels = x.shape[-1]
    own_rows = x.shape[0] // groups * mem
    scale = 1.0 / math.sqrt(channels // HEAD_COUNT)
    normed = (x * row_rsqrt(x) * gain).astype(BF16)
    query_raw = dot_nn(normed[:own_rows], project_ref[:, :channels]).astype(BF16)
    key_raw = dot_nn(normed, project_ref[:, channels : 2 * channels]).astype(BF16)
    values = dot_nn(normed, project_ref[:, 2 * channels :]).astype(BF16)
    yield
    raw = jnp.concatenate([query_raw, key_raw], axis=0)
    units = head_units(raw, same_head, rounded_sums)[3]
    yield
    queries = split_rows(units[:own_rows], mem)
    keys = split_rows(units[own_rows:], groups)
    values = split_rows(values, groups)
    soft = softmax_members(queries, keys, same_head, scale)
    yield
    mixed = jnp.concatenate([mix_values(soft[m], values) for m in range(mem)], axis=0)
    return (x[:own_rows] + dot_nn(mixed, output_ref[...])).astype(BF16)


def together(*chains):
    active = list(chains)
    while active:
        for chain in list(active):
            try:
                next(chain)
            except StopIteration:
                active.remove(chain)


def run(chain):
    while True:
        try:
            next(chain)
        except StopIteration as stop:
            return stop.value


def shift_row(scr, member, place, slab, west, east):
    cols, channels = slab.shape
    column = lax.broadcasted_iota(jnp.int32, (cols, channels), 0)
    back = jnp.where(column == 0, west, pltpu.roll(slab, 1, 0))
    ahead = jnp.where(column == cols - 1, east, pltpu.roll(slab, cols - 1, 0))
    rows_at = slice(place * cols, (place + 1) * cols)
    scr[member, rows_at, :channels] = back.astype(BF16)
    scr[member, rows_at, channels : 2 * channels] = slab.astype(BF16)
    scr[member, rows_at, 2 * channels :] = ahead.astype(BF16)


def tap_rows(taps_ref, r):
    size = taps_ref.shape[0] // 3
    return taps_ref[r * size : (r + 1) * size, :]


def own_kernel(
    both_ref,
    other_ref,
    gain_ref,
    project_ref,
    output_ref,
    conv_hbm,
    conv_ref,
    proj_ref,
    unit_ref,
    soft_ref,
    inverse_ref,
    pull_ref,
    updated_ref,
    sem,
):
    load = pltpu.make_async_copy(conv_hbm, conv_ref, sem)
    load.start()
    _, mem, rows, cols, channels = both_ref.shape
    groups = 2 * mem
    cells = rows * cols
    width = channels // HEAD_COUNT
    scale = 1.0 / math.sqrt(width)
    same_head = same_head_matrix(channels)
    own = both_ref[0].reshape(mem * cells, channels)
    other = other_ref[0].reshape(mem * cells, channels)
    x = jnp.concatenate([own, other], axis=0).astype(F32)
    normed = (x * row_rsqrt(x) * gain_ref[...]).astype(BF16)
    proj = dot_nn(normed, project_ref[...]).astype(BF16)
    proj_ref[...] = proj.reshape(groups, cells, 3 * channels)
    both_raw = jnp.concatenate([proj[:, :channels], proj[:, channels : 2 * channels]], axis=0)
    raw, mean_sq, inverse, units = head_units(both_raw, same_head)
    unit_ref[...] = units.reshape(2, groups, cells, channels)
    active = jnp.where(mean_sq > FLOOR, 1.0, jnp.where(mean_sq == FLOOR, 0.5, 0.0))
    pull = active * raw * (inverse * inverse * inverse) / width
    for kind in range(2):
        at = kind * groups * cells
        mine = slice(at, at + mem * cells)
        inverse_ref[kind] = inverse[mine].reshape(mem, cells, channels)
        pull_ref[kind] = pull[mine].reshape(mem, cells, channels)
    units = split_rows(units, 2 * groups)
    soft = softmax_members(units[:groups], units[groups:], same_head, scale)
    for m in range(groups):
        for n in range(groups):
            soft_ref[m * groups + n] = soft[m][n]
    values = split_rows(proj[:, 2 * channels :], groups)
    mixed = jnp.concatenate([mix_values(soft[m], values) for m in range(mem)], axis=0)
    updated = x[: mem * cells] + dot_nn(mixed, output_ref[...])
    updated_ref[...] = updated.astype(BF16).reshape(mem, cells, channels)
    load.wait()


def backward_cells(
    pick, grad_field, x, gain, weights_t, proj_ref, unit_ref, soft_ref, inverse_ref, pull_ref
):
    project_t_ref, output_t_ref = weights_t
    groups = proj_ref.shape[0]
    mem = inverse_ref.shape[1]
    channels = x.shape[-1]
    scale = 1.0 / math.sqrt(channels // HEAD_COUNT)
    same_head = same_head_matrix(channels)
    grad_mixed = dot_nn(grad_field.astype(BF16), output_t_ref[...]).astype(BF16)
    grads = split_rows(grad_mixed, groups)
    yield
    values = [pick(proj_ref[n, :, 2 * channels :]) for n in range(groups)]
    products = [grads[m] * values[n] for m in range(groups) for n in range(groups)]
    dprobs = split_rows(dot_nn(jnp.concatenate(products, axis=0), same_head), len(products))
    yield
    units = [[pick(unit_ref[k, n]).astype(F32) for n in range(groups)] for k in range(2)]
    query_grad = [None] * mem
    key_grad = [None] * mem
    value_grad = [None] * mem
    for m in range(groups):
        soft = [pick(soft_ref[m * groups + n]) for n in range(groups)]
        dprob = dprobs[m * groups : (m + 1) * groups]
        mean = soft[0] * dprob[0]
        for n in range(1, groups):
            mean = mean + soft[n] * dprob[n]
        for n in range(groups):
            if m >= mem and n >= mem:
                continue
            dscore = soft[n] * (dprob[n] - mean)
            if m < mem:
                term = dscore * units[1][n]
                query_grad[m] = term if query_grad[m] is None else query_grad[m] + term
            if n < mem:
                term = dscore * units[0][m]
                key_grad[n] = term if key_grad[n] is None else key_grad[n] + term
                term = soft[n] * grads[m].astype(F32)
                value_grad[n] = term if value_grad[n] is None else value_grad[n] + term

    unit_grads = [jnp.concatenate(g, axis=0) * scale for g in (query_grad, key_grad)]

    def members(take):
        return jnp.concatenate([pick(take(m)) for m in range(mem)], axis=0)

    raws = []
    for kind in range(2):
        lanes = slice(kind * channels, (kind + 1) * channels)
        raws.append(members(lambda m: proj_ref[m, :, lanes]).astype(F32))
    inner = rounded_sums(
        jnp.concatenate([g * raw for g, raw in zip(unit_grads, raws)], axis=0), same_head
    )
    inner = split_rows(inner, 2)
    yield
    pulled = []
    for kind in range(2):
        inverse = members(lambda m: inverse_ref[kind, m])
        pull = members(lambda m: pull_ref[kind, m])
        pulled.append((inverse * unit_grads[kind] - pull * inner[kind]).astype(BF16))
    pulled.append(jnp.concatenate(value_grad, axis=0).astype(BF16))
    grad_normed = dot_nn(jnp.concatenate(pulled, axis=1), project_t_ref[...]) * gain
    yield
    inverse = row_rsqrt(x)
    inner = jnp.mean(x * grad_normed, axis=-1, keepdims=True)
    total = grad_field[: x.shape[0]] + inverse * grad_normed
    return (total - x * (inverse * inverse * inverse * inner)).astype(BF16)


def centre_kernel(
    both_ref,
    other_ref,
    chip_ref,
    core_ref,
    gain_ref,
    project_ref,
    output_ref,
    conv_ref,
    project_t_ref,
    output_t_ref,
    proj_ref,
    unit_ref,
    soft_ref,
    inverse_ref,
    pull_ref,
    updated_ref,
    conv_t_ref,
    result_ref,
    grad_ref,
    result_part_ref,
    grad_part_ref,
    shift_scr,
    cot_shift_scr,
    strip_scr,
):
    _, mem, rows, cols, channels = both_ref.shape
    groups = 2 * mem
    cells = rows * cols
    gain = gain_ref[...]
    same_head = same_head_matrix(channels)
    west, east = rim_columns(chip_ref, core_ref)
    for r in range(3):
        for c in range(3):
            tap = (3 * r + c) * channels
            turned = (3 * r + 2 - c) * channels
            conv_t_ref[turned : turned + channels, :] = conv_ref[tap : tap + channels, :].T

    def convolve(scr, count, start, taps_ref, turned):
        sums = [
            [start[(m * rows + a) * cols : (m * rows + a + 1) * cols] for a in range(rows)]
            for m in range(count)
        ]
        for r in range(3):
            step = 1 - r if turned else r - 1
            outs = [a for a in range(rows) if 0 <= a + step < rows]
            begin, end = outs[0] + step, outs[-1] + step + 1
            window = jnp.concatenate(
                [scr[m, begin * cols : end * cols, :] for m in range(count)], axis=0
            )
            terms = split_rows(dot_nn(window, tap_rows(taps_ref, r)), count * len(outs))
            for m in range(count):
                for i, a in enumerate(outs):
                    sums[m][a] = sums[m][a] + terms[m * len(outs) + i]
        return sums

    cots = []
    for member in range(groups):
        for row in range(rows):
            ref, who = (both_ref, member) if member < mem else (other_ref, member - mem)
            slab = ref[1, who, row].astype(F32)
            cots.append(slab)
            at = (groups + member) * rows + row
            shift_row(cot_shift_scr, member, row, slab, west[at : at + 1], east[at : at + 1])
    sums = convolve(cot_shift_scr, groups, jnp.concatenate(cots, axis=0), conv_t_ref, True)
    for member in range(groups):
        grad_part_ref[member, :cols, :] = sums[member][0]
        grad_part_ref[member, cols:, :] = sums[member][rows - 1]
    grad_field = jnp.concatenate([slab for s in sums for slab in s[1 : rows - 1]], axis=0)

    for member in range(groups):
        at = member * rows
        strip_scr[member] = jnp.zeros((16, channels), F32)
        strip_scr[member, :rows, :] = west[at : at + rows]
        strip_scr[member, 8 : 8 + rows, :] = east[at : at + rows]
    x = strip_scr[...].reshape(groups * 16, channels)
    forward = forward_cells(x, mem, groups, gain, project_ref, output_ref, same_head)
    x = both_ref[0, :, 1 : rows - 1].reshape(mem * (cells - 2 * cols), channels).astype(F32)
    backward = backward_cells(
        lambda array: array[cols : cells - cols],
        grad_field,
        x,
        gain,
        (project_t_ref, output_t_ref),
        proj_ref,
        unit_ref,
        soft_ref,
        inverse_ref,
        pull_ref,
    )
    fresh, total = run(forward), run(backward)
    fresh = split_rows(fresh.astype(F32), mem)
    grad_ref[...] = total.reshape(mem, rows - 2, cols, channels)

    for member in range(mem):
        for row in range(rows):
            slab = updated_ref[member, row * cols : (row + 1) * cols, :].astype(F32)
            ends = fresh[member][row : row + 1], fresh[member][8 + row : 9 + row]
            shift_row(shift_scr, member, row, slab, *ends)
    start = updated_ref[...].reshape(mem * cells, channels).astype(F32)
    sums = convolve(shift_scr, mem, start, conv_ref, False)
    for member in range(mem):
        result_part_ref[member, :cols, :] = sums[member][0]
        result_part_ref[member, cols:, :] = sums[member][rows - 1]
        for row in range(1, rows - 1):
            result_ref[member, row - 1] = sums[member][row].astype(BF16)


def main_kernel(
    both_ref,
    first_ref,
    second_ref,
    gain_ref,
    project_ref,
    output_ref,
    conv_ref,
    project_t_ref,
    output_t_ref,
    conv_t_ref,
    proj_ref,
    unit_ref,
    soft_ref,
    inverse_ref,
    pull_ref,
    inner_result_ref,
    inner_grad_ref,
    result_part_ref,
    grad_part_ref,
    result_ref,
    grad_ref,
    shift_scr,
    cot_shift_scr,
    corner_scr,
    outer_scr,
    sems,
    *,
    lat_count,
):
    _, mem, rows, cols, channels = both_ref.shape
    copies = []
    for i, (ref, out_ref) in enumerate(
        ((inner_result_ref, result_ref), (inner_grad_ref, grad_ref))
    ):
        copy = pltpu.make_async_copy(ref, out_ref.at[:, pl.ds(1, rows - 2)], sems.at[i])
        copy.start()
        copies.append(copy)
    groups = 2 * mem
    slots = 2 * groups
    cells = rows * cols
    gain = gain_ref[...]
    same_head = same_head_matrix(channels)
    lat_even = is_even("lat")
    lat = lax.axis_index("lat")

    def halos(at):
        first, second = first_ref[at, :].astype(F32), second_ref[at, :].astype(F32)
        north = jnp.where(lat == 0, 0.0, jnp.where(lat_even, second, first))
        south = jnp.where(lat == lat_count - 1, 0.0, jnp.where(lat_even, first, second))
        return north, south

    halo = [halos(slice(i * cols, (i + 1) * cols)) for i in range(mem + groups)]
    corners = halos(slice((mem + groups) * cols, (mem + groups) * cols + 2 * slots))

    def corner(side, slot, end):
        at = end * slots + slot
        return corners[side][at : at + 1]

    def halo_part(scr, count, taps_ref, turned):
        north, south = (2, 0) if turned else (0, 2)
        parts = []
        for side, r in ((0, north), (1, south)):
            window = jnp.concatenate(
                [scr[m, side * cols : (side + 1) * cols, :] for m in range(count)], axis=0
            )
            parts.append(split_rows(dot_nn(window, tap_rows(taps_ref, r)), count))
        return jnp.concatenate([parts[side][m] for m in range(count) for side in (0, 1)], axis=0)

    for member in range(groups):
        slot = groups + member
        for side in (0, 1):
            ends = corner(side, slot, 0), corner(side, slot, 1)
            shift_row(cot_shift_scr, member, side, halo[mem + member][side], *ends)
    grad_field = grad_part_ref[...].reshape(groups * 2 * cols, channels)
    grad_field = grad_field + halo_part(cot_shift_scr, groups, conv_t_ref, True)

    for member in range(groups):
        corner_scr[member] = jnp.zeros((16, channels), F32)
        for side in (0, 1):
            for end in (0, 1):
                at = 2 * side + end
                corner_scr[member, at : at + 1, :] = corner(side, member, end)
    x = corner_scr[...].reshape(groups * 16, channels)
    forward = forward_cells(x, mem, groups, gain, project_ref, output_ref, same_head)
    x = [both_ref[0, m, row] for m in range(mem) for row in (0, rows - 1)]
    backward = backward_cells(
        lambda array: jnp.concatenate([array[:cols], array[cells - cols :]], axis=0),
        grad_field,
        jnp.concatenate(x, axis=0).astype(F32),
        gain,
        (project_t_ref, output_t_ref),
        proj_ref,
        unit_ref,
        soft_ref,
        inverse_ref,
        pull_ref,
    )

    def finish_result(chain):
        fresh = yield from chain
        fresh = split_rows(fresh.astype(F32), mem)
        for member in range(mem):
            for side in (0, 1):
                slab = halo[member][side]
                at = 2 * side
                ends = fresh[member][at : at + 1], fresh[member][at + 1 : at + 2]
                shift_row(shift_scr, member, side, slab, *ends)
        yield
        outer = result_part_ref[...].reshape(mem * 2 * cols, channels)
        outer = (outer + halo_part(shift_scr, mem, conv_ref, False)).astype(BF16)
        store_outer(0, outer)

    def store_outer(which, outer):
        for i, slab in enumerate(split_rows(outer, 2 * mem)):
            outer_scr[which, i % 2, i // 2] = slab
        for side, row in ((0, 0), (1, rows - 1)):
            copy = pltpu.make_async_copy(
                outer_scr.at[which, side],
                (result_ref, grad_ref)[which].at[:, row],
                sems.at[2 + 2 * which + side],
            )
            copy.start()
            copies.append(copy)

    def finish_grad(chain):
        total = yield from chain
        store_outer(1, total)

    together(finish_grad(backward), finish_result(forward))
    for copy in copies:
        copy.wait()


def local_call(kernel, name, operands, out_shape, scratch, pinned=False, cost=None, copied=False):
    whole = pl.BlockSpec(memory_space=pltpu.VMEM)
    anywhere = pl.BlockSpec(memory_space=pl.ANY)
    specs = [anywhere if in_hbm else whole for _, in_hbm in operands]
    arrays = [
        pltpu.with_memory_space_constraint(array, pltpu.HBM) if in_hbm else array
        for array, in_hbm in operands
    ]

    def keep(shape):
        return pltpu.VMEM(shape.shape, shape.dtype) if pinned else shape

    return pl.pallas_call(
        kernel,
        out_shape=jax.tree.map(keep, out_shape),
        in_specs=specs,
        out_specs=jax.tree.map(lambda _: anywhere if copied else whole, out_shape),
        scratch_shapes=scratch,
        compiler_params=pltpu.CompilerParams(vmem_limit_bytes=VMEM_LIMIT),
        cost_estimate=cost,
        name=name,
    )(*arrays)


def here(*arrays):
    return [(array, False) for array in arrays]


def in_hbm(*arrays):
    return [(array, True) for array in arrays]


def per_device_paired(ensemble, norm_gain, project_weight, output_weight, conv_kernel, cotangent):
    mem, rows, cols, channels = ensemble.shape
    if rows < 3 or cols % 16 or (2 * mem * rows) % 16:
        return per_device_general(
            ensemble, norm_gain, project_weight, output_weight, conv_kernel, cotangent
        )
    groups = 2 * mem
    slots = 2 * groups
    cells = rows * cols
    lon_count = lax.axis_size("lon")
    lat_count = lax.axis_size("lat")
    bf16 = functools.partial(jax.ShapeDtypeStruct, dtype=BF16)
    f32 = functools.partial(jax.ShapeDtypeStruct, dtype=F32)
    swap = [(0, 1), (1, 0)]
    core_pairs = [(i, i ^ 1) for i in range(lon_count)]
    chip_pairs = [(i, (i - 1 if i % 2 == 0 else i + 1) % lon_count) for i in range(lon_count)]

    def lat_swap(offset):
        pairs = []
        for lat in range(lat_count):
            for lon in range(lon_count):
                to = (lat + 1 if lat % 2 == offset else lat - 1, lon)
                if not 0 <= to[0] < lat_count:
                    to = (lat, lon ^ 1)
                pairs.append((lat * lon_count + lon, to[0] * lon_count + to[1]))
        return pairs

    ends_shape = (2, 2 * mem * rows, channels)
    both, ends = local_call(
        stack_kernel,
        "stack",
        in_hbm(ensemble, cotangent),
        (bf16((2,) + ensemble.shape), bf16(ends_shape)),
        [pltpu.VMEM(ends_shape[1:], F32)] * 2 + [pltpu.SemaphoreType.DMA((2,))],
        pinned=True,
    )
    other_ends = lax.ppermute(ends, "member", swap)
    other = lax.ppermute(both, "member", swap)

    gain, project, output, project_t, output_t = local_call(
        load_kernel,
        "load_weights",
        in_hbm(norm_gain.reshape(1, channels), project_weight, output_weight),
        (
            f32((1, channels)),
            bf16(project_weight.shape),
            bf16(output_weight.shape),
            bf16((3 * channels, channels)),
            bf16((channels, channels)),
        ),
        [pltpu.SemaphoreType.DMA((3,))],
        pinned=True,
        cost=LOAD_COST,
    )
    strip = (slots * rows, channels)
    chip_send, core_send = local_call(
        pack_strips_kernel,
        "pack_strips",
        here(ends, other_ends, gain),
        (bf16(strip), bf16(strip)),
        [pltpu.VMEM(strip, F32)] * 2,
    )
    chip = lax.ppermute(chip_send, "lon", chip_pairs)
    core = lax.ppermute(core_send, "lon", core_pairs)

    conv, *held, updated = local_call(
        own_kernel,
        "own_cells",
        here(both, other, gain, project, output)
        + in_hbm(conv_kernel.reshape(9 * channels, channels)),
        (
            bf16((9 * channels, channels)),
            bf16((groups, cells, 3 * channels)),
            bf16((2, groups, cells, channels)),
            f32((groups * groups, cells, channels)),
            f32((2, mem, cells, channels)),
            f32((2, mem, cells, channels)),
            bf16((mem, cells, channels)),
        ),
        [pltpu.SemaphoreType.DMA],
        pinned=True,
    )
    halo = bf16(((mem + groups) * cols + 2 * slots, channels))
    first_send, second_send = local_call(
        pack_rows_kernel,
        "pack_rows",
        here(both, other, chip, core, updated),
        (halo, halo),
        [pltpu.VMEM((2, 2 * slots, channels), F32)],
    )
    first = lax.ppermute(first_send, ("lat", "lon"), lat_swap(0))
    second = lax.ppermute(second_send, ("lat", "lon"), lat_swap(1))

    weights = (gain, project, output, conv)
    conv_t, *parts = local_call(
        centre_kernel,
        "centre",
        here(both, other, chip, core, *weights, project_t, output_t, *held, updated),
        (
            bf16((9 * channels, channels)),
            bf16((mem, rows - 2, cols, channels)),
            bf16((mem, rows - 2, cols, channels)),
            f32((mem, 2 * cols, channels)),
            f32((groups, 2 * cols, channels)),
        ),
        [
            pltpu.VMEM((mem, cells, 3 * channels), BF16),
            pltpu.VMEM((groups, cells, 3 * channels), BF16),
            pltpu.VMEM((groups, 16, channels), F32),
        ],
        pinned=True,
        cost=LONG,
    )
    return local_call(
        functools.partial(main_kernel, lat_count=lat_count),
        "main",
        here(both, first, second, *weights, project_t, output_t, conv_t, *held, *parts),
        (bf16(ensemble.shape), bf16(ensemble.shape)),
        [
            pltpu.VMEM((mem, 2 * cols, 3 * channels), BF16),
            pltpu.VMEM((groups, 2 * cols, 3 * channels), BF16),
            pltpu.VMEM((groups, 16, channels), F32),
            pltpu.VMEM((2, 2, mem, cols, channels), BF16),
            pltpu.SemaphoreType.DMA((6,)),
        ],
        copied=True,
    )


def solution(mesh):
    paired = mesh.shape["member"] == 2 and mesh.shape["lon"] % 2 == 0
    per_device = per_device_paired if paired else per_device_general
    in_specs = (
        P("member", "lat", "lon", None),
        P(),
        P(),
        P(),
        P(),
        P("member", "lat", "lon", None),
    )
    out_specs = (P("member", "lat", "lon", None), P("member", "lat", "lon", None))
    return jax.shard_map(
        per_device, mesh=mesh, in_specs=in_specs, out_specs=out_specs, check_vma=False
    )
```

```python
import functools
import math

import jax
import jax.numpy as jnp
from jax import lax
from jax.experimental import pallas as pl
from jax.experimental.pallas import tpu as pltpu
from jax.sharding import PartitionSpec as P

HEAD_COUNT = 8


FLOOR = 0.5
EPSILON = 1e-06


def padded_2(block, sides, width, periodic):
    for axis, dim in sides:
        count = lax.axis_size(axis)
        forward = [(i, i + 1) for i in range(count - 1)]
        if periodic:
            forward.append((count - 1, 0))
        backward = [(target, source) for source, target in forward]
        low = lax.ppermute(
            lax.slice_in_dim(block, block.shape[dim] - width, None, axis=dim), axis, forward
        )
        high = lax.ppermute(lax.slice_in_dim(block, 0, width, axis=dim), axis, backward)
        block = jnp.concatenate([low, block, high], axis=dim)
    return block


def row_norm(values, gain_vec):
    mean_sq = jnp.mean(values * values, axis=-1, keepdims=True)
    return values * lax.rsqrt(mean_sq + EPSILON) * gain_vec


def head_norm(values, head_count):
    shaped = values.reshape(values.shape[:-1] + (head_count, values.shape[-1] // head_count))
    mean_sq = jnp.mean(shaped * shaped, axis=-1, keepdims=True)
    return (shaped * lax.rsqrt(jnp.maximum(mean_sq, FLOOR))).reshape(values.shape)


def split_heads(values, head_count):
    return values.reshape(values.shape[:-1] + (head_count, values.shape[-1] // head_count))


def head_pullback(raw_rows, grad_rows):
    _, pullback = jax.vjp(lambda t: head_norm(t, HEAD_COUNT), raw_rows.astype(jnp.float32))
    return pullback(grad_rows)[0]


def pad_field(field_in):
    widened = padded_2(field_in, (("lon", 2),), 1, True)
    return padded_2(widened, (("lat", 1),), 1, False)


def conv_taps(padded, kernel, lat_n, lon_n, adjoint):
    running = None
    for row_off in range(3):
        for col_off in range(3):
            if adjoint:
                window = padded[
                    :, 2 - row_off : 2 - row_off + lat_n, 2 - col_off : 2 - col_off + lon_n
                ]
                summand = jnp.einsum(
                    "mabc,dc->mabd",
                    window,
                    kernel[row_off, col_off],
                    preferred_element_type=jnp.float32,
                )
            else:
                window = padded[:, row_off : row_off + lat_n, col_off : col_off + lon_n]
                summand = jnp.einsum(
                    "mabc,cd->mabd",
                    window,
                    kernel[row_off, col_off],
                    preferred_element_type=jnp.float32,
                )
            running = summand if running is None else running + summand
    return running


def per_device_general(ensemble, norm_gain, project_weight, output_weight, conv_kernel, cotangent):
    mem_dev, lat_dev, lon_dev, channels = ensemble.shape
    cell_count = lat_dev * lon_dev
    score_scale = 1.0 / math.sqrt(channels // HEAD_COUNT)
    inputs = ensemble.reshape(mem_dev, cell_count, channels).astype(jnp.float32)
    normed = row_norm(inputs, norm_gain).astype(jnp.bfloat16)
    spread = lax.all_to_all(normed, "member", split_axis=1, concat_axis=0, tiled=True)
    projected = jnp.dot(spread, project_weight, preferred_element_type=jnp.float32).astype(
        jnp.bfloat16
    )
    query_raw = projected[..., :channels]
    key_raw = projected[..., channels : 2 * channels]
    value_rows = projected[..., 2 * channels :]
    key_rows = head_norm(key_raw.astype(jnp.float32), HEAD_COUNT).astype(jnp.bfloat16)
    queries = head_norm(query_raw.astype(jnp.float32), HEAD_COUNT).astype(jnp.bfloat16)
    query_heads = split_heads(queries, HEAD_COUNT)
    key_heads = split_heads(key_rows, HEAD_COUNT)
    value_heads = split_heads(value_rows, HEAD_COUNT)
    scores = (
        jnp.einsum("mphd,nphd->mnhp", query_heads, key_heads, preferred_element_type=jnp.float32)
        * score_scale
    )
    expd = jnp.exp(scores)
    soft = expd / jnp.sum(expd, axis=1, keepdims=True)
    rounded = soft.astype(jnp.bfloat16)
    mixed_out = jnp.einsum(
        "mnhp,nphd->mphd", rounded, value_heads, preferred_element_type=jnp.float32
    )
    mixed_out = mixed_out.reshape(query_raw.shape).astype(jnp.bfloat16)
    mixed_out = lax.all_to_all(mixed_out, "member", split_axis=0, concat_axis=1, tiled=True)
    updated = (
        inputs + jnp.dot(mixed_out, output_weight, preferred_element_type=jnp.float32)
    ).astype(jnp.bfloat16)
    field_up = updated.reshape(mem_dev, lat_dev, lon_dev, channels)
    result = field_up.astype(jnp.float32) + conv_taps(
        pad_field(field_up), conv_kernel, lat_dev, lon_dev, False
    )
    result = result.astype(jnp.bfloat16)
    grad_field = cotangent.astype(jnp.float32) + conv_taps(
        pad_field(cotangent), conv_kernel, lat_dev, lon_dev, True
    )
    grad_rows = grad_field.reshape(mem_dev, cell_count, channels)
    grad_mixed = jnp.einsum(
        "mpc,dc->mpd",
        grad_rows.astype(jnp.bfloat16),
        output_weight,
        preferred_element_type=jnp.float32,
    )
    grad_mixed = grad_mixed.astype(jnp.bfloat16)
    grad_mixed = lax.all_to_all(grad_mixed, "member", split_axis=1, concat_axis=0, tiled=True)
    grad_heads = split_heads(grad_mixed, HEAD_COUNT)
    dprob = jnp.einsum(
        "mphd,nphd->mnhp", grad_heads, value_heads, preferred_element_type=jnp.float32
    )
    dscore = (soft * (dprob - jnp.sum(soft * dprob, axis=1, keepdims=True))).astype(jnp.bfloat16)
    query_grad = (
        jnp.einsum("mnhp,nphd->mphd", dscore, key_heads, preferred_element_type=jnp.float32)
        * score_scale
    )
    query_grad = query_grad.reshape(query_raw.shape)
    key_grad = (
        jnp.einsum("mnhp,mphd->nphd", dscore, query_heads, preferred_element_type=jnp.float32)
        * score_scale
    )
    key_grad = key_grad.reshape(key_raw.shape)
    value_grad = jnp.einsum(
        "mnhp,mphd->nphd", rounded, grad_heads, preferred_element_type=jnp.float32
    )
    value_grad = value_grad.reshape(key_raw.shape)
    grad_query_raw = head_pullback(query_raw, query_grad)
    grad_key_raw = head_pullback(key_raw, key_grad)
    grad_proj = jnp.concatenate([grad_query_raw, grad_key_raw, value_grad], axis=-1).astype(
        jnp.bfloat16
    )
    grad_proj = lax.all_to_all(grad_proj, "member", split_axis=0, concat_axis=1, tiled=True)
    grad_normed = jnp.einsum(
        "mpe,ce->mpc", grad_proj, project_weight, preferred_element_type=jnp.float32
    )
    _, pull_norm = jax.vjp(lambda t: row_norm(t, norm_gain), inputs)
    grad_inputs = pull_norm(grad_normed)[0]
    grad_ensemble = (
        (grad_rows + grad_inputs).astype(jnp.bfloat16).reshape(mem_dev, lat_dev, lon_dev, channels)
    )
    return (result, grad_ensemble)


F32 = jnp.float32
BF16 = jnp.bfloat16
VMEM_LIMIT = 24 * 1024 * 1024
LONG = pl.CostEstimate(flops=20_000_000_000, bytes_accessed=4_000_000, transcendentals=0)
MIDDLING = pl.CostEstimate(flops=3_000_000_000, bytes_accessed=2_000_000, transcendentals=0)


def is_even(axis):
    return lax.rem(lax.axis_index(axis), 2) == 0


def load_kernel(
    gain_hbm,
    project_hbm,
    output_hbm,
    conv_hbm,
    gain_ref,
    project_ref,
    output_ref,
    conv_ref,
    project_t_ref,
    output_t_ref,
    sems,
):
    channels = output_ref.shape[0]
    pairs = (
        (gain_hbm, gain_ref),
        (project_hbm, project_ref),
        (output_hbm, output_ref),
        (conv_hbm, conv_ref),
    )
    loads = [
        pltpu.make_async_copy(source, target, sems.at[i])
        for i, (source, target) in enumerate(pairs)
    ]
    for load in loads:
        load.start()
    for load in loads[:3]:
        load.wait()
    output_t_ref[...] = output_ref[...].T
    for kind in range(3):
        lanes = slice(kind * channels, (kind + 1) * channels)
        project_t_ref[lanes, :] = project_ref[:, lanes].T
    loads[3].wait()


def stack_kernel(ens_ref, cot_ref, both_ref, ends_ref, low_scr, high_scr, sems):
    _, mem, rows, cols, _ = both_ref.shape
    copies = [
        pltpu.make_async_copy(ref, both_ref.at[i], sems.at[i])
        for i, ref in enumerate((ens_ref, cot_ref))
    ]
    for copy in copies:
        copy.start()
    for copy in copies:
        copy.wait()
    index = 0
    for array in range(2):
        for member in range(mem):
            for row in range(rows):
                slab = both_ref[array, member, row].astype(F32)
                low_scr[index : index + 1, :] = slab[0:1]
                high_scr[index : index + 1, :] = slab[cols - 1 : cols]
                index += 1
    ends_ref[0] = low_scr[...].astype(BF16)
    ends_ref[1] = high_scr[...].astype(BF16)


def pack_strips_kernel(ends_ref, other_ends_ref, chip_ref, core_ref, low_scr, high_scr):
    part = ends_ref.shape[1] // 2
    for side, scr in ((0, low_scr), (1, high_scr)):
        for group, ref in enumerate((ends_ref, other_ends_ref)):
            column = ref[side].astype(F32)
            for array in range(2):
                at = (2 * array + group) * part
                scr[at : at + part, :] = column[array * part : (array + 1) * part]
    even = is_even("lon")
    low, high = low_scr[...], high_scr[...]
    core_ref[...] = jnp.where(even, high, low).astype(BF16)
    chip_ref[...] = jnp.where(even, low, high).astype(BF16)


def rim_columns(chip_ref, core_ref):
    even = is_even("lon")
    chip, core = chip_ref[...].astype(F32), core_ref[...].astype(F32)
    return jnp.where(even, chip, core), jnp.where(even, core, chip)


def pack_rows_kernel(
    both_ref, other_ref, chip_ref, core_ref, after_ref, first_ref, second_ref, edge_scr
):
    _, mem, rows, cols, _ = both_ref.shape
    slots = 4 * mem
    even = is_even("lat")
    west, east = rim_columns(chip_ref, core_ref)
    for slot in range(slots):
        array, member = divmod(slot, 2 * mem)
        ref, who = (both_ref, member) if member < mem else (other_ref, member - mem)
        start, stop = (ref[array, who, row].astype(F32) for row in (0, rows - 1))
        at = slice(slot * cols, (slot + 1) * cols)
        first_ref[at, :] = jnp.where(even, stop, start).astype(BF16)
        second_ref[at, :] = jnp.where(even, start, stop).astype(BF16)
        top, low = slot * rows, (slot + 1) * rows - 1
        for side, column in enumerate((west, east)):
            place = side * slots + slot
            start, stop = column[top : top + 1], column[low : low + 1]
            edge_scr[0, place : place + 1, :] = jnp.where(even, stop, start)
            edge_scr[1, place : place + 1, :] = jnp.where(even, start, stop)
    first_ref[slots * cols :, :] = edge_scr[0].astype(BF16)
    second_ref[slots * cols :, :] = edge_scr[1].astype(BF16)


def dot_nn(a, b):
    return lax.dot_general(a, b, (((1,), (0,)), ((), ())), preferred_element_type=F32)


def same_head_matrix(channels):
    width = channels // HEAD_COUNT
    lane_row = lax.broadcasted_iota(jnp.int32, (channels, channels), 0) // width
    lane_col = lax.broadcasted_iota(jnp.int32, (channels, channels), 1) // width
    return jnp.where(lane_row == lane_col, 1.0, 0.0).astype(BF16)


def head_sums(values, same_head):
    high = values.astype(BF16)
    low = (values - high.astype(F32)).astype(BF16)
    return dot_nn(high, same_head) + dot_nn(low, same_head)


def rounded_sums(values, same_head):
    return dot_nn(values.astype(BF16), same_head)


def head_units(raw, same_head, sums=head_sums):
    raw = raw.astype(F32)
    mean_sq = sums(raw * raw, same_head) * (HEAD_COUNT / raw.shape[-1])
    inverse = lax.rsqrt(jnp.maximum(mean_sq, FLOOR))
    return raw, mean_sq, inverse, (raw * inverse).astype(BF16)


def row_rsqrt(values):
    return lax.rsqrt(jnp.mean(values * values, axis=-1, keepdims=True) + EPSILON)


def split_rows(array, count):
    size = array.shape[0] // count
    return [array[i * size : (i + 1) * size] for i in range(count)]


def softmax_members(queries, keys, same_head, scale):
    products = [query * key for query in queries for key in keys]
    scores = dot_nn(jnp.concatenate(products, axis=0), same_head) * scale
    exps = split_rows(jnp.exp(scores), len(products))
    soft = []
    for m in range(len(queries)):
        mine = exps[m * len(keys) : (m + 1) * len(keys)]
        total = mine[0]
        for e in mine[1:]:
            total = total + e
        inverse = 1.0 / total
        soft.append([e * inverse for e in mine])
    return soft


def mix_values(probs, values):
    mixed = None
    for prob, value in zip(probs, values):
        term = prob.astype(BF16).astype(F32) * value.astype(F32)
        mixed = term if mixed is None else mixed + term
    return mixed.astype(BF16)


def forward_cells(x, mem, groups, gain, project_ref, output_ref, same_head):
    channels = x.shape[-1]
    own_rows = x.shape[0] // groups * mem
    scale = 1.0 / math.sqrt(channels // HEAD_COUNT)
    normed = (x * row_rsqrt(x) * gain).astype(BF16)
    query_raw = dot_nn(normed[:own_rows], project_ref[:, :channels]).astype(BF16)
    key_raw = dot_nn(normed, project_ref[:, channels : 2 * channels]).astype(BF16)
    values = dot_nn(normed, project_ref[:, 2 * channels :]).astype(BF16)
    yield
    raw = jnp.concatenate([query_raw, key_raw], axis=0)
    units = head_units(raw, same_head, rounded_sums)[3]
    yield
    queries = split_rows(units[:own_rows], mem)
    keys = split_rows(units[own_rows:], groups)
    values = split_rows(values, groups)
    soft = softmax_members(queries, keys, same_head, scale)
    yield
    mixed = jnp.concatenate([mix_values(soft[m], values) for m in range(mem)], axis=0)
    return (x[:own_rows] + dot_nn(mixed, output_ref[...])).astype(BF16)


def together(*chains):
    results = [None] * len(chains)
    active = list(range(len(chains)))
    while active:
        for i in list(active):
            try:
                next(chains[i])
            except StopIteration as stop:
                results[i] = stop.value
                active.remove(i)
    return results


def run(chain):
    while True:
        try:
            next(chain)
        except StopIteration as stop:
            return stop.value


def shift_row(scr, member, place, slab, west, east):
    cols, channels = slab.shape
    column = lax.broadcasted_iota(jnp.int32, (cols, channels), 0)
    back = jnp.where(column == 0, west, pltpu.roll(slab, 1, 0))
    ahead = jnp.where(column == cols - 1, east, pltpu.roll(slab, cols - 1, 0))
    rows_at = slice(place * cols, (place + 1) * cols)
    scr[member, rows_at, :channels] = back.astype(BF16)
    scr[member, rows_at, channels : 2 * channels] = slab.astype(BF16)
    scr[member, rows_at, 2 * channels :] = ahead.astype(BF16)


def tap_rows(taps_ref, r):
    size = taps_ref.shape[0] // 3
    return taps_ref[r * size : (r + 1) * size, :]


def own_kernel(
    both_ref,
    other_ref,
    gain_ref,
    project_ref,
    output_ref,
    after_ref,
    proj_ref,
    unit_ref,
    soft_ref,
    inverse_ref,
    pull_ref,
    updated_ref,
):
    _, mem, rows, cols, channels = both_ref.shape
    groups = 2 * mem
    cells = rows * cols
    width = channels // HEAD_COUNT
    scale = 1.0 / math.sqrt(width)
    same_head = same_head_matrix(channels)
    own = both_ref[0].reshape(mem * cells, channels)
    other = other_ref[0].reshape(mem * cells, channels)
    x = jnp.concatenate([own, other], axis=0).astype(F32)
    normed = (x * row_rsqrt(x) * gain_ref[...]).astype(BF16)
    proj = dot_nn(normed, project_ref[...]).astype(BF16)
    proj_ref[...] = proj.reshape(groups, cells, 3 * channels)
    both_raw = jnp.concatenate([proj[:, :channels], proj[:, channels : 2 * channels]], axis=0)
    raw, mean_sq, inverse, units = head_units(both_raw, same_head)
    unit_ref[...] = units.reshape(2, groups, cells, channels)
    active = jnp.where(mean_sq > FLOOR, 1.0, jnp.where(mean_sq == FLOOR, 0.5, 0.0))
    pull = active * raw * (inverse * inverse * inverse) / width
    for kind in range(2):
        at = kind * groups * cells
        mine = slice(at, at + mem * cells)
        inverse_ref[kind] = inverse[mine].reshape(mem, cells, channels)
        pull_ref[kind] = pull[mine].reshape(mem, cells, channels)
    units = split_rows(units, 2 * groups)
    soft = softmax_members(units[:groups], units[groups:], same_head, scale)
    for m in range(groups):
        for n in range(groups):
            soft_ref[m * groups + n] = soft[m][n]
    values = split_rows(proj[:, 2 * channels :], groups)
    mixed = jnp.concatenate([mix_values(soft[m], values) for m in range(mem)], axis=0)
    updated = x[: mem * cells] + dot_nn(mixed, output_ref[...])
    updated_ref[...] = updated.astype(BF16).reshape(mem, cells, channels)


def backward_cells(
    pick, grad_field, x, gain, weights_t, proj_ref, unit_ref, soft_ref, inverse_ref, pull_ref
):
    project_t_ref, output_t_ref = weights_t
    groups = proj_ref.shape[0]
    mem = inverse_ref.shape[1]
    channels = x.shape[-1]
    scale = 1.0 / math.sqrt(channels // HEAD_COUNT)
    same_head = same_head_matrix(channels)
    grad_mixed = dot_nn(grad_field.astype(BF16), output_t_ref[...]).astype(BF16)
    grads = split_rows(grad_mixed, groups)
    yield
    values = [pick(proj_ref[n, :, 2 * channels :]) for n in range(groups)]
    products = [grads[m] * values[n] for m in range(groups) for n in range(groups)]
    dprobs = split_rows(dot_nn(jnp.concatenate(products, axis=0), same_head), len(products))
    yield
    units = [[pick(unit_ref[k, n]).astype(F32) for n in range(groups)] for k in range(2)]
    query_grad = [None] * mem
    key_grad = [None] * mem
    value_grad = [None] * mem
    for m in range(groups):
        soft = [pick(soft_ref[m * groups + n]) for n in range(groups)]
        dprob = dprobs[m * groups : (m + 1) * groups]
        mean = soft[0] * dprob[0]
        for n in range(1, groups):
            mean = mean + soft[n] * dprob[n]
        for n in range(groups):
            if m >= mem and n >= mem:
                continue
            dscore = soft[n] * (dprob[n] - mean)
            if m < mem:
                term = dscore * units[1][n]
                query_grad[m] = term if query_grad[m] is None else query_grad[m] + term
            if n < mem:
                term = dscore * units[0][m]
                key_grad[n] = term if key_grad[n] is None else key_grad[n] + term
                term = soft[n] * grads[m].astype(F32)
                value_grad[n] = term if value_grad[n] is None else value_grad[n] + term

    unit_grads = [jnp.concatenate(g, axis=0) * scale for g in (query_grad, key_grad)]

    def members(take):
        return jnp.concatenate([pick(take(m)) for m in range(mem)], axis=0)

    raws = []
    for kind in range(2):
        lanes = slice(kind * channels, (kind + 1) * channels)
        raws.append(members(lambda m: proj_ref[m, :, lanes]).astype(F32))
    inner = rounded_sums(
        jnp.concatenate([g * raw for g, raw in zip(unit_grads, raws)], axis=0), same_head
    )
    inner = split_rows(inner, 2)
    yield
    pulled = []
    for kind in range(2):
        inverse = members(lambda m: inverse_ref[kind, m])
        pull = members(lambda m: pull_ref[kind, m])
        pulled.append((inverse * unit_grads[kind] - pull * inner[kind]).astype(BF16))
    pulled.append(jnp.concatenate(value_grad, axis=0).astype(BF16))
    grad_normed = dot_nn(jnp.concatenate(pulled, axis=1), project_t_ref[...]) * gain
    yield
    inverse = row_rsqrt(x)
    inner = jnp.mean(x * grad_normed, axis=-1, keepdims=True)
    total = grad_field[: x.shape[0]] + inverse * grad_normed
    return (total - x * (inverse * inverse * inverse * inner)).astype(BF16)


def centre_kernel(
    both_ref,
    other_ref,
    chip_ref,
    core_ref,
    gain_ref,
    project_ref,
    output_ref,
    conv_ref,
    project_t_ref,
    output_t_ref,
    proj_ref,
    unit_ref,
    soft_ref,
    inverse_ref,
    pull_ref,
    updated_ref,
    conv_t_ref,
    result_ref,
    grad_ref,
    result_part_ref,
    grad_part_ref,
    shift_scr,
    cot_shift_scr,
    strip_scr,
):
    _, mem, rows, cols, channels = both_ref.shape
    groups = 2 * mem
    cells = rows * cols
    gain = gain_ref[...]
    same_head = same_head_matrix(channels)
    west, east = rim_columns(chip_ref, core_ref)
    for r in range(3):
        for c in range(3):
            tap = (3 * r + c) * channels
            turned = (3 * r + 2 - c) * channels
            conv_t_ref[turned : turned + channels, :] = conv_ref[tap : tap + channels, :].T

    def convolve(scr, count, start, taps_ref, turned):
        sums = [
            [start[(m * rows + a) * cols : (m * rows + a + 1) * cols] for a in range(rows)]
            for m in range(count)
        ]
        for r in range(3):
            step = 1 - r if turned else r - 1
            outs = [a for a in range(rows) if 0 <= a + step < rows]
            begin, end = outs[0] + step, outs[-1] + step + 1
            window = jnp.concatenate(
                [scr[m, begin * cols : end * cols, :] for m in range(count)], axis=0
            )
            terms = split_rows(dot_nn(window, tap_rows(taps_ref, r)), count * len(outs))
            for m in range(count):
                for i, a in enumerate(outs):
                    sums[m][a] = sums[m][a] + terms[m * len(outs) + i]
        return sums

    cots = []
    for member in range(groups):
        for row in range(rows):
            ref, who = (both_ref, member) if member < mem else (other_ref, member - mem)
            slab = ref[1, who, row].astype(F32)
            cots.append(slab)
            at = (groups + member) * rows + row
            shift_row(cot_shift_scr, member, row, slab, west[at : at + 1], east[at : at + 1])
    sums = convolve(cot_shift_scr, groups, jnp.concatenate(cots, axis=0), conv_t_ref, True)
    for member in range(groups):
        grad_part_ref[member, :cols, :] = sums[member][0]
        grad_part_ref[member, cols:, :] = sums[member][rows - 1]
    grad_field = jnp.concatenate([slab for s in sums for slab in s[1 : rows - 1]], axis=0)

    for member in range(groups):
        at = member * rows
        strip_scr[member] = jnp.zeros((16, channels), F32)
        strip_scr[member, :rows, :] = west[at : at + rows]
        strip_scr[member, 8 : 8 + rows, :] = east[at : at + rows]
    x = strip_scr[...].reshape(groups * 16, channels)
    forward = forward_cells(x, mem, groups, gain, project_ref, output_ref, same_head)
    x = both_ref[0, :, 1 : rows - 1].reshape(mem * (cells - 2 * cols), channels).astype(F32)
    backward = backward_cells(
        lambda array: array[cols : cells - cols],
        grad_field,
        x,
        gain,
        (project_t_ref, output_t_ref),
        proj_ref,
        unit_ref,
        soft_ref,
        inverse_ref,
        pull_ref,
    )
    fresh, total = run(forward), run(backward)
    fresh = split_rows(fresh.astype(F32), mem)
    grad_ref[...] = total.reshape(mem, rows - 2, cols, channels)

    for member in range(mem):
        for row in range(rows):
            slab = updated_ref[member, row * cols : (row + 1) * cols, :].astype(F32)
            ends = fresh[member][row : row + 1], fresh[member][8 + row : 9 + row]
            shift_row(shift_scr, member, row, slab, *ends)
    start = updated_ref[...].reshape(mem * cells, channels).astype(F32)
    sums = convolve(shift_scr, mem, start, conv_ref, False)
    for member in range(mem):
        result_part_ref[member, :cols, :] = sums[member][0]
        result_part_ref[member, cols:, :] = sums[member][rows - 1]
        for row in range(1, rows - 1):
            result_ref[member, row - 1] = sums[member][row].astype(BF16)


def main_kernel(
    both_ref,
    second_ref,
    first_ref,
    gain_ref,
    project_ref,
    output_ref,
    conv_ref,
    project_t_ref,
    output_t_ref,
    conv_t_ref,
    proj_ref,
    unit_ref,
    soft_ref,
    inverse_ref,
    pull_ref,
    inner_result_ref,
    inner_grad_ref,
    result_part_ref,
    grad_part_ref,
    result_ref,
    grad_ref,
    shift_scr,
    cot_shift_scr,
    corner_scr,
    outer_scr,
    sems,
    *,
    lat_count,
):
    _, mem, rows, cols, channels = both_ref.shape
    copies = []
    for i, (ref, out_ref) in enumerate(
        ((inner_result_ref, result_ref), (inner_grad_ref, grad_ref))
    ):
        copy = pltpu.make_async_copy(ref, out_ref.at[:, pl.ds(1, rows - 2)], sems.at[i])
        copy.start()
        copies.append(copy)
    groups = 2 * mem
    slots = 2 * groups
    cells = rows * cols
    gain = gain_ref[...]
    same_head = same_head_matrix(channels)
    lat_even = is_even("lat")
    lat = lax.axis_index("lat")

    def halos(at):
        first, second = first_ref[at, :].astype(F32), second_ref[at, :].astype(F32)
        north = jnp.where(lat == 0, 0.0, jnp.where(lat_even, second, first))
        south = jnp.where(lat == lat_count - 1, 0.0, jnp.where(lat_even, first, second))
        return north, south

    halo = [halos(slice(slot * cols, (slot + 1) * cols)) for slot in range(slots)]
    corners = halos(slice(slots * cols, slots * cols + 2 * slots))

    def corner(side, slot, end):
        at = end * slots + slot
        return corners[side][at : at + 1]

    def halo_part(scr, count, taps_ref, turned):
        north, south = (2, 0) if turned else (0, 2)
        parts = []
        for side, r in ((0, north), (1, south)):
            window = jnp.concatenate(
                [scr[m, side * cols : (side + 1) * cols, :] for m in range(count)], axis=0
            )
            parts.append(split_rows(dot_nn(window, tap_rows(taps_ref, r)), count))
        return jnp.concatenate([parts[side][m] for m in range(count) for side in (0, 1)], axis=0)

    blocks = []
    for member in range(groups):
        corner_scr[member] = jnp.zeros((16, channels), F32)
        for side in (0, 1):
            for end in (0, 1):
                at = 2 * side + end
                corner_scr[member, at : at + 1, :] = corner(side, member, end)
        blocks += [halo[member][0], halo[member][1], corner_scr[member]]
    x = jnp.concatenate(blocks, axis=0)
    forward = forward_cells(x, mem, groups, gain, project_ref, output_ref, same_head)

    def finish_result(chain):
        fresh = yield from chain
        fresh = split_rows(fresh.astype(F32), mem)
        for member in range(mem):
            for side in (0, 1):
                slab = fresh[member][side * cols : (side + 1) * cols]
                at = 2 * cols + 2 * side
                ends = fresh[member][at : at + 1], fresh[member][at + 1 : at + 2]
                shift_row(shift_scr, member, side, slab, *ends)
        yield
        outer = result_part_ref[...].reshape(mem * 2 * cols, channels)
        outer = (outer + halo_part(shift_scr, mem, conv_ref, False)).astype(BF16)
        store_outer(0, outer)

    def store_outer(which, outer):
        for i, slab in enumerate(split_rows(outer, 2 * mem)):
            outer_scr[which, i % 2, i // 2] = slab
        for side, row in ((0, 0), (1, rows - 1)):
            copy = pltpu.make_async_copy(
                outer_scr.at[which, side],
                (result_ref, grad_ref)[which].at[:, row],
                sems.at[2 + 2 * which + side],
            )
            copy.start()
            copies.append(copy)

    result_chain = finish_result(forward)
    next(result_chain)

    for member in range(groups):
        slot = groups + member
        for side in (0, 1):
            ends = corner(side, slot, 0), corner(side, slot, 1)
            shift_row(cot_shift_scr, member, side, halo[slot][side], *ends)
    grad_field = grad_part_ref[...].reshape(groups * 2 * cols, channels)
    grad_field = grad_field + halo_part(cot_shift_scr, groups, conv_t_ref, True)

    x = [both_ref[0, m, row] for m in range(mem) for row in (0, rows - 1)]
    backward = backward_cells(
        lambda array: jnp.concatenate([array[:cols], array[cells - cols :]], axis=0),
        grad_field,
        jnp.concatenate(x, axis=0).astype(F32),
        gain,
        (project_t_ref, output_t_ref),
        proj_ref,
        unit_ref,
        soft_ref,
        inverse_ref,
        pull_ref,
    )

    def finish_grad(chain):
        total = yield from chain
        store_outer(1, total)

    together(finish_grad(backward), result_chain)
    for copy in copies:
        copy.wait()


def local_call(kernel, name, operands, out_shape, scratch, pinned=False, cost=None, copied=False):
    whole = pl.BlockSpec(memory_space=pltpu.VMEM)
    anywhere = pl.BlockSpec(memory_space=pl.ANY)
    specs = [anywhere if in_hbm else whole for _, in_hbm in operands]
    arrays = [
        pltpu.with_memory_space_constraint(array, pltpu.HBM) if in_hbm else array
        for array, in_hbm in operands
    ]

    def keep(shape):
        return pltpu.VMEM(shape.shape, shape.dtype) if pinned else shape

    return pl.pallas_call(
        kernel,
        out_shape=jax.tree.map(keep, out_shape),
        in_specs=specs,
        out_specs=jax.tree.map(lambda _: anywhere if copied else whole, out_shape),
        scratch_shapes=scratch,
        compiler_params=pltpu.CompilerParams(vmem_limit_bytes=VMEM_LIMIT),
        cost_estimate=cost,
        name=name,
    )(*arrays)


def here(*arrays):
    return [(array, False) for array in arrays]


def in_hbm(*arrays):
    return [(array, True) for array in arrays]


def per_device_paired(ensemble, norm_gain, project_weight, output_weight, conv_kernel, cotangent):
    mem, rows, cols, channels = ensemble.shape
    if rows < 3 or cols % 16 or (2 * mem * rows) % 16:
        return per_device_general(
            ensemble, norm_gain, project_weight, output_weight, conv_kernel, cotangent
        )
    groups = 2 * mem
    slots = 2 * groups
    cells = rows * cols
    lon_count = lax.axis_size("lon")
    lat_count = lax.axis_size("lat")
    bf16 = functools.partial(jax.ShapeDtypeStruct, dtype=BF16)
    f32 = functools.partial(jax.ShapeDtypeStruct, dtype=F32)
    swap = [(0, 1), (1, 0)]
    core_pairs = [(i, i ^ 1) for i in range(lon_count)]
    chip_pairs = [(i, (i - 1 if i % 2 == 0 else i + 1) % lon_count) for i in range(lon_count)]

    def lat_swap(offset):
        pairs = []
        for lat in range(lat_count):
            for lon in range(lon_count):
                to = (lat + 1 if lat % 2 == offset else lat - 1, lon)
                if not 0 <= to[0] < lat_count:
                    to = (lat, lon ^ 1)
                pairs.append((lat * lon_count + lon, to[0] * lon_count + to[1]))
        return pairs

    ends_shape = (2, 2 * mem * rows, channels)
    both, ends = local_call(
        stack_kernel,
        "stack",
        in_hbm(ensemble, cotangent),
        (bf16((2,) + ensemble.shape), bf16(ends_shape)),
        [pltpu.VMEM(ends_shape[1:], F32)] * 2 + [pltpu.SemaphoreType.DMA((2,))],
        pinned=True,
    )
    other_ends = lax.ppermute(ends, "member", swap)
    other = lax.ppermute(both, "member", swap)

    strip = (slots * rows, channels)
    chip_send, core_send = local_call(
        pack_strips_kernel,
        "pack_strips",
        here(ends, other_ends),
        (bf16(strip), bf16(strip)),
        [pltpu.VMEM(strip, F32)] * 2,
    )
    chip = lax.ppermute(chip_send, "lon", chip_pairs)
    core = lax.ppermute(core_send, "lon", core_pairs)

    weights = (
        norm_gain.reshape(1, channels),
        project_weight,
        output_weight,
        conv_kernel.reshape(9 * channels, channels),
    )
    *weights, project_t, output_t = local_call(
        load_kernel,
        "load_weights",
        in_hbm(*weights),
        tuple(jax.ShapeDtypeStruct(w.shape, w.dtype) for w in weights)
        + (bf16((3 * channels, channels)), bf16((channels, channels))),
        [pltpu.SemaphoreType.DMA((4,))],
        pinned=True,
        cost=MIDDLING,
    )
    halo = bf16((slots * (cols + 2), channels))
    first_send, second_send = local_call(
        pack_rows_kernel,
        "pack_rows",
        here(both, other, chip, core, weights[0]),
        (halo, halo),
        [pltpu.VMEM((2, 2 * slots, channels), F32)],
    )
    first = lax.ppermute(first_send, ("lat", "lon"), lat_swap(0))
    second = lax.ppermute(second_send, ("lat", "lon"), lat_swap(1))

    *held, updated = local_call(
        own_kernel,
        "own_cells",
        here(both, other, *weights[:3], second_send),
        (
            bf16((groups, cells, 3 * channels)),
            bf16((2, groups, cells, channels)),
            f32((groups * groups, cells, channels)),
            f32((2, mem, cells, channels)),
            f32((2, mem, cells, channels)),
            bf16((mem, cells, channels)),
        ),
        [],
        pinned=True,
        cost=LONG,
    )
    conv_t, *parts = local_call(
        centre_kernel,
        "centre",
        here(both, other, chip, core, *weights, project_t, output_t, *held, updated),
        (
            bf16((9 * channels, channels)),
            bf16((mem, rows - 2, cols, channels)),
            bf16((mem, rows - 2, cols, channels)),
            f32((mem, 2 * cols, channels)),
            f32((groups, 2 * cols, channels)),
        ),
        [
            pltpu.VMEM((mem, cells, 3 * channels), BF16),
            pltpu.VMEM((groups, cells, 3 * channels), BF16),
            pltpu.VMEM((groups, 16, channels), F32),
        ],
        pinned=True,
        cost=LONG,
    )
    return local_call(
        functools.partial(main_kernel, lat_count=lat_count),
        "main",
        here(both, second, first, *weights, project_t, output_t, conv_t, *held, *parts),
        (bf16(ensemble.shape), bf16(ensemble.shape)),
        [
            pltpu.VMEM((mem, 2 * cols, 3 * channels), BF16),
            pltpu.VMEM((groups, 2 * cols, 3 * channels), BF16),
            pltpu.VMEM((groups, 16, channels), F32),
            pltpu.VMEM((2, 2, mem, cols, channels), BF16),
            pltpu.SemaphoreType.DMA((6,)),
        ],
        copied=True,
    )


def solution(mesh):
    paired = mesh.shape["member"] == 2 and mesh.shape["lon"] % 2 == 0
    per_device = per_device_paired if paired else per_device_general
    in_specs = (
        P("member", "lat", "lon", None),
        P(),
        P(),
        P(),
        P(),
        P("member", "lat", "lon", None),
    )
    out_specs = (P("member", "lat", "lon", None), P("member", "lat", "lon", None))
    return jax.shard_map(
        per_device, mesh=mesh, in_specs=in_specs, out_specs=out_specs, check_vma=False
    )
```

```python
import functools
import math

import jax
import jax.numpy as jnp
from jax import lax
from jax.experimental import pallas as pl
from jax.experimental.pallas import tpu as pltpu
from jax.sharding import PartitionSpec as P

HEAD_COUNT = 8


FLOOR = 0.5
EPSILON = 1e-06


def padded_2(block, sides, width, periodic):
    for axis, dim in sides:
        count = lax.axis_size(axis)
        forward = [(i, i + 1) for i in range(count - 1)]
        if periodic:
            forward.append((count - 1, 0))
        backward = [(target, source) for source, target in forward]
        low = lax.ppermute(
            lax.slice_in_dim(block, block.shape[dim] - width, None, axis=dim), axis, forward
        )
        high = lax.ppermute(lax.slice_in_dim(block, 0, width, axis=dim), axis, backward)
        block = jnp.concatenate([low, block, high], axis=dim)
    return block


def row_norm(values, gain_vec):
    mean_sq = jnp.mean(values * values, axis=-1, keepdims=True)
    return values * lax.rsqrt(mean_sq + EPSILON) * gain_vec


def head_norm(values, head_count):
    shaped = values.reshape(values.shape[:-1] + (head_count, values.shape[-1] // head_count))
    mean_sq = jnp.mean(shaped * shaped, axis=-1, keepdims=True)
    return (shaped * lax.rsqrt(jnp.maximum(mean_sq, FLOOR))).reshape(values.shape)


def split_heads(values, head_count):
    return values.reshape(values.shape[:-1] + (head_count, values.shape[-1] // head_count))


def head_pullback(raw_rows, grad_rows):
    _, pullback = jax.vjp(lambda t: head_norm(t, HEAD_COUNT), raw_rows.astype(jnp.float32))
    return pullback(grad_rows)[0]


def pad_field(field_in):
    widened = padded_2(field_in, (("lon", 2),), 1, True)
    return padded_2(widened, (("lat", 1),), 1, False)


def conv_taps(padded, kernel, lat_n, lon_n, adjoint):
    running = None
    for row_off in range(3):
        for col_off in range(3):
            if adjoint:
                window = padded[
                    :, 2 - row_off : 2 - row_off + lat_n, 2 - col_off : 2 - col_off + lon_n
                ]
                summand = jnp.einsum(
                    "mabc,dc->mabd",
                    window,
                    kernel[row_off, col_off],
                    preferred_element_type=jnp.float32,
                )
            else:
                window = padded[:, row_off : row_off + lat_n, col_off : col_off + lon_n]
                summand = jnp.einsum(
                    "mabc,cd->mabd",
                    window,
                    kernel[row_off, col_off],
                    preferred_element_type=jnp.float32,
                )
            running = summand if running is None else running + summand
    return running


def per_device_general(ensemble, norm_gain, project_weight, output_weight, conv_kernel, cotangent):
    mem_dev, lat_dev, lon_dev, channels = ensemble.shape
    cell_count = lat_dev * lon_dev
    score_scale = 1.0 / math.sqrt(channels // HEAD_COUNT)
    inputs = ensemble.reshape(mem_dev, cell_count, channels).astype(jnp.float32)
    normed = row_norm(inputs, norm_gain).astype(jnp.bfloat16)
    spread = lax.all_to_all(normed, "member", split_axis=1, concat_axis=0, tiled=True)
    projected = jnp.dot(spread, project_weight, preferred_element_type=jnp.float32).astype(
        jnp.bfloat16
    )
    query_raw = projected[..., :channels]
    key_raw = projected[..., channels : 2 * channels]
    value_rows = projected[..., 2 * channels :]
    key_rows = head_norm(key_raw.astype(jnp.float32), HEAD_COUNT).astype(jnp.bfloat16)
    queries = head_norm(query_raw.astype(jnp.float32), HEAD_COUNT).astype(jnp.bfloat16)
    query_heads = split_heads(queries, HEAD_COUNT)
    key_heads = split_heads(key_rows, HEAD_COUNT)
    value_heads = split_heads(value_rows, HEAD_COUNT)
    scores = (
        jnp.einsum("mphd,nphd->mnhp", query_heads, key_heads, preferred_element_type=jnp.float32)
        * score_scale
    )
    expd = jnp.exp(scores)
    soft = expd / jnp.sum(expd, axis=1, keepdims=True)
    rounded = soft.astype(jnp.bfloat16)
    mixed_out = jnp.einsum(
        "mnhp,nphd->mphd", rounded, value_heads, preferred_element_type=jnp.float32
    )
    mixed_out = mixed_out.reshape(query_raw.shape).astype(jnp.bfloat16)
    mixed_out = lax.all_to_all(mixed_out, "member", split_axis=0, concat_axis=1, tiled=True)
    updated = (
        inputs + jnp.dot(mixed_out, output_weight, preferred_element_type=jnp.float32)
    ).astype(jnp.bfloat16)
    field_up = updated.reshape(mem_dev, lat_dev, lon_dev, channels)
    result = field_up.astype(jnp.float32) + conv_taps(
        pad_field(field_up), conv_kernel, lat_dev, lon_dev, False
    )
    result = result.astype(jnp.bfloat16)
    grad_field = cotangent.astype(jnp.float32) + conv_taps(
        pad_field(cotangent), conv_kernel, lat_dev, lon_dev, True
    )
    grad_rows = grad_field.reshape(mem_dev, cell_count, channels)
    grad_mixed = jnp.einsum(
        "mpc,dc->mpd",
        grad_rows.astype(jnp.bfloat16),
        output_weight,
        preferred_element_type=jnp.float32,
    )
    grad_mixed = grad_mixed.astype(jnp.bfloat16)
    grad_mixed = lax.all_to_all(grad_mixed, "member", split_axis=1, concat_axis=0, tiled=True)
    grad_heads = split_heads(grad_mixed, HEAD_COUNT)
    dprob = jnp.einsum(
        "mphd,nphd->mnhp", grad_heads, value_heads, preferred_element_type=jnp.float32
    )
    dscore = (soft * (dprob - jnp.sum(soft * dprob, axis=1, keepdims=True))).astype(jnp.bfloat16)
    query_grad = (
        jnp.einsum("mnhp,nphd->mphd", dscore, key_heads, preferred_element_type=jnp.float32)
        * score_scale
    )
    query_grad = query_grad.reshape(query_raw.shape)
    key_grad = (
        jnp.einsum("mnhp,mphd->nphd", dscore, query_heads, preferred_element_type=jnp.float32)
        * score_scale
    )
    key_grad = key_grad.reshape(key_raw.shape)
    value_grad = jnp.einsum(
        "mnhp,mphd->nphd", rounded, grad_heads, preferred_element_type=jnp.float32
    )
    value_grad = value_grad.reshape(key_raw.shape)
    grad_query_raw = head_pullback(query_raw, query_grad)
    grad_key_raw = head_pullback(key_raw, key_grad)
    grad_proj = jnp.concatenate([grad_query_raw, grad_key_raw, value_grad], axis=-1).astype(
        jnp.bfloat16
    )
    grad_proj = lax.all_to_all(grad_proj, "member", split_axis=0, concat_axis=1, tiled=True)
    grad_normed = jnp.einsum(
        "mpe,ce->mpc", grad_proj, project_weight, preferred_element_type=jnp.float32
    )
    _, pull_norm = jax.vjp(lambda t: row_norm(t, norm_gain), inputs)
    grad_inputs = pull_norm(grad_normed)[0]
    grad_ensemble = (
        (grad_rows + grad_inputs).astype(jnp.bfloat16).reshape(mem_dev, lat_dev, lon_dev, channels)
    )
    return (result, grad_ensemble)


F32 = jnp.float32
BF16 = jnp.bfloat16
VMEM_LIMIT = 24 * 1024 * 1024
LONG = pl.CostEstimate(flops=20_000_000_000, bytes_accessed=4_000_000, transcendentals=0)
MIDDLING = pl.CostEstimate(flops=3_000_000_000, bytes_accessed=2_000_000, transcendentals=0)


def is_even(axis):
    return lax.rem(lax.axis_index(axis), 2) == 0


def load_kernel(
    gain_hbm,
    project_hbm,
    output_hbm,
    conv_hbm,
    gain_ref,
    project_ref,
    output_ref,
    conv_ref,
    project_t_ref,
    output_t_ref,
    sems,
):
    channels = output_ref.shape[0]
    pairs = (
        (gain_hbm, gain_ref),
        (project_hbm, project_ref),
        (output_hbm, output_ref),
        (conv_hbm, conv_ref),
    )
    loads = [
        pltpu.make_async_copy(source, target, sems.at[i])
        for i, (source, target) in enumerate(pairs)
    ]
    for load in loads:
        load.start()
    for load in loads[:3]:
        load.wait()
    output_t_ref[...] = output_ref[...].T
    for kind in range(3):
        lanes = slice(kind * channels, (kind + 1) * channels)
        project_t_ref[lanes, :] = project_ref[:, lanes].T
    loads[3].wait()


def stack_kernel(ens_ref, cot_ref, both_ref, ends_ref, low_scr, high_scr, sems):
    _, mem, rows, cols, _ = both_ref.shape
    copies = [
        pltpu.make_async_copy(ref, both_ref.at[i], sems.at[i])
        for i, ref in enumerate((ens_ref, cot_ref))
    ]
    for copy in copies:
        copy.start()
    for copy in copies:
        copy.wait()
    index = 0
    for array in range(2):
        for member in range(mem):
            for row in range(rows):
                slab = both_ref[array, member, row].astype(F32)
                low_scr[index : index + 1, :] = slab[0:1]
                high_scr[index : index + 1, :] = slab[cols - 1 : cols]
                index += 1
    ends_ref[0] = low_scr[...].astype(BF16)
    ends_ref[1] = high_scr[...].astype(BF16)


def pack_strips_kernel(ends_ref, other_ends_ref, chip_ref, core_ref, low_scr, high_scr):
    part = ends_ref.shape[1] // 2
    for side, scr in ((0, low_scr), (1, high_scr)):
        for group, ref in enumerate((ends_ref, other_ends_ref)):
            column = ref[side].astype(F32)
            for array in range(2):
                at = (2 * array + group) * part
                scr[at : at + part, :] = column[array * part : (array + 1) * part]
    even = is_even("lon")
    low, high = low_scr[...], high_scr[...]
    core_ref[...] = jnp.where(even, high, low).astype(BF16)
    chip_ref[...] = jnp.where(even, low, high).astype(BF16)


def rim_columns(chip_ref, core_ref):
    even = is_even("lon")
    chip, core = chip_ref[...].astype(F32), core_ref[...].astype(F32)
    return jnp.where(even, chip, core), jnp.where(even, core, chip)


def pack_rows_kernel(
    both_ref, other_ref, chip_ref, core_ref, after_ref, first_ref, second_ref, edge_scr
):
    _, mem, rows, cols, _ = both_ref.shape
    slots = 4 * mem
    even = is_even("lat")
    west, east = rim_columns(chip_ref, core_ref)
    for slot in range(slots):
        array, member = divmod(slot, 2 * mem)
        ref, who = (both_ref, member) if member < mem else (other_ref, member - mem)
        start, stop = (ref[array, who, row].astype(F32) for row in (0, rows - 1))
        at = slice(slot * cols, (slot + 1) * cols)
        first_ref[at, :] = jnp.where(even, stop, start).astype(BF16)
        second_ref[at, :] = jnp.where(even, start, stop).astype(BF16)
        top, low = slot * rows, (slot + 1) * rows - 1
        for side, column in enumerate((west, east)):
            place = side * slots + slot
            start, stop = column[top : top + 1], column[low : low + 1]
            edge_scr[0, place : place + 1, :] = jnp.where(even, stop, start)
            edge_scr[1, place : place + 1, :] = jnp.where(even, start, stop)
    first_ref[slots * cols :, :] = edge_scr[0].astype(BF16)
    second_ref[slots * cols :, :] = edge_scr[1].astype(BF16)


def dot_nn(a, b):
    return lax.dot_general(a, b, (((1,), (0,)), ((), ())), preferred_element_type=F32)


def same_head_matrix(channels):
    width = channels // HEAD_COUNT
    lane_row = lax.broadcasted_iota(jnp.int32, (channels, channels), 0) // width
    lane_col = lax.broadcasted_iota(jnp.int32, (channels, channels), 1) // width
    return jnp.where(lane_row == lane_col, 1.0, 0.0).astype(BF16)


def head_sums(values, same_head):
    high = values.astype(BF16)
    low = (values - high.astype(F32)).astype(BF16)
    return dot_nn(high, same_head) + dot_nn(low, same_head)


def rounded_sums(values, same_head):
    return dot_nn(values.astype(BF16), same_head)


def head_units(raw, same_head, sums=head_sums):
    raw = raw.astype(F32)
    mean_sq = sums(raw * raw, same_head) * (HEAD_COUNT / raw.shape[-1])
    inverse = lax.rsqrt(jnp.maximum(mean_sq, FLOOR))
    return raw, mean_sq, inverse, (raw * inverse).astype(BF16)


def row_rsqrt(values):
    return lax.rsqrt(jnp.mean(values * values, axis=-1, keepdims=True) + EPSILON)


def split_rows(array, count):
    size = array.shape[0] // count
    return [array[i * size : (i + 1) * size] for i in range(count)]


def softmax_members(queries, keys, same_head, scale):
    products = [query * key for query in queries for key in keys]
    scores = dot_nn(jnp.concatenate(products, axis=0), same_head) * scale
    exps = split_rows(jnp.exp(scores), len(products))
    soft = []
    for m in range(len(queries)):
        mine = exps[m * len(keys) : (m + 1) * len(keys)]
        total = mine[0]
        for e in mine[1:]:
            total = total + e
        inverse = 1.0 / total
        soft.append([e * inverse for e in mine])
    return soft


def mix_values(probs, values):
    mixed = None
    for prob, value in zip(probs, values):
        term = prob.astype(BF16).astype(F32) * value.astype(F32)
        mixed = term if mixed is None else mixed + term
    return mixed.astype(BF16)


def forward_cells(x, mem, groups, gain, project_ref, output_ref, same_head):
    channels = x.shape[-1]
    own_rows = x.shape[0] // groups * mem
    scale = 1.0 / math.sqrt(channels // HEAD_COUNT)
    normed = (x * row_rsqrt(x) * gain).astype(BF16)
    query_raw = dot_nn(normed[:own_rows], project_ref[:, :channels]).astype(BF16)
    key_raw = dot_nn(normed, project_ref[:, channels : 2 * channels]).astype(BF16)
    values = dot_nn(normed, project_ref[:, 2 * channels :]).astype(BF16)
    yield
    raw = jnp.concatenate([query_raw, key_raw], axis=0)
    units = head_units(raw, same_head, rounded_sums)[3]
    yield
    queries = split_rows(units[:own_rows], mem)
    keys = split_rows(units[own_rows:], groups)
    values = split_rows(values, groups)
    soft = softmax_members(queries, keys, same_head, scale)
    yield
    mixed = jnp.concatenate([mix_values(soft[m], values) for m in range(mem)], axis=0)
    return (x[:own_rows] + dot_nn(mixed, output_ref[...])).astype(BF16)


def together(*chains):
    results = [None] * len(chains)
    active = list(range(len(chains)))
    while active:
        for i in list(active):
            try:
                next(chains[i])
            except StopIteration as stop:
                results[i] = stop.value
                active.remove(i)
    return results


def run(chain):
    while True:
        try:
            next(chain)
        except StopIteration as stop:
            return stop.value


def shift_row(scr, member, place, slab, west, east):
    cols, channels = slab.shape
    column = lax.broadcasted_iota(jnp.int32, (cols, channels), 0)
    back = jnp.where(column == 0, west, pltpu.roll(slab, 1, 0))
    ahead = jnp.where(column == cols - 1, east, pltpu.roll(slab, cols - 1, 0))
    rows_at = slice(place * cols, (place + 1) * cols)
    scr[member, rows_at, :channels] = back.astype(BF16)
    scr[member, rows_at, channels : 2 * channels] = slab.astype(BF16)
    scr[member, rows_at, 2 * channels :] = ahead.astype(BF16)


def tap_rows(taps_ref, r):
    size = taps_ref.shape[0] // 3
    return taps_ref[r * size : (r + 1) * size, :]


def own_kernel(
    both_ref,
    other_ref,
    gain_ref,
    project_ref,
    output_ref,
    after_ref,
    proj_ref,
    unit_ref,
    soft_ref,
    inverse_ref,
    pull_ref,
    updated_ref,
):
    _, mem, rows, cols, channels = both_ref.shape
    groups = 2 * mem
    cells = rows * cols
    width = channels // HEAD_COUNT
    scale = 1.0 / math.sqrt(width)
    same_head = same_head_matrix(channels)
    own = both_ref[0].reshape(mem * cells, channels)
    other = other_ref[0].reshape(mem * cells, channels)
    x = jnp.concatenate([own, other], axis=0).astype(F32)
    normed = (x * row_rsqrt(x) * gain_ref[...]).astype(BF16)
    proj = dot_nn(normed, project_ref[...]).astype(BF16)
    proj_ref[...] = proj.reshape(groups, cells, 3 * channels)
    both_raw = jnp.concatenate([proj[:, :channels], proj[:, channels : 2 * channels]], axis=0)
    raw, mean_sq, inverse, units = head_units(both_raw, same_head)
    unit_ref[...] = units.reshape(2, groups, cells, channels)
    active = jnp.where(mean_sq > FLOOR, 1.0, jnp.where(mean_sq == FLOOR, 0.5, 0.0))
    pull = active * raw * (inverse * inverse * inverse) / width
    for kind in range(2):
        at = kind * groups * cells
        mine = slice(at, at + mem * cells)
        inverse_ref[kind] = inverse[mine].reshape(mem, cells, channels)
        pull_ref[kind] = pull[mine].reshape(mem, cells, channels)
    units = split_rows(units, 2 * groups)
    soft = softmax_members(units[:groups], units[groups:], same_head, scale)
    for m in range(groups):
        for n in range(groups):
            soft_ref[m * groups + n] = soft[m][n]
    values = split_rows(proj[:, 2 * channels :], groups)
    mixed = jnp.concatenate([mix_values(soft[m], values) for m in range(mem)], axis=0)
    updated = x[: mem * cells] + dot_nn(mixed, output_ref[...])
    updated_ref[...] = updated.astype(BF16).reshape(mem, cells, channels)


def backward_cells(
    pick, grad_field, x, gain, weights_t, proj_ref, unit_ref, soft_ref, inverse_ref, pull_ref
):
    project_t_ref, output_t_ref = weights_t
    groups = proj_ref.shape[0]
    mem = inverse_ref.shape[1]
    channels = x.shape[-1]
    scale = 1.0 / math.sqrt(channels // HEAD_COUNT)
    same_head = same_head_matrix(channels)
    grad_mixed = dot_nn(grad_field.astype(BF16), output_t_ref[...]).astype(BF16)
    grads = split_rows(grad_mixed, groups)
    yield
    values = [pick(proj_ref[n, :, 2 * channels :]) for n in range(groups)]
    products = [grads[m] * values[n] for m in range(groups) for n in range(groups)]
    dprobs = split_rows(dot_nn(jnp.concatenate(products, axis=0), same_head), len(products))
    yield
    units = [[pick(unit_ref[k, n]).astype(F32) for n in range(groups)] for k in range(2)]
    query_grad = [None] * mem
    key_grad = [None] * mem
    value_grad = [None] * mem
    for m in range(groups):
        soft = [pick(soft_ref[m * groups + n]) for n in range(groups)]
        dprob = dprobs[m * groups : (m + 1) * groups]
        mean = soft[0] * dprob[0]
        for n in range(1, groups):
            mean = mean + soft[n] * dprob[n]
        for n in range(groups):
            if m >= mem and n >= mem:
                continue
            dscore = soft[n] * (dprob[n] - mean)
            if m < mem:
                term = dscore * units[1][n]
                query_grad[m] = term if query_grad[m] is None else query_grad[m] + term
            if n < mem:
                term = dscore * units[0][m]
                key_grad[n] = term if key_grad[n] is None else key_grad[n] + term
                term = soft[n] * grads[m].astype(F32)
                value_grad[n] = term if value_grad[n] is None else value_grad[n] + term

    unit_grads = [jnp.concatenate(g, axis=0) * scale for g in (query_grad, key_grad)]

    def members(take):
        return jnp.concatenate([pick(take(m)) for m in range(mem)], axis=0)

    raws = []
    for kind in range(2):
        lanes = slice(kind * channels, (kind + 1) * channels)
        raws.append(members(lambda m: proj_ref[m, :, lanes]).astype(F32))
    inner = rounded_sums(
        jnp.concatenate([g * raw for g, raw in zip(unit_grads, raws)], axis=0), same_head
    )
    inner = split_rows(inner, 2)
    yield
    pulled = []
    for kind in range(2):
        inverse = members(lambda m: inverse_ref[kind, m])
        pull = members(lambda m: pull_ref[kind, m])
        pulled.append((inverse * unit_grads[kind] - pull * inner[kind]).astype(BF16))
    pulled.append(jnp.concatenate(value_grad, axis=0).astype(BF16))
    grad_normed = dot_nn(jnp.concatenate(pulled, axis=1), project_t_ref[...]) * gain
    yield
    inverse = row_rsqrt(x)
    inner = jnp.mean(x * grad_normed, axis=-1, keepdims=True)
    total = grad_field[: x.shape[0]] + inverse * grad_normed
    return (total - x * (inverse * inverse * inverse * inner)).astype(BF16)


def centre_kernel(
    both_ref,
    other_ref,
    chip_ref,
    core_ref,
    gain_ref,
    project_ref,
    output_ref,
    conv_ref,
    project_t_ref,
    output_t_ref,
    proj_ref,
    unit_ref,
    soft_ref,
    inverse_ref,
    pull_ref,
    updated_ref,
    conv_t_ref,
    result_ref,
    grad_ref,
    result_part_ref,
    grad_part_ref,
    shift_scr,
    cot_shift_scr,
    strip_scr,
):
    _, mem, rows, cols, channels = both_ref.shape
    groups = 2 * mem
    cells = rows * cols
    gain = gain_ref[...]
    same_head = same_head_matrix(channels)
    west, east = rim_columns(chip_ref, core_ref)
    for r in range(3):
        for c in range(3):
            tap = (3 * r + c) * channels
            turned = (3 * r + 2 - c) * channels
            conv_t_ref[turned : turned + channels, :] = conv_ref[tap : tap + channels, :].T

    def convolve(scr, count, start, taps_ref, turned):
        sums = [
            [start[(m * rows + a) * cols : (m * rows + a + 1) * cols] for a in range(rows)]
            for m in range(count)
        ]
        for r in range(3):
            step = 1 - r if turned else r - 1
            outs = [a for a in range(rows) if 0 <= a + step < rows]
            begin, end = outs[0] + step, outs[-1] + step + 1
            window = jnp.concatenate(
                [scr[m, begin * cols : end * cols, :] for m in range(count)], axis=0
            )
            terms = split_rows(dot_nn(window, tap_rows(taps_ref, r)), count * len(outs))
            for m in range(count):
                for i, a in enumerate(outs):
                    sums[m][a] = sums[m][a] + terms[m * len(outs) + i]
        return sums

    cots = []
    for member in range(groups):
        for row in range(rows):
            ref, who = (both_ref, member) if member < mem else (other_ref, member - mem)
            slab = ref[1, who, row].astype(F32)
            cots.append(slab)
            at = (groups + member) * rows + row
            shift_row(cot_shift_scr, member, row, slab, west[at : at + 1], east[at : at + 1])
    sums = convolve(cot_shift_scr, groups, jnp.concatenate(cots, axis=0), conv_t_ref, True)
    for member in range(groups):
        grad_part_ref[member, :cols, :] = sums[member][0]
        grad_part_ref[member, cols:, :] = sums[member][rows - 1]
    grad_field = jnp.concatenate([slab for s in sums for slab in s[1 : rows - 1]], axis=0)

    for member in range(groups):
        at = member * rows
        strip_scr[member] = jnp.zeros((16, channels), F32)
        strip_scr[member, :rows, :] = west[at : at + rows]
        strip_scr[member, 8 : 8 + rows, :] = east[at : at + rows]
    x = strip_scr[...].reshape(groups * 16, channels)
    forward = forward_cells(x, mem, groups, gain, project_ref, output_ref, same_head)
    x = both_ref[0, :, 1 : rows - 1].reshape(mem * (cells - 2 * cols), channels).astype(F32)
    backward = backward_cells(
        lambda array: array[cols : cells - cols],
        grad_field,
        x,
        gain,
        (project_t_ref, output_t_ref),
        proj_ref,
        unit_ref,
        soft_ref,
        inverse_ref,
        pull_ref,
    )
    total, fresh = run(backward), run(forward)
    fresh = split_rows(fresh.astype(F32), mem)
    grad_ref[...] = total.reshape(mem, rows - 2, cols, channels)

    for member in range(mem):
        for row in range(rows):
            slab = updated_ref[member, row * cols : (row + 1) * cols, :].astype(F32)
            ends = fresh[member][row : row + 1], fresh[member][8 + row : 9 + row]
            shift_row(shift_scr, member, row, slab, *ends)
    start = updated_ref[...].reshape(mem * cells, channels).astype(F32)
    sums = convolve(shift_scr, mem, start, conv_ref, False)
    for member in range(mem):
        result_part_ref[member, :cols, :] = sums[member][0]
        result_part_ref[member, cols:, :] = sums[member][rows - 1]
        for row in range(1, rows - 1):
            result_ref[member, row - 1] = sums[member][row].astype(BF16)


def main_kernel(
    both_ref,
    second_ref,
    first_ref,
    gain_ref,
    project_ref,
    output_ref,
    conv_ref,
    project_t_ref,
    output_t_ref,
    conv_t_ref,
    proj_ref,
    unit_ref,
    soft_ref,
    inverse_ref,
    pull_ref,
    inner_result_ref,
    inner_grad_ref,
    result_part_ref,
    grad_part_ref,
    result_ref,
    grad_ref,
    shift_scr,
    cot_shift_scr,
    corner_scr,
    outer_scr,
    sems,
    *,
    lat_count,
):
    _, mem, rows, cols, channels = both_ref.shape
    copies = []
    for i, (ref, out_ref) in enumerate(
        ((inner_result_ref, result_ref), (inner_grad_ref, grad_ref))
    ):
        copy = pltpu.make_async_copy(ref, out_ref.at[:, pl.ds(1, rows - 2)], sems.at[i])
        copy.start()
        copies.append(copy)
    groups = 2 * mem
    slots = 2 * groups
    cells = rows * cols
    gain = gain_ref[...]
    same_head = same_head_matrix(channels)
    lat_even = is_even("lat")
    lat = lax.axis_index("lat")

    def halos(at):
        first, second = first_ref[at, :].astype(F32), second_ref[at, :].astype(F32)
        north = jnp.where(lat == 0, 0.0, jnp.where(lat_even, second, first))
        south = jnp.where(lat == lat_count - 1, 0.0, jnp.where(lat_even, first, second))
        return north, south

    halo = [halos(slice(slot * cols, (slot + 1) * cols)) for slot in range(slots)]
    corners = halos(slice(slots * cols, slots * cols + 2 * slots))

    def corner(side, slot, end):
        at = end * slots + slot
        return corners[side][at : at + 1]

    def halo_part(scr, count, taps_ref, turned):
        north, south = (2, 0) if turned else (0, 2)
        parts = []
        for side, r in ((0, north), (1, south)):
            window = jnp.concatenate(
                [scr[m, side * cols : (side + 1) * cols, :] for m in range(count)], axis=0
            )
            parts.append(split_rows(dot_nn(window, tap_rows(taps_ref, r)), count))
        return jnp.concatenate([parts[side][m] for m in range(count) for side in (0, 1)], axis=0)

    for member in range(groups):
        slot = groups + member
        for side in (0, 1):
            ends = corner(side, slot, 0), corner(side, slot, 1)
            shift_row(cot_shift_scr, member, side, halo[slot][side], *ends)
    grad_field = grad_part_ref[...].reshape(groups * 2 * cols, channels)
    grad_field = grad_field + halo_part(cot_shift_scr, groups, conv_t_ref, True)

    blocks = []
    for member in range(groups):
        corner_scr[member] = jnp.zeros((16, channels), F32)
        for side in (0, 1):
            for end in (0, 1):
                at = 2 * side + end
                corner_scr[member, at : at + 1, :] = corner(side, member, end)
        blocks += [halo[member][0], halo[member][1], corner_scr[member]]
    x = jnp.concatenate(blocks, axis=0)
    forward = forward_cells(x, mem, groups, gain, project_ref, output_ref, same_head)
    x = [both_ref[0, m, row] for m in range(mem) for row in (0, rows - 1)]
    backward = backward_cells(
        lambda array: jnp.concatenate([array[:cols], array[cells - cols :]], axis=0),
        grad_field,
        jnp.concatenate(x, axis=0).astype(F32),
        gain,
        (project_t_ref, output_t_ref),
        proj_ref,
        unit_ref,
        soft_ref,
        inverse_ref,
        pull_ref,
    )

    def finish_result(chain):
        fresh = yield from chain
        fresh = split_rows(fresh.astype(F32), mem)
        for member in range(mem):
            for side in (0, 1):
                slab = fresh[member][side * cols : (side + 1) * cols]
                at = 2 * cols + 2 * side
                ends = fresh[member][at : at + 1], fresh[member][at + 1 : at + 2]
                shift_row(shift_scr, member, side, slab, *ends)
        yield
        outer = result_part_ref[...].reshape(mem * 2 * cols, channels)
        outer = (outer + halo_part(shift_scr, mem, conv_ref, False)).astype(BF16)
        store_outer(0, outer)

    def store_outer(which, outer):
        for i, slab in enumerate(split_rows(outer, 2 * mem)):
            outer_scr[which, i % 2, i // 2] = slab
        for side, row in ((0, 0), (1, rows - 1)):
            copy = pltpu.make_async_copy(
                outer_scr.at[which, side],
                (result_ref, grad_ref)[which].at[:, row],
                sems.at[2 + 2 * which + side],
            )
            copy.start()
            copies.append(copy)

    def finish_grad(chain):
        total = yield from chain
        store_outer(1, total)

    grad_chain = finish_grad(backward)
    next(grad_chain)
    together(grad_chain, finish_result(forward))
    for copy in copies:
        copy.wait()


def local_call(kernel, name, operands, out_shape, scratch, pinned=False, cost=None, copied=False):
    whole = pl.BlockSpec(memory_space=pltpu.VMEM)
    anywhere = pl.BlockSpec(memory_space=pl.ANY)
    specs = [anywhere if in_hbm else whole for _, in_hbm in operands]
    arrays = [
        pltpu.with_memory_space_constraint(array, pltpu.HBM) if in_hbm else array
        for array, in_hbm in operands
    ]

    def keep(shape):
        return pltpu.VMEM(shape.shape, shape.dtype) if pinned else shape

    return pl.pallas_call(
        kernel,
        out_shape=jax.tree.map(keep, out_shape),
        in_specs=specs,
        out_specs=jax.tree.map(lambda _: anywhere if copied else whole, out_shape),
        scratch_shapes=scratch,
        compiler_params=pltpu.CompilerParams(vmem_limit_bytes=VMEM_LIMIT),
        cost_estimate=cost,
        name=name,
    )(*arrays)


def here(*arrays):
    return [(array, False) for array in arrays]


def in_hbm(*arrays):
    return [(array, True) for array in arrays]


def per_device_paired(ensemble, norm_gain, project_weight, output_weight, conv_kernel, cotangent):
    mem, rows, cols, channels = ensemble.shape
    if rows < 3 or cols % 16 or (2 * mem * rows) % 16:
        return per_device_general(
            ensemble, norm_gain, project_weight, output_weight, conv_kernel, cotangent
        )
    groups = 2 * mem
    slots = 2 * groups
    cells = rows * cols
    lon_count = lax.axis_size("lon")
    lat_count = lax.axis_size("lat")
    bf16 = functools.partial(jax.ShapeDtypeStruct, dtype=BF16)
    f32 = functools.partial(jax.ShapeDtypeStruct, dtype=F32)
    swap = [(0, 1), (1, 0)]
    core_pairs = [(i, i ^ 1) for i in range(lon_count)]
    chip_pairs = [(i, (i - 1 if i % 2 == 0 else i + 1) % lon_count) for i in range(lon_count)]

    def lat_swap(offset):
        pairs = []
        for lat in range(lat_count):
            for lon in range(lon_count):
                to = (lat + 1 if lat % 2 == offset else lat - 1, lon)
                if not 0 <= to[0] < lat_count:
                    to = (lat, lon ^ 1)
                pairs.append((lat * lon_count + lon, to[0] * lon_count + to[1]))
        return pairs

    ends_shape = (2, 2 * mem * rows, channels)
    both, ends = local_call(
        stack_kernel,
        "stack",
        in_hbm(ensemble, cotangent),
        (bf16((2,) + ensemble.shape), bf16(ends_shape)),
        [pltpu.VMEM(ends_shape[1:], F32)] * 2 + [pltpu.SemaphoreType.DMA((2,))],
        pinned=True,
    )
    other_ends = lax.ppermute(ends, "member", swap)
    other = lax.ppermute(both, "member", swap)

    strip = (slots * rows, channels)
    chip_send, core_send = local_call(
        pack_strips_kernel,
        "pack_strips",
        here(ends, other_ends),
        (bf16(strip), bf16(strip)),
        [pltpu.VMEM(strip, F32)] * 2,
    )
    chip = lax.ppermute(chip_send, "lon", chip_pairs)
    core = lax.ppermute(core_send, "lon", core_pairs)

    weights = (
        norm_gain.reshape(1, channels),
        project_weight,
        output_weight,
        conv_kernel.reshape(9 * channels, channels),
    )
    *weights, project_t, output_t = local_call(
        load_kernel,
        "load_weights",
        in_hbm(*weights),
        tuple(jax.ShapeDtypeStruct(w.shape, w.dtype) for w in weights)
        + (bf16((3 * channels, channels)), bf16((channels, channels))),
        [pltpu.SemaphoreType.DMA((4,))],
        pinned=True,
        cost=MIDDLING,
    )
    halo = bf16((slots * (cols + 2), channels))
    first_send, second_send = local_call(
        pack_rows_kernel,
        "pack_rows",
        here(both, other, chip, core, weights[0]),
        (halo, halo),
        [pltpu.VMEM((2, 2 * slots, channels), F32)],
    )
    first = lax.ppermute(first_send, ("lat", "lon"), lat_swap(0))
    second = lax.ppermute(second_send, ("lat", "lon"), lat_swap(1))

    *held, updated = local_call(
        own_kernel,
        "own_cells",
        here(both, other, *weights[:3], second_send),
        (
            bf16((groups, cells, 3 * channels)),
            bf16((2, groups, cells, channels)),
            f32((groups * groups, cells, channels)),
            f32((2, mem, cells, channels)),
            f32((2, mem, cells, channels)),
            bf16((mem, cells, channels)),
        ),
        [],
        pinned=True,
        cost=LONG,
    )
    conv_t, *parts = local_call(
        centre_kernel,
        "centre",
        here(both, other, chip, core, *weights, project_t, output_t, *held, updated),
        (
            bf16((9 * channels, channels)),
            bf16((mem, rows - 2, cols, channels)),
            bf16((mem, rows - 2, cols, channels)),
            f32((mem, 2 * cols, channels)),
            f32((groups, 2 * cols, channels)),
        ),
        [
            pltpu.VMEM((mem, cells, 3 * channels), BF16),
            pltpu.VMEM((groups, cells, 3 * channels), BF16),
            pltpu.VMEM((groups, 16, channels), F32),
        ],
        pinned=True,
        cost=LONG,
    )
    return local_call(
        functools.partial(main_kernel, lat_count=lat_count),
        "main",
        here(both, second, first, *weights, project_t, output_t, conv_t, *held, *parts),
        (bf16(ensemble.shape), bf16(ensemble.shape)),
        [
            pltpu.VMEM((mem, 2 * cols, 3 * channels), BF16),
            pltpu.VMEM((groups, 2 * cols, 3 * channels), BF16),
            pltpu.VMEM((groups, 16, channels), F32),
            pltpu.VMEM((2, 2, mem, cols, channels), BF16),
            pltpu.SemaphoreType.DMA((6,)),
        ],
        copied=True,
    )


def solution(mesh):
    paired = mesh.shape["member"] == 2 and mesh.shape["lon"] % 2 == 0
    per_device = per_device_paired if paired else per_device_general
    in_specs = (
        P("member", "lat", "lon", None),
        P(),
        P(),
        P(),
        P(),
        P("member", "lat", "lon", None),
    )
    out_specs = (P("member", "lat", "lon", None), P("member", "lat", "lon", None))
    return jax.shard_map(
        per_device, mesh=mesh, in_specs=in_specs, out_specs=out_specs, check_vma=False
    )
```

```python
import functools
import math

import jax
import jax.numpy as jnp
from jax import lax
from jax.experimental import pallas as pl
from jax.experimental.pallas import tpu as pltpu
from jax.sharding import PartitionSpec as P

HEAD_COUNT = 8


FLOOR = 0.5
EPSILON = 1e-06


def padded_2(block, sides, width, periodic):
    for axis, dim in sides:
        count = lax.axis_size(axis)
        forward = [(i, i + 1) for i in range(count - 1)]
        if periodic:
            forward.append((count - 1, 0))
        backward = [(target, source) for source, target in forward]
        low = lax.ppermute(
            lax.slice_in_dim(block, block.shape[dim] - width, None, axis=dim), axis, forward
        )
        high = lax.ppermute(lax.slice_in_dim(block, 0, width, axis=dim), axis, backward)
        block = jnp.concatenate([low, block, high], axis=dim)
    return block


def row_norm(values, gain_vec):
    mean_sq = jnp.mean(values * values, axis=-1, keepdims=True)
    return values * lax.rsqrt(mean_sq + EPSILON) * gain_vec


def head_norm(values, head_count):
    shaped = values.reshape(values.shape[:-1] + (head_count, values.shape[-1] // head_count))
    mean_sq = jnp.mean(shaped * shaped, axis=-1, keepdims=True)
    return (shaped * lax.rsqrt(jnp.maximum(mean_sq, FLOOR))).reshape(values.shape)


def split_heads(values, head_count):
    return values.reshape(values.shape[:-1] + (head_count, values.shape[-1] // head_count))


def head_pullback(raw_rows, grad_rows):
    _, pullback = jax.vjp(lambda t: head_norm(t, HEAD_COUNT), raw_rows.astype(jnp.float32))
    return pullback(grad_rows)[0]


def pad_field(field_in):
    widened = padded_2(field_in, (("lon", 2),), 1, True)
    return padded_2(widened, (("lat", 1),), 1, False)


def conv_taps(padded, kernel, lat_n, lon_n, adjoint):
    running = None
    for row_off in range(3):
        for col_off in range(3):
            if adjoint:
                window = padded[
                    :, 2 - row_off : 2 - row_off + lat_n, 2 - col_off : 2 - col_off + lon_n
                ]
                summand = jnp.einsum(
                    "mabc,dc->mabd",
                    window,
                    kernel[row_off, col_off],
                    preferred_element_type=jnp.float32,
                )
            else:
                window = padded[:, row_off : row_off + lat_n, col_off : col_off + lon_n]
                summand = jnp.einsum(
                    "mabc,cd->mabd",
                    window,
                    kernel[row_off, col_off],
                    preferred_element_type=jnp.float32,
                )
            running = summand if running is None else running + summand
    return running


def per_device_general(ensemble, norm_gain, project_weight, output_weight, conv_kernel, cotangent):
    mem_dev, lat_dev, lon_dev, channels = ensemble.shape
    cell_count = lat_dev * lon_dev
    score_scale = 1.0 / math.sqrt(channels // HEAD_COUNT)
    inputs = ensemble.reshape(mem_dev, cell_count, channels).astype(jnp.float32)
    normed = row_norm(inputs, norm_gain).astype(jnp.bfloat16)
    spread = lax.all_to_all(normed, "member", split_axis=1, concat_axis=0, tiled=True)
    projected = jnp.dot(spread, project_weight, preferred_element_type=jnp.float32).astype(
        jnp.bfloat16
    )
    query_raw = projected[..., :channels]
    key_raw = projected[..., channels : 2 * channels]
    value_rows = projected[..., 2 * channels :]
    key_rows = head_norm(key_raw.astype(jnp.float32), HEAD_COUNT).astype(jnp.bfloat16)
    queries = head_norm(query_raw.astype(jnp.float32), HEAD_COUNT).astype(jnp.bfloat16)
    query_heads = split_heads(queries, HEAD_COUNT)
    key_heads = split_heads(key_rows, HEAD_COUNT)
    value_heads = split_heads(value_rows, HEAD_COUNT)
    scores = (
        jnp.einsum("mphd,nphd->mnhp", query_heads, key_heads, preferred_element_type=jnp.float32)
        * score_scale
    )
    expd = jnp.exp(scores)
    soft = expd / jnp.sum(expd, axis=1, keepdims=True)
    rounded = soft.astype(jnp.bfloat16)
    mixed_out = jnp.einsum(
        "mnhp,nphd->mphd", rounded, value_heads, preferred_element_type=jnp.float32
    )
    mixed_out = mixed_out.reshape(query_raw.shape).astype(jnp.bfloat16)
    mixed_out = lax.all_to_all(mixed_out, "member", split_axis=0, concat_axis=1, tiled=True)
    updated = (
        inputs + jnp.dot(mixed_out, output_weight, preferred_element_type=jnp.float32)
    ).astype(jnp.bfloat16)
    field_up = updated.reshape(mem_dev, lat_dev, lon_dev, channels)
    result = field_up.astype(jnp.float32) + conv_taps(
        pad_field(field_up), conv_kernel, lat_dev, lon_dev, False
    )
    result = result.astype(jnp.bfloat16)
    grad_field = cotangent.astype(jnp.float32) + conv_taps(
        pad_field(cotangent), conv_kernel, lat_dev, lon_dev, True
    )
    grad_rows = grad_field.reshape(mem_dev, cell_count, channels)
    grad_mixed = jnp.einsum(
        "mpc,dc->mpd",
        grad_rows.astype(jnp.bfloat16),
        output_weight,
        preferred_element_type=jnp.float32,
    )
    grad_mixed = grad_mixed.astype(jnp.bfloat16)
    grad_mixed = lax.all_to_all(grad_mixed, "member", split_axis=1, concat_axis=0, tiled=True)
    grad_heads = split_heads(grad_mixed, HEAD_COUNT)
    dprob = jnp.einsum(
        "mphd,nphd->mnhp", grad_heads, value_heads, preferred_element_type=jnp.float32
    )
    dscore = (soft * (dprob - jnp.sum(soft * dprob, axis=1, keepdims=True))).astype(jnp.bfloat16)
    query_grad = (
        jnp.einsum("mnhp,nphd->mphd", dscore, key_heads, preferred_element_type=jnp.float32)
        * score_scale
    )
    query_grad = query_grad.reshape(query_raw.shape)
    key_grad = (
        jnp.einsum("mnhp,mphd->nphd", dscore, query_heads, preferred_element_type=jnp.float32)
        * score_scale
    )
    key_grad = key_grad.reshape(key_raw.shape)
    value_grad = jnp.einsum(
        "mnhp,mphd->nphd", rounded, grad_heads, preferred_element_type=jnp.float32
    )
    value_grad = value_grad.reshape(key_raw.shape)
    grad_query_raw = head_pullback(query_raw, query_grad)
    grad_key_raw = head_pullback(key_raw, key_grad)
    grad_proj = jnp.concatenate([grad_query_raw, grad_key_raw, value_grad], axis=-1).astype(
        jnp.bfloat16
    )
    grad_proj = lax.all_to_all(grad_proj, "member", split_axis=0, concat_axis=1, tiled=True)
    grad_normed = jnp.einsum(
        "mpe,ce->mpc", grad_proj, project_weight, preferred_element_type=jnp.float32
    )
    _, pull_norm = jax.vjp(lambda t: row_norm(t, norm_gain), inputs)
    grad_inputs = pull_norm(grad_normed)[0]
    grad_ensemble = (
        (grad_rows + grad_inputs).astype(jnp.bfloat16).reshape(mem_dev, lat_dev, lon_dev, channels)
    )
    return (result, grad_ensemble)


F32 = jnp.float32
BF16 = jnp.bfloat16
VMEM_LIMIT = 24 * 1024 * 1024
LONG = pl.CostEstimate(flops=20_000_000_000, bytes_accessed=4_000_000, transcendentals=0)
MIDDLING = pl.CostEstimate(flops=3_000_000_000, bytes_accessed=2_000_000, transcendentals=0)


def is_even(axis):
    return lax.rem(lax.axis_index(axis), 2) == 0


def load_kernel(
    gain_hbm,
    project_hbm,
    output_hbm,
    conv_hbm,
    gain_ref,
    project_ref,
    output_ref,
    conv_ref,
    project_t_ref,
    output_t_ref,
    sems,
):
    channels = output_ref.shape[0]
    pairs = (
        (gain_hbm, gain_ref),
        (project_hbm, project_ref),
        (output_hbm, output_ref),
        (conv_hbm, conv_ref),
    )
    loads = [
        pltpu.make_async_copy(source, target, sems.at[i])
        for i, (source, target) in enumerate(pairs)
    ]
    for load in loads:
        load.start()
    for load in loads[:3]:
        load.wait()
    output_t_ref[...] = output_ref[...].T
    for kind in range(3):
        lanes = slice(kind * channels, (kind + 1) * channels)
        project_t_ref[lanes, :] = project_ref[:, lanes].T
    loads[3].wait()


def stack_kernel(ens_ref, cot_ref, both_ref, ends_ref, low_scr, high_scr, sems):
    _, mem, rows, cols, _ = both_ref.shape
    copies = [
        pltpu.make_async_copy(ref, both_ref.at[i], sems.at[i])
        for i, ref in enumerate((ens_ref, cot_ref))
    ]
    for copy in copies:
        copy.start()
    for copy in copies:
        copy.wait()
    index = 0
    for array in range(2):
        for member in range(mem):
            for row in range(rows):
                slab = both_ref[array, member, row].astype(F32)
                low_scr[index : index + 1, :] = slab[0:1]
                high_scr[index : index + 1, :] = slab[cols - 1 : cols]
                index += 1
    ends_ref[0] = low_scr[...].astype(BF16)
    ends_ref[1] = high_scr[...].astype(BF16)


def pack_strips_kernel(ends_ref, other_ends_ref, chip_ref, core_ref, low_scr, high_scr):
    part = ends_ref.shape[1] // 2
    for side, scr in ((0, low_scr), (1, high_scr)):
        for group, ref in enumerate((ends_ref, other_ends_ref)):
            column = ref[side].astype(F32)
            for array in range(2):
                at = (2 * array + group) * part
                scr[at : at + part, :] = column[array * part : (array + 1) * part]
    even = is_even("lon")
    low, high = low_scr[...], high_scr[...]
    core_ref[...] = jnp.where(even, high, low).astype(BF16)
    chip_ref[...] = jnp.where(even, low, high).astype(BF16)


def rim_columns(chip_ref, core_ref):
    even = is_even("lon")
    chip, core = chip_ref[...].astype(F32), core_ref[...].astype(F32)
    return jnp.where(even, chip, core), jnp.where(even, core, chip)


def pack_rows_kernel(
    both_ref, other_ref, chip_ref, core_ref, after_ref, first_ref, second_ref, third_ref, edge_scr
):
    _, mem, rows, cols, _ = both_ref.shape
    slots = 4 * mem
    even = is_even("lat")
    west, east = rim_columns(chip_ref, core_ref)
    for slot in range(slots):
        array, member = divmod(slot, 2 * mem)
        ref, who = (both_ref, member) if member < mem else (other_ref, member - mem)
        start, stop = (ref[array, who, row].astype(F32) for row in (0, rows - 1))
        at = slice(slot * cols, (slot + 1) * cols)
        first_ref[at, :] = jnp.where(even, stop, start).astype(BF16)
        second_ref[at, :] = jnp.where(even, start, stop).astype(BF16)
        top, low = slot * rows, (slot + 1) * rows - 1
        for side, column in enumerate((west, east)):
            place = side * slots + slot
            start, stop = column[top : top + 1], column[low : low + 1]
            edge_scr[0, place : place + 1, :] = jnp.where(even, stop, start)
            edge_scr[1, place : place + 1, :] = jnp.where(even, start, stop)
    first_ref[slots * cols :, :] = edge_scr[0].astype(BF16)
    second_ref[slots * cols :, :] = edge_scr[1].astype(BF16)
    third_ref[...] = first_ref[...]


def dot_nn(a, b):
    return lax.dot_general(a, b, (((1,), (0,)), ((), ())), preferred_element_type=F32)


def same_head_matrix(channels):
    width = channels // HEAD_COUNT
    lane_row = lax.broadcasted_iota(jnp.int32, (channels, channels), 0) // width
    lane_col = lax.broadcasted_iota(jnp.int32, (channels, channels), 1) // width
    return jnp.where(lane_row == lane_col, 1.0, 0.0).astype(BF16)


def head_sums(values, same_head):
    high = values.astype(BF16)
    low = (values - high.astype(F32)).astype(BF16)
    return dot_nn(high, same_head) + dot_nn(low, same_head)


def rounded_sums(values, same_head):
    return dot_nn(values.astype(BF16), same_head)


def head_units(raw, same_head, sums=head_sums):
    raw = raw.astype(F32)
    mean_sq = sums(raw * raw, same_head) * (HEAD_COUNT / raw.shape[-1])
    inverse = lax.rsqrt(jnp.maximum(mean_sq, FLOOR))
    return raw, mean_sq, inverse, (raw * inverse).astype(BF16)


def row_rsqrt(values):
    return lax.rsqrt(jnp.mean(values * values, axis=-1, keepdims=True) + EPSILON)


def split_rows(array, count):
    size = array.shape[0] // count
    return [array[i * size : (i + 1) * size] for i in range(count)]


def softmax_members(queries, keys, same_head, scale):
    products = [query * key for query in queries for key in keys]
    scores = dot_nn(jnp.concatenate(products, axis=0), same_head) * scale
    exps = split_rows(jnp.exp(scores), len(products))
    soft = []
    for m in range(len(queries)):
        mine = exps[m * len(keys) : (m + 1) * len(keys)]
        total = mine[0]
        for e in mine[1:]:
            total = total + e
        inverse = 1.0 / total
        soft.append([e * inverse for e in mine])
    return soft


def mix_values(probs, values):
    mixed = None
    for prob, value in zip(probs, values):
        term = prob.astype(BF16).astype(F32) * value.astype(F32)
        mixed = term if mixed is None else mixed + term
    return mixed.astype(BF16)


def forward_cells(x, mem, groups, gain, project_ref, output_ref, same_head):
    channels = x.shape[-1]
    own_rows = x.shape[0] // groups * mem
    scale = 1.0 / math.sqrt(channels // HEAD_COUNT)
    normed = (x * row_rsqrt(x) * gain).astype(BF16)
    query_raw = dot_nn(normed[:own_rows], project_ref[:, :channels]).astype(BF16)
    key_raw = dot_nn(normed, project_ref[:, channels : 2 * channels]).astype(BF16)
    values = dot_nn(normed, project_ref[:, 2 * channels :]).astype(BF16)
    yield
    raw = jnp.concatenate([query_raw, key_raw], axis=0)
    units = head_units(raw, same_head, rounded_sums)[3]
    yield
    queries = split_rows(units[:own_rows], mem)
    keys = split_rows(units[own_rows:], groups)
    values = split_rows(values, groups)
    soft = softmax_members(queries, keys, same_head, scale)
    yield
    mixed = jnp.concatenate([mix_values(soft[m], values) for m in range(mem)], axis=0)
    return (x[:own_rows] + dot_nn(mixed, output_ref[...])).astype(BF16)


def together(*chains):
    results = [None] * len(chains)
    active = list(range(len(chains)))
    while active:
        for i in list(active):
            try:
                next(chains[i])
            except StopIteration as stop:
                results[i] = stop.value
                active.remove(i)
    return results


def run(chain):
    while True:
        try:
            next(chain)
        except StopIteration as stop:
            return stop.value


def shift_row(scr, member, place, slab, west, east):
    cols, channels = slab.shape
    column = lax.broadcasted_iota(jnp.int32, (cols, channels), 0)
    back = jnp.where(column == 0, west, pltpu.roll(slab, 1, 0))
    ahead = jnp.where(column == cols - 1, east, pltpu.roll(slab, cols - 1, 0))
    rows_at = slice(place * cols, (place + 1) * cols)
    scr[member, rows_at, :channels] = back.astype(BF16)
    scr[member, rows_at, channels : 2 * channels] = slab.astype(BF16)
    scr[member, rows_at, 2 * channels :] = ahead.astype(BF16)


def tap_rows(taps_ref, r):
    size = taps_ref.shape[0] // 3
    return taps_ref[r * size : (r + 1) * size, :]


def own_kernel(
    both_ref,
    other_ref,
    gain_ref,
    project_ref,
    output_ref,
    after_ref,
    proj_ref,
    unit_ref,
    soft_ref,
    inverse_ref,
    pull_ref,
    updated_ref,
):
    _, mem, rows, cols, channels = both_ref.shape
    groups = 2 * mem
    cells = rows * cols
    width = channels // HEAD_COUNT
    scale = 1.0 / math.sqrt(width)
    same_head = same_head_matrix(channels)
    own = both_ref[0].reshape(mem * cells, channels)
    other = other_ref[0].reshape(mem * cells, channels)
    x = jnp.concatenate([own, other], axis=0).astype(F32)
    normed = (x * row_rsqrt(x) * gain_ref[...]).astype(BF16)
    proj = dot_nn(normed, project_ref[...]).astype(BF16)
    proj_ref[...] = proj.reshape(groups, cells, 3 * channels)
    both_raw = jnp.concatenate([proj[:, :channels], proj[:, channels : 2 * channels]], axis=0)
    raw, mean_sq, inverse, units = head_units(both_raw, same_head)
    unit_ref[...] = units.reshape(2, groups, cells, channels)
    active = jnp.where(mean_sq > FLOOR, 1.0, jnp.where(mean_sq == FLOOR, 0.5, 0.0))
    pull = active * raw * (inverse * inverse * inverse) / width
    for kind in range(2):
        at = kind * groups * cells
        mine = slice(at, at + mem * cells)
        inverse_ref[kind] = inverse[mine].reshape(mem, cells, channels)
        pull_ref[kind] = pull[mine].reshape(mem, cells, channels)
    units = split_rows(units, 2 * groups)
    soft = softmax_members(units[:groups], units[groups:], same_head, scale)
    for m in range(groups):
        for n in range(groups):
            soft_ref[m * groups + n] = soft[m][n]
    values = split_rows(proj[:, 2 * channels :], groups)
    mixed = jnp.concatenate([mix_values(soft[m], values) for m in range(mem)], axis=0)
    updated = x[: mem * cells] + dot_nn(mixed, output_ref[...])
    updated_ref[...] = updated.astype(BF16).reshape(mem, cells, channels)


def backward_cells(
    pick, grad_field, x, gain, weights_t, proj_ref, unit_ref, soft_ref, inverse_ref, pull_ref
):
    project_t_ref, output_t_ref = weights_t
    groups = proj_ref.shape[0]
    mem = inverse_ref.shape[1]
    channels = x.shape[-1]
    scale = 1.0 / math.sqrt(channels // HEAD_COUNT)
    same_head = same_head_matrix(channels)
    grad_mixed = dot_nn(grad_field.astype(BF16), output_t_ref[...]).astype(BF16)
    grads = split_rows(grad_mixed, groups)
    yield
    values = [pick(proj_ref[n, :, 2 * channels :]) for n in range(groups)]
    products = [grads[m] * values[n] for m in range(groups) for n in range(groups)]
    dprobs = split_rows(dot_nn(jnp.concatenate(products, axis=0), same_head), len(products))
    yield
    units = [[pick(unit_ref[k, n]).astype(F32) for n in range(groups)] for k in range(2)]
    query_grad = [None] * mem
    key_grad = [None] * mem
    value_grad = [None] * mem
    for m in range(groups):
        soft = [pick(soft_ref[m * groups + n]) for n in range(groups)]
        dprob = dprobs[m * groups : (m + 1) * groups]
        mean = soft[0] * dprob[0]
        for n in range(1, groups):
            mean = mean + soft[n] * dprob[n]
        for n in range(groups):
            if m >= mem and n >= mem:
                continue
            dscore = soft[n] * (dprob[n] - mean)
            if m < mem:
                term = dscore * units[1][n]
                query_grad[m] = term if query_grad[m] is None else query_grad[m] + term
            if n < mem:
                term = dscore * units[0][m]
                key_grad[n] = term if key_grad[n] is None else key_grad[n] + term
                term = soft[n] * grads[m].astype(F32)
                value_grad[n] = term if value_grad[n] is None else value_grad[n] + term

    unit_grads = [jnp.concatenate(g, axis=0) * scale for g in (query_grad, key_grad)]

    def members(take):
        return jnp.concatenate([pick(take(m)) for m in range(mem)], axis=0)

    raws = []
    for kind in range(2):
        lanes = slice(kind * channels, (kind + 1) * channels)
        raws.append(members(lambda m: proj_ref[m, :, lanes]).astype(F32))
    inner = rounded_sums(
        jnp.concatenate([g * raw for g, raw in zip(unit_grads, raws)], axis=0), same_head
    )
    inner = split_rows(inner, 2)
    yield
    pulled = []
    for kind in range(2):
        inverse = members(lambda m: inverse_ref[kind, m])
        pull = members(lambda m: pull_ref[kind, m])
        pulled.append((inverse * unit_grads[kind] - pull * inner[kind]).astype(BF16))
    pulled.append(jnp.concatenate(value_grad, axis=0).astype(BF16))
    grad_normed = dot_nn(jnp.concatenate(pulled, axis=1), project_t_ref[...]) * gain
    yield
    inverse = row_rsqrt(x)
    inner = jnp.mean(x * grad_normed, axis=-1, keepdims=True)
    total = grad_field[: x.shape[0]] + inverse * grad_normed
    return (total - x * (inverse * inverse * inverse * inner)).astype(BF16)


def centre_kernel(
    both_ref,
    other_ref,
    chip_ref,
    core_ref,
    gain_ref,
    project_ref,
    output_ref,
    conv_ref,
    project_t_ref,
    output_t_ref,
    proj_ref,
    unit_ref,
    soft_ref,
    inverse_ref,
    pull_ref,
    updated_ref,
    conv_t_ref,
    result_ref,
    grad_ref,
    result_part_ref,
    grad_part_ref,
    shift_scr,
    cot_shift_scr,
    strip_scr,
):
    _, mem, rows, cols, channels = both_ref.shape
    groups = 2 * mem
    cells = rows * cols
    gain = gain_ref[...]
    same_head = same_head_matrix(channels)
    west, east = rim_columns(chip_ref, core_ref)
    for r in range(3):
        for c in range(3):
            tap = (3 * r + c) * channels
            turned = (3 * r + 2 - c) * channels
            conv_t_ref[turned : turned + channels, :] = conv_ref[tap : tap + channels, :].T

    def convolve(scr, count, start, taps_ref, turned):
        sums = [
            [start[(m * rows + a) * cols : (m * rows + a + 1) * cols] for a in range(rows)]
            for m in range(count)
        ]
        for r in range(3):
            step = 1 - r if turned else r - 1
            outs = [a for a in range(rows) if 0 <= a + step < rows]
            begin, end = outs[0] + step, outs[-1] + step + 1
            window = jnp.concatenate(
                [scr[m, begin * cols : end * cols, :] for m in range(count)], axis=0
            )
            terms = split_rows(dot_nn(window, tap_rows(taps_ref, r)), count * len(outs))
            for m in range(count):
                for i, a in enumerate(outs):
                    sums[m][a] = sums[m][a] + terms[m * len(outs) + i]
        return sums

    cots = []
    for member in range(groups):
        for row in range(rows):
            ref, who = (both_ref, member) if member < mem else (other_ref, member - mem)
            slab = ref[1, who, row].astype(F32)
            cots.append(slab)
            at = (groups + member) * rows + row
            shift_row(cot_shift_scr, member, row, slab, west[at : at + 1], east[at : at + 1])
    sums = convolve(cot_shift_scr, groups, jnp.concatenate(cots, axis=0), conv_t_ref, True)
    for member in range(groups):
        grad_part_ref[member, :cols, :] = sums[member][0]
        grad_part_ref[member, cols:, :] = sums[member][rows - 1]
    grad_field = jnp.concatenate([slab for s in sums for slab in s[1 : rows - 1]], axis=0)

    for member in range(groups):
        at = member * rows
        strip_scr[member] = jnp.zeros((16, channels), F32)
        strip_scr[member, :rows, :] = west[at : at + rows]
        strip_scr[member, 8 : 8 + rows, :] = east[at : at + rows]
    x = strip_scr[...].reshape(groups * 16, channels)
    forward = forward_cells(x, mem, groups, gain, project_ref, output_ref, same_head)
    x = both_ref[0, :, 1 : rows - 1].reshape(mem * (cells - 2 * cols), channels).astype(F32)
    backward = backward_cells(
        lambda array: array[cols : cells - cols],
        grad_field,
        x,
        gain,
        (project_t_ref, output_t_ref),
        proj_ref,
        unit_ref,
        soft_ref,
        inverse_ref,
        pull_ref,
    )
    fresh, total = run(forward), run(backward)
    fresh = split_rows(fresh.astype(F32), mem)
    grad_ref[...] = total.reshape(mem, rows - 2, cols, channels)

    for member in range(mem):
        for row in range(rows):
            slab = updated_ref[member, row * cols : (row + 1) * cols, :].astype(F32)
            ends = fresh[member][row : row + 1], fresh[member][8 + row : 9 + row]
            shift_row(shift_scr, member, row, slab, *ends)
    start = updated_ref[...].reshape(mem * cells, channels).astype(F32)
    sums = convolve(shift_scr, mem, start, conv_ref, False)
    for member in range(mem):
        result_part_ref[member, :cols, :] = sums[member][0]
        result_part_ref[member, cols:, :] = sums[member][rows - 1]
        for row in range(1, rows - 1):
            result_ref[member, row - 1] = sums[member][row].astype(BF16)


def main_kernel(
    both_ref,
    first_ref,
    second_ref,
    third_ref,
    gain_ref,
    project_ref,
    output_ref,
    conv_ref,
    project_t_ref,
    output_t_ref,
    conv_t_ref,
    proj_ref,
    unit_ref,
    soft_ref,
    inverse_ref,
    pull_ref,
    inner_result_ref,
    inner_grad_ref,
    result_part_ref,
    grad_part_ref,
    result_ref,
    grad_ref,
    shift_scr,
    cot_shift_scr,
    corner_scr,
    outer_scr,
    sems,
    *,
    lat_count,
):
    _, mem, rows, cols, channels = both_ref.shape
    copies = []
    for i, (ref, out_ref) in enumerate(
        ((inner_result_ref, result_ref), (inner_grad_ref, grad_ref))
    ):
        copy = pltpu.make_async_copy(ref, out_ref.at[:, pl.ds(1, rows - 2)], sems.at[i])
        copy.start()
        copies.append(copy)
    groups = 2 * mem
    slots = 2 * groups
    cells = rows * cols
    gain = gain_ref[...]
    same_head = same_head_matrix(channels)
    lat_even = is_even("lat")
    lat = lax.axis_index("lat")

    def halos(at):
        first, second = first_ref[at, :].astype(F32), second_ref[at, :].astype(F32)
        first = jnp.where(lax.rem(lat, 4) < 2, first, third_ref[at, :].astype(F32))
        north = jnp.where(lat == 0, 0.0, jnp.where(lat_even, second, first))
        south = jnp.where(lat == lat_count - 1, 0.0, jnp.where(lat_even, first, second))
        return north, south

    halo = [halos(slice(slot * cols, (slot + 1) * cols)) for slot in range(slots)]
    corners = halos(slice(slots * cols, slots * cols + 2 * slots))

    def corner(side, slot, end):
        at = end * slots + slot
        return corners[side][at : at + 1]

    def halo_part(scr, count, taps_ref, turned):
        north, south = (2, 0) if turned else (0, 2)
        parts = []
        for side, r in ((0, north), (1, south)):
            window = jnp.concatenate(
                [scr[m, side * cols : (side + 1) * cols, :] for m in range(count)], axis=0
            )
            parts.append(split_rows(dot_nn(window, tap_rows(taps_ref, r)), count))
        return jnp.concatenate([parts[side][m] for m in range(count) for side in (0, 1)], axis=0)

    for member in range(groups):
        slot = groups + member
        for side in (0, 1):
            ends = corner(side, slot, 0), corner(side, slot, 1)
            shift_row(cot_shift_scr, member, side, halo[slot][side], *ends)
    grad_field = grad_part_ref[...].reshape(groups * 2 * cols, channels)
    grad_field = grad_field + halo_part(cot_shift_scr, groups, conv_t_ref, True)

    blocks = []
    for member in range(groups):
        corner_scr[member] = jnp.zeros((16, channels), F32)
        for side in (0, 1):
            for end in (0, 1):
                at = 2 * side + end
                corner_scr[member, at : at + 1, :] = corner(side, member, end)
        blocks += [halo[member][0], halo[member][1], corner_scr[member]]
    x = jnp.concatenate(blocks, axis=0)
    forward = forward_cells(x, mem, groups, gain, project_ref, output_ref, same_head)
    x = [both_ref[0, m, row] for m in range(mem) for row in (0, rows - 1)]
    backward = backward_cells(
        lambda array: jnp.concatenate([array[:cols], array[cells - cols :]], axis=0),
        grad_field,
        jnp.concatenate(x, axis=0).astype(F32),
        gain,
        (project_t_ref, output_t_ref),
        proj_ref,
        unit_ref,
        soft_ref,
        inverse_ref,
        pull_ref,
    )

    def finish_result(chain):
        fresh = yield from chain
        fresh = split_rows(fresh.astype(F32), mem)
        for member in range(mem):
            for side in (0, 1):
                slab = fresh[member][side * cols : (side + 1) * cols]
                at = 2 * cols + 2 * side
                ends = fresh[member][at : at + 1], fresh[member][at + 1 : at + 2]
                shift_row(shift_scr, member, side, slab, *ends)
        yield
        outer = result_part_ref[...].reshape(mem * 2 * cols, channels)
        outer = (outer + halo_part(shift_scr, mem, conv_ref, False)).astype(BF16)
        store_outer(0, outer)

    def store_outer(which, outer):
        for i, slab in enumerate(split_rows(outer, 2 * mem)):
            outer_scr[which, i % 2, i // 2] = slab
        for side, row in ((0, 0), (1, rows - 1)):
            copy = pltpu.make_async_copy(
                outer_scr.at[which, side],
                (result_ref, grad_ref)[which].at[:, row],
                sems.at[2 + 2 * which + side],
            )
            copy.start()
            copies.append(copy)

    total, _ = together(backward, finish_result(forward))
    store_outer(1, total)
    for copy in copies:
        copy.wait()


def local_call(kernel, name, operands, out_shape, scratch, pinned=False, cost=None, copied=False):
    whole = pl.BlockSpec(memory_space=pltpu.VMEM)
    anywhere = pl.BlockSpec(memory_space=pl.ANY)
    specs = [anywhere if in_hbm else whole for _, in_hbm in operands]
    arrays = [
        pltpu.with_memory_space_constraint(array, pltpu.HBM) if in_hbm else array
        for array, in_hbm in operands
    ]

    def keep(shape):
        return pltpu.VMEM(shape.shape, shape.dtype) if pinned else shape

    return pl.pallas_call(
        kernel,
        out_shape=jax.tree.map(keep, out_shape),
        in_specs=specs,
        out_specs=jax.tree.map(lambda _: anywhere if copied else whole, out_shape),
        scratch_shapes=scratch,
        compiler_params=pltpu.CompilerParams(vmem_limit_bytes=VMEM_LIMIT),
        cost_estimate=cost,
        name=name,
    )(*arrays)


def here(*arrays):
    return [(array, False) for array in arrays]


def in_hbm(*arrays):
    return [(array, True) for array in arrays]


def per_device_paired(ensemble, norm_gain, project_weight, output_weight, conv_kernel, cotangent):
    mem, rows, cols, channels = ensemble.shape
    if rows < 3 or cols % 16 or (2 * mem * rows) % 16:
        return per_device_general(
            ensemble, norm_gain, project_weight, output_weight, conv_kernel, cotangent
        )
    groups = 2 * mem
    slots = 2 * groups
    cells = rows * cols
    lon_count = lax.axis_size("lon")
    lat_count = lax.axis_size("lat")
    bf16 = functools.partial(jax.ShapeDtypeStruct, dtype=BF16)
    f32 = functools.partial(jax.ShapeDtypeStruct, dtype=F32)
    swap = [(0, 1), (1, 0)]
    core_pairs = [(i, i ^ 1) for i in range(lon_count)]
    chip_pairs = [(i, (i - 1 if i % 2 == 0 else i + 1) % lon_count) for i in range(lon_count)]

    def lat_swap(*starts):
        pairs = []
        for lat in range(lat_count):
            for lon in range(lon_count):
                to = (lat, lon ^ 1)
                if lat % 4 in starts and lat + 1 < lat_count:
                    to = (lat + 1, lon)
                elif lat > 0 and (lat - 1) % 4 in starts:
                    to = (lat - 1, lon)
                pairs.append((lat * lon_count + lon, to[0] * lon_count + to[1]))
        return pairs

    ends_shape = (2, 2 * mem * rows, channels)
    both, ends = local_call(
        stack_kernel,
        "stack",
        in_hbm(ensemble, cotangent),
        (bf16((2,) + ensemble.shape), bf16(ends_shape)),
        [pltpu.VMEM(ends_shape[1:], F32)] * 2 + [pltpu.SemaphoreType.DMA((2,))],
        pinned=True,
    )
    other_ends = lax.ppermute(ends, "member", swap)
    other = lax.ppermute(both, "member", swap)

    strip = (slots * rows, channels)
    chip_send, core_send = local_call(
        pack_strips_kernel,
        "pack_strips",
        here(ends, other_ends),
        (bf16(strip), bf16(strip)),
        [pltpu.VMEM(strip, F32)] * 2,
    )
    chip = lax.ppermute(chip_send, "lon", chip_pairs)
    core = lax.ppermute(core_send, "lon", core_pairs)

    weights = (
        norm_gain.reshape(1, channels),
        project_weight,
        output_weight,
        conv_kernel.reshape(9 * channels, channels),
    )
    *weights, project_t, output_t = local_call(
        load_kernel,
        "load_weights",
        in_hbm(*weights),
        tuple(jax.ShapeDtypeStruct(w.shape, w.dtype) for w in weights)
        + (bf16((3 * channels, channels)), bf16((channels, channels))),
        [pltpu.SemaphoreType.DMA((4,))],
        pinned=True,
        cost=MIDDLING,
    )
    halo = bf16((slots * (cols + 2), channels))
    first_send, second_send, third_send = local_call(
        pack_rows_kernel,
        "pack_rows",
        here(both, other, chip, core, weights[0]),
        (halo, halo, halo),
        [pltpu.VMEM((2, 2 * slots, channels), F32)],
    )
    first = lax.ppermute(first_send, ("lat", "lon"), lat_swap(0))
    second = lax.ppermute(second_send, ("lat", "lon"), lat_swap(1, 3))
    third = lax.ppermute(third_send, ("lat", "lon"), lat_swap(2))

    *held, updated = local_call(
        own_kernel,
        "own_cells",
        here(both, other, *weights[:3], third_send),
        (
            bf16((groups, cells, 3 * channels)),
            bf16((2, groups, cells, channels)),
            f32((groups * groups, cells, channels)),
            f32((2, mem, cells, channels)),
            f32((2, mem, cells, channels)),
            bf16((mem, cells, channels)),
        ),
        [],
        pinned=True,
        cost=LONG,
    )
    conv_t, *parts = local_call(
        centre_kernel,
        "centre",
        here(both, other, chip, core, *weights, project_t, output_t, *held, updated),
        (
            bf16((9 * channels, channels)),
            bf16((mem, rows - 2, cols, channels)),
            bf16((mem, rows - 2, cols, channels)),
            f32((mem, 2 * cols, channels)),
            f32((groups, 2 * cols, channels)),
        ),
        [
            pltpu.VMEM((mem, cells, 3 * channels), BF16),
            pltpu.VMEM((groups, cells, 3 * channels), BF16),
            pltpu.VMEM((groups, 16, channels), F32),
        ],
        pinned=True,
        cost=LONG,
    )
    return local_call(
        functools.partial(main_kernel, lat_count=lat_count),
        "main",
        here(both, first, second, third, *weights, project_t, output_t, conv_t, *held, *parts),
        (bf16(ensemble.shape), bf16(ensemble.shape)),
        [
            pltpu.VMEM((mem, 2 * cols, 3 * channels), BF16),
            pltpu.VMEM((groups, 2 * cols, 3 * channels), BF16),
            pltpu.VMEM((groups, 16, channels), F32),
            pltpu.VMEM((2, 2, mem, cols, channels), BF16),
            pltpu.SemaphoreType.DMA((6,)),
        ],
        copied=True,
    )


def solution(mesh):
    paired = mesh.shape["member"] == 2 and mesh.shape["lon"] % 2 == 0
    per_device = per_device_paired if paired else per_device_general
    in_specs = (
        P("member", "lat", "lon", None),
        P(),
        P(),
        P(),
        P(),
        P("member", "lat", "lon", None),
    )
    out_specs = (P("member", "lat", "lon", None), P("member", "lat", "lon", None))
    return jax.shard_map(
        per_device, mesh=mesh, in_specs=in_specs, out_specs=out_specs, check_vma=False
    )
```

```python
import functools
import math

import jax
import jax.numpy as jnp
from jax import lax
from jax.experimental import pallas as pl
from jax.experimental.pallas import tpu as pltpu
from jax.sharding import PartitionSpec as P

HEAD_COUNT = 8


FLOOR = 0.5
EPSILON = 1e-06


def padded_2(block, sides, width, periodic):
    for axis, dim in sides:
        count = lax.axis_size(axis)
        forward = [(i, i + 1) for i in range(count - 1)]
        if periodic:
            forward.append((count - 1, 0))
        backward = [(target, source) for source, target in forward]
        low = lax.ppermute(
            lax.slice_in_dim(block, block.shape[dim] - width, None, axis=dim), axis, forward
        )
        high = lax.ppermute(lax.slice_in_dim(block, 0, width, axis=dim), axis, backward)
        block = jnp.concatenate([low, block, high], axis=dim)
    return block


def row_norm(values, gain_vec):
    mean_sq = jnp.mean(values * values, axis=-1, keepdims=True)
    return values * lax.rsqrt(mean_sq + EPSILON) * gain_vec


def head_norm(values, head_count):
    shaped = values.reshape(values.shape[:-1] + (head_count, values.shape[-1] // head_count))
    mean_sq = jnp.mean(shaped * shaped, axis=-1, keepdims=True)
    return (shaped * lax.rsqrt(jnp.maximum(mean_sq, FLOOR))).reshape(values.shape)


def split_heads(values, head_count):
    return values.reshape(values.shape[:-1] + (head_count, values.shape[-1] // head_count))


def head_pullback(raw_rows, grad_rows):
    _, pullback = jax.vjp(lambda t: head_norm(t, HEAD_COUNT), raw_rows.astype(jnp.float32))
    return pullback(grad_rows)[0]


def pad_field(field_in):
    widened = padded_2(field_in, (("lon", 2),), 1, True)
    return padded_2(widened, (("lat", 1),), 1, False)


def conv_taps(padded, kernel, lat_n, lon_n, adjoint):
    running = None
    for row_off in range(3):
        for col_off in range(3):
            if adjoint:
                window = padded[
                    :, 2 - row_off : 2 - row_off + lat_n, 2 - col_off : 2 - col_off + lon_n
                ]
                summand = jnp.einsum(
                    "mabc,dc->mabd",
                    window,
                    kernel[row_off, col_off],
                    preferred_element_type=jnp.float32,
                )
            else:
                window = padded[:, row_off : row_off + lat_n, col_off : col_off + lon_n]
                summand = jnp.einsum(
                    "mabc,cd->mabd",
                    window,
                    kernel[row_off, col_off],
                    preferred_element_type=jnp.float32,
                )
            running = summand if running is None else running + summand
    return running


def per_device_general(ensemble, norm_gain, project_weight, output_weight, conv_kernel, cotangent):
    mem_dev, lat_dev, lon_dev, channels = ensemble.shape
    cell_count = lat_dev * lon_dev
    score_scale = 1.0 / math.sqrt(channels // HEAD_COUNT)
    inputs = ensemble.reshape(mem_dev, cell_count, channels).astype(jnp.float32)
    normed = row_norm(inputs, norm_gain).astype(jnp.bfloat16)
    spread = lax.all_to_all(normed, "member", split_axis=1, concat_axis=0, tiled=True)
    projected = jnp.dot(spread, project_weight, preferred_element_type=jnp.float32).astype(
        jnp.bfloat16
    )
    query_raw = projected[..., :channels]
    key_raw = projected[..., channels : 2 * channels]
    value_rows = projected[..., 2 * channels :]
    key_rows = head_norm(key_raw.astype(jnp.float32), HEAD_COUNT).astype(jnp.bfloat16)
    queries = head_norm(query_raw.astype(jnp.float32), HEAD_COUNT).astype(jnp.bfloat16)
    query_heads = split_heads(queries, HEAD_COUNT)
    key_heads = split_heads(key_rows, HEAD_COUNT)
    value_heads = split_heads(value_rows, HEAD_COUNT)
    scores = (
        jnp.einsum("mphd,nphd->mnhp", query_heads, key_heads, preferred_element_type=jnp.float32)
        * score_scale
    )
    expd = jnp.exp(scores)
    soft = expd / jnp.sum(expd, axis=1, keepdims=True)
    rounded = soft.astype(jnp.bfloat16)
    mixed_out = jnp.einsum(
        "mnhp,nphd->mphd", rounded, value_heads, preferred_element_type=jnp.float32
    )
    mixed_out = mixed_out.reshape(query_raw.shape).astype(jnp.bfloat16)
    mixed_out = lax.all_to_all(mixed_out, "member", split_axis=0, concat_axis=1, tiled=True)
    updated = (
        inputs + jnp.dot(mixed_out, output_weight, preferred_element_type=jnp.float32)
    ).astype(jnp.bfloat16)
    field_up = updated.reshape(mem_dev, lat_dev, lon_dev, channels)
    result = field_up.astype(jnp.float32) + conv_taps(
        pad_field(field_up), conv_kernel, lat_dev, lon_dev, False
    )
    result = result.astype(jnp.bfloat16)
    grad_field = cotangent.astype(jnp.float32) + conv_taps(
        pad_field(cotangent), conv_kernel, lat_dev, lon_dev, True
    )
    grad_rows = grad_field.reshape(mem_dev, cell_count, channels)
    grad_mixed = jnp.einsum(
        "mpc,dc->mpd",
        grad_rows.astype(jnp.bfloat16),
        output_weight,
        preferred_element_type=jnp.float32,
    )
    grad_mixed = grad_mixed.astype(jnp.bfloat16)
    grad_mixed = lax.all_to_all(grad_mixed, "member", split_axis=1, concat_axis=0, tiled=True)
    grad_heads = split_heads(grad_mixed, HEAD_COUNT)
    dprob = jnp.einsum(
        "mphd,nphd->mnhp", grad_heads, value_heads, preferred_element_type=jnp.float32
    )
    dscore = (soft * (dprob - jnp.sum(soft * dprob, axis=1, keepdims=True))).astype(jnp.bfloat16)
    query_grad = (
        jnp.einsum("mnhp,nphd->mphd", dscore, key_heads, preferred_element_type=jnp.float32)
        * score_scale
    )
    query_grad = query_grad.reshape(query_raw.shape)
    key_grad = (
        jnp.einsum("mnhp,mphd->nphd", dscore, query_heads, preferred_element_type=jnp.float32)
        * score_scale
    )
    key_grad = key_grad.reshape(key_raw.shape)
    value_grad = jnp.einsum(
        "mnhp,mphd->nphd", rounded, grad_heads, preferred_element_type=jnp.float32
    )
    value_grad = value_grad.reshape(key_raw.shape)
    grad_query_raw = head_pullback(query_raw, query_grad)
    grad_key_raw = head_pullback(key_raw, key_grad)
    grad_proj = jnp.concatenate([grad_query_raw, grad_key_raw, value_grad], axis=-1).astype(
        jnp.bfloat16
    )
    grad_proj = lax.all_to_all(grad_proj, "member", split_axis=0, concat_axis=1, tiled=True)
    grad_normed = jnp.einsum(
        "mpe,ce->mpc", grad_proj, project_weight, preferred_element_type=jnp.float32
    )
    _, pull_norm = jax.vjp(lambda t: row_norm(t, norm_gain), inputs)
    grad_inputs = pull_norm(grad_normed)[0]
    grad_ensemble = (
        (grad_rows + grad_inputs).astype(jnp.bfloat16).reshape(mem_dev, lat_dev, lon_dev, channels)
    )
    return (result, grad_ensemble)


F32 = jnp.float32
BF16 = jnp.bfloat16
VMEM_LIMIT = 24 * 1024 * 1024
LONG = pl.CostEstimate(flops=20_000_000_000, bytes_accessed=4_000_000, transcendentals=0)
MIDDLING = pl.CostEstimate(flops=3_000_000_000, bytes_accessed=2_000_000, transcendentals=0)


def is_even(axis):
    return lax.rem(lax.axis_index(axis), 2) == 0


def load_kernel(
    gain_hbm,
    project_hbm,
    output_hbm,
    conv_hbm,
    gain_ref,
    project_ref,
    output_ref,
    conv_ref,
    project_t_ref,
    output_t_ref,
    sems,
):
    channels = output_ref.shape[0]
    pairs = (
        (gain_hbm, gain_ref),
        (project_hbm, project_ref),
        (output_hbm, output_ref),
        (conv_hbm, conv_ref),
    )
    loads = [
        pltpu.make_async_copy(source, target, sems.at[i])
        for i, (source, target) in enumerate(pairs)
    ]
    for load in loads:
        load.start()
    for load in loads[:3]:
        load.wait()
    output_t_ref[...] = output_ref[...].T
    for kind in range(3):
        lanes = slice(kind * channels, (kind + 1) * channels)
        project_t_ref[lanes, :] = project_ref[:, lanes].T
    loads[3].wait()


def stack_kernel(ens_ref, cot_ref, both_ref, ends_ref, low_scr, high_scr, sems):
    _, mem, rows, cols, _ = both_ref.shape
    copies = [
        pltpu.make_async_copy(ref, both_ref.at[i], sems.at[i])
        for i, ref in enumerate((ens_ref, cot_ref))
    ]
    for copy in copies:
        copy.start()
    for copy in copies:
        copy.wait()
    index = 0
    for array in range(2):
        for member in range(mem):
            for row in range(rows):
                slab = both_ref[array, member, row].astype(F32)
                low_scr[index : index + 1, :] = slab[0:1]
                high_scr[index : index + 1, :] = slab[cols - 1 : cols]
                index += 1
    ends_ref[0] = low_scr[...].astype(BF16)
    ends_ref[1] = high_scr[...].astype(BF16)


def pack_strips_kernel(ends_ref, other_ends_ref, chip_ref, core_ref, low_scr, high_scr):
    part = ends_ref.shape[1] // 2
    for side, scr in ((0, low_scr), (1, high_scr)):
        for group, ref in enumerate((ends_ref, other_ends_ref)):
            column = ref[side].astype(F32)
            for array in range(2):
                at = (2 * array + group) * part
                scr[at : at + part, :] = column[array * part : (array + 1) * part]
    even = is_even("lon")
    low, high = low_scr[...], high_scr[...]
    core_ref[...] = jnp.where(even, high, low).astype(BF16)
    chip_ref[...] = jnp.where(even, low, high).astype(BF16)


def rim_columns(chip_ref, core_ref):
    even = is_even("lon")
    chip, core = chip_ref[...].astype(F32), core_ref[...].astype(F32)
    return jnp.where(even, chip, core), jnp.where(even, core, chip)


def pack_rows_kernel(
    both_ref, other_ref, chip_ref, core_ref, after_ref, first_ref, second_ref, edge_scr
):
    _, mem, rows, cols, _ = both_ref.shape
    slots = 4 * mem
    even = is_even("lat")
    west, east = rim_columns(chip_ref, core_ref)
    for slot in range(slots):
        array, member = divmod(slot, 2 * mem)
        ref, who = (both_ref, member) if member < mem else (other_ref, member - mem)
        start, stop = (ref[array, who, row].astype(F32) for row in (0, rows - 1))
        at = slice(slot * cols, (slot + 1) * cols)
        first_ref[at, :] = jnp.where(even, stop, start).astype(BF16)
        second_ref[at, :] = jnp.where(even, start, stop).astype(BF16)
        top, low = slot * rows, (slot + 1) * rows - 1
        for side, column in enumerate((west, east)):
            place = side * slots + slot
            start, stop = column[top : top + 1], column[low : low + 1]
            edge_scr[0, place : place + 1, :] = jnp.where(even, stop, start)
            edge_scr[1, place : place + 1, :] = jnp.where(even, start, stop)
    first_ref[slots * cols :, :] = edge_scr[0].astype(BF16)
    second_ref[slots * cols :, :] = edge_scr[1].astype(BF16)


def dot_nn(a, b):
    return lax.dot_general(a, b, (((1,), (0,)), ((), ())), preferred_element_type=F32)


def same_head_matrix(channels):
    width = channels // HEAD_COUNT
    lane_row = lax.broadcasted_iota(jnp.int32, (channels, channels), 0) // width
    lane_col = lax.broadcasted_iota(jnp.int32, (channels, channels), 1) // width
    return jnp.where(lane_row == lane_col, 1.0, 0.0).astype(BF16)


def head_sums(values, same_head):
    high = values.astype(BF16)
    low = (values - high.astype(F32)).astype(BF16)
    return dot_nn(high, same_head) + dot_nn(low, same_head)


def rounded_sums(values, same_head):
    return dot_nn(values.astype(BF16), same_head)


def head_units(raw, same_head, sums=head_sums):
    raw = raw.astype(F32)
    mean_sq = sums(raw * raw, same_head) * (HEAD_COUNT / raw.shape[-1])
    inverse = lax.rsqrt(jnp.maximum(mean_sq, FLOOR))
    return raw, mean_sq, inverse, (raw * inverse).astype(BF16)


def row_rsqrt(values):
    return lax.rsqrt(jnp.mean(values * values, axis=-1, keepdims=True) + EPSILON)


def split_rows(array, count):
    size = array.shape[0] // count
    return [array[i * size : (i + 1) * size] for i in range(count)]


def softmax_members(queries, keys, same_head, scale):
    products = [query * key for query in queries for key in keys]
    scores = dot_nn(jnp.concatenate(products, axis=0), same_head) * scale
    exps = split_rows(jnp.exp(scores), len(products))
    soft = []
    for m in range(len(queries)):
        mine = exps[m * len(keys) : (m + 1) * len(keys)]
        total = mine[0]
        for e in mine[1:]:
            total = total + e
        inverse = 1.0 / total
        soft.append([e * inverse for e in mine])
    return soft


def mix_values(probs, values):
    mixed = None
    for prob, value in zip(probs, values):
        term = prob.astype(BF16).astype(F32) * value.astype(F32)
        mixed = term if mixed is None else mixed + term
    return mixed.astype(BF16)


def forward_cells(x, mem, groups, gain, project_ref, output_ref, same_head):
    channels = x.shape[-1]
    own_rows = x.shape[0] // groups * mem
    scale = 1.0 / math.sqrt(channels // HEAD_COUNT)
    normed = (x * row_rsqrt(x) * gain).astype(BF16)
    query_raw = dot_nn(normed[:own_rows], project_ref[:, :channels]).astype(BF16)
    key_raw = dot_nn(normed, project_ref[:, channels : 2 * channels]).astype(BF16)
    values = dot_nn(normed, project_ref[:, 2 * channels :]).astype(BF16)
    yield
    raw = jnp.concatenate([query_raw, key_raw], axis=0)
    units = head_units(raw, same_head, rounded_sums)[3]
    yield
    queries = split_rows(units[:own_rows], mem)
    keys = split_rows(units[own_rows:], groups)
    values = split_rows(values, groups)
    soft = softmax_members(queries, keys, same_head, scale)
    yield
    mixed = jnp.concatenate([mix_values(soft[m], values) for m in range(mem)], axis=0)
    return (x[:own_rows] + dot_nn(mixed, output_ref[...])).astype(BF16)


def together(*chains):
    results = [None] * len(chains)
    active = list(range(len(chains)))
    while active:
        for i in list(active):
            try:
                next(chains[i])
            except StopIteration as stop:
                results[i] = stop.value
                active.remove(i)
    return results


def run(chain):
    while True:
        try:
            next(chain)
        except StopIteration as stop:
            return stop.value


def shift_row(scr, member, place, slab, west, east):
    cols, channels = slab.shape
    column = lax.broadcasted_iota(jnp.int32, (cols, channels), 0)
    back = jnp.where(column == 0, west, pltpu.roll(slab, 1, 0))
    ahead = jnp.where(column == cols - 1, east, pltpu.roll(slab, cols - 1, 0))
    rows_at = slice(place * cols, (place + 1) * cols)
    scr[member, rows_at, :channels] = back.astype(BF16)
    scr[member, rows_at, channels : 2 * channels] = slab.astype(BF16)
    scr[member, rows_at, 2 * channels :] = ahead.astype(BF16)


def tap_rows(taps_ref, r):
    size = taps_ref.shape[0] // 3
    return taps_ref[r * size : (r + 1) * size, :]


def own_kernel(
    both_ref,
    other_ref,
    gain_ref,
    project_ref,
    output_ref,
    after_ref,
    proj_ref,
    unit_ref,
    soft_ref,
    inverse_ref,
    pull_ref,
    updated_ref,
):
    _, mem, rows, cols, channels = both_ref.shape
    groups = 2 * mem
    cells = rows * cols
    width = channels // HEAD_COUNT
    scale = 1.0 / math.sqrt(width)
    same_head = same_head_matrix(channels)
    own = both_ref[0].reshape(mem * cells, channels)
    other = other_ref[0].reshape(mem * cells, channels)
    x = jnp.concatenate([own, other], axis=0).astype(F32)
    normed = (x * row_rsqrt(x) * gain_ref[...]).astype(BF16)
    proj = dot_nn(normed, project_ref[...]).astype(BF16)
    proj_ref[...] = proj.reshape(groups, cells, 3 * channels)
    both_raw = jnp.concatenate([proj[:, :channels], proj[:, channels : 2 * channels]], axis=0)
    raw, mean_sq, inverse, units = head_units(both_raw, same_head)
    unit_ref[...] = units.reshape(2, groups, cells, channels)
    active = jnp.where(mean_sq > FLOOR, 1.0, jnp.where(mean_sq == FLOOR, 0.5, 0.0))
    pull = active * raw * (inverse * inverse * inverse) / width
    for kind in range(2):
        at = kind * groups * cells
        mine = slice(at, at + mem * cells)
        inverse_ref[kind] = inverse[mine].reshape(mem, cells, channels)
        pull_ref[kind] = pull[mine].reshape(mem, cells, channels)
    units = split_rows(units, 2 * groups)
    soft = softmax_members(units[:groups], units[groups:], same_head, scale)
    for m in range(groups):
        for n in range(groups):
            soft_ref[m * groups + n] = soft[m][n]
    values = split_rows(proj[:, 2 * channels :], groups)
    mixed = jnp.concatenate([mix_values(soft[m], values) for m in range(mem)], axis=0)
    updated = x[: mem * cells] + dot_nn(mixed, output_ref[...])
    updated_ref[...] = updated.astype(BF16).reshape(mem, cells, channels)


def backward_cells(
    pick, grad_field, x, gain, weights_t, proj_ref, unit_ref, soft_ref, inverse_ref, pull_ref
):
    project_t_ref, output_t_ref = weights_t
    groups = proj_ref.shape[0]
    mem = inverse_ref.shape[1]
    channels = x.shape[-1]
    scale = 1.0 / math.sqrt(channels // HEAD_COUNT)
    same_head = same_head_matrix(channels)
    grad_mixed = dot_nn(grad_field.astype(BF16), output_t_ref[...]).astype(BF16)
    grads = split_rows(grad_mixed, groups)
    yield
    values = [pick(proj_ref[n, :, 2 * channels :]) for n in range(groups)]
    products = [grads[m] * values[n] for m in range(groups) for n in range(groups)]
    dprobs = split_rows(dot_nn(jnp.concatenate(products, axis=0), same_head), len(products))
    yield
    units = [[pick(unit_ref[k, n]).astype(F32) for n in range(groups)] for k in range(2)]
    query_grad = [None] * mem
    key_grad = [None] * mem
    value_grad = [None] * mem
    for m in range(groups):
        soft = [pick(soft_ref[m * groups + n]) for n in range(groups)]
        dprob = dprobs[m * groups : (m + 1) * groups]
        mean = soft[0] * dprob[0]
        for n in range(1, groups):
            mean = mean + soft[n] * dprob[n]
        for n in range(groups):
            if m >= mem and n >= mem:
                continue
            dscore = soft[n] * (dprob[n] - mean)
            if m < mem:
                term = dscore * units[1][n]
                query_grad[m] = term if query_grad[m] is None else query_grad[m] + term
            if n < mem:
                term = dscore * units[0][m]
                key_grad[n] = term if key_grad[n] is None else key_grad[n] + term
                term = soft[n] * grads[m].astype(F32)
                value_grad[n] = term if value_grad[n] is None else value_grad[n] + term

    unit_grads = [jnp.concatenate(g, axis=0) * scale for g in (query_grad, key_grad)]

    def members(take):
        return jnp.concatenate([pick(take(m)) for m in range(mem)], axis=0)

    raws = []
    for kind in range(2):
        lanes = slice(kind * channels, (kind + 1) * channels)
        raws.append(members(lambda m: proj_ref[m, :, lanes]).astype(F32))
    inner = rounded_sums(
        jnp.concatenate([g * raw for g, raw in zip(unit_grads, raws)], axis=0), same_head
    )
    inner = split_rows(inner, 2)
    yield
    pulled = []
    for kind in range(2):
        inverse = members(lambda m: inverse_ref[kind, m])
        pull = members(lambda m: pull_ref[kind, m])
        pulled.append((inverse * unit_grads[kind] - pull * inner[kind]).astype(BF16))
    pulled.append(jnp.concatenate(value_grad, axis=0).astype(BF16))
    grad_normed = dot_nn(jnp.concatenate(pulled, axis=1), project_t_ref[...]) * gain
    yield
    inverse = row_rsqrt(x)
    inner = jnp.mean(x * grad_normed, axis=-1, keepdims=True)
    total = grad_field[: x.shape[0]] + inverse * grad_normed
    return (total - x * (inverse * inverse * inverse * inner)).astype(BF16)


def centre_kernel(
    both_ref,
    other_ref,
    chip_ref,
    core_ref,
    gain_ref,
    project_ref,
    output_ref,
    conv_ref,
    project_t_ref,
    output_t_ref,
    proj_ref,
    unit_ref,
    soft_ref,
    inverse_ref,
    pull_ref,
    updated_ref,
    conv_t_ref,
    result_ref,
    grad_ref,
    result_part_ref,
    grad_part_ref,
    shift_scr,
    cot_shift_scr,
    strip_scr,
):
    _, mem, rows, cols, channels = both_ref.shape
    groups = 2 * mem
    cells = rows * cols
    gain = gain_ref[...]
    same_head = same_head_matrix(channels)
    west, east = rim_columns(chip_ref, core_ref)
    for r in range(3):
        for c in range(3):
            tap = (3 * r + c) * channels
            turned = (3 * r + 2 - c) * channels
            conv_t_ref[turned : turned + channels, :] = conv_ref[tap : tap + channels, :].T

    def convolve(scr, count, start, taps_ref, turned):
        sums = [
            [start[(m * rows + a) * cols : (m * rows + a + 1) * cols] for a in range(rows)]
            for m in range(count)
        ]
        for r in range(3):
            step = 1 - r if turned else r - 1
            outs = [a for a in range(rows) if 0 <= a + step < rows]
            begin, end = outs[0] + step, outs[-1] + step + 1
            window = jnp.concatenate(
                [scr[m, begin * cols : end * cols, :] for m in range(count)], axis=0
            )
            terms = split_rows(dot_nn(window, tap_rows(taps_ref, r)), count * len(outs))
            for m in range(count):
                for i, a in enumerate(outs):
                    sums[m][a] = sums[m][a] + terms[m * len(outs) + i]
        return sums

    for member in range(groups):
        at = member * rows
        strip_scr[member] = jnp.zeros((16, channels), F32)
        strip_scr[member, :rows, :] = west[at : at + rows]
        strip_scr[member, 8 : 8 + rows, :] = east[at : at + rows]
    x = strip_scr[...].reshape(groups * 16, channels)
    forward = forward_cells(x, mem, groups, gain, project_ref, output_ref, same_head)
    fresh = split_rows(run(forward).astype(F32), mem)

    cots = []
    for member in range(groups):
        for row in range(rows):
            ref, who = (both_ref, member) if member < mem else (other_ref, member - mem)
            slab = ref[1, who, row].astype(F32)
            cots.append(slab)
            at = (groups + member) * rows + row
            shift_row(cot_shift_scr, member, row, slab, west[at : at + 1], east[at : at + 1])
    sums = convolve(cot_shift_scr, groups, jnp.concatenate(cots, axis=0), conv_t_ref, True)
    for member in range(groups):
        grad_part_ref[member, :cols, :] = sums[member][0]
        grad_part_ref[member, cols:, :] = sums[member][rows - 1]
    grad_field = jnp.concatenate([slab for s in sums for slab in s[1 : rows - 1]], axis=0)

    x = both_ref[0, :, 1 : rows - 1].reshape(mem * (cells - 2 * cols), channels).astype(F32)
    backward = backward_cells(
        lambda array: array[cols : cells - cols],
        grad_field,
        x,
        gain,
        (project_t_ref, output_t_ref),
        proj_ref,
        unit_ref,
        soft_ref,
        inverse_ref,
        pull_ref,
    )
    total = run(backward)
    grad_ref[...] = total.reshape(mem, rows - 2, cols, channels)

    for member in range(mem):
        for row in range(rows):
            slab = updated_ref[member, row * cols : (row + 1) * cols, :].astype(F32)
            ends = fresh[member][row : row + 1], fresh[member][8 + row : 9 + row]
            shift_row(shift_scr, member, row, slab, *ends)
    start = updated_ref[...].reshape(mem * cells, channels).astype(F32)
    sums = convolve(shift_scr, mem, start, conv_ref, False)
    for member in range(mem):
        result_part_ref[member, :cols, :] = sums[member][0]
        result_part_ref[member, cols:, :] = sums[member][rows - 1]
        for row in range(1, rows - 1):
            result_ref[member, row - 1] = sums[member][row].astype(BF16)


def main_kernel(
    both_ref,
    second_ref,
    first_ref,
    gain_ref,
    project_ref,
    output_ref,
    conv_ref,
    project_t_ref,
    output_t_ref,
    conv_t_ref,
    proj_ref,
    unit_ref,
    soft_ref,
    inverse_ref,
    pull_ref,
    inner_result_ref,
    inner_grad_ref,
    result_part_ref,
    grad_part_ref,
    result_ref,
    grad_ref,
    shift_scr,
    cot_shift_scr,
    corner_scr,
    outer_scr,
    sems,
    *,
    lat_count,
):
    _, mem, rows, cols, channels = both_ref.shape
    copies = []
    for i, (ref, out_ref) in enumerate(
        ((inner_result_ref, result_ref), (inner_grad_ref, grad_ref))
    ):
        copy = pltpu.make_async_copy(ref, out_ref.at[:, pl.ds(1, rows - 2)], sems.at[i])
        copy.start()
        copies.append(copy)
    groups = 2 * mem
    slots = 2 * groups
    cells = rows * cols
    gain = gain_ref[...]
    same_head = same_head_matrix(channels)
    lat_even = is_even("lat")
    lat = lax.axis_index("lat")

    def halos(at):
        first, second = first_ref[at, :].astype(F32), second_ref[at, :].astype(F32)
        north = jnp.where(lat == 0, 0.0, jnp.where(lat_even, second, first))
        south = jnp.where(lat == lat_count - 1, 0.0, jnp.where(lat_even, first, second))
        return north, south

    halo = [halos(slice(slot * cols, (slot + 1) * cols)) for slot in range(slots)]
    corners = halos(slice(slots * cols, slots * cols + 2 * slots))

    def corner(side, slot, end):
        at = end * slots + slot
        return corners[side][at : at + 1]

    def halo_part(scr, count, taps_ref, turned):
        north, south = (2, 0) if turned else (0, 2)
        parts = []
        for side, r in ((0, north), (1, south)):
            window = jnp.concatenate(
                [scr[m, side * cols : (side + 1) * cols, :] for m in range(count)], axis=0
            )
            parts.append(split_rows(dot_nn(window, tap_rows(taps_ref, r)), count))
        return jnp.concatenate([parts[side][m] for m in range(count) for side in (0, 1)], axis=0)

    for member in range(groups):
        slot = groups + member
        for side in (0, 1):
            ends = corner(side, slot, 0), corner(side, slot, 1)
            shift_row(cot_shift_scr, member, side, halo[slot][side], *ends)
    grad_field = grad_part_ref[...].reshape(groups * 2 * cols, channels)
    grad_field = grad_field + halo_part(cot_shift_scr, groups, conv_t_ref, True)

    blocks = []
    for member in range(groups):
        corner_scr[member] = jnp.zeros((16, channels), F32)
        for side in (0, 1):
            for end in (0, 1):
                at = 2 * side + end
                corner_scr[member, at : at + 1, :] = corner(side, member, end)
        blocks += [halo[member][0], halo[member][1], corner_scr[member]]
    x = jnp.concatenate(blocks, axis=0)
    forward = forward_cells(x, mem, groups, gain, project_ref, output_ref, same_head)
    x = [both_ref[0, m, row] for m in range(mem) for row in (0, rows - 1)]
    backward = backward_cells(
        lambda array: jnp.concatenate([array[:cols], array[cells - cols :]], axis=0),
        grad_field,
        jnp.concatenate(x, axis=0).astype(F32),
        gain,
        (project_t_ref, output_t_ref),
        proj_ref,
        unit_ref,
        soft_ref,
        inverse_ref,
        pull_ref,
    )

    def finish_result(chain):
        fresh = yield from chain
        fresh = split_rows(fresh.astype(F32), mem)
        for member in range(mem):
            for side in (0, 1):
                slab = fresh[member][side * cols : (side + 1) * cols]
                at = 2 * cols + 2 * side
                ends = fresh[member][at : at + 1], fresh[member][at + 1 : at + 2]
                shift_row(shift_scr, member, side, slab, *ends)
        yield
        outer = result_part_ref[...].reshape(mem * 2 * cols, channels)
        outer = (outer + halo_part(shift_scr, mem, conv_ref, False)).astype(BF16)
        store_outer(0, outer)

    def store_outer(which, outer):
        for i, slab in enumerate(split_rows(outer, 2 * mem)):
            outer_scr[which, i % 2, i // 2] = slab
        for side, row in ((0, 0), (1, rows - 1)):
            copy = pltpu.make_async_copy(
                outer_scr.at[which, side],
                (result_ref, grad_ref)[which].at[:, row],
                sems.at[2 + 2 * which + side],
            )
            copy.start()
            copies.append(copy)

    def finish_grad(chain):
        total = yield from chain
        store_outer(1, total)

    grad_chain = finish_grad(backward)
    next(grad_chain)
    together(grad_chain, finish_result(forward))
    for copy in copies:
        copy.wait()


def local_call(kernel, name, operands, out_shape, scratch, pinned=False, cost=None, copied=False):
    whole = pl.BlockSpec(memory_space=pltpu.VMEM)
    anywhere = pl.BlockSpec(memory_space=pl.ANY)
    specs = [anywhere if in_hbm else whole for _, in_hbm in operands]
    arrays = [
        pltpu.with_memory_space_constraint(array, pltpu.HBM) if in_hbm else array
        for array, in_hbm in operands
    ]

    def keep(shape):
        return pltpu.VMEM(shape.shape, shape.dtype) if pinned else shape

    return pl.pallas_call(
        kernel,
        out_shape=jax.tree.map(keep, out_shape),
        in_specs=specs,
        out_specs=jax.tree.map(lambda _: anywhere if copied else whole, out_shape),
        scratch_shapes=scratch,
        compiler_params=pltpu.CompilerParams(vmem_limit_bytes=VMEM_LIMIT),
        cost_estimate=cost,
        name=name,
    )(*arrays)


def here(*arrays):
    return [(array, False) for array in arrays]


def in_hbm(*arrays):
    return [(array, True) for array in arrays]


def per_device_paired(ensemble, norm_gain, project_weight, output_weight, conv_kernel, cotangent):
    mem, rows, cols, channels = ensemble.shape
    if rows < 3 or cols % 16 or (2 * mem * rows) % 16:
        return per_device_general(
            ensemble, norm_gain, project_weight, output_weight, conv_kernel, cotangent
        )
    groups = 2 * mem
    slots = 2 * groups
    cells = rows * cols
    lon_count = lax.axis_size("lon")
    lat_count = lax.axis_size("lat")
    bf16 = functools.partial(jax.ShapeDtypeStruct, dtype=BF16)
    f32 = functools.partial(jax.ShapeDtypeStruct, dtype=F32)
    swap = [(0, 1), (1, 0)]
    core_pairs = [(i, i ^ 1) for i in range(lon_count)]
    chip_pairs = [(i, (i - 1 if i % 2 == 0 else i + 1) % lon_count) for i in range(lon_count)]

    def lat_swap(offset):
        pairs = []
        for lat in range(lat_count):
            for lon in range(lon_count):
                to = (lat + 1 if lat % 2 == offset else lat - 1, lon)
                if not 0 <= to[0] < lat_count:
                    to = (lat, lon ^ 1)
                pairs.append((lat * lon_count + lon, to[0] * lon_count + to[1]))
        return pairs

    ends_shape = (2, 2 * mem * rows, channels)
    both, ends = local_call(
        stack_kernel,
        "stack",
        in_hbm(ensemble, cotangent),
        (bf16((2,) + ensemble.shape), bf16(ends_shape)),
        [pltpu.VMEM(ends_shape[1:], F32)] * 2 + [pltpu.SemaphoreType.DMA((2,))],
        pinned=True,
    )
    other_ends = lax.ppermute(ends, "member", swap)
    other = lax.ppermute(both, "member", swap)

    strip = (slots * rows, channels)
    chip_send, core_send = local_call(
        pack_strips_kernel,
        "pack_strips",
        here(ends, other_ends),
        (bf16(strip), bf16(strip)),
        [pltpu.VMEM(strip, F32)] * 2,
    )
    chip = lax.ppermute(chip_send, "lon", chip_pairs)
    core = lax.ppermute(core_send, "lon", core_pairs)

    weights = (
        norm_gain.reshape(1, channels),
        project_weight,
        output_weight,
        conv_kernel.reshape(9 * channels, channels),
    )
    *weights, project_t, output_t = local_call(
        load_kernel,
        "load_weights",
        in_hbm(*weights),
        tuple(jax.ShapeDtypeStruct(w.shape, w.dtype) for w in weights)
        + (bf16((3 * channels, channels)), bf16((channels, channels))),
        [pltpu.SemaphoreType.DMA((4,))],
        pinned=True,
        cost=MIDDLING,
    )
    halo = bf16((slots * (cols + 2), channels))
    first_send, second_send = local_call(
        pack_rows_kernel,
        "pack_rows",
        here(both, other, chip, core, weights[0]),
        (halo, halo),
        [pltpu.VMEM((2, 2 * slots, channels), F32)],
    )
    first = lax.ppermute(first_send, ("lat", "lon"), lat_swap(0))
    second = lax.ppermute(second_send, ("lat", "lon"), lat_swap(1))

    *held, updated = local_call(
        own_kernel,
        "own_cells",
        here(both, other, *weights[:3], second_send),
        (
            bf16((groups, cells, 3 * channels)),
            bf16((2, groups, cells, channels)),
            f32((groups * groups, cells, channels)),
            f32((2, mem, cells, channels)),
            f32((2, mem, cells, channels)),
            bf16((mem, cells, channels)),
        ),
        [],
        pinned=True,
        cost=LONG,
    )
    conv_t, *parts = local_call(
        centre_kernel,
        "centre",
        here(both, other, chip, core, *weights, project_t, output_t, *held, updated),
        (
            bf16((9 * channels, channels)),
            bf16((mem, rows - 2, cols, channels)),
            bf16((mem, rows - 2, cols, channels)),
            f32((mem, 2 * cols, channels)),
            f32((groups, 2 * cols, channels)),
        ),
        [
            pltpu.VMEM((mem, cells, 3 * channels), BF16),
            pltpu.VMEM((groups, cells, 3 * channels), BF16),
            pltpu.VMEM((groups, 16, channels), F32),
        ],
        pinned=True,
        cost=LONG,
    )
    return local_call(
        functools.partial(main_kernel, lat_count=lat_count),
        "main",
        here(both, second, first, *weights, project_t, output_t, conv_t, *held, *parts),
        (bf16(ensemble.shape), bf16(ensemble.shape)),
        [
            pltpu.VMEM((mem, 2 * cols, 3 * channels), BF16),
            pltpu.VMEM((groups, 2 * cols, 3 * channels), BF16),
            pltpu.VMEM((groups, 16, channels), F32),
            pltpu.VMEM((2, 2, mem, cols, channels), BF16),
            pltpu.SemaphoreType.DMA((6,)),
        ],
        copied=True,
    )


def solution(mesh):
    paired = mesh.shape["member"] == 2 and mesh.shape["lon"] % 2 == 0
    per_device = per_device_paired if paired else per_device_general
    in_specs = (
        P("member", "lat", "lon", None),
        P(),
        P(),
        P(),
        P(),
        P("member", "lat", "lon", None),
    )
    out_specs = (P("member", "lat", "lon", None), P("member", "lat", "lon", None))
    return jax.shard_map(
        per_device, mesh=mesh, in_specs=in_specs, out_specs=out_specs, check_vma=False
    )
```

```python
import functools
import math

import jax
import jax.numpy as jnp
from jax import lax
from jax.experimental import pallas as pl
from jax.experimental.pallas import tpu as pltpu
from jax.sharding import PartitionSpec as P

HEAD_COUNT = 8


FLOOR = 0.5
EPSILON = 1e-06


def padded_2(block, sides, width, periodic):
    for axis, dim in sides:
        count = lax.axis_size(axis)
        forward = [(i, i + 1) for i in range(count - 1)]
        if periodic:
            forward.append((count - 1, 0))
        backward = [(target, source) for source, target in forward]
        low = lax.ppermute(
            lax.slice_in_dim(block, block.shape[dim] - width, None, axis=dim), axis, forward
        )
        high = lax.ppermute(lax.slice_in_dim(block, 0, width, axis=dim), axis, backward)
        block = jnp.concatenate([low, block, high], axis=dim)
    return block


def row_norm(values, gain_vec):
    mean_sq = jnp.mean(values * values, axis=-1, keepdims=True)
    return values * lax.rsqrt(mean_sq + EPSILON) * gain_vec


def head_norm(values, head_count):
    shaped = values.reshape(values.shape[:-1] + (head_count, values.shape[-1] // head_count))
    mean_sq = jnp.mean(shaped * shaped, axis=-1, keepdims=True)
    return (shaped * lax.rsqrt(jnp.maximum(mean_sq, FLOOR))).reshape(values.shape)


def split_heads(values, head_count):
    return values.reshape(values.shape[:-1] + (head_count, values.shape[-1] // head_count))


def head_pullback(raw_rows, grad_rows):
    _, pullback = jax.vjp(lambda t: head_norm(t, HEAD_COUNT), raw_rows.astype(jnp.float32))
    return pullback(grad_rows)[0]


def pad_field(field_in):
    widened = padded_2(field_in, (("lon", 2),), 1, True)
    return padded_2(widened, (("lat", 1),), 1, False)


def conv_taps(padded, kernel, lat_n, lon_n, adjoint):
    running = None
    for row_off in range(3):
        for col_off in range(3):
            if adjoint:
                window = padded[
                    :, 2 - row_off : 2 - row_off + lat_n, 2 - col_off : 2 - col_off + lon_n
                ]
                summand = jnp.einsum(
                    "mabc,dc->mabd",
                    window,
                    kernel[row_off, col_off],
                    preferred_element_type=jnp.float32,
                )
            else:
                window = padded[:, row_off : row_off + lat_n, col_off : col_off + lon_n]
                summand = jnp.einsum(
                    "mabc,cd->mabd",
                    window,
                    kernel[row_off, col_off],
                    preferred_element_type=jnp.float32,
                )
            running = summand if running is None else running + summand
    return running


def per_device_general(ensemble, norm_gain, project_weight, output_weight, conv_kernel, cotangent):
    mem_dev, lat_dev, lon_dev, channels = ensemble.shape
    cell_count = lat_dev * lon_dev
    score_scale = 1.0 / math.sqrt(channels // HEAD_COUNT)
    inputs = ensemble.reshape(mem_dev, cell_count, channels).astype(jnp.float32)
    normed = row_norm(inputs, norm_gain).astype(jnp.bfloat16)
    spread = lax.all_to_all(normed, "member", split_axis=1, concat_axis=0, tiled=True)
    projected = jnp.dot(spread, project_weight, preferred_element_type=jnp.float32).astype(
        jnp.bfloat16
    )
    query_raw = projected[..., :channels]
    key_raw = projected[..., channels : 2 * channels]
    value_rows = projected[..., 2 * channels :]
    key_rows = head_norm(key_raw.astype(jnp.float32), HEAD_COUNT).astype(jnp.bfloat16)
    queries = head_norm(query_raw.astype(jnp.float32), HEAD_COUNT).astype(jnp.bfloat16)
    query_heads = split_heads(queries, HEAD_COUNT)
    key_heads = split_heads(key_rows, HEAD_COUNT)
    value_heads = split_heads(value_rows, HEAD_COUNT)
    scores = (
        jnp.einsum("mphd,nphd->mnhp", query_heads, key_heads, preferred_element_type=jnp.float32)
        * score_scale
    )
    expd = jnp.exp(scores)
    soft = expd / jnp.sum(expd, axis=1, keepdims=True)
    rounded = soft.astype(jnp.bfloat16)
    mixed_out = jnp.einsum(
        "mnhp,nphd->mphd", rounded, value_heads, preferred_element_type=jnp.float32
    )
    mixed_out = mixed_out.reshape(query_raw.shape).astype(jnp.bfloat16)
    mixed_out = lax.all_to_all(mixed_out, "member", split_axis=0, concat_axis=1, tiled=True)
    updated = (
        inputs + jnp.dot(mixed_out, output_weight, preferred_element_type=jnp.float32)
    ).astype(jnp.bfloat16)
    field_up = updated.reshape(mem_dev, lat_dev, lon_dev, channels)
    result = field_up.astype(jnp.float32) + conv_taps(
        pad_field(field_up), conv_kernel, lat_dev, lon_dev, False
    )
    result = result.astype(jnp.bfloat16)
    grad_field = cotangent.astype(jnp.float32) + conv_taps(
        pad_field(cotangent), conv_kernel, lat_dev, lon_dev, True
    )
    grad_rows = grad_field.reshape(mem_dev, cell_count, channels)
    grad_mixed = jnp.einsum(
        "mpc,dc->mpd",
        grad_rows.astype(jnp.bfloat16),
        output_weight,
        preferred_element_type=jnp.float32,
    )
    grad_mixed = grad_mixed.astype(jnp.bfloat16)
    grad_mixed = lax.all_to_all(grad_mixed, "member", split_axis=1, concat_axis=0, tiled=True)
    grad_heads = split_heads(grad_mixed, HEAD_COUNT)
    dprob = jnp.einsum(
        "mphd,nphd->mnhp", grad_heads, value_heads, preferred_element_type=jnp.float32
    )
    dscore = (soft * (dprob - jnp.sum(soft * dprob, axis=1, keepdims=True))).astype(jnp.bfloat16)
    query_grad = (
        jnp.einsum("mnhp,nphd->mphd", dscore, key_heads, preferred_element_type=jnp.float32)
        * score_scale
    )
    query_grad = query_grad.reshape(query_raw.shape)
    key_grad = (
        jnp.einsum("mnhp,mphd->nphd", dscore, query_heads, preferred_element_type=jnp.float32)
        * score_scale
    )
    key_grad = key_grad.reshape(key_raw.shape)
    value_grad = jnp.einsum(
        "mnhp,mphd->nphd", rounded, grad_heads, preferred_element_type=jnp.float32
    )
    value_grad = value_grad.reshape(key_raw.shape)
    grad_query_raw = head_pullback(query_raw, query_grad)
    grad_key_raw = head_pullback(key_raw, key_grad)
    grad_proj = jnp.concatenate([grad_query_raw, grad_key_raw, value_grad], axis=-1).astype(
        jnp.bfloat16
    )
    grad_proj = lax.all_to_all(grad_proj, "member", split_axis=0, concat_axis=1, tiled=True)
    grad_normed = jnp.einsum(
        "mpe,ce->mpc", grad_proj, project_weight, preferred_element_type=jnp.float32
    )
    _, pull_norm = jax.vjp(lambda t: row_norm(t, norm_gain), inputs)
    grad_inputs = pull_norm(grad_normed)[0]
    grad_ensemble = (
        (grad_rows + grad_inputs).astype(jnp.bfloat16).reshape(mem_dev, lat_dev, lon_dev, channels)
    )
    return (result, grad_ensemble)


F32 = jnp.float32
BF16 = jnp.bfloat16
VMEM_LIMIT = 24 * 1024 * 1024
LONG = pl.CostEstimate(flops=20_000_000_000, bytes_accessed=4_000_000, transcendentals=0)
MIDDLING = pl.CostEstimate(flops=3_000_000_000, bytes_accessed=2_000_000, transcendentals=0)


def is_even(axis):
    return lax.rem(lax.axis_index(axis), 2) == 0


def load_kernel(
    gain_hbm,
    project_hbm,
    output_hbm,
    conv_hbm,
    gain_ref,
    project_ref,
    output_ref,
    conv_ref,
    project_t_ref,
    output_t_ref,
    sems,
):
    channels = output_ref.shape[0]
    pairs = (
        (gain_hbm, gain_ref),
        (project_hbm, project_ref),
        (output_hbm, output_ref),
        (conv_hbm, conv_ref),
    )
    loads = [
        pltpu.make_async_copy(source, target, sems.at[i])
        for i, (source, target) in enumerate(pairs)
    ]
    for load in loads:
        load.start()
    for load in loads[:3]:
        load.wait()
    output_t_ref[...] = output_ref[...].T
    for kind in range(3):
        lanes = slice(kind * channels, (kind + 1) * channels)
        project_t_ref[lanes, :] = project_ref[:, lanes].T
    loads[3].wait()


def stack_kernel(ens_ref, cot_ref, both_ref, ends_ref, low_scr, high_scr, sems):
    _, mem, rows, cols, _ = both_ref.shape
    copies = [
        pltpu.make_async_copy(ref, both_ref.at[i], sems.at[i])
        for i, ref in enumerate((ens_ref, cot_ref))
    ]
    for copy in copies:
        copy.start()
    for copy in copies:
        copy.wait()
    index = 0
    for array in range(2):
        for member in range(mem):
            for row in range(rows):
                slab = both_ref[array, member, row].astype(F32)
                low_scr[index : index + 1, :] = slab[0:1]
                high_scr[index : index + 1, :] = slab[cols - 1 : cols]
                index += 1
    ends_ref[0] = low_scr[...].astype(BF16)
    ends_ref[1] = high_scr[...].astype(BF16)


def pack_strips_kernel(ends_ref, other_ends_ref, chip_ref, core_ref, low_scr, high_scr):
    part = ends_ref.shape[1] // 2
    for side, scr in ((0, low_scr), (1, high_scr)):
        for group, ref in enumerate((ends_ref, other_ends_ref)):
            column = ref[side].astype(F32)
            for array in range(2):
                at = (2 * array + group) * part
                scr[at : at + part, :] = column[array * part : (array + 1) * part]
    even = is_even("lon")
    low, high = low_scr[...], high_scr[...]
    core_ref[...] = jnp.where(even, high, low).astype(BF16)
    chip_ref[...] = jnp.where(even, low, high).astype(BF16)


def rim_columns(chip_ref, core_ref):
    even = is_even("lon")
    chip, core = chip_ref[...].astype(F32), core_ref[...].astype(F32)
    return jnp.where(even, chip, core), jnp.where(even, core, chip)


def pack_rows_kernel(
    both_ref, other_ref, chip_ref, core_ref, after_ref, first_ref, second_ref, edge_scr
):
    _, mem, rows, cols, _ = both_ref.shape
    slots = 4 * mem
    even = is_even("lat")
    west, east = rim_columns(chip_ref, core_ref)
    for slot in range(slots):
        array, member = divmod(slot, 2 * mem)
        ref, who = (both_ref, member) if member < mem else (other_ref, member - mem)
        start, stop = (ref[array, who, row].astype(F32) for row in (0, rows - 1))
        at = slice(slot * cols, (slot + 1) * cols)
        first_ref[at, :] = jnp.where(even, stop, start).astype(BF16)
        second_ref[at, :] = jnp.where(even, start, stop).astype(BF16)
        top, low = slot * rows, (slot + 1) * rows - 1
        for side, column in enumerate((west, east)):
            place = side * slots + slot
            start, stop = column[top : top + 1], column[low : low + 1]
            edge_scr[0, place : place + 1, :] = jnp.where(even, stop, start)
            edge_scr[1, place : place + 1, :] = jnp.where(even, start, stop)
    first_ref[slots * cols :, :] = edge_scr[0].astype(BF16)
    second_ref[slots * cols :, :] = edge_scr[1].astype(BF16)


def dot_nn(a, b):
    return lax.dot_general(a, b, (((1,), (0,)), ((), ())), preferred_element_type=F32)


def same_head_matrix(channels):
    width = channels // HEAD_COUNT
    lane_row = lax.broadcasted_iota(jnp.int32, (channels, channels), 0) // width
    lane_col = lax.broadcasted_iota(jnp.int32, (channels, channels), 1) // width
    return jnp.where(lane_row == lane_col, 1.0, 0.0).astype(BF16)


def head_sums(values, same_head):
    high = values.astype(BF16)
    low = (values - high.astype(F32)).astype(BF16)
    return dot_nn(high, same_head) + dot_nn(low, same_head)


def rounded_sums(values, same_head):
    return dot_nn(values.astype(BF16), same_head)


def head_units(raw, same_head, sums=head_sums):
    raw = raw.astype(F32)
    mean_sq = sums(raw * raw, same_head) * (HEAD_COUNT / raw.shape[-1])
    inverse = lax.rsqrt(jnp.maximum(mean_sq, FLOOR))
    return raw, mean_sq, inverse, (raw * inverse).astype(BF16)


def row_rsqrt(values):
    return lax.rsqrt(jnp.mean(values * values, axis=-1, keepdims=True) + EPSILON)


def split_rows(array, count):
    size = array.shape[0] // count
    return [array[i * size : (i + 1) * size] for i in range(count)]


def softmax_members(queries, keys, same_head, scale):
    products = [query * key for query in queries for key in keys]
    scores = dot_nn(jnp.concatenate(products, axis=0), same_head) * scale
    exps = split_rows(jnp.exp(scores), len(products))
    soft = []
    for m in range(len(queries)):
        mine = exps[m * len(keys) : (m + 1) * len(keys)]
        total = mine[0]
        for e in mine[1:]:
            total = total + e
        inverse = 1.0 / total
        soft.append([e * inverse for e in mine])
    return soft


def mix_values(probs, values):
    mixed = None
    for prob, value in zip(probs, values):
        term = prob.astype(BF16).astype(F32) * value.astype(F32)
        mixed = term if mixed is None else mixed + term
    return mixed.astype(BF16)


def forward_cells(x, mem, groups, gain, project_ref, output_ref, same_head):
    channels = x.shape[-1]
    own_rows = x.shape[0] // groups * mem
    scale = 1.0 / math.sqrt(channels // HEAD_COUNT)
    normed = (x * row_rsqrt(x) * gain).astype(BF16)
    query_raw = dot_nn(normed[:own_rows], project_ref[:, :channels]).astype(BF16)
    key_raw = dot_nn(normed, project_ref[:, channels : 2 * channels]).astype(BF16)
    values = dot_nn(normed, project_ref[:, 2 * channels :]).astype(BF16)
    yield
    raw = jnp.concatenate([query_raw, key_raw], axis=0)
    units = head_units(raw, same_head, rounded_sums)[3]
    yield
    queries = split_rows(units[:own_rows], mem)
    keys = split_rows(units[own_rows:], groups)
    values = split_rows(values, groups)
    soft = softmax_members(queries, keys, same_head, scale)
    yield
    mixed = jnp.concatenate([mix_values(soft[m], values) for m in range(mem)], axis=0)
    return (x[:own_rows] + dot_nn(mixed, output_ref[...])).astype(BF16)


def together(*chains):
    results = [None] * len(chains)
    active = list(range(len(chains)))
    while active:
        for i in list(active):
            try:
                next(chains[i])
            except StopIteration as stop:
                results[i] = stop.value
                active.remove(i)
    return results


def run(chain):
    while True:
        try:
            next(chain)
        except StopIteration as stop:
            return stop.value


def shift_row(scr, member, place, slab, west, east):
    cols, channels = slab.shape
    column = lax.broadcasted_iota(jnp.int32, (cols, channels), 0)
    back = jnp.where(column == 0, west, pltpu.roll(slab, 1, 0))
    ahead = jnp.where(column == cols - 1, east, pltpu.roll(slab, cols - 1, 0))
    rows_at = slice(place * cols, (place + 1) * cols)
    scr[member, rows_at, :channels] = back.astype(BF16)
    scr[member, rows_at, channels : 2 * channels] = slab.astype(BF16)
    scr[member, rows_at, 2 * channels :] = ahead.astype(BF16)


def tap_rows(taps_ref, r):
    size = taps_ref.shape[0] // 3
    return taps_ref[r * size : (r + 1) * size, :]


def own_kernel(
    both_ref,
    other_ref,
    gain_ref,
    project_ref,
    output_ref,
    after_ref,
    proj_ref,
    unit_ref,
    soft_ref,
    inverse_ref,
    pull_ref,
    updated_ref,
):
    _, mem, rows, cols, channels = both_ref.shape
    groups = 2 * mem
    cells = rows * cols
    width = channels // HEAD_COUNT
    scale = 1.0 / math.sqrt(width)
    same_head = same_head_matrix(channels)
    own = both_ref[0].reshape(mem * cells, channels)
    other = other_ref[0].reshape(mem * cells, channels)
    x = jnp.concatenate([own, other], axis=0).astype(F32)
    normed = (x * row_rsqrt(x) * gain_ref[...]).astype(BF16)
    proj = dot_nn(normed, project_ref[...]).astype(BF16)
    proj_ref[...] = proj.reshape(groups, cells, 3 * channels)
    both_raw = jnp.concatenate([proj[:, :channels], proj[:, channels : 2 * channels]], axis=0)
    raw, mean_sq, inverse, units = head_units(both_raw, same_head)
    unit_ref[...] = units.reshape(2, groups, cells, channels)
    active = jnp.where(mean_sq > FLOOR, 1.0, jnp.where(mean_sq == FLOOR, 0.5, 0.0))
    pull = active * raw * (inverse * inverse * inverse) / width
    for kind in range(2):
        at = kind * groups * cells
        mine = slice(at, at + mem * cells)
        inverse_ref[kind] = inverse[mine].reshape(mem, cells, channels)
        pull_ref[kind] = pull[mine].reshape(mem, cells, channels)
    units = split_rows(units, 2 * groups)
    soft = softmax_members(units[:groups], units[groups:], same_head, scale)
    for m in range(groups):
        for n in range(groups):
            soft_ref[m * groups + n] = soft[m][n]
    values = split_rows(proj[:, 2 * channels :], groups)
    mixed = jnp.concatenate([mix_values(soft[m], values) for m in range(mem)], axis=0)
    updated = x[: mem * cells] + dot_nn(mixed, output_ref[...])
    updated_ref[...] = updated.astype(BF16).reshape(mem, cells, channels)


def backward_cells(
    pick, grad_field, x, gain, weights_t, proj_ref, unit_ref, soft_ref, inverse_ref, pull_ref
):
    project_t_ref, output_t_ref = weights_t
    groups = proj_ref.shape[0]
    mem = inverse_ref.shape[1]
    channels = x.shape[-1]
    scale = 1.0 / math.sqrt(channels // HEAD_COUNT)
    same_head = same_head_matrix(channels)
    grad_mixed = dot_nn(grad_field.astype(BF16), output_t_ref[...]).astype(BF16)
    grads = split_rows(grad_mixed, groups)
    yield
    values = [pick(proj_ref[n, :, 2 * channels :]) for n in range(groups)]
    products = [grads[m] * values[n] for m in range(groups) for n in range(groups)]
    dprobs = split_rows(dot_nn(jnp.concatenate(products, axis=0), same_head), len(products))
    yield
    units = [[pick(unit_ref[k, n]).astype(F32) for n in range(groups)] for k in range(2)]
    query_grad = [None] * mem
    key_grad = [None] * mem
    value_grad = [None] * mem
    for m in range(groups):
        soft = [pick(soft_ref[m * groups + n]) for n in range(groups)]
        dprob = dprobs[m * groups : (m + 1) * groups]
        mean = soft[0] * dprob[0]
        for n in range(1, groups):
            mean = mean + soft[n] * dprob[n]
        for n in range(groups):
            if m >= mem and n >= mem:
                continue
            dscore = soft[n] * (dprob[n] - mean)
            if m < mem:
                term = dscore * units[1][n]
                query_grad[m] = term if query_grad[m] is None else query_grad[m] + term
            if n < mem:
                term = dscore * units[0][m]
                key_grad[n] = term if key_grad[n] is None else key_grad[n] + term
                term = soft[n] * grads[m].astype(F32)
                value_grad[n] = term if value_grad[n] is None else value_grad[n] + term

    unit_grads = [jnp.concatenate(g, axis=0) * scale for g in (query_grad, key_grad)]

    def members(take):
        return jnp.concatenate([pick(take(m)) for m in range(mem)], axis=0)

    raws = []
    for kind in range(2):
        lanes = slice(kind * channels, (kind + 1) * channels)
        raws.append(members(lambda m: proj_ref[m, :, lanes]).astype(F32))
    inner = rounded_sums(
        jnp.concatenate([g * raw for g, raw in zip(unit_grads, raws)], axis=0), same_head
    )
    inner = split_rows(inner, 2)
    yield
    pulled = []
    for kind in range(2):
        inverse = members(lambda m: inverse_ref[kind, m])
        pull = members(lambda m: pull_ref[kind, m])
        pulled.append((inverse * unit_grads[kind] - pull * inner[kind]).astype(BF16))
    pulled.append(jnp.concatenate(value_grad, axis=0).astype(BF16))
    grad_normed = dot_nn(jnp.concatenate(pulled, axis=1), project_t_ref[...]) * gain
    yield
    inverse = row_rsqrt(x)
    inner = jnp.mean(x * grad_normed, axis=-1, keepdims=True)
    total = grad_field[: x.shape[0]] + inverse * grad_normed
    return (total - x * (inverse * inverse * inverse * inner)).astype(BF16)


def centre_kernel(
    both_ref,
    other_ref,
    chip_ref,
    core_ref,
    gain_ref,
    project_ref,
    output_ref,
    conv_ref,
    project_t_ref,
    output_t_ref,
    proj_ref,
    unit_ref,
    soft_ref,
    inverse_ref,
    pull_ref,
    updated_ref,
    conv_t_ref,
    result_ref,
    grad_ref,
    result_part_ref,
    grad_part_ref,
    shift_scr,
    cot_shift_scr,
    strip_scr,
):
    _, mem, rows, cols, channels = both_ref.shape
    groups = 2 * mem
    cells = rows * cols
    gain = gain_ref[...]
    same_head = same_head_matrix(channels)
    west, east = rim_columns(chip_ref, core_ref)
    for r in range(3):
        for c in range(3):
            tap = (3 * r + c) * channels
            turned = (3 * r + 2 - c) * channels
            conv_t_ref[turned : turned + channels, :] = conv_ref[tap : tap + channels, :].T

    def convolve(scr, count, start, taps_ref, turned):
        sums = [
            [start[(m * rows + a) * cols : (m * rows + a + 1) * cols] for a in range(rows)]
            for m in range(count)
        ]
        for r in range(3):
            step = 1 - r if turned else r - 1
            outs = [a for a in range(rows) if 0 <= a + step < rows]
            begin, end = outs[0] + step, outs[-1] + step + 1
            window = jnp.concatenate(
                [scr[m, begin * cols : end * cols, :] for m in range(count)], axis=0
            )
            terms = split_rows(dot_nn(window, tap_rows(taps_ref, r)), count * len(outs))
            for m in range(count):
                for i, a in enumerate(outs):
                    sums[m][a] = sums[m][a] + terms[m * len(outs) + i]
        return sums

    cots = []
    for member in range(groups):
        for row in range(rows):
            ref, who = (both_ref, member) if member < mem else (other_ref, member - mem)
            slab = ref[1, who, row].astype(F32)
            cots.append(slab)
            at = (groups + member) * rows + row
            shift_row(cot_shift_scr, member, row, slab, west[at : at + 1], east[at : at + 1])
    sums = convolve(cot_shift_scr, groups, jnp.concatenate(cots, axis=0), conv_t_ref, True)
    for member in range(groups):
        grad_part_ref[member, :cols, :] = sums[member][0]
        grad_part_ref[member, cols:, :] = sums[member][rows - 1]
    grad_field = jnp.concatenate([slab for s in sums for slab in s[1 : rows - 1]], axis=0)

    for member in range(groups):
        at = member * rows
        strip_scr[member] = jnp.zeros((16, channels), F32)
        strip_scr[member, :rows, :] = west[at : at + rows]
        strip_scr[member, 8 : 8 + rows, :] = east[at : at + rows]
    x = strip_scr[...].reshape(groups * 16, channels)
    forward = forward_cells(x, mem, groups, gain, project_ref, output_ref, same_head)
    x = both_ref[0, :, 1 : rows - 1].reshape(mem * (cells - 2 * cols), channels).astype(F32)
    backward = backward_cells(
        lambda array: array[cols : cells - cols],
        grad_field,
        x,
        gain,
        (project_t_ref, output_t_ref),
        proj_ref,
        unit_ref,
        soft_ref,
        inverse_ref,
        pull_ref,
    )
    fresh = split_rows(run(forward).astype(F32), mem)
    next(backward)
    next(backward)

    for member in range(mem):
        for row in range(rows):
            slab = updated_ref[member, row * cols : (row + 1) * cols, :].astype(F32)
            ends = fresh[member][row : row + 1], fresh[member][8 + row : 9 + row]
            shift_row(shift_scr, member, row, slab, *ends)
    start = updated_ref[...].reshape(mem * cells, channels).astype(F32)
    sums = convolve(shift_scr, mem, start, conv_ref, False)
    for member in range(mem):
        result_part_ref[member, :cols, :] = sums[member][0]
        result_part_ref[member, cols:, :] = sums[member][rows - 1]
        for row in range(1, rows - 1):
            result_ref[member, row - 1] = sums[member][row].astype(BF16)

    grad_ref[...] = run(backward).reshape(mem, rows - 2, cols, channels)


def main_kernel(
    both_ref,
    second_ref,
    first_ref,
    gain_ref,
    project_ref,
    output_ref,
    conv_ref,
    project_t_ref,
    output_t_ref,
    conv_t_ref,
    proj_ref,
    unit_ref,
    soft_ref,
    inverse_ref,
    pull_ref,
    inner_result_ref,
    inner_grad_ref,
    result_part_ref,
    grad_part_ref,
    result_ref,
    grad_ref,
    shift_scr,
    cot_shift_scr,
    corner_scr,
    outer_scr,
    sems,
    *,
    lat_count,
):
    _, mem, rows, cols, channels = both_ref.shape
    copies = []
    for i, (ref, out_ref) in enumerate(
        ((inner_result_ref, result_ref), (inner_grad_ref, grad_ref))
    ):
        copy = pltpu.make_async_copy(ref, out_ref.at[:, pl.ds(1, rows - 2)], sems.at[i])
        copy.start()
        copies.append(copy)
    groups = 2 * mem
    slots = 2 * groups
    cells = rows * cols
    gain = gain_ref[...]
    same_head = same_head_matrix(channels)
    lat_even = is_even("lat")
    lat = lax.axis_index("lat")

    def halos(at):
        first, second = first_ref[at, :].astype(F32), second_ref[at, :].astype(F32)
        north = jnp.where(lat == 0, 0.0, jnp.where(lat_even, second, first))
        south = jnp.where(lat == lat_count - 1, 0.0, jnp.where(lat_even, first, second))
        return north, south

    halo = [halos(slice(slot * cols, (slot + 1) * cols)) for slot in range(slots)]
    corners = halos(slice(slots * cols, slots * cols + 2 * slots))

    def corner(side, slot, end):
        at = end * slots + slot
        return corners[side][at : at + 1]

    def halo_part(scr, count, taps_ref, turned):
        north, south = (2, 0) if turned else (0, 2)
        parts = []
        for side, r in ((0, north), (1, south)):
            window = jnp.concatenate(
                [scr[m, side * cols : (side + 1) * cols, :] for m in range(count)], axis=0
            )
            parts.append(split_rows(dot_nn(window, tap_rows(taps_ref, r)), count))
        return jnp.concatenate([parts[side][m] for m in range(count) for side in (0, 1)], axis=0)

    for member in range(groups):
        slot = groups + member
        for side in (0, 1):
            ends = corner(side, slot, 0), corner(side, slot, 1)
            shift_row(cot_shift_scr, member, side, halo[slot][side], *ends)
    grad_field = grad_part_ref[...].reshape(groups * 2 * cols, channels)
    grad_field = grad_field + halo_part(cot_shift_scr, groups, conv_t_ref, True)

    blocks = []
    for member in range(groups):
        corner_scr[member] = jnp.zeros((16, channels), F32)
        for side in (0, 1):
            for end in (0, 1):
                at = 2 * side + end
                corner_scr[member, at : at + 1, :] = corner(side, member, end)
        blocks += [halo[member][0], halo[member][1], corner_scr[member]]
    x = jnp.concatenate(blocks, axis=0)
    forward = forward_cells(x, mem, groups, gain, project_ref, output_ref, same_head)
    x = [both_ref[0, m, row] for m in range(mem) for row in (0, rows - 1)]
    backward = backward_cells(
        lambda array: jnp.concatenate([array[:cols], array[cells - cols :]], axis=0),
        grad_field,
        jnp.concatenate(x, axis=0).astype(F32),
        gain,
        (project_t_ref, output_t_ref),
        proj_ref,
        unit_ref,
        soft_ref,
        inverse_ref,
        pull_ref,
    )

    def finish_result(chain):
        fresh = yield from chain
        fresh = split_rows(fresh.astype(F32), mem)
        for member in range(mem):
            for side in (0, 1):
                slab = fresh[member][side * cols : (side + 1) * cols]
                at = 2 * cols + 2 * side
                ends = fresh[member][at : at + 1], fresh[member][at + 1 : at + 2]
                shift_row(shift_scr, member, side, slab, *ends)
        yield
        outer = result_part_ref[...].reshape(mem * 2 * cols, channels)
        outer = (outer + halo_part(shift_scr, mem, conv_ref, False)).astype(BF16)
        store_outer(0, outer)

    def store_outer(which, outer):
        for i, slab in enumerate(split_rows(outer, 2 * mem)):
            outer_scr[which, i % 2, i // 2] = slab
        for side, row in ((0, 0), (1, rows - 1)):
            copy = pltpu.make_async_copy(
                outer_scr.at[which, side],
                (result_ref, grad_ref)[which].at[:, row],
                sems.at[2 + 2 * which + side],
            )
            copy.start()
            copies.append(copy)

    def finish_grad(chain):
        total = yield from chain
        store_outer(1, total)

    grad_chain = finish_grad(backward)
    next(grad_chain)
    together(grad_chain, finish_result(forward))
    for copy in copies:
        copy.wait()


def local_call(kernel, name, operands, out_shape, scratch, pinned=False, cost=None, copied=False):
    whole = pl.BlockSpec(memory_space=pltpu.VMEM)
    anywhere = pl.BlockSpec(memory_space=pl.ANY)
    specs = [anywhere if in_hbm else whole for _, in_hbm in operands]
    arrays = [
        pltpu.with_memory_space_constraint(array, pltpu.HBM) if in_hbm else array
        for array, in_hbm in operands
    ]

    def keep(shape):
        return pltpu.VMEM(shape.shape, shape.dtype) if pinned else shape

    return pl.pallas_call(
        kernel,
        out_shape=jax.tree.map(keep, out_shape),
        in_specs=specs,
        out_specs=jax.tree.map(lambda _: anywhere if copied else whole, out_shape),
        scratch_shapes=scratch,
        compiler_params=pltpu.CompilerParams(vmem_limit_bytes=VMEM_LIMIT),
        cost_estimate=cost,
        name=name,
    )(*arrays)


def here(*arrays):
    return [(array, False) for array in arrays]


def in_hbm(*arrays):
    return [(array, True) for array in arrays]


def per_device_paired(ensemble, norm_gain, project_weight, output_weight, conv_kernel, cotangent):
    mem, rows, cols, channels = ensemble.shape
    if rows < 3 or cols % 16 or (2 * mem * rows) % 16:
        return per_device_general(
            ensemble, norm_gain, project_weight, output_weight, conv_kernel, cotangent
        )
    groups = 2 * mem
    slots = 2 * groups
    cells = rows * cols
    lon_count = lax.axis_size("lon")
    lat_count = lax.axis_size("lat")
    bf16 = functools.partial(jax.ShapeDtypeStruct, dtype=BF16)
    f32 = functools.partial(jax.ShapeDtypeStruct, dtype=F32)
    swap = [(0, 1), (1, 0)]
    core_pairs = [(i, i ^ 1) for i in range(lon_count)]
    chip_pairs = [(i, (i - 1 if i % 2 == 0 else i + 1) % lon_count) for i in range(lon_count)]

    def lat_swap(offset):
        pairs = []
        for lat in range(lat_count):
            for lon in range(lon_count):
                to = (lat + 1 if lat % 2 == offset else lat - 1, lon)
                if not 0 <= to[0] < lat_count:
                    to = (lat, lon ^ 1)
                pairs.append((lat * lon_count + lon, to[0] * lon_count + to[1]))
        return pairs

    ends_shape = (2, 2 * mem * rows, channels)
    both, ends = local_call(
        stack_kernel,
        "stack",
        in_hbm(ensemble, cotangent),
        (bf16((2,) + ensemble.shape), bf16(ends_shape)),
        [pltpu.VMEM(ends_shape[1:], F32)] * 2 + [pltpu.SemaphoreType.DMA((2,))],
        pinned=True,
    )
    other_ends = lax.ppermute(ends, "member", swap)
    other = lax.ppermute(both, "member", swap)

    strip = (slots * rows, channels)
    chip_send, core_send = local_call(
        pack_strips_kernel,
        "pack_strips",
        here(ends, other_ends),
        (bf16(strip), bf16(strip)),
        [pltpu.VMEM(strip, F32)] * 2,
    )
    chip = lax.ppermute(chip_send, "lon", chip_pairs)
    core = lax.ppermute(core_send, "lon", core_pairs)

    weights = (
        norm_gain.reshape(1, channels),
        project_weight,
        output_weight,
        conv_kernel.reshape(9 * channels, channels),
    )
    *weights, project_t, output_t = local_call(
        load_kernel,
        "load_weights",
        in_hbm(*weights),
        tuple(jax.ShapeDtypeStruct(w.shape, w.dtype) for w in weights)
        + (bf16((3 * channels, channels)), bf16((channels, channels))),
        [pltpu.SemaphoreType.DMA((4,))],
        pinned=True,
        cost=MIDDLING,
    )
    halo = bf16((slots * (cols + 2), channels))
    first_send, second_send = local_call(
        pack_rows_kernel,
        "pack_rows",
        here(both, other, chip, core, weights[0]),
        (halo, halo),
        [pltpu.VMEM((2, 2 * slots, channels), F32)],
    )
    first = lax.ppermute(first_send, ("lat", "lon"), lat_swap(0))
    second = lax.ppermute(second_send, ("lat", "lon"), lat_swap(1))

    *held, updated = local_call(
        own_kernel,
        "own_cells",
        here(both, other, *weights[:3], second_send),
        (
            bf16((groups, cells, 3 * channels)),
            bf16((2, groups, cells, channels)),
            f32((groups * groups, cells, channels)),
            f32((2, mem, cells, channels)),
            f32((2, mem, cells, channels)),
            bf16((mem, cells, channels)),
        ),
        [],
        pinned=True,
        cost=LONG,
    )
    conv_t, *parts = local_call(
        centre_kernel,
        "centre",
        here(both, other, chip, core, *weights, project_t, output_t, *held, updated),
        (
            bf16((9 * channels, channels)),
            bf16((mem, rows - 2, cols, channels)),
            bf16((mem, rows - 2, cols, channels)),
            f32((mem, 2 * cols, channels)),
            f32((groups, 2 * cols, channels)),
        ),
        [
            pltpu.VMEM((mem, cells, 3 * channels), BF16),
            pltpu.VMEM((groups, cells, 3 * channels), BF16),
            pltpu.VMEM((groups, 16, channels), F32),
        ],
        pinned=True,
        cost=LONG,
    )
    return local_call(
        functools.partial(main_kernel, lat_count=lat_count),
        "main",
        here(both, second, first, *weights, project_t, output_t, conv_t, *held, *parts),
        (bf16(ensemble.shape), bf16(ensemble.shape)),
        [
            pltpu.VMEM((mem, 2 * cols, 3 * channels), BF16),
            pltpu.VMEM((groups, 2 * cols, 3 * channels), BF16),
            pltpu.VMEM((groups, 16, channels), F32),
            pltpu.VMEM((2, 2, mem, cols, channels), BF16),
            pltpu.SemaphoreType.DMA((6,)),
        ],
        copied=True,
    )


def solution(mesh):
    paired = mesh.shape["member"] == 2 and mesh.shape["lon"] % 2 == 0
    per_device = per_device_paired if paired else per_device_general
    in_specs = (
        P("member", "lat", "lon", None),
        P(),
        P(),
        P(),
        P(),
        P("member", "lat", "lon", None),
    )
    out_specs = (P("member", "lat", "lon", None), P("member", "lat", "lon", None))
    return jax.shard_map(
        per_device, mesh=mesh, in_specs=in_specs, out_specs=out_specs, check_vma=False
    )
```

```python
import functools
import math

import jax
import jax.numpy as jnp
from jax import lax
from jax.experimental import pallas as pl
from jax.experimental.pallas import tpu as pltpu
from jax.sharding import PartitionSpec as P

HEAD_COUNT = 8


FLOOR = 0.5
EPSILON = 1e-06


def padded_2(block, sides, width, periodic):
    for axis, dim in sides:
        count = lax.axis_size(axis)
        forward = [(i, i + 1) for i in range(count - 1)]
        if periodic:
            forward.append((count - 1, 0))
        backward = [(target, source) for source, target in forward]
        low = lax.ppermute(
            lax.slice_in_dim(block, block.shape[dim] - width, None, axis=dim), axis, forward
        )
        high = lax.ppermute(lax.slice_in_dim(block, 0, width, axis=dim), axis, backward)
        block = jnp.concatenate([low, block, high], axis=dim)
    return block


def row_norm(values, gain_vec):
    mean_sq = jnp.mean(values * values, axis=-1, keepdims=True)
    return values * lax.rsqrt(mean_sq + EPSILON) * gain_vec


def head_norm(values, head_count):
    shaped = values.reshape(values.shape[:-1] + (head_count, values.shape[-1] // head_count))
    mean_sq = jnp.mean(shaped * shaped, axis=-1, keepdims=True)
    return (shaped * lax.rsqrt(jnp.maximum(mean_sq, FLOOR))).reshape(values.shape)


def split_heads(values, head_count):
    return values.reshape(values.shape[:-1] + (head_count, values.shape[-1] // head_count))


def head_pullback(raw_rows, grad_rows):
    _, pullback = jax.vjp(lambda t: head_norm(t, HEAD_COUNT), raw_rows.astype(jnp.float32))
    return pullback(grad_rows)[0]


def pad_field(field_in):
    widened = padded_2(field_in, (("lon", 2),), 1, True)
    return padded_2(widened, (("lat", 1),), 1, False)


def conv_taps(padded, kernel, lat_n, lon_n, adjoint):
    running = None
    for row_off in range(3):
        for col_off in range(3):
            if adjoint:
                window = padded[
                    :, 2 - row_off : 2 - row_off + lat_n, 2 - col_off : 2 - col_off + lon_n
                ]
                summand = jnp.einsum(
                    "mabc,dc->mabd",
                    window,
                    kernel[row_off, col_off],
                    preferred_element_type=jnp.float32,
                )
            else:
                window = padded[:, row_off : row_off + lat_n, col_off : col_off + lon_n]
                summand = jnp.einsum(
                    "mabc,cd->mabd",
                    window,
                    kernel[row_off, col_off],
                    preferred_element_type=jnp.float32,
                )
            running = summand if running is None else running + summand
    return running


def per_device_general(ensemble, norm_gain, project_weight, output_weight, conv_kernel, cotangent):
    mem_dev, lat_dev, lon_dev, channels = ensemble.shape
    cell_count = lat_dev * lon_dev
    score_scale = 1.0 / math.sqrt(channels // HEAD_COUNT)
    inputs = ensemble.reshape(mem_dev, cell_count, channels).astype(jnp.float32)
    normed = row_norm(inputs, norm_gain).astype(jnp.bfloat16)
    spread = lax.all_to_all(normed, "member", split_axis=1, concat_axis=0, tiled=True)
    projected = jnp.dot(spread, project_weight, preferred_element_type=jnp.float32).astype(
        jnp.bfloat16
    )
    query_raw = projected[..., :channels]
    key_raw = projected[..., channels : 2 * channels]
    value_rows = projected[..., 2 * channels :]
    key_rows = head_norm(key_raw.astype(jnp.float32), HEAD_COUNT).astype(jnp.bfloat16)
    queries = head_norm(query_raw.astype(jnp.float32), HEAD_COUNT).astype(jnp.bfloat16)
    query_heads = split_heads(queries, HEAD_COUNT)
    key_heads = split_heads(key_rows, HEAD_COUNT)
    value_heads = split_heads(value_rows, HEAD_COUNT)
    scores = (
        jnp.einsum("mphd,nphd->mnhp", query_heads, key_heads, preferred_element_type=jnp.float32)
        * score_scale
    )
    expd = jnp.exp(scores)
    soft = expd / jnp.sum(expd, axis=1, keepdims=True)
    rounded = soft.astype(jnp.bfloat16)
    mixed_out = jnp.einsum(
        "mnhp,nphd->mphd", rounded, value_heads, preferred_element_type=jnp.float32
    )
    mixed_out = mixed_out.reshape(query_raw.shape).astype(jnp.bfloat16)
    mixed_out = lax.all_to_all(mixed_out, "member", split_axis=0, concat_axis=1, tiled=True)
    updated = (
        inputs + jnp.dot(mixed_out, output_weight, preferred_element_type=jnp.float32)
    ).astype(jnp.bfloat16)
    field_up = updated.reshape(mem_dev, lat_dev, lon_dev, channels)
    result = field_up.astype(jnp.float32) + conv_taps(
        pad_field(field_up), conv_kernel, lat_dev, lon_dev, False
    )
    result = result.astype(jnp.bfloat16)
    grad_field = cotangent.astype(jnp.float32) + conv_taps(
        pad_field(cotangent), conv_kernel, lat_dev, lon_dev, True
    )
    grad_rows = grad_field.reshape(mem_dev, cell_count, channels)
    grad_mixed = jnp.einsum(
        "mpc,dc->mpd",
        grad_rows.astype(jnp.bfloat16),
        output_weight,
        preferred_element_type=jnp.float32,
    )
    grad_mixed = grad_mixed.astype(jnp.bfloat16)
    grad_mixed = lax.all_to_all(grad_mixed, "member", split_axis=1, concat_axis=0, tiled=True)
    grad_heads = split_heads(grad_mixed, HEAD_COUNT)
    dprob = jnp.einsum(
        "mphd,nphd->mnhp", grad_heads, value_heads, preferred_element_type=jnp.float32
    )
    dscore = (soft * (dprob - jnp.sum(soft * dprob, axis=1, keepdims=True))).astype(jnp.bfloat16)
    query_grad = (
        jnp.einsum("mnhp,nphd->mphd", dscore, key_heads, preferred_element_type=jnp.float32)
        * score_scale
    )
    query_grad = query_grad.reshape(query_raw.shape)
    key_grad = (
        jnp.einsum("mnhp,mphd->nphd", dscore, query_heads, preferred_element_type=jnp.float32)
        * score_scale
    )
    key_grad = key_grad.reshape(key_raw.shape)
    value_grad = jnp.einsum(
        "mnhp,mphd->nphd", rounded, grad_heads, preferred_element_type=jnp.float32
    )
    value_grad = value_grad.reshape(key_raw.shape)
    grad_query_raw = head_pullback(query_raw, query_grad)
    grad_key_raw = head_pullback(key_raw, key_grad)
    grad_proj = jnp.concatenate([grad_query_raw, grad_key_raw, value_grad], axis=-1).astype(
        jnp.bfloat16
    )
    grad_proj = lax.all_to_all(grad_proj, "member", split_axis=0, concat_axis=1, tiled=True)
    grad_normed = jnp.einsum(
        "mpe,ce->mpc", grad_proj, project_weight, preferred_element_type=jnp.float32
    )
    _, pull_norm = jax.vjp(lambda t: row_norm(t, norm_gain), inputs)
    grad_inputs = pull_norm(grad_normed)[0]
    grad_ensemble = (
        (grad_rows + grad_inputs).astype(jnp.bfloat16).reshape(mem_dev, lat_dev, lon_dev, channels)
    )
    return (result, grad_ensemble)


F32 = jnp.float32
BF16 = jnp.bfloat16
VMEM_LIMIT = 24 * 1024 * 1024
LONG = pl.CostEstimate(flops=20_000_000_000, bytes_accessed=4_000_000, transcendentals=0)
MIDDLING = pl.CostEstimate(flops=3_000_000_000, bytes_accessed=2_000_000, transcendentals=0)


def is_even(axis):
    return lax.rem(lax.axis_index(axis), 2) == 0


def load_kernel(
    gain_hbm,
    project_hbm,
    output_hbm,
    conv_hbm,
    gain_ref,
    project_ref,
    output_ref,
    conv_ref,
    project_t_ref,
    output_t_ref,
    sems,
):
    channels = output_ref.shape[0]
    pairs = (
        (gain_hbm, gain_ref),
        (project_hbm, project_ref),
        (output_hbm, output_ref),
        (conv_hbm, conv_ref),
    )
    loads = [
        pltpu.make_async_copy(source, target, sems.at[i])
        for i, (source, target) in enumerate(pairs)
    ]
    for load in loads:
        load.start()
    for load in loads[:3]:
        load.wait()
    output_t_ref[...] = output_ref[...].T
    for kind in range(3):
        lanes = slice(kind * channels, (kind + 1) * channels)
        project_t_ref[lanes, :] = project_ref[:, lanes].T
    loads[3].wait()


def stack_kernel(ens_ref, cot_ref, both_ref, ends_ref, low_scr, high_scr, sems):
    _, mem, rows, cols, _ = both_ref.shape
    copies = [
        pltpu.make_async_copy(ref, both_ref.at[i], sems.at[i])
        for i, ref in enumerate((ens_ref, cot_ref))
    ]
    for copy in copies:
        copy.start()
    for copy in copies:
        copy.wait()
    index = 0
    for array in range(2):
        for member in range(mem):
            for row in range(rows):
                slab = both_ref[array, member, row].astype(F32)
                low_scr[index : index + 1, :] = slab[0:1]
                high_scr[index : index + 1, :] = slab[cols - 1 : cols]
                index += 1
    ends_ref[0] = low_scr[...].astype(BF16)
    ends_ref[1] = high_scr[...].astype(BF16)


def pack_strips_kernel(ends_ref, other_ends_ref, chip_ref, core_ref, low_scr, high_scr):
    part = ends_ref.shape[1] // 2
    for side, scr in ((0, low_scr), (1, high_scr)):
        for group, ref in enumerate((ends_ref, other_ends_ref)):
            column = ref[side].astype(F32)
            for array in range(2):
                at = (2 * array + group) * part
                scr[at : at + part, :] = column[array * part : (array + 1) * part]
    even = is_even("lon")
    low, high = low_scr[...], high_scr[...]
    core_ref[...] = jnp.where(even, high, low).astype(BF16)
    chip_ref[...] = jnp.where(even, low, high).astype(BF16)


def rim_columns(chip_ref, core_ref):
    even = is_even("lon")
    chip, core = chip_ref[...].astype(F32), core_ref[...].astype(F32)
    return jnp.where(even, chip, core), jnp.where(even, core, chip)


def pack_rows_kernel(
    both_ref, other_ref, chip_ref, core_ref, after_ref, first_ref, second_ref, edge_scr
):
    _, mem, rows, cols, _ = both_ref.shape
    slots = 4 * mem
    even = is_even("lat")
    west, east = rim_columns(chip_ref, core_ref)
    for slot in range(slots):
        array, member = divmod(slot, 2 * mem)
        ref, who = (both_ref, member) if member < mem else (other_ref, member - mem)
        start, stop = (ref[array, who, row].astype(F32) for row in (0, rows - 1))
        at = slice(slot * cols, (slot + 1) * cols)
        first_ref[at, :] = jnp.where(even, stop, start).astype(BF16)
        second_ref[at, :] = jnp.where(even, start, stop).astype(BF16)
        top, low = slot * rows, (slot + 1) * rows - 1
        for side, column in enumerate((west, east)):
            place = side * slots + slot
            start, stop = column[top : top + 1], column[low : low + 1]
            edge_scr[0, place : place + 1, :] = jnp.where(even, stop, start)
            edge_scr[1, place : place + 1, :] = jnp.where(even, start, stop)
    first_ref[slots * cols :, :] = edge_scr[0].astype(BF16)
    second_ref[slots * cols :, :] = edge_scr[1].astype(BF16)


def dot_nn(a, b):
    return lax.dot_general(a, b, (((1,), (0,)), ((), ())), preferred_element_type=F32)


def same_head_matrix(channels):
    width = channels // HEAD_COUNT
    lane_row = lax.broadcasted_iota(jnp.int32, (channels, channels), 0) // width
    lane_col = lax.broadcasted_iota(jnp.int32, (channels, channels), 1) // width
    return jnp.where(lane_row == lane_col, 1.0, 0.0).astype(BF16)


def head_sums(values, same_head):
    high = values.astype(BF16)
    low = (values - high.astype(F32)).astype(BF16)
    return dot_nn(high, same_head) + dot_nn(low, same_head)


def rounded_sums(values, same_head):
    return dot_nn(values.astype(BF16), same_head)


def head_units(raw, same_head, sums=head_sums):
    raw = raw.astype(F32)
    mean_sq = sums(raw * raw, same_head) * (HEAD_COUNT / raw.shape[-1])
    inverse = lax.rsqrt(jnp.maximum(mean_sq, FLOOR))
    return raw, mean_sq, inverse, (raw * inverse).astype(BF16)


def row_rsqrt(values):
    return lax.rsqrt(jnp.mean(values * values, axis=-1, keepdims=True) + EPSILON)


def split_rows(array, count):
    size = array.shape[0] // count
    return [array[i * size : (i + 1) * size] for i in range(count)]


def softmax_members(queries, keys, same_head, scale):
    products = [query * key for query in queries for key in keys]
    scores = dot_nn(jnp.concatenate(products, axis=0), same_head) * scale
    exps = split_rows(jnp.exp(scores), len(products))
    soft = []
    for m in range(len(queries)):
        mine = exps[m * len(keys) : (m + 1) * len(keys)]
        total = mine[0]
        for e in mine[1:]:
            total = total + e
        inverse = 1.0 / total
        soft.append([e * inverse for e in mine])
    return soft


def mix_values(probs, values):
    mixed = None
    for prob, value in zip(probs, values):
        term = prob.astype(BF16).astype(F32) * value.astype(F32)
        mixed = term if mixed is None else mixed + term
    return mixed.astype(BF16)


def forward_cells(x, mem, groups, gain, project_ref, output_ref, same_head):
    channels = x.shape[-1]
    own_rows = x.shape[0] // groups * mem
    scale = 1.0 / math.sqrt(channels // HEAD_COUNT)
    normed = (x * row_rsqrt(x) * gain).astype(BF16)
    query_raw = dot_nn(normed[:own_rows], project_ref[:, :channels]).astype(BF16)
    key_raw = dot_nn(normed, project_ref[:, channels : 2 * channels]).astype(BF16)
    values = dot_nn(normed, project_ref[:, 2 * channels :]).astype(BF16)
    yield
    raw = jnp.concatenate([query_raw, key_raw], axis=0)
    units = head_units(raw, same_head, rounded_sums)[3]
    yield
    queries = split_rows(units[:own_rows], mem)
    keys = split_rows(units[own_rows:], groups)
    values = split_rows(values, groups)
    soft = softmax_members(queries, keys, same_head, scale)
    yield
    mixed = jnp.concatenate([mix_values(soft[m], values) for m in range(mem)], axis=0)
    return (x[:own_rows] + dot_nn(mixed, output_ref[...])).astype(BF16)


def together(*chains):
    results = [None] * len(chains)
    active = list(range(len(chains)))
    while active:
        for i in list(active):
            try:
                next(chains[i])
            except StopIteration as stop:
                results[i] = stop.value
                active.remove(i)
    return results


def run(chain):
    while True:
        try:
            next(chain)
        except StopIteration as stop:
            return stop.value


def shift_row(scr, member, place, slab, west, east):
    cols, channels = slab.shape
    column = lax.broadcasted_iota(jnp.int32, (cols, channels), 0)
    back = jnp.where(column == 0, west, pltpu.roll(slab, 1, 0))
    ahead = jnp.where(column == cols - 1, east, pltpu.roll(slab, cols - 1, 0))
    rows_at = slice(place * cols, (place + 1) * cols)
    scr[member, rows_at, :channels] = back.astype(BF16)
    scr[member, rows_at, channels : 2 * channels] = slab.astype(BF16)
    scr[member, rows_at, 2 * channels :] = ahead.astype(BF16)


def tap_rows(taps_ref, r):
    size = taps_ref.shape[0] // 3
    return taps_ref[r * size : (r + 1) * size, :]


def own_kernel(
    both_ref,
    other_ref,
    gain_ref,
    project_ref,
    output_ref,
    after_ref,
    proj_ref,
    unit_ref,
    soft_ref,
    inverse_ref,
    pull_ref,
    updated_ref,
):
    _, mem, rows, cols, channels = both_ref.shape
    groups = 2 * mem
    cells = rows * cols
    width = channels // HEAD_COUNT
    scale = 1.0 / math.sqrt(width)
    same_head = same_head_matrix(channels)
    own = both_ref[0].reshape(mem * cells, channels)
    other = other_ref[0].reshape(mem * cells, channels)
    x = jnp.concatenate([own, other], axis=0).astype(F32)
    normed = (x * row_rsqrt(x) * gain_ref[...]).astype(BF16)
    proj = dot_nn(normed, project_ref[...]).astype(BF16)
    proj_ref[...] = proj.reshape(groups, cells, 3 * channels)
    both_raw = jnp.concatenate([proj[:, :channels], proj[:, channels : 2 * channels]], axis=0)
    raw, mean_sq, inverse, units = head_units(both_raw, same_head)
    unit_ref[...] = units.reshape(2, groups, cells, channels)
    active = jnp.where(mean_sq > FLOOR, 1.0, jnp.where(mean_sq == FLOOR, 0.5, 0.0))
    pull = active * raw * (inverse * inverse * inverse) / width
    for kind in range(2):
        at = kind * groups * cells
        mine = slice(at, at + mem * cells)
        inverse_ref[kind] = inverse[mine].reshape(mem, cells, channels)
        pull_ref[kind] = pull[mine].reshape(mem, cells, channels)
    units = split_rows(units, 2 * groups)
    soft = softmax_members(units[:groups], units[groups:], same_head, scale)
    for m in range(groups):
        for n in range(groups):
            soft_ref[m * groups + n] = soft[m][n]
    values = split_rows(proj[:, 2 * channels :], groups)
    mixed = jnp.concatenate([mix_values(soft[m], values) for m in range(mem)], axis=0)
    updated = x[: mem * cells] + dot_nn(mixed, output_ref[...])
    updated_ref[...] = updated.astype(BF16).reshape(mem, cells, channels)


def backward_cells(
    pick, grad_field, x, gain, weights_t, proj_ref, unit_ref, soft_ref, inverse_ref, pull_ref
):
    project_t_ref, output_t_ref = weights_t
    groups = proj_ref.shape[0]
    mem = inverse_ref.shape[1]
    channels = x.shape[-1]
    scale = 1.0 / math.sqrt(channels // HEAD_COUNT)
    same_head = same_head_matrix(channels)
    grad_mixed = dot_nn(grad_field.astype(BF16), output_t_ref[...]).astype(BF16)
    grads = split_rows(grad_mixed, groups)
    yield
    values = [pick(proj_ref[n, :, 2 * channels :]) for n in range(groups)]
    products = [grads[m] * values[n] for m in range(groups) for n in range(groups)]
    dprobs = split_rows(dot_nn(jnp.concatenate(products, axis=0), same_head), len(products))
    yield
    units = [[pick(unit_ref[k, n]).astype(F32) for n in range(groups)] for k in range(2)]
    query_grad = [None] * mem
    key_grad = [None] * mem
    value_grad = [None] * mem
    for m in range(groups):
        soft = [pick(soft_ref[m * groups + n]) for n in range(groups)]
        dprob = dprobs[m * groups : (m + 1) * groups]
        mean = soft[0] * dprob[0]
        for n in range(1, groups):
            mean = mean + soft[n] * dprob[n]
        for n in range(groups):
            if m >= mem and n >= mem:
                continue
            dscore = soft[n] * (dprob[n] - mean)
            if m < mem:
                term = dscore * units[1][n]
                query_grad[m] = term if query_grad[m] is None else query_grad[m] + term
            if n < mem:
                term = dscore * units[0][m]
                key_grad[n] = term if key_grad[n] is None else key_grad[n] + term
                term = soft[n] * grads[m].astype(F32)
                value_grad[n] = term if value_grad[n] is None else value_grad[n] + term

    unit_grads = [jnp.concatenate(g, axis=0) * scale for g in (query_grad, key_grad)]

    def members(take):
        return jnp.concatenate([pick(take(m)) for m in range(mem)], axis=0)

    raws = []
    for kind in range(2):
        lanes = slice(kind * channels, (kind + 1) * channels)
        raws.append(members(lambda m: proj_ref[m, :, lanes]).astype(F32))
    inner = rounded_sums(
        jnp.concatenate([g * raw for g, raw in zip(unit_grads, raws)], axis=0), same_head
    )
    inner = split_rows(inner, 2)
    yield
    pulled = []
    for kind in range(2):
        inverse = members(lambda m: inverse_ref[kind, m])
        pull = members(lambda m: pull_ref[kind, m])
        pulled.append((inverse * unit_grads[kind] - pull * inner[kind]).astype(BF16))
    pulled.append(jnp.concatenate(value_grad, axis=0).astype(BF16))
    grad_normed = dot_nn(jnp.concatenate(pulled, axis=1), project_t_ref[...]) * gain
    yield
    inverse = row_rsqrt(x)
    inner = jnp.mean(x * grad_normed, axis=-1, keepdims=True)
    total = grad_field[: x.shape[0]] + inverse * grad_normed
    return (total - x * (inverse * inverse * inverse * inner)).astype(BF16)


def centre_kernel(
    both_ref,
    other_ref,
    chip_ref,
    core_ref,
    gain_ref,
    project_ref,
    output_ref,
    conv_ref,
    project_t_ref,
    output_t_ref,
    proj_ref,
    unit_ref,
    soft_ref,
    inverse_ref,
    pull_ref,
    updated_ref,
    conv_t_ref,
    result_ref,
    grad_ref,
    result_part_ref,
    grad_part_ref,
    shift_scr,
    cot_shift_scr,
    strip_scr,
):
    _, mem, rows, cols, channels = both_ref.shape
    groups = 2 * mem
    cells = rows * cols
    gain = gain_ref[...]
    same_head = same_head_matrix(channels)
    west, east = rim_columns(chip_ref, core_ref)
    for r in range(3):
        for c in range(3):
            tap = (3 * r + c) * channels
            turned = (3 * r + 2 - c) * channels
            conv_t_ref[turned : turned + channels, :] = conv_ref[tap : tap + channels, :].T

    def convolve(scr, count, start, taps_ref, turned):
        sums = [
            [start[(m * rows + a) * cols : (m * rows + a + 1) * cols] for a in range(rows)]
            for m in range(count)
        ]
        for r in range(3):
            step = 1 - r if turned else r - 1
            outs = [a for a in range(rows) if 0 <= a + step < rows]
            begin, end = outs[0] + step, outs[-1] + step + 1
            window = jnp.concatenate(
                [scr[m, begin * cols : end * cols, :] for m in range(count)], axis=0
            )
            terms = split_rows(dot_nn(window, tap_rows(taps_ref, r)), count * len(outs))
            for m in range(count):
                for i, a in enumerate(outs):
                    sums[m][a] = sums[m][a] + terms[m * len(outs) + i]
        return sums

    cots = []
    for member in range(groups):
        for row in range(rows):
            ref, who = (both_ref, member) if member < mem else (other_ref, member - mem)
            slab = ref[1, who, row].astype(F32)
            cots.append(slab)
            at = (groups + member) * rows + row
            shift_row(cot_shift_scr, member, row, slab, west[at : at + 1], east[at : at + 1])
    sums = convolve(cot_shift_scr, groups, jnp.concatenate(cots, axis=0), conv_t_ref, True)
    for member in range(groups):
        grad_part_ref[member, :cols, :] = sums[member][0]
        grad_part_ref[member, cols:, :] = sums[member][rows - 1]
    grad_field = jnp.concatenate([slab for s in sums for slab in s[1 : rows - 1]], axis=0)

    for member in range(groups):
        at = member * rows
        strip_scr[member] = jnp.zeros((16, channels), F32)
        strip_scr[member, :rows, :] = west[at : at + rows]
        strip_scr[member, 8 : 8 + rows, :] = east[at : at + rows]
    x = strip_scr[...].reshape(groups * 16, channels)
    forward = forward_cells(x, mem, groups, gain, project_ref, output_ref, same_head)
    x = both_ref[0, :, 1 : rows - 1].reshape(mem * (cells - 2 * cols), channels).astype(F32)
    backward = backward_cells(
        lambda array: array[cols : cells - cols],
        grad_field,
        x,
        gain,
        (project_t_ref, output_t_ref),
        proj_ref,
        unit_ref,
        soft_ref,
        inverse_ref,
        pull_ref,
    )
    fresh, total = run(forward), run(backward)
    fresh = split_rows(fresh.astype(F32), mem)
    grad_ref[...] = total.reshape(mem, rows - 2, cols, channels)

    for member in range(mem):
        for row in range(rows):
            slab = updated_ref[member, row * cols : (row + 1) * cols, :].astype(F32)
            ends = fresh[member][row : row + 1], fresh[member][8 + row : 9 + row]
            shift_row(shift_scr, member, row, slab, *ends)
    start = updated_ref[...].reshape(mem * cells, channels).astype(F32)
    sums = convolve(shift_scr, mem, start, conv_ref, False)
    for member in range(mem):
        result_part_ref[member, :cols, :] = sums[member][0]
        result_part_ref[member, cols:, :] = sums[member][rows - 1]
        for row in range(1, rows - 1):
            result_ref[member, row - 1] = sums[member][row].astype(BF16)


def main_kernel(
    both_ref,
    second_ref,
    first_ref,
    gain_ref,
    project_ref,
    output_ref,
    conv_ref,
    project_t_ref,
    output_t_ref,
    conv_t_ref,
    proj_ref,
    unit_ref,
    soft_ref,
    inverse_ref,
    pull_ref,
    inner_result_ref,
    inner_grad_ref,
    result_part_ref,
    grad_part_ref,
    result_ref,
    grad_ref,
    shift_scr,
    cot_shift_scr,
    corner_scr,
    outer_scr,
    sems,
    *,
    lat_count,
):
    _, mem, rows, cols, channels = both_ref.shape
    copies = []
    for i, (ref, out_ref) in enumerate(
        ((inner_result_ref, result_ref), (inner_grad_ref, grad_ref))
    ):
        copy = pltpu.make_async_copy(ref, out_ref.at[:, pl.ds(1, rows - 2)], sems.at[i])
        copy.start()
        copies.append(copy)
    groups = 2 * mem
    slots = 2 * groups
    cells = rows * cols
    gain = gain_ref[...]
    same_head = same_head_matrix(channels)
    lat_even = is_even("lat")
    lat = lax.axis_index("lat")

    def halos(at):
        first, second = first_ref[at, :].astype(F32), second_ref[at, :].astype(F32)
        north = jnp.where(lat == 0, 0.0, jnp.where(lat_even, second, first))
        south = jnp.where(lat == lat_count - 1, 0.0, jnp.where(lat_even, first, second))
        return north, south

    halo = [halos(slice(slot * cols, (slot + 1) * cols)) for slot in range(slots)]
    corners = halos(slice(slots * cols, slots * cols + 2 * slots))

    def corner(side, slot, end):
        at = end * slots + slot
        return corners[side][at : at + 1]

    def halo_part(scr, count, taps_ref, turned):
        north, south = (2, 0) if turned else (0, 2)
        parts = []
        for side, r in ((0, north), (1, south)):
            window = jnp.concatenate(
                [scr[m, side * cols : (side + 1) * cols, :] for m in range(count)], axis=0
            )
            parts.append(split_rows(dot_nn(window, tap_rows(taps_ref, r)), count))
        return jnp.concatenate([parts[side][m] for m in range(count) for side in (0, 1)], axis=0)

    for member in range(groups):
        slot = groups + member
        for side in (0, 1):
            ends = corner(side, slot, 0), corner(side, slot, 1)
            shift_row(cot_shift_scr, member, side, halo[slot][side], *ends)
    grad_field = grad_part_ref[...].reshape(groups * 2 * cols, channels)
    grad_field = grad_field + halo_part(cot_shift_scr, groups, conv_t_ref, True)

    blocks = []
    for member in range(groups):
        corner_scr[member] = jnp.zeros((16, channels), F32)
        for side in (0, 1):
            for end in (0, 1):
                at = 2 * side + end
                corner_scr[member, at : at + 1, :] = corner(side, member, end)
        blocks += [halo[member][0], halo[member][1], corner_scr[member]]
    x = jnp.concatenate(blocks, axis=0)
    forward = forward_cells(x, mem, groups, gain, project_ref, output_ref, same_head)
    x = [both_ref[0, m, row] for m in range(mem) for row in (0, rows - 1)]
    backward = backward_cells(
        lambda array: jnp.concatenate([array[:cols], array[cells - cols :]], axis=0),
        grad_field,
        jnp.concatenate(x, axis=0).astype(F32),
        gain,
        (project_t_ref, output_t_ref),
        proj_ref,
        unit_ref,
        soft_ref,
        inverse_ref,
        pull_ref,
    )

    def finish_result(chain):
        fresh = yield from chain
        fresh = split_rows(fresh.astype(F32), mem)
        for member in range(mem):
            for side in (0, 1):
                slab = fresh[member][side * cols : (side + 1) * cols]
                at = 2 * cols + 2 * side
                ends = fresh[member][at : at + 1], fresh[member][at + 1 : at + 2]
                shift_row(shift_scr, member, side, slab, *ends)
        yield
        outer = result_part_ref[...].reshape(mem * 2 * cols, channels)
        outer = (outer + halo_part(shift_scr, mem, conv_ref, False)).astype(BF16)
        store_outer(0, outer)

    def store_outer(which, outer):
        for i, slab in enumerate(split_rows(outer, 2 * mem)):
            outer_scr[which, i % 2, i // 2] = slab
        for side, row in ((0, 0), (1, rows - 1)):
            copy = pltpu.make_async_copy(
                outer_scr.at[which, side],
                (result_ref, grad_ref)[which].at[:, row],
                sems.at[2 + 2 * which + side],
            )
            copy.start()
            copies.append(copy)

    def finish_grad(chain):
        total = yield from chain
        store_outer(1, total)

    grad_chain = finish_grad(backward)
    next(grad_chain)
    next(grad_chain)
    together(grad_chain, finish_result(forward))
    for copy in copies:
        copy.wait()


def local_call(kernel, name, operands, out_shape, scratch, pinned=False, cost=None, copied=False):
    whole = pl.BlockSpec(memory_space=pltpu.VMEM)
    anywhere = pl.BlockSpec(memory_space=pl.ANY)
    specs = [anywhere if in_hbm else whole for _, in_hbm in operands]
    arrays = [
        pltpu.with_memory_space_constraint(array, pltpu.HBM) if in_hbm else array
        for array, in_hbm in operands
    ]

    def keep(shape):
        return pltpu.VMEM(shape.shape, shape.dtype) if pinned else shape

    return pl.pallas_call(
        kernel,
        out_shape=jax.tree.map(keep, out_shape),
        in_specs=specs,
        out_specs=jax.tree.map(lambda _: anywhere if copied else whole, out_shape),
        scratch_shapes=scratch,
        compiler_params=pltpu.CompilerParams(vmem_limit_bytes=VMEM_LIMIT),
        cost_estimate=cost,
        name=name,
    )(*arrays)


def here(*arrays):
    return [(array, False) for array in arrays]


def in_hbm(*arrays):
    return [(array, True) for array in arrays]


def per_device_paired(ensemble, norm_gain, project_weight, output_weight, conv_kernel, cotangent):
    mem, rows, cols, channels = ensemble.shape
    if rows < 3 or cols % 16 or (2 * mem * rows) % 16:
        return per_device_general(
            ensemble, norm_gain, project_weight, output_weight, conv_kernel, cotangent
        )
    groups = 2 * mem
    slots = 2 * groups
    cells = rows * cols
    lon_count = lax.axis_size("lon")
    lat_count = lax.axis_size("lat")
    bf16 = functools.partial(jax.ShapeDtypeStruct, dtype=BF16)
    f32 = functools.partial(jax.ShapeDtypeStruct, dtype=F32)
    swap = [(0, 1), (1, 0)]
    core_pairs = [(i, i ^ 1) for i in range(lon_count)]
    chip_pairs = [(i, (i - 1 if i % 2 == 0 else i + 1) % lon_count) for i in range(lon_count)]

    def lat_swap(offset):
        pairs = []
        for lat in range(lat_count):
            for lon in range(lon_count):
                to = (lat + 1 if lat % 2 == offset else lat - 1, lon)
                if not 0 <= to[0] < lat_count:
                    to = (lat, lon ^ 1)
                pairs.append((lat * lon_count + lon, to[0] * lon_count + to[1]))
        return pairs

    ends_shape = (2, 2 * mem * rows, channels)
    both, ends = local_call(
        stack_kernel,
        "stack",
        in_hbm(ensemble, cotangent),
        (bf16((2,) + ensemble.shape), bf16(ends_shape)),
        [pltpu.VMEM(ends_shape[1:], F32)] * 2 + [pltpu.SemaphoreType.DMA((2,))],
        pinned=True,
    )
    other_ends = lax.ppermute(ends, "member", swap)
    other = lax.ppermute(both, "member", swap)

    strip = (slots * rows, channels)
    chip_send, core_send = local_call(
        pack_strips_kernel,
        "pack_strips",
        here(ends, other_ends),
        (bf16(strip), bf16(strip)),
        [pltpu.VMEM(strip, F32)] * 2,
    )
    chip = lax.ppermute(chip_send, "lon", chip_pairs)
    core = lax.ppermute(core_send, "lon", core_pairs)

    weights = (
        norm_gain.reshape(1, channels),
        project_weight,
        output_weight,
        conv_kernel.reshape(9 * channels, channels),
    )
    *weights, project_t, output_t = local_call(
        load_kernel,
        "load_weights",
        in_hbm(*weights),
        tuple(jax.ShapeDtypeStruct(w.shape, w.dtype) for w in weights)
        + (bf16((3 * channels, channels)), bf16((channels, channels))),
        [pltpu.SemaphoreType.DMA((4,))],
        pinned=True,
        cost=MIDDLING,
    )
    halo = bf16((slots * (cols + 2), channels))
    first_send, second_send = local_call(
        pack_rows_kernel,
        "pack_rows",
        here(both, other, chip, core, weights[0]),
        (halo, halo),
        [pltpu.VMEM((2, 2 * slots, channels), F32)],
    )
    first = lax.ppermute(first_send, ("lat", "lon"), lat_swap(0))
    second = lax.ppermute(second_send, ("lat", "lon"), lat_swap(1))

    *held, updated = local_call(
        own_kernel,
        "own_cells",
        here(both, other, *weights[:3], second_send),
        (
            bf16((groups, cells, 3 * channels)),
            bf16((2, groups, cells, channels)),
            f32((groups * groups, cells, channels)),
            f32((2, mem, cells, channels)),
            f32((2, mem, cells, channels)),
            bf16((mem, cells, channels)),
        ),
        [],
        pinned=True,
        cost=LONG,
    )
    conv_t, *parts = local_call(
        centre_kernel,
        "centre",
        here(both, other, chip, core, *weights, project_t, output_t, *held, updated),
        (
            bf16((9 * channels, channels)),
            bf16((mem, rows - 2, cols, channels)),
            bf16((mem, rows - 2, cols, channels)),
            f32((mem, 2 * cols, channels)),
            f32((groups, 2 * cols, channels)),
        ),
        [
            pltpu.VMEM((mem, cells, 3 * channels), BF16),
            pltpu.VMEM((groups, cells, 3 * channels), BF16),
            pltpu.VMEM((groups, 16, channels), F32),
        ],
        pinned=True,
        cost=LONG,
    )
    return local_call(
        functools.partial(main_kernel, lat_count=lat_count),
        "main",
        here(both, second, first, *weights, project_t, output_t, conv_t, *held, *parts),
        (bf16(ensemble.shape), bf16(ensemble.shape)),
        [
            pltpu.VMEM((mem, 2 * cols, 3 * channels), BF16),
            pltpu.VMEM((groups, 2 * cols, 3 * channels), BF16),
            pltpu.VMEM((groups, 16, channels), F32),
            pltpu.VMEM((2, 2, mem, cols, channels), BF16),
            pltpu.SemaphoreType.DMA((6,)),
        ],
        copied=True,
    )


def solution(mesh):
    paired = mesh.shape["member"] == 2 and mesh.shape["lon"] % 2 == 0
    per_device = per_device_paired if paired else per_device_general
    in_specs = (
        P("member", "lat", "lon", None),
        P(),
        P(),
        P(),
        P(),
        P("member", "lat", "lon", None),
    )
    out_specs = (P("member", "lat", "lon", None), P("member", "lat", "lon", None))
    return jax.shard_map(
        per_device, mesh=mesh, in_specs=in_specs, out_specs=out_specs, check_vma=False
    )
```
